32 devices in a mesh: seg: 8 (over z, core), dp: 4 (over y, x).
Axes of the slice: x: 2, y: 2, z: 4, core: 2. Of those that a mesh axis runs over, the one named last changes fastest.
Arguments:
- frames: bfloat16 [8, 4096, 80], P('dp', 'seg'), may hold values from -6 to 6
- speech_mask: int32 [8, 4096], P('dp', 'seg'), may hold values from 0 to 1
- targets: int32 [8, 4096], P('dp', 'seg'), may hold values from 0 to 1023
- in_proj: float32 [80, 512], replicated, may hold values from -0.625 to 0.625
- in_moment: float32 [80, 512], replicated, may hold values from -0.00061035156 to 0.00061035156
- in_second: float32 [80, 512], replicated, may hold values from 9.187344e-11 to 3.6749376e-10
- out_proj: float32 [512, 1024], replicated, may hold values from -0.25 to 0.25
- out_moment: float32 [512, 1024], replicated, may hold values from -0.00061035156 to 0.00061035156
- out_second: float32 [512, 1024], replicated, may hold values from 9.187344e-11 to 3.6749376e-10
- layer_vectors: float32 [2, 12, 512], replicated, may hold values from -0.5 to 2.07
- vectors_moment: float32 [2, 12, 512], replicated, may hold values from -0.0029296875 to 0.0029296875
- vectors_second: float32 [2, 12, 512], replicated, may hold values from 2.296836e-09 to 9.187344e-09
- outer_vectors: float32 [5, 512], replicated, may hold values from -0.5 to 2.07
- outer_moment: float32 [5, 512], replicated, may hold values from -0.0029296875 to 0.0029296875
- outer_second: float32 [5, 512], replicated, may hold values from 2.296836e-09 to 9.187344e-09
- attn_proj: float32 [2, 4, 512, 512], P(None, None, 'seg'), may hold values from -0.25 to 0.25
- attn_momentum: float32 [2, 4, 512, 512], P(None, None, 'seg'), may hold values from -0.00061035156 to 0.00061035156
- ff_up: float32 [2, 512, 2048], P(None, 'seg'), may hold values from -0.25 to 0.25
- up_momentum: float32 [2, 512, 2048], P(None, 'seg'), may hold values from -0.00061035156 to 0.00061035156
- ff_down: float32 [2, 2048, 512], P(None, 'seg'), may hold values from -0.125 to 0.125
- down_momentum: float32 [2, 2048, 512], P(None, 'seg'), may hold values from -0.00061035156 to 0.00061035156
- in_copy: bfloat16 [80, 512], replicated, may hold values from -0.625 to 0.625
- out_copy: bfloat16 [512, 1024], replicated, may hold values from -0.25 to 0.25
- attn_copy: bfloat16 [2, 4, 512, 512], replicated, may hold values from -0.25 to 0.25
- up_copy: bfloat16 [2, 512, 2048], replicated, may hold values from -0.25 to 0.25
- down_copy: bfloat16 [2, 2048, 512], replicated, may hold values from -0.125 to 0.125
Outputs:
- loss_sum: float32 [], replicated
- grad_norm: float32 [], replicated
- in_new: float32 [80, 512], replicated
- in_moment_new: float32 [80, 512], replicated
- in_second_new: float32 [80, 512], replicated
- out_new: float32 [512, 1024], replicated
- out_moment_new: float32 [512, 1024], replicated
- out_second_new: float32 [512, 1024], replicated
- vectors_new: float32 [2, 12, 512], replicated
- vectors_moment_new: float32 [2, 12, 512], replicated
- vectors_second_new: float32 [2, 12, 512], replicated
- outer_new: float32 [5, 512], replicated
- outer_moment_new: float32 [5, 512], replicated
- outer_second_new: float32 [5, 512], replicated
- attn_new: float32 [2, 4, 512, 512], P(None, None, 'seg')
- attn_momentum_new: float32 [2, 4, 512, 512], P(None, None, 'seg')
- up_new: float32 [2, 512, 2048], P(None, 'seg')
- up_momentum_new: float32 [2, 512, 2048], P(None, 'seg')
- down_new: float32 [2, 2048, 512], P(None, 'seg')
- down_momentum_new: float32 [2, 2048, 512], P(None, 'seg')
- in_copy_new: bfloat16 [80, 512], replicated
- out_copy_new: bfloat16 [512, 1024], replicated
- attn_copy_new: bfloat16 [2, 4, 512, 512], P(None, None, 'seg')
- up_copy_new: bfloat16 [2, 512, 2048], P(None, 'seg')
- down_copy_new: bfloat16 [2, 2048, 512], P(None, 'seg')
The draws below stay inside these ranges and needn't reach their ends.
All inputs are finite; a program needn't handle non-finite values.
Results may differ from the reference program's by a relative error of at most 0.008.
Values may be sent and summed in bfloat16 or wider, within the bound.
A program may use at most 448 MiB of HBM per device.

```python
import math
import jax
import jax.numpy as jnp
from jax import lax

D = 512
HEAD_DIM = 64
FF = 2048
FRAME_DIM = 80
CODES = 1024
LAYERS = 2
SEG_LEN = 512
STEP = 10
STREAMS = 8
FRAMES = 4096
PARAMS = 6871552
N_SEG = 8


def draw_speech_mask(key, part):
    key = jax.random.fold_in(key, 3)
    ticket = jax.random.randint(key, (STREAMS, FRAMES), 0, 1000)
    limit = 250 + 500 * jnp.arange(FRAMES) // (FRAMES - 1)
    return (ticket < limit[None, :]).astype(jnp.int32)


def rising_rows(key, row_count, gain_rows):
    noise = jax.random.uniform(key, row_count + (D,), jnp.float32, -1.0, 1.0)
    rise = 0.6 + 1.2 * jnp.arange(D, dtype=jnp.float32) / (D - 1)
    gains = rise * (1.0 + 0.15 * noise)
    row_index = jnp.arange(row_count[-1])[:, None]
    is_gain = jnp.zeros_like(row_index, dtype=bool)
    for gain_row in gain_rows:
        is_gain = is_gain | (row_index == gain_row)
    return jnp.where(is_gain, gains, 0.5 * noise)


def draw_layer_vectors(key, part):
    key = jax.random.fold_in(key, 5)
    return rising_rows(key, (LAYERS, 8 + FF // D), (0, 2))


def draw_outer_vectors(key, part):
    key = jax.random.fold_in(key, 7)
    return rising_rows(key, (3 + CODES // D,), (1,))


def touch_ends(entries, rng, least, high):
    dims = entries.shape
    spot = [jax.random.randint(jax.random.fold_in(rng, axis), (), 0, dims[axis]) for axis in range(len(dims))]
    entries = entries.at[tuple(spot)].set(least)
    longest = dims.index(max(dims))
    spot[longest] = (spot[longest] + 1) % dims[longest]
    return entries.at[tuple(spot)].set(high)


def block_levels(rng, extent, split, low, largest):
    level = 1.0
    for dim, parts in split:
        draws = jax.random.uniform(jax.random.fold_in(jax.random.fold_in(rng, 6), dim), (parts,), jnp.float32, low / len(split), largest / len(split))
        level = level * jnp.repeat(jnp.exp(draws), extent[dim] // parts).reshape((-1,) + (1,) * (len(extent) - 1 - dim))
    return level


def scatter_about(own_key, shape, deviation, most, split=(), kind=jnp.bfloat16):
    result = jax.random.normal(own_key, shape, jnp.float32) * deviation
    if len(split) > 0:
        result = block_levels(own_key, shape, split, -0.22, 0.18) * result
    return jnp.clip(result, min=-most, max=most).astype(kind)


def setup_inputs(seed: int = 0) -> dict:
    key_list = jax.random.split(jax.random.key(seed), 27)
    frames = scatter_about(key_list[0], (STREAMS, FRAMES, FRAME_DIM), 1.0, 6.0, ((0, 4), (1, 8)))
    speech_mask = draw_speech_mask(jax.random.fold_in(key_list[26], 71), 0)
    targets = touch_ends(jax.random.randint(key_list[2], (STREAMS, FRAMES), 0, CODES), jax.random.fold_in(key_list[2], 1), 0, CODES - 1).astype(jnp.int32)
    in_proj = scatter_about(key_list[3], (FRAME_DIM, D), FRAME_DIM ** -0.5, 0.625, (), jnp.float32)
    in_moment = scatter_about(key_list[4], (FRAME_DIM, D), (0.25 / PARAMS ** 0.5), 0.00061035156, (), jnp.float32)
    in_second = jnp.clip(jnp.exp(jax.random.uniform(key_list[5], (FRAME_DIM, D), jnp.float32, math.log(9.18734394117493e-11), math.log(3.674937576469972e-10))), 9.18734394117493e-11, 3.674937576469972e-10)
    out_proj = scatter_about(key_list[6], (D, CODES), D ** -0.5, 0.25, (), jnp.float32)
    out_moment = scatter_about(key_list[7], (D, CODES), (0.25 / PARAMS ** 0.5), 0.00061035156, (), jnp.float32)
    out_second = jnp.clip(jnp.exp(jax.random.uniform(key_list[8], (D, CODES), jnp.float32, math.log(9.18734394117493e-11), math.log(3.674937576469972e-10))), 9.18734394117493e-11, 3.674937576469972e-10)
    layer_vectors = draw_layer_vectors(jax.random.fold_in(key_list[26], 71), 0)
    vectors_moment = scatter_about(key_list[10], (LAYERS, 8 + FF // D, D), (1.25 / PARAMS ** 0.5), 0.0029296875, (), jnp.float32)
    vectors_second = jnp.clip(jnp.exp(jax.random.uniform(key_list[11], (LAYERS, 8 + FF // D, D), jnp.float32, math.log(2.2968360546826716e-09), math.log(9.187344218730686e-09))), 2.2968360546826716e-09, 9.187344218730686e-09)
    outer_vectors = draw_outer_vectors(jax.random.fold_in(key_list[26], 71), 0)
    outer_moment = scatter_about(key_list[13], (3 + CODES // D, D), (1.25 / PARAMS ** 0.5), 0.0029296875, (), jnp.float32)
    outer_second = jnp.clip(jnp.exp(jax.random.uniform(key_list[14], (3 + CODES // D, D), jnp.float32, math.log(2.2968360546826716e-09), math.log(9.187344218730686e-09))), 2.2968360546826716e-09, 9.187344218730686e-09)
    attn_proj = scatter_about(key_list[15], (LAYERS, 4, D, D), D ** -0.5, 0.25, ((2, 8),), jnp.float32)
    attn_momentum = scatter_about(key_list[16], (LAYERS, 4, D, D), (0.25 / PARAMS ** 0.5), 0.00061035156, ((2, 8),), jnp.float32)
    ff_up = scatter_about(key_list[17], (LAYERS, D, FF), D ** -0.5, 0.25, ((1, 8),), jnp.float32)
    up_momentum = scatter_about(key_list[18], (LAYERS, D, FF), (0.25 / PARAMS ** 0.5), 0.00061035156, ((1, 8),), jnp.float32)
    ff_down = scatter_about(key_list[19], (LAYERS, FF, D), FF ** -0.5, 0.125, ((1, 8),), jnp.float32)
    down_momentum = scatter_about(key_list[20], (LAYERS, FF, D), (0.25 / PARAMS ** 0.5), 0.00061035156, ((1, 8),), jnp.float32)
    in_copy = scatter_about(key_list[21], (FRAME_DIM, D), FRAME_DIM ** -0.5, 0.625)
    out_copy = scatter_about(key_list[22], (D, CODES), D ** -0.5, 0.25)
    attn_copy = scatter_about(key_list[23], (LAYERS, 4, D, D), D ** -0.5, 0.25)
    up_copy = scatter_about(key_list[24], (LAYERS, D, FF), D ** -0.5, 0.25)
    down_copy = scatter_about(key_list[25], (LAYERS, FF, D), FF ** -0.5, 0.125)
    return {"frames": frames, "speech_mask": speech_mask, "targets": targets, "in_proj": in_proj, "in_moment": in_moment, "in_second": in_second, "out_proj": out_proj, "out_moment": out_moment, "out_second": out_second, "layer_vectors": layer_vectors, "vectors_moment": vectors_moment, "vectors_second": vectors_second, "outer_vectors": outer_vectors, "outer_moment": outer_moment, "outer_second": outer_second, "attn_proj": attn_proj, "attn_momentum": attn_momentum, "ff_up": ff_up, "up_momentum": up_momentum, "ff_down": ff_down, "down_momentum": down_momentum, "in_copy": in_copy, "out_copy": out_copy, "attn_copy": attn_copy, "up_copy": up_copy, "down_copy": down_copy}


@jax.custom_vjp
def low(v):
    return lax.optimization_barrier(v.astype(jnp.bfloat16)).astype(jnp.float32)

@jax.custom_vjp
def low_back(v):
    return v

def low_keep(v):
    return (low(v), None)

def low_pass(kept, grad):
    return (grad,)

def back_keep(v):
    return (v, None)

def back_low(kept, grad):
    return (low(grad),)
low.defvjp(low_keep, low_pass)
low_back.defvjp(back_keep, back_low)
HIGHEST = lax.Precision.HIGHEST

def matmul(left, right):
    return jnp.matmul(left, right, precision=HIGHEST)

def layer_norm(values, gain, shift):
    centred = values - lax.optimization_barrier(jnp.mean(values, -1, keepdims=True))
    spread = lax.optimization_barrier(jnp.mean(centred * centred, -1, keepdims=True))
    return centred * lax.rsqrt(spread + 1e-05) * gain + shift

def attention_layer(hidden, memory, has_memory, attn, upper, lower, vectors):
    length, width = hidden.shape
    heads = width // HEAD_DIM
    normed = low(layer_norm(hidden, vectors[0], vectors[1]))
    memory_normed = low(layer_norm(memory, vectors[0], vectors[1]))
    keyin = jnp.concatenate([memory_normed, normed], 0)
    queries = low(low_back(matmul(normed, attn[0]) + vectors[4])).reshape(length, heads, HEAD_DIM)
    keys_all = low(low_back(matmul(keyin, attn[1]))).reshape(2 * length, heads, HEAD_DIM)
    values = low(low_back(matmul(keyin, attn[2]) + vectors[5])).reshape(2 * length, heads, HEAD_DIM)
    scores = low_back(jnp.einsum('qhd,khd->hqk', queries, keys_all, precision=HIGHEST) * HEAD_DIM ** (-0.5))
    query_pos = jnp.arange(length)[:, None]
    key_pos = jnp.arange(2 * length)[None, :]
    allowed = jnp.where(key_pos < length, has_memory, key_pos - length <= query_pos)
    scores = jnp.where(allowed[None], scores, -1e+30)
    weights = low(jax.nn.softmax(scores, -1))
    mixed = jnp.einsum('hqk,khd->qhd', weights, values, precision=HIGHEST).reshape(length, width)
    mixed = low(low_back(mixed))
    after_attn = hidden + low_back(matmul(mixed, attn[3]) + vectors[6])
    normed_two = low(layer_norm(after_attn, vectors[2], vectors[3]))
    inner = low_back(matmul(normed_two, upper) + vectors[8:].reshape(-1))
    active = low(jax.nn.gelu(inner))
    return after_attn + low_back(matmul(active, lower) + vectors[7])

def segment(params, frames, targets, weighting, memories, has_memory):
    in_weight, out_weight, layer_vectors, outer_vectors, attn, upper, lower = params
    hidden = matmul(frames, in_weight) + outer_vectors[0]
    inputs = []
    for depth in range(LAYERS):
        inputs.append(hidden)
        hidden = attention_layer(hidden, memories[depth], has_memory, attn[depth], upper[depth], lower[depth], layer_vectors[depth])
    normed = low(layer_norm(hidden, outer_vectors[1], outer_vectors[2]))
    logits = low_back(matmul(normed, out_weight) + outer_vectors[3:].reshape(-1))
    log_probs = jax.nn.log_softmax(logits, -1)
    picked = jnp.take_along_axis(log_probs, targets[:, None], 1)[:, 0]
    return (-jnp.sum(picked * weighting), jnp.stack(inputs))

def adamw(weight, moment, second, grad, rate, decay):
    moment = 0.5 * moment + 0.5 * grad
    second = 0.99 * second + 0.01 * grad * grad
    fixed_moment = moment / (1.0 - 0.5 ** STEP)
    fixed_second = second / (1.0 - 0.99 ** STEP)
    weight = weight * (1.0 - rate * decay) - rate * fixed_moment / (jnp.sqrt(fixed_second) + 1e-08)
    return (weight, moment, second)

def orthogonal(matrix):
    flipped = matrix.shape[0] > matrix.shape[1]
    if flipped:
        matrix = matrix.T
    matrix = matrix / (jnp.sqrt(jnp.sum(matrix * matrix)) + 1e-07)
    for sweep in range(5):
        gram_matrix = matmul(matrix, matrix.T)
        poly_term = -4.775 * gram_matrix + 2.0315 * matmul(gram_matrix, gram_matrix)
        matrix = 3.4445 * matrix + matmul(poly_term, matrix)
    return matrix.T if flipped else matrix

def muon(weight, momentum, grad):
    momentum = 0.5 * momentum + grad
    flat_mom = momentum.reshape((-1,) + momentum.shape[-2:])
    update = jax.vmap(orthogonal)(flat_mom).reshape(momentum.shape)
    scale = max(1.0, weight.shape[-1] / weight.shape[-2]) ** 0.5
    return (weight * (1.0 - 0.3 * 0.01) - 0.3 * scale * update, momentum)

def reference(frames, speech_mask, targets, in_proj, in_moment, in_second, out_proj, out_moment, out_second, layer_vectors, vectors_moment, vectors_second, outer_vectors, outer_moment, outer_second, attn_proj, attn_momentum, ff_up, up_momentum, ff_down, down_momentum, in_copy, out_copy, attn_copy, up_copy, down_copy):
    params = (in_copy.astype(jnp.float32), out_copy.astype(jnp.float32), layer_vectors, outer_vectors, attn_copy.astype(jnp.float32), up_copy.astype(jnp.float32), down_copy.astype(jnp.float32))
    keep_float = speech_mask.astype(jnp.float32)
    inverse = 1.0 / lax.optimization_barrier(jnp.sum(keep_float, 1))
    streams = (frames.astype(jnp.float32).reshape(STREAMS, N_SEG, SEG_LEN, FRAME_DIM), targets.reshape(STREAMS, N_SEG, SEG_LEN), (keep_float * inverse[:, None]).reshape(STREAMS, N_SEG, SEG_LEN))

    def memories(stream):

        def advance(carry, item):
            held, index = carry
            unused, inputs = segment(params, item[0], item[1], item[2], held, index > 0)
            return ((low(inputs), index + 1), held)
        start = (jnp.zeros((LAYERS, SEG_LEN, D), jnp.float32), jnp.int32(0))
        unused, used = lax.scan(advance, start, stream)
        return used
    used = lax.map(memories, streams)

    def total(weights):

        def stream_loss(stream):

            def one_segment(item):
                part, unused = segment(weights, item[0], item[1], item[2], item[3], item[4] > 0)
                return part
            return jnp.sum(lax.map(jax.checkpoint(one_segment), stream + (jnp.arange(N_SEG),)))
        return jnp.sum(lax.map(stream_loss, streams + (used,)))
    loss_sum, pullback = jax.vjp(total, params)
    grads = pullback(jnp.ones_like(loss_sum) / STREAMS)[0]
    grad_norm = jnp.sqrt(sum((jnp.sum(grad * grad) for grad in grads)))
    clip = jnp.minimum(1.0, 0.25 / (grad_norm + 1e-06))
    grad_in, grad_out, grad_vectors, grad_outer, grad_attn, grad_up, grad_down = [grad * clip for grad in grads]
    in_new, in_moment_new, in_second_new = adamw(in_proj, in_moment, in_second, grad_in, 0.05, 0.01)
    out_new, out_moment_new, out_second_new = adamw(out_proj, out_moment, out_second, grad_out, 0.05, 0.01)
    vectors_new, vectors_moment_new, vectors_second_new = adamw(layer_vectors, vectors_moment, vectors_second, grad_vectors, 0.25, 0.0)
    outer_new, outer_moment_new, outer_second_new = adamw(outer_vectors, outer_moment, outer_second, grad_outer, 0.25, 0.0)
    attn_new, attn_momentum_new = muon(attn_proj, attn_momentum, grad_attn)
    up_new, up_momentum_new = muon(ff_up, up_momentum, grad_up)
    down_new, down_momentum_new = muon(ff_down, down_momentum, grad_down)
    return (loss_sum, grad_norm, in_new, in_moment_new, in_second_new, out_new, out_moment_new, out_second_new, vectors_new, vectors_moment_new, vectors_second_new, outer_new, outer_moment_new, outer_second_new, attn_new, attn_momentum_new, up_new, up_momentum_new, down_new, down_momentum_new, in_new.astype(jnp.bfloat16), out_new.astype(jnp.bfloat16), attn_new.astype(jnp.bfloat16), up_new.astype(jnp.bfloat16), down_new.astype(jnp.bfloat16))
```

```python
import functools
import math

import jax
import jax.numpy as jnp
from jax import lax
from jax.experimental import pallas as pl
from jax.experimental.pallas import tpu as pltpu
from jax.sharding import PartitionSpec as P

D = 512
HEAD_DIM = 64
HEADS = D // HEAD_DIM
FF = 2048
LAYERS = 2
STEP = 10
SEG = 512
HALF = 256
PAIR = 2 * HEAD_DIM
TILE = 512
VMEM_LIMIT = 56 * 1024 * 1024
GELU_SCALE = math.sqrt(2.0 / math.pi)

f32 = jnp.float32
bf16 = jnp.bfloat16


def dot_nn(left, right):
    return lax.dot_general(left, right, (((1,), (0,)), ((), ())), preferred_element_type=f32)


def dot_nt(left, right):
    return lax.dot_general(left, right, (((1,), (1,)), ((), ())), preferred_element_type=f32)


def dot_tn(left, right):
    return lax.dot_general(left, right, (((0,), (0,)), ((), ())), preferred_element_type=f32)


def normalised(values):
    centred = values - jnp.mean(values, -1, keepdims=True)
    scale = lax.rsqrt(jnp.mean(centred * centred, -1, keepdims=True) + 1e-05)
    return centred * scale, scale


def norm_back(grad, gain, unit, scale):
    part = grad * gain
    mean_part = jnp.mean(part, -1, keepdims=True)
    mean_unit = jnp.mean(part * unit, -1, keepdims=True)
    return scale * (part - mean_part - unit * mean_unit)


def column_sum(values):
    return jnp.sum(values, 0, keepdims=True)


def head_masks():
    lane = lax.broadcasted_iota(jnp.int32, (1, PAIR), 1)
    return (lane < HEAD_DIM).astype(bf16), (lane >= HEAD_DIM).astype(bf16)


def pair_lanes(pair):
    return pl.ds(pl.multiple_of(pair * PAIR, PAIR), PAIR)


def forward_kernel(
    bias_ref,
    x_ref,
    mem_ref,
    attn_ref,
    up_ref,
    down_ref,
    vec_ref,
    *refs,
):
    hid_ref, hid16_ref, keyin_ref, q_ref, k_ref, v_ref, lse_ref, mixed_ref, after_ref, act_s, lse_s = refs[-11:]
    x = x_ref[...]
    own_unit, _ = normalised(x)
    gain, shift = vec_ref[0:1, :], vec_ref[1:2, :]
    normed = (own_unit * gain + shift).astype(bf16)
    mem_unit, _ = normalised(mem_ref[...].astype(f32))
    mem_normed = (mem_unit * gain + shift).astype(bf16)
    keyin_ref[0:SEG, :] = mem_normed
    keyin_ref[SEG:, :] = normed
    q_ref[...] = (dot_nn(normed, attn_ref[0]) + vec_ref[4:5, :]).astype(bf16) * jnp.asarray(HEAD_DIM**-0.5, bf16)
    k_ref[0:SEG, :] = dot_nn(mem_normed, attn_ref[1]).astype(bf16)
    k_ref[SEG:, :] = dot_nn(normed, attn_ref[1]).astype(bf16)
    v_ref[0:SEG, :] = (dot_nn(mem_normed, attn_ref[2]) + vec_ref[5:6, :]).astype(bf16)
    v_ref[SEG:, :] = (dot_nn(normed, attn_ref[2]) + vec_ref[5:6, :]).astype(bf16)
    first, second = head_masks()
    memory_bias = bias_ref[0]
    lane = lax.broadcasted_iota(jnp.int32, (HALF, PAIR), 1)
    query_pos = lax.broadcasted_iota(jnp.int32, (2 * HALF, HALF), 0) % HALF
    key_pos = lax.broadcasted_iota(jnp.int32, (2 * HALF, HALF), 1)
    diagonal = key_pos <= query_pos
    lse_s[...] = jnp.zeros_like(lse_s)

    def pair_body(pair, carry):
        lanes = pair_lanes(pair)
        for block in range(2):
            rows = slice(block * HALF, (block + 1) * HALF)
            q_pair = q_ref[rows, lanes]
            q_both = jnp.concatenate([q_pair * first, q_pair * second], 0)
            spans = [(0, SEG, 0)]
            if block:
                spans.append((SEG, SEG + HALF, 1))
            spans.append((SEG + block * HALF, SEG + (block + 1) * HALF, 2))
            scores = []
            for low, high, kind in spans:
                part = dot_nt(q_both, k_ref[low:high, lanes])
                if kind == 0:
                    part = part + memory_bias
                if kind == 2:
                    part = jnp.where(diagonal, part, -1e30)
                scores.append(part)
            most = functools.reduce(jnp.maximum, [jnp.max(part, -1, keepdims=True) for part in scores])
            weights = [jnp.exp(part - most) for part in scores]
            total = functools.reduce(jnp.add, [jnp.sum(part, -1, keepdims=True) for part in weights])
            mixed = functools.reduce(
                jnp.add,
                [
                    dot_nn(part.astype(bf16), v_ref[low:high, lanes])
                    for part, (low, high, kind) in zip(weights, spans)
                ],
            )
            mixed = mixed / total
            mixed_ref[rows, lanes] = jnp.where(lane < HEAD_DIM, mixed[:HALF], mixed[HALF:]).astype(bf16)
            lse = most + jnp.log(total)
            kept = jnp.where(lane == 2 * pair, lse[:HALF], lse_s[rows, :])
            lse_s[rows, :] = jnp.where(lane == 2 * pair + 1, lse[HALF:], kept)
        return carry

    lax.fori_loop(0, HEADS // 2, pair_body, 0)
    lse_ref[...] = jnp.transpose(lse_s[...])[0:HEADS, :]
    after = x + (dot_nn(mixed_ref[...], attn_ref[3]) + vec_ref[6:7, :])
    after_ref[...] = after
    unit, _ = normalised(after)
    normed_two = (unit * vec_ref[2:3, :] + vec_ref[3:4, :]).astype(bf16)
    for tile in range(FF // TILE):
        columns = slice(tile * TILE, (tile + 1) * TILE)
        inner = dot_nn(normed_two, up_ref[:, columns]) + vec_ref[8 + tile : 9 + tile, :]
        act_s[:, columns] = (
            0.5 * inner * (1.0 + jnp.tanh(GELU_SCALE * (inner + 0.044715 * inner * inner * inner)))
        ).astype(bf16)
    hidden = after + (dot_nn(act_s[...], down_ref[...]) + vec_ref[7:8, :])
    hid_ref[...] = hidden
    hid16_ref[...] = hidden.astype(bf16)


SAVED = (
    ((SEG, D), f32),
    ((2 * SEG, D), bf16),
    ((SEG, D), bf16),
    ((2 * SEG, D), bf16),
    ((2 * SEG, D), bf16),
    ((HEADS, SEG), f32),
    ((SEG, D), bf16),
    ((SEG, D), f32),
)


def whole_spec(shape):
    return pl.BlockSpec(shape, lambda *_: (0,) * len(shape))


def stream_spec(shape, stream=None):
    zeros = (0,) * len(shape)
    if stream is None:
        return pl.BlockSpec((None,) + shape, lambda i: (i,) + zeros)
    return pl.BlockSpec((None,) + shape, lambda i: (stream,) + zeros)


def forward_layer(stream, streams, bias, hidden, memory, attn, upper, lower, vectors, earlier):
    saved_shapes = [jax.ShapeDtypeStruct((streams,) + shape, dtype) for shape, dtype in SAVED]
    saved_specs = [stream_spec(shape, stream) for shape, dtype in SAVED]
    out_shape = [saved_shapes[0], jax.ShapeDtypeStruct((SEG, D), bf16)] + saved_shapes[1:]
    out_specs = [saved_specs[0], whole_spec((SEG, D))] + saved_specs[1:]
    operands = [bias, hidden, memory, attn, upper, lower, vectors]
    in_specs = [
        pl.BlockSpec(memory_space=pltpu.SMEM),
        stream_spec((SEG, D), stream),
        whole_spec((SEG, D)),
        whole_spec(attn.shape),
        whole_spec(upper.shape),
        whole_spec(lower.shape),
        whole_spec(vectors.shape),
    ]
    aliases = {}
    if earlier is not None:
        for place, array in enumerate(earlier):
            aliases[len(operands)] = place if place == 0 else place + 1
            operands.append(array)
            in_specs.append(pl.BlockSpec(memory_space=pl.ANY))
    out = pl.pallas_call(
        forward_kernel,
        grid=(1,),
        out_shape=out_shape,
        in_specs=in_specs,
        out_specs=out_specs,
        scratch_shapes=[pltpu.VMEM((SEG, FF), bf16), pltpu.VMEM((SEG, PAIR), f32)],
        input_output_aliases=aliases,
        compiler_params=pltpu.CompilerParams(vmem_limit_bytes=VMEM_LIMIT),
        cost_estimate=pl.CostEstimate(flops=10**10, bytes_accessed=2 * 10**7, transcendentals=10**7),
        name="layer_forward",
    )(*operands)
    return [out[0]] + list(out[2:]), out[1]


def head_kernel(scale, x_ref, target_ref, weight_ref, out_ref, outer_ref, bias_ref, g_ref, dout_ref, douter_ref, loss_ref, acc_s):
    step = pl.program_id(0)

    @pl.when(step == 0)
    def _():
        acc_s[...] = jnp.zeros_like(acc_s)
        douter_ref[...] = jnp.zeros_like(douter_ref)
        loss_ref[...] = jnp.zeros_like(loss_ref)

    unit, rscale = normalised(x_ref[...])
    gain = outer_ref[1:2, :]
    normed = (unit * gain + outer_ref[2:3, :]).astype(bf16)
    logits = dot_nn(normed, out_ref[...]) + bias_ref[...]
    most = jnp.max(logits, -1, keepdims=True)
    powers = jnp.exp(logits - most)
    total = jnp.sum(powers, -1, keepdims=True)
    chosen = lax.broadcasted_iota(jnp.int32, logits.shape, 1) == target_ref[...]
    picked = jnp.sum(jnp.where(chosen, logits, 0.0), -1, keepdims=True)
    weight = weight_ref[...]
    loss_ref[...] += jnp.sum(weight * (most + jnp.log(total) - picked), 0, keepdims=True)
    spread = weight * scale
    dlogits = (powers * (spread / total) - jnp.where(chosen, spread, 0.0)).astype(bf16)
    acc_s[...] += dot_tn(normed, dlogits)
    bias_grad = column_sum(dlogits.astype(f32))
    dnormed = dot_nt(dlogits, out_ref[...])
    g_ref[...] = norm_back(dnormed, gain, unit, rscale)
    douter_ref[1:2, :] += column_sum(dnormed * unit)
    douter_ref[2:3, :] += column_sum(dnormed)
    douter_ref[3:4, :] += bias_grad[:, :D]
    douter_ref[4:5, :] += bias_grad[:, D:]

    @pl.when(step == pl.num_programs(0) - 1)
    def _():
        dout_ref[...] = acc_s[...]


def head(hidden, targets, weighting, out_weight, outer_vectors, scale):
    streams = hidden.shape[0]
    codes = out_weight.shape[1]
    bias = outer_vectors[3:].reshape(1, codes)
    return pl.pallas_call(
        functools.partial(head_kernel, scale),
        grid=(streams,),
        out_shape=[
            jax.ShapeDtypeStruct((streams, SEG, D), f32),
            jax.ShapeDtypeStruct((D, codes), f32),
            jax.ShapeDtypeStruct((8, D), f32),
            jax.ShapeDtypeStruct((1, 1), f32),
        ],
        in_specs=[
            stream_spec((SEG, D)),
            stream_spec((SEG, 1)),
            stream_spec((SEG, 1)),
            whole_spec((D, codes)),
            whole_spec(outer_vectors.shape),
            whole_spec((1, codes)),
        ],
        out_specs=[stream_spec((SEG, D)), whole_spec((D, codes)), whole_spec((8, D)), whole_spec((1, 1))],
        scratch_shapes=[pltpu.VMEM((D, codes), f32)],
        compiler_params=pltpu.CompilerParams(vmem_limit_bytes=VMEM_LIMIT),
        cost_estimate=pl.CostEstimate(flops=33 * 10**8, bytes_accessed=10**7, transcendentals=10**6),
        name="head",
    )(hidden, targets[..., None], weighting[..., None], out_weight, outer_vectors, bias)


def feed_back_kernel(g_ref, after_ref, up_ref, down_ref, vec_ref, dafter_ref, dup_ref, ddown_ref, dvec_ref, up_s, down_s, act_s, inner_s):
    step = pl.program_id(0)

    @pl.when(step == 0)
    def _():
        up_s[...] = jnp.zeros_like(up_s)
        down_s[...] = jnp.zeros_like(down_s)
        dvec_ref[...] = jnp.zeros_like(dvec_ref)

    grad = g_ref[...]
    branch = grad.astype(bf16)
    dvec_ref[2:3, :] += column_sum(branch.astype(f32))
    unit, scale = normalised(after_ref[...])
    gain = vec_ref[2:3, :]
    normed = (unit * gain + vec_ref[3:4, :]).astype(bf16)
    for tile in range(FF // TILE):
        columns = slice(tile * TILE, (tile + 1) * TILE)
        inner = dot_nn(normed, up_ref[:, columns]) + vec_ref[8 + tile : 9 + tile, :]
        dact = dot_nt(branch, down_ref[columns, :])
        square = inner * inner
        bent = jnp.tanh(GELU_SCALE * (inner + 0.044715 * square * inner))
        half = 0.5 * (1.0 + bent)
        act_s[:, columns] = (inner * half).astype(bf16)
        slope = half + (0.5 * GELU_SCALE) * inner * (1.0 - bent * bent) * (1.0 + 0.134145 * square)
        dinner = (dact * slope).astype(bf16)
        inner_s[:, columns] = dinner
        dvec_ref[4 + tile : 5 + tile, :] += column_sum(dinner.astype(f32))
    dnormed = dot_nt(inner_s[...], up_ref[...])
    dvec_ref[0:1, :] += column_sum(dnormed * unit)
    dvec_ref[1:2, :] += column_sum(dnormed)
    dafter_ref[...] = grad + norm_back(dnormed, gain, unit, scale)
    normed_t = jnp.transpose(normed)
    branch_t = jnp.transpose(branch)
    up_s[...] += dot_nn(normed_t, inner_s[...])
    down_s[...] += dot_nn(branch_t, act_s[...])

    @pl.when(step == pl.num_programs(0) - 1)
    def _():
        dup_ref[...] = up_s[...].astype(bf16)
        ddown_ref[...] = jnp.transpose(down_s[...].astype(bf16))


def feed_back(grad, after, upper, lower, vectors):
    streams = grad.shape[0]
    return pl.pallas_call(
        feed_back_kernel,
        grid=(streams,),
        out_shape=[
            jax.ShapeDtypeStruct((streams, SEG, D), f32),
            jax.ShapeDtypeStruct((D, FF), bf16),
            jax.ShapeDtypeStruct((FF, D), bf16),
            jax.ShapeDtypeStruct((8, D), f32),
        ],
        in_specs=[
            stream_spec((SEG, D)),
            stream_spec((SEG, D)),
            whole_spec(upper.shape),
            whole_spec(lower.shape),
            whole_spec(vectors.shape),
        ],
        out_specs=[stream_spec((SEG, D)), whole_spec((D, FF)), whole_spec((FF, D)), whole_spec((8, D))],
        scratch_shapes=[
            pltpu.VMEM((D, FF), f32),
            pltpu.VMEM((D, FF), f32),
            pltpu.VMEM((SEG, FF), bf16),
            pltpu.VMEM((SEG, FF), bf16),
        ],
        compiler_params=pltpu.CompilerParams(vmem_limit_bytes=VMEM_LIMIT),
        cost_estimate=pl.CostEstimate(flops=11 * 10**9, bytes_accessed=2 * 10**7, transcendentals=2 * 10**6),
        name="feed_back",
    )(grad, after, upper, lower, vectors)


def attend_back_kernel(
    bias_ref,
    dafter_ref,
    x_ref,
    mem_ref,
    keyin_ref,
    q_ref,
    k_ref,
    v_ref,
    lse_ref,
    mixed_ref,
    attn_ref,
    vec_ref,
    dx_ref,
    dattn_ref,
    dvec_ref,
    attn_s,
    dmixed_s,
    dq_s,
    dk_s,
    dv_s,
    ds_s,
    delta_s,
):
    step = pl.program_id(0)

    @pl.when(step == 0)
    def _():
        attn_s[...] = jnp.zeros_like(attn_s)
        dvec_ref[...] = jnp.zeros_like(dvec_ref)

    dafter = dafter_ref[...]
    branch = dafter.astype(bf16)
    dvec_ref[4:5, :] += column_sum(branch.astype(f32))
    dmixed = dot_nt(branch, attn_ref[3]).astype(bf16)
    dmixed_s[...] = dmixed
    attn_s[3] += dot_nn(jnp.transpose(mixed_ref[...]), branch)
    product = dmixed.astype(f32) * mixed_ref[...].astype(f32)
    high = product.astype(bf16)
    rest = (product - high.astype(f32)).astype(bf16)
    owner = lax.broadcasted_iota(jnp.int32, (HEADS, D), 1) // HEAD_DIM
    pick = (owner == lax.broadcasted_iota(jnp.int32, (HEADS, D), 0)).astype(bf16)
    delta_s[...] = dot_nt(pick, high) + dot_nt(pick, rest)
    first, second = head_masks()
    memory_bias = bias_ref[0]
    key_pos = lax.broadcasted_iota(jnp.int32, (HALF, 2 * HALF), 0)
    query_pos = lax.broadcasted_iota(jnp.int32, (HALF, 2 * HALF), 1) % HALF
    diagonal = key_pos <= query_pos
    head_row = lax.broadcasted_iota(jnp.int32, (PAIR, HALF), 0)

    def pair_body(pair, carry):
        lanes = pair_lanes(pair)
        q_pair, do_pair = q_ref[:, lanes], dmixed_s[:, lanes]

        def spread(value):
            return jnp.concatenate(
                [value[:HALF] * first, value[:HALF] * second, value[HALF:] * first, value[HALF:] * second], 0
            )

        q_all, do_all = spread(q_pair), spread(do_pair)

        def rows_of(ref):
            one, two = ref[pl.ds(2 * pair, 1), :], ref[pl.ds(2 * pair + 1, 1), :]
            return jnp.concatenate([one[:, :HALF], two[:, :HALF], one[:, HALF:], two[:, HALF:]], 1)

        lse_all, delta_all = rows_of(lse_ref), rows_of(delta_s)
        for block in range(4):
            keys = slice(block * HALF, (block + 1) * HALF)
            start = 2 * HALF if block == 3 else 0
            scores = dot_nt(k_ref[keys, lanes], q_all[start:])
            if block < 2:
                scores = scores + memory_bias
            weights = jnp.exp(scores - lse_all[:, start:])
            if block == 2:
                weights = jnp.concatenate(
                    [jnp.where(diagonal, weights[:, : 2 * HALF], 0.0), weights[:, 2 * HALF :]], 1
                )
            if block == 3:
                weights = jnp.where(diagonal, weights, 0.0)
            dweights = dot_nt(v_ref[keys, lanes], do_all[start:])
            dscores = (weights * (dweights - delta_all[:, start:])).astype(bf16)
            dv_s[keys, lanes] = dot_nn(weights.astype(bf16), do_all[start:]).astype(bf16)
            dk_s[keys, lanes] = dot_nn(dscores, q_all[start:]).astype(bf16)
            ds_s[keys, start:] = dscores
        k_t = jnp.transpose(k_ref[:, lanes])
        for block in range(2):
            seen = SEG + (block + 1) * HALF
            grads = dot_nn(k_t[:, :seen], ds_s[:seen, block * 2 * HALF : (block + 1) * 2 * HALF])
            grads = jnp.where(head_row < HEAD_DIM, grads[:, :HALF], grads[:, HALF:])
            dq_s[block * HALF : (block + 1) * HALF, lanes] = (
                jnp.transpose(grads) * (HEAD_DIM**-0.5)
            ).astype(bf16)
        return carry

    lax.fori_loop(0, HEADS // 2, pair_body, 0)
    dq, dk, dv = dq_s[...], dk_s[...], dv_s[...]
    keyin_t = jnp.transpose(keyin_ref[...])
    attn_s[0] += dot_nn(keyin_t[:, SEG:], dq)
    attn_s[1] += dot_nn(keyin_t, dk)
    attn_s[2] += dot_nn(keyin_t, dv)
    dvec_ref[2:3, :] += column_sum(dq.astype(f32))
    dvec_ref[3:4, :] += column_sum(dv.astype(f32))
    dkeyin = dot_nt(dk, attn_ref[1]) + dot_nt(dv, attn_ref[2])
    dmem = dkeyin[:SEG]
    down = dkeyin[SEG:] + dot_nt(dq, attn_ref[0])
    gain = vec_ref[0:1, :]
    unit, scale = normalised(x_ref[...])
    mem_unit, _ = normalised(mem_ref[...].astype(f32))
    dvec_ref[0:1, :] += column_sum(down * unit + dmem * mem_unit)
    dvec_ref[1:2, :] += column_sum(down + dmem)
    dx_ref[...] = dafter + norm_back(down, gain, unit, scale)

    @pl.when(step == pl.num_programs(0) - 1)
    def _():
        dattn_ref[...] = attn_s[...].astype(bf16)


def attend_back(bias, dafter, x, memory, saved, attn, vectors):
    streams = dafter.shape[0]
    keyin, q, k, v, lse, mixed = saved
    return pl.pallas_call(
        attend_back_kernel,
        grid=(streams,),
        out_shape=[
            jax.ShapeDtypeStruct((streams, SEG, D), f32),
            jax.ShapeDtypeStruct((4, D, D), bf16),
            jax.ShapeDtypeStruct((8, D), f32),
        ],
        in_specs=[
            pl.BlockSpec(memory_space=pltpu.SMEM),
            stream_spec((SEG, D)),
            stream_spec((SEG, D)),
            stream_spec((SEG, D)),
            stream_spec((2 * SEG, D)),
            stream_spec((SEG, D)),
            stream_spec((2 * SEG, D)),
            stream_spec((2 * SEG, D)),
            stream_spec((HEADS, SEG)),
            stream_spec((SEG, D)),
            whole_spec(attn.shape),
            whole_spec(vectors.shape),
        ],
        out_specs=[stream_spec((SEG, D)), whole_spec((4, D, D)), whole_spec((8, D))],
        scratch_shapes=[
            pltpu.VMEM((4, D, D), f32),
            pltpu.VMEM((SEG, D), bf16),
            pltpu.VMEM((SEG, D), bf16),
            pltpu.VMEM((2 * SEG, D), bf16),
            pltpu.VMEM((2 * SEG, D), bf16),
            pltpu.VMEM((2 * SEG, 2 * SEG), bf16),
            pltpu.VMEM((HEADS, SEG), f32),
        ],
        compiler_params=pltpu.CompilerParams(vmem_limit_bytes=VMEM_LIMIT),
        cost_estimate=pl.CostEstimate(flops=3 * 10**10, bytes_accessed=2 * 10**7, transcendentals=10**7),
        name="attend_back",
    )(bias, dafter, x, memory, keyin, q, k, v, lse, mixed, attn, vectors)


HIGH = lax.Precision.HIGH


def from_behind(value, axis, steps):
    count = lax.axis_size(axis)
    leading, last = (max(0, -steps), min(count, count - steps))
    return lax.ppermute(value, axis, [(source, source + steps) for source in range(leading, last)])


def shortened(value):

    def short(part):
        return part.astype(jnp.bfloat16) if part.dtype == jnp.float32 else part

    return jax.tree.map(short, value)


def adamw(weight, moment, second, grad, rate, decay):
    moment = 0.5 * moment + 0.5 * grad
    second = 0.99 * second + 0.01 * grad * grad
    fixed_moment = moment / (1.0 - 0.5**STEP)
    fixed_second = second / (1.0 - 0.99**STEP)
    weight = weight * (1.0 - rate * decay) - rate * fixed_moment / (jnp.sqrt(fixed_second) + 1e-08)
    return (weight, moment, second)


def orthogonal(matrix):
    flipped = matrix.shape[0] > matrix.shape[1]
    if flipped:
        matrix = matrix.T
    matrix = matrix / (jnp.sqrt(jnp.sum(matrix * matrix)) + 1e-07)
    for sweep in range(5):
        gram_matrix = jnp.matmul(matrix, matrix.T, precision=HIGH)
        poly_term = -4.775 * gram_matrix + 2.0315 * jnp.matmul(
            gram_matrix, gram_matrix, precision=HIGH
        )
        matrix = 3.4445 * matrix + jnp.matmul(poly_term, matrix, precision=HIGH)
    return matrix.T if flipped else matrix


def owner_layout(stack, offset, owner_count):
    total_count = stack.shape[0]
    slot_count = -(-total_count // owner_count)
    filler = jnp.zeros((slot_count * owner_count - total_count,) + stack.shape[1:], stack.dtype)
    rolled = jnp.roll(jnp.concatenate([stack, filler], 0), offset, 0)
    return rolled.reshape((slot_count, owner_count) + stack.shape[1:])


def to_owner(stack, offset, owner_count, owner):
    return lax.dynamic_index_in_dim(
        owner_layout(stack, offset, owner_count), owner, 1, keepdims=False
    )


def from_owner(gathered, offset, total_count):
    owner_count, slot_count = (gathered.shape[0], gathered.shape[1])
    flat = jnp.swapaxes(gathered, 0, 1).reshape((slot_count * owner_count,) + gathered.shape[2:])
    return jnp.roll(flat, -offset, 0)[:total_count]


def own_rows(whole, row_count):
    return lax.dynamic_slice_in_dim(whole, lax.axis_index("seg") * row_count, row_count, 1)


def local(
    frames,
    speech_mask,
    targets,
    in_proj,
    in_moment,
    in_second,
    out_proj,
    out_moment,
    out_second,
    layer_vectors,
    vectors_moment,
    vectors_second,
    outer_vectors,
    outer_moment,
    outer_second,
    attn_proj,
    attn_momentum,
    ff_up,
    up_momentum,
    ff_down,
    down_momentum,
    in_copy,
    out_copy,
    attn_copy,
    up_copy,
    down_copy,
):
    segment = lax.axis_index("seg")
    stream_total = frames.shape[0] * lax.axis_size("dp")
    streams = frames.shape[0]
    behind = from_behind(frames, "seg", 1)
    local_counts = jnp.sum(speech_mask, 1)
    counts = lax.psum(local_counts, "seg")
    weighting = speech_mask.astype(f32) / counts.astype(f32)[:, None]
    bias = jnp.where(segment > 0, 0.0, -1e30).astype(f32)[None]
    hidden = jnp.dot(frames, in_copy, preferred_element_type=f32) + outer_vectors[0]
    memory = (jnp.dot(behind, in_copy, preferred_element_type=f32) + outer_vectors[0]).astype(bf16)
    memory = [memory[stream] for stream in range(streams)]
    kept = []
    for depth in range(LAYERS):
        saved, passed = None, []
        for stream in range(streams):
            saved, short = forward_layer(
                stream,
                streams,
                bias,
                hidden,
                memory[stream],
                attn_copy[depth],
                up_copy[depth],
                down_copy[depth],
                layer_vectors[depth],
                saved,
            )
            if depth + 1 < LAYERS:
                passed.append(from_behind(short, "seg", 1))
        kept.append((hidden, jnp.stack(memory), saved))
        hidden = saved[0]
        memory = passed
    grad_hidden, grad_out, head_outer, loss_here = head(
        hidden, targets, weighting, out_copy, outer_vectors, 1.0 / stream_total
    )
    loss_here = loss_here[0, 0]
    attn_grads, up_grads, down_grads, vector_grads = ([], [], [], [])
    for depth in reversed(range(LAYERS)):
        entering, held, saved = kept[depth]
        dafter, grad_up, grad_down, feed_vec = feed_back(
            grad_hidden, saved[7], up_copy[depth], down_copy[depth], layer_vectors[depth]
        )
        grad_hidden, grad_attn, attn_vec = attend_back(
            bias, dafter, entering, held, saved[1:7], attn_copy[depth], layer_vectors[depth]
        )
        attn_grads.insert(0, grad_attn)
        up_grads.insert(0, grad_up)
        down_grads.insert(0, grad_down)
        vector_grads.insert(
            0,
            jnp.concatenate([attn_vec[0:2], feed_vec[0:2], attn_vec[2:5], feed_vec[2:3], feed_vec[4:8]], 0),
        )
    rows = grad_hidden.reshape(streams * SEG, D)
    rows_high = rows.astype(bf16)
    rows_rest = (rows - rows_high.astype(f32)).astype(bf16)
    frame_rows = frames.reshape(streams * SEG, frames.shape[2])
    grad_in = dot_tn(frame_rows, rows_high) + dot_tn(frame_rows, rows_rest)
    grad_outer = jnp.concatenate([jnp.sum(rows, 0, keepdims=True), head_outer[1:5]], 0)
    grad_vectors = jnp.stack(vector_grads)
    grad_in, grad_out, grad_vectors, grad_outer, loss_sum = lax.psum(
        (grad_in, grad_out, grad_vectors, grad_outer, loss_here), ("seg", "dp")
    )
    attn_local = jnp.stack(attn_grads).reshape(4 * LAYERS, D, D)
    up_local = jnp.stack(up_grads)
    down_local = jnp.stack(down_grads)
    offsets = (0, 4 * LAYERS, 5 * LAYERS)
    owner = lax.axis_index("dp")
    owner_count = lax.axis_size("dp")
    attn_sum, up_sum, down_sum = (
        lax.psum_scatter(
            attn_local.astype(jnp.bfloat16), "seg", scatter_dimension=1, tiled=True
        ).astype(jnp.float32),
        lax.psum_scatter(
            up_local.astype(jnp.bfloat16), "seg", scatter_dimension=1, tiled=True
        ).astype(jnp.float32),
        lax.psum_scatter(
            down_local.astype(jnp.bfloat16), "seg", scatter_dimension=1, tiled=True
        ).astype(jnp.float32),
    )
    attn_sum, up_sum, down_sum = lax.psum((attn_sum, up_sum, down_sum), "dp")
    shard_squares = (
        jnp.sum(attn_sum * attn_sum) + jnp.sum(up_sum * up_sum) + jnp.sum(down_sum * down_sum)
    )
    matrix_squares = lax.psum(shard_squares, "seg")
    small_squares = (
        jnp.sum(grad_in * grad_in)
        + jnp.sum(grad_out * grad_out)
        + jnp.sum(grad_vectors * grad_vectors)
        + jnp.sum(grad_outer * grad_outer)
    )
    grad_norm = jnp.sqrt(matrix_squares + small_squares)
    clip = jnp.minimum(1.0, 0.25 / (grad_norm + 1e-06))
    in_new, in_moment_new, in_second_new = adamw(
        in_proj, in_moment, in_second, grad_in * clip, 0.05, 0.01
    )
    out_new, out_moment_new, out_second_new = adamw(
        out_proj, out_moment, out_second, grad_out * clip, 0.05, 0.01
    )
    vectors_new, vectors_moment_new, vectors_second_new = adamw(
        layer_vectors, vectors_moment, vectors_second, grad_vectors * clip, 0.25, 0.0
    )
    outer_new, outer_moment_new, outer_second_new = adamw(
        outer_vectors, outer_moment, outer_second, grad_outer * clip, 0.25, 0.0
    )
    block_rows = attn_momentum.shape[2]
    attn_old = attn_momentum.reshape(4 * LAYERS, block_rows, D)
    row_counts = (block_rows, up_momentum.shape[1], down_momentum.shape[1])
    attn_mom = 0.5 * attn_old + clip * attn_sum
    up_mom = 0.5 * up_momentum + clip * up_sum
    down_mom = 0.5 * down_momentum + clip * down_sum
    owned_attn = to_owner(attn_mom, offsets[0], owner_count, owner)
    owned_up = to_owner(up_mom, offsets[1], owner_count, owner)
    owned_down = to_owner(down_mom, offsets[2], owner_count, owner)
    whole_attn, whole_up, whole_down = (
        lax.all_gather(owned_attn, "seg", axis=1, tiled=True),
        lax.all_gather(owned_up, "seg", axis=1, tiled=True),
        lax.all_gather(owned_down, "seg", axis=1, tiled=True),
    )
    part_attn = own_rows(jax.vmap(orthogonal)(whole_attn), row_counts[0])
    part_up = own_rows(jax.vmap(orthogonal)(whole_up), row_counts[1])
    part_down = own_rows(jax.vmap(orthogonal)(whole_down), row_counts[2])
    back_attn, back_up, back_down = (
        lax.all_gather(shortened(part_attn[None]), "dp", axis=0, tiled=True),
        lax.all_gather(shortened(part_up[None]), "dp", axis=0, tiled=True),
        lax.all_gather(shortened(part_down[None]), "dp", axis=0, tiled=True),
    )
    attn_update = from_owner(back_attn, offsets[0], 4 * LAYERS)
    up_update = from_owner(back_up, offsets[1], LAYERS)
    down_update = from_owner(back_down, offsets[2], LAYERS)
    attn_new = attn_proj * (1.0 - 0.3 * 0.01) - 0.3 * attn_update.reshape(attn_proj.shape)
    up_new = ff_up * (1.0 - 0.3 * 0.01) - 0.3 * max(1.0, FF / D) ** 0.5 * up_update
    down_new = ff_down * (1.0 - 0.3 * 0.01) - 0.3 * max(1.0, D / FF) ** 0.5 * down_update
    return (
        loss_sum,
        grad_norm,
        in_new,
        in_moment_new,
        in_second_new,
        out_new,
        out_moment_new,
        out_second_new,
        vectors_new,
        vectors_moment_new,
        vectors_second_new,
        outer_new,
        outer_moment_new,
        outer_second_new,
        attn_new,
        attn_mom.reshape(attn_proj.shape),
        up_new,
        up_mom,
        down_new,
        down_mom,
        in_new.astype(jnp.bfloat16),
        out_new.astype(jnp.bfloat16),
        attn_new.astype(jnp.bfloat16),
        up_new.astype(jnp.bfloat16),
        down_new.astype(jnp.bfloat16),
    )


def solution(mesh):
    return jax.shard_map(
        local,
        mesh=mesh,
        in_specs=(
            P("dp", "seg", None),
            P("dp", "seg"),
            P("dp", "seg"),
            P(),
            P(),
            P(),
            P(),
            P(),
            P(),
            P(),
            P(),
            P(),
            P(),
            P(),
            P(),
            P(None, None, "seg", None),
            P(None, None, "seg", None),
            P(None, "seg", None),
            P(None, "seg", None),
            P(None, "seg", None),
            P(None, "seg", None),
            P(),
            P(),
            P(),
            P(),
            P(),
        ),
        out_specs=(
            P(),
            P(),
            P(),
            P(),
            P(),
            P(),
            P(),
            P(),
            P(),
            P(),
            P(),
            P(),
            P(),
            P(),
            P(None, None, "seg", None),
            P(None, None, "seg", None),
            P(None, "seg", None),
            P(None, "seg", None),
            P(None, "seg", None),
            P(None, "seg", None),
            P(),
            P(),
            P(None, None, "seg", None),
            P(None, "seg", None),
            P(None, "seg", None),
        ),
        check_vma=False,
    )
```

```python
import functools
import math

import jax
import jax.numpy as jnp
from jax import lax
from jax.experimental import pallas as pl
from jax.experimental.pallas import tpu as pltpu
from jax.sharding import PartitionSpec as P

D = 512
HEAD_DIM = 64
HEADS = D // HEAD_DIM
FF = 2048
LAYERS = 2
STEP = 10
SEG = 512
HALF = 256
PAIR = 2 * HEAD_DIM
TILE = 512
VMEM_LIMIT = 56 * 1024 * 1024
GELU_SCALE = math.sqrt(2.0 / math.pi)

f32 = jnp.float32
bf16 = jnp.bfloat16


def dot_nn(left, right):
    return lax.dot_general(left, right, (((1,), (0,)), ((), ())), preferred_element_type=f32)


def dot_nt(left, right):
    return lax.dot_general(left, right, (((1,), (1,)), ((), ())), preferred_element_type=f32)


def dot_tn(left, right):
    return lax.dot_general(left, right, (((0,), (0,)), ((), ())), preferred_element_type=f32)


def normalised(values):
    centred = values - jnp.mean(values, -1, keepdims=True)
    scale = lax.rsqrt(jnp.mean(centred * centred, -1, keepdims=True) + 1e-05)
    return centred * scale, scale


def norm_back(grad, gain, unit, scale):
    part = grad * gain
    mean_part = jnp.mean(part, -1, keepdims=True)
    mean_unit = jnp.mean(part * unit, -1, keepdims=True)
    return scale * (part - mean_part - unit * mean_unit)


def column_sum(values):
    return jnp.sum(values, 0, keepdims=True)


def head_masks():
    lane = lax.broadcasted_iota(jnp.int32, (1, PAIR), 1)
    return (lane < HEAD_DIM).astype(bf16), (lane >= HEAD_DIM).astype(bf16)


def pair_lanes(pair):
    return pl.ds(pl.multiple_of(pair * PAIR, PAIR), PAIR)


def forward_kernel(
    bias_ref,
    x_ref,
    mem_ref,
    attn_ref,
    up_ref,
    down_ref,
    vec_ref,
    *refs,
):
    hid_ref, hid16_ref, keyin_ref, q_ref, k_ref, v_ref, lse_ref, mixed_ref, after_ref, act_s, lse_s = refs[-11:]
    x = x_ref[...]
    own_unit, _ = normalised(x)
    gain, shift = vec_ref[0:1, :], vec_ref[1:2, :]
    normed = (own_unit * gain + shift).astype(bf16)
    mem_unit, _ = normalised(mem_ref[...].astype(f32))
    mem_normed = (mem_unit * gain + shift).astype(bf16)
    keyin_ref[0:SEG, :] = mem_normed
    keyin_ref[SEG:, :] = normed
    q_ref[...] = (dot_nn(normed, attn_ref[0]) + vec_ref[4:5, :]).astype(bf16) * jnp.asarray(HEAD_DIM**-0.5, bf16)
    k_ref[0:SEG, :] = dot_nn(mem_normed, attn_ref[1]).astype(bf16)
    k_ref[SEG:, :] = dot_nn(normed, attn_ref[1]).astype(bf16)
    v_ref[0:SEG, :] = (dot_nn(mem_normed, attn_ref[2]) + vec_ref[5:6, :]).astype(bf16)
    v_ref[SEG:, :] = (dot_nn(normed, attn_ref[2]) + vec_ref[5:6, :]).astype(bf16)
    first, second = head_masks()
    memory_bias = bias_ref[0]
    lane = lax.broadcasted_iota(jnp.int32, (HALF, PAIR), 1)
    query_pos = lax.broadcasted_iota(jnp.int32, (2 * HALF, HALF), 0) % HALF
    key_pos = lax.broadcasted_iota(jnp.int32, (2 * HALF, HALF), 1)
    diagonal = key_pos <= query_pos
    lse_s[...] = jnp.zeros_like(lse_s)

    def pair_body(pair, carry):
        lanes = pair_lanes(pair)
        for block in range(2):
            rows = slice(block * HALF, (block + 1) * HALF)
            q_pair = q_ref[rows, lanes]
            q_both = jnp.concatenate([q_pair * first, q_pair * second], 0)
            spans = [(0, SEG, 0)]
            if block:
                spans.append((SEG, SEG + HALF, 1))
            spans.append((SEG + block * HALF, SEG + (block + 1) * HALF, 2))
            scores = []
            for low, high, kind in spans:
                part = dot_nt(q_both, k_ref[low:high, lanes])
                if kind == 0:
                    part = part + memory_bias
                if kind == 2:
                    part = jnp.where(diagonal, part, -1e30)
                scores.append(part)
            most = functools.reduce(jnp.maximum, [jnp.max(part, -1, keepdims=True) for part in scores])
            weights = [jnp.exp(part - most) for part in scores]
            total = functools.reduce(jnp.add, [jnp.sum(part, -1, keepdims=True) for part in weights])
            mixed = functools.reduce(
                jnp.add,
                [
                    dot_nn(part.astype(bf16), v_ref[low:high, lanes])
                    for part, (low, high, kind) in zip(weights, spans)
                ],
            )
            mixed = mixed / total
            mixed_ref[rows, lanes] = jnp.where(lane < HEAD_DIM, mixed[:HALF], mixed[HALF:]).astype(bf16)
            lse = most + jnp.log(total)
            kept = jnp.where(lane == 2 * pair, lse[:HALF], lse_s[rows, :])
            lse_s[rows, :] = jnp.where(lane == 2 * pair + 1, lse[HALF:], kept)
        return carry

    lax.fori_loop(0, HEADS // 2, pair_body, 0)
    lse_ref[...] = jnp.transpose(lse_s[...])[0:HEADS, :]
    after = x + (dot_nn(mixed_ref[...], attn_ref[3]) + vec_ref[6:7, :])
    after_ref[...] = after
    unit, _ = normalised(after)
    normed_two = (unit * vec_ref[2:3, :] + vec_ref[3:4, :]).astype(bf16)
    for tile in range(FF // TILE):
        columns = slice(tile * TILE, (tile + 1) * TILE)
        inner = dot_nn(normed_two, up_ref[:, columns]) + vec_ref[8 + tile : 9 + tile, :]
        act_s[:, columns] = (
            0.5 * inner * (1.0 + jnp.tanh(GELU_SCALE * (inner + 0.044715 * inner * inner * inner)))
        ).astype(bf16)
    hidden = after + (dot_nn(act_s[...], down_ref[...]) + vec_ref[7:8, :])
    hid_ref[...] = hidden
    hid16_ref[...] = hidden.astype(bf16)


SAVED = (
    ((SEG, D), f32),
    ((2 * SEG, D), bf16),
    ((SEG, D), bf16),
    ((2 * SEG, D), bf16),
    ((2 * SEG, D), bf16),
    ((HEADS, SEG), f32),
    ((SEG, D), bf16),
    ((SEG, D), f32),
)


def whole_spec(shape):
    return pl.BlockSpec(shape, lambda *_: (0,) * len(shape))


def stream_spec(shape, stream=None):
    zeros = (0,) * len(shape)
    if stream is None:
        return pl.BlockSpec((None,) + shape, lambda i: (i,) + zeros)
    return pl.BlockSpec((None,) + shape, lambda i: (stream,) + zeros)


def forward_layer(stream, streams, bias, hidden, memory, attn, upper, lower, vectors, earlier):
    saved_shapes = [jax.ShapeDtypeStruct((streams,) + shape, dtype) for shape, dtype in SAVED]
    saved_specs = [stream_spec(shape, stream) for shape, dtype in SAVED]
    out_shape = [saved_shapes[0], jax.ShapeDtypeStruct((SEG, D), bf16)] + saved_shapes[1:]
    out_specs = [saved_specs[0], whole_spec((SEG, D))] + saved_specs[1:]
    operands = [bias, hidden, memory, attn, upper, lower, vectors]
    in_specs = [
        pl.BlockSpec(memory_space=pltpu.SMEM),
        stream_spec((SEG, D), stream),
        whole_spec((SEG, D)),
        whole_spec(attn.shape),
        whole_spec(upper.shape),
        whole_spec(lower.shape),
        whole_spec(vectors.shape),
    ]
    aliases = {}
    if earlier is not None:
        for place, array in enumerate(earlier):
            aliases[len(operands)] = place if place == 0 else place + 1
            operands.append(array)
            in_specs.append(pl.BlockSpec(memory_space=pl.ANY))
    out = pl.pallas_call(
        forward_kernel,
        grid=(1,),
        out_shape=out_shape,
        in_specs=in_specs,
        out_specs=out_specs,
        scratch_shapes=[pltpu.VMEM((SEG, FF), bf16), pltpu.VMEM((SEG, PAIR), f32)],
        input_output_aliases=aliases,
        compiler_params=pltpu.CompilerParams(vmem_limit_bytes=VMEM_LIMIT),
        cost_estimate=pl.CostEstimate(flops=10**10, bytes_accessed=2 * 10**7, transcendentals=10**7),
        name="layer_forward",
    )(*operands)
    return [out[0]] + list(out[2:]), out[1]


def head_kernel(scale, x_ref, target_ref, weight_ref, out_ref, outer_ref, bias_ref, g_ref, dout_ref, douter_ref, loss_ref, acc_s):
    step = pl.program_id(0)

    @pl.when(step == 0)
    def _():
        acc_s[...] = jnp.zeros_like(acc_s)
        douter_ref[...] = jnp.zeros_like(douter_ref)
        loss_ref[...] = jnp.zeros_like(loss_ref)

    unit, rscale = normalised(x_ref[...])
    gain = outer_ref[1:2, :]
    normed = (unit * gain + outer_ref[2:3, :]).astype(bf16)
    logits = dot_nn(normed, out_ref[...]) + bias_ref[...]
    most = jnp.max(logits, -1, keepdims=True)
    powers = jnp.exp(logits - most)
    total = jnp.sum(powers, -1, keepdims=True)
    chosen = lax.broadcasted_iota(jnp.int32, logits.shape, 1) == target_ref[...]
    picked = jnp.sum(jnp.where(chosen, logits, 0.0), -1, keepdims=True)
    weight = weight_ref[...]
    loss_ref[...] += jnp.sum(weight * (most + jnp.log(total) - picked), 0, keepdims=True)
    spread = weight * scale
    dlogits = (powers * (spread / total) - jnp.where(chosen, spread, 0.0)).astype(bf16)
    acc_s[...] += dot_tn(normed, dlogits)
    bias_grad = column_sum(dlogits.astype(f32))
    dnormed = dot_nt(dlogits, out_ref[...])
    g_ref[...] = norm_back(dnormed, gain, unit, rscale)
    douter_ref[1:2, :] += column_sum(dnormed * unit)
    douter_ref[2:3, :] += column_sum(dnormed)
    douter_ref[3:4, :] += bias_grad[:, :D]
    douter_ref[4:5, :] += bias_grad[:, D:]

    @pl.when(step == pl.num_programs(0) - 1)
    def _():
        dout_ref[...] = acc_s[...]


def head(hidden, targets, weighting, out_weight, outer_vectors, scale):
    streams = hidden.shape[0]
    codes = out_weight.shape[1]
    bias = outer_vectors[3:].reshape(1, codes)
    return pl.pallas_call(
        functools.partial(head_kernel, scale),
        grid=(streams,),
        out_shape=[
            jax.ShapeDtypeStruct((streams, SEG, D), f32),
            jax.ShapeDtypeStruct((D, codes), f32),
            jax.ShapeDtypeStruct((8, D), f32),
            jax.ShapeDtypeStruct((1, 1), f32),
        ],
        in_specs=[
            stream_spec((SEG, D)),
            stream_spec((SEG, 1)),
            stream_spec((SEG, 1)),
            whole_spec((D, codes)),
            whole_spec(outer_vectors.shape),
            whole_spec((1, codes)),
        ],
        out_specs=[stream_spec((SEG, D)), whole_spec((D, codes)), whole_spec((8, D)), whole_spec((1, 1))],
        scratch_shapes=[pltpu.VMEM((D, codes), f32)],
        compiler_params=pltpu.CompilerParams(vmem_limit_bytes=VMEM_LIMIT),
        cost_estimate=pl.CostEstimate(flops=33 * 10**8, bytes_accessed=10**7, transcendentals=10**6),
        name="head",
    )(hidden, targets[..., None], weighting[..., None], out_weight, outer_vectors, bias)


def feed_back_kernel(g_ref, after_ref, up_ref, down_ref, vec_ref, dafter_ref, dup_ref, ddown_ref, dvec_ref, up_s, down_s, act_s, inner_s):
    step = pl.program_id(0)

    @pl.when(step == 0)
    def _():
        up_s[...] = jnp.zeros_like(up_s)
        down_s[...] = jnp.zeros_like(down_s)
        dvec_ref[...] = jnp.zeros_like(dvec_ref)

    grad = g_ref[...]
    branch = grad.astype(bf16)
    dvec_ref[2:3, :] += column_sum(branch.astype(f32))
    unit, scale = normalised(after_ref[...])
    gain = vec_ref[2:3, :]
    normed = (unit * gain + vec_ref[3:4, :]).astype(bf16)
    for tile in range(FF // TILE):
        columns = slice(tile * TILE, (tile + 1) * TILE)
        inner = dot_nn(normed, up_ref[:, columns]) + vec_ref[8 + tile : 9 + tile, :]
        dact = dot_nt(branch, down_ref[columns, :])
        square = inner * inner
        bent = jnp.tanh(GELU_SCALE * (inner + 0.044715 * square * inner))
        half = 0.5 * (1.0 + bent)
        act_s[:, columns] = (inner * half).astype(bf16)
        slope = half + (0.5 * GELU_SCALE) * inner * (1.0 - bent * bent) * (1.0 + 0.134145 * square)
        dinner = (dact * slope).astype(bf16)
        inner_s[:, columns] = dinner
        dvec_ref[4 + tile : 5 + tile, :] += column_sum(dinner.astype(f32))
    dnormed = dot_nt(inner_s[...], up_ref[...])
    dvec_ref[0:1, :] += column_sum(dnormed * unit)
    dvec_ref[1:2, :] += column_sum(dnormed)
    dafter_ref[...] = grad + norm_back(dnormed, gain, unit, scale)
    normed_t = jnp.transpose(normed)
    branch_t = jnp.transpose(branch)
    up_s[...] += dot_nn(normed_t, inner_s[...])
    down_s[...] += dot_nn(branch_t, act_s[...])

    @pl.when(step == pl.num_programs(0) - 1)
    def _():
        for tile in range(FF // TILE):
            dup_ref[tile] = up_s[:, tile * TILE : (tile + 1) * TILE].astype(bf16)
        ddown_ref[...] = jnp.transpose(down_s[...].astype(bf16))


def feed_back(grad, after, upper, lower, vectors):
    streams = grad.shape[0]
    return pl.pallas_call(
        feed_back_kernel,
        grid=(streams,),
        out_shape=[
            jax.ShapeDtypeStruct((streams, SEG, D), f32),
            jax.ShapeDtypeStruct((FF // TILE, D, TILE), bf16),
            jax.ShapeDtypeStruct((FF, D), bf16),
            jax.ShapeDtypeStruct((8, D), f32),
        ],
        in_specs=[
            stream_spec((SEG, D)),
            stream_spec((SEG, D)),
            whole_spec(upper.shape),
            whole_spec(lower.shape),
            whole_spec(vectors.shape),
        ],
        out_specs=[
            stream_spec((SEG, D)),
            whole_spec((FF // TILE, D, TILE)),
            whole_spec((FF, D)),
            whole_spec((8, D)),
        ],
        scratch_shapes=[
            pltpu.VMEM((D, FF), f32),
            pltpu.VMEM((D, FF), f32),
            pltpu.VMEM((SEG, FF), bf16),
            pltpu.VMEM((SEG, FF), bf16),
        ],
        compiler_params=pltpu.CompilerParams(vmem_limit_bytes=VMEM_LIMIT),
        cost_estimate=pl.CostEstimate(flops=11 * 10**9, bytes_accessed=2 * 10**7, transcendentals=2 * 10**6),
        name="feed_back",
    )(grad, after, upper, lower, vectors)


def attend_back_kernel(
    bias_ref,
    dafter_ref,
    x_ref,
    mem_ref,
    keyin_ref,
    q_ref,
    k_ref,
    v_ref,
    lse_ref,
    mixed_ref,
    attn_ref,
    vec_ref,
    dx_ref,
    dattn_ref,
    dvec_ref,
    attn_s,
    dmixed_s,
    dq_s,
    dk_s,
    dv_s,
    ds_s,
    delta_s,
):
    step = pl.program_id(0)

    @pl.when(step == 0)
    def _():
        attn_s[...] = jnp.zeros_like(attn_s)
        dvec_ref[...] = jnp.zeros_like(dvec_ref)

    dafter = dafter_ref[...]
    branch = dafter.astype(bf16)
    dvec_ref[4:5, :] += column_sum(branch.astype(f32))
    dmixed = dot_nt(branch, attn_ref[3]).astype(bf16)
    dmixed_s[...] = dmixed
    attn_s[3] += dot_nn(jnp.transpose(mixed_ref[...]), branch)
    product = dmixed.astype(f32) * mixed_ref[...].astype(f32)
    high = product.astype(bf16)
    rest = (product - high.astype(f32)).astype(bf16)
    owner = lax.broadcasted_iota(jnp.int32, (HEADS, D), 1) // HEAD_DIM
    pick = (owner == lax.broadcasted_iota(jnp.int32, (HEADS, D), 0)).astype(bf16)
    delta_s[...] = dot_nt(pick, high) + dot_nt(pick, rest)
    first, second = head_masks()
    memory_bias = bias_ref[0]
    key_pos = lax.broadcasted_iota(jnp.int32, (HALF, 2 * HALF), 0)
    query_pos = lax.broadcasted_iota(jnp.int32, (HALF, 2 * HALF), 1) % HALF
    diagonal = key_pos <= query_pos
    head_row = lax.broadcasted_iota(jnp.int32, (PAIR, HALF), 0)

    def pair_body(pair, carry):
        lanes = pair_lanes(pair)
        q_pair, do_pair = q_ref[:, lanes], dmixed_s[:, lanes]

        def spread(value):
            return jnp.concatenate(
                [value[:HALF] * first, value[:HALF] * second, value[HALF:] * first, value[HALF:] * second], 0
            )

        q_all, do_all = spread(q_pair), spread(do_pair)

        def rows_of(ref):
            one, two = ref[pl.ds(2 * pair, 1), :], ref[pl.ds(2 * pair + 1, 1), :]
            return jnp.concatenate([one[:, :HALF], two[:, :HALF], one[:, HALF:], two[:, HALF:]], 1)

        lse_all, delta_all = rows_of(lse_ref), rows_of(delta_s)
        for block in range(4):
            keys = slice(block * HALF, (block + 1) * HALF)
            start = 2 * HALF if block == 3 else 0
            scores = dot_nt(k_ref[keys, lanes], q_all[start:])
            if block < 2:
                scores = scores + memory_bias
            weights = jnp.exp(scores - lse_all[:, start:])
            if block == 2:
                weights = jnp.concatenate(
                    [jnp.where(diagonal, weights[:, : 2 * HALF], 0.0), weights[:, 2 * HALF :]], 1
                )
            if block == 3:
                weights = jnp.where(diagonal, weights, 0.0)
            dweights = dot_nt(v_ref[keys, lanes], do_all[start:])
            dscores = (weights * (dweights - delta_all[:, start:])).astype(bf16)
            dv_s[keys, lanes] = dot_nn(weights.astype(bf16), do_all[start:]).astype(bf16)
            dk_s[keys, lanes] = dot_nn(dscores, q_all[start:]).astype(bf16)
            ds_s[keys, start:] = dscores
        k_t = jnp.transpose(k_ref[:, lanes])
        for block in range(2):
            seen = SEG + (block + 1) * HALF
            grads = dot_nn(k_t[:, :seen], ds_s[:seen, block * 2 * HALF : (block + 1) * 2 * HALF])
            grads = jnp.where(head_row < HEAD_DIM, grads[:, :HALF], grads[:, HALF:])
            dq_s[block * HALF : (block + 1) * HALF, lanes] = (
                jnp.transpose(grads) * (HEAD_DIM**-0.5)
            ).astype(bf16)
        return carry

    lax.fori_loop(0, HEADS // 2, pair_body, 0)
    dq, dk, dv = dq_s[...], dk_s[...], dv_s[...]
    keyin_t = jnp.transpose(keyin_ref[...])
    attn_s[0] += dot_nn(keyin_t[:, SEG:], dq)
    attn_s[1] += dot_nn(keyin_t, dk)
    attn_s[2] += dot_nn(keyin_t, dv)
    dvec_ref[2:3, :] += column_sum(dq.astype(f32))
    dvec_ref[3:4, :] += column_sum(dv.astype(f32))
    dkeyin = dot_nt(dk, attn_ref[1]) + dot_nt(dv, attn_ref[2])
    dmem = dkeyin[:SEG]
    down = dkeyin[SEG:] + dot_nt(dq, attn_ref[0])
    gain = vec_ref[0:1, :]
    unit, scale = normalised(x_ref[...])
    mem_unit, _ = normalised(mem_ref[...].astype(f32))
    dvec_ref[0:1, :] += column_sum(down * unit + dmem * mem_unit)
    dvec_ref[1:2, :] += column_sum(down + dmem)
    dx_ref[...] = dafter + norm_back(down, gain, unit, scale)

    @pl.when(step == pl.num_programs(0) - 1)
    def _():
        dattn_ref[...] = attn_s[...].astype(bf16)


def attend_back(bias, dafter, x, memory, saved, attn, vectors):
    streams = dafter.shape[0]
    keyin, q, k, v, lse, mixed = saved
    return pl.pallas_call(
        attend_back_kernel,
        grid=(streams,),
        out_shape=[
            jax.ShapeDtypeStruct((streams, SEG, D), f32),
            jax.ShapeDtypeStruct((4, D, D), bf16),
            jax.ShapeDtypeStruct((8, D), f32),
        ],
        in_specs=[
            pl.BlockSpec(memory_space=pltpu.SMEM),
            stream_spec((SEG, D)),
            stream_spec((SEG, D)),
            stream_spec((SEG, D)),
            stream_spec((2 * SEG, D)),
            stream_spec((SEG, D)),
            stream_spec((2 * SEG, D)),
            stream_spec((2 * SEG, D)),
            stream_spec((HEADS, SEG)),
            stream_spec((SEG, D)),
            whole_spec(attn.shape),
            whole_spec(vectors.shape),
        ],
        out_specs=[stream_spec((SEG, D)), whole_spec((4, D, D)), whole_spec((8, D))],
        scratch_shapes=[
            pltpu.VMEM((4, D, D), f32),
            pltpu.VMEM((SEG, D), bf16),
            pltpu.VMEM((SEG, D), bf16),
            pltpu.VMEM((2 * SEG, D), bf16),
            pltpu.VMEM((2 * SEG, D), bf16),
            pltpu.VMEM((2 * SEG, 2 * SEG), bf16),
            pltpu.VMEM((HEADS, SEG), f32),
        ],
        compiler_params=pltpu.CompilerParams(vmem_limit_bytes=VMEM_LIMIT),
        cost_estimate=pl.CostEstimate(flops=3 * 10**10, bytes_accessed=2 * 10**7, transcendentals=10**7),
        name="attend_back",
    )(bias, dafter, x, memory, keyin, q, k, v, lse, mixed, attn, vectors)


def from_behind(value, axis, steps):
    count = lax.axis_size(axis)
    leading, last = (max(0, -steps), min(count, count - steps))
    return lax.ppermute(value, axis, [(source, source + steps) for source in range(leading, last)])


def adamw(weight, moment, second, grad, rate, decay):
    moment = 0.5 * moment + 0.5 * grad
    second = 0.99 * second + 0.01 * grad * grad
    fixed_moment = moment / (1.0 - 0.5**STEP)
    fixed_second = second / (1.0 - 0.99**STEP)
    weight = weight * (1.0 - rate * decay) - rate * fixed_moment / (jnp.sqrt(fixed_second) + 1e-08)
    return (weight, moment, second)


GROUPS = 4
UNITS = 6
SMALL = 112


def peers():
    count = {"seg": lax.axis_size("seg"), "dp": lax.axis_size("dp")}
    seg, dp = lax.axis_index("seg"), lax.axis_index("dp")
    core, x, y = seg % 2, dp % 2, (dp // 2) % 2
    across_core = {"seg": seg + 1 - 2 * core}
    across_x = {"dp": dp + 1 - 2 * x}
    across_y = {"dp": dp + 2 - 4 * y}
    across_both = {"dp": dp + 3 - 2 * x - 4 * y}
    far = []
    step = GROUPS
    while step < count["dp"]:
        far.append({"dp": dp + step - 2 * step * ((dp // step) % 2)})
        step *= 2
    return seg, dp, core, x, y, across_core, (across_x, across_y, across_both), far


def others(seg, count):
    return [lax.rem(seg + step, count) for step in range(1, count)]


def greet(seg, count, near, far):
    barrier = pltpu.get_barrier_semaphore()
    targets = [{"seg": other} for other in others(seg, count)] + list(near) + list(far)
    for target in targets:
        pl.semaphore_signal(barrier, inc=1, device_id=target, device_id_type=pl.DeviceIdType.MESH)
    pl.semaphore_wait(barrier, len(targets))


def remote(source, target, send, recv, device):
    return pltpu.make_async_remote_copy(
        src_ref=source,
        dst_ref=target,
        send_sem=send,
        recv_sem=recv,
        device_id=device,
        device_id_type=pl.DeviceIdType.MESH,
    )


def wait_bytes(ref, sem):
    pltpu.make_async_copy(ref, ref, sem).wait()


def plus(left, right):
    return (left.astype(f32) + right.astype(f32)).astype(bf16)


def owners(count):
    attn, feed = count // 4 - 1, count // 4
    return (
        (0, 1, 2 * attn, 0),
        (1, 1, 2 * attn + 1, 0),
        (2, 2, 2 * feed, 0),
        (4, 2, 2 * feed + 1, 2),
    )


def reduce_kernel(
    count,
    attn0,
    attn1,
    up0,
    up1,
    down0,
    down1,
    small_ref,
    whole_ref,
    every_ref,
    small_out,
    square_out,
    mine,
    got0,
    got1,
    got2,
    got3,
    goth,
    small_core,
    small_s,
    small_got,
    sq_seg,
    sq_dp,
    load_sem,
    send0,
    recv0,
    send1,
    recv1,
    send2,
    recv2,
    send3,
    recv3,
    sendh,
    recvh,
    small_send,
    small_recv,
    every_send,
    every_recv,
    whole_send,
    whole_recv,
    half_sem,
    sq_send,
    sq_recv,
    sqd_send,
    sqd_recv,
):
    seg, dp, core, x, y, across_core, near, far = peers()
    across_x, across_y, across_both = near
    planes = count // 2
    plane = seg // 2
    group = 2 * y + x

    def pieces(row):
        return (
            (attn0.at[:, :, row], (slice(None), slice(None), 0)),
            (attn1.at[:, :, row], (slice(None), slice(None), 1)),
            (up0.at[:, row], (0, 0, slice(2, 6))),
            (up1.at[:, row], (0, 1, slice(2, 6))),
            (down0.at[row], (1, 0, slice(2, 6))),
            (down1.at[row], (1, 1, slice(2, 6))),
        )

    order = [lax.rem(plane + 1 + step, planes) for step in range(planes)]
    for step in range(planes):
        for source, place in pieces(2 * order[step] + core):
            pltpu.make_async_copy(source, mine.at[(step,) + place], load_sem.at[step]).start()
    greet(seg, count, near, far)
    for step in range(planes):
        for source, place in pieces(2 * order[step] + 1 - core):
            remote(source, got0.at[(step,) + place], send0.at[step], recv0.at[step], across_core).start()

    def small_steps():
        copy = remote(small_ref, small_core, small_send.at[0], small_recv.at[0], across_core)
        copy.start()
        yield
        copy.wait()
        small_s[...] = small_ref[...] + small_core[...]
        half = pl.ds(pl.multiple_of(core * (SMALL // 2), 8), SMALL // 2)
        targets = [across_x, across_y] + far
        step = 1
        while step < planes:
            targets.append({"seg": seg + 2 * step - 4 * step * ((plane // step) % 2)})
            step *= 2
        for place, target in enumerate(targets):
            copy = remote(
                small_s.at[half],
                small_got.at[place],
                small_send.at[place + 1],
                small_recv.at[place + 1],
                target,
            )
            copy.start()
            yield
            copy.wait()
            small_s[half, :] += small_got[place]
        small_out[half, :] = small_s[half, :]
        last = len(targets) + 1
        copy = remote(small_out.at[half], small_out.at[half], small_send.at[last], small_recv.at[last], across_core)
        copy.start()
        yield
        copy.wait()

    small_run = small_steps()
    next(small_run)

    def first_of(step):
        return (
            remote(mine.at[step, :, 1 - x, 0:3], got1.at[step, 0], send1.at[step, 0], recv1.at[step, 0], across_x),
            remote(mine.at[step, 1 - y, :, 3:6], got1.at[step, 1], send1.at[step, 1], recv1.at[step, 1], across_y),
        )

    def second_of(step):
        return (
            remote(mine.at[step, 1 - y, x, 0:3], got2.at[step, 0], send2.at[step, 0], recv2.at[step, 0], across_y),
            remote(mine.at[step, y, 1 - x, 3:6], got2.at[step, 1], send2.at[step, 1], recv2.at[step, 1], across_x),
        )

    def third_of(step):
        return remote(
            mine.at[step, y, x],
            got3.at[plane],
            send3.at[step],
            recv3.at[plane],
            {"seg": 2 * order[step] + core},
        )

    def begin(step):
        wait_bytes(mine.at[step], load_sem.at[step])
        wait_bytes(got0.at[step], recv0.at[step])

        def body(place, carry):
            mine[step, place // 2, place % 2] = plus(mine[step, place // 2, place % 2], got0[step, place // 2, place % 2])
            return carry

        lax.fori_loop(0, GROUPS, body, 0)
        for copy in first_of(step):
            copy.start()

    def middle(step):
        for copy in first_of(step):
            copy.wait_recv()
        for place in range(2):
            mine[step, place, x, 0:3] = plus(mine[step, place, x, 0:3], got1[step, 0, place])
            mine[step, y, place, 3:6] = plus(mine[step, y, place, 3:6], got1[step, 1, place])
        for copy in second_of(step):
            copy.start()

    def end(step):
        for copy in second_of(step):
            copy.wait_recv()
        mine[step, y, x, 0:3] = plus(mine[step, y, x, 0:3], got2[step, 0])
        mine[step, y, x, 3:6] = plus(mine[step, y, x, 3:6], got2[step, 1])
        for place, target in enumerate(far):
            copy = remote(
                mine.at[step, y, x], goth.at[place, step], sendh.at[place, step], recvh.at[place, step], target
            )
            copy.start()
            copy.wait()
            mine[step, y, x] = plus(mine[step, y, x], goth[place, step])
        if step < planes - 1:
            third_of(step).start()

    for step in range(planes + 2):
        if step < planes:
            begin(step)
        if 1 <= step <= planes:
            middle(step - 1)
        if step >= 2:
            end(step - 2)
        next(small_run, None)
    for _ in small_run:
        pass

    total = mine[planes - 1, y, x].astype(f32)
    for step in range(1, planes):
        sender = lax.rem(plane + step, planes)
        wait_bytes(got3.at[sender], recv3.at[sender])
        total = total + got3[sender].astype(f32)
    every_ref[group] = total.astype(bf16)
    square = jnp.sum(jnp.sum(jnp.sum(total * total, 0), 0, keepdims=True), 1, keepdims=True)
    sq_seg[seg] = jnp.broadcast_to(square, (8, 128))

    roles = owners(count)

    def gift(place):
        first, width, owner, spot = roles[place]
        return remote(
            every_ref.at[group, first : first + width],
            whole_ref.at[seg, spot : spot + width],
            whole_send.at[place],
            whole_recv.at[seg],
            {"seg": owner},
        )

    for place, (first, width, owner, spot) in enumerate(roles):

        @pl.when(seg != owner)
        def _():
            gift(place).start()

        @pl.when(seg == owner)
        def _():
            whole_ref[seg, spot : spot + width] = every_ref[group, first : first + width]

    for step, other in enumerate(others(seg, count)):
        remote(sq_seg.at[seg], sq_seg.at[seg], sq_send.at[step], sq_recv.at[seg], {"seg": other}).start()
    for place, target in enumerate(near):
        remote(
            every_ref.at[group], every_ref.at[group], every_send.at[place], every_recv.at[place], target
        ).start()
    for other in others(seg, count):
        wait_bytes(sq_seg.at[other], sq_recv.at[other])
    sq_dp[group] = jnp.sum(sq_seg[...], 0)
    for place, target in enumerate(near):
        remote(sq_dp.at[group], sq_dp.at[group], sqd_send.at[place], sqd_recv.at[place], target).start()
    for place, target in enumerate(near):
        remote(sq_dp.at[group], sq_dp.at[group], sqd_send.at[place], sqd_recv.at[place], target).wait()
    square_out[...] = jnp.sum(sq_dp[...], 0)

    for place, (first, width, owner, spot) in enumerate(roles):

        @pl.when(seg == owner)
        def _():
            for other in others(seg, count):
                wait_bytes(whole_ref.at[other, spot : spot + width], whole_recv.at[other])
            if width == 2:
                span = slice(spot, spot + width)
                copy = remote(
                    whole_ref.at[:, span], whole_ref.at[:, span], half_sem.at[0], half_sem.at[1], across_core
                )
                copy.start()
                copy.wait()

    for step in range(planes):
        wait_bytes(mine.at[step], send0.at[step])
        for copy in first_of(step) + second_of(step):
            copy.wait_send()
        if step < planes - 1:
            third_of(step).wait_send()
    for place, (first, width, owner, spot) in enumerate(roles):

        @pl.when(seg != owner)
        def _():
            gift(place).wait_send()

    for step in range(count - 1):
        wait_bytes(sq_seg.at[0], sq_send.at[step])
    for place, target in enumerate(near):
        remote(
            every_ref.at[group], every_ref.at[group], every_send.at[place], every_recv.at[place], target
        ).wait()


def reduce_grads(count, dp_count, attn, up, down, small):
    rows = D // count
    planes = count // 2
    far = max(1, dp_count.bit_length() - 3)
    shape = (UNITS, rows, D)
    attn = [grad.reshape(2, 2, count, rows, D) for grad in attn]
    up = [grad.reshape(4, count, rows, D) for grad in up]
    down = [grad.reshape(count, 4, rows, D) for grad in down]
    stages = 2 + planes.bit_length() + max(0, dp_count.bit_length() - 3)
    dma = pltpu.SemaphoreType.DMA
    return pl.pallas_call(
        functools.partial(reduce_kernel, count),
        out_shape=[
            jax.ShapeDtypeStruct((count, 4, rows, D), bf16),
            jax.ShapeDtypeStruct((GROUPS,) + shape, bf16),
            jax.ShapeDtypeStruct((SMALL, D), f32),
            jax.ShapeDtypeStruct((8, 128), f32),
        ],
        in_specs=[pl.BlockSpec(memory_space=pl.ANY)] * 6 + [pl.BlockSpec(memory_space=pltpu.VMEM)],
        out_specs=[pl.BlockSpec(memory_space=pltpu.VMEM)] * 4,
        scratch_shapes=[
            pltpu.VMEM((planes, 2, 2) + shape, bf16),
            pltpu.VMEM((planes, 2, 2) + shape, bf16),
            pltpu.VMEM((planes, 2, 2, 3, rows, D), bf16),
            pltpu.VMEM((planes, 2, 3, rows, D), bf16),
            pltpu.VMEM((planes,) + shape, bf16),
            pltpu.VMEM((far, planes) + shape, bf16),
            pltpu.VMEM((SMALL, D), f32),
            pltpu.VMEM((SMALL, D), f32),
            pltpu.VMEM((stages, SMALL // 2, D), f32),
            pltpu.VMEM((count, 8, 128), f32),
            pltpu.VMEM((GROUPS, 8, 128), f32),
            dma((planes,)),
            dma((planes,)),
            dma((planes,)),
            dma((planes, 2)),
            dma((planes, 2)),
            dma((planes, 2)),
            dma((planes, 2)),
            dma((planes,)),
            dma((planes,)),
            dma((far, planes)),
            dma((far, planes)),
            dma((stages + 2,)),
            dma((stages + 2,)),
            dma((3,)),
            dma((3,)),
            dma((4,)),
            dma((count,)),
            dma((2,)),
            dma((count,)),
            dma((count,)),
            dma((3,)),
            dma((3,)),
        ],
        compiler_params=pltpu.CompilerParams(
            collective_id=1, has_side_effects=True, vmem_limit_bytes=VMEM_LIMIT
        ),
        cost_estimate=pl.CostEstimate(flops=10**8, bytes_accessed=2 * 10**8, transcendentals=0),
        name="reduce_grads",
    )(*attn, *up, *down, small)


def halves(value):
    high = value.astype(bf16)
    return high, (value - high.astype(f32)).astype(bf16)


def times(left, right):
    (left_high, left_low), (right_high, right_low) = left, right
    return dot_nn(
        jnp.concatenate([left_high, left_high, left_low], 1),
        jnp.concatenate([right_high, right_low, right_high], 0),
    )


def times_t(left, right):
    (left_high, left_low), (right_high, right_low) = left, right
    return dot_nt(
        jnp.concatenate([left_high, left_high, left_low], 1),
        jnp.concatenate([right_high, right_low, right_high], 1),
    )


def muon_kernel(role_ref, clip_ref, whole_ref, mom_ref, out_ref, x_s, q_s, gram_s, high_s, low_s):
    count, rows = whole_ref.shape[0], whole_ref.shape[2]
    core = role_ref[1]
    clip = clip_ref[0]
    eye = (
        lax.broadcasted_iota(jnp.int32, (D, D), 0) == lax.broadcasted_iota(jnp.int32, (D, D), 1)
    ).astype(f32)

    @pl.when(role_ref[0] == 1)
    def _():
        start = 0.5 * mom_ref[:, core] + clip * whole_ref[:, 0].astype(f32)
        start = start.reshape(D, D)
        size = jnp.sum(jnp.sum(start * start, 0, keepdims=True), 1, keepdims=True)
        x_s[...] = start / (jnp.sqrt(size) + 1e-07)

        def sweep(_, carry):
            value = x_s[...]
            both = halves(value)
            gram = times_t(both, both)
            gram_both = halves(gram)
            poly = -4.775 * gram + 2.0315 * times(gram_both, gram_both)
            x_s[...] = 3.4445 * value + times(halves(poly), both)
            return carry

        lax.fori_loop(0, 5, sweep, 0)
        out_ref[:, 0] = x_s[...].astype(bf16).reshape(count, rows, D)

    @pl.when(role_ref[0] == 2)
    def _():
        gram_s[...] = jnp.zeros_like(gram_s)

        def gather(tile, size):
            value = 0.5 * mom_ref[:, 2 + tile] + clip * whole_ref[:, tile].astype(f32)
            value = value.reshape(D, D)
            high, low = halves(value)
            high_s[tile] = high
            low_s[tile] = low

            @pl.when(role_ref[2] == 1)
            def _():
                high_s[tile] = jnp.transpose(high_s[tile])
                low_s[tile] = jnp.transpose(low_s[tile])

            both = high_s[tile], low_s[tile]
            gram_s[...] += times_t(both, both)
            return size + jnp.sum(jnp.sum(value * value, 0, keepdims=True), 1, keepdims=True)

        size = lax.fori_loop(0, 4, gather, jnp.zeros((1, 1), f32))
        scale = 1.0 / (jnp.sqrt(size) + 1e-07)
        gram_s[...] = gram_s[...] * (scale * scale)

        def poly_of(gram, gram_both):
            return 3.4445 * eye - 4.775 * gram + 2.0315 * times(gram_both, gram_both)

        def advance(gram_both, poly_both):
            gram_s[...] = times(halves(times(gram_both, poly_both)), poly_both)

        gram = gram_s[...]
        gram_both = halves(gram)
        poly = poly_of(gram, gram_both)
        q_s[...] = poly
        advance(gram_both, halves(poly))

        def sweep(_, carry):
            gram = gram_s[...]
            gram_both = halves(gram)
            poly_both = halves(poly_of(gram, gram_both))
            q_s[...] = times(halves(q_s[...]), poly_both)
            advance(gram_both, poly_both)
            return carry

        lax.fori_loop(0, 3, sweep, 0)
        gram = gram_s[...]
        last = times(halves(q_s[...]), halves(poly_of(gram, halves(gram)))) * scale
        last_both = halves(last)

        def finish(step, carry):
            tile = 2 * core + step
            x_s[...] = times(last_both, (high_s[tile], low_s[tile]))

            @pl.when(role_ref[2] == 1)
            def _():
                x_s[...] = jnp.transpose(x_s[...])

            out_ref[:, step] = x_s[...].astype(bf16).reshape(count, rows, D)
            return carry

        lax.fori_loop(0, 2, finish, 0)


def muon(role, clip, whole, momenta):
    count, _, rows, _ = whole.shape
    return pl.pallas_call(
        muon_kernel,
        out_shape=jax.ShapeDtypeStruct((count, 2, rows, D), bf16),
        in_specs=[
            pl.BlockSpec(memory_space=pltpu.SMEM),
            pl.BlockSpec(memory_space=pltpu.SMEM),
            pl.BlockSpec(memory_space=pltpu.VMEM),
            pl.BlockSpec(memory_space=pltpu.VMEM),
        ],
        out_specs=pl.BlockSpec(memory_space=pltpu.VMEM),
        scratch_shapes=[
            pltpu.VMEM((D, D), f32),
            pltpu.VMEM((D, D), f32),
            pltpu.VMEM((D, D), f32),
            pltpu.VMEM((4, D, D), bf16),
            pltpu.VMEM((4, D, D), bf16),
        ],
        compiler_params=pltpu.CompilerParams(vmem_limit_bytes=VMEM_LIMIT),
        cost_estimate=pl.CostEstimate(flops=2 * 10**10, bytes_accessed=10**7, transcendentals=0),
        name="muon",
    )(role, clip, whole, momenta)


def spread_kernel(count, made_ref, every_ref, send, recv, on_send, on_recv):
    seg, dp, core, x, y, across_core, near, far = peers()
    group = 2 * y + x
    greet(seg, count, near, ())
    roles = owners(count)

    def gift(place, other):
        first, width, owner, spot = roles[place]
        return remote(
            made_ref.at[other, 0:width],
            every_ref.at[group, first : first + width],
            send.at[other],
            recv.at[place],
            {"seg": other},
        )

    def onward(place, side):
        first, width, owner, spot = roles[place]
        block = every_ref.at[group, first : first + width]
        return remote(block, block, on_send.at[side, place], on_recv.at[side, place], near[side])

    for place, (first, width, owner, spot) in enumerate(roles):

        @pl.when(seg == owner)
        def _():
            for other in others(seg, count):
                gift(place, other).start()
            every_ref[group, first : first + width] = made_ref[seg, 0:width]

    for place, (first, width, owner, spot) in enumerate(roles):

        @pl.when(seg != owner)
        def _():
            wait_bytes(every_ref.at[group, first : first + width], recv.at[place])

        for side in range(3):
            onward(place, side).start()
    for place, (first, width, owner, spot) in enumerate(roles):
        for side in range(3):
            onward(place, side).wait()

        @pl.when(seg == owner)
        def _():
            for other in others(seg, count):
                gift(place, other).wait_send()


def spread(count, made):
    rows = made.shape[2]
    dma = pltpu.SemaphoreType.DMA
    return pl.pallas_call(
        functools.partial(spread_kernel, count),
        out_shape=jax.ShapeDtypeStruct((GROUPS, UNITS, rows, D), bf16),
        in_specs=[pl.BlockSpec(memory_space=pltpu.VMEM)],
        out_specs=pl.BlockSpec(memory_space=pltpu.VMEM),
        scratch_shapes=[dma((count,)), dma((4,)), dma((3, 4)), dma((3, 4))],
        compiler_params=pltpu.CompilerParams(
            collective_id=2, has_side_effects=True, vmem_limit_bytes=VMEM_LIMIT
        ),
        cost_estimate=pl.CostEstimate(flops=10**6, bytes_accessed=4 * 10**7, transcendentals=0),
        name="spread",
    )(made)


def local(
    frames,
    speech_mask,
    targets,
    in_proj,
    in_moment,
    in_second,
    out_proj,
    out_moment,
    out_second,
    layer_vectors,
    vectors_moment,
    vectors_second,
    outer_vectors,
    outer_moment,
    outer_second,
    attn_proj,
    attn_momentum,
    ff_up,
    up_momentum,
    ff_down,
    down_momentum,
    in_copy,
    out_copy,
    attn_copy,
    up_copy,
    down_copy,
):
    segment = lax.axis_index("seg")
    stream_total = frames.shape[0] * lax.axis_size("dp")
    streams = frames.shape[0]
    behind = from_behind(frames, "seg", 1)
    group = lax.axis_index("dp") % GROUPS
    block = D // lax.axis_size("seg")
    feeds = jnp.concatenate(
        [
            jnp.swapaxes(up_momentum.reshape(LAYERS, block, 4, D), 1, 2),
            down_momentum.reshape(LAYERS, 4, block, D),
        ],
        0,
    )
    owned = jnp.concatenate(
        [
            lax.dynamic_index_in_dim(attn_momentum, group, 1, keepdims=False),
            lax.dynamic_index_in_dim(feeds, group, 0, keepdims=False),
        ],
        0,
    )
    momenta = lax.all_gather(owned, "seg", axis=0, tiled=False)
    local_counts = jnp.sum(speech_mask, 1)
    counts = lax.psum(local_counts, "seg")
    weighting = speech_mask.astype(f32) / counts.astype(f32)[:, None]
    bias = jnp.where(segment > 0, 0.0, -1e30).astype(f32)[None]
    hidden = jnp.dot(frames, in_copy, preferred_element_type=f32) + outer_vectors[0]
    memory = (jnp.dot(behind, in_copy, preferred_element_type=f32) + outer_vectors[0]).astype(bf16)
    memory = [memory[stream] for stream in range(streams)]
    kept = []
    for depth in range(LAYERS):
        saved, passed = None, []
        for stream in range(streams):
            saved, short = forward_layer(
                stream,
                streams,
                bias,
                hidden,
                memory[stream],
                attn_copy[depth],
                up_copy[depth],
                down_copy[depth],
                layer_vectors[depth],
                saved,
            )
            if depth + 1 < LAYERS:
                passed.append(from_behind(short, "seg", 1))
        kept.append((hidden, jnp.stack(memory), saved))
        hidden = saved[0]
        memory = passed
    grad_hidden, grad_out, head_outer, loss_here = head(
        hidden, targets, weighting, out_copy, outer_vectors, 1.0 / stream_total
    )
    loss_here = loss_here[0, 0]
    attn_grads, up_grads, down_grads, vector_grads = ([], [], [], [])
    for depth in reversed(range(LAYERS)):
        entering, held, saved = kept[depth]
        dafter, grad_up, grad_down, feed_vec = feed_back(
            grad_hidden, saved[7], up_copy[depth], down_copy[depth], layer_vectors[depth]
        )
        grad_hidden, grad_attn, attn_vec = attend_back(
            bias, dafter, entering, held, saved[1:7], attn_copy[depth], layer_vectors[depth]
        )
        attn_grads.insert(0, grad_attn)
        up_grads.insert(0, grad_up)
        down_grads.insert(0, grad_down)
        vector_grads.insert(
            0,
            jnp.concatenate([attn_vec[0:2], feed_vec[0:2], attn_vec[2:5], feed_vec[2:3], feed_vec[4:8]], 0),
        )
    rows = grad_hidden.reshape(streams * SEG, D)
    rows_high = rows.astype(bf16)
    rows_rest = (rows - rows_high.astype(f32)).astype(bf16)
    frame_rows = frames.reshape(streams * SEG, frames.shape[2])
    grad_in = dot_tn(frame_rows, rows_high) + dot_tn(frame_rows, rows_rest)
    grad_outer = jnp.concatenate([jnp.sum(rows, 0, keepdims=True), head_outer[1:5]], 0)
    grad_vectors = jnp.stack(vector_grads)
    grad_out = lax.psum(grad_out, ("seg", "dp"))
    count, dp_count = lax.axis_size("seg"), lax.axis_size("dp")
    rows = D // count
    small = jnp.concatenate(
        [
            grad_in,
            grad_vectors.reshape(-1, D),
            grad_outer,
            jnp.full((1, D), loss_here),
            jnp.zeros((SMALL - 110, D), f32),
        ],
        0,
    )
    whole, every, small, squares = reduce_grads(count, dp_count, attn_grads, up_grads, down_grads, small)
    grad_in, grad_vectors, grad_outer = small[0:80], small[80:104].reshape(layer_vectors.shape), small[104:109]
    loss_sum = small[109, 0]
    small_squares = (
        jnp.sum(grad_in * grad_in)
        + jnp.sum(grad_out * grad_out)
        + jnp.sum(grad_vectors * grad_vectors)
        + jnp.sum(grad_outer * grad_outer)
    )
    grad_norm = jnp.sqrt(squares[0, 0] + small_squares)
    clip = jnp.minimum(1.0, 0.25 / (grad_norm + 1e-06))
    plane, core = segment // 2, segment % 2
    kind = jnp.where(plane == count // 4 - 1, 1, jnp.where(plane == count // 4, 2, 0))
    role = jnp.stack([kind, core, (group >= 2).astype(jnp.int32), core]).astype(jnp.int32)
    made = muon(role, clip[None], whole, momenta)
    updates = spread(count, made)

    def arranged(blocks):
        attn_part = jnp.swapaxes(blocks[:, 0:2], 0, 1)
        up_part = jnp.swapaxes(blocks[0:2, 2:6], 1, 2).reshape(ff_up.shape)
        down_part = blocks[2:4, 2:6].reshape(ff_down.shape)
        return attn_part.astype(f32), up_part.astype(f32), down_part.astype(f32)

    attn_sum, up_sum, down_sum = arranged(every)
    attn_mom = 0.5 * attn_momentum + clip * attn_sum
    up_mom = 0.5 * up_momentum + clip * up_sum
    down_mom = 0.5 * down_momentum + clip * down_sum
    in_new, in_moment_new, in_second_new = adamw(
        in_proj, in_moment, in_second, grad_in * clip, 0.05, 0.01
    )
    out_new, out_moment_new, out_second_new = adamw(
        out_proj, out_moment, out_second, grad_out * clip, 0.05, 0.01
    )
    vectors_new, vectors_moment_new, vectors_second_new = adamw(
        layer_vectors, vectors_moment, vectors_second, grad_vectors * clip, 0.25, 0.0
    )
    outer_new, outer_moment_new, outer_second_new = adamw(
        outer_vectors, outer_moment, outer_second, grad_outer * clip, 0.25, 0.0
    )
    attn_update, up_update, down_update = arranged(updates)
    attn_new = attn_proj * (1.0 - 0.3 * 0.01) - 0.3 * attn_update
    up_new = ff_up * (1.0 - 0.3 * 0.01) - 0.3 * max(1.0, FF / D) ** 0.5 * up_update
    down_new = ff_down * (1.0 - 0.3 * 0.01) - 0.3 * max(1.0, D / FF) ** 0.5 * down_update
    return (
        loss_sum,
        grad_norm,
        in_new,
        in_moment_new,
        in_second_new,
        out_new,
        out_moment_new,
        out_second_new,
        vectors_new,
        vectors_moment_new,
        vectors_second_new,
        outer_new,
        outer_moment_new,
        outer_second_new,
        attn_new,
        attn_mom,
        up_new,
        up_mom,
        down_new,
        down_mom,
        in_new.astype(jnp.bfloat16),
        out_new.astype(jnp.bfloat16),
        attn_new.astype(jnp.bfloat16),
        up_new.astype(jnp.bfloat16),
        down_new.astype(jnp.bfloat16),
    )


def solution(mesh):
    return jax.shard_map(
        local,
        mesh=mesh,
        in_specs=(
            P("dp", "seg", None),
            P("dp", "seg"),
            P("dp", "seg"),
            P(),
            P(),
            P(),
            P(),
            P(),
            P(),
            P(),
            P(),
            P(),
            P(),
            P(),
            P(),
            P(None, None, "seg", None),
            P(None, None, "seg", None),
            P(None, "seg", None),
            P(None, "seg", None),
            P(None, "seg", None),
            P(None, "seg", None),
            P(),
            P(),
            P(),
            P(),
            P(),
        ),
        out_specs=(
            P(),
            P(),
            P(),
            P(),
            P(),
            P(),
            P(),
            P(),
            P(),
            P(),
            P(),
            P(),
            P(),
            P(),
            P(None, None, "seg", None),
            P(None, None, "seg", None),
            P(None, "seg", None),
            P(None, "seg", None),
            P(None, "seg", None),
            P(None, "seg", None),
            P(),
            P(),
            P(None, None, "seg", None),
            P(None, "seg", None),
            P(None, "seg", None),
        ),
        check_vma=False,
    )
```

```python
import functools
import math

import jax
import jax.numpy as jnp
from jax import lax
from jax.experimental import pallas as pl
from jax.experimental.pallas import tpu as pltpu
from jax.sharding import PartitionSpec as P

D = 512
HEAD_DIM = 64
HEADS = D // HEAD_DIM
FF = 2048
LAYERS = 2
STEP = 10
SEG = 512
HALF = 256
PAIR = 2 * HEAD_DIM
TILE = 512
VMEM_LIMIT = 56 * 1024 * 1024
GELU_SCALE = math.sqrt(2.0 / math.pi)

f32 = jnp.float32
bf16 = jnp.bfloat16


def dot_nn(left, right):
    return lax.dot_general(left, right, (((1,), (0,)), ((), ())), preferred_element_type=f32)


def dot_nt(left, right):
    return lax.dot_general(left, right, (((1,), (1,)), ((), ())), preferred_element_type=f32)


def dot_tn(left, right):
    return lax.dot_general(left, right, (((0,), (0,)), ((), ())), preferred_element_type=f32)


def normalised(values):
    centred = values - jnp.mean(values, -1, keepdims=True)
    scale = lax.rsqrt(jnp.mean(centred * centred, -1, keepdims=True) + 1e-05)
    return centred * scale, scale


def norm_back(grad, gain, unit, scale):
    part = grad * gain
    mean_part = jnp.mean(part, -1, keepdims=True)
    mean_unit = jnp.mean(part * unit, -1, keepdims=True)
    return scale * (part - mean_part - unit * mean_unit)


def column_sum(values):
    return jnp.sum(values, 0, keepdims=True)


def head_masks():
    lane = lax.broadcasted_iota(jnp.int32, (1, PAIR), 1)
    return (lane < HEAD_DIM).astype(bf16), (lane >= HEAD_DIM).astype(bf16)


def pair_lanes(pair):
    return pl.ds(pl.multiple_of(pair * PAIR, PAIR), PAIR)


def forward_kernel(
    bias_ref,
    x_ref,
    mem_ref,
    attn_ref,
    up_ref,
    down_ref,
    vec_ref,
    *refs,
):
    hid_ref, hid16_ref, keyin_ref, q_ref, k_ref, v_ref, lse_ref, mixed_ref, after_ref, act_s, lse_s = refs[-11:]
    x = x_ref[...]
    own_unit, _ = normalised(x)
    gain, shift = vec_ref[0:1, :], vec_ref[1:2, :]
    normed = (own_unit * gain + shift).astype(bf16)
    mem_unit, _ = normalised(mem_ref[...].astype(f32))
    mem_normed = (mem_unit * gain + shift).astype(bf16)
    keyin_ref[0:SEG, :] = mem_normed
    keyin_ref[SEG:, :] = normed
    q_ref[...] = (dot_nn(normed, attn_ref[0]) + vec_ref[4:5, :]).astype(bf16) * jnp.asarray(HEAD_DIM**-0.5, bf16)
    k_ref[0:SEG, :] = dot_nn(mem_normed, attn_ref[1]).astype(bf16)
    k_ref[SEG:, :] = dot_nn(normed, attn_ref[1]).astype(bf16)
    v_ref[0:SEG, :] = (dot_nn(mem_normed, attn_ref[2]) + vec_ref[5:6, :]).astype(bf16)
    v_ref[SEG:, :] = (dot_nn(normed, attn_ref[2]) + vec_ref[5:6, :]).astype(bf16)
    first, second = head_masks()
    memory_bias = bias_ref[0]
    lane = lax.broadcasted_iota(jnp.int32, (HALF, PAIR), 1)
    query_pos = lax.broadcasted_iota(jnp.int32, (2 * HALF, HALF), 0) % HALF
    key_pos = lax.broadcasted_iota(jnp.int32, (2 * HALF, HALF), 1)
    diagonal = key_pos <= query_pos
    lse_s[...] = jnp.zeros_like(lse_s)

    def pair_body(pair, carry):
        lanes = pair_lanes(pair)
        for block in range(2):
            rows = slice(block * HALF, (block + 1) * HALF)
            q_pair = q_ref[rows, lanes]
            q_both = jnp.concatenate([q_pair * first, q_pair * second], 0)
            spans = [(0, SEG, 0)]
            if block:
                spans.append((SEG, SEG + HALF, 1))
            spans.append((SEG + block * HALF, SEG + (block + 1) * HALF, 2))
            scores = []
            for low, high, kind in spans:
                part = dot_nt(q_both, k_ref[low:high, lanes])
                if kind == 0:
                    part = part + memory_bias
                if kind == 2:
                    part = jnp.where(diagonal, part, -1e30)
                scores.append(part)
            most = functools.reduce(jnp.maximum, [jnp.max(part, -1, keepdims=True) for part in scores])
            weights = [jnp.exp(part - most) for part in scores]
            total = functools.reduce(jnp.add, [jnp.sum(part, -1, keepdims=True) for part in weights])
            mixed = functools.reduce(
                jnp.add,
                [
                    dot_nn(part.astype(bf16), v_ref[low:high, lanes])
                    for part, (low, high, kind) in zip(weights, spans)
                ],
            )
            mixed = mixed / total
            mixed_ref[rows, lanes] = jnp.where(lane < HEAD_DIM, mixed[:HALF], mixed[HALF:]).astype(bf16)
            lse = most + jnp.log(total)
            kept = jnp.where(lane == 2 * pair, lse[:HALF], lse_s[rows, :])
            lse_s[rows, :] = jnp.where(lane == 2 * pair + 1, lse[HALF:], kept)
        return carry

    lax.fori_loop(0, HEADS // 2, pair_body, 0)
    lse_ref[...] = jnp.transpose(lse_s[...])[0:HEADS, :]
    after = x + (dot_nn(mixed_ref[...], attn_ref[3]) + vec_ref[6:7, :])
    after_ref[...] = after
    unit, _ = normalised(after)
    normed_two = (unit * vec_ref[2:3, :] + vec_ref[3:4, :]).astype(bf16)
    for tile in range(FF // TILE):
        columns = slice(tile * TILE, (tile + 1) * TILE)
        inner = dot_nn(normed_two, up_ref[:, columns]) + vec_ref[8 + tile : 9 + tile, :]
        act_s[:, columns] = (
            0.5 * inner * (1.0 + jnp.tanh(GELU_SCALE * (inner + 0.044715 * inner * inner * inner)))
        ).astype(bf16)
    hidden = after + (dot_nn(act_s[...], down_ref[...]) + vec_ref[7:8, :])
    hid_ref[...] = hidden
    hid16_ref[...] = hidden.astype(bf16)


SAVED = (
    ((SEG, D), f32),
    ((2 * SEG, D), bf16),
    ((SEG, D), bf16),
    ((2 * SEG, D), bf16),
    ((2 * SEG, D), bf16),
    ((HEADS, SEG), f32),
    ((SEG, D), bf16),
    ((SEG, D), f32),
)


def whole_spec(shape):
    return pl.BlockSpec(shape, lambda *_: (0,) * len(shape))


def stream_spec(shape, stream=None):
    zeros = (0,) * len(shape)
    if stream is None:
        return pl.BlockSpec((None,) + shape, lambda i: (i,) + zeros)
    return pl.BlockSpec((None,) + shape, lambda i: (stream,) + zeros)


def layer_spec(shape, depth):
    zeros = (0,) * len(shape)
    return pl.BlockSpec((None,) + shape, lambda *_: (depth,) + zeros)


def forward_layer(depth, stream, streams, bias, hidden, memory, attn, upper, lower, vectors, earlier):
    saved_shapes = [jax.ShapeDtypeStruct((streams,) + shape, dtype) for shape, dtype in SAVED]
    saved_specs = [stream_spec(shape, stream) for shape, dtype in SAVED]
    out_shape = [saved_shapes[0], jax.ShapeDtypeStruct((SEG, D), bf16)] + saved_shapes[1:]
    out_specs = [saved_specs[0], whole_spec((SEG, D))] + saved_specs[1:]
    operands = [bias, hidden, memory, attn, upper, lower, vectors]
    in_specs = [
        pl.BlockSpec(memory_space=pltpu.SMEM),
        stream_spec((SEG, D), stream),
        stream_spec((SEG, D), stream) if memory.ndim == 3 else whole_spec((SEG, D)),
        layer_spec(attn.shape[1:], depth),
        layer_spec(upper.shape[1:], depth),
        layer_spec(lower.shape[1:], depth),
        layer_spec(vectors.shape[1:], depth),
    ]
    aliases = {}
    if earlier is not None:
        for place, array in enumerate(earlier):
            aliases[len(operands)] = place if place == 0 else place + 1
            operands.append(array)
            in_specs.append(pl.BlockSpec(memory_space=pl.ANY))
    out = pl.pallas_call(
        forward_kernel,
        grid=(1,),
        out_shape=out_shape,
        in_specs=in_specs,
        out_specs=out_specs,
        scratch_shapes=[pltpu.VMEM((SEG, FF), bf16), pltpu.VMEM((SEG, PAIR), f32)],
        input_output_aliases=aliases,
        compiler_params=pltpu.CompilerParams(vmem_limit_bytes=VMEM_LIMIT),
        cost_estimate=pl.CostEstimate(flops=10**10, bytes_accessed=2 * 10**7, transcendentals=10**7),
        name="layer_forward",
    )(*operands)
    return [out[0]] + list(out[2:]), out[1]


def head_kernel(scale, x_ref, target_ref, mask_ref, total_ref, out_ref, outer_ref, bias_ref, mom_ref, g_ref, dout_ref, douter_ref, acc_s):
    step = pl.program_id(0)

    @pl.when(step == 0)
    def _():
        acc_s[...] = jnp.zeros_like(acc_s)
        douter_ref[...] = jnp.zeros_like(douter_ref)

    unit, rscale = normalised(x_ref[...])
    gain = outer_ref[1:2, :]
    normed = (unit * gain + outer_ref[2:3, :]).astype(bf16)
    logits = dot_nn(normed, out_ref[...]) + bias_ref[...]
    most = jnp.max(logits, -1, keepdims=True)
    powers = jnp.exp(logits - most)
    total = jnp.sum(powers, -1, keepdims=True)
    target_row = target_ref[pl.ds(step, 1), :].astype(f32)
    weight_row = mask_ref[pl.ds(step, 1), :].astype(f32) * (1.0 / total_ref[pl.ds(step, 1), 0:1])
    columns = jnp.transpose(jnp.concatenate([target_row, weight_row, jnp.zeros((6, SEG), f32)], 0))
    target, weight = columns[:, 0:1].astype(jnp.int32), columns[:, 1:2]
    chosen = lax.broadcasted_iota(jnp.int32, logits.shape, 1) == target
    picked = jnp.sum(jnp.where(chosen, logits, 0.0), -1, keepdims=True)
    loss = jnp.sum(weight * (most + jnp.log(total) - picked), 0, keepdims=True)
    spread = weight * scale
    dlogits = (powers * (spread / total) - jnp.where(chosen, spread, 0.0)).astype(bf16)
    acc_s[...] += dot_nn(jnp.transpose(normed), dlogits)
    bias_grad = column_sum(dlogits.astype(f32))
    dnormed = dot_nt(dlogits, out_ref[...])
    g_ref[...] = norm_back(dnormed, gain, unit, rscale)
    douter_ref[1:2, :] += column_sum(dnormed * unit)
    douter_ref[2:3, :] += column_sum(dnormed)
    douter_ref[3:4, :] += bias_grad[:, :D]
    douter_ref[4:5, :] += bias_grad[:, D:]
    douter_ref[5:6, :] += jnp.broadcast_to(loss, (1, D))

    @pl.when(step == pl.num_programs(0) - 1)
    def _():
        dout_ref[...] = acc_s[...]


def head(hidden, targets, mask, totals, out_weight, outer_vectors, scale, momenta):
    streams = hidden.shape[0]
    codes = out_weight.shape[1]
    bias = outer_vectors[3:].reshape(1, codes)
    return pl.pallas_call(
        functools.partial(head_kernel, scale),
        grid=(streams,),
        out_shape=[
            jax.ShapeDtypeStruct((streams, SEG, D), f32),
            jax.ShapeDtypeStruct((D, codes), f32),
            jax.ShapeDtypeStruct((8, D), f32),
        ],
        in_specs=[
            stream_spec((SEG, D)),
            whole_spec((streams, SEG)),
            whole_spec((streams, SEG)),
            whole_spec((8, 128)),
            whole_spec((D, codes)),
            whole_spec(outer_vectors.shape),
            whole_spec((1, codes)),
            pl.BlockSpec(memory_space=pl.ANY),
        ],
        out_specs=[stream_spec((SEG, D)), whole_spec((D, codes)), whole_spec((8, D))],
        scratch_shapes=[pltpu.VMEM((D, codes), f32)],
        compiler_params=pltpu.CompilerParams(vmem_limit_bytes=VMEM_LIMIT),
        cost_estimate=pl.CostEstimate(flops=33 * 10**8, bytes_accessed=10**7, transcendentals=10**6),
        name="head",
    )(hidden, targets, mask, totals, out_weight, outer_vectors, bias, momenta)


def feed_back_kernel(g_ref, after_ref, up_ref, down_ref, vec_ref, dafter_ref, dup_ref, ddown_ref, dvec_ref, up_s, down_s, act_s, inner_s):
    step = pl.program_id(0)

    @pl.when(step == 0)
    def _():
        up_s[...] = jnp.zeros_like(up_s)
        down_s[...] = jnp.zeros_like(down_s)
        dvec_ref[...] = jnp.zeros_like(dvec_ref)

    grad = g_ref[...]
    branch = grad.astype(bf16)
    dvec_ref[2:3, :] += column_sum(branch.astype(f32))
    unit, scale = normalised(after_ref[...])
    gain = vec_ref[2:3, :]
    normed = (unit * gain + vec_ref[3:4, :]).astype(bf16)
    for tile in range(FF // TILE):
        columns = slice(tile * TILE, (tile + 1) * TILE)
        inner = dot_nn(normed, up_ref[:, columns]) + vec_ref[8 + tile : 9 + tile, :]
        dact = dot_nt(branch, down_ref[columns, :])
        square = inner * inner
        bent = jnp.tanh(GELU_SCALE * (inner + 0.044715 * square * inner))
        half = 0.5 * (1.0 + bent)
        act_s[:, columns] = (inner * half).astype(bf16)
        slope = half + (0.5 * GELU_SCALE) * inner * (1.0 - bent * bent) * (1.0 + 0.134145 * square)
        dinner = (dact * slope).astype(bf16)
        inner_s[:, columns] = dinner
        dvec_ref[4 + tile : 5 + tile, :] += column_sum(dinner.astype(f32))
    dnormed = dot_nt(inner_s[...], up_ref[...])
    dvec_ref[0:1, :] += column_sum(dnormed * unit)
    dvec_ref[1:2, :] += column_sum(dnormed)
    dafter_ref[...] = grad + norm_back(dnormed, gain, unit, scale)
    normed_t = jnp.transpose(normed)
    branch_t = jnp.transpose(branch)
    up_s[...] += dot_nn(normed_t, inner_s[...])
    down_s[...] += dot_nn(branch_t, act_s[...])

    @pl.when(step == pl.num_programs(0) - 1)
    def _():
        for tile in range(FF // TILE):
            dup_ref[tile] = up_s[:, tile * TILE : (tile + 1) * TILE].astype(bf16)
        ddown_ref[...] = jnp.transpose(down_s[...].astype(bf16))


def feed_back(depth, grad, after, upper, lower, vectors):
    streams = grad.shape[0]
    return pl.pallas_call(
        feed_back_kernel,
        grid=(streams,),
        out_shape=[
            jax.ShapeDtypeStruct((streams, SEG, D), f32),
            jax.ShapeDtypeStruct((FF // TILE, D, TILE), bf16),
            jax.ShapeDtypeStruct((FF, D), bf16),
            jax.ShapeDtypeStruct((8, D), f32),
        ],
        in_specs=[
            stream_spec((SEG, D)),
            stream_spec((SEG, D)),
            layer_spec(upper.shape[1:], depth),
            layer_spec(lower.shape[1:], depth),
            layer_spec(vectors.shape[1:], depth),
        ],
        out_specs=[
            stream_spec((SEG, D)),
            whole_spec((FF // TILE, D, TILE)),
            whole_spec((FF, D)),
            whole_spec((8, D)),
        ],
        scratch_shapes=[
            pltpu.VMEM((D, FF), f32),
            pltpu.VMEM((D, FF), f32),
            pltpu.VMEM((SEG, FF), bf16),
            pltpu.VMEM((SEG, FF), bf16),
        ],
        compiler_params=pltpu.CompilerParams(vmem_limit_bytes=VMEM_LIMIT),
        cost_estimate=pl.CostEstimate(flops=11 * 10**9, bytes_accessed=2 * 10**7, transcendentals=2 * 10**6),
        name="feed_back",
    )(grad, after, upper, lower, vectors)


def attend_back_kernel(
    lowest,
    bias_ref,
    dafter_ref,
    x_ref,
    mem_ref,
    keyin_ref,
    q_ref,
    k_ref,
    v_ref,
    lse_ref,
    mixed_ref,
    attn_ref,
    vec_ref,
    frames_ref,
    dx_ref,
    dattn_ref,
    dvec_ref,
    din_ref,
    attn_s,
    dmixed_s,
    dq_s,
    dk_s,
    dv_s,
    ds_s,
    delta_s,
):
    step = pl.program_id(0)

    @pl.when(step == 0)
    def _():
        attn_s[...] = jnp.zeros_like(attn_s)
        dvec_ref[...] = jnp.zeros_like(dvec_ref)
        din_ref[...] = jnp.zeros_like(din_ref)

    dafter = dafter_ref[...]
    branch = dafter.astype(bf16)
    dvec_ref[4:5, :] += column_sum(branch.astype(f32))
    dmixed = dot_nt(branch, attn_ref[3]).astype(bf16)
    dmixed_s[...] = dmixed
    attn_s[3] += dot_nn(jnp.transpose(mixed_ref[...]), branch)
    product = dmixed.astype(f32) * mixed_ref[...].astype(f32)
    high = product.astype(bf16)
    rest = (product - high.astype(f32)).astype(bf16)
    owner = lax.broadcasted_iota(jnp.int32, (HEADS, D), 1) // HEAD_DIM
    pick = (owner == lax.broadcasted_iota(jnp.int32, (HEADS, D), 0)).astype(bf16)
    delta_s[...] = dot_nt(pick, high) + dot_nt(pick, rest)
    first, second = head_masks()
    memory_bias = bias_ref[0]
    key_pos = lax.broadcasted_iota(jnp.int32, (HALF, 2 * HALF), 0)
    query_pos = lax.broadcasted_iota(jnp.int32, (HALF, 2 * HALF), 1) % HALF
    diagonal = key_pos <= query_pos
    head_row = lax.broadcasted_iota(jnp.int32, (PAIR, HALF), 0)

    def pair_body(pair, carry):
        lanes = pair_lanes(pair)
        q_pair, do_pair = q_ref[:, lanes], dmixed_s[:, lanes]

        def spread(value):
            return jnp.concatenate(
                [value[:HALF] * first, value[:HALF] * second, value[HALF:] * first, value[HALF:] * second], 0
            )

        q_all, do_all = spread(q_pair), spread(do_pair)

        def rows_of(ref):
            one, two = ref[pl.ds(2 * pair, 1), :], ref[pl.ds(2 * pair + 1, 1), :]
            return jnp.concatenate([one[:, :HALF], two[:, :HALF], one[:, HALF:], two[:, HALF:]], 1)

        lse_all, delta_all = rows_of(lse_ref), rows_of(delta_s)
        for block in range(4):
            keys = slice(block * HALF, (block + 1) * HALF)
            start = 2 * HALF if block == 3 else 0
            scores = dot_nt(k_ref[keys, lanes], q_all[start:])
            if block < 2:
                scores = scores + memory_bias
            weights = jnp.exp(scores - lse_all[:, start:])
            if block == 2:
                weights = jnp.concatenate(
                    [jnp.where(diagonal, weights[:, : 2 * HALF], 0.0), weights[:, 2 * HALF :]], 1
                )
            if block == 3:
                weights = jnp.where(diagonal, weights, 0.0)
            dweights = dot_nt(v_ref[keys, lanes], do_all[start:])
            dscores = (weights * (dweights - delta_all[:, start:])).astype(bf16)
            dv_s[keys, lanes] = dot_nn(weights.astype(bf16), do_all[start:]).astype(bf16)
            dk_s[keys, lanes] = dot_nn(dscores, q_all[start:]).astype(bf16)
            ds_s[keys, start:] = dscores
        k_t = jnp.transpose(k_ref[:, lanes])
        for block in range(2):
            seen = SEG + (block + 1) * HALF
            grads = dot_nn(k_t[:, :seen], ds_s[:seen, block * 2 * HALF : (block + 1) * 2 * HALF])
            grads = jnp.where(head_row < HEAD_DIM, grads[:, :HALF], grads[:, HALF:])
            dq_s[block * HALF : (block + 1) * HALF, lanes] = (
                jnp.transpose(grads) * (HEAD_DIM**-0.5)
            ).astype(bf16)
        return carry

    lax.fori_loop(0, HEADS // 2, pair_body, 0)
    dq, dk, dv = dq_s[...], dk_s[...], dv_s[...]
    keyin_t = jnp.transpose(keyin_ref[...])
    attn_s[0] += dot_nn(keyin_t[:, SEG:], dq)
    attn_s[1] += dot_nn(keyin_t, dk)
    attn_s[2] += dot_nn(keyin_t, dv)
    dvec_ref[2:3, :] += column_sum(dq.astype(f32))
    dvec_ref[3:4, :] += column_sum(dv.astype(f32))
    dkeyin = dot_nt(dk, attn_ref[1]) + dot_nt(dv, attn_ref[2])
    dmem = dkeyin[:SEG]
    down = dkeyin[SEG:] + dot_nt(dq, attn_ref[0])
    gain = vec_ref[0:1, :]
    unit, scale = normalised(x_ref[...])
    mem_unit, _ = normalised(mem_ref[...].astype(f32))
    dvec_ref[0:1, :] += column_sum(down * unit + dmem * mem_unit)
    dvec_ref[1:2, :] += column_sum(down + dmem)
    dx = dafter + norm_back(down, gain, unit, scale)
    dx_ref[...] = dx
    if lowest:
        dx_high = dx.astype(bf16)
        dx_rest = (dx - dx_high.astype(f32)).astype(bf16)
        din_ref[...] += dot_nn(frames_ref[...], dx_high) + dot_nn(frames_ref[...], dx_rest)
        dvec_ref[5:6, :] += column_sum(dx)

    @pl.when(step == pl.num_programs(0) - 1)
    def _():
        dattn_ref[...] = attn_s[...].astype(bf16)


def attend_back(depth, bias, dafter, x, memory, saved, attn, vectors, frames):
    streams = dafter.shape[0]
    keyin, q, k, v, lse, mixed = saved
    inputs = frames.shape[1]
    return pl.pallas_call(
        functools.partial(attend_back_kernel, depth == 0),
        grid=(streams,),
        out_shape=[
            jax.ShapeDtypeStruct((streams, SEG, D), f32),
            jax.ShapeDtypeStruct((4, D, D), bf16),
            jax.ShapeDtypeStruct((8, D), f32),
            jax.ShapeDtypeStruct((inputs, D), f32),
        ],
        in_specs=[
            pl.BlockSpec(memory_space=pltpu.SMEM),
            stream_spec((SEG, D)),
            stream_spec((SEG, D)),
            stream_spec((SEG, D)),
            stream_spec((2 * SEG, D)),
            stream_spec((SEG, D)),
            stream_spec((2 * SEG, D)),
            stream_spec((2 * SEG, D)),
            stream_spec((HEADS, SEG)),
            stream_spec((SEG, D)),
            layer_spec(attn.shape[1:], depth),
            layer_spec(vectors.shape[1:], depth),
            stream_spec((inputs, SEG)),
        ],
        out_specs=[
            stream_spec((SEG, D)),
            whole_spec((4, D, D)),
            whole_spec((8, D)),
            whole_spec((inputs, D)),
        ],
        scratch_shapes=[
            pltpu.VMEM((4, D, D), f32),
            pltpu.VMEM((SEG, D), bf16),
            pltpu.VMEM((SEG, D), bf16),
            pltpu.VMEM((2 * SEG, D), bf16),
            pltpu.VMEM((2 * SEG, D), bf16),
            pltpu.VMEM((2 * SEG, 2 * SEG), bf16),
            pltpu.VMEM((HEADS, SEG), f32),
        ],
        compiler_params=pltpu.CompilerParams(vmem_limit_bytes=VMEM_LIMIT),
        cost_estimate=pl.CostEstimate(flops=3 * 10**10, bytes_accessed=2 * 10**7, transcendentals=10**7),
        name="attend_back",
    )(bias, dafter, x, memory, keyin, q, k, v, lse, mixed, attn, vectors, frames)


def from_behind(value, axis, steps):
    count = lax.axis_size(axis)
    leading, last = (max(0, -steps), min(count, count - steps))
    return lax.ppermute(value, axis, [(source, source + steps) for source in range(leading, last)])


def adamw(weight, moment, second, grad, rate, decay):
    moment = 0.5 * moment + 0.5 * grad
    second = 0.99 * second + 0.01 * grad * grad
    fixed_moment = moment / (1.0 - 0.5**STEP)
    fixed_second = second / (1.0 - 0.99**STEP)
    weight = weight * (1.0 - rate * decay) - rate * fixed_moment / (jnp.sqrt(fixed_second) + 1e-08)
    return (weight, moment, second)


GROUPS = 4
UNITS = 6
SMALL = 128


def peers():
    count = {"seg": lax.axis_size("seg"), "dp": lax.axis_size("dp")}
    seg, dp = lax.axis_index("seg"), lax.axis_index("dp")
    core, x, y = seg % 2, dp % 2, (dp // 2) % 2
    across_core = {"seg": seg + 1 - 2 * core}
    across_x = {"dp": dp + 1 - 2 * x}
    across_y = {"dp": dp + 2 - 4 * y}
    across_both = {"dp": dp + 3 - 2 * x - 4 * y}
    far = []
    step = GROUPS
    while step < count["dp"]:
        far.append({"dp": dp + step - 2 * step * ((dp // step) % 2)})
        step *= 2
    return seg, dp, core, x, y, across_core, (across_x, across_y, across_both), far


def others(seg, count):
    return [lax.rem(seg + step, count) for step in range(1, count)]


def greet(seg, count, near, far):
    barrier = pltpu.get_barrier_semaphore()
    targets = [{"seg": other} for other in others(seg, count)] + list(near) + list(far)
    for target in targets:
        pl.semaphore_signal(barrier, inc=1, device_id=target, device_id_type=pl.DeviceIdType.MESH)
    pl.semaphore_wait(barrier, len(targets))


def remote(source, target, send, recv, device):
    return pltpu.make_async_remote_copy(
        src_ref=source,
        dst_ref=target,
        send_sem=send,
        recv_sem=recv,
        device_id=device,
        device_id_type=pl.DeviceIdType.MESH,
    )


def wait_bytes(ref, sem):
    pltpu.make_async_copy(ref, ref, sem).wait()


def plus(left, right):
    return (left.astype(f32) + right.astype(f32)).astype(bf16)


def owners(count):
    attn, feed = count // 4 - 1, count // 4
    return (
        (0, 1, 2 * attn, 0),
        (1, 1, 2 * attn + 1, 0),
        (2, 2, 2 * feed, 0),
        (4, 2, 2 * feed + 1, 2),
    )


def reduce_kernel(
    count,
    attn0,
    attn1,
    up0,
    up1,
    down0,
    down1,
    din_ref,
    vec0_ref,
    vec1_ref,
    vec2_ref,
    vec3_ref,
    outer_ref,
    whole_ref,
    every_ref,
    small_out,
    square_out,
    mine,
    got0,
    got1,
    got2,
    got3,
    goth,
    small_ref,
    small_core,
    small_s,
    small_got,
    sq_seg,
    sq_dp,
    load_sem,
    send0,
    recv0,
    send1,
    recv1,
    send2,
    recv2,
    send3,
    recv3,
    sendh,
    recvh,
    small_send,
    small_recv,
    every_send,
    every_recv,
    whole_send,
    whole_recv,
    half_sem,
    sq_send,
    sq_recv,
    sqd_send,
    sqd_recv,
):
    seg, dp, core, x, y, across_core, near, far = peers()
    across_x, across_y, across_both = near
    planes = count // 2
    plane = seg // 2
    group = 2 * y + x

    def pieces(row):
        return (
            (attn0.at[:, :, row], (slice(None), slice(None), 0)),
            (attn1.at[:, :, row], (slice(None), slice(None), 1)),
            (up1.at[:, row], (0, 0, slice(2, 6))),
            (up0.at[:, row], (0, 1, slice(2, 6))),
            (down0.at[row], (1, 0, slice(2, 6))),
            (down1.at[row], (1, 1, slice(2, 6))),
        )

    order = [lax.rem(plane + 1 + step, planes) for step in range(planes)]
    for step in range(planes):
        for source, place in pieces(2 * order[step] + core):
            pltpu.make_async_copy(source, mine.at[(step,) + place], load_sem.at[step]).start()
    inputs = din_ref.shape[0]
    small_ref[0:inputs, :] = din_ref[...]
    for place, ref in enumerate((vec0_ref, vec1_ref, vec2_ref, vec3_ref, outer_ref)):
        small_ref[inputs + 8 * place : inputs + 8 * place + 8, :] = ref[...]
    small_ref[inputs + 40 :, :] = jnp.zeros((SMALL - inputs - 40, D), f32)
    greet(seg, count, near, far)
    for step in range(planes):
        for source, place in pieces(2 * order[step] + 1 - core):
            remote(source, got0.at[(step,) + place], send0.at[step], recv0.at[step], across_core).start()

    def small_steps():
        copy = remote(small_ref, small_core, small_send.at[0], small_recv.at[0], across_core)
        copy.start()
        yield
        copy.wait()
        small_s[...] = small_ref[...] + small_core[...]
        half = pl.ds(pl.multiple_of(core * (SMALL // 2), 8), SMALL // 2)
        targets = [across_x, across_y] + far
        step = 1
        while step < planes:
            targets.append({"seg": seg + 2 * step - 4 * step * ((plane // step) % 2)})
            step *= 2
        for place, target in enumerate(targets):
            copy = remote(
                small_s.at[half],
                small_got.at[place],
                small_send.at[place + 1],
                small_recv.at[place + 1],
                target,
            )
            copy.start()
            yield
            copy.wait()
            small_s[half, :] += small_got[place]
        small_out[half, :] = small_s[half, :]
        last = len(targets) + 1
        copy = remote(small_out.at[half], small_out.at[half], small_send.at[last], small_recv.at[last], across_core)
        copy.start()
        yield
        copy.wait()

    small_run = small_steps()
    next(small_run)

    def first_of(step):
        return (
            remote(mine.at[step, :, 1 - x, 0:3], got1.at[step, 0], send1.at[step, 0], recv1.at[step, 0], across_x),
            remote(mine.at[step, 1 - y, :, 3:6], got1.at[step, 1], send1.at[step, 1], recv1.at[step, 1], across_y),
        )

    def second_of(step):
        return (
            remote(mine.at[step, 1 - y, x, 0:3], got2.at[step, 0], send2.at[step, 0], recv2.at[step, 0], across_y),
            remote(mine.at[step, y, 1 - x, 3:6], got2.at[step, 1], send2.at[step, 1], recv2.at[step, 1], across_x),
        )

    def third_of(step):
        return remote(
            mine.at[step, y, x],
            got3.at[plane],
            send3.at[step],
            recv3.at[plane],
            {"seg": 2 * order[step] + core},
        )

    def begin(step):
        wait_bytes(mine.at[step], load_sem.at[step])
        wait_bytes(got0.at[step], recv0.at[step])

        def body(place, carry):
            mine[step, place // 2, place % 2] = plus(mine[step, place // 2, place % 2], got0[step, place // 2, place % 2])
            return carry

        lax.fori_loop(0, GROUPS, body, 0)
        for copy in first_of(step):
            copy.start()

    def middle(step):
        for copy in first_of(step):
            copy.wait_recv()
        for place in range(2):
            mine[step, place, x, 0:3] = plus(mine[step, place, x, 0:3], got1[step, 0, place])
            mine[step, y, place, 3:6] = plus(mine[step, y, place, 3:6], got1[step, 1, place])
        for copy in second_of(step):
            copy.start()

    def end(step):
        for copy in second_of(step):
            copy.wait_recv()
        mine[step, y, x, 0:3] = plus(mine[step, y, x, 0:3], got2[step, 0])
        mine[step, y, x, 3:6] = plus(mine[step, y, x, 3:6], got2[step, 1])
        for place, target in enumerate(far):
            copy = remote(
                mine.at[step, y, x], goth.at[place, step], sendh.at[place, step], recvh.at[place, step], target
            )
            copy.start()
            copy.wait()
            mine[step, y, x] = plus(mine[step, y, x], goth[place, step])
        if step < planes - 1:
            third_of(step).start()

    for step in range(planes + 2):
        if step < planes:
            begin(step)
        if 1 <= step <= planes:
            middle(step - 1)
        if step >= 2:
            end(step - 2)
        next(small_run, None)
    for _ in small_run:
        pass

    total = mine[planes - 1, y, x].astype(f32)
    for step in range(1, planes):
        sender = lax.rem(plane + step, planes)
        wait_bytes(got3.at[sender], recv3.at[sender])
        total = total + got3[sender].astype(f32)
    every_ref[group] = total.astype(bf16)
    square = jnp.sum(jnp.sum(jnp.sum(total * total, 0), 0, keepdims=True), 1, keepdims=True)
    sq_seg[seg] = jnp.broadcast_to(square, (8, 128))

    roles = owners(count)

    def gift(place):
        first, width, owner, spot = roles[place]
        return remote(
            every_ref.at[group, first : first + width],
            whole_ref.at[seg, spot : spot + width],
            whole_send.at[place],
            whole_recv.at[seg],
            {"seg": owner},
        )

    for place, (first, width, owner, spot) in enumerate(roles):

        @pl.when(seg != owner)
        def _():
            gift(place).start()

        @pl.when(seg == owner)
        def _():
            whole_ref[seg, spot : spot + width] = every_ref[group, first : first + width]

    for step, other in enumerate(others(seg, count)):
        remote(sq_seg.at[seg], sq_seg.at[seg], sq_send.at[step], sq_recv.at[seg], {"seg": other}).start()
    for place, target in enumerate(near):
        remote(
            every_ref.at[group], every_ref.at[group], every_send.at[place], every_recv.at[place], target
        ).start()
    for other in others(seg, count):
        wait_bytes(sq_seg.at[other], sq_recv.at[other])
    sq_dp[group] = jnp.sum(sq_seg[...], 0)
    for place, target in enumerate(near):
        remote(sq_dp.at[group], sq_dp.at[group], sqd_send.at[place], sqd_recv.at[place], target).start()
    for place, target in enumerate(near):
        remote(sq_dp.at[group], sq_dp.at[group], sqd_send.at[place], sqd_recv.at[place], target).wait()
    sums = small_out[...]
    is_loss = lax.broadcasted_iota(jnp.int32, (SMALL, D), 0) == inputs + 37
    sums = jnp.where(is_loss, 0.0, sums)
    small_square = jnp.sum(jnp.sum(sums * sums, 0, keepdims=True), 1, keepdims=True)
    square_out[...] = jnp.sum(sq_dp[...], 0) + jnp.broadcast_to(small_square, (8, 128))

    for place, (first, width, owner, spot) in enumerate(roles):

        @pl.when(seg == owner)
        def _():
            for other in others(seg, count):
                wait_bytes(whole_ref.at[other, spot : spot + width], whole_recv.at[other])
            if width == 2:
                span = slice(spot, spot + width)
                copy = remote(
                    whole_ref.at[:, span], whole_ref.at[:, span], half_sem.at[0], half_sem.at[1], across_core
                )
                copy.start()
                copy.wait()

    for step in range(planes):
        wait_bytes(mine.at[step], send0.at[step])
        for copy in first_of(step) + second_of(step):
            copy.wait_send()
        if step < planes - 1:
            third_of(step).wait_send()
    for place, (first, width, owner, spot) in enumerate(roles):

        @pl.when(seg != owner)
        def _():
            gift(place).wait_send()

    for step in range(count - 1):
        wait_bytes(sq_seg.at[0], sq_send.at[step])
    for place, target in enumerate(near):
        remote(
            every_ref.at[group], every_ref.at[group], every_send.at[place], every_recv.at[place], target
        ).wait()


def reduce_grads(count, dp_count, attn, up, down, pieces):
    rows = D // count
    planes = count // 2
    far = max(1, dp_count.bit_length() - 3)
    shape = (UNITS, rows, D)
    attn = [grad.reshape(2, 2, count, rows, D) for grad in attn]
    up = [grad.reshape(4, count, rows, D) for grad in up]
    down = [grad.reshape(count, 4, rows, D) for grad in down]
    stages = 2 + planes.bit_length() + max(0, dp_count.bit_length() - 3)
    dma = pltpu.SemaphoreType.DMA
    return pl.pallas_call(
        functools.partial(reduce_kernel, count),
        out_shape=[
            jax.ShapeDtypeStruct((count, 4, rows, D), bf16),
            jax.ShapeDtypeStruct((GROUPS,) + shape, bf16),
            jax.ShapeDtypeStruct((SMALL, D), f32),
            jax.ShapeDtypeStruct((8, 128), f32),
        ],
        in_specs=[pl.BlockSpec(memory_space=pl.ANY)] * 6 + [pl.BlockSpec(memory_space=pltpu.VMEM)] * 6,
        out_specs=[pl.BlockSpec(memory_space=pltpu.VMEM)] * 4,
        scratch_shapes=[
            pltpu.VMEM((planes, 2, 2) + shape, bf16),
            pltpu.VMEM((planes, 2, 2) + shape, bf16),
            pltpu.VMEM((planes, 2, 2, 3, rows, D), bf16),
            pltpu.VMEM((planes, 2, 3, rows, D), bf16),
            pltpu.VMEM((planes,) + shape, bf16),
            pltpu.VMEM((far, planes) + shape, bf16),
            pltpu.VMEM((SMALL, D), f32),
            pltpu.VMEM((SMALL, D), f32),
            pltpu.VMEM((SMALL, D), f32),
            pltpu.VMEM((stages, SMALL // 2, D), f32),
            pltpu.VMEM((count, 8, 128), f32),
            pltpu.VMEM((GROUPS, 8, 128), f32),
            dma((planes,)),
            dma((planes,)),
            dma((planes,)),
            dma((planes, 2)),
            dma((planes, 2)),
            dma((planes, 2)),
            dma((planes, 2)),
            dma((planes,)),
            dma((planes,)),
            dma((far, planes)),
            dma((far, planes)),
            dma((stages + 2,)),
            dma((stages + 2,)),
            dma((3,)),
            dma((3,)),
            dma((4,)),
            dma((count,)),
            dma((2,)),
            dma((count,)),
            dma((count,)),
            dma((3,)),
            dma((3,)),
        ],
        compiler_params=pltpu.CompilerParams(
            collective_id=1, has_side_effects=True, vmem_limit_bytes=VMEM_LIMIT
        ),
        cost_estimate=pl.CostEstimate(flops=10**8, bytes_accessed=2 * 10**8, transcendentals=0),
        name="reduce_grads",
    )(*attn, *up, *down, *pieces)


def halves(value):
    high = value.astype(bf16)
    return high, (value - high.astype(f32)).astype(bf16)


def times(left, right):
    (left_high, left_low), (right_high, right_low) = left, right
    return dot_nn(
        jnp.concatenate([left_high, left_high, left_low], 1),
        jnp.concatenate([right_high, right_low, right_high], 0),
    )


def times_t(left, right):
    (left_high, left_low), (right_high, right_low) = left, right
    return dot_nt(
        jnp.concatenate([left_high, left_high, left_low], 1),
        jnp.concatenate([right_high, right_low, right_high], 1),
    )


def clip_of(norm):
    return jnp.minimum(1.0, 0.25 / (norm + 1e-06))


def muon_kernel(role_ref, square_ref, dout_ref, whole_ref, mom_ref, out_ref, norm_ref, x_s, q_s, gram_s, high_s, low_s):
    count, rows = whole_ref.shape[0], whole_ref.shape[2]
    core = role_ref[1]
    dout = dout_ref[...]
    norm = jnp.sqrt(square_ref[0:1, 0:1] + jnp.sum(jnp.sum(dout * dout, 0, keepdims=True), 1, keepdims=True))
    norm_ref[...] = jnp.broadcast_to(norm, norm_ref.shape)
    clip = clip_of(norm)
    eye = (
        lax.broadcasted_iota(jnp.int32, (D, D), 0) == lax.broadcasted_iota(jnp.int32, (D, D), 1)
    ).astype(f32)

    @pl.when(role_ref[0] == 1)
    def _():
        start = (0.5 * mom_ref[:, core].astype(f32)).reshape(D, D)
        start = start + clip * whole_ref[:, 0].astype(f32).reshape(D, D)
        size = jnp.sum(jnp.sum(start * start, 0, keepdims=True), 1, keepdims=True)
        x_s[...] = start / (jnp.sqrt(size) + 1e-07)

        def sweep(_, carry):
            value = x_s[...]
            both = halves(value)
            gram = times_t(both, both)
            gram_both = halves(gram)
            poly = -4.775 * gram + 2.0315 * times(gram_both, gram_both)
            x_s[...] = 3.4445 * value + times(halves(poly), both)
            return carry

        lax.fori_loop(0, 5, sweep, 0)
        out_ref[:, 0] = x_s[...].astype(bf16).reshape(count, rows, D)

    @pl.when(role_ref[0] == 2)
    def _():
        gram_s[...] = jnp.zeros_like(gram_s)

        def gather(tile, size):
            value = (0.5 * mom_ref[:, 2 + tile].astype(f32)).reshape(D, D)
            value = value + clip * whole_ref[:, tile].astype(f32).reshape(D, D)
            high, low = halves(value)
            high_s[tile] = high
            low_s[tile] = low

            @pl.when(role_ref[2] == 1)
            def _():
                high_s[tile] = jnp.transpose(high_s[tile])
                low_s[tile] = jnp.transpose(low_s[tile])

            both = high_s[tile], low_s[tile]
            gram_s[...] += times_t(both, both)
            return size + jnp.sum(jnp.sum(value * value, 0, keepdims=True), 1, keepdims=True)

        size = lax.fori_loop(0, 4, gather, jnp.zeros((1, 1), f32))
        scale = 1.0 / (jnp.sqrt(size) + 1e-07)
        gram_s[...] = gram_s[...] * (scale * scale)

        def poly_of(gram, gram_both):
            return 3.4445 * eye - 4.775 * gram + 2.0315 * times(gram_both, gram_both)

        def advance(gram_both, poly_both):
            gram_s[...] = times(halves(times(gram_both, poly_both)), poly_both)

        gram = gram_s[...]
        gram_both = halves(gram)
        poly = poly_of(gram, gram_both)
        q_s[...] = poly
        advance(gram_both, halves(poly))

        def sweep(_, carry):
            gram = gram_s[...]
            gram_both = halves(gram)
            poly_both = halves(poly_of(gram, gram_both))
            q_s[...] = times(halves(q_s[...]), poly_both)
            advance(gram_both, poly_both)
            return carry

        lax.fori_loop(0, 3, sweep, 0)
        gram = gram_s[...]
        last = times(halves(q_s[...]), halves(poly_of(gram, halves(gram)))) * scale
        last_both = halves(last)

        def finish(step, carry):
            tile = 2 * core + step
            x_s[...] = times(last_both, (high_s[tile], low_s[tile]))

            @pl.when(role_ref[2] == 1)
            def _():
                x_s[...] = jnp.transpose(x_s[...])

            out_ref[:, step] = x_s[...].astype(bf16).reshape(count, rows, D)
            return carry

        lax.fori_loop(0, 2, finish, 0)


def muon(role, squares, dout, whole, momenta):
    count, _, rows, _ = whole.shape
    return pl.pallas_call(
        muon_kernel,
        out_shape=[jax.ShapeDtypeStruct((count, 2, rows, D), bf16), jax.ShapeDtypeStruct((8, 128), f32)],
        in_specs=[pl.BlockSpec(memory_space=pltpu.SMEM)] + [pl.BlockSpec(memory_space=pltpu.VMEM)] * 4,
        out_specs=[pl.BlockSpec(memory_space=pltpu.VMEM)] * 2,
        scratch_shapes=[
            pltpu.VMEM((D, D), f32),
            pltpu.VMEM((D, D), f32),
            pltpu.VMEM((D, D), f32),
            pltpu.VMEM((4, D, D), bf16),
            pltpu.VMEM((4, D, D), bf16),
        ],
        compiler_params=pltpu.CompilerParams(vmem_limit_bytes=VMEM_LIMIT),
        cost_estimate=pl.CostEstimate(flops=2 * 10**10, bytes_accessed=10**7, transcendentals=0),
        name="muon",
    )(role, squares, dout, whole, momenta)


def spread_kernel(count, made_ref, every_ref, send, recv, on_send, on_recv):
    seg, dp, core, x, y, across_core, near, far = peers()
    group = 2 * y + x
    greet(seg, count, near, ())
    roles = owners(count)

    def gift(place, other):
        first, width, owner, spot = roles[place]
        return remote(
            made_ref.at[other, 0:width],
            every_ref.at[group, first : first + width],
            send.at[other],
            recv.at[place],
            {"seg": other},
        )

    def onward(place, side):
        first, width, owner, spot = roles[place]
        block = every_ref.at[group, first : first + width]
        return remote(block, block, on_send.at[side, place], on_recv.at[side, place], near[side])

    for place, (first, width, owner, spot) in enumerate(roles):

        @pl.when(seg == owner)
        def _():
            for other in others(seg, count):
                gift(place, other).start()
            every_ref[group, first : first + width] = made_ref[seg, 0:width]

    for place, (first, width, owner, spot) in enumerate(roles):

        @pl.when(seg != owner)
        def _():
            wait_bytes(every_ref.at[group, first : first + width], recv.at[place])

        for side in range(3):
            onward(place, side).start()
    for place, (first, width, owner, spot) in enumerate(roles):
        for side in range(3):
            onward(place, side).wait()

        @pl.when(seg == owner)
        def _():
            for other in others(seg, count):
                gift(place, other).wait_send()


def spread(count, made):
    rows = made.shape[2]
    dma = pltpu.SemaphoreType.DMA
    return pl.pallas_call(
        functools.partial(spread_kernel, count),
        out_shape=jax.ShapeDtypeStruct((GROUPS, UNITS, rows, D), bf16),
        in_specs=[pl.BlockSpec(memory_space=pltpu.VMEM)],
        out_specs=pl.BlockSpec(memory_space=pltpu.VMEM),
        scratch_shapes=[dma((count,)), dma((4,)), dma((3, 4)), dma((3, 4))],
        compiler_params=pltpu.CompilerParams(
            collective_id=2, has_side_effects=True, vmem_limit_bytes=VMEM_LIMIT
        ),
        cost_estimate=pl.CostEstimate(flops=10**6, bytes_accessed=4 * 10**7, transcendentals=0),
        name="spread",
    )(made)


def embed_kernel(
    count,
    frames_ref,
    mask_ref,
    in_ref,
    outer_ref,
    x_ref,
    mem_ref,
    total_ref,
    got_s,
    count_s,
    frame_send,
    frame_recv,
    count_send,
    count_recv,
):
    seg = lax.axis_index("seg")
    after, before = lax.rem(seg + 1, count), lax.rem(seg + count - 1, count)
    streams = frames_ref.shape[0]
    tally = jnp.sum(mask_ref[...].astype(f32), 1, keepdims=True)
    count_s[seg] = jnp.broadcast_to(
        jnp.concatenate([tally, jnp.zeros((8 - streams, 1), f32)], 0), (8, 128)
    )
    greet(seg, count, (), ())
    frame_copy = remote(frames_ref, got_s, frame_send.at[0], frame_recv.at[0], {"seg": after})
    frame_copy.start()
    for step, other in enumerate(others(seg, count)):
        remote(count_s.at[seg], count_s.at[seg], count_send.at[step], count_recv.at[seg], {"seg": other}).start()
    weight, shift = in_ref[...], outer_ref[0:1, :]
    for stream in range(streams):
        x_ref[stream] = dot_nn(jnp.transpose(frames_ref[stream]), weight) + shift
    frame_copy.wait()
    for stream in range(streams):
        mem_ref[stream] = (dot_nn(jnp.transpose(got_s[stream]), weight) + shift).astype(bf16)
    for other in others(seg, count):
        wait_bytes(count_s.at[other], count_recv.at[other])
    total_ref[...] = jnp.sum(count_s[...], 0)
    for step in range(count - 1):
        wait_bytes(count_s.at[0], count_send.at[step])


def embed(count, frames, mask, in_weight, outer_vectors):
    streams = frames.shape[0]
    dma = pltpu.SemaphoreType.DMA
    return pl.pallas_call(
        functools.partial(embed_kernel, count),
        out_shape=[
            jax.ShapeDtypeStruct((streams, SEG, D), f32),
            jax.ShapeDtypeStruct((streams, SEG, D), bf16),
            jax.ShapeDtypeStruct((8, 128), f32),
        ],
        in_specs=[pl.BlockSpec(memory_space=pltpu.VMEM)] * 4,
        out_specs=[pl.BlockSpec(memory_space=pltpu.VMEM)] * 3,
        scratch_shapes=[
            pltpu.VMEM(frames.shape, bf16),
            pltpu.VMEM((count, 8, 128), f32),
            dma((1,)),
            dma((1,)),
            dma((count,)),
            dma((count,)),
        ],
        compiler_params=pltpu.CompilerParams(
            collective_id=3, has_side_effects=True, vmem_limit_bytes=VMEM_LIMIT
        ),
        cost_estimate=pl.CostEstimate(flops=2 * 10**8, bytes_accessed=4 * 10**6, transcendentals=0),
        name="embed",
    )(frames, mask, in_weight, outer_vectors)


FEED_UP = (1, 0)
FEED_DOWN = (2, 3)
KEEP = 1.0 - 0.3 * 0.01


def finish_kernel(norm_ref, every_ref, update_ref, dout_ref, small_ref, *refs):
    (
        attn_ref,
        attn_mom_ref,
        up_ref,
        up_mom_ref,
        down_ref,
        down_mom_ref,
        out_ref,
        out_mom_ref,
        out_sec_ref,
        in_ref,
        in_mom_ref,
        in_sec_ref,
        vec_ref,
        vec_mom_ref,
        vec_sec_ref,
        outer_ref,
        outer_mom_ref,
        outer_sec_ref,
        attn_new,
        attn_mom_new,
        attn_copy_new,
        up_new,
        up_mom_new,
        up_copy_new,
        down_new,
        down_mom_new,
        down_copy_new,
        out_new,
        out_mom_new,
        out_sec_new,
        out_copy_new,
        in_new,
        in_mom_new,
        in_sec_new,
        in_copy_new,
        vec_new,
        vec_mom_new,
        vec_sec_new,
        outer_new,
        outer_mom_new,
        outer_sec_new,
    ) = refs
    clip = clip_of(norm_ref[0:1, 0:1])

    def muon_step(weight, momentum, grad, update, scale):
        weight = weight * KEEP - (0.3 * scale) * update.astype(f32)
        return weight, 0.5 * momentum + clip * grad.astype(f32)

    up_scale, down_scale = max(1.0, FF / D) ** 0.5, max(1.0, D / FF) ** 0.5
    for depth in range(LAYERS):
        for kind in range(4):
            weight, momentum = muon_step(
                attn_ref[depth, kind],
                attn_mom_ref[depth, kind],
                every_ref[kind, depth],
                update_ref[kind, depth],
                1.0,
            )
            attn_new[depth, kind] = weight
            attn_mom_new[depth, kind] = momentum
            attn_copy_new[depth, kind] = weight.astype(bf16)
            columns = slice(kind * TILE, (kind + 1) * TILE)
            weight, momentum = muon_step(
                up_ref[depth, :, columns],
                up_mom_ref[depth, :, columns],
                every_ref[FEED_UP[depth], 2 + kind],
                update_ref[FEED_UP[depth], 2 + kind],
                up_scale,
            )
            up_new[depth, :, columns] = weight
            up_mom_new[depth, :, columns] = momentum
            up_copy_new[depth, :, columns] = weight.astype(bf16)
            weight, momentum = muon_step(
                down_ref[depth, kind],
                down_mom_ref[depth, kind],
                every_ref[FEED_DOWN[depth], 2 + kind],
                update_ref[FEED_DOWN[depth], 2 + kind],
                down_scale,
            )
            down_new[depth, kind] = weight
            down_mom_new[depth, kind] = momentum
            down_copy_new[depth, kind] = weight.astype(bf16)
    weight, moment, second = adamw(out_ref[...], out_mom_ref[...], out_sec_ref[...], dout_ref[...] * clip, 0.05, 0.01)
    out_new[...] = weight
    out_mom_new[...] = moment
    out_sec_new[...] = second
    out_copy_new[...] = weight.astype(bf16)

    @pl.when(pl.program_id(0) == 0)
    def _():
        inputs = in_ref.shape[0]
        weight, moment, second = adamw(
            in_ref[...], in_mom_ref[...], in_sec_ref[...], small_ref[0:inputs, :] * clip, 0.05, 0.01
        )
        in_new[...] = weight
        in_mom_new[...] = moment
        in_sec_new[...] = second
        in_copy_new[...] = weight.astype(bf16)

        def rows_of(first, last, base):
            return small_ref[inputs + base + first : inputs + base + last, :]

        for depth in range(LAYERS):
            base = 16 * depth
            for low, high, grad in (
                (0, 2, rows_of(0, 2, base)),
                (2, 4, rows_of(0, 2, base + 8)),
                (4, 7, rows_of(2, 5, base)),
                (7, 8, rows_of(2, 3, base + 8)),
                (8, 12, rows_of(4, 8, base + 8)),
            ):
                weight, moment, second = adamw(
                    vec_ref[depth, low:high],
                    vec_mom_ref[depth, low:high],
                    vec_sec_ref[depth, low:high],
                    grad * clip,
                    0.25,
                    0.0,
                )
                vec_new[depth, low:high] = weight
                vec_mom_new[depth, low:high] = moment
                vec_sec_new[depth, low:high] = second
        for low, high, grad in ((0, 1, rows_of(5, 6, 0)), (1, 5, rows_of(1, 5, 32))):
            weight, moment, second = adamw(
                outer_ref[low:high, :], outer_mom_ref[low:high, :], outer_sec_ref[low:high, :], grad * clip, 0.25, 0.0
            )
            outer_new[low:high, :] = weight
            outer_mom_new[low:high, :] = moment
            outer_sec_new[low:high, :] = second


def finish(rows, norm, every, updates, dout, small, arrays):
    steps = rows // 16
    attn, _, up, _, down, _, out, _, _, inp, _, _, vec, _, _, outer, _, _ = arrays
    codes = out.shape[1]
    blocks = pl.BlockSpec((GROUPS, UNITS, 16, D), lambda i: (0, 0, i, 0))
    attn_spec = pl.BlockSpec((LAYERS, 4, 16, D), lambda i: (0, 0, i, 0))
    up_spec = pl.BlockSpec((LAYERS, 16, FF), lambda i: (0, i, 0))
    out_spec = pl.BlockSpec((D // steps, codes), lambda i: (i, 0))
    in_spec, vec_spec, outer_spec = whole_spec(inp.shape), whole_spec(vec.shape), whole_spec(outer.shape)

    def like(array, dtype=f32):
        return jax.ShapeDtypeStruct(array.shape, dtype)

    return pl.pallas_call(
        finish_kernel,
        grid=(steps,),
        out_shape=[like(attn), like(attn), like(attn, bf16)]
        + [like(up), like(up), like(up, bf16)]
        + [like(down), like(down), like(down, bf16)]
        + [like(out)] * 3
        + [like(out, bf16)]
        + [like(inp)] * 3
        + [like(inp, bf16)]
        + [like(vec)] * 3
        + [like(outer)] * 3,
        in_specs=[whole_spec((8, 128)), blocks, blocks, out_spec, whole_spec(small.shape)]
        + [attn_spec] * 2
        + [up_spec] * 2
        + [attn_spec] * 2
        + [out_spec] * 3
        + [in_spec] * 3
        + [vec_spec] * 3
        + [outer_spec] * 3,
        out_specs=[attn_spec] * 3
        + [up_spec] * 3
        + [attn_spec] * 3
        + [out_spec] * 4
        + [in_spec] * 4
        + [vec_spec] * 3
        + [outer_spec] * 3,
        compiler_params=pltpu.CompilerParams(vmem_limit_bytes=VMEM_LIMIT),
        cost_estimate=pl.CostEstimate(flops=10**8, bytes_accessed=4 * 10**7, transcendentals=0),
        name="finish",
    )(norm, every, updates, dout, small, *arrays)


def local(
    frames,
    speech_mask,
    targets,
    in_proj,
    in_moment,
    in_second,
    out_proj,
    out_moment,
    out_second,
    layer_vectors,
    vectors_moment,
    vectors_second,
    outer_vectors,
    outer_moment,
    outer_second,
    attn_proj,
    attn_momentum,
    ff_up,
    up_momentum,
    ff_down,
    down_momentum,
    in_copy,
    out_copy,
    attn_copy,
    up_copy,
    down_copy,
):
    segment = lax.axis_index("seg")
    count, dp_count = lax.axis_size("seg"), lax.axis_size("dp")
    rows = D // count
    streams = frames.shape[0]
    stream_total = streams * dp_count
    group = lax.axis_index("dp") % GROUPS
    feeds = jnp.stack(
        [
            jnp.swapaxes(up_momentum[1].reshape(rows, 4, D), 0, 1),
            jnp.swapaxes(up_momentum[0].reshape(rows, 4, D), 0, 1),
            down_momentum[0].reshape(4, rows, D),
            down_momentum[1].reshape(4, rows, D),
        ]
    )
    owned = jnp.concatenate(
        [
            lax.dynamic_index_in_dim(attn_momentum, group, 1, keepdims=False),
            lax.dynamic_index_in_dim(feeds, group, 0, keepdims=False),
        ],
        0,
    ).astype(bf16)
    momenta = lax.all_gather(owned, "seg", axis=0, tiled=False)
    frames_t = jnp.swapaxes(frames, 1, 2)
    bias = jnp.where(segment > 0, 0.0, -1e30).astype(f32)[None]
    hidden, memory, totals = embed(count, frames_t, speech_mask, in_copy, outer_vectors)
    memory = [memory] * streams
    kept = []
    for depth in range(LAYERS):
        saved, passed = None, []
        for stream in range(streams):
            saved, short = forward_layer(
                depth,
                stream,
                streams,
                bias,
                hidden,
                memory[stream],
                attn_copy,
                up_copy,
                down_copy,
                layer_vectors,
                saved,
            )
            if depth + 1 < LAYERS:
                passed.append(from_behind(short, "seg", 1))
        kept.append((hidden, memory[0] if depth == 0 else jnp.stack(memory), saved))
        hidden = saved[0]
        memory = passed
    grad_hidden, grad_out, head_outer = head(
        hidden, targets, speech_mask, totals, out_copy, outer_vectors, 1.0 / stream_total, momenta
    )
    grad_out = lax.psum(grad_out, ("seg", "dp"))
    attn_grads, up_grads, down_grads, vector_grads = ([], [], [], [])
    for depth in reversed(range(LAYERS)):
        entering, held, saved = kept[depth]
        dafter, grad_up, grad_down, feed_vec = feed_back(
            depth, grad_hidden, saved[7], up_copy, down_copy, layer_vectors
        )
        grad_hidden, grad_attn, attn_vec, grad_in = attend_back(
            depth, bias, dafter, entering, held, saved[1:7], attn_copy, layer_vectors, frames_t
        )
        attn_grads.insert(0, grad_attn)
        up_grads.insert(0, grad_up)
        down_grads.insert(0, grad_down)
        vector_grads = [attn_vec, feed_vec] + vector_grads
    whole, every, small, squares = reduce_grads(
        count, dp_count, attn_grads, up_grads, down_grads, [grad_in] + vector_grads + [head_outer]
    )
    loss_sum = small[grad_in.shape[0] + 37, 0]
    plane, core = segment // 2, segment % 2
    kind = jnp.where(plane == count // 4 - 1, 1, jnp.where(plane == count // 4, 2, 0))
    role = jnp.stack([kind, core, (group >= 2).astype(jnp.int32), core]).astype(jnp.int32)
    made, norm = muon(role, squares, grad_out, whole, momenta)
    updates = spread(count, made)
    split = (LAYERS, 4, rows, D)
    (
        attn_new,
        attn_mom,
        attn_copy_new,
        up_new,
        up_mom,
        up_copy_new,
        down_new,
        down_mom,
        down_copy_new,
        out_new,
        out_moment_new,
        out_second_new,
        out_copy_new,
        in_new,
        in_moment_new,
        in_second_new,
        in_copy_new,
        vectors_new,
        vectors_moment_new,
        vectors_second_new,
        outer_new,
        outer_moment_new,
        outer_second_new,
    ) = finish(
        rows,
        norm,
        every,
        updates,
        grad_out,
        small,
        [
            attn_proj,
            attn_momentum,
            ff_up,
            up_momentum,
            ff_down.reshape(split),
            down_momentum.reshape(split),
            out_proj,
            out_moment,
            out_second,
            in_proj,
            in_moment,
            in_second,
            layer_vectors,
            vectors_moment,
            vectors_second,
            outer_vectors,
            outer_moment,
            outer_second,
        ],
    )
    return (
        loss_sum,
        norm[0, 0],
        in_new,
        in_moment_new,
        in_second_new,
        out_new,
        out_moment_new,
        out_second_new,
        vectors_new,
        vectors_moment_new,
        vectors_second_new,
        outer_new,
        outer_moment_new,
        outer_second_new,
        attn_new,
        attn_mom,
        up_new,
        up_mom,
        down_new.reshape(ff_down.shape),
        down_mom.reshape(ff_down.shape),
        in_copy_new,
        out_copy_new,
        attn_copy_new,
        up_copy_new,
        down_copy_new.reshape(ff_down.shape),
    )


def solution(mesh):
    return jax.shard_map(
        local,
        mesh=mesh,
        in_specs=(
            P("dp", "seg", None),
            P("dp", "seg"),
            P("dp", "seg"),
            P(),
            P(),
            P(),
            P(),
            P(),
            P(),
            P(),
            P(),
            P(),
            P(),
            P(),
            P(),
            P(None, None, "seg", None),
            P(None, None, "seg", None),
            P(None, "seg", None),
            P(None, "seg", None),
            P(None, "seg", None),
            P(None, "seg", None),
            P(),
            P(),
            P(),
            P(),
            P(),
        ),
        out_specs=(
            P(),
            P(),
            P(),
            P(),
            P(),
            P(),
            P(),
            P(),
            P(),
            P(),
            P(),
            P(),
            P(),
            P(),
            P(None, None, "seg", None),
            P(None, None, "seg", None),
            P(None, "seg", None),
            P(None, "seg", None),
            P(None, "seg", None),
            P(None, "seg", None),
            P(),
            P(),
            P(None, None, "seg", None),
            P(None, "seg", None),
            P(None, "seg", None),
        ),
        check_vma=False,
    )
```

```python
import functools
import math

import jax
import jax.numpy as jnp
from jax import lax
from jax.experimental import pallas as pl
from jax.experimental.pallas import tpu as pltpu
from jax.sharding import PartitionSpec as P

D = 512
HEAD_DIM = 64
HEADS = D // HEAD_DIM
FF = 2048
LAYERS = 2
STEP = 10
SEG = 512
HALF = 256
PAIR = 2 * HEAD_DIM
TILE = 512
VMEM_LIMIT = 56 * 1024 * 1024
GELU_SCALE = math.sqrt(2.0 / math.pi)

f32 = jnp.float32
bf16 = jnp.bfloat16


def dot_nn(left, right):
    return lax.dot_general(left, right, (((1,), (0,)), ((), ())), preferred_element_type=f32)


def dot_nt(left, right):
    return lax.dot_general(left, right, (((1,), (1,)), ((), ())), preferred_element_type=f32)


def dot_tn(left, right):
    return lax.dot_general(left, right, (((0,), (0,)), ((), ())), preferred_element_type=f32)


def normalised(values):
    centred = values - jnp.mean(values, -1, keepdims=True)
    scale = lax.rsqrt(jnp.mean(centred * centred, -1, keepdims=True) + 1e-05)
    return centred * scale, scale


def norm_back(grad, gain, unit, scale):
    part = grad * gain
    mean_part = jnp.mean(part, -1, keepdims=True)
    mean_unit = jnp.mean(part * unit, -1, keepdims=True)
    return scale * (part - mean_part - unit * mean_unit)


def column_sum(values):
    return jnp.sum(values, 0, keepdims=True)


def head_masks():
    lane = lax.broadcasted_iota(jnp.int32, (1, PAIR), 1)
    return (lane < HEAD_DIM).astype(bf16), (lane >= HEAD_DIM).astype(bf16)


def pair_lanes(pair):
    return pl.ds(pl.multiple_of(pair * PAIR, PAIR), PAIR)


def forward_kernel(
    bias_ref,
    x_ref,
    mem_ref,
    attn_ref,
    up_ref,
    down_ref,
    vec_ref,
    *refs,
):
    hid_ref, hid16_ref, keyin_ref, q_ref, k_ref, v_ref, lse_ref, mixed_ref, after_ref, act_s, lse_s = refs[-11:]
    x = x_ref[...]
    own_unit, _ = normalised(x)
    gain, shift = vec_ref[0:1, :], vec_ref[1:2, :]
    normed = (own_unit * gain + shift).astype(bf16)
    mem_unit, _ = normalised(mem_ref[...].astype(f32))
    mem_normed = (mem_unit * gain + shift).astype(bf16)
    keyin_ref[0:SEG, :] = mem_normed
    keyin_ref[SEG:, :] = normed
    q_ref[...] = (dot_nn(normed, attn_ref[0]) + vec_ref[4:5, :]).astype(bf16) * jnp.asarray(HEAD_DIM**-0.5, bf16)
    k_ref[0:SEG, :] = dot_nn(mem_normed, attn_ref[1]).astype(bf16)
    k_ref[SEG:, :] = dot_nn(normed, attn_ref[1]).astype(bf16)
    v_ref[0:SEG, :] = (dot_nn(mem_normed, attn_ref[2]) + vec_ref[5:6, :]).astype(bf16)
    v_ref[SEG:, :] = (dot_nn(normed, attn_ref[2]) + vec_ref[5:6, :]).astype(bf16)
    first, second = head_masks()
    memory_bias = bias_ref[0]
    lane = lax.broadcasted_iota(jnp.int32, (HALF, PAIR), 1)
    query_pos = lax.broadcasted_iota(jnp.int32, (2 * HALF, HALF), 0) % HALF
    key_pos = lax.broadcasted_iota(jnp.int32, (2 * HALF, HALF), 1)
    diagonal = key_pos <= query_pos
    lse_s[...] = jnp.zeros_like(lse_s)

    def pair_body(pair, carry):
        lanes = pair_lanes(pair)
        for block in range(2):
            rows = slice(block * HALF, (block + 1) * HALF)
            q_pair = q_ref[rows, lanes]
            q_both = jnp.concatenate([q_pair * first, q_pair * second], 0)
            spans = [(0, SEG, 0)]
            if block:
                spans.append((SEG, SEG + HALF, 1))
            spans.append((SEG + block * HALF, SEG + (block + 1) * HALF, 2))
            scores = []
            for low, high, kind in spans:
                part = dot_nt(q_both, k_ref[low:high, lanes])
                if kind == 0:
                    part = part + memory_bias
                if kind == 2:
                    part = jnp.where(diagonal, part, -1e30)
                scores.append(part)
            most = functools.reduce(jnp.maximum, [jnp.max(part, -1, keepdims=True) for part in scores])
            weights = [jnp.exp(part - most) for part in scores]
            total = functools.reduce(jnp.add, [jnp.sum(part, -1, keepdims=True) for part in weights])
            mixed = functools.reduce(
                jnp.add,
                [
                    dot_nn(part.astype(bf16), v_ref[low:high, lanes])
                    for part, (low, high, kind) in zip(weights, spans)
                ],
            )
            mixed = mixed / total
            mixed_ref[rows, lanes] = jnp.where(lane < HEAD_DIM, mixed[:HALF], mixed[HALF:]).astype(bf16)
            lse = most + jnp.log(total)
            kept = jnp.where(lane == 2 * pair, lse[:HALF], lse_s[rows, :])
            lse_s[rows, :] = jnp.where(lane == 2 * pair + 1, lse[HALF:], kept)
        return carry

    lax.fori_loop(0, HEADS // 2, pair_body, 0)
    lse_ref[...] = jnp.transpose(lse_s[...])[0:HEADS, :]
    after = x + (dot_nn(mixed_ref[...], attn_ref[3]) + vec_ref[6:7, :])
    after_ref[...] = after
    unit, _ = normalised(after)
    normed_two = (unit * vec_ref[2:3, :] + vec_ref[3:4, :]).astype(bf16)
    for tile in range(FF // TILE):
        columns = slice(tile * TILE, (tile + 1) * TILE)
        inner = dot_nn(normed_two, up_ref[:, columns]) + vec_ref[8 + tile : 9 + tile, :]
        act_s[:, columns] = (
            0.5 * inner * (1.0 + jnp.tanh(GELU_SCALE * (inner + 0.044715 * inner * inner * inner)))
        ).astype(bf16)
    hidden = after + (dot_nn(act_s[...], down_ref[...]) + vec_ref[7:8, :])
    hid_ref[...] = hidden
    hid16_ref[...] = hidden.astype(bf16)


SAVED = (
    ((SEG, D), f32),
    ((2 * SEG, D), bf16),
    ((SEG, D), bf16),
    ((2 * SEG, D), bf16),
    ((2 * SEG, D), bf16),
    ((HEADS, SEG), f32),
    ((SEG, D), bf16),
    ((SEG, D), f32),
)


def whole_spec(shape):
    return pl.BlockSpec(shape, lambda *_: (0,) * len(shape))


def stream_spec(shape, stream=None):
    zeros = (0,) * len(shape)
    if stream is None:
        return pl.BlockSpec((None,) + shape, lambda i: (i,) + zeros)
    return pl.BlockSpec((None,) + shape, lambda i: (stream,) + zeros)


def layer_spec(shape, depth):
    zeros = (0,) * len(shape)
    return pl.BlockSpec((None,) + shape, lambda *_: (depth,) + zeros)


def forward_layer(depth, stream, streams, bias, hidden, memory, attn, upper, lower, vectors, earlier):
    saved_shapes = [jax.ShapeDtypeStruct((streams,) + shape, dtype) for shape, dtype in SAVED]
    saved_specs = [stream_spec(shape, stream) for shape, dtype in SAVED]
    out_shape = [saved_shapes[0], jax.ShapeDtypeStruct((SEG, D), bf16)] + saved_shapes[1:]
    out_specs = [saved_specs[0], whole_spec((SEG, D))] + saved_specs[1:]
    operands = [bias, hidden, memory, attn, upper, lower, vectors]
    in_specs = [
        pl.BlockSpec(memory_space=pltpu.SMEM),
        stream_spec((SEG, D), stream),
        stream_spec((SEG, D), stream) if memory.ndim == 3 else whole_spec((SEG, D)),
        layer_spec(attn.shape[1:], depth),
        layer_spec(upper.shape[1:], depth),
        layer_spec(lower.shape[1:], depth),
        layer_spec(vectors.shape[1:], depth),
    ]
    aliases = {}
    if earlier is not None:
        for place, array in enumerate(earlier):
            aliases[len(operands)] = place if place == 0 else place + 1
            operands.append(array)
            in_specs.append(pl.BlockSpec(memory_space=pl.ANY))
    out = pl.pallas_call(
        forward_kernel,
        grid=(1,),
        out_shape=out_shape,
        in_specs=in_specs,
        out_specs=out_specs,
        scratch_shapes=[pltpu.VMEM((SEG, FF), bf16), pltpu.VMEM((SEG, PAIR), f32)],
        input_output_aliases=aliases,
        compiler_params=pltpu.CompilerParams(vmem_limit_bytes=VMEM_LIMIT),
        cost_estimate=pl.CostEstimate(flops=10**10, bytes_accessed=2 * 10**7, transcendentals=10**7),
        name="layer_forward",
    )(*operands)
    return [out[0]] + list(out[2:]), out[1]


def head_kernel(scale, x_ref, target_ref, mask_ref, total_ref, out_ref, outer_ref, bias_ref, mom_ref, g_ref, dout_ref, douter_ref, acc_s):
    step = pl.program_id(0)

    @pl.when(step == 0)
    def _():
        acc_s[...] = jnp.zeros_like(acc_s)
        douter_ref[...] = jnp.zeros_like(douter_ref)

    unit, rscale = normalised(x_ref[...])
    gain = outer_ref[1:2, :]
    normed = (unit * gain + outer_ref[2:3, :]).astype(bf16)
    logits = dot_nn(normed, out_ref[...]) + bias_ref[...]
    most = jnp.max(logits, -1, keepdims=True)
    powers = jnp.exp(logits - most)
    total = jnp.sum(powers, -1, keepdims=True)
    target_row = target_ref[pl.ds(step, 1), :].astype(f32)
    weight_row = mask_ref[pl.ds(step, 1), :].astype(f32) * (1.0 / total_ref[pl.ds(step, 1), 0:1])
    columns = jnp.transpose(jnp.concatenate([target_row, weight_row, jnp.zeros((6, SEG), f32)], 0))
    target, weight = columns[:, 0:1].astype(jnp.int32), columns[:, 1:2]
    chosen = lax.broadcasted_iota(jnp.int32, logits.shape, 1) == target
    picked = jnp.sum(jnp.where(chosen, logits, 0.0), -1, keepdims=True)
    loss = jnp.sum(weight * (most + jnp.log(total) - picked), 0, keepdims=True)
    spread = weight * scale
    dlogits = (powers * (spread / total) - jnp.where(chosen, spread, 0.0)).astype(bf16)
    acc_s[...] += dot_nn(jnp.transpose(normed), dlogits)
    bias_grad = column_sum(dlogits.astype(f32))
    dnormed = dot_nt(dlogits, out_ref[...])
    g_ref[...] = norm_back(dnormed, gain, unit, rscale)
    douter_ref[1:2, :] += column_sum(dnormed * unit)
    douter_ref[2:3, :] += column_sum(dnormed)
    douter_ref[3:4, :] += bias_grad[:, :D]
    douter_ref[4:5, :] += bias_grad[:, D:]
    douter_ref[5:6, :] += jnp.broadcast_to(loss, (1, D))

    @pl.when(step == pl.num_programs(0) - 1)
    def _():
        dout_ref[...] = acc_s[...]


def head(hidden, targets, mask, totals, out_weight, outer_vectors, scale, momenta):
    streams = hidden.shape[0]
    codes = out_weight.shape[1]
    bias = outer_vectors[3:].reshape(1, codes)
    return pl.pallas_call(
        functools.partial(head_kernel, scale),
        grid=(streams,),
        out_shape=[
            jax.ShapeDtypeStruct((streams, SEG, D), f32),
            jax.ShapeDtypeStruct((D, codes), f32),
            jax.ShapeDtypeStruct((8, D), f32),
        ],
        in_specs=[
            stream_spec((SEG, D)),
            whole_spec((streams, SEG)),
            whole_spec((streams, SEG)),
            whole_spec((8, 128)),
            whole_spec((D, codes)),
            whole_spec(outer_vectors.shape),
            whole_spec((1, codes)),
            pl.BlockSpec(memory_space=pl.ANY),
        ],
        out_specs=[stream_spec((SEG, D)), whole_spec((D, codes)), whole_spec((8, D))],
        scratch_shapes=[pltpu.VMEM((D, codes), f32)],
        compiler_params=pltpu.CompilerParams(vmem_limit_bytes=VMEM_LIMIT),
        cost_estimate=pl.CostEstimate(flops=33 * 10**8, bytes_accessed=10**7, transcendentals=10**6),
        name="head",
    )(hidden, targets, mask, totals, out_weight, outer_vectors, bias, momenta)


def feed_back_kernel(streams, carried, g_ref, after_ref, up_ref, down_ref, vec_ref, *refs):
    step = pl.program_id(0)
    tiles = FF // TILE
    if carried:
        grad_ref, refs = refs[0], refs[1:]
        dafter_ref, dup_ref, ddown_ref, dvec_ref, done_ref, up_s, down_s, act_s, inner_s = refs[:9]
        carry = AttnCarry(grad_ref, refs[9 : 9 + CARRY_REFS], refs[9 + CARRY_REFS :])

        @pl.when(step == 0)
        def _():
            hail(carry.targets)
            carry.load_all()

    else:
        dafter_ref, dup_ref, ddown_ref, dvec_ref, up_s, down_s, act_s, inner_s = refs

    @pl.when(step == 0)
    def _():
        up_s[...] = jnp.zeros_like(up_s)
        down_s[...] = jnp.zeros_like(down_s)
        dvec_ref[...] = jnp.zeros_like(dvec_ref)

    grad = g_ref[...]
    branch = grad.astype(bf16)
    dvec_ref[2:3, :] += column_sum(branch.astype(f32))
    unit, scale = normalised(after_ref[...])
    gain = vec_ref[2:3, :]
    normed = (unit * gain + vec_ref[3:4, :]).astype(bf16)
    for tile in range(FF // TILE):
        columns = slice(tile * TILE, (tile + 1) * TILE)
        inner = dot_nn(normed, up_ref[:, columns]) + vec_ref[8 + tile : 9 + tile, :]
        dact = dot_nt(branch, down_ref[columns, :])
        square = inner * inner
        bent = jnp.tanh(GELU_SCALE * (inner + 0.044715 * square * inner))
        half = 0.5 * (1.0 + bent)
        act_s[:, columns] = (inner * half).astype(bf16)
        slope = half + (0.5 * GELU_SCALE) * inner * (1.0 - bent * bent) * (1.0 + 0.134145 * square)
        dinner = (dact * slope).astype(bf16)
        inner_s[:, columns] = dinner
        dvec_ref[4 + tile : 5 + tile, :] += column_sum(dinner.astype(f32))
        if carried:
            if tile == 0:

                @pl.when(step == 0)
                def _():
                    meet(carry.targets)
                    carry.send_all()

            carry.tick(tiles * step + tile - 1)
    dnormed = dot_nt(inner_s[...], up_ref[...])
    dvec_ref[0:1, :] += column_sum(dnormed * unit)
    dvec_ref[1:2, :] += column_sum(dnormed)
    dafter_ref[...] = grad + norm_back(dnormed, gain, unit, scale)
    normed_t = jnp.transpose(normed)
    branch_t = jnp.transpose(branch)
    up_s[...] += dot_nn(normed_t, inner_s[...])
    down_s[...] += dot_nn(branch_t, act_s[...])

    @pl.when(step == pl.num_programs(0) - 1)
    def _():
        for tile in range(FF // TILE):
            dup_ref[tile] = up_s[:, tile * TILE : (tile + 1) * TILE].astype(bf16)
        ddown_ref[...] = jnp.transpose(down_s[...].astype(bf16))
        if carried:
            for time in range(tiles * streams - 1, carry.planes + 2):
                carry.tick(time)
            carry.finish(done_ref)


def feed_back(depth, grad, after, upper, lower, vectors, count, dp_count, attn_grad=None):
    streams = grad.shape[0]
    rows = D // count
    carried = attn_grad is not None
    in_specs = [
        stream_spec((SEG, D)),
        stream_spec((SEG, D)),
        layer_spec(upper.shape[1:], depth),
        layer_spec(lower.shape[1:], depth),
        layer_spec(vectors.shape[1:], depth),
    ]
    out_shape = [
        jax.ShapeDtypeStruct((streams, SEG, D), f32),
        jax.ShapeDtypeStruct((FF // TILE, D, TILE), bf16),
        jax.ShapeDtypeStruct((FF, D), bf16),
        jax.ShapeDtypeStruct((8, D), f32),
    ]
    out_specs = [
        stream_spec((SEG, D)),
        whole_spec((FF // TILE, D, TILE)),
        whole_spec((FF, D)),
        whole_spec((8, D)),
    ]
    scratch = [
        pltpu.VMEM((D, FF), f32),
        pltpu.VMEM((D, FF), f32),
        pltpu.VMEM((SEG, FF), bf16),
        pltpu.VMEM((SEG, FF), bf16),
    ]
    operands = [grad, after, upper, lower, vectors]
    params = {}
    if carried:
        in_specs.append(pl.BlockSpec(memory_space=pl.ANY))
        operands.append(attn_grad.reshape(2, 2, count, rows, D))
        out_shape.append(jax.ShapeDtypeStruct((rows, D), bf16))
        out_specs.append(whole_spec((rows, D)))
        scratch = scratch + carry_scratch("attn", count, dp_count)
        params = {"collective_id": 6, "has_side_effects": True}
    return pl.pallas_call(
        functools.partial(feed_back_kernel, streams, carried),
        grid=(streams,),
        out_shape=out_shape,
        in_specs=in_specs,
        out_specs=out_specs,
        scratch_shapes=scratch,
        compiler_params=pltpu.CompilerParams(vmem_limit_bytes=VMEM_LIMIT, **params),
        cost_estimate=pl.CostEstimate(flops=11 * 10**9, bytes_accessed=2 * 10**7, transcendentals=2 * 10**6),
        name="feed_back",
    )(*operands)


def attend_back_kernel(
    streams,
    depth,
    bias_ref,
    dafter_ref,
    x_ref,
    mem_ref,
    keyin_ref,
    q_ref,
    k_ref,
    v_ref,
    lse_ref,
    mixed_ref,
    attn_ref,
    vec_ref,
    frames_ref,
    dup_ref,
    ddown_ref,
    dx_ref,
    dattn_ref,
    dvec_ref,
    din_ref,
    done_ref,
    attn_s,
    dmixed_s,
    dq_s,
    dk_s,
    dv_s,
    ds_s,
    delta_s,
    *refs,
):
    step = pl.program_id(0)
    pairs = HEADS // 2
    carry = FeedCarry(depth, dup_ref, ddown_ref, refs[:CARRY_REFS], refs[CARRY_REFS:])

    @pl.when(step == 0)
    def _():
        hail(carry.targets)
        carry.load_all()
        attn_s[...] = jnp.zeros_like(attn_s)
        dvec_ref[...] = jnp.zeros_like(dvec_ref)
        din_ref[...] = jnp.zeros_like(din_ref)

    dafter = dafter_ref[...]
    branch = dafter.astype(bf16)
    dvec_ref[4:5, :] += column_sum(branch.astype(f32))
    dmixed = dot_nt(branch, attn_ref[3]).astype(bf16)
    dmixed_s[...] = dmixed
    attn_s[3] += dot_nn(jnp.transpose(mixed_ref[...]), branch)
    product = dmixed.astype(f32) * mixed_ref[...].astype(f32)
    high = product.astype(bf16)
    rest = (product - high.astype(f32)).astype(bf16)
    owner = lax.broadcasted_iota(jnp.int32, (HEADS, D), 1) // HEAD_DIM
    pick = (owner == lax.broadcasted_iota(jnp.int32, (HEADS, D), 0)).astype(bf16)
    delta_s[...] = dot_nt(pick, high) + dot_nt(pick, rest)
    first, second = head_masks()
    memory_bias = bias_ref[0]
    key_pos = lax.broadcasted_iota(jnp.int32, (HALF, 2 * HALF), 0)
    query_pos = lax.broadcasted_iota(jnp.int32, (HALF, 2 * HALF), 1) % HALF
    diagonal = key_pos <= query_pos
    head_row = lax.broadcasted_iota(jnp.int32, (PAIR, HALF), 0)

    @pl.when(step == 0)
    def _():
        meet(carry.targets)
        carry.send_all()

    def pair_body(pair, state):
        lanes = pair_lanes(pair)
        q_pair, do_pair = q_ref[:, lanes], dmixed_s[:, lanes]

        def spread(value):
            return jnp.concatenate(
                [value[:HALF] * first, value[:HALF] * second, value[HALF:] * first, value[HALF:] * second], 0
            )

        q_all, do_all = spread(q_pair), spread(do_pair)

        def rows_of(ref):
            one, two = ref[pl.ds(2 * pair, 1), :], ref[pl.ds(2 * pair + 1, 1), :]
            return jnp.concatenate([one[:, :HALF], two[:, :HALF], one[:, HALF:], two[:, HALF:]], 1)

        lse_all, delta_all = rows_of(lse_ref), rows_of(delta_s)
        for block in range(4):
            keys = slice(block * HALF, (block + 1) * HALF)
            start = 2 * HALF if block == 3 else 0
            scores = dot_nt(k_ref[keys, lanes], q_all[start:])
            if block < 2:
                scores = scores + memory_bias
            weights = jnp.exp(scores - lse_all[:, start:])
            if block == 2:
                weights = jnp.concatenate(
                    [jnp.where(diagonal, weights[:, : 2 * HALF], 0.0), weights[:, 2 * HALF :]], 1
                )
            if block == 3:
                weights = jnp.where(diagonal, weights, 0.0)
            dweights = dot_nt(v_ref[keys, lanes], do_all[start:])
            dscores = (weights * (dweights - delta_all[:, start:])).astype(bf16)
            dv_s[keys, lanes] = dot_nn(weights.astype(bf16), do_all[start:]).astype(bf16)
            dk_s[keys, lanes] = dot_nn(dscores, q_all[start:]).astype(bf16)
            ds_s[keys, start:] = dscores
        k_t = jnp.transpose(k_ref[:, lanes])
        for block in range(2):
            seen = SEG + (block + 1) * HALF
            grads = dot_nn(k_t[:, :seen], ds_s[:seen, block * 2 * HALF : (block + 1) * 2 * HALF])
            grads = jnp.where(head_row < HEAD_DIM, grads[:, :HALF], grads[:, HALF:])
            dq_s[block * HALF : (block + 1) * HALF, lanes] = (
                jnp.transpose(grads) * (HEAD_DIM**-0.5)
            ).astype(bf16)
        carry.tick(pairs * step + pair)
        return state

    lax.fori_loop(0, pairs, pair_body, 0)
    dq, dk, dv = dq_s[...], dk_s[...], dv_s[...]
    keyin_t = jnp.transpose(keyin_ref[...])
    attn_s[0] += dot_nn(keyin_t[:, SEG:], dq)
    attn_s[1] += dot_nn(keyin_t, dk)
    attn_s[2] += dot_nn(keyin_t, dv)
    dvec_ref[2:3, :] += column_sum(dq.astype(f32))
    dvec_ref[3:4, :] += column_sum(dv.astype(f32))
    dkeyin = dot_nt(dk, attn_ref[1]) + dot_nt(dv, attn_ref[2])
    dmem = dkeyin[:SEG]
    down = dkeyin[SEG:] + dot_nt(dq, attn_ref[0])
    gain = vec_ref[0:1, :]
    unit, scale = normalised(x_ref[...])
    mem_unit, _ = normalised(mem_ref[...].astype(f32))
    dvec_ref[0:1, :] += column_sum(down * unit + dmem * mem_unit)
    dvec_ref[1:2, :] += column_sum(down + dmem)
    dx = dafter + norm_back(down, gain, unit, scale)
    dx_ref[...] = dx
    if depth == 0:
        dx_high = dx.astype(bf16)
        dx_rest = (dx - dx_high.astype(f32)).astype(bf16)
        din_ref[...] += dot_nn(frames_ref[...], dx_high) + dot_nn(frames_ref[...], dx_rest)
        dvec_ref[5:6, :] += column_sum(dx)

    @pl.when(step == pl.num_programs(0) - 1)
    def _():
        dattn_ref[...] = attn_s[...].astype(bf16)
        for time in range(pairs * streams, carry.planes + 2):
            carry.tick(time)
        carry.finish(done_ref)


def attend_back(depth, bias, dafter, x, memory, saved, attn, vectors, frames, up_grad, down_grad, count, dp_count):
    streams = dafter.shape[0]
    keyin, q, k, v, lse, mixed = saved
    inputs = frames.shape[1]
    rows = D // count
    up_grad, down_grad = up_grad.reshape(4, count, rows, D), down_grad.reshape(count, 4, rows, D)
    return pl.pallas_call(
        functools.partial(attend_back_kernel, streams, depth),
        grid=(streams,),
        out_shape=[
            jax.ShapeDtypeStruct((streams, SEG, D), f32),
            jax.ShapeDtypeStruct((4, D, D), bf16),
            jax.ShapeDtypeStruct((8, D), f32),
            jax.ShapeDtypeStruct((inputs, D), f32),
            jax.ShapeDtypeStruct((4, rows, D), bf16),
        ],
        in_specs=[
            pl.BlockSpec(memory_space=pltpu.SMEM),
            stream_spec((SEG, D)),
            stream_spec((SEG, D)),
            stream_spec((SEG, D)),
            stream_spec((2 * SEG, D)),
            stream_spec((SEG, D)),
            stream_spec((2 * SEG, D)),
            stream_spec((2 * SEG, D)),
            stream_spec((HEADS, SEG)),
            stream_spec((SEG, D)),
            layer_spec(attn.shape[1:], depth),
            layer_spec(vectors.shape[1:], depth),
            stream_spec((inputs, SEG)),
            pl.BlockSpec(memory_space=pl.ANY),
            pl.BlockSpec(memory_space=pl.ANY),
        ],
        out_specs=[
            stream_spec((SEG, D)),
            whole_spec((4, D, D)),
            whole_spec((8, D)),
            whole_spec((inputs, D)),
            whole_spec((4, rows, D)),
        ],
        scratch_shapes=[
            pltpu.VMEM((4, D, D), f32),
            pltpu.VMEM((SEG, D), bf16),
            pltpu.VMEM((SEG, D), bf16),
            pltpu.VMEM((2 * SEG, D), bf16),
            pltpu.VMEM((2 * SEG, D), bf16),
            pltpu.VMEM((2 * SEG, 2 * SEG), bf16),
            pltpu.VMEM((HEADS, SEG), f32),
        ]
        + carry_scratch("feed", count, dp_count),
        compiler_params=pltpu.CompilerParams(
            collective_id=4 + depth, has_side_effects=True, vmem_limit_bytes=VMEM_LIMIT
        ),
        cost_estimate=pl.CostEstimate(flops=3 * 10**10, bytes_accessed=2 * 10**7, transcendentals=10**7),
        name="attend_back",
    )(bias, dafter, x, memory, keyin, q, k, v, lse, mixed, attn, vectors, frames, up_grad, down_grad)


def from_behind(value, axis, steps):
    count = lax.axis_size(axis)
    leading, last = (max(0, -steps), min(count, count - steps))
    return lax.ppermute(value, axis, [(source, source + steps) for source in range(leading, last)])


def adamw(weight, moment, second, grad, rate, decay):
    moment = 0.5 * moment + 0.5 * grad
    second = 0.99 * second + 0.01 * grad * grad
    fixed_moment = moment / (1.0 - 0.5**STEP)
    fixed_second = second / (1.0 - 0.99**STEP)
    weight = weight * (1.0 - rate * decay) - rate * fixed_moment / (jnp.sqrt(fixed_second) + 1e-08)
    return (weight, moment, second)


GROUPS = 4
UNITS = 6
SMALL = 128


def peers():
    count = {"seg": lax.axis_size("seg"), "dp": lax.axis_size("dp")}
    seg, dp = lax.axis_index("seg"), lax.axis_index("dp")
    core, x, y = seg % 2, dp % 2, (dp // 2) % 2
    across_core = {"seg": seg + 1 - 2 * core}
    across_x = {"dp": dp + 1 - 2 * x}
    across_y = {"dp": dp + 2 - 4 * y}
    across_both = {"dp": dp + 3 - 2 * x - 4 * y}
    far = []
    step = GROUPS
    while step < count["dp"]:
        far.append({"dp": dp + step - 2 * step * ((dp // step) % 2)})
        step *= 2
    return seg, dp, core, x, y, across_core, (across_x, across_y, across_both), far


def others(seg, count):
    return [lax.rem(seg + step, count) for step in range(1, count)]


def hail(targets):
    barrier = pltpu.get_barrier_semaphore()
    for target in targets:
        pl.semaphore_signal(barrier, inc=1, device_id=target, device_id_type=pl.DeviceIdType.MESH)


def meet(targets):
    pl.semaphore_wait(pltpu.get_barrier_semaphore(), len(targets))


def greet(seg, count, near, far):
    targets = [{"seg": other} for other in others(seg, count)] + list(near) + list(far)
    hail(targets)
    meet(targets)


def remote(source, target, send, recv, device):
    return pltpu.make_async_remote_copy(
        src_ref=source,
        dst_ref=target,
        send_sem=send,
        recv_sem=recv,
        device_id=device,
        device_id_type=pl.DeviceIdType.MESH,
    )


def wait_bytes(ref, sem):
    pltpu.make_async_copy(ref, ref, sem).wait()


def plus(left, right):
    return (left.astype(f32) + right.astype(f32)).astype(bf16)


def owners(count):
    attn, feed = count // 4 - 1, count // 4
    return (
        (0, 1, 2 * attn, 0),
        (1, 1, 2 * attn + 1, 0),
        (2, 2, 2 * feed, 0),
        (4, 2, 2 * feed + 1, 2),
    )


class Carry:
    def __init__(self, refs, sems):
        self.mine, self.got0, self.got1, self.got2, self.got3, self.goth = refs
        (
            self.load,
            self.send0,
            self.recv0,
            self.send1,
            self.recv1,
            self.send2,
            self.recv2,
            self.send3,
            self.recv3,
            self.sendh,
            self.recvh,
        ) = sems
        self.seg, self.dp, self.core, self.x, self.y, self.across_core, near, self.far = peers()
        self.across_x, self.across_y, _ = near
        self.planes = self.mine.shape[0]
        self.plane = self.seg // 2
        self.targets = [self.across_core, self.across_x, self.across_y] + self.far
        for step in range(1, self.planes):
            self.targets.append({"seg": 2 * lax.rem(self.plane + step, self.planes) + self.core})

    def block(self, step):
        return lax.rem(self.plane + 1 + step, self.planes)

    def load_all(self):
        for step in range(self.planes):
            for source, place in self.pieces(2 * self.block(step) + self.core):
                pltpu.make_async_copy(source, self.mine.at[(step,) + place], self.load.at[step]).start()

    def send_all(self):
        for step in range(self.planes):
            for source, place in self.pieces(2 * self.block(step) + 1 - self.core):
                remote(
                    source, self.got0.at[(step,) + place], self.send0.at[step], self.recv0.at[step], self.across_core
                ).start()

    def begin(self, step):
        wait_bytes(self.mine.at[step], self.load.at[step])
        wait_bytes(self.got0.at[step], self.recv0.at[step])
        for place in range(2):
            self.mine[step, place] = plus(self.mine[step, place], self.got0[step, place])
        for copy in self.first(step):
            copy.start()

    def across(self, place, step):
        return remote(
            self.held(step),
            self.goth.at[place, step],
            self.sendh.at[place, step],
            self.recvh.at[place, step],
            self.far[place],
        )

    def third(self, step):
        return remote(
            self.held(step),
            self.got3.at[self.plane],
            self.send3.at[step],
            self.recv3.at[self.plane],
            {"seg": 2 * self.block(step) + self.core},
        )

    def onward(self, step):
        for place in range(len(self.far)):
            copy = self.across(place, step)
            copy.start()
            copy.wait()
            held = self.held(step)
            held[...] = plus(held[...], self.goth[place, step])

        @pl.when(step < self.planes - 1)
        def _():
            self.third(step).start()

    def total(self):
        value = self.held(self.planes - 1)[...].astype(f32)
        for step in range(1, self.planes):
            sender = lax.rem(self.plane + step, self.planes)
            wait_bytes(self.got3.at[sender], self.recv3.at[sender])
            value = value + self.got3[sender].astype(f32)
        return value

    def tick(self, time):
        planes = self.planes

        @pl.when((time >= 0) & (time < planes))
        def _():
            self.begin(time)

        @pl.when((time >= 1) & (time < planes + 1))
        def _():
            self.middle(time - 1)

        @pl.when((time >= 2) & (time < planes + 2))
        def _():
            self.end(time - 2)


class AttnCarry(Carry):
    def __init__(self, source, refs, sems):
        super().__init__(refs, sems)
        self.source = source

    def pieces(self, row):
        return ((self.source.at[:, :, row], ()),)

    def held(self, step):
        return self.mine.at[step, self.y, self.x]

    def first(self, step):
        return (
            remote(
                self.mine.at[step, :, 1 - self.x],
                self.got1.at[step],
                self.send1.at[step],
                self.recv1.at[step],
                self.across_x,
            ),
        )

    def second(self, step):
        return remote(
            self.mine.at[step, 1 - self.y, self.x],
            self.got2.at[step],
            self.send2.at[step],
            self.recv2.at[step],
            self.across_y,
        )

    def middle(self, step):
        for copy in self.first(step):
            copy.wait_recv()
        for place in range(2):
            self.mine[step, place, self.x] = plus(self.mine[step, place, self.x], self.got1[step, place])
        self.second(step).start()

    def end(self, step):
        self.second(step).wait_recv()
        self.mine[step, self.y, self.x] = plus(self.mine[step, self.y, self.x], self.got2[step])
        self.onward(step)

    def finish(self, out_ref):
        value = self.total()
        out_ref[...] = value.astype(bf16)
        self.drain()

    def drain(self):
        for step in range(self.planes):
            wait_bytes(self.mine.at[step], self.send0.at[step])
            for copy in self.first(step):
                copy.wait_send()
            self.second(step).wait_send()
            if step < self.planes - 1:
                self.third(step).wait_send()


class FeedCarry(Carry):
    def __init__(self, depth, up, down, refs, sems):
        super().__init__(refs, sems)
        self.up, self.down = up, down
        self.owner = (self.x == self.y) if depth == 1 else (self.x != self.y)
        self.keep = self.x if depth == 1 else 1 - self.x

    def pieces(self, row):
        return ((self.up.at[:, row], (0,)), (self.down.at[row], (1,)))

    def held(self, step):
        return self.mine.at[step, self.y]

    def first(self, step):
        return (
            remote(
                self.mine.at[step, 1 - self.keep, 0:2],
                self.got1.at[step, 0],
                self.send1.at[step, 0],
                self.recv1.at[step, 0],
                self.across_x,
            ),
            remote(
                self.mine.at[step, 1 - self.y, 2:4],
                self.got1.at[step, 1],
                self.send1.at[step, 1],
                self.recv1.at[step, 1],
                self.across_y,
            ),
        )

    def second(self, step):
        return (
            remote(
                self.mine.at[step, self.keep, 0:2],
                self.got2.at[step, 0],
                self.send2.at[step, 0],
                self.recv2.at[step, 0],
                self.across_y,
            ),
            remote(
                self.mine.at[step, self.y, 2:4],
                self.got2.at[step, 1],
                self.send2.at[step, 1],
                self.recv2.at[step, 1],
                self.across_x,
            ),
        )

    def middle(self, step):
        for copy in self.first(step):
            copy.wait_recv()
        self.mine[step, self.keep, 0:2] = plus(self.mine[step, self.keep, 0:2], self.got1[step, 0])
        self.mine[step, self.y, 2:4] = plus(self.mine[step, self.y, 2:4], self.got1[step, 1])

        @pl.when(jnp.logical_not(self.owner))
        def _():
            for copy in self.second(step):
                copy.start()

    def end(self, step):
        @pl.when(self.owner)
        def _():
            for place in range(2):
                wait_bytes(self.got2.at[step, place], self.recv2.at[step, place])
                span = slice(2 * place, 2 * place + 2)
                self.mine[step, self.y, span] = plus(self.mine[step, self.y, span], self.got2[step, place])
            self.onward(step)

    def finish(self, out_ref):
        @pl.when(self.owner)
        def _():
            out_ref[...] = self.total().astype(bf16)
            for step in range(self.planes - 1):
                self.third(step).wait_send()

        @pl.when(jnp.logical_not(self.owner))
        def _():
            out_ref[...] = jnp.zeros_like(out_ref)
            for step in range(self.planes):
                for copy in self.second(step):
                    copy.wait_send()

        for step in range(self.planes):
            wait_bytes(self.mine.at[step], self.send0.at[step])
            for copy in self.first(step):
                copy.wait_send()


CARRY_REFS = 6
CARRY_SEMS = 11


def carry_scratch(kind, count, dp_count):
    rows, planes = D // count, count // 2
    far = max(1, dp_count.bit_length() - 3)
    dma = pltpu.SemaphoreType.DMA
    if kind == "attn":
        shapes = ((planes, 2, 2), (planes, 2, 2), (planes, 2), (planes,), (planes,), (far, planes))
        pair = (planes,)
    else:
        shapes = (
            (planes, 2, 4),
            (planes, 2, 4),
            (planes, 2, 2),
            (planes, 2, 2),
            (planes, 4),
            (far, planes, 4),
        )
        pair = (planes, 2)
    one = (planes,)
    sems = (one, one, one, pair, pair, pair, pair, one, one, (far, planes), (far, planes))
    return [pltpu.VMEM(shape + (rows, D), bf16) for shape in shapes] + [dma(shape) for shape in sems]


def reduce_kernel(
    count,
    attn_grad_ref,
    attn_done_ref,
    feed_low_ref,
    feed_high_ref,
    din_ref,
    vec0_ref,
    vec1_ref,
    vec2_ref,
    vec3_ref,
    outer_ref,
    whole_ref,
    own_ref,
    small_out,
    square_out,
    small_ref,
    small_core,
    small_s,
    small_got,
    sq_seg,
    sq_dp,
    small_send,
    small_recv,
    whole_send,
    whole_recv,
    half_sem,
    sq_send,
    sq_recv,
    sqd_send,
    sqd_recv,
    *refs,
):
    carry = AttnCarry(attn_grad_ref, refs[:CARRY_REFS], refs[CARRY_REFS:])
    seg, dp, core, x, y, across_core, near, far = peers()
    across_x, across_y, across_both = near
    planes = count // 2
    plane = seg // 2
    group = 2 * y + x
    targets = [{"seg": other} for other in others(seg, count)] + list(near) + list(far)
    hail(targets)
    carry.load_all()
    own_ref[1] = attn_done_ref[...]

    @pl.when(x == y)
    def _():
        own_ref[2:6] = feed_high_ref[...]

    @pl.when(x != y)
    def _():
        own_ref[2:6] = feed_low_ref[...]

    inputs = din_ref.shape[0]
    small_ref[0:inputs, :] = din_ref[...]
    for place, ref in enumerate((vec0_ref, vec1_ref, vec2_ref, vec3_ref, outer_ref)):
        small_ref[inputs + 8 * place : inputs + 8 * place + 8, :] = ref[...]
    small_ref[inputs + 40 :, :] = jnp.zeros((SMALL - inputs - 40, D), f32)
    meet(targets)
    carry.send_all()

    def small_steps():
        copy = remote(small_ref, small_core, small_send.at[0], small_recv.at[0], across_core)
        copy.start()
        yield
        copy.wait()
        small_s[...] = small_ref[...] + small_core[...]
        half = pl.ds(pl.multiple_of(core * (SMALL // 2), 8), SMALL // 2)
        targets = [across_x, across_y] + far
        step = 1
        while step < planes:
            targets.append({"seg": seg + 2 * step - 4 * step * ((plane // step) % 2)})
            step *= 2
        for place, target in enumerate(targets):
            copy = remote(
                small_s.at[half],
                small_got.at[place],
                small_send.at[place + 1],
                small_recv.at[place + 1],
                target,
            )
            copy.start()
            yield
            copy.wait()
            small_s[half, :] += small_got[place]
        small_out[half, :] = small_s[half, :]
        last = len(targets) + 1
        copy = remote(small_out.at[half], small_out.at[half], small_send.at[last], small_recv.at[last], across_core)
        copy.start()
        yield
        copy.wait()

    small_run = small_steps()
    next(small_run)
    roles = owners(count)

    def gift(place):
        first, width, owner, spot = roles[place]
        return remote(
            own_ref.at[first : first + width],
            whole_ref.at[seg, spot : spot + width],
            whole_send.at[place],
            whole_recv.at[seg],
            {"seg": owner},
        )

    def give(place):
        first, width, owner, spot = roles[place]

        @pl.when(seg != owner)
        def _():
            gift(place).start()

        @pl.when(seg == owner)
        def _():
            whole_ref[seg, spot : spot + width] = own_ref[first : first + width]

    for place in (2, 3, 1):
        give(place)
    for time in range(planes + 2):
        if time < planes:
            carry.begin(time)
        if 1 <= time <= planes:
            carry.middle(time - 1)
        if time >= 2:
            carry.end(time - 2)
        next(small_run, None)
    for _ in small_run:
        pass
    own_ref[0] = carry.total().astype(bf16)
    give(0)
    square = jnp.zeros((1, 1), f32)
    for unit in range(UNITS):
        value = own_ref[unit].astype(f32)
        square = square + jnp.sum(jnp.sum(value * value, 0, keepdims=True), 1, keepdims=True)
    sq_seg[seg] = jnp.broadcast_to(square, (8, 128))
    for step, other in enumerate(others(seg, count)):
        remote(sq_seg.at[seg], sq_seg.at[seg], sq_send.at[step], sq_recv.at[seg], {"seg": other}).start()
    for other in others(seg, count):
        wait_bytes(sq_seg.at[other], sq_recv.at[other])
    sq_dp[group] = jnp.sum(sq_seg[...], 0)
    for place, target in enumerate(near):
        remote(sq_dp.at[group], sq_dp.at[group], sqd_send.at[place], sqd_recv.at[place], target).start()
    sums = small_out[...]
    is_loss = lax.broadcasted_iota(jnp.int32, (SMALL, D), 0) == inputs + 37
    sums = jnp.where(is_loss, 0.0, sums)
    small_square = jnp.sum(jnp.sum(sums * sums, 0, keepdims=True), 1, keepdims=True)
    for place, target in enumerate(near):
        remote(sq_dp.at[group], sq_dp.at[group], sqd_send.at[place], sqd_recv.at[place], target).wait()
    square_out[...] = jnp.sum(sq_dp[...], 0) + jnp.broadcast_to(small_square, (8, 128))

    for place, (first, width, owner, spot) in enumerate(roles):

        @pl.when(seg == owner)
        def _():
            for other in others(seg, count):
                wait_bytes(whole_ref.at[other, spot : spot + width], whole_recv.at[other])
            if width == 2:
                span = slice(spot, spot + width)
                copy = remote(
                    whole_ref.at[:, span], whole_ref.at[:, span], half_sem.at[0], half_sem.at[1], across_core
                )
                copy.start()
                copy.wait()

    carry.drain()
    for place, (first, width, owner, spot) in enumerate(roles):

        @pl.when(seg != owner)
        def _():
            gift(place).wait_send()

    for step in range(count - 1):
        wait_bytes(sq_seg.at[0], sq_send.at[step])


def reduce_grads(count, dp_count, attn, done, feed_low, feed_high, pieces):
    rows = D // count
    planes = count // 2
    stages = 2 + planes.bit_length() + max(0, dp_count.bit_length() - 3)
    dma = pltpu.SemaphoreType.DMA
    vmem = pl.BlockSpec(memory_space=pltpu.VMEM)
    return pl.pallas_call(
        functools.partial(reduce_kernel, count),
        out_shape=[
            jax.ShapeDtypeStruct((count, 4, rows, D), bf16),
            jax.ShapeDtypeStruct((UNITS, rows, D), bf16),
            jax.ShapeDtypeStruct((SMALL, D), f32),
            jax.ShapeDtypeStruct((8, 128), f32),
        ],
        in_specs=[pl.BlockSpec(memory_space=pl.ANY)] + [vmem] * 9,
        out_specs=[vmem] * 4,
        scratch_shapes=[
            pltpu.VMEM((SMALL, D), f32),
            pltpu.VMEM((SMALL, D), f32),
            pltpu.VMEM((SMALL, D), f32),
            pltpu.VMEM((stages, SMALL // 2, D), f32),
            pltpu.VMEM((count, 8, 128), f32),
            pltpu.VMEM((GROUPS, 8, 128), f32),
            dma((stages + 2,)),
            dma((stages + 2,)),
            dma((4,)),
            dma((count,)),
            dma((2,)),
            dma((count,)),
            dma((count,)),
            dma((3,)),
            dma((3,)),
        ]
        + carry_scratch("attn", count, dp_count),
        compiler_params=pltpu.CompilerParams(
            collective_id=1, has_side_effects=True, vmem_limit_bytes=VMEM_LIMIT
        ),
        cost_estimate=pl.CostEstimate(flops=10**8, bytes_accessed=10**8, transcendentals=0),
        name="reduce_grads",
    )(attn.reshape(2, 2, count, rows, D), done, feed_low, feed_high, *pieces)


def halves(value):
    high = value.astype(bf16)
    return high, (value - high.astype(f32)).astype(bf16)


def times(left, right):
    (left_high, left_low), (right_high, right_low) = left, right
    return dot_nn(
        jnp.concatenate([left_high, left_high, left_low], 1),
        jnp.concatenate([right_high, right_low, right_high], 0),
    )


def times_t(left, right):
    (left_high, left_low), (right_high, right_low) = left, right
    return dot_nt(
        jnp.concatenate([left_high, left_high, left_low], 1),
        jnp.concatenate([right_high, right_low, right_high], 1),
    )


def clip_of(norm):
    return jnp.minimum(1.0, 0.25 / (norm + 1e-06))


def muon_kernel(role_ref, square_ref, dout_ref, whole_ref, mom_ref, out_ref, norm_ref, x_s, q_s, gram_s, high_s, low_s):
    count, rows = whole_ref.shape[0], whole_ref.shape[2]
    core = role_ref[1]
    dout = dout_ref[...]
    norm = jnp.sqrt(square_ref[0:1, 0:1] + jnp.sum(jnp.sum(dout * dout, 0, keepdims=True), 1, keepdims=True))
    norm_ref[...] = jnp.broadcast_to(norm, norm_ref.shape)
    clip = clip_of(norm)
    eye = (
        lax.broadcasted_iota(jnp.int32, (D, D), 0) == lax.broadcasted_iota(jnp.int32, (D, D), 1)
    ).astype(f32)

    @pl.when(role_ref[0] == 1)
    def _():
        start = (0.5 * mom_ref[:, core].astype(f32)).reshape(D, D)
        start = start + clip * whole_ref[:, 0].astype(f32).reshape(D, D)
        size = jnp.sum(jnp.sum(start * start, 0, keepdims=True), 1, keepdims=True)
        x_s[...] = start / (jnp.sqrt(size) + 1e-07)

        def sweep(_, carry):
            value = x_s[...]
            both = halves(value)
            gram = times_t(both, both)
            gram_both = halves(gram)
            poly = -4.775 * gram + 2.0315 * times(gram_both, gram_both)
            x_s[...] = 3.4445 * value + times(halves(poly), both)
            return carry

        lax.fori_loop(0, 5, sweep, 0)
        out_ref[:, 0] = x_s[...].astype(bf16).reshape(count, rows, D)

    @pl.when(role_ref[0] == 2)
    def _():
        gram_s[...] = jnp.zeros_like(gram_s)

        def gather(tile, size):
            value = (0.5 * mom_ref[:, 2 + tile].astype(f32)).reshape(D, D)
            value = value + clip * whole_ref[:, tile].astype(f32).reshape(D, D)
            high, low = halves(value)
            high_s[tile] = high
            low_s[tile] = low

            @pl.when(role_ref[2] == 1)
            def _():
                high_s[tile] = jnp.transpose(high_s[tile])
                low_s[tile] = jnp.transpose(low_s[tile])

            both = high_s[tile], low_s[tile]
            gram_s[...] += times_t(both, both)
            return size + jnp.sum(jnp.sum(value * value, 0, keepdims=True), 1, keepdims=True)

        size = lax.fori_loop(0, 4, gather, jnp.zeros((1, 1), f32))
        scale = 1.0 / (jnp.sqrt(size) + 1e-07)
        gram_s[...] = gram_s[...] * (scale * scale)

        def poly_of(gram, gram_both):
            return 3.4445 * eye - 4.775 * gram + 2.0315 * times(gram_both, gram_both)

        def advance(gram_both, poly_both):
            gram_s[...] = times(halves(times(gram_both, poly_both)), poly_both)

        gram = gram_s[...]
        gram_both = halves(gram)
        poly = poly_of(gram, gram_both)
        q_s[...] = poly
        advance(gram_both, halves(poly))

        def sweep(_, carry):
            gram = gram_s[...]
            gram_both = halves(gram)
            poly_both = halves(poly_of(gram, gram_both))
            q_s[...] = times(halves(q_s[...]), poly_both)
            advance(gram_both, poly_both)
            return carry

        lax.fori_loop(0, 3, sweep, 0)
        gram = gram_s[...]
        last = times(halves(q_s[...]), halves(poly_of(gram, halves(gram)))) * scale
        last_both = halves(last)

        def finish(step, carry):
            tile = 2 * core + step
            x_s[...] = times(last_both, (high_s[tile], low_s[tile]))

            @pl.when(role_ref[2] == 1)
            def _():
                x_s[...] = jnp.transpose(x_s[...])

            out_ref[:, step] = x_s[...].astype(bf16).reshape(count, rows, D)
            return carry

        lax.fori_loop(0, 2, finish, 0)


def muon(role, squares, dout, whole, momenta):
    count, _, rows, _ = whole.shape
    return pl.pallas_call(
        muon_kernel,
        out_shape=[jax.ShapeDtypeStruct((count, 2, rows, D), bf16), jax.ShapeDtypeStruct((8, 128), f32)],
        in_specs=[pl.BlockSpec(memory_space=pltpu.SMEM)] + [pl.BlockSpec(memory_space=pltpu.VMEM)] * 4,
        out_specs=[pl.BlockSpec(memory_space=pltpu.VMEM)] * 2,
        scratch_shapes=[
            pltpu.VMEM((D, D), f32),
            pltpu.VMEM((D, D), f32),
            pltpu.VMEM((D, D), f32),
            pltpu.VMEM((4, D, D), bf16),
            pltpu.VMEM((4, D, D), bf16),
        ],
        compiler_params=pltpu.CompilerParams(vmem_limit_bytes=VMEM_LIMIT),
        cost_estimate=pl.CostEstimate(flops=2 * 10**10, bytes_accessed=10**7, transcendentals=0),
        name="muon",
    )(role, squares, dout, whole, momenta)


def spread_kernel(count, made_ref, own_ref, update_ref, every_ref, send, recv, on_send, on_recv, own_send, own_recv):
    seg, dp, core, x, y, across_core, near, far = peers()
    group = 2 * y + x
    greet(seg, count, near, ())
    roles = owners(count)

    def gift(place, other):
        first, width, owner, spot = roles[place]
        return remote(
            made_ref.at[other, 0:width],
            update_ref.at[group, first : first + width],
            send.at[other],
            recv.at[place],
            {"seg": other},
        )

    def onward(place, side):
        first, width, owner, spot = roles[place]
        block = update_ref.at[group, first : first + width]
        return remote(block, block, on_send.at[side, place], on_recv.at[side, place], near[side])

    def own_rows(side):
        return remote(own_ref, every_ref.at[group], own_send.at[side], own_recv.at[side], near[side])

    for place, (first, width, owner, spot) in enumerate(roles):

        @pl.when(seg == owner)
        def _():
            for other in others(seg, count):
                gift(place, other).start()
            update_ref[group, first : first + width] = made_ref[seg, 0:width]

    for side in range(3):
        own_rows(side).start()
    every_ref[group] = own_ref[...]
    for place, (first, width, owner, spot) in enumerate(roles):

        @pl.when(seg != owner)
        def _():
            wait_bytes(update_ref.at[group, first : first + width], recv.at[place])

        for side in range(3):
            onward(place, side).start()
    for side in range(3):
        own_rows(side).wait()
    for place, (first, width, owner, spot) in enumerate(roles):
        for side in range(3):
            onward(place, side).wait()

        @pl.when(seg == owner)
        def _():
            for other in others(seg, count):
                gift(place, other).wait_send()


def spread(count, made, own):
    rows = made.shape[2]
    dma = pltpu.SemaphoreType.DMA
    vmem = pl.BlockSpec(memory_space=pltpu.VMEM)
    return pl.pallas_call(
        functools.partial(spread_kernel, count),
        out_shape=[jax.ShapeDtypeStruct((GROUPS, UNITS, rows, D), bf16)] * 2,
        in_specs=[vmem] * 2,
        out_specs=[vmem] * 2,
        scratch_shapes=[dma((count,)), dma((4,)), dma((3, 4)), dma((3, 4)), dma((3,)), dma((3,))],
        compiler_params=pltpu.CompilerParams(
            collective_id=2, has_side_effects=True, vmem_limit_bytes=VMEM_LIMIT
        ),
        cost_estimate=pl.CostEstimate(flops=10**6, bytes_accessed=4 * 10**7, transcendentals=0),
        name="spread",
    )(made, own)


def embed_kernel(
    count,
    frames_ref,
    mask_ref,
    in_ref,
    outer_ref,
    x_ref,
    mem_ref,
    total_ref,
    got_s,
    count_s,
    frame_send,
    frame_recv,
    count_send,
    count_recv,
):
    seg = lax.axis_index("seg")
    after, before = lax.rem(seg + 1, count), lax.rem(seg + count - 1, count)
    streams = frames_ref.shape[0]
    tally = jnp.sum(mask_ref[...].astype(f32), 1, keepdims=True)
    count_s[seg] = jnp.broadcast_to(
        jnp.concatenate([tally, jnp.zeros((8 - streams, 1), f32)], 0), (8, 128)
    )
    greet(seg, count, (), ())
    frame_copy = remote(frames_ref, got_s, frame_send.at[0], frame_recv.at[0], {"seg": after})
    frame_copy.start()
    for step, other in enumerate(others(seg, count)):
        remote(count_s.at[seg], count_s.at[seg], count_send.at[step], count_recv.at[seg], {"seg": other}).start()
    weight, shift = in_ref[...], outer_ref[0:1, :]
    for stream in range(streams):
        x_ref[stream] = dot_nn(jnp.transpose(frames_ref[stream]), weight) + shift
    frame_copy.wait()
    for stream in range(streams):
        mem_ref[stream] = (dot_nn(jnp.transpose(got_s[stream]), weight) + shift).astype(bf16)
    for other in others(seg, count):
        wait_bytes(count_s.at[other], count_recv.at[other])
    total_ref[...] = jnp.sum(count_s[...], 0)
    for step in range(count - 1):
        wait_bytes(count_s.at[0], count_send.at[step])


def embed(count, frames, mask, in_weight, outer_vectors):
    streams = frames.shape[0]
    dma = pltpu.SemaphoreType.DMA
    return pl.pallas_call(
        functools.partial(embed_kernel, count),
        out_shape=[
            jax.ShapeDtypeStruct((streams, SEG, D), f32),
            jax.ShapeDtypeStruct((streams, SEG, D), bf16),
            jax.ShapeDtypeStruct((8, 128), f32),
        ],
        in_specs=[pl.BlockSpec(memory_space=pltpu.VMEM)] * 4,
        out_specs=[pl.BlockSpec(memory_space=pltpu.VMEM)] * 3,
        scratch_shapes=[
            pltpu.VMEM(frames.shape, bf16),
            pltpu.VMEM((count, 8, 128), f32),
            dma((1,)),
            dma((1,)),
            dma((count,)),
            dma((count,)),
        ],
        compiler_params=pltpu.CompilerParams(
            collective_id=3, has_side_effects=True, vmem_limit_bytes=VMEM_LIMIT
        ),
        cost_estimate=pl.CostEstimate(flops=2 * 10**8, bytes_accessed=4 * 10**6, transcendentals=0),
        name="embed",
    )(frames, mask, in_weight, outer_vectors)


FEED_UP = (1, 0)
FEED_DOWN = (2, 3)
KEEP = 1.0 - 0.3 * 0.01


def finish_kernel(norm_ref, every_ref, update_ref, dout_ref, small_ref, *refs):
    (
        attn_ref,
        attn_mom_ref,
        up_ref,
        up_mom_ref,
        down_ref,
        down_mom_ref,
        out_ref,
        out_mom_ref,
        out_sec_ref,
        in_ref,
        in_mom_ref,
        in_sec_ref,
        vec_ref,
        vec_mom_ref,
        vec_sec_ref,
        outer_ref,
        outer_mom_ref,
        outer_sec_ref,
        attn_new,
        attn_mom_new,
        attn_copy_new,
        up_new,
        up_mom_new,
        up_copy_new,
        down_new,
        down_mom_new,
        down_copy_new,
        out_new,
        out_mom_new,
        out_sec_new,
        out_copy_new,
        in_new,
        in_mom_new,
        in_sec_new,
        in_copy_new,
        vec_new,
        vec_mom_new,
        vec_sec_new,
        outer_new,
        outer_mom_new,
        outer_sec_new,
    ) = refs
    clip = clip_of(norm_ref[0:1, 0:1])

    def muon_step(weight, momentum, grad, update, scale):
        weight = weight * KEEP - (0.3 * scale) * update.astype(f32)
        return weight, 0.5 * momentum + clip * grad.astype(f32)

    up_scale, down_scale = max(1.0, FF / D) ** 0.5, max(1.0, D / FF) ** 0.5
    for depth in range(LAYERS):
        for kind in range(4):
            weight, momentum = muon_step(
                attn_ref[depth, kind],
                attn_mom_ref[depth, kind],
                every_ref[kind, depth],
                update_ref[kind, depth],
                1.0,
            )
            attn_new[depth, kind] = weight
            attn_mom_new[depth, kind] = momentum
            attn_copy_new[depth, kind] = weight.astype(bf16)
            columns = slice(kind * TILE, (kind + 1) * TILE)
            weight, momentum = muon_step(
                up_ref[depth, :, columns],
                up_mom_ref[depth, :, columns],
                every_ref[FEED_UP[depth], 2 + kind],
                update_ref[FEED_UP[depth], 2 + kind],
                up_scale,
            )
            up_new[depth, :, columns] = weight
            up_mom_new[depth, :, columns] = momentum
            up_copy_new[depth, :, columns] = weight.astype(bf16)
            weight, momentum = muon_step(
                down_ref[depth, kind],
                down_mom_ref[depth, kind],
                every_ref[FEED_DOWN[depth], 2 + kind],
                update_ref[FEED_DOWN[depth], 2 + kind],
                down_scale,
            )
            down_new[depth, kind] = weight
            down_mom_new[depth, kind] = momentum
            down_copy_new[depth, kind] = weight.astype(bf16)
    weight, moment, second = adamw(out_ref[...], out_mom_ref[...], out_sec_ref[...], dout_ref[...] * clip, 0.05, 0.01)
    out_new[...] = weight
    out_mom_new[...] = moment
    out_sec_new[...] = second
    out_copy_new[...] = weight.astype(bf16)

    @pl.when(pl.program_id(0) == 0)
    def _():
        inputs = in_ref.shape[0]
        weight, moment, second = adamw(
            in_ref[...], in_mom_ref[...], in_sec_ref[...], small_ref[0:inputs, :] * clip, 0.05, 0.01
        )
        in_new[...] = weight
        in_mom_new[...] = moment
        in_sec_new[...] = second
        in_copy_new[...] = weight.astype(bf16)

        def rows_of(first, last, base):
            return small_ref[inputs + base + first : inputs + base + last, :]

        for depth in range(LAYERS):
            base = 16 * depth
            for low, high, grad in (
                (0, 2, rows_of(0, 2, base)),
                (2, 4, rows_of(0, 2, base + 8)),
                (4, 7, rows_of(2, 5, base)),
                (7, 8, rows_of(2, 3, base + 8)),
                (8, 12, rows_of(4, 8, base + 8)),
            ):
                weight, moment, second = adamw(
                    vec_ref[depth, low:high],
                    vec_mom_ref[depth, low:high],
                    vec_sec_ref[depth, low:high],
                    grad * clip,
                    0.25,
                    0.0,
                )
                vec_new[depth, low:high] = weight
                vec_mom_new[depth, low:high] = moment
                vec_sec_new[depth, low:high] = second
        for low, high, grad in ((0, 1, rows_of(5, 6, 0)), (1, 5, rows_of(1, 5, 32))):
            weight, moment, second = adamw(
                outer_ref[low:high, :], outer_mom_ref[low:high, :], outer_sec_ref[low:high, :], grad * clip, 0.25, 0.0
            )
            outer_new[low:high, :] = weight
            outer_mom_new[low:high, :] = moment
            outer_sec_new[low:high, :] = second


def finish(rows, norm, every, updates, dout, small, arrays):
    steps = rows // 16
    attn, _, up, _, down, _, out, _, _, inp, _, _, vec, _, _, outer, _, _ = arrays
    codes = out.shape[1]
    blocks = pl.BlockSpec((GROUPS, UNITS, 16, D), lambda i: (0, 0, i, 0))
    attn_spec = pl.BlockSpec((LAYERS, 4, 16, D), lambda i: (0, 0, i, 0))
    up_spec = pl.BlockSpec((LAYERS, 16, FF), lambda i: (0, i, 0))
    out_spec = pl.BlockSpec((D // steps, codes), lambda i: (i, 0))
    in_spec, vec_spec, outer_spec = whole_spec(inp.shape), whole_spec(vec.shape), whole_spec(outer.shape)

    def like(array, dtype=f32):
        return jax.ShapeDtypeStruct(array.shape, dtype)

    return pl.pallas_call(
        finish_kernel,
        grid=(steps,),
        out_shape=[like(attn), like(attn), like(attn, bf16)]
        + [like(up), like(up), like(up, bf16)]
        + [like(down), like(down), like(down, bf16)]
        + [like(out)] * 3
        + [like(out, bf16)]
        + [like(inp)] * 3
        + [like(inp, bf16)]
        + [like(vec)] * 3
        + [like(outer)] * 3,
        in_specs=[whole_spec((8, 128)), blocks, blocks, out_spec, whole_spec(small.shape)]
        + [attn_spec] * 2
        + [up_spec] * 2
        + [attn_spec] * 2
        + [out_spec] * 3
        + [in_spec] * 3
        + [vec_spec] * 3
        + [outer_spec] * 3,
        out_specs=[attn_spec] * 3
        + [up_spec] * 3
        + [attn_spec] * 3
        + [out_spec] * 4
        + [in_spec] * 4
        + [vec_spec] * 3
        + [outer_spec] * 3,
        compiler_params=pltpu.CompilerParams(vmem_limit_bytes=VMEM_LIMIT),
        cost_estimate=pl.CostEstimate(flops=10**8, bytes_accessed=4 * 10**7, transcendentals=0),
        name="finish",
    )(norm, every, updates, dout, small, *arrays)


def local(
    frames,
    speech_mask,
    targets,
    in_proj,
    in_moment,
    in_second,
    out_proj,
    out_moment,
    out_second,
    layer_vectors,
    vectors_moment,
    vectors_second,
    outer_vectors,
    outer_moment,
    outer_second,
    attn_proj,
    attn_momentum,
    ff_up,
    up_momentum,
    ff_down,
    down_momentum,
    in_copy,
    out_copy,
    attn_copy,
    up_copy,
    down_copy,
):
    segment = lax.axis_index("seg")
    count, dp_count = lax.axis_size("seg"), lax.axis_size("dp")
    rows = D // count
    streams = frames.shape[0]
    stream_total = streams * dp_count
    group = lax.axis_index("dp") % GROUPS
    feeds = jnp.stack(
        [
            jnp.swapaxes(up_momentum[1].reshape(rows, 4, D), 0, 1),
            jnp.swapaxes(up_momentum[0].reshape(rows, 4, D), 0, 1),
            down_momentum[0].reshape(4, rows, D),
            down_momentum[1].reshape(4, rows, D),
        ]
    )
    owned = jnp.concatenate(
        [
            lax.dynamic_index_in_dim(attn_momentum, group, 1, keepdims=False),
            lax.dynamic_index_in_dim(feeds, group, 0, keepdims=False),
        ],
        0,
    ).astype(bf16)
    momenta = lax.all_gather(owned, "seg", axis=0, tiled=False)
    frames_t = jnp.swapaxes(frames, 1, 2)
    bias = jnp.where(segment > 0, 0.0, -1e30).astype(f32)[None]
    hidden, memory, totals = embed(count, frames_t, speech_mask, in_copy, outer_vectors)
    memory = [memory] * streams
    kept = []
    for depth in range(LAYERS):
        saved, passed = None, []
        for stream in range(streams):
            saved, short = forward_layer(
                depth,
                stream,
                streams,
                bias,
                hidden,
                memory[stream],
                attn_copy,
                up_copy,
                down_copy,
                layer_vectors,
                saved,
            )
            if depth + 1 < LAYERS:
                passed.append(from_behind(short, "seg", 1))
        kept.append((hidden, memory[0] if depth == 0 else jnp.stack(memory), saved))
        hidden = saved[0]
        memory = passed
    grad_hidden, grad_out, head_outer = head(
        hidden, targets, speech_mask, totals, out_copy, outer_vectors, 1.0 / stream_total, momenta
    )
    grad_out = lax.psum(grad_out, ("seg", "dp"))
    vector_grads, feed_done = [], [None, None]
    grad_attn = None
    attn_done = None
    for depth in reversed(range(LAYERS)):
        entering, held, saved = kept[depth]
        dafter, grad_up, grad_down, feed_vec, *done = feed_back(
            depth, grad_hidden, saved[7], up_copy, down_copy, layer_vectors, count, dp_count, grad_attn
        )
        if done:
            attn_done = done[0]
        grad_hidden, grad_attn, attn_vec, grad_in, feed_done[depth] = attend_back(
            depth,
            bias,
            dafter,
            entering,
            held,
            saved[1:7],
            attn_copy,
            layer_vectors,
            frames_t,
            grad_up,
            grad_down,
            count,
            dp_count,
        )
        vector_grads = [attn_vec, feed_vec] + vector_grads
    whole, own, small, squares = reduce_grads(
        count,
        dp_count,
        grad_attn,
        attn_done,
        feed_done[0],
        feed_done[1],
        [grad_in] + vector_grads + [head_outer],
    )
    loss_sum = small[grad_in.shape[0] + 37, 0]
    plane, core = segment // 2, segment % 2
    kind = jnp.where(plane == count // 4 - 1, 1, jnp.where(plane == count // 4, 2, 0))
    role = jnp.stack([kind, core, (group >= 2).astype(jnp.int32), core]).astype(jnp.int32)
    made, norm = muon(role, squares, grad_out, whole, momenta)
    updates, every = spread(count, made, own)
    split = (LAYERS, 4, rows, D)
    (
        attn_new,
        attn_mom,
        attn_copy_new,
        up_new,
        up_mom,
        up_copy_new,
        down_new,
        down_mom,
        down_copy_new,
        out_new,
        out_moment_new,
        out_second_new,
        out_copy_new,
        in_new,
        in_moment_new,
        in_second_new,
        in_copy_new,
        vectors_new,
        vectors_moment_new,
        vectors_second_new,
        outer_new,
        outer_moment_new,
        outer_second_new,
    ) = finish(
        rows,
        norm,
        every,
        updates,
        grad_out,
        small,
        [
            attn_proj,
            attn_momentum,
            ff_up,
            up_momentum,
            ff_down.reshape(split),
            down_momentum.reshape(split),
            out_proj,
            out_moment,
            out_second,
            in_proj,
            in_moment,
            in_second,
            layer_vectors,
            vectors_moment,
            vectors_second,
            outer_vectors,
            outer_moment,
            outer_second,
        ],
    )
    return (
        loss_sum,
        norm[0, 0],
        in_new,
        in_moment_new,
        in_second_new,
        out_new,
        out_moment_new,
        out_second_new,
        vectors_new,
        vectors_moment_new,
        vectors_second_new,
        outer_new,
        outer_moment_new,
        outer_second_new,
        attn_new,
        attn_mom,
        up_new,
        up_mom,
        down_new.reshape(ff_down.shape),
        down_mom.reshape(ff_down.shape),
        in_copy_new,
        out_copy_new,
        attn_copy_new,
        up_copy_new,
        down_copy_new.reshape(ff_down.shape),
    )


def solution(mesh):
    return jax.shard_map(
        local,
        mesh=mesh,
        in_specs=(
            P("dp", "seg", None),
            P("dp", "seg"),
            P("dp", "seg"),
            P(),
            P(),
            P(),
            P(),
            P(),
            P(),
            P(),
            P(),
            P(),
            P(),
            P(),
            P(),
            P(None, None, "seg", None),
            P(None, None, "seg", None),
            P(None, "seg", None),
            P(None, "seg", None),
            P(None, "seg", None),
            P(None, "seg", None),
            P(),
            P(),
            P(),
            P(),
            P(),
        ),
        out_specs=(
            P(),
            P(),
            P(),
            P(),
            P(),
            P(),
            P(),
            P(),
            P(),
            P(),
            P(),
            P(),
            P(),
            P(),
            P(None, None, "seg", None),
            P(None, None, "seg", None),
            P(None, "seg", None),
            P(None, "seg", None),
            P(None, "seg", None),
            P(None, "seg", None),
            P(),
            P(),
            P(None, None, "seg", None),
            P(None, "seg", None),
            P(None, "seg", None),
        ),
        check_vma=False,
    )
```

```python
import functools
import math

import jax
import jax.numpy as jnp
from jax import lax
from jax.experimental import pallas as pl
from jax.experimental.pallas import tpu as pltpu
from jax.sharding import PartitionSpec as P

D = 512
HEAD_DIM = 64
HEADS = D // HEAD_DIM
FF = 2048
LAYERS = 2
STEP = 10
SEG = 512
HALF = 256
PAIR = 2 * HEAD_DIM
TILE = 512
VMEM_LIMIT = 56 * 1024 * 1024
GELU_SCALE = math.sqrt(2.0 / math.pi)

f32 = jnp.float32
bf16 = jnp.bfloat16


def dot_nn(left, right):
    return lax.dot_general(left, right, (((1,), (0,)), ((), ())), preferred_element_type=f32)


def dot_nt(left, right):
    return lax.dot_general(left, right, (((1,), (1,)), ((), ())), preferred_element_type=f32)


def dot_tn(left, right):
    return lax.dot_general(left, right, (((0,), (0,)), ((), ())), preferred_element_type=f32)


def normalised(values):
    centred = values - jnp.mean(values, -1, keepdims=True)
    scale = lax.rsqrt(jnp.mean(centred * centred, -1, keepdims=True) + 1e-05)
    return centred * scale, scale


def norm_back(grad, gain, unit, scale):
    part = grad * gain
    mean_part = jnp.mean(part, -1, keepdims=True)
    mean_unit = jnp.mean(part * unit, -1, keepdims=True)
    return scale * (part - mean_part - unit * mean_unit)


def column_sum(values):
    return jnp.sum(values, 0, keepdims=True)


def head_masks():
    lane = lax.broadcasted_iota(jnp.int32, (1, PAIR), 1)
    return (lane < HEAD_DIM).astype(bf16), (lane >= HEAD_DIM).astype(bf16)


def pair_lanes(pair):
    return pl.ds(pl.multiple_of(pair * PAIR, PAIR), PAIR)


def forward_kernel(
    bias_ref,
    x_ref,
    mem_ref,
    attn_ref,
    up_ref,
    down_ref,
    vec_ref,
    *refs,
):
    hid_ref, hid16_ref, keyin_ref, q_ref, k_ref, v_ref, lse_ref, mixed_ref, after_ref, kept_ref, act_s, lse_s = refs[-12:]
    kept_ref[...] = mem_ref[...]
    x = x_ref[...]
    own_unit, _ = normalised(x)
    gain, shift = vec_ref[0:1, :], vec_ref[1:2, :]
    normed = (own_unit * gain + shift).astype(bf16)
    mem_unit, _ = normalised(mem_ref[...].astype(f32))
    mem_normed = (mem_unit * gain + shift).astype(bf16)
    keyin_ref[0:SEG, :] = mem_normed
    keyin_ref[SEG:, :] = normed
    q_ref[...] = (dot_nn(normed, attn_ref[0]) + vec_ref[4:5, :]).astype(bf16) * jnp.asarray(HEAD_DIM**-0.5, bf16)
    k_ref[0:SEG, :] = dot_nn(mem_normed, attn_ref[1]).astype(bf16)
    k_ref[SEG:, :] = dot_nn(normed, attn_ref[1]).astype(bf16)
    v_ref[0:SEG, :] = (dot_nn(mem_normed, attn_ref[2]) + vec_ref[5:6, :]).astype(bf16)
    v_ref[SEG:, :] = (dot_nn(normed, attn_ref[2]) + vec_ref[5:6, :]).astype(bf16)
    first, second = head_masks()
    memory_bias = bias_ref[0]
    lane = lax.broadcasted_iota(jnp.int32, (HALF, PAIR), 1)
    query_pos = lax.broadcasted_iota(jnp.int32, (2 * HALF, HALF), 0) % HALF
    key_pos = lax.broadcasted_iota(jnp.int32, (2 * HALF, HALF), 1)
    diagonal = key_pos <= query_pos
    lse_s[...] = jnp.zeros_like(lse_s)

    def pair_body(pair, carry):
        lanes = pair_lanes(pair)
        for block in range(2):
            rows = slice(block * HALF, (block + 1) * HALF)
            q_pair = q_ref[rows, lanes]
            q_both = jnp.concatenate([q_pair * first, q_pair * second], 0)
            spans = [(0, SEG, 0)]
            if block:
                spans.append((SEG, SEG + HALF, 1))
            spans.append((SEG + block * HALF, SEG + (block + 1) * HALF, 2))
            scores = []
            for low, high, kind in spans:
                part = dot_nt(q_both, k_ref[low:high, lanes])
                if kind == 0:
                    part = part + memory_bias
                if kind == 2:
                    part = jnp.where(diagonal, part, -1e30)
                scores.append(part)
            most = functools.reduce(jnp.maximum, [jnp.max(part, -1, keepdims=True) for part in scores])
            weights = [jnp.exp(part - most) for part in scores]
            total = functools.reduce(jnp.add, [jnp.sum(part, -1, keepdims=True) for part in weights])
            mixed = functools.reduce(
                jnp.add,
                [
                    dot_nn(part.astype(bf16), v_ref[low:high, lanes])
                    for part, (low, high, kind) in zip(weights, spans)
                ],
            )
            mixed = mixed / total
            mixed_ref[rows, lanes] = jnp.where(lane < HEAD_DIM, mixed[:HALF], mixed[HALF:]).astype(bf16)
            lse = most + jnp.log(total)
            kept = jnp.where(lane == 2 * pair, lse[:HALF], lse_s[rows, :])
            lse_s[rows, :] = jnp.where(lane == 2 * pair + 1, lse[HALF:], kept)
        return carry

    lax.fori_loop(0, HEADS // 2, pair_body, 0)
    lse_ref[...] = jnp.transpose(lse_s[...])[0:HEADS, :]
    after = x + (dot_nn(mixed_ref[...], attn_ref[3]) + vec_ref[6:7, :])
    after_ref[...] = after
    unit, _ = normalised(after)
    normed_two = (unit * vec_ref[2:3, :] + vec_ref[3:4, :]).astype(bf16)
    for tile in range(FF // TILE):
        columns = slice(tile * TILE, (tile + 1) * TILE)
        inner = dot_nn(normed_two, up_ref[:, columns]) + vec_ref[8 + tile : 9 + tile, :]
        act_s[:, columns] = (
            0.5 * inner * (1.0 + jnp.tanh(GELU_SCALE * (inner + 0.044715 * inner * inner * inner)))
        ).astype(bf16)
    hidden = after + (dot_nn(act_s[...], down_ref[...]) + vec_ref[7:8, :])
    hid_ref[...] = hidden
    hid16_ref[...] = hidden.astype(bf16)


SAVED = (
    ((SEG, D), f32),
    ((2 * SEG, D), bf16),
    ((SEG, D), bf16),
    ((2 * SEG, D), bf16),
    ((2 * SEG, D), bf16),
    ((HEADS, SEG), f32),
    ((SEG, D), bf16),
    ((SEG, D), f32),
    ((SEG, D), bf16),
)


def whole_spec(shape):
    return pl.BlockSpec(shape, lambda *_: (0,) * len(shape))


def stream_spec(shape, stream=None):
    zeros = (0,) * len(shape)
    if stream is None:
        return pl.BlockSpec((None,) + shape, lambda i: (i,) + zeros)
    return pl.BlockSpec((None,) + shape, lambda i: (stream,) + zeros)


def layer_spec(shape, depth):
    zeros = (0,) * len(shape)
    return pl.BlockSpec((None,) + shape, lambda *_: (depth,) + zeros)


def forward_layer(depth, stream, streams, bias, hidden, memory, attn, upper, lower, vectors, earlier):
    saved_shapes = [jax.ShapeDtypeStruct((streams,) + shape, dtype) for shape, dtype in SAVED]
    saved_specs = [stream_spec(shape, stream) for shape, dtype in SAVED]
    out_shape = [saved_shapes[0], jax.ShapeDtypeStruct((SEG, D), bf16)] + saved_shapes[1:]
    out_specs = [saved_specs[0], whole_spec((SEG, D))] + saved_specs[1:]
    operands = [bias, hidden, memory, attn, upper, lower, vectors]
    in_specs = [
        pl.BlockSpec(memory_space=pltpu.SMEM),
        stream_spec((SEG, D), stream),
        stream_spec((SEG, D), stream) if memory.ndim == 3 else whole_spec((SEG, D)),
        layer_spec(attn.shape[1:], depth),
        layer_spec(upper.shape[1:], depth),
        layer_spec(lower.shape[1:], depth),
        layer_spec(vectors.shape[1:], depth),
    ]
    aliases = {}
    if earlier is not None:
        for place, array in enumerate(earlier):
            aliases[len(operands)] = place if place == 0 else place + 1
            operands.append(array)
            in_specs.append(pl.BlockSpec(memory_space=pl.ANY))
    out = pl.pallas_call(
        forward_kernel,
        grid=(1,),
        out_shape=out_shape,
        in_specs=in_specs,
        out_specs=out_specs,
        scratch_shapes=[pltpu.VMEM((SEG, FF), bf16), pltpu.VMEM((SEG, PAIR), f32)],
        input_output_aliases=aliases,
        compiler_params=pltpu.CompilerParams(vmem_limit_bytes=VMEM_LIMIT),
        cost_estimate=pl.CostEstimate(flops=10**10, bytes_accessed=2 * 10**7, transcendentals=10**7),
        name="layer_forward",
    )(*operands)
    return [out[0]] + list(out[2:]), out[1]


def head_kernel(scale, x_ref, target_ref, mask_ref, total_ref, out_ref, outer_ref, bias_ref, mom_ref, g_ref, dout_ref, douter_ref, acc_s):
    step = pl.program_id(0)

    @pl.when(step == 0)
    def _():
        acc_s[...] = jnp.zeros_like(acc_s)
        douter_ref[...] = jnp.zeros_like(douter_ref)

    unit, rscale = normalised(x_ref[...])
    gain = outer_ref[1:2, :]
    normed = (unit * gain + outer_ref[2:3, :]).astype(bf16)
    logits = dot_nn(normed, out_ref[...]) + bias_ref[...]
    most = jnp.max(logits, -1, keepdims=True)
    powers = jnp.exp(logits - most)
    total = jnp.sum(powers, -1, keepdims=True)
    target_row = target_ref[pl.ds(step, 1), :].astype(f32)
    weight_row = mask_ref[pl.ds(step, 1), :].astype(f32) * (1.0 / total_ref[pl.ds(step, 1), 0:1])
    columns = jnp.transpose(jnp.concatenate([target_row, weight_row, jnp.zeros((6, SEG), f32)], 0))
    target, weight = columns[:, 0:1].astype(jnp.int32), columns[:, 1:2]
    chosen = lax.broadcasted_iota(jnp.int32, logits.shape, 1) == target
    picked = jnp.sum(jnp.where(chosen, logits, 0.0), -1, keepdims=True)
    loss = jnp.sum(weight * (most + jnp.log(total) - picked), 0, keepdims=True)
    spread = weight * scale
    dlogits = (powers * (spread / total) - jnp.where(chosen, spread, 0.0)).astype(bf16)
    acc_s[...] += dot_nn(jnp.transpose(normed), dlogits)
    bias_grad = column_sum(dlogits.astype(f32))
    dnormed = dot_nt(dlogits, out_ref[...])
    g_ref[...] = norm_back(dnormed, gain, unit, rscale)
    douter_ref[1:2, :] += column_sum(dnormed * unit)
    douter_ref[2:3, :] += column_sum(dnormed)
    douter_ref[3:4, :] += bias_grad[:, :D]
    douter_ref[4:5, :] += bias_grad[:, D:]
    douter_ref[5:6, :] += jnp.broadcast_to(loss, (1, D))

    @pl.when(step == pl.num_programs(0) - 1)
    def _():
        half = D // 2
        for right in range(2):
            for low in range(2):
                dout_ref[right, low] = acc_s[
                    low * half : (low + 1) * half, right * D : (right + 1) * D
                ]


def head(hidden, targets, mask, totals, out_weight, outer_vectors, scale, momenta):
    streams = hidden.shape[0]
    codes = out_weight.shape[1]
    bias = outer_vectors[3:].reshape(1, codes)
    return pl.pallas_call(
        functools.partial(head_kernel, scale),
        grid=(streams,),
        out_shape=[
            jax.ShapeDtypeStruct((streams, SEG, D), f32),
            jax.ShapeDtypeStruct((2, 2, D // 2, D), f32),
            jax.ShapeDtypeStruct((8, D), f32),
        ],
        in_specs=[
            stream_spec((SEG, D)),
            whole_spec((streams, SEG)),
            whole_spec((streams, SEG)),
            whole_spec((8, 128)),
            whole_spec((D, codes)),
            whole_spec(outer_vectors.shape),
            whole_spec((1, codes)),
            pl.BlockSpec(memory_space=pl.ANY),
        ],
        out_specs=[stream_spec((SEG, D)), whole_spec((2, 2, D // 2, D)), whole_spec((8, D))],
        scratch_shapes=[pltpu.VMEM((D, codes), f32)],
        compiler_params=pltpu.CompilerParams(vmem_limit_bytes=VMEM_LIMIT),
        cost_estimate=pl.CostEstimate(flops=33 * 10**8, bytes_accessed=10**7, transcendentals=10**6),
        name="head",
    )(hidden, targets, mask, totals, out_weight, outer_vectors, bias, momenta)


def feed_back_kernel(streams, g_ref, after_ref, up_ref, down_ref, vec_ref, *refs):
    step = pl.program_id(0)
    grad_ref, dafter_ref, dup_ref, ddown_ref, dvec_ref, done_ref, up_s, down_s, act_s, inner_s = refs[:10]
    carry = AttnCarry(grad_ref, refs[10 : 10 + CARRY_REFS], refs[10 + CARRY_REFS :])

    def beat(place):
        carry.tick(4 * step + place, 4 * streams, 2)

    @pl.when(step == 0)
    def _():
        hail(carry.targets)
        carry.load_all()

    @pl.when(step == 0)
    def _():
        up_s[...] = jnp.zeros_like(up_s)
        down_s[...] = jnp.zeros_like(down_s)
        dvec_ref[...] = jnp.zeros_like(dvec_ref)

    grad = g_ref[...]
    branch = grad.astype(bf16)
    dvec_ref[2:3, :] += column_sum(branch.astype(f32))
    unit, scale = normalised(after_ref[...])
    gain = vec_ref[2:3, :]
    normed = (unit * gain + vec_ref[3:4, :]).astype(bf16)

    @pl.when(step == 0)
    def _():
        meet(carry.targets)
        carry.send_all()

    for tile in range(FF // TILE):
        columns = slice(tile * TILE, (tile + 1) * TILE)
        inner = dot_nn(normed, up_ref[:, columns]) + vec_ref[8 + tile : 9 + tile, :]
        dact = dot_nt(branch, down_ref[columns, :])
        square = inner * inner
        bent = jnp.tanh(GELU_SCALE * (inner + 0.044715 * square * inner))
        half = 0.5 * (1.0 + bent)
        act_s[:, columns] = (inner * half).astype(bf16)
        slope = half + (0.5 * GELU_SCALE) * inner * (1.0 - bent * bent) * (1.0 + 0.134145 * square)
        dinner = (dact * slope).astype(bf16)
        inner_s[:, columns] = dinner
        dvec_ref[4 + tile : 5 + tile, :] += column_sum(dinner.astype(f32))
        if tile % 2:
            beat(tile // 2)
    dnormed = dot_nt(inner_s[...], up_ref[...])
    dvec_ref[0:1, :] += column_sum(dnormed * unit)
    dvec_ref[1:2, :] += column_sum(dnormed)
    dafter_ref[...] = grad + norm_back(dnormed, gain, unit, scale)
    beat(2)
    normed_t = jnp.transpose(normed)
    branch_t = jnp.transpose(branch)
    up_s[...] += dot_nn(normed_t, inner_s[...])
    down_s[...] += dot_nn(branch_t, act_s[...])
    beat(3)

    @pl.when(step == pl.num_programs(0) - 1)
    def _():
        for tile in range(FF // TILE):
            dup_ref[tile] = up_s[:, tile * TILE : (tile + 1) * TILE].astype(bf16)
        ddown_ref[...] = jnp.transpose(down_s[...].astype(bf16))
        carry.rest(4 * streams, 2)
        carry.finish(done_ref)


def feed_back(depth, grad, after, upper, lower, vectors, count, dp_count, attn_grad):
    streams = grad.shape[0]
    rows = attn_grad.shape[0] // (GROUPS * count)
    in_specs = [
        stream_spec((SEG, D)),
        stream_spec((SEG, D)),
        layer_spec(upper.shape[1:], depth),
        layer_spec(lower.shape[1:], depth),
        layer_spec(vectors.shape[1:], depth),
    ]
    out_shape = [
        jax.ShapeDtypeStruct((streams, SEG, D), f32),
        jax.ShapeDtypeStruct((FF // TILE, D, TILE), bf16),
        jax.ShapeDtypeStruct((FF, D), bf16),
        jax.ShapeDtypeStruct((8, D), f32),
    ]
    out_specs = [
        stream_spec((SEG, D)),
        whole_spec((FF // TILE, D, TILE)),
        whole_spec((FF, D)),
        whole_spec((8, D)),
    ]
    scratch = [
        pltpu.VMEM((D, FF), f32),
        pltpu.VMEM((D, FF), f32),
        pltpu.VMEM((SEG, FF), bf16),
        pltpu.VMEM((SEG, FF), bf16),
    ]
    operands = [grad, after, upper, lower, vectors]
    in_specs.append(pl.BlockSpec(memory_space=pl.ANY))
    operands.append(attn_grad.reshape(2, 2, count, rows, D))
    out_shape.append(jax.ShapeDtypeStruct((rows, D), bf16))
    out_specs.append(whole_spec((rows, D)))
    scratch = scratch + carry_scratch("attn", rows, count, dp_count, attn_grad.dtype)
    params = {"collective_id": 6 + depth, "has_side_effects": True}
    return pl.pallas_call(
        functools.partial(feed_back_kernel, streams),
        grid=(streams,),
        out_shape=out_shape,
        in_specs=in_specs,
        out_specs=out_specs,
        scratch_shapes=scratch,
        compiler_params=pltpu.CompilerParams(vmem_limit_bytes=VMEM_LIMIT, **params),
        cost_estimate=pl.CostEstimate(flops=11 * 10**9, bytes_accessed=2 * 10**7, transcendentals=2 * 10**6),
        name="feed_back",
    )(*operands)


def attend_back_kernel(
    streams,
    depth,
    bias_ref,
    dafter_ref,
    x_ref,
    mem_ref,
    keyin_ref,
    q_ref,
    k_ref,
    v_ref,
    lse_ref,
    mixed_ref,
    attn_ref,
    vec_ref,
    frames_ref,
    dup_ref,
    ddown_ref,
    dx_ref,
    dattn_ref,
    dvec_ref,
    din_ref,
    done_ref,
    attn_s,
    dmixed_s,
    dq_s,
    dk_s,
    dv_s,
    ds_s,
    delta_s,
    *refs,
):
    step = pl.program_id(0)
    pairs = HEADS // 2
    carry = FeedCarry(depth, dup_ref, ddown_ref, refs[:CARRY_REFS], refs[CARRY_REFS:])

    @pl.when(step == 0)
    def _():
        hail(carry.targets)
        carry.load_all()
        attn_s[...] = jnp.zeros_like(attn_s)
        dvec_ref[...] = jnp.zeros_like(dvec_ref)
        din_ref[...] = jnp.zeros_like(din_ref)

    dafter = dafter_ref[...]
    branch = dafter.astype(bf16)
    dvec_ref[4:5, :] += column_sum(branch.astype(f32))
    dmixed = dot_nt(branch, attn_ref[3]).astype(bf16)
    dmixed_s[...] = dmixed
    attn_s[3] += dot_nn(jnp.transpose(mixed_ref[...]), branch)
    product = dmixed.astype(f32) * mixed_ref[...].astype(f32)
    high = product.astype(bf16)
    rest = (product - high.astype(f32)).astype(bf16)
    owner = lax.broadcasted_iota(jnp.int32, (HEADS, D), 1) // HEAD_DIM
    pick = (owner == lax.broadcasted_iota(jnp.int32, (HEADS, D), 0)).astype(bf16)
    delta_s[...] = dot_nt(pick, high) + dot_nt(pick, rest)
    first, second = head_masks()
    memory_bias = bias_ref[0]
    key_pos = lax.broadcasted_iota(jnp.int32, (HALF, 2 * HALF), 0)
    query_pos = lax.broadcasted_iota(jnp.int32, (HALF, 2 * HALF), 1) % HALF
    diagonal = key_pos <= query_pos
    head_row = lax.broadcasted_iota(jnp.int32, (PAIR, HALF), 0)

    @pl.when(step == 0)
    def _():
        meet(carry.targets)
        carry.send_all()

    def pair_body(pair, state):
        lanes = pair_lanes(pair)
        q_pair, do_pair = q_ref[:, lanes], dmixed_s[:, lanes]

        def spread(value):
            return jnp.concatenate(
                [value[:HALF] * first, value[:HALF] * second, value[HALF:] * first, value[HALF:] * second], 0
            )

        q_all, do_all = spread(q_pair), spread(do_pair)

        def rows_of(ref):
            one, two = ref[pl.ds(2 * pair, 1), :], ref[pl.ds(2 * pair + 1, 1), :]
            return jnp.concatenate([one[:, :HALF], two[:, :HALF], one[:, HALF:], two[:, HALF:]], 1)

        lse_all, delta_all = rows_of(lse_ref), rows_of(delta_s)
        for block in range(4):
            keys = slice(block * HALF, (block + 1) * HALF)
            start = 2 * HALF if block == 3 else 0
            scores = dot_nt(k_ref[keys, lanes], q_all[start:])
            if block < 2:
                scores = scores + memory_bias
            weights = jnp.exp(scores - lse_all[:, start:])
            if block == 2:
                weights = jnp.concatenate(
                    [jnp.where(diagonal, weights[:, : 2 * HALF], 0.0), weights[:, 2 * HALF :]], 1
                )
            if block == 3:
                weights = jnp.where(diagonal, weights, 0.0)
            dweights = dot_nt(v_ref[keys, lanes], do_all[start:])
            dscores = (weights * (dweights - delta_all[:, start:])).astype(bf16)
            dv_s[keys, lanes] = dot_nn(weights.astype(bf16), do_all[start:]).astype(bf16)
            dk_s[keys, lanes] = dot_nn(dscores, q_all[start:]).astype(bf16)
            ds_s[keys, start:] = dscores
        k_t = jnp.transpose(k_ref[:, lanes])
        for block in range(2):
            seen = SEG + (block + 1) * HALF
            grads = dot_nn(k_t[:, :seen], ds_s[:seen, block * 2 * HALF : (block + 1) * 2 * HALF])
            grads = jnp.where(head_row < HEAD_DIM, grads[:, :HALF], grads[:, HALF:])
            dq_s[block * HALF : (block + 1) * HALF, lanes] = (
                jnp.transpose(grads) * (HEAD_DIM**-0.5)
            ).astype(bf16)
        carry.tick(pairs * step + pair, pairs * streams, 1)
        return state

    lax.fori_loop(0, pairs, pair_body, 0)
    dq, dk, dv = dq_s[...], dk_s[...], dv_s[...]
    keyin_t = jnp.transpose(keyin_ref[...])
    attn_s[0] += dot_nn(keyin_t[:, SEG:], dq)
    attn_s[1] += dot_nn(keyin_t, dk)
    attn_s[2] += dot_nn(keyin_t, dv)
    dvec_ref[2:3, :] += column_sum(dq.astype(f32))
    dvec_ref[3:4, :] += column_sum(dv.astype(f32))
    dkeyin = dot_nt(dk, attn_ref[1]) + dot_nt(dv, attn_ref[2])
    dmem = dkeyin[:SEG]
    down = dkeyin[SEG:] + dot_nt(dq, attn_ref[0])
    gain = vec_ref[0:1, :]
    unit, scale = normalised(x_ref[...])
    mem_unit, _ = normalised(mem_ref[...].astype(f32))
    dvec_ref[0:1, :] += column_sum(down * unit + dmem * mem_unit)
    dvec_ref[1:2, :] += column_sum(down + dmem)
    dx = dafter + norm_back(down, gain, unit, scale)
    dx_ref[...] = dx
    if depth == 0:
        dx_high = dx.astype(bf16)
        dx_rest = (dx - dx_high.astype(f32)).astype(bf16)
        din_ref[...] += dot_nn(frames_ref[...], dx_high) + dot_nn(frames_ref[...], dx_rest)
        dvec_ref[5:6, :] += column_sum(dx)

    @pl.when(step == pl.num_programs(0) - 1)
    def _():
        dattn_ref[...] = attn_s[...].astype(bf16)
        carry.rest(pairs * streams, 1)
        carry.finish(done_ref)


def attend_back(depth, bias, dafter, x, memory, saved, attn, vectors, frames, up_grad, down_grad, count, dp_count):
    streams = dafter.shape[0]
    keyin, q, k, v, lse, mixed = saved
    inputs = frames.shape[1]
    rows = D // count
    up_grad, down_grad = up_grad.reshape(4, count, rows, D), down_grad.reshape(count, 4, rows, D)
    return pl.pallas_call(
        functools.partial(attend_back_kernel, streams, depth),
        grid=(streams,),
        out_shape=[
            jax.ShapeDtypeStruct((streams, SEG, D), f32),
            jax.ShapeDtypeStruct((4, D, D), bf16),
            jax.ShapeDtypeStruct((8, D), f32),
            jax.ShapeDtypeStruct((inputs, D), f32),
            jax.ShapeDtypeStruct((4, rows, D), bf16),
        ],
        in_specs=[
            pl.BlockSpec(memory_space=pltpu.SMEM),
            stream_spec((SEG, D)),
            stream_spec((SEG, D)),
            stream_spec((SEG, D)),
            stream_spec((2 * SEG, D)),
            stream_spec((SEG, D)),
            stream_spec((2 * SEG, D)),
            stream_spec((2 * SEG, D)),
            stream_spec((HEADS, SEG)),
            stream_spec((SEG, D)),
            layer_spec(attn.shape[1:], depth),
            layer_spec(vectors.shape[1:], depth),
            stream_spec((inputs, SEG)),
            pl.BlockSpec(memory_space=pl.ANY),
            pl.BlockSpec(memory_space=pl.ANY),
        ],
        out_specs=[
            stream_spec((SEG, D)),
            whole_spec((4, D, D)),
            whole_spec((8, D)),
            whole_spec((inputs, D)),
            whole_spec((4, rows, D)),
        ],
        scratch_shapes=[
            pltpu.VMEM((4, D, D), f32),
            pltpu.VMEM((SEG, D), bf16),
            pltpu.VMEM((SEG, D), bf16),
            pltpu.VMEM((2 * SEG, D), bf16),
            pltpu.VMEM((2 * SEG, D), bf16),
            pltpu.VMEM((2 * SEG, 2 * SEG), bf16),
            pltpu.VMEM((HEADS, SEG), f32),
        ]
        + carry_scratch("feed", rows, count, dp_count),
        compiler_params=pltpu.CompilerParams(
            collective_id=4 + depth, has_side_effects=True, vmem_limit_bytes=VMEM_LIMIT
        ),
        cost_estimate=pl.CostEstimate(flops=3 * 10**10, bytes_accessed=2 * 10**7, transcendentals=10**7),
        name="attend_back",
    )(bias, dafter, x, memory, keyin, q, k, v, lse, mixed, attn, vectors, frames, up_grad, down_grad)


def from_behind(value, axis, steps):
    count = lax.axis_size(axis)
    leading, last = (max(0, -steps), min(count, count - steps))
    return lax.ppermute(value, axis, [(source, source + steps) for source in range(leading, last)])


def adamw(weight, moment, second, grad, rate, decay):
    moment = 0.5 * moment + 0.5 * grad
    second = 0.99 * second + 0.01 * grad * grad
    fixed_moment = moment / (1.0 - 0.5**STEP)
    fixed_second = second / (1.0 - 0.99**STEP)
    weight = weight * (1.0 - rate * decay) - rate * fixed_moment / (jnp.sqrt(fixed_second) + 1e-08)
    return (weight, moment, second)


GROUPS = 4
UNITS = 6
SMALL = 128


def peers():
    count = {"seg": lax.axis_size("seg"), "dp": lax.axis_size("dp")}
    seg, dp = lax.axis_index("seg"), lax.axis_index("dp")
    core, x, y = seg % 2, dp % 2, (dp // 2) % 2
    across_core = {"seg": seg + 1 - 2 * core}
    across_x = {"dp": dp + 1 - 2 * x}
    across_y = {"dp": dp + 2 - 4 * y}
    across_both = {"dp": dp + 3 - 2 * x - 4 * y}
    far = []
    step = GROUPS
    while step < count["dp"]:
        far.append({"dp": dp + step - 2 * step * ((dp // step) % 2)})
        step *= 2
    return seg, dp, core, x, y, across_core, (across_x, across_y, across_both), far


def others(seg, count):
    return [lax.rem(seg + step, count) for step in range(1, count)]


def hail(targets):
    barrier = pltpu.get_barrier_semaphore()
    for target in targets:
        pl.semaphore_signal(barrier, inc=1, device_id=target, device_id_type=pl.DeviceIdType.MESH)


def meet(targets):
    pl.semaphore_wait(pltpu.get_barrier_semaphore(), len(targets))


def greet(seg, count, near, far):
    targets = [{"seg": other} for other in others(seg, count)] + list(near) + list(far)
    hail(targets)
    meet(targets)


def remote(source, target, send, recv, device):
    return pltpu.make_async_remote_copy(
        src_ref=source,
        dst_ref=target,
        send_sem=send,
        recv_sem=recv,
        device_id=device,
        device_id_type=pl.DeviceIdType.MESH,
    )


def wait_bytes(ref, sem):
    pltpu.make_async_copy(ref, ref, sem).wait()


def plus(left, right):
    return (left.astype(f32) + right.astype(f32)).astype(left.dtype)


def owners(count):
    attn, feed = count // 4 - 1, count // 4
    return (
        (0, 1, 2 * attn, 0),
        (1, 1, 2 * attn + 1, 0),
        (2, 2, 2 * feed, 0),
        (4, 2, 2 * feed + 1, 2),
    )


def lowest_bit(mask, planes):
    bit = 1
    while bit < planes and not mask & bit:
        bit *= 2
    return bit


class Carry:
    def __init__(self, refs, sems):
        self.mine, self.got0, self.got1, self.got2, self.got3, self.goth = refs
        (
            self.load,
            self.send0,
            self.recv0,
            self.send1,
            self.recv1,
            self.send2,
            self.recv2,
            self.send3,
            self.recv3,
            self.sendh,
            self.recvh,
        ) = sems
        self.seg, self.dp, self.core, self.x, self.y, self.across_core, near, self.far = peers()
        self.across_x, self.across_y, _ = near
        self.planes = self.mine.shape[0]
        self.plane = self.seg // 2
        self.targets = [self.across_core, self.across_x, self.across_y] + self.far
        bit = 1
        while bit < self.planes:
            self.targets.append({"seg": 2 * self.toggled(bit) + self.core})
            bit *= 2

        places = []
        for low in range(self.planes.bit_length()):
            places += [mask for mask in reversed(range(self.planes)) if lowest_bit(mask, self.planes) == 1 << low]
        self.order = places

    def toggled(self, mask):
        place, bit = self.plane, 1
        while bit <= mask:
            if mask & bit:
                place = place + bit - 2 * bit * ((self.plane // bit) % 2)
            bit *= 2
        return place

    def load_all(self):
        for step in range(self.planes):
            for source, place in self.pieces(2 * self.toggled(self.order[step]) + self.core):
                pltpu.make_async_copy(source, self.mine.at[(step,) + place], self.load.at[step]).start()

    def send_all(self):
        for step in range(self.planes):
            for source, place in self.pieces(2 * self.toggled(self.order[step]) + 1 - self.core):
                remote(
                    source, self.got0.at[(step,) + place], self.send0.at[step], self.recv0.at[step], self.across_core
                ).start()

    def begin(self, step):
        wait_bytes(self.mine.at[step], self.load.at[step])
        wait_bytes(self.got0.at[step], self.recv0.at[step])
        for place in range(2):
            self.mine[step, place] = plus(self.mine[step, place], self.got0[step, place])
        for copy in self.first(step):
            copy.start()

    def across(self, place, step):
        return remote(
            self.held(step),
            self.goth.at[place, step],
            self.sendh.at[place, step],
            self.recvh.at[place, step],
            self.far[place],
        )

    def third(self, step):
        mask = self.order[step]
        return remote(
            self.held(step),
            self.got3.at[mask],
            self.send3.at[step],
            self.recv3.at[mask],
            {"seg": 2 * self.toggled(lowest_bit(mask, self.planes)) + self.core},
        )

    def onward(self, step):
        held = self.held(step)
        for place in range(len(self.far)):
            copy = self.across(place, step)
            copy.start()
            copy.wait()
            held[...] = plus(held[...], self.goth[place, step])
        mask, bit = self.order[step], 1
        value = held[...].astype(f32)
        while bit < lowest_bit(mask, self.planes):
            wait_bytes(self.got3.at[mask + bit], self.recv3.at[mask + bit])
            value = value + self.got3[mask + bit].astype(f32)
            bit *= 2
        held[...] = value.astype(held.dtype)
        if mask:
            self.third(step).start()

    def total(self):
        return self.held(self.planes - 1)[...]

    def actions(self, time, slack):
        planes = self.planes
        started = range(2) if time == 0 else range(time + 1, time + 2)
        for step in started:
            if step < planes:
                self.begin(step)
        if 0 <= time - slack < planes:
            self.middle(time - slack)
        if 0 <= time - slack - 2 < planes:
            self.end(time - slack - 2)

    def tick(self, time, last, slack):
        for place in range(last):

            @pl.when(time == place)
            def _():
                self.actions(place, slack)

    def rest(self, first, slack):
        for time in range(first, self.planes + slack + 2):
            self.actions(time, slack)


class AttnCarry(Carry):
    def __init__(self, source, refs, sems):
        super().__init__(refs, sems)
        self.source = source

    def pieces(self, row):
        return ((self.source.at[:, :, row], ()),)

    def held(self, step):
        return self.mine.at[step, self.y, self.x]

    def first(self, step):
        return (
            remote(
                self.mine.at[step, :, 1 - self.x],
                self.got1.at[step],
                self.send1.at[step],
                self.recv1.at[step],
                self.across_x,
            ),
        )

    def second(self, step):
        return remote(
            self.mine.at[step, 1 - self.y, self.x],
            self.got2.at[step],
            self.send2.at[step],
            self.recv2.at[step],
            self.across_y,
        )

    def middle(self, step):
        for copy in self.first(step):
            copy.wait_recv()
        for place in range(2):
            self.mine[step, place, self.x] = plus(self.mine[step, place, self.x], self.got1[step, place])
        self.second(step).start()

    def end(self, step):
        self.second(step).wait_recv()
        self.mine[step, self.y, self.x] = plus(self.mine[step, self.y, self.x], self.got2[step])
        self.onward(step)

    def finish(self, out_ref):
        out_ref[...] = self.total().astype(out_ref.dtype)
        self.drain()

    def drain(self):
        for step in range(self.planes):
            wait_bytes(self.mine.at[step], self.send0.at[step])
            for copy in self.first(step):
                copy.wait_send()
            self.second(step).wait_send()
            if step < self.planes - 1:
                self.third(step).wait_send()


class FeedCarry(Carry):
    def __init__(self, depth, up, down, refs, sems):
        super().__init__(refs, sems)
        self.up, self.down = up, down
        self.owner = (self.x == self.y) if depth == 1 else (self.x != self.y)
        self.keep = self.x if depth == 1 else 1 - self.x

    def pieces(self, row):
        return ((self.up.at[:, row], (0,)), (self.down.at[row], (1,)))

    def held(self, step):
        return self.mine.at[step, self.y]

    def first(self, step):
        return (
            remote(
                self.mine.at[step, 1 - self.keep, 0:2],
                self.got1.at[step, 0],
                self.send1.at[step, 0],
                self.recv1.at[step, 0],
                self.across_x,
            ),
            remote(
                self.mine.at[step, 1 - self.y, 2:4],
                self.got1.at[step, 1],
                self.send1.at[step, 1],
                self.recv1.at[step, 1],
                self.across_y,
            ),
        )

    def second(self, step):
        return (
            remote(
                self.mine.at[step, self.keep, 0:2],
                self.got2.at[step, 0],
                self.send2.at[step, 0],
                self.recv2.at[step, 0],
                self.across_y,
            ),
            remote(
                self.mine.at[step, self.y, 2:4],
                self.got2.at[step, 1],
                self.send2.at[step, 1],
                self.recv2.at[step, 1],
                self.across_x,
            ),
        )

    def middle(self, step):
        for copy in self.first(step):
            copy.wait_recv()
        self.mine[step, self.keep, 0:2] = plus(self.mine[step, self.keep, 0:2], self.got1[step, 0])
        self.mine[step, self.y, 2:4] = plus(self.mine[step, self.y, 2:4], self.got1[step, 1])

        @pl.when(jnp.logical_not(self.owner))
        def _():
            for copy in self.second(step):
                copy.start()

    def end(self, step):
        @pl.when(self.owner)
        def _():
            for place in range(2):
                wait_bytes(self.got2.at[step, place], self.recv2.at[step, place])
                span = slice(2 * place, 2 * place + 2)
                self.mine[step, self.y, span] = plus(self.mine[step, self.y, span], self.got2[step, place])
            self.onward(step)

    def finish(self, out_ref):
        @pl.when(self.owner)
        def _():
            out_ref[...] = self.total().astype(out_ref.dtype)
            for step in range(self.planes - 1):
                self.third(step).wait_send()

        @pl.when(jnp.logical_not(self.owner))
        def _():
            out_ref[...] = jnp.zeros_like(out_ref)
            for step in range(self.planes):
                for copy in self.second(step):
                    copy.wait_send()

        for step in range(self.planes):
            wait_bytes(self.mine.at[step], self.send0.at[step])
            for copy in self.first(step):
                copy.wait_send()


CARRY_REFS = 6
CARRY_SEMS = 11


def carry_scratch(kind, rows, count, dp_count, dtype=bf16):
    planes = count // 2
    far = max(1, dp_count.bit_length() - 3)
    dma = pltpu.SemaphoreType.DMA
    if kind == "attn":
        shapes = ((planes, 2, 2), (planes, 2, 2), (planes, 2), (planes,), (planes,), (far, planes))
        pair = (planes,)
    else:
        shapes = (
            (planes, 2, 4),
            (planes, 2, 4),
            (planes, 2, 2),
            (planes, 2, 2),
            (planes, 4),
            (far, planes, 4),
        )
        pair = (planes, 2)
    one = (planes,)
    sems = (one, one, one, pair, pair, pair, pair, one, one, (far, planes), (far, planes))
    return [pltpu.VMEM(shape + (rows, D), dtype) for shape in shapes] + [dma(shape) for shape in sems]


def reduce_kernel(
    count,
    attn_grad_ref,
    attn_done_ref,
    feed_low_ref,
    feed_high_ref,
    dout_ref,
    din_ref,
    vec0_ref,
    vec1_ref,
    vec2_ref,
    vec3_ref,
    outer_ref,
    whole_ref,
    own_ref,
    small_out,
    square_out,
    small_ref,
    small_core,
    small_s,
    small_got,
    sq_seg,
    sq_dp,
    small_send,
    small_recv,
    whole_send,
    whole_recv,
    half_sem,
    sq_send,
    sq_recv,
    sqd_send,
    sqd_recv,
    *refs,
):
    carry = AttnCarry(attn_grad_ref, refs[:CARRY_REFS], refs[CARRY_REFS:])
    seg, dp, core, x, y, across_core, near, far = peers()
    across_x, across_y, across_both = near
    planes = count // 2
    plane = seg // 2
    group = 2 * y + x
    targets = [{"seg": other} for other in others(seg, count)] + list(near) + list(far)
    hail(targets)
    carry.load_all()
    own_ref[1] = attn_done_ref[...]

    @pl.when(x == y)
    def _():
        own_ref[2:6] = feed_high_ref[...]

    @pl.when(x != y)
    def _():
        own_ref[2:6] = feed_low_ref[...]

    inputs = din_ref.shape[0]
    small_ref[0:inputs, :] = din_ref[...]
    for place, ref in enumerate((vec0_ref, vec1_ref, vec2_ref, vec3_ref, outer_ref)):
        small_ref[inputs + 8 * place : inputs + 8 * place + 8, :] = ref[...]
    small_ref[inputs + 40 :, :] = jnp.zeros((SMALL - inputs - 40, D), f32)
    meet(targets)
    carry.send_all()

    def small_steps():
        copy = remote(small_ref, small_core, small_send.at[0], small_recv.at[0], across_core)
        copy.start()
        yield
        copy.wait()
        small_s[...] = small_ref[...] + small_core[...]
        half = pl.ds(pl.multiple_of(core * (SMALL // 2), 8), SMALL // 2)
        targets = [across_x, across_y] + far
        step = 1
        while step < planes:
            targets.append({"seg": seg + 2 * step - 4 * step * ((plane // step) % 2)})
            step *= 2
        for place, target in enumerate(targets):
            copy = remote(
                small_s.at[half],
                small_got.at[place],
                small_send.at[place + 1],
                small_recv.at[place + 1],
                target,
            )
            copy.start()
            yield
            copy.wait()
            small_s[half, :] += small_got[place]
        small_out[half, :] = small_s[half, :]
        last = len(targets) + 1
        copy = remote(small_out.at[half], small_out.at[half], small_send.at[last], small_recv.at[last], across_core)
        copy.start()
        yield
        copy.wait()

    small_run = small_steps()
    next(small_run)
    roles = owners(count)

    def gift(place):
        first, width, owner, spot = roles[place]
        return remote(
            own_ref.at[first : first + width],
            whole_ref.at[seg, spot : spot + width],
            whole_send.at[place],
            whole_recv.at[seg],
            {"seg": owner},
        )

    def give(place):
        first, width, owner, spot = roles[place]

        @pl.when(seg != owner)
        def _():
            gift(place).start()

        @pl.when(seg == owner)
        def _():
            whole_ref[seg, spot : spot + width] = own_ref[first : first + width]

    for place in (2, 3, 1):
        give(place)
    for time in range(planes + 3):
        carry.actions(time, 1)
        next(small_run, None)
    own_ref[0] = carry.total()
    give(0)
    for _ in small_run:
        pass
    shard = dout_ref[...].astype(f32)
    square = jnp.sum(jnp.sum(shard * shard, 0, keepdims=True), 1, keepdims=True)
    for unit in range(UNITS):
        value = own_ref[unit].astype(f32)
        square = square + jnp.sum(jnp.sum(value * value, 0, keepdims=True), 1, keepdims=True)
    sq_seg[seg] = jnp.broadcast_to(square, (8, 128))
    for step, other in enumerate(others(seg, count)):
        remote(sq_seg.at[seg], sq_seg.at[seg], sq_send.at[step], sq_recv.at[seg], {"seg": other}).start()
    for other in others(seg, count):
        wait_bytes(sq_seg.at[other], sq_recv.at[other])
    sq_dp[group] = jnp.sum(sq_seg[...], 0)
    for place, target in enumerate(near):
        remote(sq_dp.at[group], sq_dp.at[group], sqd_send.at[place], sqd_recv.at[place], target).start()
    sums = small_out[...]
    is_loss = lax.broadcasted_iota(jnp.int32, (SMALL, D), 0) == inputs + 37
    sums = jnp.where(is_loss, 0.0, sums)
    small_square = jnp.sum(jnp.sum(sums * sums, 0, keepdims=True), 1, keepdims=True)
    for place, target in enumerate(near):
        remote(sq_dp.at[group], sq_dp.at[group], sqd_send.at[place], sqd_recv.at[place], target).wait()
    square_out[...] = jnp.sum(sq_dp[...], 0) + jnp.broadcast_to(small_square, (8, 128))

    for place, (first, width, owner, spot) in enumerate(roles):

        @pl.when(seg == owner)
        def _():
            for other in others(seg, count):
                wait_bytes(whole_ref.at[other, spot : spot + width], whole_recv.at[other])
            if width == 2:
                span = slice(spot, spot + width)
                copy = remote(
                    whole_ref.at[:, span], whole_ref.at[:, span], half_sem.at[0], half_sem.at[1], across_core
                )
                copy.start()
                copy.wait()

    carry.drain()
    for place, (first, width, owner, spot) in enumerate(roles):

        @pl.when(seg != owner)
        def _():
            gift(place).wait_send()

    for step in range(count - 1):
        wait_bytes(sq_seg.at[0], sq_send.at[step])


def reduce_grads(count, dp_count, attn, done, feed_low, feed_high, dout, pieces):
    rows = D // count
    planes = count // 2
    stages = 2 + planes.bit_length() + max(0, dp_count.bit_length() - 3)
    dma = pltpu.SemaphoreType.DMA
    vmem = pl.BlockSpec(memory_space=pltpu.VMEM)
    return pl.pallas_call(
        functools.partial(reduce_kernel, count),
        out_shape=[
            jax.ShapeDtypeStruct((count, 4, rows, D), bf16),
            jax.ShapeDtypeStruct((UNITS, rows, D), bf16),
            jax.ShapeDtypeStruct((SMALL, D), f32),
            jax.ShapeDtypeStruct((8, 128), f32),
        ],
        in_specs=[pl.BlockSpec(memory_space=pl.ANY)] + [vmem] * 10,
        out_specs=[vmem] * 4,
        scratch_shapes=[
            pltpu.VMEM((SMALL, D), f32),
            pltpu.VMEM((SMALL, D), f32),
            pltpu.VMEM((SMALL, D), f32),
            pltpu.VMEM((stages, SMALL // 2, D), f32),
            pltpu.VMEM((count, 8, 128), f32),
            pltpu.VMEM((GROUPS, 8, 128), f32),
            dma((stages + 2,)),
            dma((stages + 2,)),
            dma((4,)),
            dma((count,)),
            dma((2,)),
            dma((count,)),
            dma((count,)),
            dma((3,)),
            dma((3,)),
        ]
        + carry_scratch("attn", rows, count, dp_count),
        compiler_params=pltpu.CompilerParams(
            collective_id=1, has_side_effects=True, vmem_limit_bytes=VMEM_LIMIT
        ),
        cost_estimate=pl.CostEstimate(flops=10**8, bytes_accessed=10**8, transcendentals=0),
        name="reduce_grads",
    )(attn.reshape(2, 2, count, rows, D), done, feed_low, feed_high, dout, *pieces)


def halves(value):
    high = value.astype(bf16)
    return high, (value - high.astype(f32)).astype(bf16)


def times(left, right):
    (left_high, left_low), (right_high, right_low) = left, right
    return dot_nn(
        jnp.concatenate([left_high, left_high, left_low], 1),
        jnp.concatenate([right_high, right_low, right_high], 0),
    )


def times_t(left, right):
    (left_high, left_low), (right_high, right_low) = left, right
    return dot_nt(
        jnp.concatenate([left_high, left_high, left_low], 1),
        jnp.concatenate([right_high, right_low, right_high], 1),
    )


def clip_of(norm):
    return jnp.minimum(1.0, 0.25 / (norm + 1e-06))


def muon_kernel(
    count,
    square_ref,
    whole_ref,
    mom_ref,
    own_ref,
    update_ref,
    every_ref,
    norm_ref,
    made_ref,
    x_s,
    q_s,
    gram_s,
    high_s,
    low_s,
    send,
    recv,
    on_send,
    on_recv,
    own_send,
    own_recv,
):
    seg, dp, core, x, y, across_core, near, far = peers()
    group = 2 * y + x
    plane = seg // 2
    targets = [{"seg": other} for other in others(seg, count)] + list(near)
    hail(targets)
    is_down = group >= 2
    norm = jnp.sqrt(square_ref[0:1, 0:1])
    norm_ref[...] = jnp.broadcast_to(norm, norm_ref.shape)
    clip = clip_of(norm)
    eye = (
        lax.broadcasted_iota(jnp.int32, (D, D), 0) == lax.broadcasted_iota(jnp.int32, (D, D), 1)
    ).astype(f32)
    rows = whole_ref.shape[2]
    makers = [attn for _, _, attn, _ in owners(count)]
    units = [makers[0], makers[1], makers[2], makers[2], makers[3], makers[3]]

    def own_rows(side):
        return remote(own_ref, every_ref.at[group], own_send.at[side], own_recv.at[side], near[side])

    def gift(unit, slot, other):
        return remote(
            made_ref.at[other, slot],
            update_ref.at[group, unit],
            send.at[slot, other],
            recv.at[unit],
            {"seg": other},
        )

    def give(unit, slot):
        for other in others(seg, count):
            gift(unit, slot, other).start()
        update_ref[group, unit] = made_ref[seg, slot]

    def onward(unit, side):
        block = update_ref.at[group, unit]
        return remote(block, block, on_send.at[side, unit], on_recv.at[side, unit], near[side])

    meet(targets)
    for side in range(3):
        own_rows(side).start()
    every_ref[group] = own_ref[...]

    @pl.when(plane == count // 4 - 1)
    def _():
        start = (0.5 * mom_ref[:, core].astype(f32)).reshape(D, D)
        start = start + clip * whole_ref[:, 0].astype(f32).reshape(D, D)
        size = jnp.sum(jnp.sum(start * start, 0, keepdims=True), 1, keepdims=True)
        x_s[...] = start / (jnp.sqrt(size) + 1e-07)

        def sweep(_, carry):
            value = x_s[...]
            both = halves(value)
            gram = times_t(both, both)
            gram_both = halves(gram)
            poly = -4.775 * gram + 2.0315 * times(gram_both, gram_both)
            x_s[...] = 3.4445 * value + times(halves(poly), both)
            return carry

        lax.fori_loop(0, 5, sweep, 0)
        made_ref[:, 0] = x_s[...].astype(bf16).reshape(count, rows, D)
        for unit in range(2):

            @pl.when(core == unit)
            def _():
                give(unit, 0)

    @pl.when(plane == count // 4)
    def _():
        gram_s[...] = jnp.zeros_like(gram_s)

        def gather(tile, size):
            value = (0.5 * mom_ref[:, 2 + tile].astype(f32)).reshape(D, D)
            value = value + clip * whole_ref[:, tile].astype(f32).reshape(D, D)
            high, low = halves(value)
            high_s[tile] = high
            low_s[tile] = low

            @pl.when(is_down)
            def _():
                high_s[tile] = jnp.transpose(high_s[tile])
                low_s[tile] = jnp.transpose(low_s[tile])

            both = high_s[tile], low_s[tile]
            gram_s[...] += times_t(both, both)
            return size + jnp.sum(jnp.sum(value * value, 0, keepdims=True), 1, keepdims=True)

        size = lax.fori_loop(0, 4, gather, jnp.zeros((1, 1), f32))
        scale = 1.0 / (jnp.sqrt(size) + 1e-07)
        gram_s[...] = gram_s[...] * (scale * scale)

        def poly_of(gram, gram_both):
            return 3.4445 * eye - 4.775 * gram + 2.0315 * times(gram_both, gram_both)

        def advance(gram_both, poly_both):
            gram_s[...] = times(halves(times(gram_both, poly_both)), poly_both)

        gram = gram_s[...]
        gram_both = halves(gram)
        poly = poly_of(gram, gram_both)
        q_s[...] = poly
        advance(gram_both, halves(poly))

        def sweep(_, carry):
            gram = gram_s[...]
            gram_both = halves(gram)
            poly_both = halves(poly_of(gram, gram_both))
            q_s[...] = times(halves(q_s[...]), poly_both)
            advance(gram_both, poly_both)
            return carry

        lax.fori_loop(0, 3, sweep, 0)
        gram = gram_s[...]
        last = times(halves(q_s[...]), halves(poly_of(gram, halves(gram)))) * scale
        last_both = halves(last)
        for slot in range(2):
            tile = 2 * core + slot
            x_s[...] = times(last_both, (high_s[tile], low_s[tile]))

            @pl.when(is_down)
            def _():
                x_s[...] = jnp.transpose(x_s[...])

            made_ref[:, slot] = x_s[...].astype(bf16).reshape(count, rows, D)
            for half in range(2):

                @pl.when(core == half)
                def _():
                    give(2 + 2 * half + slot, slot)

    for unit in (0, 1, 2, 4, 3, 5):

        @pl.when(seg != units[unit])
        def _():
            wait_bytes(update_ref.at[group, unit], recv.at[unit])

        for side in range(3):
            onward(unit, side).start()
    for side in range(3):
        own_rows(side).wait()
    for unit in range(UNITS):
        for side in range(3):
            onward(unit, side).wait()

        @pl.when(seg == units[unit])
        def _():
            slot = 0 if unit < 2 else unit % 2
            for other in others(seg, count):
                gift(unit, slot, other).wait_send()


def muon(count, squares, whole, momenta, own):
    rows = whole.shape[2]
    dma = pltpu.SemaphoreType.DMA
    vmem = pl.BlockSpec(memory_space=pltpu.VMEM)
    blocks = jax.ShapeDtypeStruct((GROUPS, UNITS, rows, D), bf16)
    return pl.pallas_call(
        functools.partial(muon_kernel, count),
        out_shape=[blocks, blocks, jax.ShapeDtypeStruct((8, 128), f32)],
        in_specs=[vmem] * 4,
        out_specs=[vmem] * 3,
        scratch_shapes=[
            pltpu.VMEM((count, 2, rows, D), bf16),
            pltpu.VMEM((D, D), f32),
            pltpu.VMEM((D, D), f32),
            pltpu.VMEM((D, D), f32),
            pltpu.VMEM((4, D, D), bf16),
            pltpu.VMEM((4, D, D), bf16),
            dma((2, count)),
            dma((UNITS,)),
            dma((3, UNITS)),
            dma((3, UNITS)),
            dma((3,)),
            dma((3,)),
        ],
        compiler_params=pltpu.CompilerParams(
            collective_id=2, has_side_effects=True, vmem_limit_bytes=VMEM_LIMIT
        ),
        cost_estimate=pl.CostEstimate(flops=2 * 10**10, bytes_accessed=4 * 10**7, transcendentals=0),
        name="muon",
    )(squares, whole, momenta, own)


def embed_kernel(
    count,
    frames_ref,
    mask_ref,
    in_ref,
    outer_ref,
    x_ref,
    mem_ref,
    total_ref,
    got_s,
    count_s,
    frame_send,
    frame_recv,
    count_send,
    count_recv,
):
    seg = lax.axis_index("seg")
    after, before = lax.rem(seg + 1, count), lax.rem(seg + count - 1, count)
    streams = frames_ref.shape[0]
    tally = jnp.sum(mask_ref[...].astype(f32), 1, keepdims=True)
    count_s[seg] = jnp.broadcast_to(
        jnp.concatenate([tally, jnp.zeros((8 - streams, 1), f32)], 0), (8, 128)
    )
    greet(seg, count, (), ())
    frame_copy = remote(frames_ref, got_s, frame_send.at[0], frame_recv.at[0], {"seg": after})
    frame_copy.start()
    for step, other in enumerate(others(seg, count)):
        remote(count_s.at[seg], count_s.at[seg], count_send.at[step], count_recv.at[seg], {"seg": other}).start()
    weight, shift = in_ref[...], outer_ref[0:1, :]
    for stream in range(streams):
        x_ref[stream] = dot_nn(jnp.transpose(frames_ref[stream]), weight) + shift
    frame_copy.wait()
    for stream in range(streams):
        mem_ref[stream] = (dot_nn(jnp.transpose(got_s[stream]), weight) + shift).astype(bf16)
    for other in others(seg, count):
        wait_bytes(count_s.at[other], count_recv.at[other])
    total_ref[...] = jnp.sum(count_s[...], 0)
    for step in range(count - 1):
        wait_bytes(count_s.at[0], count_send.at[step])


def embed(count, frames, mask, in_weight, outer_vectors):
    streams = frames.shape[0]
    dma = pltpu.SemaphoreType.DMA
    return pl.pallas_call(
        functools.partial(embed_kernel, count),
        out_shape=[
            jax.ShapeDtypeStruct((streams, SEG, D), f32),
            jax.ShapeDtypeStruct((streams, SEG, D), bf16),
            jax.ShapeDtypeStruct((8, 128), f32),
        ],
        in_specs=[pl.BlockSpec(memory_space=pltpu.VMEM)] * 4,
        out_specs=[pl.BlockSpec(memory_space=pltpu.VMEM)] * 3,
        scratch_shapes=[
            pltpu.VMEM(frames.shape, bf16),
            pltpu.VMEM((count, 8, 128), f32),
            dma((1,)),
            dma((1,)),
            dma((count,)),
            dma((count,)),
        ],
        compiler_params=pltpu.CompilerParams(
            collective_id=3, has_side_effects=True, vmem_limit_bytes=VMEM_LIMIT
        ),
        cost_estimate=pl.CostEstimate(flops=2 * 10**8, bytes_accessed=4 * 10**6, transcendentals=0),
        name="embed",
    )(frames, mask, in_weight, outer_vectors)


FEED_UP = (1, 0)
FEED_DOWN = (2, 3)
KEEP = 1.0 - 0.3 * 0.01


def finish_kernel(norm_ref, every_ref, update_ref, dout_ref, small_ref, *refs):
    (
        attn_ref,
        attn_mom_ref,
        up_ref,
        up_mom_ref,
        down_ref,
        down_mom_ref,
        out_ref,
        out_mom_ref,
        out_sec_ref,
        in_ref,
        in_mom_ref,
        in_sec_ref,
        vec_ref,
        vec_mom_ref,
        vec_sec_ref,
        outer_ref,
        outer_mom_ref,
        outer_sec_ref,
        attn_new,
        attn_mom_new,
        attn_copy_new,
        up_new,
        up_mom_new,
        up_copy_new,
        down_new,
        down_mom_new,
        down_copy_new,
        out_new,
        out_mom_new,
        out_sec_new,
        out_copy_new,
        in_new,
        in_mom_new,
        in_sec_new,
        in_copy_new,
        vec_new,
        vec_mom_new,
        vec_sec_new,
        outer_new,
        outer_mom_new,
        outer_sec_new,
        loss_new,
        norm_new,
    ) = refs
    clip = clip_of(norm_ref[0:1, 0:1])

    def muon_step(weight, momentum, grad, update, scale):
        weight = weight * KEEP - (0.3 * scale) * update.astype(f32)
        return weight, 0.5 * momentum + clip * grad.astype(f32)

    up_scale, down_scale = max(1.0, FF / D) ** 0.5, max(1.0, D / FF) ** 0.5
    for depth in range(LAYERS):
        for kind in range(4):
            weight, momentum = muon_step(
                attn_ref[depth, kind],
                attn_mom_ref[depth, kind],
                every_ref[kind, depth],
                update_ref[kind, depth],
                1.0,
            )
            attn_new[depth, kind] = weight
            attn_mom_new[depth, kind] = momentum
            attn_copy_new[depth, kind] = weight.astype(bf16)
            columns = slice(kind * TILE, (kind + 1) * TILE)
            weight, momentum = muon_step(
                up_ref[depth, :, columns],
                up_mom_ref[depth, :, columns],
                every_ref[FEED_UP[depth], 2 + kind],
                update_ref[FEED_UP[depth], 2 + kind],
                up_scale,
            )
            up_new[depth, :, columns] = weight
            up_mom_new[depth, :, columns] = momentum
            up_copy_new[depth, :, columns] = weight.astype(bf16)
            weight, momentum = muon_step(
                down_ref[depth, kind],
                down_mom_ref[depth, kind],
                every_ref[FEED_DOWN[depth], 2 + kind],
                update_ref[FEED_DOWN[depth], 2 + kind],
                down_scale,
            )
            down_new[depth, kind] = weight
            down_mom_new[depth, kind] = momentum
            down_copy_new[depth, kind] = weight.astype(bf16)
    for low in range(2):
        for right in range(2):
            columns = slice(right * D, (right + 1) * D)
            weight, moment, second = adamw(
                out_ref[low, :, columns],
                out_mom_ref[low, :, columns],
                out_sec_ref[low, :, columns],
                dout_ref[2 * right + low].astype(f32) * clip,
                0.05,
                0.01,
            )
            out_new[low, :, columns] = weight
            out_mom_new[low, :, columns] = moment
            out_sec_new[low, :, columns] = second
            out_copy_new[low, :, columns] = weight.astype(bf16)

    @pl.when(pl.program_id(0) == 0)
    def _():
        inputs = in_ref.shape[0]
        weight, moment, second = adamw(
            in_ref[...], in_mom_ref[...], in_sec_ref[...], small_ref[0:inputs, :] * clip, 0.05, 0.01
        )
        in_new[...] = weight
        in_mom_new[...] = moment
        in_sec_new[...] = second
        in_copy_new[...] = weight.astype(bf16)

        norm_new[...] = norm_ref[0:1, 0:1]
        loss_new[...] = small_ref[inputs + 37 : inputs + 38, 0:1]

        def rows_of(first, last, base):
            return small_ref[inputs + base + first : inputs + base + last, :]

        for depth in range(LAYERS):
            base = 16 * depth
            for low, high, grad in (
                (0, 2, rows_of(0, 2, base)),
                (2, 4, rows_of(0, 2, base + 8)),
                (4, 7, rows_of(2, 5, base)),
                (7, 8, rows_of(2, 3, base + 8)),
                (8, 12, rows_of(4, 8, base + 8)),
            ):
                weight, moment, second = adamw(
                    vec_ref[low:high, depth],
                    vec_mom_ref[low:high, depth],
                    vec_sec_ref[low:high, depth],
                    grad * clip,
                    0.25,
                    0.0,
                )
                vec_new[low:high, depth] = weight
                vec_mom_new[low:high, depth] = moment
                vec_sec_new[low:high, depth] = second
        for low, high, grad in ((0, 1, rows_of(5, 6, 0)), (1, 5, rows_of(1, 5, 32))):
            weight, moment, second = adamw(
                outer_ref[low:high, :], outer_mom_ref[low:high, :], outer_sec_ref[low:high, :], grad * clip, 0.25, 0.0
            )
            outer_new[low:high, :] = weight
            outer_mom_new[low:high, :] = moment
            outer_sec_new[low:high, :] = second


def finish(rows, norm, every, updates, dout, small, arrays):
    steps = rows // 16
    attn, _, up, _, down, _, out, _, _, inp, _, _, vec, _, _, outer, _, _ = arrays
    codes = out.shape[2]
    part = out.shape[1] // steps
    blocks = pl.BlockSpec((GROUPS, UNITS, 16, D), lambda i: (0, 0, i, 0))
    attn_spec = pl.BlockSpec((LAYERS, 4, 16, D), lambda i: (0, 0, i, 0))
    up_spec = pl.BlockSpec((LAYERS, 16, FF), lambda i: (0, i, 0))
    out_spec = pl.BlockSpec((2, part, codes), lambda i: (0, i, 0))
    dout_spec = pl.BlockSpec((GROUPS, part, D), lambda i: (0, i, 0))
    in_spec, vec_spec, outer_spec = whole_spec(inp.shape), whole_spec(vec.shape), whole_spec(outer.shape)

    def like(array, dtype=f32):
        return jax.ShapeDtypeStruct(array.shape, dtype)

    return pl.pallas_call(
        finish_kernel,
        grid=(steps,),
        out_shape=[like(attn), like(attn), like(attn, bf16)]
        + [like(up), like(up), like(up, bf16)]
        + [like(down), like(down), like(down, bf16)]
        + [like(out)] * 3
        + [like(out, bf16)]
        + [like(inp)] * 3
        + [like(inp, bf16)]
        + [like(vec)] * 3
        + [like(outer)] * 3
        + [jax.ShapeDtypeStruct((1, 1), f32)] * 2,
        in_specs=[whole_spec((8, 128)), blocks, blocks, dout_spec, whole_spec(small.shape)]
        + [attn_spec] * 2
        + [up_spec] * 2
        + [attn_spec] * 2
        + [out_spec] * 3
        + [in_spec] * 3
        + [vec_spec] * 3
        + [outer_spec] * 3,
        out_specs=[attn_spec] * 3
        + [up_spec] * 3
        + [attn_spec] * 3
        + [out_spec] * 4
        + [in_spec] * 4
        + [vec_spec] * 3
        + [outer_spec] * 3
        + [whole_spec((1, 1))] * 2,
        compiler_params=pltpu.CompilerParams(vmem_limit_bytes=VMEM_LIMIT),
        cost_estimate=pl.CostEstimate(flops=10**8, bytes_accessed=4 * 10**7, transcendentals=0),
        name="finish",
    )(norm, every, updates, dout, small, *arrays)


def local(
    frames,
    speech_mask,
    targets,
    in_proj,
    in_moment,
    in_second,
    out_proj,
    out_moment,
    out_second,
    layer_vectors,
    vectors_moment,
    vectors_second,
    outer_vectors,
    outer_moment,
    outer_second,
    attn_proj,
    attn_momentum,
    ff_up,
    up_momentum,
    ff_down,
    down_momentum,
    in_copy,
    out_copy,
    attn_copy,
    up_copy,
    down_copy,
):
    segment = lax.axis_index("seg")
    count, dp_count = lax.axis_size("seg"), lax.axis_size("dp")
    rows = D // count
    streams = frames.shape[0]
    stream_total = streams * dp_count
    group = lax.axis_index("dp") % GROUPS
    feeds = jnp.stack(
        [
            jnp.swapaxes(up_momentum[1].reshape(rows, 4, D), 0, 1),
            jnp.swapaxes(up_momentum[0].reshape(rows, 4, D), 0, 1),
            down_momentum[0].reshape(4, rows, D),
            down_momentum[1].reshape(4, rows, D),
        ]
    )
    owned = jnp.concatenate(
        [
            lax.dynamic_index_in_dim(attn_momentum, group, 1, keepdims=False),
            lax.dynamic_index_in_dim(feeds, group, 0, keepdims=False),
        ],
        0,
    ).astype(bf16)
    momenta = lax.all_gather(owned, "seg", axis=0, tiled=False)
    frames_t = jnp.swapaxes(frames, 1, 2)
    bias = jnp.where(segment > 0, 0.0, -1e30).astype(f32)[None]
    hidden, memory, totals = embed(count, frames_t, speech_mask, in_copy, outer_vectors)
    memory = [memory] * streams
    kept = []
    for depth in range(LAYERS):
        saved, passed = None, []
        for stream in range(streams):
            saved, short = forward_layer(
                depth,
                stream,
                streams,
                bias,
                hidden,
                memory[stream],
                attn_copy,
                up_copy,
                down_copy,
                layer_vectors,
                saved,
            )
            if depth + 1 < LAYERS:
                passed.append(from_behind(short, "seg", 1))
        kept.append((hidden, saved[8], saved))
        hidden = saved[0]
        memory = passed
    grad_hidden, grad_out, head_outer = head(
        hidden, targets, speech_mask, totals, out_copy, outer_vectors, 1.0 / stream_total, momenta
    )
    vector_grads, feed_done = [], [None, None]
    carried = grad_out.reshape(GROUPS * D // 2, D)
    carried_done = []
    for depth in reversed(range(LAYERS)):
        entering, held, saved = kept[depth]
        dafter, grad_up, grad_down, feed_vec, done = feed_back(
            depth, grad_hidden, saved[7], up_copy, down_copy, layer_vectors, count, dp_count, carried
        )
        carried_done.append(done)
        grad_hidden, grad_attn, attn_vec, grad_in, feed_done[depth] = attend_back(
            depth,
            bias,
            dafter,
            entering,
            held,
            saved[1:7],
            attn_copy,
            layer_vectors,
            frames_t,
            grad_up,
            grad_down,
            count,
            dp_count,
        )
        carried = grad_attn.reshape(4 * D, D)
        vector_grads = [attn_vec, feed_vec] + vector_grads
    out_done, attn_done = carried_done
    every_out = lax.all_gather(out_done, ("dp", "seg"), axis=0, tiled=True)[: GROUPS * D // 2]
    every_out = every_out.reshape(GROUPS, D // 2, D)
    whole, own, small, squares = reduce_grads(
        count,
        dp_count,
        grad_attn,
        attn_done,
        feed_done[0],
        feed_done[1],
        out_done,
        [grad_in] + vector_grads + [head_outer],
    )
    updates, every, norm = muon(count, squares, whole, momenta, own)
    split = (LAYERS, 4, rows, D)
    halved = (2, D // 2, out_proj.shape[1])
    (
        attn_new,
        attn_mom,
        attn_copy_new,
        up_new,
        up_mom,
        up_copy_new,
        down_new,
        down_mom,
        down_copy_new,
        out_new,
        out_moment_new,
        out_second_new,
        out_copy_new,
        in_new,
        in_moment_new,
        in_second_new,
        in_copy_new,
        vectors_new,
        vectors_moment_new,
        vectors_second_new,
        outer_new,
        outer_moment_new,
        outer_second_new,
        loss_sum,
        norm,
    ) = finish(
        rows,
        norm,
        every,
        updates,
        every_out,
        small,
        [
            attn_proj,
            attn_momentum,
            ff_up,
            up_momentum,
            ff_down.reshape(split),
            down_momentum.reshape(split),
            out_proj.reshape(halved),
            out_moment.reshape(halved),
            out_second.reshape(halved),
            in_proj,
            in_moment,
            in_second,
            jnp.swapaxes(layer_vectors, 0, 1),
            jnp.swapaxes(vectors_moment, 0, 1),
            jnp.swapaxes(vectors_second, 0, 1),
            outer_vectors,
            outer_moment,
            outer_second,
        ],
    )
    return (
        loss_sum.reshape(()),
        norm.reshape(()),
        in_new,
        in_moment_new,
        in_second_new,
        out_new.reshape(out_proj.shape),
        out_moment_new.reshape(out_proj.shape),
        out_second_new.reshape(out_proj.shape),
        jnp.swapaxes(vectors_new, 0, 1),
        jnp.swapaxes(vectors_moment_new, 0, 1),
        jnp.swapaxes(vectors_second_new, 0, 1),
        outer_new,
        outer_moment_new,
        outer_second_new,
        attn_new,
        attn_mom,
        up_new,
        up_mom,
        down_new.reshape(ff_down.shape),
        down_mom.reshape(ff_down.shape),
        in_copy_new,
        out_copy_new.reshape(out_proj.shape),
        attn_copy_new,
        up_copy_new,
        down_copy_new.reshape(ff_down.shape),
    )


def solution(mesh):
    return jax.shard_map(
        local,
        mesh=mesh,
        in_specs=(
            P("dp", "seg", None),
            P("dp", "seg"),
            P("dp", "seg"),
            P(),
            P(),
            P(),
            P(),
            P(),
            P(),
            P(),
            P(),
            P(),
            P(),
            P(),
            P(),
            P(None, None, "seg", None),
            P(None, None, "seg", None),
            P(None, "seg", None),
            P(None, "seg", None),
            P(None, "seg", None),
            P(None, "seg", None),
            P(),
            P(),
            P(),
            P(),
            P(),
        ),
        out_specs=(
            P(),
            P(),
            P(),
            P(),
            P(),
            P(),
            P(),
            P(),
            P(),
            P(),
            P(),
            P(),
            P(),
            P(),
            P(None, None, "seg", None),
            P(None, None, "seg", None),
            P(None, "seg", None),
            P(None, "seg", None),
            P(None, "seg", None),
            P(None, "seg", None),
            P(),
            P(),
            P(None, None, "seg", None),
            P(None, "seg", None),
            P(None, "seg", None),
        ),
        check_vma=False,
    )
```

```python
import functools
import math

import jax
import jax.numpy as jnp
from jax import lax
from jax.experimental import pallas as pl
from jax.experimental.pallas import tpu as pltpu
from jax.sharding import PartitionSpec as P

D = 512
HEAD_DIM = 64
HEADS = D // HEAD_DIM
FF = 2048
LAYERS = 2
STEP = 10
SEG = 512
HALF = 256
PAIR = 2 * HEAD_DIM
TILE = 512
VMEM_LIMIT = 56 * 1024 * 1024
GELU_SCALE = math.sqrt(2.0 / math.pi)

f32 = jnp.float32
bf16 = jnp.bfloat16


def dot_nn(left, right):
    return lax.dot_general(left, right, (((1,), (0,)), ((), ())), preferred_element_type=f32)


def dot_nt(left, right):
    return lax.dot_general(left, right, (((1,), (1,)), ((), ())), preferred_element_type=f32)


def dot_tn(left, right):
    return lax.dot_general(left, right, (((0,), (0,)), ((), ())), preferred_element_type=f32)


def normalised(values):
    centred = values - jnp.mean(values, -1, keepdims=True)
    scale = lax.rsqrt(jnp.mean(centred * centred, -1, keepdims=True) + 1e-05)
    return centred * scale, scale


def norm_back(grad, gain, unit, scale):
    part = grad * gain
    mean_part = jnp.mean(part, -1, keepdims=True)
    mean_unit = jnp.mean(part * unit, -1, keepdims=True)
    return scale * (part - mean_part - unit * mean_unit)


def column_sum(values):
    return jnp.sum(values, 0, keepdims=True)


def head_masks():
    lane = lax.broadcasted_iota(jnp.int32, (1, PAIR), 1)
    return (lane < HEAD_DIM).astype(bf16), (lane >= HEAD_DIM).astype(bf16)


def pair_lanes(pair):
    return pl.ds(pl.multiple_of(pair * PAIR, PAIR), PAIR)


def forward_kernel(
    bias_ref,
    x_ref,
    mem_ref,
    attn_ref,
    up_ref,
    down_ref,
    vec_ref,
    *refs,
):
    hid_ref, hid16_ref, keyin_ref, q_ref, k_ref, v_ref, lse_ref, mixed_ref, after_ref, kept_ref, act_s, lse_s = refs[-12:]
    kept_ref[...] = mem_ref[...]
    x = x_ref[...]
    own_unit, _ = normalised(x)
    gain, shift = vec_ref[0:1, :], vec_ref[1:2, :]
    normed = (own_unit * gain + shift).astype(bf16)
    mem_unit, _ = normalised(mem_ref[...].astype(f32))
    mem_normed = (mem_unit * gain + shift).astype(bf16)
    keyin_ref[0:SEG, :] = mem_normed
    keyin_ref[SEG:, :] = normed
    q_ref[...] = (dot_nn(normed, attn_ref[0]) + vec_ref[4:5, :]).astype(bf16) * jnp.asarray(HEAD_DIM**-0.5, bf16)
    k_ref[0:SEG, :] = dot_nn(mem_normed, attn_ref[1]).astype(bf16)
    k_ref[SEG:, :] = dot_nn(normed, attn_ref[1]).astype(bf16)
    v_ref[0:SEG, :] = (dot_nn(mem_normed, attn_ref[2]) + vec_ref[5:6, :]).astype(bf16)
    v_ref[SEG:, :] = (dot_nn(normed, attn_ref[2]) + vec_ref[5:6, :]).astype(bf16)
    first, second = head_masks()
    memory_bias = bias_ref[0]
    lane = lax.broadcasted_iota(jnp.int32, (HALF, PAIR), 1)
    query_pos = lax.broadcasted_iota(jnp.int32, (2 * HALF, HALF), 0) % HALF
    key_pos = lax.broadcasted_iota(jnp.int32, (2 * HALF, HALF), 1)
    diagonal = key_pos <= query_pos
    lse_s[...] = jnp.zeros_like(lse_s)

    def pair_body(pair, carry):
        lanes = pair_lanes(pair)
        for block in range(2):
            rows = slice(block * HALF, (block + 1) * HALF)
            q_pair = q_ref[rows, lanes]
            q_both = jnp.concatenate([q_pair * first, q_pair * second], 0)
            spans = [(0, SEG, 0)]
            if block:
                spans.append((SEG, SEG + HALF, 1))
            spans.append((SEG + block * HALF, SEG + (block + 1) * HALF, 2))
            scores = []
            for low, high, kind in spans:
                part = dot_nt(q_both, k_ref[low:high, lanes])
                if kind == 2:
                    part = jnp.where(diagonal, part, -1e30)
                scores.append(part)
            peaks = [jnp.max(part, -1, keepdims=True) for part in scores]
            peaks[0] = peaks[0] + memory_bias
            most = functools.reduce(jnp.maximum, peaks)
            weights = [
                jnp.exp(part - (most if place else most - memory_bias)) for place, part in enumerate(scores)
            ]
            total = functools.reduce(jnp.add, [jnp.sum(part, -1, keepdims=True) for part in weights])
            mixed = functools.reduce(
                jnp.add,
                [
                    dot_nn(part.astype(bf16), v_ref[low:high, lanes])
                    for part, (low, high, kind) in zip(weights, spans)
                ],
            )
            mixed = mixed / total
            mixed_ref[rows, lanes] = jnp.where(lane < HEAD_DIM, mixed[:HALF], mixed[HALF:]).astype(bf16)
            lse = most + jnp.log(total)
            kept = jnp.where(lane == 2 * pair, lse[:HALF], lse_s[rows, :])
            lse_s[rows, :] = jnp.where(lane == 2 * pair + 1, lse[HALF:], kept)
        return carry

    lax.fori_loop(0, HEADS // 2, pair_body, 0)
    lse_ref[...] = jnp.transpose(lse_s[...])[0:HEADS, :]
    after = x + (dot_nn(mixed_ref[...], attn_ref[3]) + vec_ref[6:7, :])
    after_ref[...] = after
    unit, _ = normalised(after)
    normed_two = (unit * vec_ref[2:3, :] + vec_ref[3:4, :]).astype(bf16)
    for tile in range(FF // TILE):
        columns = slice(tile * TILE, (tile + 1) * TILE)
        inner = dot_nn(normed_two, up_ref[:, columns]) + vec_ref[8 + tile : 9 + tile, :]
        act_s[:, columns] = (
            0.5 * inner * (1.0 + jnp.tanh(GELU_SCALE * (inner + 0.044715 * inner * inner * inner)))
        ).astype(bf16)
    hidden = after + (dot_nn(act_s[...], down_ref[...]) + vec_ref[7:8, :])
    hid_ref[...] = hidden
    hid16_ref[...] = hidden.astype(bf16)


SAVED = (
    ((SEG, D), f32),
    ((2 * SEG, D), bf16),
    ((SEG, D), bf16),
    ((2 * SEG, D), bf16),
    ((2 * SEG, D), bf16),
    ((HEADS, SEG), f32),
    ((SEG, D), bf16),
    ((SEG, D), f32),
    ((SEG, D), bf16),
)


def whole_spec(shape):
    return pl.BlockSpec(shape, lambda *_: (0,) * len(shape))


def stream_spec(shape, stream=None):
    zeros = (0,) * len(shape)
    if stream is None:
        return pl.BlockSpec((None,) + shape, lambda i: (i,) + zeros)
    return pl.BlockSpec((None,) + shape, lambda i: (stream,) + zeros)


def layer_spec(shape, depth):
    zeros = (0,) * len(shape)
    return pl.BlockSpec((None,) + shape, lambda *_: (depth,) + zeros)


def forward_layer(depth, stream, streams, bias, hidden, memory, attn, upper, lower, vectors, earlier):
    saved_shapes = [jax.ShapeDtypeStruct((streams,) + shape, dtype) for shape, dtype in SAVED]
    saved_specs = [stream_spec(shape, stream) for shape, dtype in SAVED]
    out_shape = [saved_shapes[0], jax.ShapeDtypeStruct((SEG, D), bf16)] + saved_shapes[1:]
    out_specs = [saved_specs[0], whole_spec((SEG, D))] + saved_specs[1:]
    operands = [bias, hidden, memory, attn, upper, lower, vectors]
    in_specs = [
        pl.BlockSpec(memory_space=pltpu.SMEM),
        stream_spec((SEG, D), stream),
        stream_spec((SEG, D), stream) if memory.ndim == 3 else whole_spec((SEG, D)),
        layer_spec(attn.shape[1:], depth),
        layer_spec(upper.shape[1:], depth),
        layer_spec(lower.shape[1:], depth),
        layer_spec(vectors.shape[1:], depth),
    ]
    aliases = {}
    if earlier is not None:
        for place, array in enumerate(earlier):
            aliases[len(operands)] = place if place == 0 else place + 1
            operands.append(array)
            in_specs.append(pl.BlockSpec(memory_space=pl.ANY))
    out = pl.pallas_call(
        forward_kernel,
        grid=(1,),
        out_shape=out_shape,
        in_specs=in_specs,
        out_specs=out_specs,
        scratch_shapes=[pltpu.VMEM((SEG, FF), bf16), pltpu.VMEM((SEG, PAIR), f32)],
        input_output_aliases=aliases,
        compiler_params=pltpu.CompilerParams(vmem_limit_bytes=VMEM_LIMIT),
        cost_estimate=pl.CostEstimate(flops=10**10, bytes_accessed=2 * 10**7, transcendentals=10**7),
        name="layer_forward",
    )(*operands)
    return [out[0]] + list(out[2:]), out[1]


def head_kernel(scale, x_ref, target_ref, mask_ref, total_ref, out_ref, outer_ref, bias_ref, mom_ref, g_ref, dout_ref, douter_ref, acc_s):
    step = pl.program_id(0)

    @pl.when(step == 0)
    def _():
        acc_s[...] = jnp.zeros_like(acc_s)
        douter_ref[...] = jnp.zeros_like(douter_ref)

    unit, rscale = normalised(x_ref[...])
    gain = outer_ref[1:2, :]
    normed = (unit * gain + outer_ref[2:3, :]).astype(bf16)
    logits = dot_nn(normed, out_ref[...]) + bias_ref[...]
    most = jnp.max(logits, -1, keepdims=True)
    powers = jnp.exp(logits - most)
    total = jnp.sum(powers, -1, keepdims=True)
    target_row = target_ref[pl.ds(step, 1), :].astype(f32)
    weight_row = mask_ref[pl.ds(step, 1), :].astype(f32) * (1.0 / total_ref[pl.ds(step, 1), 0:1])
    columns = jnp.transpose(jnp.concatenate([target_row, weight_row, jnp.zeros((6, SEG), f32)], 0))
    target, weight = columns[:, 0:1].astype(jnp.int32), columns[:, 1:2]
    chosen = lax.broadcasted_iota(jnp.int32, logits.shape, 1) == target
    picked = jnp.sum(jnp.where(chosen, logits, 0.0), -1, keepdims=True)
    loss = jnp.sum(weight * (most + jnp.log(total) - picked), 0, keepdims=True)
    spread = weight * scale
    dlogits = (powers * (spread / total) - jnp.where(chosen, spread, 0.0)).astype(bf16)
    acc_s[...] += dot_nn(jnp.transpose(normed), dlogits)
    bias_grad = column_sum(dlogits.astype(f32))
    dnormed = dot_nt(dlogits, out_ref[...])
    g_ref[...] = norm_back(dnormed, gain, unit, rscale)
    douter_ref[1:2, :] += column_sum(dnormed * unit)
    douter_ref[2:3, :] += column_sum(dnormed)
    douter_ref[3:4, :] += bias_grad[:, :D]
    douter_ref[4:5, :] += bias_grad[:, D:]
    douter_ref[5:6, :] += jnp.broadcast_to(loss, (1, D))

    @pl.when(step == pl.num_programs(0) - 1)
    def _():
        half = D // 2
        for right in range(2):
            for low in range(2):
                dout_ref[right, low] = acc_s[
                    low * half : (low + 1) * half, right * D : (right + 1) * D
                ]


def head(hidden, targets, mask, totals, out_weight, outer_vectors, scale, momenta):
    streams = hidden.shape[0]
    codes = out_weight.shape[1]
    bias = outer_vectors[3:].reshape(1, codes)
    return pl.pallas_call(
        functools.partial(head_kernel, scale),
        grid=(streams,),
        out_shape=[
            jax.ShapeDtypeStruct((streams, SEG, D), f32),
            jax.ShapeDtypeStruct((2, 2, D // 2, D), f32),
            jax.ShapeDtypeStruct((8, D), f32),
        ],
        in_specs=[
            stream_spec((SEG, D)),
            whole_spec((streams, SEG)),
            whole_spec((streams, SEG)),
            whole_spec((8, 128)),
            whole_spec((D, codes)),
            whole_spec(outer_vectors.shape),
            whole_spec((1, codes)),
            pl.BlockSpec(memory_space=pl.ANY),
        ],
        out_specs=[stream_spec((SEG, D)), whole_spec((2, 2, D // 2, D)), whole_spec((8, D))],
        scratch_shapes=[pltpu.VMEM((D, codes), f32)],
        compiler_params=pltpu.CompilerParams(vmem_limit_bytes=VMEM_LIMIT),
        cost_estimate=pl.CostEstimate(flops=33 * 10**8, bytes_accessed=10**7, transcendentals=10**6),
        name="head",
    )(hidden, targets, mask, totals, out_weight, outer_vectors, bias, momenta)


def feed_back_kernel(streams, g_ref, after_ref, up_ref, down_ref, vec_ref, *refs):
    step = pl.program_id(0)
    grad_ref, dafter_ref, dup_ref, ddown_ref, dvec_ref, done_ref, normed_s, branch_s, act_s, inner_s = refs[:10]
    carry = AttnCarry(grad_ref, refs[10 : 10 + CARRY_REFS], refs[10 + CARRY_REFS :])
    planes = carry.planes
    later = range(1, planes)
    beats = [
        [("b", place) for place in range(planes)],
        [("m", 0)],
        [("m", place) for place in later] + [("e", 0)],
        [("e", place) for place in range(1, planes // 2)],
        [("e", place) for place in range(planes // 2, planes)],
    ]

    @pl.when(step == 0)
    def _():
        hail(carry.targets)
        carry.load_all()
        dvec_ref[...] = jnp.zeros_like(dvec_ref)

    rows = pl.ds(pl.multiple_of(step * SEG, SEG), SEG)
    grad = g_ref[...]
    branch = grad.astype(bf16)
    dvec_ref[2:3, :] += column_sum(branch.astype(f32))
    unit, scale = normalised(after_ref[...])
    gain = vec_ref[2:3, :]
    normed = (unit * gain + vec_ref[3:4, :]).astype(bf16)
    normed_s[:, rows] = jnp.transpose(normed)
    branch_s[:, rows] = jnp.transpose(branch)

    @pl.when(step == 0)
    def _():
        meet(carry.targets)
        carry.send_all()

    for tile in range(FF // TILE):
        columns = slice(tile * TILE, (tile + 1) * TILE)
        inner = dot_nn(normed, up_ref[:, columns]) + vec_ref[8 + tile : 9 + tile, :]
        dact = dot_nt(branch, down_ref[columns, :])
        square = inner * inner
        bent = jnp.tanh(inner * (GELU_SCALE + (GELU_SCALE * 0.044715) * square))
        half = 0.5 * (1.0 + bent)
        act_s[rows, columns] = (inner * half).astype(bf16)
        slope = half + inner * (half * (1.0 - bent)) * (GELU_SCALE + (GELU_SCALE * 0.134145) * square)
        dinner = (dact * slope).astype(bf16)
        inner_s[rows, columns] = dinner
        dvec_ref[4 + tile : 5 + tile, :] += column_sum(dinner.astype(f32))

    @pl.when(step == 0)
    def _():
        carry.run(beats[0])

    @pl.when(step == streams - 1)
    def _():
        carry.run(beats[2])

    dnormed = dot_nt(inner_s[rows, :], up_ref[...])
    dvec_ref[0:1, :] += column_sum(dnormed * unit)
    dvec_ref[1:2, :] += column_sum(dnormed)
    dafter_ref[...] = grad + norm_back(dnormed, gain, unit, scale)

    @pl.when(step == 0)
    def _():
        carry.run(beats[1])

    @pl.when(step == streams - 1)
    def _():
        carry.run(beats[3])
        for tile in range(FF // TILE):
            columns = slice(tile * TILE, (tile + 1) * TILE)
            dup_ref[tile] = dot_nn(normed_s[...], inner_s[:, columns]).astype(bf16)
        carry.run(beats[4])
        for tile in range(FF // TILE):
            columns = slice(tile * TILE, (tile + 1) * TILE)
            ddown_ref[columns, :] = jnp.transpose(dot_nn(branch_s[...], act_s[:, columns]).astype(bf16))
        carry.finish(done_ref)


def feed_back(depth, grad, after, upper, lower, vectors, count, dp_count, attn_grad):
    streams = grad.shape[0]
    rows = attn_grad.shape[0] // (GROUPS * count)
    in_specs = [
        stream_spec((SEG, D)),
        stream_spec((SEG, D)),
        layer_spec(upper.shape[1:], depth),
        layer_spec(lower.shape[1:], depth),
        layer_spec(vectors.shape[1:], depth),
    ]
    out_shape = [
        jax.ShapeDtypeStruct((streams, SEG, D), f32),
        jax.ShapeDtypeStruct((FF // TILE, D, TILE), bf16),
        jax.ShapeDtypeStruct((FF, D), bf16),
        jax.ShapeDtypeStruct((8, D), f32),
    ]
    out_specs = [
        stream_spec((SEG, D)),
        whole_spec((FF // TILE, D, TILE)),
        whole_spec((FF, D)),
        whole_spec((8, D)),
    ]
    scratch = [
        pltpu.VMEM((D, streams * SEG), bf16),
        pltpu.VMEM((D, streams * SEG), bf16),
        pltpu.VMEM((streams * SEG, FF), bf16),
        pltpu.VMEM((streams * SEG, FF), bf16),
    ]
    operands = [grad, after, upper, lower, vectors]
    in_specs.append(pl.BlockSpec(memory_space=pl.ANY))
    operands.append(attn_grad.reshape(2, 2, count, rows, D))
    out_shape.append(jax.ShapeDtypeStruct((rows, D), bf16))
    out_specs.append(whole_spec((rows, D)))
    scratch = scratch + carry_scratch("attn", rows, count, dp_count, attn_grad.dtype)
    params = {"collective_id": 6 + depth, "has_side_effects": True}
    return pl.pallas_call(
        functools.partial(feed_back_kernel, streams),
        grid=(streams,),
        out_shape=out_shape,
        in_specs=in_specs,
        out_specs=out_specs,
        scratch_shapes=scratch,
        compiler_params=pltpu.CompilerParams(vmem_limit_bytes=VMEM_LIMIT, **params),
        cost_estimate=pl.CostEstimate(flops=11 * 10**9, bytes_accessed=2 * 10**7, transcendentals=2 * 10**6),
        name="feed_back",
    )(*operands)


def attend_back_kernel(
    streams,
    depth,
    bias_ref,
    dafter_ref,
    x_ref,
    mem_ref,
    keyin_ref,
    q_ref,
    k_ref,
    v_ref,
    lse_ref,
    mixed_ref,
    attn_ref,
    vec_ref,
    frames_ref,
    dup_ref,
    ddown_ref,
    dx_ref,
    dattn_ref,
    dvec_ref,
    din_ref,
    done_ref,
    attn_s,
    dmixed_s,
    dq_s,
    dk_s,
    dv_s,
    ds_s,
    delta_s,
    *refs,
):
    step = pl.program_id(0)
    pairs = HEADS // 2
    carry = FeedCarry(depth, dup_ref, ddown_ref, refs[:CARRY_REFS], refs[CARRY_REFS:])

    @pl.when(step == 0)
    def _():
        hail(carry.targets)
        carry.load_all()
        attn_s[...] = jnp.zeros_like(attn_s)
        dvec_ref[...] = jnp.zeros_like(dvec_ref)
        din_ref[...] = jnp.zeros_like(din_ref)

    dafter = dafter_ref[...]
    branch = dafter.astype(bf16)
    dvec_ref[4:5, :] += column_sum(branch.astype(f32))
    dmixed = dot_nt(branch, attn_ref[3]).astype(bf16)
    dmixed_s[...] = dmixed
    attn_s[3] += dot_nn(jnp.transpose(mixed_ref[...]), branch)
    product = dmixed.astype(f32) * mixed_ref[...].astype(f32)
    high = product.astype(bf16)
    rest = (product - high.astype(f32)).astype(bf16)
    owner = lax.broadcasted_iota(jnp.int32, (HEADS, D), 1) // HEAD_DIM
    pick = (owner == lax.broadcasted_iota(jnp.int32, (HEADS, D), 0)).astype(bf16)
    delta_s[...] = dot_nt(pick, high) + dot_nt(pick, rest)
    first, second = head_masks()
    memory_bias = bias_ref[0]
    key_pos = lax.broadcasted_iota(jnp.int32, (HALF, 2 * HALF), 0)
    query_pos = lax.broadcasted_iota(jnp.int32, (HALF, 2 * HALF), 1) % HALF
    diagonal = key_pos <= query_pos
    head_row = lax.broadcasted_iota(jnp.int32, (PAIR, HALF), 0)

    @pl.when(step == 0)
    def _():
        meet(carry.targets)
        carry.send_all()

    def pair_body(pair, state):
        lanes = pair_lanes(pair)
        q_pair, do_pair = q_ref[:, lanes], dmixed_s[:, lanes]

        def spread(value):
            return jnp.concatenate(
                [value[:HALF] * first, value[:HALF] * second, value[HALF:] * first, value[HALF:] * second], 0
            )

        q_all, do_all = spread(q_pair), spread(do_pair)

        def rows_of(ref):
            one, two = ref[pl.ds(2 * pair, 1), :], ref[pl.ds(2 * pair + 1, 1), :]
            return jnp.concatenate([one[:, :HALF], two[:, :HALF], one[:, HALF:], two[:, HALF:]], 1)

        lse_all, delta_all = rows_of(lse_ref), rows_of(delta_s)
        for block in range(4):
            keys = slice(block * HALF, (block + 1) * HALF)
            start = 2 * HALF if block == 3 else 0
            scores = dot_nt(k_ref[keys, lanes], q_all[start:])
            shift = lse_all - memory_bias if block < 2 else lse_all[:, start:]
            weights = jnp.exp(scores - shift)
            if block == 2:
                weights = jnp.concatenate(
                    [jnp.where(diagonal, weights[:, : 2 * HALF], 0.0), weights[:, 2 * HALF :]], 1
                )
            if block == 3:
                weights = jnp.where(diagonal, weights, 0.0)
            dweights = dot_nt(v_ref[keys, lanes], do_all[start:])
            dscores = (weights * (dweights - delta_all[:, start:])).astype(bf16)
            dv_s[keys, lanes] = dot_nn(weights.astype(bf16), do_all[start:]).astype(bf16)
            dk_s[keys, lanes] = dot_nn(dscores, q_all[start:]).astype(bf16)
            ds_s[keys, start:] = dscores
        k_t = jnp.transpose(k_ref[:, lanes])
        for block in range(2):
            seen = SEG + (block + 1) * HALF
            grads = dot_nn(k_t[:, :seen], ds_s[:seen, block * 2 * HALF : (block + 1) * 2 * HALF])
            grads = jnp.where(head_row < HEAD_DIM, grads[:, :HALF], grads[:, HALF:])
            dq_s[block * HALF : (block + 1) * HALF, lanes] = (
                jnp.transpose(grads) * (HEAD_DIM**-0.5)
            ).astype(bf16)
        carry.tick(pairs * step + pair, pairs * streams, 1)
        return state

    lax.fori_loop(0, pairs, pair_body, 0)
    dq, dk, dv = dq_s[...], dk_s[...], dv_s[...]
    keyin_t = jnp.transpose(keyin_ref[...])
    attn_s[0] += dot_nn(keyin_t[:, SEG:], dq)
    attn_s[1] += dot_nn(keyin_t, dk)
    attn_s[2] += dot_nn(keyin_t, dv)
    dvec_ref[2:3, :] += column_sum(dq.astype(f32))
    dvec_ref[3:4, :] += column_sum(dv.astype(f32))
    dkeyin = dot_nt(dk, attn_ref[1]) + dot_nt(dv, attn_ref[2])
    dmem = dkeyin[:SEG]
    down = dkeyin[SEG:] + dot_nt(dq, attn_ref[0])
    gain = vec_ref[0:1, :]
    unit, scale = normalised(x_ref[...])
    mem_unit, _ = normalised(mem_ref[...].astype(f32))
    dvec_ref[0:1, :] += column_sum(down * unit + dmem * mem_unit)
    dvec_ref[1:2, :] += column_sum(down + dmem)
    dx = dafter + norm_back(down, gain, unit, scale)
    dx_ref[...] = dx
    if depth == 0:
        dx_high = dx.astype(bf16)
        dx_rest = (dx - dx_high.astype(f32)).astype(bf16)
        din_ref[...] += dot_nn(frames_ref[...], dx_high) + dot_nn(frames_ref[...], dx_rest)
        dvec_ref[5:6, :] += column_sum(dx)

    @pl.when(step == pl.num_programs(0) - 1)
    def _():
        dattn_ref[...] = attn_s[...].astype(bf16)
        carry.rest(pairs * streams, 1)
        carry.finish(done_ref)


def attend_back(depth, bias, dafter, x, memory, saved, attn, vectors, frames, up_grad, down_grad, count, dp_count):
    streams = dafter.shape[0]
    keyin, q, k, v, lse, mixed = saved
    inputs = frames.shape[1]
    rows = D // count
    up_grad, down_grad = up_grad.reshape(4, count, rows, D), down_grad.reshape(count, 4, rows, D)
    return pl.pallas_call(
        functools.partial(attend_back_kernel, streams, depth),
        grid=(streams,),
        out_shape=[
            jax.ShapeDtypeStruct((streams, SEG, D), f32),
            jax.ShapeDtypeStruct((4, D, D), bf16),
            jax.ShapeDtypeStruct((8, D), f32),
            jax.ShapeDtypeStruct((inputs, D), f32),
            jax.ShapeDtypeStruct((4, rows, D), bf16),
        ],
        in_specs=[
            pl.BlockSpec(memory_space=pltpu.SMEM),
            stream_spec((SEG, D)),
            stream_spec((SEG, D)),
            stream_spec((SEG, D)),
            stream_spec((2 * SEG, D)),
            stream_spec((SEG, D)),
            stream_spec((2 * SEG, D)),
            stream_spec((2 * SEG, D)),
            stream_spec((HEADS, SEG)),
            stream_spec((SEG, D)),
            layer_spec(attn.shape[1:], depth),
            layer_spec(vectors.shape[1:], depth),
            stream_spec((inputs, SEG)),
            pl.BlockSpec(memory_space=pl.ANY),
            pl.BlockSpec(memory_space=pl.ANY),
        ],
        out_specs=[
            stream_spec((SEG, D)),
            whole_spec((4, D, D)),
            whole_spec((8, D)),
            whole_spec((inputs, D)),
            whole_spec((4, rows, D)),
        ],
        scratch_shapes=[
            pltpu.VMEM((4, D, D), f32),
            pltpu.VMEM((SEG, D), bf16),
            pltpu.VMEM((SEG, D), bf16),
            pltpu.VMEM((2 * SEG, D), bf16),
            pltpu.VMEM((2 * SEG, D), bf16),
            pltpu.VMEM((2 * SEG, 2 * SEG), bf16),
            pltpu.VMEM((HEADS, SEG), f32),
        ]
        + carry_scratch("feed", rows, count, dp_count),
        compiler_params=pltpu.CompilerParams(
            collective_id=4 + depth, has_side_effects=True, vmem_limit_bytes=VMEM_LIMIT
        ),
        cost_estimate=pl.CostEstimate(flops=3 * 10**10, bytes_accessed=2 * 10**7, transcendentals=10**7),
        name="attend_back",
    )(bias, dafter, x, memory, keyin, q, k, v, lse, mixed, attn, vectors, frames, up_grad, down_grad)


def from_behind(value, axis, steps):
    count = lax.axis_size(axis)
    leading, last = (max(0, -steps), min(count, count - steps))
    return lax.ppermute(value, axis, [(source, source + steps) for source in range(leading, last)])


def adamw(weight, moment, second, grad, rate, decay):
    moment = 0.5 * moment + 0.5 * grad
    second = 0.99 * second + 0.01 * grad * grad
    fixed_moment = moment / (1.0 - 0.5**STEP)
    fixed_second = second / (1.0 - 0.99**STEP)
    weight = weight * (1.0 - rate * decay) - rate * fixed_moment / (jnp.sqrt(fixed_second) + 1e-08)
    return (weight, moment, second)


GROUPS = 4
UNITS = 6
SMALL = 128


def peers():
    count = {"seg": lax.axis_size("seg"), "dp": lax.axis_size("dp")}
    seg, dp = lax.axis_index("seg"), lax.axis_index("dp")
    core, x, y = seg % 2, dp % 2, (dp // 2) % 2
    across_core = {"seg": seg + 1 - 2 * core}
    across_x = {"dp": dp + 1 - 2 * x}
    across_y = {"dp": dp + 2 - 4 * y}
    across_both = {"dp": dp + 3 - 2 * x - 4 * y}
    far = []
    step = GROUPS
    while step < count["dp"]:
        far.append({"dp": dp + step - 2 * step * ((dp // step) % 2)})
        step *= 2
    return seg, dp, core, x, y, across_core, (across_x, across_y, across_both), far


def others(seg, count):
    return [lax.rem(seg + step, count) for step in range(1, count)]


def hail(targets):
    barrier = pltpu.get_barrier_semaphore()
    for target in targets:
        pl.semaphore_signal(barrier, inc=1, device_id=target, device_id_type=pl.DeviceIdType.MESH)


def meet(targets):
    pl.semaphore_wait(pltpu.get_barrier_semaphore(), len(targets))


def greet(seg, count, near, far):
    targets = [{"seg": other} for other in others(seg, count)] + list(near) + list(far)
    hail(targets)
    meet(targets)


def remote(source, target, send, recv, device):
    return pltpu.make_async_remote_copy(
        src_ref=source,
        dst_ref=target,
        send_sem=send,
        recv_sem=recv,
        device_id=device,
        device_id_type=pl.DeviceIdType.MESH,
    )


def wait_bytes(ref, sem):
    pltpu.make_async_copy(ref, ref, sem).wait()


def plus(left, right):
    return (left.astype(f32) + right.astype(f32)).astype(left.dtype)


def owners(count):
    attn, feed = count // 4 - 1, count // 4
    return (
        (0, 1, 2 * attn, 0),
        (1, 1, 2 * attn + 1, 0),
        (2, 2, 2 * feed, 0),
        (4, 2, 2 * feed + 1, 2),
    )


def lowest_bit(mask, planes):
    bit = 1
    while bit < planes and not mask & bit:
        bit *= 2
    return bit


class Carry:
    def __init__(self, refs, sems):
        self.mine, self.got0, self.got1, self.got2, self.got3, self.goth = refs
        (
            self.load,
            self.send0,
            self.recv0,
            self.send1,
            self.recv1,
            self.send2,
            self.recv2,
            self.send3,
            self.recv3,
            self.sendh,
            self.recvh,
        ) = sems
        self.seg, self.dp, self.core, self.x, self.y, self.across_core, near, self.far = peers()
        self.across_x, self.across_y, _ = near
        self.planes = self.mine.shape[0]
        self.plane = self.seg // 2
        self.targets = [self.across_core, self.across_x, self.across_y] + self.far
        bit = 1
        while bit < self.planes:
            self.targets.append({"seg": 2 * self.toggled(bit) + self.core})
            bit *= 2

        self.order = list(reversed(range(self.planes)))

    def toggled(self, mask):
        place, bit = self.plane, 1
        while bit <= mask:
            if mask & bit:
                place = place + bit - 2 * bit * ((self.plane // bit) % 2)
            bit *= 2
        return place

    def load_all(self):
        for step in range(self.planes):
            for source, place in self.pieces(2 * self.toggled(self.order[step]) + self.core):
                pltpu.make_async_copy(source, self.mine.at[(step,) + place], self.load.at[step]).start()

    def send_all(self):
        for step in range(self.planes):
            for source, place in self.pieces(2 * self.toggled(self.order[step]) + 1 - self.core):
                remote(
                    source, self.got0.at[(step,) + place], self.send0.at[step], self.recv0.at[step], self.across_core
                ).start()

    def begin(self, step):
        wait_bytes(self.mine.at[step], self.load.at[step])
        wait_bytes(self.got0.at[step], self.recv0.at[step])
        for place in range(2):
            self.mine[step, place] = plus(self.mine[step, place], self.got0[step, place])
        for copy in self.first(step):
            copy.start()

    def across(self, place, step):
        return remote(
            self.held(step),
            self.goth.at[place, step],
            self.sendh.at[place, step],
            self.recvh.at[place, step],
            self.far[place],
        )

    def third(self, step):
        mask = self.order[step]
        return remote(
            self.held(step),
            self.got3.at[mask],
            self.send3.at[step],
            self.recv3.at[mask],
            {"seg": 2 * self.toggled(lowest_bit(mask, self.planes)) + self.core},
        )

    def onward(self, step):
        held = self.held(step)
        for place in range(len(self.far)):
            copy = self.across(place, step)
            copy.start()
            copy.wait()
            held[...] = plus(held[...], self.goth[place, step])
        mask = self.order[step]
        if mask:
            self.gathered(mask, held)
            self.third(step).start()

    def gathered(self, mask, held):
        value, bit = held[...].astype(f32), 1
        while bit < lowest_bit(mask, self.planes):
            wait_bytes(self.got3.at[mask + bit], self.recv3.at[mask + bit])
            value = value + self.got3[mask + bit].astype(f32)
            bit *= 2
        held[...] = value.astype(held.dtype)

    def total(self):
        held = self.held(self.planes - 1)
        self.gathered(0, held)
        return held[...]

    def run(self, acts):
        for kind, step in acts:
            if step < self.planes:
                {"b": self.begin, "m": self.middle, "e": self.end}[kind](step)

    def actions(self, time, slack):
        planes = self.planes
        started = range(2) if time == 0 else range(time + 1, time + 2)
        for step in started:
            if step < planes:
                self.begin(step)
        if 0 <= time - slack < planes:
            self.middle(time - slack)
        if 0 <= time - slack - 2 < planes:
            self.end(time - slack - 2)

    def tick(self, time, last, slack):
        for place in range(last):

            @pl.when(time == place)
            def _():
                self.actions(place, slack)

    def rest(self, first, slack):
        for time in range(first, self.planes + slack + 2):
            self.actions(time, slack)


class AttnCarry(Carry):
    def __init__(self, source, refs, sems):
        super().__init__(refs, sems)
        self.source = source

    def pieces(self, row):
        return ((self.source.at[:, :, row], ()),)

    def held(self, step):
        return self.mine.at[step, self.y, self.x]

    def first(self, step):
        half = self.mine.shape[3] // 2
        return (
            remote(
                self.mine.at[step, :, 1 - self.x, 0:half],
                self.got1.at[step, 0],
                self.send1.at[step, 0],
                self.recv1.at[step, 0],
                self.across_x,
            ),
            remote(
                self.mine.at[step, 1 - self.y, :, half:],
                self.got1.at[step, 1],
                self.send1.at[step, 1],
                self.recv1.at[step, 1],
                self.across_y,
            ),
        )

    def second(self, step):
        half = self.mine.shape[3] // 2
        return (
            remote(
                self.mine.at[step, 1 - self.y, self.x, 0:half],
                self.got2.at[step, 0],
                self.send2.at[step, 0],
                self.recv2.at[step, 0],
                self.across_y,
            ),
            remote(
                self.mine.at[step, self.y, 1 - self.x, half:],
                self.got2.at[step, 1],
                self.send2.at[step, 1],
                self.recv2.at[step, 1],
                self.across_x,
            ),
        )

    def middle(self, step):
        mine, half = self.mine, self.mine.shape[3] // 2
        for copy in self.first(step):
            copy.wait_recv()
        for place in range(2):
            mine[step, place, self.x, 0:half] = plus(mine[step, place, self.x, 0:half], self.got1[step, 0, place])
            mine[step, self.y, place, half:] = plus(mine[step, self.y, place, half:], self.got1[step, 1, place])
        for copy in self.second(step):
            copy.start()

    def end(self, step):
        mine, half = self.mine, self.mine.shape[3] // 2
        for copy in self.second(step):
            copy.wait_recv()
        mine[step, self.y, self.x, 0:half] = plus(mine[step, self.y, self.x, 0:half], self.got2[step, 0])
        mine[step, self.y, self.x, half:] = plus(mine[step, self.y, self.x, half:], self.got2[step, 1])
        self.onward(step)

    def finish(self, out_ref):
        out_ref[...] = self.total().astype(out_ref.dtype)
        self.drain()

    def drain(self):
        for step in range(self.planes):
            wait_bytes(self.mine.at[step], self.send0.at[step])
            for copy in self.first(step) + self.second(step):
                copy.wait_send()
            if step < self.planes - 1:
                self.third(step).wait_send()


class FeedCarry(Carry):
    def __init__(self, depth, up, down, refs, sems):
        super().__init__(refs, sems)
        self.up, self.down = up, down
        self.owner = (self.x == self.y) if depth == 1 else (self.x != self.y)
        self.keep = self.x if depth == 1 else 1 - self.x

    def pieces(self, row):
        return ((self.up.at[:, row], (0,)), (self.down.at[row], (1,)))

    def held(self, step):
        return self.mine.at[step, self.y]

    def first(self, step):
        return (
            remote(
                self.mine.at[step, 1 - self.keep, 0:2],
                self.got1.at[step, 0],
                self.send1.at[step, 0],
                self.recv1.at[step, 0],
                self.across_x,
            ),
            remote(
                self.mine.at[step, 1 - self.y, 2:4],
                self.got1.at[step, 1],
                self.send1.at[step, 1],
                self.recv1.at[step, 1],
                self.across_y,
            ),
        )

    def second(self, step):
        return (
            remote(
                self.mine.at[step, self.keep, 0:2],
                self.got2.at[step, 0],
                self.send2.at[step, 0],
                self.recv2.at[step, 0],
                self.across_y,
            ),
            remote(
                self.mine.at[step, self.y, 2:4],
                self.got2.at[step, 1],
                self.send2.at[step, 1],
                self.recv2.at[step, 1],
                self.across_x,
            ),
        )

    def middle(self, step):
        for copy in self.first(step):
            copy.wait_recv()
        self.mine[step, self.keep, 0:2] = plus(self.mine[step, self.keep, 0:2], self.got1[step, 0])
        self.mine[step, self.y, 2:4] = plus(self.mine[step, self.y, 2:4], self.got1[step, 1])

        @pl.when(jnp.logical_not(self.owner))
        def _():
            for copy in self.second(step):
                copy.start()

    def end(self, step):
        @pl.when(self.owner)
        def _():
            for place in range(2):
                wait_bytes(self.got2.at[step, place], self.recv2.at[step, place])
                span = slice(2 * place, 2 * place + 2)
                self.mine[step, self.y, span] = plus(self.mine[step, self.y, span], self.got2[step, place])
            self.onward(step)

    def finish(self, out_ref):
        @pl.when(self.owner)
        def _():
            out_ref[...] = self.total().astype(out_ref.dtype)
            for step in range(self.planes - 1):
                self.third(step).wait_send()

        @pl.when(jnp.logical_not(self.owner))
        def _():
            out_ref[...] = jnp.zeros_like(out_ref)
            for step in range(self.planes):
                for copy in self.second(step):
                    copy.wait_send()

        for step in range(self.planes):
            wait_bytes(self.mine.at[step], self.send0.at[step])
            for copy in self.first(step):
                copy.wait_send()


CARRY_REFS = 6
CARRY_SEMS = 11


def carry_scratch(kind, rows, count, dp_count, dtype=bf16):
    planes = count // 2
    far = max(1, dp_count.bit_length() - 3)
    dma = pltpu.SemaphoreType.DMA
    half = rows // 2
    if kind == "attn":
        shapes = (
            (planes, 2, 2, rows),
            (planes, 2, 2, rows),
            (planes, 2, 2, half),
            (planes, 2, half),
            (planes, rows),
            (far, planes, rows),
        )
    else:
        shapes = (
            (planes, 2, 4, rows),
            (planes, 2, 4, rows),
            (planes, 2, 2, rows),
            (planes, 2, 2, rows),
            (planes, 4, rows),
            (far, planes, 4, rows),
        )
    pair = (planes, 2)
    one = (planes,)
    sems = (one, one, one, pair, pair, pair, pair, one, one, (far, planes), (far, planes))
    return [pltpu.VMEM(shape + (D,), dtype) for shape in shapes] + [dma(shape) for shape in sems]


def reduce_kernel(
    count,
    attn_grad_ref,
    attn_done_ref,
    feed_low_ref,
    feed_high_ref,
    dout_ref,
    din_ref,
    vec0_ref,
    vec1_ref,
    vec2_ref,
    vec3_ref,
    outer_ref,
    whole_ref,
    own_ref,
    small_out,
    square_out,
    small_ref,
    small_core,
    small_s,
    small_got,
    sq_seg,
    sq_dp,
    small_send,
    small_recv,
    whole_send,
    whole_recv,
    half_sem,
    sq_send,
    sq_recv,
    sqd_send,
    sqd_recv,
    *refs,
):
    carry = AttnCarry(attn_grad_ref, refs[:CARRY_REFS], refs[CARRY_REFS:])
    seg, dp, core, x, y, across_core, near, far = peers()
    across_x, across_y, across_both = near
    planes = count // 2
    plane = seg // 2
    group = 2 * y + x
    targets = [{"seg": other} for other in others(seg, count)] + list(near) + list(far)
    hail(targets)
    carry.load_all()
    own_ref[1] = attn_done_ref[...]

    @pl.when(x == y)
    def _():
        own_ref[2:6] = feed_high_ref[...]

    @pl.when(x != y)
    def _():
        own_ref[2:6] = feed_low_ref[...]

    inputs = din_ref.shape[0]
    small_ref[0:inputs, :] = din_ref[...]
    for place, ref in enumerate((vec0_ref, vec1_ref, vec2_ref, vec3_ref, outer_ref)):
        small_ref[inputs + 8 * place : inputs + 8 * place + 8, :] = ref[...]
    small_ref[inputs + 40 :, :] = jnp.zeros((SMALL - inputs - 40, D), f32)
    meet(targets)
    def small_steps():
        copy = remote(small_ref, small_core, small_send.at[0], small_recv.at[0], across_core)
        copy.start()
        yield
        copy.wait()
        small_s[...] = small_ref[...] + small_core[...]
        half = pl.ds(pl.multiple_of(core * (SMALL // 2), 8), SMALL // 2)
        targets = [across_x, across_y] + far
        step = 1
        while step < planes:
            targets.append({"seg": seg + 2 * step - 4 * step * ((plane // step) % 2)})
            step *= 2
        for place, target in enumerate(targets):
            copy = remote(
                small_s.at[half],
                small_got.at[place],
                small_send.at[place + 1],
                small_recv.at[place + 1],
                target,
            )
            copy.start()
            yield
            copy.wait()
            small_s[half, :] += small_got[place]
        small_out[half, :] = small_s[half, :]
        last = len(targets) + 1
        copy = remote(small_out.at[half], small_out.at[half], small_send.at[last], small_recv.at[last], across_core)
        copy.start()
        yield
        copy.wait()

    small_run = small_steps()
    next(small_run)
    carry.send_all()
    roles = owners(count)

    def gift(place):
        first, width, owner, spot = roles[place]
        return remote(
            own_ref.at[first : first + width],
            whole_ref.at[seg, spot : spot + width],
            whole_send.at[place],
            whole_recv.at[seg],
            {"seg": owner},
        )

    def give(place):
        first, width, owner, spot = roles[place]

        @pl.when(seg != owner)
        def _():
            gift(place).start()

        @pl.when(seg == owner)
        def _():
            whole_ref[seg, spot : spot + width] = own_ref[first : first + width]

    for place in (2, 3, 1):
        give(place)
    acts = [
        [("b", 0), ("b", 1)],
        [("b", step) for step in range(2, planes)],
        [("m", 0), ("m", 1)],
        [("m", step) for step in range(2, planes)] + [("e", 0)],
    ] + [[("e", step)] for step in range(1, planes)]
    next(small_run)
    for part in acts:
        carry.run(part)
        next(small_run, None)
    own_ref[0] = carry.total()
    give(0)
    for _ in small_run:
        pass
    shard = dout_ref[...].astype(f32)
    square = jnp.sum(jnp.sum(shard * shard, 0, keepdims=True), 1, keepdims=True)
    for unit in range(UNITS):
        value = own_ref[unit].astype(f32)
        square = square + jnp.sum(jnp.sum(value * value, 0, keepdims=True), 1, keepdims=True)
    sq_seg[seg] = jnp.broadcast_to(square, (8, 128))
    for step, other in enumerate(others(seg, count)):
        remote(sq_seg.at[seg], sq_seg.at[seg], sq_send.at[step], sq_recv.at[seg], {"seg": other}).start()

    def halves_copy(spot):
        span = slice(spot, spot + 2)
        return remote(whole_ref.at[:, span], whole_ref.at[:, span], half_sem.at[0], half_sem.at[1], across_core)

    for place, (first, width, owner, spot) in enumerate(roles):
        if width == 2:

            @pl.when(seg == owner)
            def _():
                for other in others(seg, count):
                    wait_bytes(whole_ref.at[other, spot : spot + width], whole_recv.at[other])
                halves_copy(spot).start()

    for other in others(seg, count):
        wait_bytes(sq_seg.at[other], sq_recv.at[other])
    sq_dp[group] = jnp.sum(sq_seg[...], 0)
    for place, target in enumerate(near):
        remote(sq_dp.at[group], sq_dp.at[group], sqd_send.at[place], sqd_recv.at[place], target).start()
    sums = small_out[...]
    is_loss = lax.broadcasted_iota(jnp.int32, (SMALL, D), 0) == inputs + 37
    sums = jnp.where(is_loss, 0.0, sums)
    small_square = jnp.sum(jnp.sum(sums * sums, 0, keepdims=True), 1, keepdims=True)
    for place, target in enumerate(near):
        remote(sq_dp.at[group], sq_dp.at[group], sqd_send.at[place], sqd_recv.at[place], target).wait()
    square_out[...] = jnp.sum(sq_dp[...], 0) + jnp.broadcast_to(small_square, (8, 128))

    for place, (first, width, owner, spot) in enumerate(roles):

        @pl.when(seg == owner)
        def _():
            if width == 2:
                halves_copy(spot).wait()
            else:
                for other in others(seg, count):
                    wait_bytes(whole_ref.at[other, spot : spot + width], whole_recv.at[other])

    carry.drain()
    for place, (first, width, owner, spot) in enumerate(roles):

        @pl.when(seg != owner)
        def _():
            gift(place).wait_send()

    for step in range(count - 1):
        wait_bytes(sq_seg.at[0], sq_send.at[step])


def reduce_grads(count, dp_count, attn, done, feed_low, feed_high, dout, pieces):
    rows = D // count
    planes = count // 2
    stages = 2 + planes.bit_length() + max(0, dp_count.bit_length() - 3)
    dma = pltpu.SemaphoreType.DMA
    vmem = pl.BlockSpec(memory_space=pltpu.VMEM)
    return pl.pallas_call(
        functools.partial(reduce_kernel, count),
        out_shape=[
            jax.ShapeDtypeStruct((count, 4, rows, D), bf16),
            jax.ShapeDtypeStruct((UNITS, rows, D), bf16),
            jax.ShapeDtypeStruct((SMALL, D), f32),
            jax.ShapeDtypeStruct((8, 128), f32),
        ],
        in_specs=[pl.BlockSpec(memory_space=pl.ANY)] + [vmem] * 10,
        out_specs=[vmem] * 4,
        scratch_shapes=[
            pltpu.VMEM((SMALL, D), f32),
            pltpu.VMEM((SMALL, D), f32),
            pltpu.VMEM((SMALL, D), f32),
            pltpu.VMEM((stages, SMALL // 2, D), f32),
            pltpu.VMEM((count, 8, 128), f32),
            pltpu.VMEM((GROUPS, 8, 128), f32),
            dma((stages + 2,)),
            dma((stages + 2,)),
            dma((4,)),
            dma((count,)),
            dma((2,)),
            dma((count,)),
            dma((count,)),
            dma((3,)),
            dma((3,)),
        ]
        + carry_scratch("attn", rows, count, dp_count),
        compiler_params=pltpu.CompilerParams(
            collective_id=1, has_side_effects=True, vmem_limit_bytes=VMEM_LIMIT
        ),
        cost_estimate=pl.CostEstimate(flops=10**8, bytes_accessed=10**8, transcendentals=0),
        name="reduce_grads",
    )(attn.reshape(2, 2, count, rows, D), done, feed_low, feed_high, dout, *pieces)


def halves(value):
    high = value.astype(bf16)
    return high, (value - high.astype(f32)).astype(bf16)


def times(left, right):
    (left_high, left_low), (right_high, right_low) = left, right
    return dot_nn(
        jnp.concatenate([left_high, left_high, left_low], 1),
        jnp.concatenate([right_high, right_low, right_high], 0),
    )


def times_t(left, right):
    (left_high, left_low), (right_high, right_low) = left, right
    return dot_nt(
        jnp.concatenate([left_high, left_high, left_low], 1),
        jnp.concatenate([right_high, right_low, right_high], 1),
    )


def clip_of(norm):
    return jnp.minimum(1.0, 0.25 / (norm + 1e-06))


def muon_kernel(
    count,
    square_ref,
    whole_ref,
    mom_ref,
    own_ref,
    update_ref,
    every_ref,
    norm_ref,
    made_ref,
    x_s,
    q_s,
    gram_s,
    high_s,
    low_s,
    send,
    recv,
    on_send,
    on_recv,
    own_send,
    own_recv,
):
    seg, dp, core, x, y, across_core, near, far = peers()
    group = 2 * y + x
    plane = seg // 2
    targets = [{"seg": other} for other in others(seg, count)] + list(near)
    hail(targets)
    is_down = group >= 2
    norm = jnp.sqrt(square_ref[0:1, 0:1])
    norm_ref[...] = jnp.broadcast_to(norm, norm_ref.shape)
    clip = clip_of(norm)
    eye = (
        lax.broadcasted_iota(jnp.int32, (D, D), 0) == lax.broadcasted_iota(jnp.int32, (D, D), 1)
    ).astype(f32)
    rows = whole_ref.shape[2]
    makers = [attn for _, _, attn, _ in owners(count)]
    units = [makers[0], makers[1], makers[2], makers[2], makers[3], makers[3]]

    def own_rows(side):
        return remote(own_ref, every_ref.at[group], own_send.at[side], own_recv.at[side], near[side])

    def gift(unit, slot, other):
        return remote(
            made_ref.at[other, slot],
            update_ref.at[group, unit],
            send.at[slot, other],
            recv.at[unit],
            {"seg": other},
        )

    def give(unit, slot):
        for other in others(seg, count):
            gift(unit, slot, other).start()
        update_ref[group, unit] = made_ref[seg, slot]

    def onward(unit, side):
        block = update_ref.at[group, unit]
        return remote(block, block, on_send.at[side, unit], on_recv.at[side, unit], near[side])

    meet(targets)
    for side in range(3):
        own_rows(side).start()
    every_ref[group] = own_ref[...]

    @pl.when(plane == count // 4 - 1)
    def _():
        start = (0.5 * mom_ref[:, core].astype(f32)).reshape(D, D)
        start = start + clip * whole_ref[:, 0].astype(f32).reshape(D, D)
        size = jnp.sum(jnp.sum(start * start, 0, keepdims=True), 1, keepdims=True)
        x_s[...] = start / (jnp.sqrt(size) + 1e-07)

        def sweep(_, carry):
            value = x_s[...]
            both = halves(value)
            gram = times_t(both, both)
            gram_both = halves(gram)
            poly = -4.775 * gram + 2.0315 * times(gram_both, gram_both)
            x_s[...] = 3.4445 * value + times(halves(poly), both)
            return carry

        lax.fori_loop(0, 5, sweep, 0)
        made_ref[:, 0] = x_s[...].astype(bf16).reshape(count, rows, D)
        for unit in range(2):

            @pl.when(core == unit)
            def _():
                give(unit, 0)

    @pl.when(plane == count // 4)
    def _():
        gram_s[...] = jnp.zeros_like(gram_s)

        def gather(tile, size):
            value = (0.5 * mom_ref[:, 2 + tile].astype(f32)).reshape(D, D)
            value = value + clip * whole_ref[:, tile].astype(f32).reshape(D, D)
            high, low = halves(value)
            high_s[tile] = high
            low_s[tile] = low

            @pl.when(is_down)
            def _():
                high_s[tile] = jnp.transpose(high_s[tile])
                low_s[tile] = jnp.transpose(low_s[tile])

            both = high_s[tile], low_s[tile]
            gram_s[...] += times_t(both, both)
            return size + jnp.sum(jnp.sum(value * value, 0, keepdims=True), 1, keepdims=True)

        size = lax.fori_loop(0, 4, gather, jnp.zeros((1, 1), f32))
        scale = 1.0 / (jnp.sqrt(size) + 1e-07)
        gram_s[...] = gram_s[...] * (scale * scale)

        def poly_of(gram, gram_both):
            return 3.4445 * eye - 4.775 * gram + 2.0315 * times(gram_both, gram_both)

        def advance(gram_both, poly_both):
            gram_s[...] = times(halves(times(gram_both, poly_both)), poly_both)

        gram = gram_s[...]
        gram_both = halves(gram)
        poly = poly_of(gram, gram_both)
        q_s[...] = poly
        advance(gram_both, halves(poly))

        def sweep(_, carry):
            gram = gram_s[...]
            gram_both = halves(gram)
            poly_both = halves(poly_of(gram, gram_both))
            q_s[...] = times(halves(q_s[...]), poly_both)
            advance(gram_both, poly_both)
            return carry

        lax.fori_loop(0, 3, sweep, 0)
        gram = gram_s[...]
        last = times(halves(q_s[...]), halves(poly_of(gram, halves(gram)))) * scale
        last_both = halves(last)
        for slot in range(2):
            tile = 2 * core + slot
            x_s[...] = times(last_both, (high_s[tile], low_s[tile]))

            @pl.when(is_down)
            def _():
                x_s[...] = jnp.transpose(x_s[...])

            made_ref[:, slot] = x_s[...].astype(bf16).reshape(count, rows, D)
            for half in range(2):

                @pl.when(core == half)
                def _():
                    give(2 + 2 * half + slot, slot)

    for unit in (0, 1, 2, 4, 3, 5):

        @pl.when(seg != units[unit])
        def _():
            wait_bytes(update_ref.at[group, unit], recv.at[unit])

        for side in range(3):
            onward(unit, side).start()
    for side in range(3):
        own_rows(side).wait()
    for unit in range(UNITS):
        for side in range(3):
            onward(unit, side).wait()

        @pl.when(seg == units[unit])
        def _():
            slot = 0 if unit < 2 else unit % 2
            for other in others(seg, count):
                gift(unit, slot, other).wait_send()


def muon(count, squares, whole, momenta, own):
    rows = whole.shape[2]
    dma = pltpu.SemaphoreType.DMA
    vmem = pl.BlockSpec(memory_space=pltpu.VMEM)
    blocks = jax.ShapeDtypeStruct((GROUPS, UNITS, rows, D), bf16)
    return pl.pallas_call(
        functools.partial(muon_kernel, count),
        out_shape=[blocks, blocks, jax.ShapeDtypeStruct((8, 128), f32)],
        in_specs=[vmem] * 4,
        out_specs=[vmem] * 3,
        scratch_shapes=[
            pltpu.VMEM((count, 2, rows, D), bf16),
            pltpu.VMEM((D, D), f32),
            pltpu.VMEM((D, D), f32),
            pltpu.VMEM((D, D), f32),
            pltpu.VMEM((4, D, D), bf16),
            pltpu.VMEM((4, D, D), bf16),
            dma((2, count)),
            dma((UNITS,)),
            dma((3, UNITS)),
            dma((3, UNITS)),
            dma((3,)),
            dma((3,)),
        ],
        compiler_params=pltpu.CompilerParams(
            collective_id=2, has_side_effects=True, vmem_limit_bytes=VMEM_LIMIT
        ),
        cost_estimate=pl.CostEstimate(flops=2 * 10**10, bytes_accessed=4 * 10**7, transcendentals=0),
        name="muon",
    )(squares, whole, momenta, own)


def embed_kernel(
    count,
    frames_ref,
    mask_ref,
    in_ref,
    outer_ref,
    x_ref,
    mem_ref,
    total_ref,
    got_s,
    count_s,
    frame_send,
    frame_recv,
    count_send,
    count_recv,
):
    seg = lax.axis_index("seg")
    after, before = lax.rem(seg + 1, count), lax.rem(seg + count - 1, count)
    streams = frames_ref.shape[0]
    tally = jnp.sum(mask_ref[...].astype(f32), 1, keepdims=True)
    count_s[seg] = jnp.broadcast_to(
        jnp.concatenate([tally, jnp.zeros((8 - streams, 1), f32)], 0), (8, 128)
    )
    greet(seg, count, (), ())
    frame_copy = remote(frames_ref, got_s, frame_send.at[0], frame_recv.at[0], {"seg": after})
    frame_copy.start()
    for step, other in enumerate(others(seg, count)):
        remote(count_s.at[seg], count_s.at[seg], count_send.at[step], count_recv.at[seg], {"seg": other}).start()
    weight, shift = in_ref[...], outer_ref[0:1, :]
    for stream in range(streams):
        x_ref[stream] = dot_nn(jnp.transpose(frames_ref[stream]), weight) + shift
    frame_copy.wait()
    for stream in range(streams):
        mem_ref[stream] = (dot_nn(jnp.transpose(got_s[stream]), weight) + shift).astype(bf16)
    for other in others(seg, count):
        wait_bytes(count_s.at[other], count_recv.at[other])
    total_ref[...] = jnp.sum(count_s[...], 0)
    for step in range(count - 1):
        wait_bytes(count_s.at[0], count_send.at[step])


def embed(count, frames, mask, in_weight, outer_vectors):
    streams = frames.shape[0]
    dma = pltpu.SemaphoreType.DMA
    return pl.pallas_call(
        functools.partial(embed_kernel, count),
        out_shape=[
            jax.ShapeDtypeStruct((streams, SEG, D), f32),
            jax.ShapeDtypeStruct((streams, SEG, D), bf16),
            jax.ShapeDtypeStruct((8, 128), f32),
        ],
        in_specs=[pl.BlockSpec(memory_space=pltpu.VMEM)] * 4,
        out_specs=[pl.BlockSpec(memory_space=pltpu.VMEM)] * 3,
        scratch_shapes=[
            pltpu.VMEM(frames.shape, bf16),
            pltpu.VMEM((count, 8, 128), f32),
            dma((1,)),
            dma((1,)),
            dma((count,)),
            dma((count,)),
        ],
        compiler_params=pltpu.CompilerParams(
            collective_id=3, has_side_effects=True, vmem_limit_bytes=VMEM_LIMIT
        ),
        cost_estimate=pl.CostEstimate(flops=2 * 10**8, bytes_accessed=4 * 10**6, transcendentals=0),
        name="embed",
    )(frames, mask, in_weight, outer_vectors)


FEED_UP = (1, 0)
FEED_DOWN = (2, 3)
KEEP = 1.0 - 0.3 * 0.01


def finish_kernel(norm_ref, every_ref, update_ref, dout_ref, small_ref, *refs):
    (
        attn_ref,
        attn_mom_ref,
        up_ref,
        up_mom_ref,
        down_ref,
        down_mom_ref,
        out_ref,
        out_mom_ref,
        out_sec_ref,
        in_ref,
        in_mom_ref,
        in_sec_ref,
        vec_ref,
        vec_mom_ref,
        vec_sec_ref,
        outer_ref,
        outer_mom_ref,
        outer_sec_ref,
        attn_new,
        attn_mom_new,
        attn_copy_new,
        up_new,
        up_mom_new,
        up_copy_new,
        down_new,
        down_mom_new,
        down_copy_new,
        out_new,
        out_mom_new,
        out_sec_new,
        out_copy_new,
        in_new,
        in_mom_new,
        in_sec_new,
        in_copy_new,
        vec_new,
        vec_mom_new,
        vec_sec_new,
        outer_new,
        outer_mom_new,
        outer_sec_new,
        loss_new,
        norm_new,
    ) = refs
    clip = clip_of(norm_ref[0:1, 0:1])

    def muon_step(weight, momentum, grad, update, scale):
        weight = weight * KEEP - (0.3 * scale) * update.astype(f32)
        return weight, 0.5 * momentum + clip * grad.astype(f32)

    up_scale, down_scale = max(1.0, FF / D) ** 0.5, max(1.0, D / FF) ** 0.5
    for depth in range(LAYERS):
        for kind in range(4):
            weight, momentum = muon_step(
                attn_ref[depth, kind],
                attn_mom_ref[depth, kind],
                every_ref[kind, depth],
                update_ref[kind, depth],
                1.0,
            )
            attn_new[depth, kind] = weight
            attn_mom_new[depth, kind] = momentum
            attn_copy_new[depth, kind] = weight.astype(bf16)
            columns = slice(kind * TILE, (kind + 1) * TILE)
            weight, momentum = muon_step(
                up_ref[depth, :, columns],
                up_mom_ref[depth, :, columns],
                every_ref[FEED_UP[depth], 2 + kind],
                update_ref[FEED_UP[depth], 2 + kind],
                up_scale,
            )
            up_new[depth, :, columns] = weight
            up_mom_new[depth, :, columns] = momentum
            up_copy_new[depth, :, columns] = weight.astype(bf16)
            weight, momentum = muon_step(
                down_ref[depth, kind],
                down_mom_ref[depth, kind],
                every_ref[FEED_DOWN[depth], 2 + kind],
                update_ref[FEED_DOWN[depth], 2 + kind],
                down_scale,
            )
            down_new[depth, kind] = weight
            down_mom_new[depth, kind] = momentum
            down_copy_new[depth, kind] = weight.astype(bf16)
    for low in range(2):
        for right in range(2):
            columns = slice(right * D, (right + 1) * D)
            weight, moment, second = adamw(
                out_ref[low, :, columns],
                out_mom_ref[low, :, columns],
                out_sec_ref[low, :, columns],
                dout_ref[2 * right + low].astype(f32) * clip,
                0.05,
                0.01,
            )
            out_new[low, :, columns] = weight
            out_mom_new[low, :, columns] = moment
            out_sec_new[low, :, columns] = second
            out_copy_new[low, :, columns] = weight.astype(bf16)

    @pl.when(pl.program_id(0) == 0)
    def _():
        inputs = in_ref.shape[0]
        weight, moment, second = adamw(
            in_ref[...], in_mom_ref[...], in_sec_ref[...], small_ref[0:inputs, :] * clip, 0.05, 0.01
        )
        in_new[...] = weight
        in_mom_new[...] = moment
        in_sec_new[...] = second
        in_copy_new[...] = weight.astype(bf16)

        norm_new[...] = norm_ref[0:1, 0:1]
        loss_new[...] = small_ref[inputs + 37 : inputs + 38, 0:1]

        def rows_of(first, last, base):
            return small_ref[inputs + base + first : inputs + base + last, :]

        for depth in range(LAYERS):
            base = 16 * depth
            for low, high, grad in (
                (0, 2, rows_of(0, 2, base)),
                (2, 4, rows_of(0, 2, base + 8)),
                (4, 7, rows_of(2, 5, base)),
                (7, 8, rows_of(2, 3, base + 8)),
                (8, 12, rows_of(4, 8, base + 8)),
            ):
                weight, moment, second = adamw(
                    vec_ref[low:high, depth],
                    vec_mom_ref[low:high, depth],
                    vec_sec_ref[low:high, depth],
                    grad * clip,
                    0.25,
                    0.0,
                )
                vec_new[low:high, depth] = weight
                vec_mom_new[low:high, depth] = moment
                vec_sec_new[low:high, depth] = second
        for low, high, grad in ((0, 1, rows_of(5, 6, 0)), (1, 5, rows_of(1, 5, 32))):
            weight, moment, second = adamw(
                outer_ref[low:high, :], outer_mom_ref[low:high, :], outer_sec_ref[low:high, :], grad * clip, 0.25, 0.0
            )
            outer_new[low:high, :] = weight
            outer_mom_new[low:high, :] = moment
            outer_sec_new[low:high, :] = second


def finish(rows, norm, every, updates, dout, small, arrays):
    steps = rows // 16
    attn, _, up, _, down, _, out, _, _, inp, _, _, vec, _, _, outer, _, _ = arrays
    codes = out.shape[2]
    part = out.shape[1] // steps
    blocks = pl.BlockSpec((GROUPS, UNITS, 16, D), lambda i: (0, 0, i, 0))
    attn_spec = pl.BlockSpec((LAYERS, 4, 16, D), lambda i: (0, 0, i, 0))
    up_spec = pl.BlockSpec((LAYERS, 16, FF), lambda i: (0, i, 0))
    out_spec = pl.BlockSpec((2, part, codes), lambda i: (0, i, 0))
    dout_spec = pl.BlockSpec((GROUPS, part, D), lambda i: (0, i, 0))
    in_spec, vec_spec, outer_spec = whole_spec(inp.shape), whole_spec(vec.shape), whole_spec(outer.shape)

    def like(array, dtype=f32):
        return jax.ShapeDtypeStruct(array.shape, dtype)

    return pl.pallas_call(
        finish_kernel,
        grid=(steps,),
        out_shape=[like(attn), like(attn), like(attn, bf16)]
        + [like(up), like(up), like(up, bf16)]
        + [like(down), like(down), like(down, bf16)]
        + [like(out)] * 3
        + [like(out, bf16)]
        + [like(inp)] * 3
        + [like(inp, bf16)]
        + [like(vec)] * 3
        + [like(outer)] * 3
        + [jax.ShapeDtypeStruct((1, 1), f32)] * 2,
        in_specs=[whole_spec((8, 128)), blocks, blocks, dout_spec, whole_spec(small.shape)]
        + [attn_spec] * 2
        + [up_spec] * 2
        + [attn_spec] * 2
        + [out_spec] * 3
        + [in_spec] * 3
        + [vec_spec] * 3
        + [outer_spec] * 3,
        out_specs=[attn_spec] * 3
        + [up_spec] * 3
        + [attn_spec] * 3
        + [out_spec] * 4
        + [in_spec] * 4
        + [vec_spec] * 3
        + [outer_spec] * 3
        + [whole_spec((1, 1))] * 2,
        compiler_params=pltpu.CompilerParams(vmem_limit_bytes=VMEM_LIMIT),
        cost_estimate=pl.CostEstimate(flops=10**8, bytes_accessed=4 * 10**7, transcendentals=0),
        name="finish",
    )(norm, every, updates, dout, small, *arrays)


def local(
    frames,
    speech_mask,
    targets,
    in_proj,
    in_moment,
    in_second,
    out_proj,
    out_moment,
    out_second,
    layer_vectors,
    vectors_moment,
    vectors_second,
    outer_vectors,
    outer_moment,
    outer_second,
    attn_proj,
    attn_momentum,
    ff_up,
    up_momentum,
    ff_down,
    down_momentum,
    in_copy,
    out_copy,
    attn_copy,
    up_copy,
    down_copy,
):
    segment = lax.axis_index("seg")
    count, dp_count = lax.axis_size("seg"), lax.axis_size("dp")
    rows = D // count
    streams = frames.shape[0]
    stream_total = streams * dp_count
    group = lax.axis_index("dp") % GROUPS
    feeds = jnp.stack(
        [
            jnp.swapaxes(up_momentum[1].reshape(rows, 4, D), 0, 1),
            jnp.swapaxes(up_momentum[0].reshape(rows, 4, D), 0, 1),
            down_momentum[0].reshape(4, rows, D),
            down_momentum[1].reshape(4, rows, D),
        ]
    )
    owned = jnp.concatenate(
        [
            lax.dynamic_index_in_dim(attn_momentum, group, 1, keepdims=False),
            lax.dynamic_index_in_dim(feeds, group, 0, keepdims=False),
        ],
        0,
    ).astype(bf16)
    momenta = lax.all_gather(owned, "seg", axis=0, tiled=False)
    frames_t = jnp.swapaxes(frames, 1, 2)
    bias = jnp.where(segment > 0, 0.0, -1e30).astype(f32)[None]
    hidden, memory, totals = embed(count, frames_t, speech_mask, in_copy, outer_vectors)
    memory = [memory] * streams
    kept = []
    for depth in range(LAYERS):
        saved, passed = None, []
        for stream in range(streams):
            saved, short = forward_layer(
                depth,
                stream,
                streams,
                bias,
                hidden,
                memory[stream],
                attn_copy,
                up_copy,
                down_copy,
                layer_vectors,
                saved,
            )
            if depth + 1 < LAYERS:
                passed.append(from_behind(short, "seg", 1))
        kept.append((hidden, saved[8], saved))
        hidden = saved[0]
        memory = passed
    grad_hidden, grad_out, head_outer = head(
        hidden, targets, speech_mask, totals, out_copy, outer_vectors, 1.0 / stream_total, momenta
    )
    vector_grads, feed_done = [], [None, None]
    carried = grad_out.reshape(GROUPS * D // 2, D)
    carried_done = []
    for depth in reversed(range(LAYERS)):
        entering, held, saved = kept[depth]
        dafter, grad_up, grad_down, feed_vec, done = feed_back(
            depth, grad_hidden, saved[7], up_copy, down_copy, layer_vectors, count, dp_count, carried
        )
        carried_done.append(done)
        grad_hidden, grad_attn, attn_vec, grad_in, feed_done[depth] = attend_back(
            depth,
            bias,
            dafter,
            entering,
            held,
            saved[1:7],
            attn_copy,
            layer_vectors,
            frames_t,
            grad_up,
            grad_down,
            count,
            dp_count,
        )
        carried = grad_attn.reshape(4 * D, D)
        vector_grads = [attn_vec, feed_vec] + vector_grads
    out_done, attn_done = carried_done
    every_out = lax.all_gather(out_done, ("dp", "seg"), axis=0, tiled=True)[: GROUPS * D // 2]
    every_out = every_out.reshape(GROUPS, D // 2, D)
    whole, own, small, squares = reduce_grads(
        count,
        dp_count,
        grad_attn,
        attn_done,
        feed_done[0],
        feed_done[1],
        out_done,
        [grad_in] + vector_grads + [head_outer],
    )
    updates, every, norm = muon(count, squares, whole, momenta, own)
    split = (LAYERS, 4, rows, D)
    halved = (2, D // 2, out_proj.shape[1])
    (
        attn_new,
        attn_mom,
        attn_copy_new,
        up_new,
        up_mom,
        up_copy_new,
        down_new,
        down_mom,
        down_copy_new,
        out_new,
        out_moment_new,
        out_second_new,
        out_copy_new,
        in_new,
        in_moment_new,
        in_second_new,
        in_copy_new,
        vectors_new,
        vectors_moment_new,
        vectors_second_new,
        outer_new,
        outer_moment_new,
        outer_second_new,
        loss_sum,
        norm,
    ) = finish(
        rows,
        norm,
        every,
        updates,
        every_out,
        small,
        [
            attn_proj,
            attn_momentum,
            ff_up,
            up_momentum,
            ff_down.reshape(split),
            down_momentum.reshape(split),
            out_proj.reshape(halved),
            out_moment.reshape(halved),
            out_second.reshape(halved),
            in_proj,
            in_moment,
            in_second,
            jnp.swapaxes(layer_vectors, 0, 1),
            jnp.swapaxes(vectors_moment, 0, 1),
            jnp.swapaxes(vectors_second, 0, 1),
            outer_vectors,
            outer_moment,
            outer_second,
        ],
    )
    return (
        loss_sum.reshape(()),
        norm.reshape(()),
        in_new,
        in_moment_new,
        in_second_new,
        out_new.reshape(out_proj.shape),
        out_moment_new.reshape(out_proj.shape),
        out_second_new.reshape(out_proj.shape),
        jnp.swapaxes(vectors_new, 0, 1),
        jnp.swapaxes(vectors_moment_new, 0, 1),
        jnp.swapaxes(vectors_second_new, 0, 1),
        outer_new,
        outer_moment_new,
        outer_second_new,
        attn_new,
        attn_mom,
        up_new,
        up_mom,
        down_new.reshape(ff_down.shape),
        down_mom.reshape(ff_down.shape),
        in_copy_new,
        out_copy_new.reshape(out_proj.shape),
        attn_copy_new,
        up_copy_new,
        down_copy_new.reshape(ff_down.shape),
    )


def solution(mesh):
    return jax.shard_map(
        local,
        mesh=mesh,
        in_specs=(
            P("dp", "seg", None),
            P("dp", "seg"),
            P("dp", "seg"),
            P(),
            P(),
            P(),
            P(),
            P(),
            P(),
            P(),
            P(),
            P(),
            P(),
            P(),
            P(),
            P(None, None, "seg", None),
            P(None, None, "seg", None),
            P(None, "seg", None),
            P(None, "seg", None),
            P(None, "seg", None),
            P(None, "seg", None),
            P(),
            P(),
            P(),
            P(),
            P(),
        ),
        out_specs=(
            P(),
            P(),
            P(),
            P(),
            P(),
            P(),
            P(),
            P(),
            P(),
            P(),
            P(),
            P(),
            P(),
            P(),
            P(None, None, "seg", None),
            P(None, None, "seg", None),
            P(None, "seg", None),
            P(None, "seg", None),
            P(None, "seg", None),
            P(None, "seg", None),
            P(),
            P(),
            P(None, None, "seg", None),
            P(None, "seg", None),
            P(None, "seg", None),
        ),
        check_vma=False,
    )
```

```python
import functools
import math

import jax
import jax.numpy as jnp
from jax import lax
from jax.experimental import pallas as pl
from jax.experimental.pallas import tpu as pltpu
from jax.sharding import PartitionSpec as P

D = 512
HEAD_DIM = 64
HEADS = D // HEAD_DIM
FF = 2048
LAYERS = 2
STEP = 10
SEG = 512
HALF = 256
PAIR = 2 * HEAD_DIM
TILE = 512
VMEM_LIMIT = 56 * 1024 * 1024
GELU_SCALE = math.sqrt(2.0 / math.pi)

f32 = jnp.float32
bf16 = jnp.bfloat16


def dot_nn(left, right):
    return lax.dot_general(left, right, (((1,), (0,)), ((), ())), preferred_element_type=f32)


def dot_nt(left, right):
    return lax.dot_general(left, right, (((1,), (1,)), ((), ())), preferred_element_type=f32)


def dot_tn(left, right):
    return lax.dot_general(left, right, (((0,), (0,)), ((), ())), preferred_element_type=f32)


def normalised(values):
    centred = values - jnp.mean(values, -1, keepdims=True)
    scale = lax.rsqrt(jnp.mean(centred * centred, -1, keepdims=True) + 1e-05)
    return centred * scale, scale


def norm_back(grad, gain, unit, scale):
    part = grad * gain
    mean_part = jnp.mean(part, -1, keepdims=True)
    mean_unit = jnp.mean(part * unit, -1, keepdims=True)
    return scale * (part - mean_part - unit * mean_unit)


def column_sum(values):
    return jnp.sum(values, 0, keepdims=True)


def head_masks():
    lane = lax.broadcasted_iota(jnp.int32, (1, PAIR), 1)
    return (lane < HEAD_DIM).astype(bf16), (lane >= HEAD_DIM).astype(bf16)


def pair_lanes(pair):
    return pl.ds(pl.multiple_of(pair * PAIR, PAIR), PAIR)


def forward_kernel(
    depth,
    stream,
    bias_ref,
    x_ref,
    mem_ref,
    attn_ref,
    up_ref,
    down_ref,
    vec_ref,
    *refs,
):
    (
        hid_ref,
        hid16_ref,
        keyin_out,
        q_out,
        k_out,
        v_out,
        lse_ref,
        mixed_ref,
        after_ref,
        kept_out,
        act_s,
        lse_s,
        up_s,
        down_s,
        keyin_ref,
        q_ref,
        k_ref,
        v_ref,
        in_sem,
        out_sem,
    ) = refs[-20:]
    weights_in = (
        pltpu.make_async_copy(up_ref.at[depth], up_s, in_sem.at[0]),
        pltpu.make_async_copy(down_ref.at[depth], down_s, in_sem.at[1]),
    )
    for copy in weights_in:
        copy.start()
    saved_out = [
        pltpu.make_async_copy(source, target.at[stream], out_sem.at[place])
        for place, (source, target) in enumerate(
            ((keyin_ref, keyin_out), (q_ref, q_out), (k_ref, k_out), (v_ref, v_out))
        )
    ]
    kept_out[...] = mem_ref[...]
    x = x_ref[...]
    own_unit, _ = normalised(x)
    gain, shift = vec_ref[0:1, :], vec_ref[1:2, :]
    normed = (own_unit * gain + shift).astype(bf16)
    mem_unit, _ = normalised(mem_ref[...].astype(f32))
    mem_normed = (mem_unit * gain + shift).astype(bf16)
    keyin_ref[0:SEG, :] = mem_normed
    keyin_ref[SEG:, :] = normed
    q_ref[...] = (dot_nn(normed, attn_ref[0]) + vec_ref[4:5, :]).astype(bf16) * jnp.asarray(HEAD_DIM**-0.5, bf16)
    k_ref[0:SEG, :] = dot_nn(mem_normed, attn_ref[1]).astype(bf16)
    k_ref[SEG:, :] = dot_nn(normed, attn_ref[1]).astype(bf16)
    v_ref[0:SEG, :] = (dot_nn(mem_normed, attn_ref[2]) + vec_ref[5:6, :]).astype(bf16)
    v_ref[SEG:, :] = (dot_nn(normed, attn_ref[2]) + vec_ref[5:6, :]).astype(bf16)
    for copy in saved_out:
        copy.start()
    first, second = head_masks()
    memory_bias = bias_ref[0]
    lane = lax.broadcasted_iota(jnp.int32, (HALF, PAIR), 1)
    query_pos = lax.broadcasted_iota(jnp.int32, (2 * HALF, HALF), 0) % HALF
    key_pos = lax.broadcasted_iota(jnp.int32, (2 * HALF, HALF), 1)
    diagonal = key_pos <= query_pos
    lse_s[...] = jnp.zeros_like(lse_s)

    def pair_body(pair, carry):
        lanes = pair_lanes(pair)
        for block in range(2):
            rows = slice(block * HALF, (block + 1) * HALF)
            q_pair = q_ref[rows, lanes]
            q_both = jnp.concatenate([q_pair * first, q_pair * second], 0)
            spans = [(0, SEG, 0)]
            if block:
                spans.append((SEG, SEG + HALF, 1))
            spans.append((SEG + block * HALF, SEG + (block + 1) * HALF, 2))
            scores = []
            for low, high, kind in spans:
                part = dot_nt(q_both, k_ref[low:high, lanes])
                if kind == 2:
                    part = jnp.where(diagonal, part, -1e30)
                scores.append(part)
            peaks = [jnp.max(part, -1, keepdims=True) for part in scores]
            peaks[0] = peaks[0] + memory_bias
            most = functools.reduce(jnp.maximum, peaks)
            weights = [
                jnp.exp(part - (most if place else most - memory_bias)) for place, part in enumerate(scores)
            ]
            total = functools.reduce(jnp.add, [jnp.sum(part, -1, keepdims=True) for part in weights])
            mixed = functools.reduce(
                jnp.add,
                [
                    dot_nn(part.astype(bf16), v_ref[low:high, lanes])
                    for part, (low, high, kind) in zip(weights, spans)
                ],
            )
            mixed = mixed / total
            mixed_ref[rows, lanes] = jnp.where(lane < HEAD_DIM, mixed[:HALF], mixed[HALF:]).astype(bf16)
            lse = most + jnp.log(total)
            kept = jnp.where(lane == 2 * pair, lse[:HALF], lse_s[rows, :])
            lse_s[rows, :] = jnp.where(lane == 2 * pair + 1, lse[HALF:], kept)
        return carry

    lax.fori_loop(0, HEADS // 2, pair_body, 0)
    lse_ref[...] = jnp.transpose(lse_s[...])[0:HEADS, :]
    after = x + (dot_nn(mixed_ref[...], attn_ref[3]) + vec_ref[6:7, :])
    after_ref[...] = after
    unit, _ = normalised(after)
    normed_two = (unit * vec_ref[2:3, :] + vec_ref[3:4, :]).astype(bf16)
    for copy in weights_in:
        copy.wait()
    for tile in range(FF // TILE):
        columns = slice(tile * TILE, (tile + 1) * TILE)
        inner = dot_nn(normed_two, up_s[:, columns]) + vec_ref[8 + tile : 9 + tile, :]
        act_s[:, columns] = (
            0.5 * inner * (1.0 + jnp.tanh(GELU_SCALE * (inner + 0.044715 * inner * inner * inner)))
        ).astype(bf16)
    hidden = after + (dot_nn(act_s[...], down_s[...]) + vec_ref[7:8, :])
    hid_ref[...] = hidden
    hid16_ref[...] = hidden.astype(bf16)
    for copy in saved_out:
        copy.wait()


SAVED = (
    ((SEG, D), f32),
    ((2 * SEG, D), bf16),
    ((SEG, D), bf16),
    ((2 * SEG, D), bf16),
    ((2 * SEG, D), bf16),
    ((HEADS, SEG), f32),
    ((SEG, D), bf16),
    ((SEG, D), f32),
    ((SEG, D), bf16),
)


def whole_spec(shape):
    return pl.BlockSpec(shape, lambda *_: (0,) * len(shape))


def stream_spec(shape, stream=None):
    zeros = (0,) * len(shape)
    if stream is None:
        return pl.BlockSpec((None,) + shape, lambda i: (i,) + zeros)
    return pl.BlockSpec((None,) + shape, lambda i: (stream,) + zeros)


def layer_spec(shape, depth):
    zeros = (0,) * len(shape)
    return pl.BlockSpec((None,) + shape, lambda *_: (depth,) + zeros)


def forward_layer(depth, stream, streams, bias, hidden, memory, attn, upper, lower, vectors, earlier):
    saved_shapes = [jax.ShapeDtypeStruct((streams,) + shape, dtype) for shape, dtype in SAVED]
    saved_specs = [stream_spec(shape, stream) for shape, dtype in SAVED]
    out_shape = [saved_shapes[0], jax.ShapeDtypeStruct((SEG, D), bf16)] + saved_shapes[1:]
    out_specs = [saved_specs[0], whole_spec((SEG, D))] + saved_specs[1:]
    for place in (2, 3, 4, 5):
        out_specs[place] = pl.BlockSpec(memory_space=pl.ANY)
    operands = [bias, hidden, memory, attn, upper, lower, vectors]
    in_specs = [
        pl.BlockSpec(memory_space=pltpu.SMEM),
        stream_spec((SEG, D), stream),
        stream_spec((SEG, D), stream) if memory.ndim == 3 else whole_spec((SEG, D)),
        layer_spec(attn.shape[1:], depth),
        pl.BlockSpec(memory_space=pl.ANY),
        pl.BlockSpec(memory_space=pl.ANY),
        layer_spec(vectors.shape[1:], depth),
    ]
    aliases = {}
    if earlier is not None:
        for place, array in enumerate(earlier):
            aliases[len(operands)] = place if place == 0 else place + 1
            operands.append(array)
            in_specs.append(pl.BlockSpec(memory_space=pl.ANY))
    out = pl.pallas_call(
        functools.partial(forward_kernel, depth, stream),
        grid=(1,),
        out_shape=out_shape,
        in_specs=in_specs,
        out_specs=out_specs,
        scratch_shapes=[
            pltpu.VMEM((SEG, FF), bf16),
            pltpu.VMEM((SEG, PAIR), f32),
            pltpu.VMEM((D, FF), bf16),
            pltpu.VMEM((FF, D), bf16),
            pltpu.VMEM((2 * SEG, D), bf16),
            pltpu.VMEM((SEG, D), bf16),
            pltpu.VMEM((2 * SEG, D), bf16),
            pltpu.VMEM((2 * SEG, D), bf16),
            pltpu.SemaphoreType.DMA((2,)),
            pltpu.SemaphoreType.DMA((4,)),
        ],
        input_output_aliases=aliases,
        compiler_params=pltpu.CompilerParams(vmem_limit_bytes=VMEM_LIMIT),
        cost_estimate=pl.CostEstimate(flops=10**10, bytes_accessed=2 * 10**7, transcendentals=10**7),
        name="layer_forward",
    )(*operands)
    return [out[0]] + list(out[2:]), out[1]


def head_kernel(scale, x_ref, target_ref, mask_ref, total_ref, out_ref, outer_ref, mom_ref, g_ref, dout_ref, douter_ref, acc_s):
    step = pl.program_id(0)

    @pl.when(step == 0)
    def _():
        acc_s[...] = jnp.zeros_like(acc_s)
        douter_ref[...] = jnp.zeros_like(douter_ref)

    unit, rscale = normalised(x_ref[...])
    gain = outer_ref[1:2, :]
    normed = (unit * gain + outer_ref[2:3, :]).astype(bf16)
    shift = jnp.concatenate([outer_ref[3:4, :], outer_ref[4:5, :]], 1)
    logits = dot_nn(normed, out_ref[...]) + shift
    most = jnp.max(logits, -1, keepdims=True)
    powers = jnp.exp(logits - most)
    total = jnp.sum(powers, -1, keepdims=True)
    target_row = target_ref[pl.ds(step, 1), :].astype(f32)
    weight_row = mask_ref[pl.ds(step, 1), :].astype(f32) * (1.0 / total_ref[pl.ds(step, 1), 0:1])
    columns = jnp.transpose(jnp.concatenate([target_row, weight_row, jnp.zeros((6, SEG), f32)], 0))
    target, weight = columns[:, 0:1].astype(jnp.int32), columns[:, 1:2]
    chosen = lax.broadcasted_iota(jnp.int32, logits.shape, 1) == target
    picked = jnp.sum(jnp.where(chosen, logits, 0.0), -1, keepdims=True)
    loss = jnp.sum(weight * (most + jnp.log(total) - picked), 0, keepdims=True)
    spread = weight * scale
    dlogits = (powers * (spread / total) - jnp.where(chosen, spread, 0.0)).astype(bf16)
    acc_s[...] += dot_nn(jnp.transpose(normed), dlogits)
    bias_grad = column_sum(dlogits.astype(f32))
    dnormed = dot_nt(dlogits, out_ref[...])
    g_ref[...] = norm_back(dnormed, gain, unit, rscale)
    douter_ref[1:2, :] += column_sum(dnormed * unit)
    douter_ref[2:3, :] += column_sum(dnormed)
    douter_ref[3:4, :] += bias_grad[:, :D]
    douter_ref[4:5, :] += bias_grad[:, D:]
    douter_ref[5:6, :] += jnp.broadcast_to(loss, (1, D))

    @pl.when(step == pl.num_programs(0) - 1)
    def _():
        half = D // 2
        for right in range(2):
            for low in range(2):
                dout_ref[right, low] = acc_s[
                    low * half : (low + 1) * half, right * D : (right + 1) * D
                ]


def head(hidden, targets, mask, totals, out_weight, outer_vectors, scale, momenta):
    streams = hidden.shape[0]
    codes = out_weight.shape[1]
    return pl.pallas_call(
        functools.partial(head_kernel, scale),
        grid=(streams,),
        out_shape=[
            jax.ShapeDtypeStruct((streams, SEG, D), f32),
            jax.ShapeDtypeStruct((2, 2, D // 2, D), f32),
            jax.ShapeDtypeStruct((8, D), f32),
        ],
        in_specs=[
            stream_spec((SEG, D)),
            whole_spec((streams, SEG)),
            whole_spec((streams, SEG)),
            whole_spec((8, 128)),
            whole_spec((D, codes)),
            whole_spec(outer_vectors.shape),
            pl.BlockSpec(memory_space=pl.ANY),
        ],
        out_specs=[stream_spec((SEG, D)), whole_spec((2, 2, D // 2, D)), whole_spec((8, D))],
        scratch_shapes=[pltpu.VMEM((D, codes), f32)],
        compiler_params=pltpu.CompilerParams(vmem_limit_bytes=VMEM_LIMIT),
        cost_estimate=pl.CostEstimate(flops=33 * 10**8, bytes_accessed=10**7, transcendentals=10**6),
        name="head",
    )(hidden, targets, mask, totals, out_weight, outer_vectors, momenta)


def feed_back_kernel(streams, g_ref, after_ref, up_ref, down_ref, vec_ref, *refs):
    step = pl.program_id(0)
    grad_ref, dafter_ref, dup_ref, ddown_ref, dvec_ref, done_ref, normed_s, branch_s, act_s, inner_s = refs[:10]
    carry = AttnCarry(grad_ref, refs[10 : 10 + CARRY_REFS], refs[10 + CARRY_REFS :])
    planes = carry.planes
    later = range(1, planes)
    beats = [
        [("b", place) for place in range(planes)],
        [("m", 0)],
        [("m", place) for place in later] + [("e", 0)],
        [("e", place) for place in range(1, planes // 2)],
        [("e", place) for place in range(planes // 2, planes)],
    ]

    @pl.when(step == 0)
    def _():
        hail(carry.targets)
        carry.load_all()
        dvec_ref[...] = jnp.zeros_like(dvec_ref)

    rows = pl.ds(pl.multiple_of(step * SEG, SEG), SEG)
    grad = g_ref[...]
    branch = grad.astype(bf16)
    dvec_ref[2:3, :] += column_sum(branch.astype(f32))
    unit, scale = normalised(after_ref[...])
    gain = vec_ref[2:3, :]
    normed = (unit * gain + vec_ref[3:4, :]).astype(bf16)
    normed_s[:, rows] = jnp.transpose(normed)
    branch_s[:, rows] = jnp.transpose(branch)

    @pl.when(step == 0)
    def _():
        meet(carry.targets)
        carry.send_all()

    for tile in range(FF // TILE):
        columns = slice(tile * TILE, (tile + 1) * TILE)
        inner = dot_nn(normed, up_ref[:, columns]) + vec_ref[8 + tile : 9 + tile, :]
        dact = dot_nt(branch, down_ref[columns, :])
        square = inner * inner
        bent = jnp.tanh(inner * (GELU_SCALE + (GELU_SCALE * 0.044715) * square))
        half = 0.5 * (1.0 + bent)
        act_s[rows, columns] = (inner * half).astype(bf16)
        slope = half + inner * (half * (1.0 - bent)) * (GELU_SCALE + (GELU_SCALE * 0.134145) * square)
        dinner = (dact * slope).astype(bf16)
        inner_s[rows, columns] = dinner
        dvec_ref[4 + tile : 5 + tile, :] += column_sum(dinner.astype(f32))

    @pl.when(step == 0)
    def _():
        carry.run(beats[0])

    @pl.when(step == streams - 1)
    def _():
        carry.run(beats[2])

    dnormed = dot_nt(inner_s[rows, :], up_ref[...])
    dvec_ref[0:1, :] += column_sum(dnormed * unit)
    dvec_ref[1:2, :] += column_sum(dnormed)
    dafter_ref[...] = grad + norm_back(dnormed, gain, unit, scale)

    @pl.when(step == 0)
    def _():
        carry.run(beats[1])

    @pl.when(step == streams - 1)
    def _():
        carry.run(beats[3])
        for tile in range(FF // TILE):
            columns = slice(tile * TILE, (tile + 1) * TILE)
            dup_ref[tile] = dot_nn(normed_s[...], inner_s[:, columns]).astype(bf16)
        carry.run(beats[4])
        for tile in range(FF // TILE):
            columns = slice(tile * TILE, (tile + 1) * TILE)
            ddown_ref[columns, :] = jnp.transpose(dot_nn(branch_s[...], act_s[:, columns]).astype(bf16))
        carry.finish(done_ref)


def feed_back(depth, grad, after, upper, lower, vectors, count, dp_count, attn_grad):
    streams = grad.shape[0]
    rows = attn_grad.shape[0] // (GROUPS * count)
    in_specs = [
        stream_spec((SEG, D)),
        stream_spec((SEG, D)),
        layer_spec(upper.shape[1:], depth),
        layer_spec(lower.shape[1:], depth),
        layer_spec(vectors.shape[1:], depth),
    ]
    out_shape = [
        jax.ShapeDtypeStruct((streams, SEG, D), f32),
        jax.ShapeDtypeStruct((FF // TILE, D, TILE), bf16),
        jax.ShapeDtypeStruct((FF, D), bf16),
        jax.ShapeDtypeStruct((8, D), f32),
    ]
    out_specs = [
        stream_spec((SEG, D)),
        whole_spec((FF // TILE, D, TILE)),
        whole_spec((FF, D)),
        whole_spec((8, D)),
    ]
    scratch = [
        pltpu.VMEM((D, streams * SEG), bf16),
        pltpu.VMEM((D, streams * SEG), bf16),
        pltpu.VMEM((streams * SEG, FF), bf16),
        pltpu.VMEM((streams * SEG, FF), bf16),
    ]
    operands = [grad, after, upper, lower, vectors]
    in_specs.append(pl.BlockSpec(memory_space=pl.ANY))
    operands.append(attn_grad.reshape(2, 2, count, rows, D))
    out_shape.append(jax.ShapeDtypeStruct((rows, D), bf16))
    out_specs.append(whole_spec((rows, D)))
    scratch = scratch + carry_scratch("attn", rows, count, dp_count, attn_grad.dtype)
    params = {"collective_id": 6 + depth, "has_side_effects": True}
    return pl.pallas_call(
        functools.partial(feed_back_kernel, streams),
        grid=(streams,),
        out_shape=out_shape,
        in_specs=in_specs,
        out_specs=out_specs,
        scratch_shapes=scratch,
        compiler_params=pltpu.CompilerParams(vmem_limit_bytes=VMEM_LIMIT, **params),
        cost_estimate=pl.CostEstimate(flops=11 * 10**9, bytes_accessed=2 * 10**7, transcendentals=2 * 10**6),
        name="feed_back",
    )(*operands)


def attend_back_kernel(
    streams,
    depth,
    bias_ref,
    dafter_ref,
    x_ref,
    mem_ref,
    keyin_ref,
    q_ref,
    k_ref,
    v_ref,
    lse_ref,
    mixed_ref,
    attn_ref,
    vec_ref,
    frames_ref,
    dup_ref,
    ddown_ref,
    dx_ref,
    dattn_ref,
    dvec_ref,
    din_ref,
    done_ref,
    attn_s,
    dmixed_s,
    dq_s,
    dk_s,
    dv_s,
    ds_s,
    delta_s,
    *refs,
):
    step = pl.program_id(0)
    pairs = HEADS // 2
    carry = FeedCarry(depth, dup_ref, ddown_ref, refs[: CARRY_REFS + 2], refs[CARRY_REFS + 2 :])

    @pl.when(step == 0)
    def _():
        hail(carry.targets)
        carry.load_all()
        attn_s[...] = jnp.zeros_like(attn_s)
        dvec_ref[...] = jnp.zeros_like(dvec_ref)
        din_ref[...] = jnp.zeros_like(din_ref)

    dafter = dafter_ref[...]
    branch = dafter.astype(bf16)
    dvec_ref[4:5, :] += column_sum(branch.astype(f32))
    dmixed = dot_nt(branch, attn_ref[3]).astype(bf16)
    dmixed_s[...] = dmixed
    attn_s[3] += dot_nn(jnp.transpose(mixed_ref[...]), branch)
    product = dmixed.astype(f32) * mixed_ref[...].astype(f32)
    high = product.astype(bf16)
    rest = (product - high.astype(f32)).astype(bf16)
    owner = lax.broadcasted_iota(jnp.int32, (HEADS, D), 1) // HEAD_DIM
    pick = (owner == lax.broadcasted_iota(jnp.int32, (HEADS, D), 0)).astype(bf16)
    delta_s[...] = dot_nt(pick, high) + dot_nt(pick, rest)
    first, second = head_masks()
    memory_bias = bias_ref[0]
    key_pos = lax.broadcasted_iota(jnp.int32, (HALF, 2 * HALF), 0)
    query_pos = lax.broadcasted_iota(jnp.int32, (HALF, 2 * HALF), 1) % HALF
    diagonal = key_pos <= query_pos
    head_row = lax.broadcasted_iota(jnp.int32, (PAIR, HALF), 0)

    @pl.when(step == 0)
    def _():
        meet(carry.targets)
        carry.send_all()

    def pair_body(pair, state):
        lanes = pair_lanes(pair)
        q_pair, do_pair = q_ref[:, lanes], dmixed_s[:, lanes]

        def spread(value):
            return jnp.concatenate(
                [value[:HALF] * first, value[:HALF] * second, value[HALF:] * first, value[HALF:] * second], 0
            )

        q_all, do_all = spread(q_pair), spread(do_pair)

        def rows_of(ref):
            one, two = ref[pl.ds(2 * pair, 1), :], ref[pl.ds(2 * pair + 1, 1), :]
            return jnp.concatenate([one[:, :HALF], two[:, :HALF], one[:, HALF:], two[:, HALF:]], 1)

        lse_all, delta_all = rows_of(lse_ref), rows_of(delta_s)
        for block in range(4):
            keys = slice(block * HALF, (block + 1) * HALF)
            start = 2 * HALF if block == 3 else 0
            scores = dot_nt(k_ref[keys, lanes], q_all[start:])
            shift = lse_all - memory_bias if block < 2 else lse_all[:, start:]
            weights = jnp.exp(scores - shift)
            if block == 2:
                weights = jnp.concatenate(
                    [jnp.where(diagonal, weights[:, : 2 * HALF], 0.0), weights[:, 2 * HALF :]], 1
                )
            if block == 3:
                weights = jnp.where(diagonal, weights, 0.0)
            dweights = dot_nt(v_ref[keys, lanes], do_all[start:])
            dscores = (weights * (dweights - delta_all[:, start:])).astype(bf16)
            dv_s[keys, lanes] = dot_nn(weights.astype(bf16), do_all[start:]).astype(bf16)
            dk_s[keys, lanes] = dot_nn(dscores, q_all[start:]).astype(bf16)
            ds_s[keys, start:] = dscores
        k_t = jnp.transpose(k_ref[:, lanes])
        for block in range(2):
            seen = SEG + (block + 1) * HALF
            grads = dot_nn(k_t[:, :seen], ds_s[:seen, block * 2 * HALF : (block + 1) * 2 * HALF])
            grads = jnp.where(head_row < HEAD_DIM, grads[:, :HALF], grads[:, HALF:])
            dq_s[block * HALF : (block + 1) * HALF, lanes] = (
                jnp.transpose(grads) * (HEAD_DIM**-0.5)
            ).astype(bf16)
        carry.tick(pairs * step + pair, pairs * streams, 1)
        return state

    lax.fori_loop(0, pairs, pair_body, 0)
    dq, dk, dv = dq_s[...], dk_s[...], dv_s[...]
    keyin_t = jnp.transpose(keyin_ref[...])
    attn_s[0] += dot_nn(keyin_t[:, SEG:], dq)
    attn_s[1] += dot_nn(keyin_t, dk)
    attn_s[2] += dot_nn(keyin_t, dv)
    dvec_ref[2:3, :] += column_sum(dq.astype(f32))
    dvec_ref[3:4, :] += column_sum(dv.astype(f32))
    dkeyin = dot_nt(dk, attn_ref[1]) + dot_nt(dv, attn_ref[2])
    dmem = dkeyin[:SEG]
    down = dkeyin[SEG:] + dot_nt(dq, attn_ref[0])
    gain = vec_ref[0:1, :]
    unit, scale = normalised(x_ref[...])
    mem_unit, _ = normalised(mem_ref[...].astype(f32))
    dvec_ref[0:1, :] += column_sum(down * unit + dmem * mem_unit)
    dvec_ref[1:2, :] += column_sum(down + dmem)
    dx = dafter + norm_back(down, gain, unit, scale)
    dx_ref[...] = dx
    if depth == 0:
        dx_high = dx.astype(bf16)
        dx_rest = (dx - dx_high.astype(f32)).astype(bf16)
        din_ref[...] += dot_nn(frames_ref[...], dx_high) + dot_nn(frames_ref[...], dx_rest)
        dvec_ref[5:6, :] += column_sum(dx)

    @pl.when(step == pl.num_programs(0) - 1)
    def _():
        dattn_ref[...] = attn_s[...].astype(bf16)
        carry.rest(pairs * streams, 1)
        carry.finish(done_ref)


def attend_back(depth, bias, dafter, x, memory, saved, attn, vectors, frames, up_grad, down_grad, count, dp_count):
    streams = dafter.shape[0]
    keyin, q, k, v, lse, mixed = saved
    inputs = frames.shape[1]
    rows = D // count
    up_grad, down_grad = up_grad.reshape(4, count, rows, D), down_grad.reshape(count, 4, rows, D)
    return pl.pallas_call(
        functools.partial(attend_back_kernel, streams, depth),
        grid=(streams,),
        out_shape=[
            jax.ShapeDtypeStruct((streams, SEG, D), f32),
            jax.ShapeDtypeStruct((4, D, D), bf16),
            jax.ShapeDtypeStruct((8, D), f32),
            jax.ShapeDtypeStruct((inputs, D), f32),
            jax.ShapeDtypeStruct((4, rows, D), bf16),
        ],
        in_specs=[
            pl.BlockSpec(memory_space=pltpu.SMEM),
            stream_spec((SEG, D)),
            stream_spec((SEG, D)),
            stream_spec((SEG, D)),
            stream_spec((2 * SEG, D)),
            stream_spec((SEG, D)),
            stream_spec((2 * SEG, D)),
            stream_spec((2 * SEG, D)),
            stream_spec((HEADS, SEG)),
            stream_spec((SEG, D)),
            layer_spec(attn.shape[1:], depth),
            layer_spec(vectors.shape[1:], depth),
            stream_spec((inputs, SEG)),
            pl.BlockSpec(memory_space=pl.ANY),
            pl.BlockSpec(memory_space=pl.ANY),
        ],
        out_specs=[
            stream_spec((SEG, D)),
            whole_spec((4, D, D)),
            whole_spec((8, D)),
            whole_spec((inputs, D)),
            whole_spec((4, rows, D)),
        ],
        scratch_shapes=[
            pltpu.VMEM((4, D, D), f32),
            pltpu.VMEM((SEG, D), bf16),
            pltpu.VMEM((SEG, D), bf16),
            pltpu.VMEM((2 * SEG, D), bf16),
            pltpu.VMEM((2 * SEG, D), bf16),
            pltpu.VMEM((2 * SEG, 2 * SEG), bf16),
            pltpu.VMEM((HEADS, SEG), f32),
        ]
        + carry_scratch("feed", rows, count, dp_count),
        compiler_params=pltpu.CompilerParams(
            collective_id=4 + depth, has_side_effects=True, vmem_limit_bytes=VMEM_LIMIT
        ),
        cost_estimate=pl.CostEstimate(flops=3 * 10**10, bytes_accessed=2 * 10**7, transcendentals=10**7),
        name="attend_back",
    )(bias, dafter, x, memory, keyin, q, k, v, lse, mixed, attn, vectors, frames, up_grad, down_grad)


def from_behind(value, axis, steps):
    count = lax.axis_size(axis)
    leading, last = (max(0, -steps), min(count, count - steps))
    return lax.ppermute(value, axis, [(source, source + steps) for source in range(leading, last)])


def adamw(weight, moment, second, grad, rate, decay):
    moment = 0.5 * moment + 0.5 * grad
    second = 0.99 * second + 0.01 * grad * grad
    fixed_moment = moment / (1.0 - 0.5**STEP)
    fixed_second = second / (1.0 - 0.99**STEP)
    weight = weight * (1.0 - rate * decay) - rate * fixed_moment / (jnp.sqrt(fixed_second) + 1e-08)
    return (weight, moment, second)


GROUPS = 4
UNITS = 6
SMALL = 128


def peers():
    count = {"seg": lax.axis_size("seg"), "dp": lax.axis_size("dp")}
    seg, dp = lax.axis_index("seg"), lax.axis_index("dp")
    core, x, y = seg % 2, dp % 2, (dp // 2) % 2
    across_core = {"seg": seg + 1 - 2 * core}
    across_x = {"dp": dp + 1 - 2 * x}
    across_y = {"dp": dp + 2 - 4 * y}
    across_both = {"dp": dp + 3 - 2 * x - 4 * y}
    far = []
    step = GROUPS
    while step < count["dp"]:
        far.append({"dp": dp + step - 2 * step * ((dp // step) % 2)})
        step *= 2
    return seg, dp, core, x, y, across_core, (across_x, across_y, across_both), far


def others(seg, count):
    return [lax.rem(seg + step, count) for step in range(1, count)]


def hail(targets):
    barrier = pltpu.get_barrier_semaphore()
    for target in targets:
        pl.semaphore_signal(barrier, inc=1, device_id=target, device_id_type=pl.DeviceIdType.MESH)


def meet(targets):
    pl.semaphore_wait(pltpu.get_barrier_semaphore(), len(targets))


def greet(seg, count, near, far):
    targets = [{"seg": other} for other in others(seg, count)] + list(near) + list(far)
    hail(targets)
    meet(targets)


def remote(source, target, send, recv, device):
    return pltpu.make_async_remote_copy(
        src_ref=source,
        dst_ref=target,
        send_sem=send,
        recv_sem=recv,
        device_id=device,
        device_id_type=pl.DeviceIdType.MESH,
    )


def wait_bytes(ref, sem):
    pltpu.make_async_copy(ref, ref, sem).wait()


def plus(left, right):
    return (left.astype(f32) + right.astype(f32)).astype(left.dtype)


def owners(count):
    attn, feed = count // 4 - 1, count // 4
    return (
        (0, 1, 2 * attn, 0),
        (1, 1, 2 * attn + 1, 0),
        (2, 2, 2 * feed, 0),
        (4, 2, 2 * feed + 1, 2),
    )


def lowest_bit(mask, planes):
    bit = 1
    while bit < planes and not mask & bit:
        bit *= 2
    return bit


class Carry:
    def __init__(self, refs, sems):
        self.mine, self.got0, self.got1, self.got2, self.got3, self.goth = refs
        (
            self.load,
            self.send0,
            self.recv0,
            self.send1,
            self.recv1,
            self.send2,
            self.recv2,
            self.send3,
            self.recv3,
            self.sendh,
            self.recvh,
        ) = sems
        self.seg, self.dp, self.core, self.x, self.y, self.across_core, near, self.far = peers()
        self.across_x, self.across_y, _ = near
        self.planes = self.mine.shape[0]
        self.plane = self.seg // 2
        self.targets = [self.across_core, self.across_x, self.across_y] + self.far
        bit = 1
        while bit < self.planes:
            self.targets.append({"seg": 2 * self.toggled(bit) + self.core})
            bit *= 2

        self.order = list(reversed(range(self.planes)))

    def toggled(self, mask):
        place, bit = self.plane, 1
        while bit <= mask:
            if mask & bit:
                place = place + bit - 2 * bit * ((self.plane // bit) % 2)
            bit *= 2
        return place

    def load_all(self):
        for step in range(self.planes):
            for source, place in self.pieces(2 * self.toggled(self.order[step]) + self.core):
                pltpu.make_async_copy(source, self.mine.at[(step,) + place], self.load.at[step]).start()

    def send_all(self):
        for step in range(self.planes):
            for source, place in self.pieces(2 * self.toggled(self.order[step]) + 1 - self.core):
                remote(
                    source, self.got0.at[(step,) + place], self.send0.at[step], self.recv0.at[step], self.across_core
                ).start()

    def begin(self, step):
        wait_bytes(self.mine.at[step], self.load.at[step])
        wait_bytes(self.got0.at[step], self.recv0.at[step])
        for place in range(2):
            self.mine[step, place] = plus(self.mine[step, place], self.got0[step, place])
        for copy in self.first(step):
            copy.start()

    def across(self, place, step):
        return remote(
            self.held(step),
            self.goth.at[place, step],
            self.sendh.at[place, step],
            self.recvh.at[place, step],
            self.far[place],
        )

    def third(self, step):
        mask = self.order[step]
        return remote(
            self.held(step),
            self.got3.at[mask],
            self.send3.at[step],
            self.recv3.at[mask],
            {"seg": 2 * self.toggled(lowest_bit(mask, self.planes)) + self.core},
        )

    def onward(self, step):
        held = self.held(step)
        for place in range(len(self.far)):
            copy = self.across(place, step)
            copy.start()
            copy.wait()
            held[...] = plus(held[...], self.goth[place, step])
        mask = self.order[step]
        if mask:
            self.gathered(mask, held)
            self.third(step).start()

    def gathered(self, mask, held):
        value, bit = held[...].astype(f32), 1
        while bit < lowest_bit(mask, self.planes):
            wait_bytes(self.got3.at[mask + bit], self.recv3.at[mask + bit])
            value = value + self.got3[mask + bit].astype(f32)
            bit *= 2
        held[...] = value.astype(held.dtype)

    def total(self):
        held = self.held(self.planes - 1)
        self.gathered(0, held)
        return held[...]

    def run(self, acts):
        for kind, step in acts:
            if step < self.planes:
                {"b": self.begin, "m": self.middle, "e": self.end}[kind](step)

    def actions(self, time, slack):
        planes = self.planes
        started = range(2) if time == 0 else range(time + 1, time + 2)
        for step in started:
            if step < planes:
                self.begin(step)
        if 0 <= time - slack < planes:
            self.middle(time - slack)
        if 0 <= time - slack - 2 < planes:
            self.end(time - slack - 2)

    def tick(self, time, last, slack):
        for place in range(last):

            @pl.when(time == place)
            def _():
                self.actions(place, slack)

    def rest(self, first, slack):
        for time in range(first, self.planes + slack + 2):
            self.actions(time, slack)


class AttnCarry(Carry):
    def __init__(self, source, refs, sems):
        super().__init__(refs, sems)
        self.source = source

    def pieces(self, row):
        return ((self.source.at[:, :, row], ()),)

    def held(self, step):
        return self.mine.at[step, self.y, self.x]

    def first(self, step):
        half = self.mine.shape[3] // 2
        return (
            remote(
                self.mine.at[step, :, 1 - self.x, 0:half],
                self.got1.at[step, 0],
                self.send1.at[step, 0],
                self.recv1.at[step, 0],
                self.across_x,
            ),
            remote(
                self.mine.at[step, 1 - self.y, :, half:],
                self.got1.at[step, 1],
                self.send1.at[step, 1],
                self.recv1.at[step, 1],
                self.across_y,
            ),
        )

    def second(self, step):
        half = self.mine.shape[3] // 2
        return (
            remote(
                self.mine.at[step, 1 - self.y, self.x, 0:half],
                self.got2.at[step, 0],
                self.send2.at[step, 0],
                self.recv2.at[step, 0],
                self.across_y,
            ),
            remote(
                self.mine.at[step, self.y, 1 - self.x, half:],
                self.got2.at[step, 1],
                self.send2.at[step, 1],
                self.recv2.at[step, 1],
                self.across_x,
            ),
        )

    def middle(self, step):
        mine, half = self.mine, self.mine.shape[3] // 2
        for copy in self.first(step):
            copy.wait_recv()
        for place in range(2):
            mine[step, place, self.x, 0:half] = plus(mine[step, place, self.x, 0:half], self.got1[step, 0, place])
            mine[step, self.y, place, half:] = plus(mine[step, self.y, place, half:], self.got1[step, 1, place])
        for copy in self.second(step):
            copy.start()

    def end(self, step):
        mine, half = self.mine, self.mine.shape[3] // 2
        for copy in self.second(step):
            copy.wait_recv()
        mine[step, self.y, self.x, 0:half] = plus(mine[step, self.y, self.x, 0:half], self.got2[step, 0])
        mine[step, self.y, self.x, half:] = plus(mine[step, self.y, self.x, half:], self.got2[step, 1])
        self.onward(step)

    def finish(self, out_ref):
        out_ref[...] = self.total().astype(out_ref.dtype)
        self.drain()

    def drain(self):
        for step in range(self.planes):
            wait_bytes(self.mine.at[step], self.send0.at[step])
            for copy in self.first(step) + self.second(step):
                copy.wait_send()
            if step < self.planes - 1:
                self.third(step).wait_send()


class FeedCarry(Carry):
    def __init__(self, depth, up, down, refs, sems):
        super().__init__(refs[:CARRY_REFS], sems[:CARRY_SEMS])
        self.sums, self.got4 = refs[CARRY_REFS:]
        self.send4, self.recv4 = sems[CARRY_SEMS:]
        self.up, self.down = up, down
        self.owner = (self.x == self.y) if depth == 1 else (self.x != self.y)
        self.keep = self.x if depth == 1 else 1 - self.x

    def pieces(self, row):
        return ((self.up.at[:, row], (0,)), (self.down.at[row], (1,)))

    def held(self, step):
        return self.sums.at[step]

    def first(self, step):
        return (
            remote(
                self.mine.at[step, 1 - self.keep, 0:2],
                self.got1.at[step, 0],
                self.send1.at[step, 0],
                self.recv1.at[step, 0],
                self.across_x,
            ),
            remote(
                self.mine.at[step, 1 - self.y, 2:4],
                self.got1.at[step, 1],
                self.send1.at[step, 1],
                self.recv1.at[step, 1],
                self.across_y,
            ),
        )

    def second(self, step):
        return (
            remote(
                self.mine.at[step, self.keep, 1 - self.y],
                self.got2.at[step, 0],
                self.send2.at[step, 0],
                self.recv2.at[step, 0],
                self.across_y,
            ),
            remote(
                self.mine.at[step, self.y, 3 - self.x],
                self.got2.at[step, 1],
                self.send2.at[step, 1],
                self.recv2.at[step, 1],
                self.across_x,
            ),
        )

    def middle(self, step):
        for copy in self.first(step):
            copy.wait_recv()
        self.mine[step, self.keep, 0:2] = plus(self.mine[step, self.keep, 0:2], self.got1[step, 0])
        self.mine[step, self.y, 2:4] = plus(self.mine[step, self.y, 2:4], self.got1[step, 1])
        for copy in self.second(step):
            copy.start()

    def end(self, step):
        for copy in self.second(step):
            copy.wait_recv()
        self.sums[step, 0] = plus(self.mine[step, self.keep, self.y], self.got2[step, 0])
        self.sums[step, 1] = plus(self.mine[step, self.y, 2 + self.x], self.got2[step, 1])
        self.onward(step)

    def last(self):
        step = self.planes - 1
        return (
            remote(self.sums.at[step, 0], self.got4.at[0], self.send4.at[0], self.recv4.at[0], self.across_y),
            remote(self.sums.at[step, 1], self.got4.at[1], self.send4.at[1], self.recv4.at[1], self.across_x),
        )

    def finish(self, out_ref):
        value = self.total()

        @pl.when(self.owner)
        def _():
            for place in range(2):
                wait_bytes(self.got4.at[place], self.recv4.at[place])
            out_ref[self.y] = value[0]
            out_ref[1 - self.y] = self.got4[0]
            out_ref[2 + self.x] = value[1]
            out_ref[3 - self.x] = self.got4[1]

        @pl.when(jnp.logical_not(self.owner))
        def _():
            for copy in self.last():
                copy.start()
            out_ref[...] = jnp.zeros_like(out_ref)
            for copy in self.last():
                copy.wait_send()

        for step in range(self.planes):
            wait_bytes(self.mine.at[step], self.send0.at[step])
            for copy in self.first(step) + self.second(step):
                copy.wait_send()
            if step < self.planes - 1:
                self.third(step).wait_send()


CARRY_REFS = 6
CARRY_SEMS = 11


def carry_scratch(kind, rows, count, dp_count, dtype=bf16):
    planes = count // 2
    far = max(1, dp_count.bit_length() - 3)
    dma = pltpu.SemaphoreType.DMA
    half = rows // 2
    if kind == "attn":
        shapes = (
            (planes, 2, 2, rows),
            (planes, 2, 2, rows),
            (planes, 2, 2, half),
            (planes, 2, half),
            (planes, rows),
            (far, planes, rows),
        )
    else:
        shapes = (
            (planes, 2, 4, rows),
            (planes, 2, 4, rows),
            (planes, 2, 2, rows),
            (planes, 2, rows),
            (planes, 2, rows),
            (far, planes, 2, rows),
            (planes, 2, rows),
            (2, rows),
        )
    pair = (planes, 2)
    one = (planes,)
    sems = (one, one, one, pair, pair, pair, pair, one, one, (far, planes), (far, planes))
    if kind == "feed":
        sems = sems + ((2,), (2,))
    return [pltpu.VMEM(shape + (D,), dtype) for shape in shapes] + [dma(shape) for shape in sems]


def reduce_kernel(
    count,
    attn_grad_ref,
    attn_done_ref,
    feed_low_ref,
    feed_high_ref,
    dout_ref,
    din_ref,
    vec0_ref,
    vec1_ref,
    vec2_ref,
    vec3_ref,
    outer_ref,
    whole_ref,
    own_ref,
    small_out,
    square_out,
    small_ref,
    small_core,
    small_s,
    small_got,
    sq_seg,
    sq_dp,
    small_send,
    small_recv,
    whole_send,
    whole_recv,
    half_sem,
    sq_send,
    sq_recv,
    sqd_send,
    sqd_recv,
    *refs,
):
    carry = AttnCarry(attn_grad_ref, refs[:CARRY_REFS], refs[CARRY_REFS:])
    seg, dp, core, x, y, across_core, near, far = peers()
    across_x, across_y, across_both = near
    planes = count // 2
    plane = seg // 2
    group = 2 * y + x
    targets = [{"seg": other} for other in others(seg, count)] + list(near) + list(far)
    hail(targets)
    carry.load_all()
    own_ref[1] = attn_done_ref[...]

    @pl.when(x == y)
    def _():
        own_ref[2:6] = feed_high_ref[...]

    @pl.when(x != y)
    def _():
        own_ref[2:6] = feed_low_ref[...]

    inputs = din_ref.shape[0]
    small_ref[0:inputs, :] = din_ref[...]
    for place, ref in enumerate((vec0_ref, vec1_ref, vec2_ref, vec3_ref, outer_ref)):
        small_ref[inputs + 8 * place : inputs + 8 * place + 8, :] = ref[...]
    small_ref[inputs + 40 :, :] = jnp.zeros((SMALL - inputs - 40, D), f32)
    meet(targets)
    def small_steps():
        copy = remote(small_ref, small_core, small_send.at[0], small_recv.at[0], across_core)
        copy.start()
        yield
        copy.wait()
        small_s[...] = small_ref[...] + small_core[...]
        half = pl.ds(pl.multiple_of(core * (SMALL // 2), 8), SMALL // 2)
        targets = [across_x, across_y] + far
        step = 1
        while step < planes:
            targets.append({"seg": seg + 2 * step - 4 * step * ((plane // step) % 2)})
            step *= 2
        for place, target in enumerate(targets):
            copy = remote(
                small_s.at[half],
                small_got.at[place],
                small_send.at[place + 1],
                small_recv.at[place + 1],
                target,
            )
            copy.start()
            yield
            copy.wait()
            small_s[half, :] += small_got[place]
        small_out[half, :] = small_s[half, :]
        last = len(targets) + 1
        copy = remote(small_out.at[half], small_out.at[half], small_send.at[last], small_recv.at[last], across_core)
        copy.start()
        yield
        copy.wait()

    small_run = small_steps()
    next(small_run)
    carry.send_all()
    roles = owners(count)

    def gift(place):
        first, width, owner, spot = roles[place]
        return remote(
            own_ref.at[first : first + width],
            whole_ref.at[seg, spot : spot + width],
            whole_send.at[place],
            whole_recv.at[seg],
            {"seg": owner},
        )

    def give(place):
        first, width, owner, spot = roles[place]

        @pl.when(seg != owner)
        def _():
            gift(place).start()

        @pl.when(seg == owner)
        def _():
            whole_ref[seg, spot : spot + width] = own_ref[first : first + width]

    for place in (2, 3, 1):
        give(place)
    acts = [
        [("b", 0), ("b", 1)],
        [("b", step) for step in range(2, planes)],
        [("m", 0), ("m", 1)],
        [("m", step) for step in range(2, planes)] + [("e", 0)],
    ] + [[("e", step)] for step in range(1, planes)]
    next(small_run)
    for part in acts:
        carry.run(part)
        next(small_run, None)
    own_ref[0] = carry.total()
    give(0)
    for _ in small_run:
        pass
    shard = dout_ref[...].astype(f32)
    square = jnp.sum(jnp.sum(shard * shard, 0, keepdims=True), 1, keepdims=True)
    for unit in range(UNITS):
        value = own_ref[unit].astype(f32)
        square = square + jnp.sum(jnp.sum(value * value, 0, keepdims=True), 1, keepdims=True)
    sq_seg[seg] = jnp.broadcast_to(square, (8, 128))
    for step, other in enumerate(others(seg, count)):
        remote(sq_seg.at[seg], sq_seg.at[seg], sq_send.at[step], sq_recv.at[seg], {"seg": other}).start()

    def halves_copy(spot):
        span = slice(spot, spot + 2)
        return remote(whole_ref.at[:, span], whole_ref.at[:, span], half_sem.at[0], half_sem.at[1], across_core)

    for place, (first, width, owner, spot) in enumerate(roles):
        if width == 2:

            @pl.when(seg == owner)
            def _():
                for other in others(seg, count):
                    wait_bytes(whole_ref.at[other, spot : spot + width], whole_recv.at[other])
                halves_copy(spot).start()

    for other in others(seg, count):
        wait_bytes(sq_seg.at[other], sq_recv.at[other])
    sq_dp[group] = jnp.sum(sq_seg[...], 0)
    for place, target in enumerate(near):
        remote(sq_dp.at[group], sq_dp.at[group], sqd_send.at[place], sqd_recv.at[place], target).start()
    sums = small_out[...]
    is_loss = lax.broadcasted_iota(jnp.int32, (SMALL, D), 0) == inputs + 37
    sums = jnp.where(is_loss, 0.0, sums)
    small_square = jnp.sum(jnp.sum(sums * sums, 0, keepdims=True), 1, keepdims=True)
    for place, target in enumerate(near):
        remote(sq_dp.at[group], sq_dp.at[group], sqd_send.at[place], sqd_recv.at[place], target).wait()
    square_out[...] = jnp.sum(sq_dp[...], 0) + jnp.broadcast_to(small_square, (8, 128))

    for place, (first, width, owner, spot) in enumerate(roles):

        @pl.when(seg == owner)
        def _():
            if width == 2:
                halves_copy(spot).wait()
            else:
                for other in others(seg, count):
                    wait_bytes(whole_ref.at[other, spot : spot + width], whole_recv.at[other])

    carry.drain()
    for place, (first, width, owner, spot) in enumerate(roles):

        @pl.when(seg != owner)
        def _():
            gift(place).wait_send()

    for step in range(count - 1):
        wait_bytes(sq_seg.at[0], sq_send.at[step])


def reduce_grads(count, dp_count, attn, done, feed_low, feed_high, dout, pieces):
    rows = D // count
    planes = count // 2
    stages = 2 + planes.bit_length() + max(0, dp_count.bit_length() - 3)
    dma = pltpu.SemaphoreType.DMA
    vmem = pl.BlockSpec(memory_space=pltpu.VMEM)
    return pl.pallas_call(
        functools.partial(reduce_kernel, count),
        out_shape=[
            jax.ShapeDtypeStruct((count, 4, rows, D), bf16),
            jax.ShapeDtypeStruct((UNITS, rows, D), bf16),
            jax.ShapeDtypeStruct((SMALL, D), f32),
            jax.ShapeDtypeStruct((8, 128), f32),
        ],
        in_specs=[pl.BlockSpec(memory_space=pl.ANY)] + [vmem] * 10,
        out_specs=[vmem] * 4,
        scratch_shapes=[
            pltpu.VMEM((SMALL, D), f32),
            pltpu.VMEM((SMALL, D), f32),
            pltpu.VMEM((SMALL, D), f32),
            pltpu.VMEM((stages, SMALL // 2, D), f32),
            pltpu.VMEM((count, 8, 128), f32),
            pltpu.VMEM((GROUPS, 8, 128), f32),
            dma((stages + 2,)),
            dma((stages + 2,)),
            dma((4,)),
            dma((count,)),
            dma((2,)),
            dma((count,)),
            dma((count,)),
            dma((3,)),
            dma((3,)),
        ]
        + carry_scratch("attn", rows, count, dp_count),
        compiler_params=pltpu.CompilerParams(
            collective_id=1, has_side_effects=True, vmem_limit_bytes=VMEM_LIMIT
        ),
        cost_estimate=pl.CostEstimate(flops=10**8, bytes_accessed=10**8, transcendentals=0),
        name="reduce_grads",
    )(attn.reshape(2, 2, count, rows, D), done, feed_low, feed_high, dout, *pieces)


def halves(value):
    high = value.astype(bf16)
    return high, (value - high.astype(f32)).astype(bf16)


def times(left, right):
    (left_high, left_low), (right_high, right_low) = left, right
    return dot_nn(
        jnp.concatenate([left_high, left_high, left_low], 1),
        jnp.concatenate([right_high, right_low, right_high], 0),
    )


def mirrored(first, second, third):
    return jnp.concatenate(
        [
            jnp.concatenate([first, second], 1),
            jnp.concatenate([jnp.transpose(second), third], 1),
        ],
        0,
    )


def times_even(left, right):
    (left_high, left_low), (right_high, right_low) = left, right
    wide = jnp.concatenate([left_high, left_high, left_low], 1)
    tall = jnp.concatenate([right_high, right_low, right_high], 0)
    return mirrored(
        dot_nn(wide[:HALF], tall[:, :HALF]),
        dot_nn(wide[:HALF], tall[:, HALF:]),
        dot_nn(wide[HALF:], tall[:, HALF:]),
    )


def gram_of(both):
    high, low = both
    wide = jnp.concatenate([high, high, low], 1)
    tall = jnp.concatenate([high, low, high], 1)
    return mirrored(
        dot_nt(wide[:HALF], tall[:HALF]),
        dot_nt(wide[:HALF], tall[HALF:]),
        dot_nt(wide[HALF:], tall[HALF:]),
    )


def clip_of(norm):
    return jnp.minimum(1.0, 0.25 / (norm + 1e-06))


def muon_kernel(
    count,
    square_ref,
    whole_ref,
    mom_ref,
    own_ref,
    update_ref,
    every_ref,
    norm_ref,
    made_ref,
    x_s,
    q_s,
    gram_s,
    high_s,
    low_s,
    send,
    recv,
    on_send,
    on_recv,
    own_send,
    own_recv,
):
    seg, dp, core, x, y, across_core, near, far = peers()
    group = 2 * y + x
    plane = seg // 2
    targets = [{"seg": other} for other in others(seg, count)] + list(near)
    hail(targets)
    is_down = group >= 2
    norm = jnp.sqrt(square_ref[0:1, 0:1])
    norm_ref[...] = jnp.broadcast_to(norm, norm_ref.shape)
    clip = clip_of(norm)
    eye = (
        lax.broadcasted_iota(jnp.int32, (D, D), 0) == lax.broadcasted_iota(jnp.int32, (D, D), 1)
    ).astype(f32)
    rows = whole_ref.shape[2]
    makers = [attn for _, _, attn, _ in owners(count)]
    units = [makers[0], makers[1], makers[2], makers[2], makers[3], makers[3]]

    def own_rows(side):
        return remote(own_ref, every_ref.at[group], own_send.at[side], own_recv.at[side], near[side])

    def gift(unit, slot, other):
        return remote(
            made_ref.at[other, slot],
            update_ref.at[group, unit],
            send.at[slot, other],
            recv.at[unit],
            {"seg": other},
        )

    def give(unit, slot):
        for other in others(seg, count):
            gift(unit, slot, other).start()
        update_ref[group, unit] = made_ref[seg, slot]

    def onward(unit, side):
        block = update_ref.at[group, unit]
        return remote(block, block, on_send.at[side, unit], on_recv.at[side, unit], near[side])

    meet(targets)
    for side in range(3):
        own_rows(side).start()
    every_ref[group] = own_ref[...]

    @pl.when(plane == count // 4 - 1)
    def _():
        start = (0.5 * mom_ref[:, core].astype(f32)).reshape(D, D)
        start = start + clip * whole_ref[:, 0].astype(f32).reshape(D, D)
        size = jnp.sum(jnp.sum(start * start, 0, keepdims=True), 1, keepdims=True)
        x_s[...] = start / (jnp.sqrt(size) + 1e-07)

        def sweep(_, carry):
            value = x_s[...]
            both = halves(value)
            gram = gram_of(both)
            gram_both = halves(gram)
            poly = -4.775 * gram + 2.0315 * times_even(gram_both, gram_both)
            x_s[...] = 3.4445 * value + times(halves(poly), both)
            return carry

        lax.fori_loop(0, 5, sweep, 0)
        made_ref[:, 0] = x_s[...].astype(bf16).reshape(count, rows, D)
        for unit in range(2):

            @pl.when(core == unit)
            def _():
                give(unit, 0)

    @pl.when(plane == count // 4)
    def _():
        gram_s[...] = jnp.zeros_like(gram_s)

        def gather(tile, size):
            value = (0.5 * mom_ref[:, 2 + tile].astype(f32)).reshape(D, D)
            value = value + clip * whole_ref[:, tile].astype(f32).reshape(D, D)
            high, low = halves(value)
            high_s[tile] = high
            low_s[tile] = low

            @pl.when(is_down)
            def _():
                high_s[tile] = jnp.transpose(high_s[tile])
                low_s[tile] = jnp.transpose(low_s[tile])

            both = high_s[tile], low_s[tile]
            gram_s[...] += gram_of(both)
            return size + jnp.sum(jnp.sum(value * value, 0, keepdims=True), 1, keepdims=True)

        size = lax.fori_loop(0, 4, gather, jnp.zeros((1, 1), f32))
        scale = 1.0 / (jnp.sqrt(size) + 1e-07)
        gram_s[...] = gram_s[...] * (scale * scale)

        def poly_of(gram, gram_both):
            return 3.4445 * eye - 4.775 * gram + 2.0315 * times_even(gram_both, gram_both)

        def advance(gram_both, poly_both):
            gram_s[...] = times_even(halves(times_even(gram_both, poly_both)), poly_both)

        gram = gram_s[...]
        gram_both = halves(gram)
        poly = poly_of(gram, gram_both)
        q_s[...] = poly
        advance(gram_both, halves(poly))

        def sweep(_, carry):
            gram = gram_s[...]
            gram_both = halves(gram)
            poly_both = halves(poly_of(gram, gram_both))
            q_s[...] = times_even(halves(q_s[...]), poly_both)
            advance(gram_both, poly_both)
            return carry

        lax.fori_loop(0, 3, sweep, 0)
        gram = gram_s[...]
        last = times_even(halves(q_s[...]), halves(poly_of(gram, halves(gram)))) * scale
        last_both = halves(last)
        for slot in range(2):
            tile = 2 * core + slot
            x_s[...] = times(last_both, (high_s[tile], low_s[tile]))

            @pl.when(is_down)
            def _():
                x_s[...] = jnp.transpose(x_s[...])

            made_ref[:, slot] = x_s[...].astype(bf16).reshape(count, rows, D)
            for half in range(2):

                @pl.when(core == half)
                def _():
                    give(2 + 2 * half + slot, slot)

    for unit in (0, 1, 2, 4, 3, 5):

        @pl.when(seg != units[unit])
        def _():
            wait_bytes(update_ref.at[group, unit], recv.at[unit])

        for side in range(3):
            onward(unit, side).start()
    for side in range(3):
        own_rows(side).wait()
    for unit in range(UNITS):
        for side in range(3):
            onward(unit, side).wait()

        @pl.when(seg == units[unit])
        def _():
            slot = 0 if unit < 2 else unit % 2
            for other in others(seg, count):
                gift(unit, slot, other).wait_send()


def muon(count, squares, whole, momenta, own):
    rows = whole.shape[2]
    dma = pltpu.SemaphoreType.DMA
    vmem = pl.BlockSpec(memory_space=pltpu.VMEM)
    blocks = jax.ShapeDtypeStruct((GROUPS, UNITS, rows, D), bf16)
    return pl.pallas_call(
        functools.partial(muon_kernel, count),
        out_shape=[blocks, blocks, jax.ShapeDtypeStruct((8, 128), f32)],
        in_specs=[vmem] * 4,
        out_specs=[vmem] * 3,
        scratch_shapes=[
            pltpu.VMEM((count, 2, rows, D), bf16),
            pltpu.VMEM((D, D), f32),
            pltpu.VMEM((D, D), f32),
            pltpu.VMEM((D, D), f32),
            pltpu.VMEM((4, D, D), bf16),
            pltpu.VMEM((4, D, D), bf16),
            dma((2, count)),
            dma((UNITS,)),
            dma((3, UNITS)),
            dma((3, UNITS)),
            dma((3,)),
            dma((3,)),
        ],
        compiler_params=pltpu.CompilerParams(
            collective_id=2, has_side_effects=True, vmem_limit_bytes=VMEM_LIMIT
        ),
        cost_estimate=pl.CostEstimate(flops=2 * 10**10, bytes_accessed=4 * 10**7, transcendentals=0),
        name="muon",
    )(squares, whole, momenta, own)


def embed_kernel(
    count,
    frames_ref,
    mask_ref,
    in_ref,
    outer_ref,
    attn_mom_ref,
    up_mom_ref,
    down_mom_ref,
    x_ref,
    mem_ref,
    total_ref,
    owned_ref,
    got_s,
    count_s,
    mom_s,
    mom_sem,
    frame_send,
    frame_recv,
    count_send,
    count_recv,
):
    seg = lax.axis_index("seg")
    after, before = lax.rem(seg + 1, count), lax.rem(seg + count - 1, count)
    streams = frames_ref.shape[0]
    group = lax.rem(lax.axis_index("dp"), GROUPS)
    for depth in range(LAYERS):
        pltpu.make_async_copy(attn_mom_ref.at[depth, group], mom_s.at[depth], mom_sem.at[0]).start()

        @pl.when(group == FEED_UP[depth])
        def _():
            for tile in range(4):
                source = up_mom_ref.at[depth, :, pl.ds(tile * TILE, TILE)]
                pltpu.make_async_copy(source, mom_s.at[2 + tile], mom_sem.at[0]).start()

        @pl.when(group == FEED_DOWN[depth])
        def _():
            pltpu.make_async_copy(down_mom_ref.at[depth], mom_s.at[2:6], mom_sem.at[0]).start()

    tally = jnp.sum(mask_ref[...].astype(f32), 1, keepdims=True)
    count_s[seg] = jnp.broadcast_to(
        jnp.concatenate([tally, jnp.zeros((8 - streams, 1), f32)], 0), (8, 128)
    )
    greet(seg, count, (), ())
    frame_copy = remote(frames_ref, got_s, frame_send.at[0], frame_recv.at[0], {"seg": after})
    frame_copy.start()
    for step, other in enumerate(others(seg, count)):
        remote(count_s.at[seg], count_s.at[seg], count_send.at[step], count_recv.at[seg], {"seg": other}).start()
    weight, shift = in_ref[...], outer_ref[0:1, :]
    for stream in range(streams):
        x_ref[stream] = dot_nn(jnp.transpose(frames_ref[stream]), weight) + shift
    wait_bytes(mom_s, mom_sem.at[0])
    owned_ref[...] = mom_s[...].astype(bf16)
    frame_copy.wait()
    for stream in range(streams):
        mem_ref[stream] = (dot_nn(jnp.transpose(got_s[stream]), weight) + shift).astype(bf16)
    for other in others(seg, count):
        wait_bytes(count_s.at[other], count_recv.at[other])
    total_ref[...] = jnp.sum(count_s[...], 0)
    for step in range(count - 1):
        wait_bytes(count_s.at[0], count_send.at[step])


def embed(count, frames, mask, in_weight, outer_vectors, attn_mom, up_mom, down_mom):
    streams = frames.shape[0]
    rows = D // count
    dma = pltpu.SemaphoreType.DMA
    return pl.pallas_call(
        functools.partial(embed_kernel, count),
        out_shape=[
            jax.ShapeDtypeStruct((streams, SEG, D), f32),
            jax.ShapeDtypeStruct((streams, SEG, D), bf16),
            jax.ShapeDtypeStruct((8, 128), f32),
            jax.ShapeDtypeStruct((UNITS, rows, D), bf16),
        ],
        in_specs=[pl.BlockSpec(memory_space=pltpu.VMEM)] * 4 + [pl.BlockSpec(memory_space=pl.ANY)] * 3,
        out_specs=[pl.BlockSpec(memory_space=pltpu.VMEM)] * 4,
        scratch_shapes=[
            pltpu.VMEM(frames.shape, bf16),
            pltpu.VMEM((count, 8, 128), f32),
            pltpu.VMEM((UNITS, rows, D), f32),
            dma((1,)),
            dma((1,)),
            dma((1,)),
            dma((count,)),
            dma((count,)),
        ],
        compiler_params=pltpu.CompilerParams(
            collective_id=3, has_side_effects=True, vmem_limit_bytes=VMEM_LIMIT
        ),
        cost_estimate=pl.CostEstimate(flops=2 * 10**8, bytes_accessed=4 * 10**6, transcendentals=0),
        name="embed",
    )(frames, mask, in_weight, outer_vectors, attn_mom, up_mom, down_mom.reshape(LAYERS, 4, rows, D))


FEED_UP = (1, 0)
FEED_DOWN = (2, 3)
KEEP = 1.0 - 0.3 * 0.01


def finish_kernel(norm_ref, every_ref, update_ref, dout_ref, small_ref, *refs):
    (
        attn_ref,
        attn_mom_ref,
        up_ref,
        up_mom_ref,
        down_ref,
        down_mom_ref,
        out_ref,
        out_mom_ref,
        out_sec_ref,
        in_ref,
        in_mom_ref,
        in_sec_ref,
        vec_ref,
        vec_mom_ref,
        vec_sec_ref,
        outer_ref,
        outer_mom_ref,
        outer_sec_ref,
        attn_new,
        attn_mom_new,
        attn_copy_new,
        up_new,
        up_mom_new,
        up_copy_new,
        down_new,
        down_mom_new,
        down_copy_new,
        out_new,
        out_mom_new,
        out_sec_new,
        out_copy_new,
        in_new,
        in_mom_new,
        in_sec_new,
        in_copy_new,
        vec_new,
        vec_mom_new,
        vec_sec_new,
        outer_new,
        outer_mom_new,
        outer_sec_new,
        loss_new,
        norm_new,
    ) = refs
    clip = clip_of(norm_ref[0:1, 0:1])

    def muon_step(weight, momentum, grad, update, scale):
        weight = weight * KEEP - (0.3 * scale) * update.astype(f32)
        return weight, 0.5 * momentum + clip * grad.astype(f32)

    up_scale, down_scale = max(1.0, FF / D) ** 0.5, max(1.0, D / FF) ** 0.5
    for depth in range(LAYERS):
        for kind in range(4):
            weight, momentum = muon_step(
                attn_ref[depth, kind],
                attn_mom_ref[depth, kind],
                every_ref[kind, depth],
                update_ref[kind, depth],
                1.0,
            )
            attn_new[depth, kind] = weight
            attn_mom_new[depth, kind] = momentum
            attn_copy_new[depth, kind] = weight.astype(bf16)
            columns = slice(kind * TILE, (kind + 1) * TILE)
            weight, momentum = muon_step(
                up_ref[depth, :, columns],
                up_mom_ref[depth, :, columns],
                every_ref[FEED_UP[depth], 2 + kind],
                update_ref[FEED_UP[depth], 2 + kind],
                up_scale,
            )
            up_new[depth, :, columns] = weight
            up_mom_new[depth, :, columns] = momentum
            up_copy_new[depth, :, columns] = weight.astype(bf16)
            weight, momentum = muon_step(
                down_ref[depth, kind],
                down_mom_ref[depth, kind],
                every_ref[FEED_DOWN[depth], 2 + kind],
                update_ref[FEED_DOWN[depth], 2 + kind],
                down_scale,
            )
            down_new[depth, kind] = weight
            down_mom_new[depth, kind] = momentum
            down_copy_new[depth, kind] = weight.astype(bf16)
    for low in range(2):
        for right in range(2):
            columns = slice(right * D, (right + 1) * D)
            weight, moment, second = adamw(
                out_ref[low, :, columns],
                out_mom_ref[low, :, columns],
                out_sec_ref[low, :, columns],
                dout_ref[2 * right + low].astype(f32) * clip,
                0.05,
                0.01,
            )
            out_new[low, :, columns] = weight
            out_mom_new[low, :, columns] = moment
            out_sec_new[low, :, columns] = second
            out_copy_new[low, :, columns] = weight.astype(bf16)

    @pl.when(pl.program_id(0) == 0)
    def _():
        inputs = in_ref.shape[0]
        weight, moment, second = adamw(
            in_ref[...], in_mom_ref[...], in_sec_ref[...], small_ref[0:inputs, :] * clip, 0.05, 0.01
        )
        in_new[...] = weight
        in_mom_new[...] = moment
        in_sec_new[...] = second
        in_copy_new[...] = weight.astype(bf16)

        norm_new[...] = norm_ref[0:1, 0:1]
        loss_new[...] = small_ref[inputs + 37 : inputs + 38, 0:1]

        def rows_of(first, last, base):
            return small_ref[inputs + base + first : inputs + base + last, :]

        for depth in range(LAYERS):
            base = 16 * depth
            for low, high, grad in (
                (0, 2, rows_of(0, 2, base)),
                (2, 4, rows_of(0, 2, base + 8)),
                (4, 7, rows_of(2, 5, base)),
                (7, 8, rows_of(2, 3, base + 8)),
                (8, 12, rows_of(4, 8, base + 8)),
            ):
                weight, moment, second = adamw(
                    vec_ref[low:high, depth],
                    vec_mom_ref[low:high, depth],
                    vec_sec_ref[low:high, depth],
                    grad * clip,
                    0.25,
                    0.0,
                )
                vec_new[low:high, depth] = weight
                vec_mom_new[low:high, depth] = moment
                vec_sec_new[low:high, depth] = second
        for low, high, grad in ((0, 1, rows_of(5, 6, 0)), (1, 5, rows_of(1, 5, 32))):
            weight, moment, second = adamw(
                outer_ref[low:high, :], outer_mom_ref[low:high, :], outer_sec_ref[low:high, :], grad * clip, 0.25, 0.0
            )
            outer_new[low:high, :] = weight
            outer_mom_new[low:high, :] = moment
            outer_sec_new[low:high, :] = second


def finish(rows, norm, every, updates, dout, small, arrays):
    steps = rows // 16
    attn, _, up, _, down, _, out, _, _, inp, _, _, vec, _, _, outer, _, _ = arrays
    codes = out.shape[2]
    part = out.shape[1] // steps
    blocks = pl.BlockSpec((GROUPS, UNITS, 16, D), lambda i: (0, 0, i, 0))
    attn_spec = pl.BlockSpec((LAYERS, 4, 16, D), lambda i: (0, 0, i, 0))
    up_spec = pl.BlockSpec((LAYERS, 16, FF), lambda i: (0, i, 0))
    out_spec = pl.BlockSpec((2, part, codes), lambda i: (0, i, 0))
    dout_spec = pl.BlockSpec((GROUPS, part, D), lambda i: (0, i, 0))
    in_spec, vec_spec, outer_spec = whole_spec(inp.shape), whole_spec(vec.shape), whole_spec(outer.shape)

    def like(array, dtype=f32):
        return jax.ShapeDtypeStruct(array.shape, dtype)

    return pl.pallas_call(
        finish_kernel,
        grid=(steps,),
        out_shape=[like(attn), like(attn), like(attn, bf16)]
        + [like(up), like(up), like(up, bf16)]
        + [like(down), like(down), like(down, bf16)]
        + [like(out)] * 3
        + [like(out, bf16)]
        + [like(inp)] * 3
        + [like(inp, bf16)]
        + [like(vec)] * 3
        + [like(outer)] * 3
        + [jax.ShapeDtypeStruct((1, 1), f32)] * 2,
        in_specs=[whole_spec((8, 128)), blocks, blocks, dout_spec, whole_spec(small.shape)]
        + [attn_spec] * 2
        + [up_spec] * 2
        + [attn_spec] * 2
        + [out_spec] * 3
        + [in_spec] * 3
        + [vec_spec] * 3
        + [outer_spec] * 3,
        out_specs=[attn_spec] * 3
        + [up_spec] * 3
        + [attn_spec] * 3
        + [out_spec] * 4
        + [in_spec] * 4
        + [vec_spec] * 3
        + [outer_spec] * 3
        + [whole_spec((1, 1))] * 2,
        compiler_params=pltpu.CompilerParams(vmem_limit_bytes=VMEM_LIMIT),
        cost_estimate=pl.CostEstimate(flops=10**8, bytes_accessed=4 * 10**7, transcendentals=0),
        name="finish",
    )(norm, every, updates, dout, small, *arrays)


def local(
    frames,
    speech_mask,
    targets,
    in_proj,
    in_moment,
    in_second,
    out_proj,
    out_moment,
    out_second,
    layer_vectors,
    vectors_moment,
    vectors_second,
    outer_vectors,
    outer_moment,
    outer_second,
    attn_proj,
    attn_momentum,
    ff_up,
    up_momentum,
    ff_down,
    down_momentum,
    in_copy,
    out_copy,
    attn_copy,
    up_copy,
    down_copy,
):
    segment = lax.axis_index("seg")
    count, dp_count = lax.axis_size("seg"), lax.axis_size("dp")
    rows = D // count
    streams = frames.shape[0]
    stream_total = streams * dp_count
    frames_t = jnp.swapaxes(frames, 1, 2)
    bias = jnp.where(segment > 0, 0.0, -1e30).astype(f32)[None]
    hidden, memory, totals, owned = embed(
        count, frames_t, speech_mask, in_copy, outer_vectors, attn_momentum, up_momentum, down_momentum
    )
    momenta = lax.all_gather(owned, "seg", axis=0, tiled=False)
    memory = [memory] * streams
    kept = []
    for depth in range(LAYERS):
        saved, passed = None, []
        for stream in range(streams):
            saved, short = forward_layer(
                depth,
                stream,
                streams,
                bias,
                hidden,
                memory[stream],
                attn_copy,
                up_copy,
                down_copy,
                layer_vectors,
                saved,
            )
            if depth + 1 < LAYERS:
                passed.append(from_behind(short, "seg", 1))
        kept.append((hidden, saved[8], saved))
        hidden = saved[0]
        memory = passed
    grad_hidden, grad_out, head_outer = head(
        hidden, targets, speech_mask, totals, out_copy, outer_vectors, 1.0 / stream_total, momenta
    )
    vector_grads, feed_done = [], [None, None]
    carried = grad_out.reshape(GROUPS * D // 2, D)
    carried_done = []
    for depth in reversed(range(LAYERS)):
        entering, held, saved = kept[depth]
        dafter, grad_up, grad_down, feed_vec, done = feed_back(
            depth, grad_hidden, saved[7], up_copy, down_copy, layer_vectors, count, dp_count, carried
        )
        carried_done.append(done)
        grad_hidden, grad_attn, attn_vec, grad_in, feed_done[depth] = attend_back(
            depth,
            bias,
            dafter,
            entering,
            held,
            saved[1:7],
            attn_copy,
            layer_vectors,
            frames_t,
            grad_up,
            grad_down,
            count,
            dp_count,
        )
        carried = grad_attn.reshape(4 * D, D)
        vector_grads = [attn_vec, feed_vec] + vector_grads
    out_done, attn_done = carried_done
    every_out = lax.all_gather(out_done, ("dp", "seg"), axis=0, tiled=True)[: GROUPS * D // 2]
    every_out = every_out.reshape(GROUPS, D // 2, D)
    whole, own, small, squares = reduce_grads(
        count,
        dp_count,
        grad_attn,
        attn_done,
        feed_done[0],
        feed_done[1],
        out_done,
        [grad_in] + vector_grads + [head_outer],
    )
    updates, every, norm = muon(count, squares, whole, momenta, own)
    split = (LAYERS, 4, rows, D)
    halved = (2, D // 2, out_proj.shape[1])
    (
        attn_new,
        attn_mom,
        attn_copy_new,
        up_new,
        up_mom,
        up_copy_new,
        down_new,
        down_mom,
        down_copy_new,
        out_new,
        out_moment_new,
        out_second_new,
        out_copy_new,
        in_new,
        in_moment_new,
        in_second_new,
        in_copy_new,
        vectors_new,
        vectors_moment_new,
        vectors_second_new,
        outer_new,
        outer_moment_new,
        outer_second_new,
        loss_sum,
        norm,
    ) = finish(
        rows,
        norm,
        every,
        updates,
        every_out,
        small,
        [
            attn_proj,
            attn_momentum,
            ff_up,
            up_momentum,
            ff_down.reshape(split),
            down_momentum.reshape(split),
            out_proj.reshape(halved),
            out_moment.reshape(halved),
            out_second.reshape(halved),
            in_proj,
            in_moment,
            in_second,
            jnp.swapaxes(layer_vectors, 0, 1),
            jnp.swapaxes(vectors_moment, 0, 1),
            jnp.swapaxes(vectors_second, 0, 1),
            outer_vectors,
            outer_moment,
            outer_second,
        ],
    )
    return (
        loss_sum.reshape(()),
        norm.reshape(()),
        in_new,
        in_moment_new,
        in_second_new,
        out_new.reshape(out_proj.shape),
        out_moment_new.reshape(out_proj.shape),
        out_second_new.reshape(out_proj.shape),
        jnp.swapaxes(vectors_new, 0, 1),
        jnp.swapaxes(vectors_moment_new, 0, 1),
        jnp.swapaxes(vectors_second_new, 0, 1),
        outer_new,
        outer_moment_new,
        outer_second_new,
        attn_new,
        attn_mom,
        up_new,
        up_mom,
        down_new.reshape(ff_down.shape),
        down_mom.reshape(ff_down.shape),
        in_copy_new,
        out_copy_new.reshape(out_proj.shape),
        attn_copy_new,
        up_copy_new,
        down_copy_new.reshape(ff_down.shape),
    )


def solution(mesh):
    return jax.shard_map(
        local,
        mesh=mesh,
        in_specs=(
            P("dp", "seg", None),
            P("dp", "seg"),
            P("dp", "seg"),
            P(),
            P(),
            P(),
            P(),
            P(),
            P(),
            P(),
            P(),
            P(),
            P(),
            P(),
            P(),
            P(None, None, "seg", None),
            P(None, None, "seg", None),
            P(None, "seg", None),
            P(None, "seg", None),
            P(None, "seg", None),
            P(None, "seg", None),
            P(),
            P(),
            P(),
            P(),
            P(),
        ),
        out_specs=(
            P(),
            P(),
            P(),
            P(),
            P(),
            P(),
            P(),
            P(),
            P(),
            P(),
            P(),
            P(),
            P(),
            P(),
            P(None, None, "seg", None),
            P(None, None, "seg", None),
            P(None, "seg", None),
            P(None, "seg", None),
            P(None, "seg", None),
            P(None, "seg", None),
            P(),
            P(),
            P(None, None, "seg", None),
            P(None, "seg", None),
            P(None, "seg", None),
        ),
        check_vma=False,
    )
```

```python
import functools
import math

import jax
import jax.numpy as jnp
from jax import lax
from jax.experimental import pallas as pl
from jax.experimental.pallas import tpu as pltpu
from jax.sharding import PartitionSpec as P

D = 512
HEAD_DIM = 64
HEADS = D // HEAD_DIM
FF = 2048
LAYERS = 2
STEP = 10
SEG = 512
HALF = 256
PAIR = 2 * HEAD_DIM
TILE = 512
VMEM_LIMIT = 56 * 1024 * 1024
GELU_SCALE = math.sqrt(2.0 / math.pi)

f32 = jnp.float32
bf16 = jnp.bfloat16


def dot_nn(left, right):
    return lax.dot_general(left, right, (((1,), (0,)), ((), ())), preferred_element_type=f32)


def dot_nt(left, right):
    return lax.dot_general(left, right, (((1,), (1,)), ((), ())), preferred_element_type=f32)


def dot_tn(left, right):
    return lax.dot_general(left, right, (((0,), (0,)), ((), ())), preferred_element_type=f32)


def normalised(values):
    centred = values - jnp.mean(values, -1, keepdims=True)
    scale = lax.rsqrt(jnp.mean(centred * centred, -1, keepdims=True) + 1e-05)
    return centred * scale, scale


def norm_back(grad, gain, unit, scale):
    part = grad * gain
    mean_part = jnp.mean(part, -1, keepdims=True)
    mean_unit = jnp.mean(part * unit, -1, keepdims=True)
    return scale * (part - mean_part - unit * mean_unit)


def column_sum(values):
    return jnp.sum(values, 0, keepdims=True)


def head_masks():
    lane = lax.broadcasted_iota(jnp.int32, (1, PAIR), 1)
    return (lane < HEAD_DIM).astype(bf16), (lane >= HEAD_DIM).astype(bf16)


def pair_lanes(pair):
    return pl.ds(pl.multiple_of(pair * PAIR, PAIR), PAIR)


def forward_kernel(
    depth,
    stream,
    bias_ref,
    x_ref,
    mem_ref,
    attn_ref,
    up_ref,
    down_ref,
    vec_ref,
    *refs,
):
    (
        hid_ref,
        hid16_ref,
        keyin_out,
        q_out,
        k_out,
        v_out,
        lse_ref,
        mixed_ref,
        after_ref,
        kept_out,
        act_s,
        lse_s,
        up_s,
        down_s,
        keyin_ref,
        q_ref,
        k_ref,
        v_ref,
        in_sem,
        out_sem,
    ) = refs[-20:]
    weights_in = (
        pltpu.make_async_copy(up_ref.at[depth], up_s, in_sem.at[0]),
        pltpu.make_async_copy(down_ref.at[depth], down_s, in_sem.at[1]),
    )
    for copy in weights_in:
        copy.start()
    saved_out = [
        pltpu.make_async_copy(source, target.at[stream], out_sem.at[place])
        for place, (source, target) in enumerate(
            ((keyin_ref, keyin_out), (q_ref, q_out), (k_ref, k_out), (v_ref, v_out))
        )
    ]
    kept_out[...] = mem_ref[...]
    x = x_ref[...]
    own_unit, _ = normalised(x)
    gain, shift = vec_ref[0:1, :], vec_ref[1:2, :]
    normed = (own_unit * gain + shift).astype(bf16)
    mem_unit, _ = normalised(mem_ref[...].astype(f32))
    mem_normed = (mem_unit * gain + shift).astype(bf16)
    keyin_ref[0:SEG, :] = mem_normed
    keyin_ref[SEG:, :] = normed
    q_ref[...] = (dot_nn(normed, attn_ref[0]) + vec_ref[4:5, :]).astype(bf16) * jnp.asarray(HEAD_DIM**-0.5, bf16)
    k_ref[0:SEG, :] = dot_nn(mem_normed, attn_ref[1]).astype(bf16)
    k_ref[SEG:, :] = dot_nn(normed, attn_ref[1]).astype(bf16)
    v_ref[0:SEG, :] = (dot_nn(mem_normed, attn_ref[2]) + vec_ref[5:6, :]).astype(bf16)
    v_ref[SEG:, :] = (dot_nn(normed, attn_ref[2]) + vec_ref[5:6, :]).astype(bf16)
    for copy in saved_out:
        copy.start()
    first, second = head_masks()
    memory_bias = bias_ref[0]
    lane = lax.broadcasted_iota(jnp.int32, (HALF, PAIR), 1)
    query_pos = lax.broadcasted_iota(jnp.int32, (2 * HALF, HALF), 0) % HALF
    key_pos = lax.broadcasted_iota(jnp.int32, (2 * HALF, HALF), 1)
    diagonal = key_pos <= query_pos
    lse_s[...] = jnp.zeros_like(lse_s)

    def pair_body(pair, carry):
        lanes = pair_lanes(pair)
        for block in range(2):
            rows = slice(block * HALF, (block + 1) * HALF)
            q_pair = q_ref[rows, lanes]
            q_both = jnp.concatenate([q_pair * first, q_pair * second], 0)
            spans = [(0, SEG, 0)]
            if block:
                spans.append((SEG, SEG + HALF, 1))
            spans.append((SEG + block * HALF, SEG + (block + 1) * HALF, 2))
            scores = []
            for low, high, kind in spans:
                part = dot_nt(q_both, k_ref[low:high, lanes])
                if kind == 2:
                    part = jnp.where(diagonal, part, -1e30)
                scores.append(part)
            peaks = [jnp.max(part, -1, keepdims=True) for part in scores]
            peaks[0] = peaks[0] + memory_bias
            most = functools.reduce(jnp.maximum, peaks)
            weights = [
                jnp.exp(part - (most if place else most - memory_bias)) for place, part in enumerate(scores)
            ]
            total = functools.reduce(jnp.add, [jnp.sum(part, -1, keepdims=True) for part in weights])
            mixed = functools.reduce(
                jnp.add,
                [
                    dot_nn(part.astype(bf16), v_ref[low:high, lanes])
                    for part, (low, high, kind) in zip(weights, spans)
                ],
            )
            mixed = mixed / total
            mixed_ref[rows, lanes] = jnp.where(lane < HEAD_DIM, mixed[:HALF], mixed[HALF:]).astype(bf16)
            lse = most + jnp.log(total)
            kept = jnp.where(lane == 2 * pair, lse[:HALF], lse_s[rows, :])
            lse_s[rows, :] = jnp.where(lane == 2 * pair + 1, lse[HALF:], kept)
        return carry

    lax.fori_loop(0, HEADS // 2, pair_body, 0)
    lse_ref[...] = jnp.transpose(lse_s[...])[0:HEADS, :]
    after = x + (dot_nn(mixed_ref[...], attn_ref[3]) + vec_ref[6:7, :])
    after_ref[...] = after
    unit, _ = normalised(after)
    normed_two = (unit * vec_ref[2:3, :] + vec_ref[3:4, :]).astype(bf16)
    for copy in weights_in:
        copy.wait()
    for tile in range(FF // TILE):
        columns = slice(tile * TILE, (tile + 1) * TILE)
        inner = dot_nn(normed_two, up_s[:, columns]) + vec_ref[8 + tile : 9 + tile, :]
        act_s[:, columns] = (
            0.5 * inner * (1.0 + jnp.tanh(GELU_SCALE * (inner + 0.044715 * inner * inner * inner)))
        ).astype(bf16)
    hidden = after + (dot_nn(act_s[...], down_s[...]) + vec_ref[7:8, :])
    hid_ref[...] = hidden
    hid16_ref[...] = hidden.astype(bf16)
    for copy in saved_out:
        copy.wait()


SAVED = (
    ((SEG, D), f32),
    ((2 * SEG, D), bf16),
    ((SEG, D), bf16),
    ((2 * SEG, D), bf16),
    ((2 * SEG, D), bf16),
    ((HEADS, SEG), f32),
    ((SEG, D), bf16),
    ((SEG, D), f32),
    ((SEG, D), bf16),
)


def whole_spec(shape):
    return pl.BlockSpec(shape, lambda *_: (0,) * len(shape))


def stream_spec(shape, stream=None):
    zeros = (0,) * len(shape)
    if stream is None:
        return pl.BlockSpec((None,) + shape, lambda i: (i,) + zeros)
    return pl.BlockSpec((None,) + shape, lambda i: (stream,) + zeros)


def layer_spec(shape, depth):
    zeros = (0,) * len(shape)
    return pl.BlockSpec((None,) + shape, lambda *_: (depth,) + zeros)


def forward_layer(depth, stream, streams, bias, hidden, memory, attn, upper, lower, vectors, earlier):
    saved_shapes = [jax.ShapeDtypeStruct((streams,) + shape, dtype) for shape, dtype in SAVED]
    saved_specs = [stream_spec(shape, stream) for shape, dtype in SAVED]
    out_shape = [saved_shapes[0], jax.ShapeDtypeStruct((SEG, D), bf16)] + saved_shapes[1:]
    out_specs = [saved_specs[0], whole_spec((SEG, D))] + saved_specs[1:]
    for place in (2, 3, 4, 5):
        out_specs[place] = pl.BlockSpec(memory_space=pl.ANY)
    operands = [bias, hidden, memory, attn, upper, lower, vectors]
    in_specs = [
        pl.BlockSpec(memory_space=pltpu.SMEM),
        stream_spec((SEG, D), stream),
        stream_spec((SEG, D), stream) if memory.ndim == 3 else whole_spec((SEG, D)),
        layer_spec(attn.shape[1:], depth),
        pl.BlockSpec(memory_space=pl.ANY),
        pl.BlockSpec(memory_space=pl.ANY),
        layer_spec(vectors.shape[1:], depth),
    ]
    aliases = {}
    if earlier is not None:
        for place, array in enumerate(earlier):
            aliases[len(operands)] = place if place == 0 else place + 1
            operands.append(array)
            in_specs.append(pl.BlockSpec(memory_space=pl.ANY))
    out = pl.pallas_call(
        functools.partial(forward_kernel, depth, stream),
        grid=(1,),
        out_shape=out_shape,
        in_specs=in_specs,
        out_specs=out_specs,
        scratch_shapes=[
            pltpu.VMEM((SEG, FF), bf16),
            pltpu.VMEM((SEG, PAIR), f32),
            pltpu.VMEM((D, FF), bf16),
            pltpu.VMEM((FF, D), bf16),
            pltpu.VMEM((2 * SEG, D), bf16),
            pltpu.VMEM((SEG, D), bf16),
            pltpu.VMEM((2 * SEG, D), bf16),
            pltpu.VMEM((2 * SEG, D), bf16),
            pltpu.SemaphoreType.DMA((2,)),
            pltpu.SemaphoreType.DMA((4,)),
        ],
        input_output_aliases=aliases,
        compiler_params=pltpu.CompilerParams(vmem_limit_bytes=VMEM_LIMIT),
        cost_estimate=pl.CostEstimate(flops=10**10, bytes_accessed=2 * 10**7, transcendentals=10**7),
        name="layer_forward",
    )(*operands)
    return [out[0]] + list(out[2:]), out[1]


def head_kernel(scale, x_ref, target_ref, mask_ref, total_ref, out_ref, outer_ref, mom_ref, g_ref, dout_ref, douter_ref, acc_s):
    step = pl.program_id(0)

    @pl.when(step == 0)
    def _():
        acc_s[...] = jnp.zeros_like(acc_s)
        douter_ref[...] = jnp.zeros_like(douter_ref)

    unit, rscale = normalised(x_ref[...])
    gain = outer_ref[1:2, :]
    normed = (unit * gain + outer_ref[2:3, :]).astype(bf16)
    shift = jnp.concatenate([outer_ref[3:4, :], outer_ref[4:5, :]], 1)
    logits = dot_nn(normed, out_ref[...]) + shift
    most = jnp.max(logits, -1, keepdims=True)
    powers = jnp.exp(logits - most)
    total = jnp.sum(powers, -1, keepdims=True)
    target_row = target_ref[pl.ds(step, 1), :].astype(f32)
    weight_row = mask_ref[pl.ds(step, 1), :].astype(f32) * (1.0 / total_ref[pl.ds(step, 1), 0:1])
    columns = jnp.transpose(jnp.concatenate([target_row, weight_row, jnp.zeros((6, SEG), f32)], 0))
    target, weight = columns[:, 0:1].astype(jnp.int32), columns[:, 1:2]
    chosen = lax.broadcasted_iota(jnp.int32, logits.shape, 1) == target
    picked = jnp.sum(jnp.where(chosen, logits, 0.0), -1, keepdims=True)
    loss = jnp.sum(weight * (most + jnp.log(total) - picked), 0, keepdims=True)
    spread = weight * scale
    dlogits = (powers * (spread / total) - jnp.where(chosen, spread, 0.0)).astype(bf16)
    acc_s[...] += dot_nn(jnp.transpose(normed), dlogits)
    bias_grad = column_sum(dlogits.astype(f32))
    dnormed = dot_nt(dlogits, out_ref[...])
    g_ref[...] = norm_back(dnormed, gain, unit, rscale)
    douter_ref[1:2, :] += column_sum(dnormed * unit)
    douter_ref[2:3, :] += column_sum(dnormed)
    douter_ref[3:4, :] += bias_grad[:, :D]
    douter_ref[4:5, :] += bias_grad[:, D:]
    douter_ref[5:6, :] += jnp.broadcast_to(loss, (1, D))

    @pl.when(step == pl.num_programs(0) - 1)
    def _():
        half = D // 2
        for right in range(2):
            for low in range(2):
                dout_ref[right, low] = acc_s[
                    low * half : (low + 1) * half, right * D : (right + 1) * D
                ]


def head(hidden, targets, mask, totals, out_weight, outer_vectors, scale, momenta):
    streams = hidden.shape[0]
    codes = out_weight.shape[1]
    return pl.pallas_call(
        functools.partial(head_kernel, scale),
        grid=(streams,),
        out_shape=[
            jax.ShapeDtypeStruct((streams, SEG, D), f32),
            jax.ShapeDtypeStruct((2, 2, D // 2, D), f32),
            jax.ShapeDtypeStruct((8, D), f32),
        ],
        in_specs=[
            stream_spec((SEG, D)),
            whole_spec((streams, SEG)),
            whole_spec((streams, SEG)),
            whole_spec((8, 128)),
            whole_spec((D, codes)),
            whole_spec(outer_vectors.shape),
            pl.BlockSpec(memory_space=pl.ANY),
        ],
        out_specs=[stream_spec((SEG, D)), whole_spec((2, 2, D // 2, D)), whole_spec((8, D))],
        scratch_shapes=[pltpu.VMEM((D, codes), f32)],
        compiler_params=pltpu.CompilerParams(vmem_limit_bytes=VMEM_LIMIT),
        cost_estimate=pl.CostEstimate(flops=33 * 10**8, bytes_accessed=10**7, transcendentals=10**6),
        name="head",
    )(hidden, targets, mask, totals, out_weight, outer_vectors, momenta)


def feed_back_kernel(streams, g_ref, after_ref, up_ref, down_ref, vec_ref, *refs):
    step = pl.program_id(0)
    grad_ref, dafter_ref, dup_ref, ddown_ref, dvec_ref, done_ref, normed_s, branch_s, act_s, inner_s = refs[:10]
    carry = AttnCarry(grad_ref, refs[10 : 10 + CARRY_REFS], refs[10 + CARRY_REFS :], done_ref)
    planes = carry.planes
    early, late = range(planes // 2), range(planes // 2, planes)
    beats = [
        [("b", place) for place in range(planes)],
        [("m", place) for place in early],
        [("m", place) for place in late],
        [("e", place) for place in early],
        [("e", place) for place in late],
    ]

    @pl.when(step == 0)
    def _():
        hail(carry.targets)
        carry.load_all()
        dvec_ref[...] = jnp.zeros_like(dvec_ref)

    rows = pl.ds(pl.multiple_of(step * SEG, SEG), SEG)
    grad = g_ref[...]
    branch = grad.astype(bf16)
    dvec_ref[2:3, :] += column_sum(branch.astype(f32))
    unit, scale = normalised(after_ref[...])
    gain = vec_ref[2:3, :]
    normed = (unit * gain + vec_ref[3:4, :]).astype(bf16)
    normed_s[:, rows] = jnp.transpose(normed)
    branch_s[:, rows] = jnp.transpose(branch)

    @pl.when(step == 0)
    def _():
        meet(carry.targets)
        carry.send_all()

    for tile in range(FF // TILE):
        columns = slice(tile * TILE, (tile + 1) * TILE)
        inner = dot_nn(normed, up_ref[:, columns]) + vec_ref[8 + tile : 9 + tile, :]
        dact = dot_nt(branch, down_ref[columns, :])
        square = inner * inner
        bent = jnp.tanh(inner * (GELU_SCALE + (GELU_SCALE * 0.044715) * square))
        half = 0.5 * (1.0 + bent)
        act_s[rows, columns] = (inner * half).astype(bf16)
        slope = half + inner * (half * (1.0 - bent)) * (GELU_SCALE + (GELU_SCALE * 0.134145) * square)
        dinner = (dact * slope).astype(bf16)
        inner_s[rows, columns] = dinner
        dvec_ref[4 + tile : 5 + tile, :] += column_sum(dinner.astype(f32))

    @pl.when(step == 0)
    def _():
        carry.run(beats[0])

    @pl.when(step == streams - 1)
    def _():
        carry.run(beats[1])

    dnormed = dot_nt(inner_s[rows, :], up_ref[...])
    dvec_ref[0:1, :] += column_sum(dnormed * unit)
    dvec_ref[1:2, :] += column_sum(dnormed)
    dafter_ref[...] = grad + norm_back(dnormed, gain, unit, scale)

    @pl.when(step == streams - 1)
    def _():
        carry.run(beats[2])
        for tile in range(FF // TILE):
            columns = slice(tile * TILE, (tile + 1) * TILE)
            dup_ref[tile] = dot_nn(normed_s[...], inner_s[:, columns]).astype(bf16)
        carry.run(beats[3])
        for tile in range(FF // TILE):
            columns = slice(tile * TILE, (tile + 1) * TILE)
            ddown_ref[columns, :] = jnp.transpose(dot_nn(branch_s[...], act_s[:, columns]).astype(bf16))
        carry.run(beats[4])
        carry.drain()


def feed_back(depth, grad, after, upper, lower, vectors, count, dp_count, attn_grad):
    streams = grad.shape[0]
    rows = attn_grad.shape[0] // (GROUPS * count)
    in_specs = [
        stream_spec((SEG, D)),
        stream_spec((SEG, D)),
        layer_spec(upper.shape[1:], depth),
        layer_spec(lower.shape[1:], depth),
        layer_spec(vectors.shape[1:], depth),
    ]
    out_shape = [
        jax.ShapeDtypeStruct((streams, SEG, D), f32),
        jax.ShapeDtypeStruct((FF // TILE, D, TILE), bf16),
        jax.ShapeDtypeStruct((FF, D), bf16),
        jax.ShapeDtypeStruct((8, D), f32),
    ]
    out_specs = [
        stream_spec((SEG, D)),
        whole_spec((FF // TILE, D, TILE)),
        whole_spec((FF, D)),
        whole_spec((8, D)),
    ]
    scratch = [
        pltpu.VMEM((D, streams * SEG), bf16),
        pltpu.VMEM((D, streams * SEG), bf16),
        pltpu.VMEM((streams * SEG, FF), bf16),
        pltpu.VMEM((streams * SEG, FF), bf16),
    ]
    operands = [grad, after, upper, lower, vectors]
    in_specs.append(pl.BlockSpec(memory_space=pl.ANY))
    operands.append(attn_grad.reshape(2, 2, count, rows, D))
    out_shape.append(jax.ShapeDtypeStruct((count // 2, rows, D), attn_grad.dtype))
    out_specs.append(whole_spec((count // 2, rows, D)))
    scratch = scratch + carry_scratch("attn", rows, count, dp_count, attn_grad.dtype)
    params = {"collective_id": 6 + depth, "has_side_effects": True}
    return pl.pallas_call(
        functools.partial(feed_back_kernel, streams),
        grid=(streams,),
        out_shape=out_shape,
        in_specs=in_specs,
        out_specs=out_specs,
        scratch_shapes=scratch,
        compiler_params=pltpu.CompilerParams(vmem_limit_bytes=VMEM_LIMIT, **params),
        cost_estimate=pl.CostEstimate(flops=11 * 10**9, bytes_accessed=2 * 10**7, transcendentals=2 * 10**6),
        name="feed_back",
    )(*operands)


def attend_back_kernel(
    streams,
    depth,
    bias_ref,
    dafter_ref,
    x_ref,
    mem_ref,
    keyin_ref,
    q_ref,
    k_ref,
    v_ref,
    lse_ref,
    mixed_ref,
    attn_ref,
    vec_ref,
    frames_ref,
    dup_ref,
    ddown_ref,
    sums_ref,
    dx_ref,
    dattn_ref,
    dvec_ref,
    din_ref,
    done_ref,
    along_ref,
    attn_s,
    dmixed_s,
    dq_s,
    dk_s,
    dv_s,
    ds_s,
    delta_s,
    *refs,
):
    step = pl.program_id(0)
    pairs = HEADS // 2
    split = CARRY_REFS + 1 + CARRY_SEMS
    carry = FeedCarry(depth, dup_ref, ddown_ref, refs[: CARRY_REFS + 1], refs[CARRY_REFS + 1 : split])
    along = ZCarry(refs[split : split + Z_REFS], refs[split + Z_REFS :])
    plans, (free, bound) = carry.plans(), along.plans()

    @pl.when(step == 0)
    def _():
        hail(carry.targets)
        carry.load_all()
        along.sums[...] = sums_ref[...]
        attn_s[...] = jnp.zeros_like(attn_s)
        dvec_ref[...] = jnp.zeros_like(dvec_ref)
        din_ref[...] = jnp.zeros_like(din_ref)

    dafter = dafter_ref[...]
    branch = dafter.astype(bf16)
    dvec_ref[4:5, :] += column_sum(branch.astype(f32))
    dmixed = dot_nt(branch, attn_ref[3]).astype(bf16)
    dmixed_s[...] = dmixed
    attn_s[3] += dot_nn(jnp.transpose(mixed_ref[...]), branch)
    product = dmixed.astype(f32) * mixed_ref[...].astype(f32)
    high = product.astype(bf16)
    rest = (product - high.astype(f32)).astype(bf16)
    owner = lax.broadcasted_iota(jnp.int32, (HEADS, D), 1) // HEAD_DIM
    pick = (owner == lax.broadcasted_iota(jnp.int32, (HEADS, D), 0)).astype(bf16)
    delta_s[...] = dot_nt(pick, high) + dot_nt(pick, rest)
    first, second = head_masks()
    memory_bias = bias_ref[0]
    key_pos = lax.broadcasted_iota(jnp.int32, (HALF, 2 * HALF), 0)
    query_pos = lax.broadcasted_iota(jnp.int32, (HALF, 2 * HALF), 1) % HALF
    diagonal = key_pos <= query_pos
    head_row = lax.broadcasted_iota(jnp.int32, (PAIR, HALF), 0)

    @pl.when(step == 0)
    def _():
        meet(carry.targets)
        carry.send_all()
        along.run(free)

    @pl.when(step == 1)
    def _():
        carry.run(plans[-1])

    def pair_body(pair, state):
        lanes = pair_lanes(pair)
        q_pair, do_pair = q_ref[:, lanes], dmixed_s[:, lanes]

        def spread(value):
            return jnp.concatenate(
                [value[:HALF] * first, value[:HALF] * second, value[HALF:] * first, value[HALF:] * second], 0
            )

        q_all, do_all = spread(q_pair), spread(do_pair)

        def rows_of(ref):
            one, two = ref[pl.ds(2 * pair, 1), :], ref[pl.ds(2 * pair + 1, 1), :]
            return jnp.concatenate([one[:, :HALF], two[:, :HALF], one[:, HALF:], two[:, HALF:]], 1)

        lse_all, delta_all = rows_of(lse_ref), rows_of(delta_s)
        for block in range(4):
            keys = slice(block * HALF, (block + 1) * HALF)
            start = 2 * HALF if block == 3 else 0
            scores = dot_nt(k_ref[keys, lanes], q_all[start:])
            shift = lse_all - memory_bias if block < 2 else lse_all[:, start:]
            weights = jnp.exp(scores - shift)
            if block == 2:
                weights = jnp.concatenate(
                    [jnp.where(diagonal, weights[:, : 2 * HALF], 0.0), weights[:, 2 * HALF :]], 1
                )
            if block == 3:
                weights = jnp.where(diagonal, weights, 0.0)
            dweights = dot_nt(v_ref[keys, lanes], do_all[start:])
            dscores = (weights * (dweights - delta_all[:, start:])).astype(bf16)
            dv_s[keys, lanes] = dot_nn(weights.astype(bf16), do_all[start:]).astype(bf16)
            dk_s[keys, lanes] = dot_nn(dscores, q_all[start:]).astype(bf16)
            ds_s[keys, start:] = dscores
        k_t = jnp.transpose(k_ref[:, lanes])
        for block in range(2):
            seen = SEG + (block + 1) * HALF
            grads = dot_nn(k_t[:, :seen], ds_s[:seen, block * 2 * HALF : (block + 1) * 2 * HALF])
            grads = jnp.where(head_row < HEAD_DIM, grads[:, :HALF], grads[:, HALF:])
            dq_s[block * HALF : (block + 1) * HALF, lanes] = (
                jnp.transpose(grads) * (HEAD_DIM**-0.5)
            ).astype(bf16)
        for time, acts in enumerate(plans[:-1]):
            if acts:

                @pl.when(pairs * step + pair == time)
                def _():
                    carry.run(acts)
                    if time == 3:
                        along.run(bound)

        return state

    lax.fori_loop(0, pairs, pair_body, 0)
    dq, dk, dv = dq_s[...], dk_s[...], dv_s[...]
    keyin_t = jnp.transpose(keyin_ref[...])
    attn_s[0] += dot_nn(keyin_t[:, SEG:], dq)
    attn_s[1] += dot_nn(keyin_t, dk)
    attn_s[2] += dot_nn(keyin_t, dv)
    dvec_ref[2:3, :] += column_sum(dq.astype(f32))
    dvec_ref[3:4, :] += column_sum(dv.astype(f32))
    dkeyin = dot_nt(dk, attn_ref[1]) + dot_nt(dv, attn_ref[2])
    dmem = dkeyin[:SEG]
    down = dkeyin[SEG:] + dot_nt(dq, attn_ref[0])
    gain = vec_ref[0:1, :]
    unit, scale = normalised(x_ref[...])
    mem_unit, _ = normalised(mem_ref[...].astype(f32))
    dvec_ref[0:1, :] += column_sum(down * unit + dmem * mem_unit)
    dvec_ref[1:2, :] += column_sum(down + dmem)
    dx = dafter + norm_back(down, gain, unit, scale)
    dx_ref[...] = dx
    if depth == 0:
        dx_high = dx.astype(bf16)
        dx_rest = (dx - dx_high.astype(f32)).astype(bf16)
        din_ref[...] += dot_nn(frames_ref[...], dx_high) + dot_nn(frames_ref[...], dx_rest)
        dvec_ref[5:6, :] += column_sum(dx)

    @pl.when(step == pl.num_programs(0) - 1)
    def _():
        dattn_ref[...] = attn_s[...].astype(bf16)
        carry.finish(done_ref)
        along.finish(along_ref)


def attend_back(depth, bias, dafter, x, memory, saved, attn, vectors, frames, up_grad, down_grad, sums, count, dp_count):
    streams = dafter.shape[0]
    keyin, q, k, v, lse, mixed = saved
    inputs = frames.shape[1]
    rows = D // count
    up_grad, down_grad = up_grad.reshape(4, count, rows, D), down_grad.reshape(count, 4, rows, D)
    return pl.pallas_call(
        functools.partial(attend_back_kernel, streams, depth),
        grid=(streams,),
        out_shape=[
            jax.ShapeDtypeStruct((streams, SEG, D), f32),
            jax.ShapeDtypeStruct((4, D, D), bf16),
            jax.ShapeDtypeStruct((8, D), f32),
            jax.ShapeDtypeStruct((inputs, D), f32),
            jax.ShapeDtypeStruct((2, rows, D), bf16),
            jax.ShapeDtypeStruct(sums.shape[1:], bf16),
        ],
        in_specs=[
            pl.BlockSpec(memory_space=pltpu.SMEM),
            stream_spec((SEG, D)),
            stream_spec((SEG, D)),
            stream_spec((SEG, D)),
            stream_spec((2 * SEG, D)),
            stream_spec((SEG, D)),
            stream_spec((2 * SEG, D)),
            stream_spec((2 * SEG, D)),
            stream_spec((HEADS, SEG)),
            stream_spec((SEG, D)),
            layer_spec(attn.shape[1:], depth),
            layer_spec(vectors.shape[1:], depth),
            stream_spec((inputs, SEG)),
            pl.BlockSpec(memory_space=pl.ANY),
            pl.BlockSpec(memory_space=pl.ANY),
            whole_spec(sums.shape),
        ],
        out_specs=[
            stream_spec((SEG, D)),
            whole_spec((4, D, D)),
            whole_spec((8, D)),
            whole_spec((inputs, D)),
            whole_spec((2, rows, D)),
            whole_spec(sums.shape[1:]),
        ],
        scratch_shapes=[
            pltpu.VMEM((4, D, D), f32),
            pltpu.VMEM((SEG, D), bf16),
            pltpu.VMEM((SEG, D), bf16),
            pltpu.VMEM((2 * SEG, D), bf16),
            pltpu.VMEM((2 * SEG, D), bf16),
            pltpu.VMEM((2 * SEG, 2 * SEG), bf16),
            pltpu.VMEM((HEADS, SEG), f32),
        ]
        + carry_scratch("feed", rows, count, dp_count)
        + z_scratch(sums.shape[1], count, dp_count, sums.dtype),
        compiler_params=pltpu.CompilerParams(
            collective_id=4 + depth, has_side_effects=True, vmem_limit_bytes=VMEM_LIMIT
        ),
        cost_estimate=pl.CostEstimate(flops=3 * 10**10, bytes_accessed=2 * 10**7, transcendentals=10**7),
        name="attend_back",
    )(bias, dafter, x, memory, keyin, q, k, v, lse, mixed, attn, vectors, frames, up_grad, down_grad, sums)


def from_behind(value, axis, steps):
    count = lax.axis_size(axis)
    leading, last = (max(0, -steps), min(count, count - steps))
    return lax.ppermute(value, axis, [(source, source + steps) for source in range(leading, last)])


def adamw(weight, moment, second, grad, rate, decay):
    moment = 0.5 * moment + 0.5 * grad
    second = 0.99 * second + 0.01 * grad * grad
    fixed_moment = moment / (1.0 - 0.5**STEP)
    fixed_second = second / (1.0 - 0.99**STEP)
    weight = weight * (1.0 - rate * decay) - rate * fixed_moment / (jnp.sqrt(fixed_second) + 1e-08)
    return (weight, moment, second)


GROUPS = 4
UNITS = 6
SMALL = 128


def peers():
    count = {"seg": lax.axis_size("seg"), "dp": lax.axis_size("dp")}
    seg, dp = lax.axis_index("seg"), lax.axis_index("dp")
    core, x, y = seg % 2, dp % 2, (dp // 2) % 2
    across_core = {"seg": seg + 1 - 2 * core}
    across_x = {"dp": dp + 1 - 2 * x}
    across_y = {"dp": dp + 2 - 4 * y}
    across_both = {"dp": dp + 3 - 2 * x - 4 * y}
    far = []
    step = GROUPS
    while step < count["dp"]:
        far.append({"dp": dp + step - 2 * step * ((dp // step) % 2)})
        step *= 2
    return seg, dp, core, x, y, across_core, (across_x, across_y, across_both), far


def others(seg, count):
    return [lax.rem(seg + step, count) for step in range(1, count)]


def hail(targets):
    barrier = pltpu.get_barrier_semaphore()
    for target in targets:
        pl.semaphore_signal(barrier, inc=1, device_id=target, device_id_type=pl.DeviceIdType.MESH)


def meet(targets):
    pl.semaphore_wait(pltpu.get_barrier_semaphore(), len(targets))


def greet(seg, count, near, far):
    targets = [{"seg": other} for other in others(seg, count)] + list(near) + list(far)
    hail(targets)
    meet(targets)


def remote(source, target, send, recv, device):
    return pltpu.make_async_remote_copy(
        src_ref=source,
        dst_ref=target,
        send_sem=send,
        recv_sem=recv,
        device_id=device,
        device_id_type=pl.DeviceIdType.MESH,
    )


def wait_bytes(ref, sem):
    pltpu.make_async_copy(ref, ref, sem).wait()


def plus(left, right):
    return (left.astype(f32) + right.astype(f32)).astype(left.dtype)


def owners(count):
    attn, feed = count // 4 - 1, count // 4
    return (
        (0, 1, 2 * attn, 0),
        (1, 1, 2 * attn + 1, 0),
        (2, 2, 2 * feed, 0),
        (4, 2, 2 * feed + 1, 2),
    )


def lowest_bit(mask, planes):
    bit = 1
    while bit < planes and not mask & bit:
        bit *= 2
    return bit


class Carry:
    def __init__(self, refs, sems):
        self.mine, self.got0, self.got1, self.got2, self.got3, self.goth = refs
        (
            self.load,
            self.send0,
            self.recv0,
            self.send1,
            self.recv1,
            self.send2,
            self.recv2,
            self.send3,
            self.recv3,
            self.sendh,
            self.recvh,
        ) = sems
        self.settle(self.mine.shape[0])

    def settle(self, planes):
        self.seg, self.dp, self.core, self.x, self.y, self.across_core, near, self.far = peers()
        self.across_x, self.across_y, _ = near
        self.planes = planes
        self.plane = self.seg // 2
        self.targets = [self.across_core, self.across_x, self.across_y] + self.far
        bit = 1
        while bit < planes:
            self.targets.append({"seg": 2 * self.toggled(bit) + self.core})
            bit *= 2
        self.order = list(reversed(range(planes)))

    def toggled(self, mask):
        place, bit = self.plane, 1
        while bit <= mask:
            if mask & bit:
                place = place + bit - 2 * bit * ((self.plane // bit) % 2)
            bit *= 2
        return place

    def load_all(self):
        for step in range(self.planes):
            for source, place in self.pieces(2 * self.toggled(self.order[step]) + self.core):
                pltpu.make_async_copy(source, self.mine.at[(step,) + place], self.load.at[step]).start()

    def send_all(self):
        for step in range(self.planes):
            for source, place in self.pieces(2 * self.toggled(self.order[step]) + 1 - self.core):
                remote(
                    source, self.got0.at[(step,) + place], self.send0.at[step], self.recv0.at[step], self.across_core
                ).start()

    def begin(self, step):
        wait_bytes(self.mine.at[step], self.load.at[step])
        wait_bytes(self.got0.at[step], self.recv0.at[step])
        for place in range(2):
            self.mine[step, place] = plus(self.mine[step, place], self.got0[step, place])
        for copy in self.first(step):
            copy.start()

    def across(self, place, step):
        return remote(
            self.held(step),
            self.goth.at[place, step],
            self.sendh.at[place, step],
            self.recvh.at[place, step],
            self.far[place],
        )

    def third(self, step):
        mask = self.order[step]
        return remote(
            self.held(step),
            self.got3.at[mask],
            self.send3.at[step],
            self.recv3.at[mask],
            {"seg": 2 * self.toggled(lowest_bit(mask, self.planes)) + self.core},
        )

    def onward(self, step):
        held = self.held(step)
        for place in range(len(self.far)):
            copy = self.across(place, step)
            copy.start()
            copy.wait()
            held[...] = plus(held[...], self.goth[place, step])
        mask = self.order[step]
        if mask:
            self.gathered(mask, held)
            self.third(step).start()

    def gathered(self, mask, held):
        value, bit = held[...].astype(f32), 1
        while bit < lowest_bit(mask, self.planes):
            wait_bytes(self.got3.at[mask + bit], self.recv3.at[mask + bit])
            value = value + self.got3[mask + bit].astype(f32)
            bit *= 2
        held[...] = value.astype(held.dtype)

    def total(self):
        held = self.held(self.planes - 1)
        self.gathered(0, held)
        return held[...]

    def run(self, acts):
        for kind, step in acts:
            getattr(self, {"b": "begin", "m": "middle", "e": "end", "z": "onward"}[kind])(step)


class ZCarry(Carry):
    def __init__(self, refs, sems):
        self.sums, self.got3, self.goth = refs
        self.send3, self.recv3, self.sendh, self.recvh = sems
        self.settle(self.sums.shape[0])

    def held(self, step):
        return self.sums.at[step]

    def plans(self):
        free = [("z", step) for step in range(self.planes) if self.order[step] % 2]
        bound = [("z", step) for step in range(self.planes) if self.order[step] and not self.order[step] % 2]
        return free, bound

    def finish(self, out_ref):
        out_ref[...] = self.total().astype(out_ref.dtype)
        for step in range(self.planes - 1):
            self.third(step).wait_send()


class AttnCarry(Carry):
    def __init__(self, source, refs, sems, sums=None):
        super().__init__(refs, sems)
        self.source, self.sums = source, sums

    def pieces(self, row):
        return ((self.source.at[:, :, row], ()),)

    def held(self, step):
        return self.mine.at[step, self.y, self.x]

    def first(self, step):
        half = self.mine.shape[3] // 2
        return (
            remote(
                self.mine.at[step, :, 1 - self.x, 0:half],
                self.got1.at[step, 0],
                self.send1.at[step, 0],
                self.recv1.at[step, 0],
                self.across_x,
            ),
            remote(
                self.mine.at[step, 1 - self.y, :, half:],
                self.got1.at[step, 1],
                self.send1.at[step, 1],
                self.recv1.at[step, 1],
                self.across_y,
            ),
        )

    def second(self, step):
        half = self.mine.shape[3] // 2
        return (
            remote(
                self.mine.at[step, 1 - self.y, self.x, 0:half],
                self.got2.at[step, 0],
                self.send2.at[step, 0],
                self.recv2.at[step, 0],
                self.across_y,
            ),
            remote(
                self.mine.at[step, self.y, 1 - self.x, half:],
                self.got2.at[step, 1],
                self.send2.at[step, 1],
                self.recv2.at[step, 1],
                self.across_x,
            ),
        )

    def middle(self, step):
        mine, half = self.mine, self.mine.shape[3] // 2
        for copy in self.first(step):
            copy.wait_recv()
        for place in range(2):
            mine[step, place, self.x, 0:half] = plus(mine[step, place, self.x, 0:half], self.got1[step, 0, place])
            mine[step, self.y, place, half:] = plus(mine[step, self.y, place, half:], self.got1[step, 1, place])
        for copy in self.second(step):
            copy.start()

    def end(self, step):
        mine, half = self.mine, self.mine.shape[3] // 2
        for copy in self.second(step):
            copy.wait_recv()
        upper = plus(mine[step, self.y, self.x, 0:half], self.got2[step, 0])
        lower = plus(mine[step, self.y, self.x, half:], self.got2[step, 1])
        if self.sums is not None:
            self.sums[step, 0:half] = upper
            self.sums[step, half:] = lower
            return
        mine[step, self.y, self.x, 0:half] = upper
        mine[step, self.y, self.x, half:] = lower
        self.onward(step)

    def drain(self):
        for step in range(self.planes):
            wait_bytes(self.mine.at[step], self.send0.at[step])
            for copy in self.first(step) + self.second(step):
                copy.wait_send()
            if self.sums is None and step < self.planes - 1:
                self.third(step).wait_send()


class FeedCarry(Carry):
    def __init__(self, depth, up, down, refs, sems):
        super().__init__(refs[:CARRY_REFS], sems)
        (self.sums,) = refs[CARRY_REFS:]
        self.up, self.down = up, down
        self.keep = self.x if depth == 1 else 1 - self.x

    def pieces(self, row):
        return ((self.up.at[:, row], (0,)), (self.down.at[row], (1,)))

    def held(self, step):
        return self.sums.at[step]

    def first(self, step):
        return (
            remote(
                self.mine.at[step, 1 - self.keep, 0:2],
                self.got1.at[step, 0],
                self.send1.at[step, 0],
                self.recv1.at[step, 0],
                self.across_x,
            ),
            remote(
                self.mine.at[step, 1 - self.y, 2:4],
                self.got1.at[step, 1],
                self.send1.at[step, 1],
                self.recv1.at[step, 1],
                self.across_y,
            ),
        )

    def second(self, step):
        return (
            remote(
                self.mine.at[step, self.keep, 1 - self.y],
                self.got2.at[step, 0],
                self.send2.at[step, 0],
                self.recv2.at[step, 0],
                self.across_y,
            ),
            remote(
                self.mine.at[step, self.y, 3 - self.x],
                self.got2.at[step, 1],
                self.send2.at[step, 1],
                self.recv2.at[step, 1],
                self.across_x,
            ),
        )

    def middle(self, step):
        for copy in self.first(step):
            copy.wait_recv()
        self.mine[step, self.keep, 0:2] = plus(self.mine[step, self.keep, 0:2], self.got1[step, 0])
        self.mine[step, self.y, 2:4] = plus(self.mine[step, self.y, 2:4], self.got1[step, 1])
        for copy in self.second(step):
            copy.start()

    def end(self, step):
        for copy in self.second(step):
            copy.wait_recv()
        self.sums[step, 0] = plus(self.mine[step, self.keep, self.y], self.got2[step, 0])
        self.sums[step, 1] = plus(self.mine[step, self.y, 2 + self.x], self.got2[step, 1])
        self.onward(step)

    def plans(self):
        planes = self.planes
        return (
            [("b", step) for step in range(planes - 1)],
            [],
            [("m", 0), ("b", planes - 1)],
            [("m", 1)],
            [("m", step) for step in range(3, planes)],
            [("e", 1)],
            [("e", 2)],
            [("e", step) for step in range(3, planes)],
            [("m", 2), ("e", 0)],
        )

    def finish(self, out_ref):
        out_ref[...] = self.total()
        for step in range(self.planes):
            wait_bytes(self.mine.at[step], self.send0.at[step])
            for copy in self.first(step) + self.second(step):
                copy.wait_send()
            if step < self.planes - 1:
                self.third(step).wait_send()


CARRY_REFS = 6
CARRY_SEMS = 11


def carry_scratch(kind, rows, count, dp_count, dtype=bf16):
    planes = count // 2
    far = max(1, dp_count.bit_length() - 3)
    dma = pltpu.SemaphoreType.DMA
    half = rows // 2
    if kind == "attn":
        shapes = (
            (planes, 2, 2, rows),
            (planes, 2, 2, rows),
            (planes, 2, 2, half),
            (planes, 2, half),
            (planes, rows),
            (far, planes, rows),
        )
    else:
        shapes = (
            (planes, 2, 4, rows),
            (planes, 2, 4, rows),
            (planes, 2, 2, rows),
            (planes, 2, rows),
            (planes, 2, rows),
            (far, planes, 2, rows),
            (planes, 2, rows),
        )
    pair = (planes, 2)
    one = (planes,)
    sems = (one, one, one, pair, pair, pair, pair, one, one, (far, planes), (far, planes))
    return [pltpu.VMEM(shape + (D,), dtype) for shape in shapes] + [dma(shape) for shape in sems]


def z_scratch(rows, count, dp_count, dtype):
    planes = count // 2
    far = max(1, dp_count.bit_length() - 3)
    dma = pltpu.SemaphoreType.DMA
    shapes = ((planes, rows), (planes, rows), (far, planes, rows))
    sems = ((planes,), (planes,), (far, planes), (far, planes))
    return [pltpu.VMEM(shape + (D,), dtype) for shape in shapes] + [dma(shape) for shape in sems]


Z_REFS = 3
Z_SEMS = 4


def reduce_kernel(
    count,
    attn_grad_ref,
    attn_done_ref,
    feed_low_ref,
    feed_high_ref,
    dout_ref,
    din_ref,
    vec0_ref,
    vec1_ref,
    vec2_ref,
    vec3_ref,
    outer_ref,
    whole_ref,
    own_ref,
    small_out,
    square_out,
    small_ref,
    small_core,
    small_s,
    small_got,
    sq_seg,
    sq_dp,
    keep_s,
    give_s,
    last_send,
    last_recv,
    small_send,
    small_recv,
    whole_send,
    whole_recv,
    half_sem,
    sq_send,
    sq_recv,
    sqd_send,
    sqd_recv,
    *refs,
):
    carry = AttnCarry(attn_grad_ref, refs[:CARRY_REFS], refs[CARRY_REFS:])
    seg, dp, core, x, y, across_core, near, far = peers()
    across_x, across_y, across_both = near
    planes = count // 2
    plane = seg // 2
    group = 2 * y + x
    targets = [{"seg": other} for other in others(seg, count)] + list(near) + list(far)
    hail(targets)
    carry.load_all()
    own_ref[1] = attn_done_ref[...]

    @pl.when(x == y)
    def _():
        keep_s[...] = feed_high_ref[...]
        give_s[...] = feed_low_ref[...]

    @pl.when(x != y)
    def _():
        keep_s[...] = feed_low_ref[...]
        give_s[...] = feed_high_ref[...]

    own_ref[2 + y] = keep_s[0]
    own_ref[4 + x] = keep_s[1]
    last = (
        remote(give_s.at[0], own_ref.at[2 + y], last_send.at[0], last_recv.at[0], across_y),
        remote(give_s.at[1], own_ref.at[4 + x], last_send.at[1], last_recv.at[1], across_x),
    )

    inputs = din_ref.shape[0]
    small_ref[0:inputs, :] = din_ref[...]
    for place, ref in enumerate((vec0_ref, vec1_ref, vec2_ref, vec3_ref, outer_ref)):
        small_ref[inputs + 8 * place : inputs + 8 * place + 8, :] = ref[...]
    small_ref[inputs + 40 :, :] = jnp.zeros((SMALL - inputs - 40, D), f32)
    meet(targets)
    def small_steps():
        copy = remote(small_ref, small_core, small_send.at[0], small_recv.at[0], across_core)
        copy.start()
        yield
        copy.wait()
        small_s[...] = small_ref[...] + small_core[...]
        half = pl.ds(pl.multiple_of(core * (SMALL // 2), 8), SMALL // 2)
        targets = [across_x, across_y] + far
        step = 1
        while step < planes:
            targets.append({"seg": seg + 2 * step - 4 * step * ((plane // step) % 2)})
            step *= 2
        for place, target in enumerate(targets):
            copy = remote(
                small_s.at[half],
                small_got.at[place],
                small_send.at[place + 1],
                small_recv.at[place + 1],
                target,
            )
            copy.start()
            yield
            copy.wait()
            small_s[half, :] += small_got[place]
        small_out[half, :] = small_s[half, :]
        last = len(targets) + 1
        copy = remote(small_out.at[half], small_out.at[half], small_send.at[last], small_recv.at[last], across_core)
        copy.start()
        yield
        copy.wait()

    small_run = small_steps()
    next(small_run)
    carry.send_all()
    for copy in last:
        copy.start()
    roles = owners(count)

    def gift(place):
        first, width, owner, spot = roles[place]
        return remote(
            own_ref.at[first : first + width],
            whole_ref.at[seg, spot : spot + width],
            whole_send.at[place],
            whole_recv.at[seg],
            {"seg": owner},
        )

    def give(place):
        first, width, owner, spot = roles[place]

        @pl.when(seg != owner)
        def _():
            gift(place).start()

        @pl.when(seg == owner)
        def _():
            whole_ref[seg, spot : spot + width] = own_ref[first : first + width]

    acts = [
        [("b", step) for step in range(planes - 1)],
        [("m", 0), ("b", planes - 1)],
        [("m", 1)],
        [("m", 2), ("e", 0)],
        [("m", step) for step in range(3, planes)],
    ] + [[("e", step)] for step in range(1, planes)]
    give(1)
    next(small_run)
    for turn, part in enumerate(acts):
        carry.run(part)
        if turn == 0:
            for copy in last:
                copy.wait()
            for place in (2, 3):
                give(place)
        next(small_run, None)
    own_ref[0] = carry.total()
    give(0)
    for _ in small_run:
        pass
    shard = dout_ref[...].astype(f32)
    square = jnp.sum(jnp.sum(shard * shard, 0, keepdims=True), 1, keepdims=True)
    for unit in range(UNITS):
        value = own_ref[unit].astype(f32)
        square = square + jnp.sum(jnp.sum(value * value, 0, keepdims=True), 1, keepdims=True)
    sq_seg[seg] = jnp.broadcast_to(square, (8, 128))
    for step, other in enumerate(others(seg, count)):
        remote(sq_seg.at[seg], sq_seg.at[seg], sq_send.at[step], sq_recv.at[seg], {"seg": other}).start()

    def halves_copy(spot):
        span = slice(spot, spot + 2)
        return remote(whole_ref.at[:, span], whole_ref.at[:, span], half_sem.at[0], half_sem.at[1], across_core)

    for place, (first, width, owner, spot) in enumerate(roles):
        if width == 2:

            @pl.when(seg == owner)
            def _():
                for other in others(seg, count):
                    wait_bytes(whole_ref.at[other, spot : spot + width], whole_recv.at[other])
                halves_copy(spot).start()

    for other in others(seg, count):
        wait_bytes(sq_seg.at[other], sq_recv.at[other])
    sq_dp[group] = jnp.sum(sq_seg[...], 0)
    for place, target in enumerate(near):
        remote(sq_dp.at[group], sq_dp.at[group], sqd_send.at[place], sqd_recv.at[place], target).start()
    sums = small_out[...]
    is_loss = lax.broadcasted_iota(jnp.int32, (SMALL, D), 0) == inputs + 37
    sums = jnp.where(is_loss, 0.0, sums)
    small_square = jnp.sum(jnp.sum(sums * sums, 0, keepdims=True), 1, keepdims=True)
    for place, target in enumerate(near):
        remote(sq_dp.at[group], sq_dp.at[group], sqd_send.at[place], sqd_recv.at[place], target).wait()
    square_out[...] = jnp.sum(sq_dp[...], 0) + jnp.broadcast_to(small_square, (8, 128))

    for place, (first, width, owner, spot) in enumerate(roles):

        @pl.when(seg == owner)
        def _():
            if width == 2:
                halves_copy(spot).wait()
            else:
                for other in others(seg, count):
                    wait_bytes(whole_ref.at[other, spot : spot + width], whole_recv.at[other])

    carry.drain()
    for place, (first, width, owner, spot) in enumerate(roles):

        @pl.when(seg != owner)
        def _():
            gift(place).wait_send()

    for step in range(count - 1):
        wait_bytes(sq_seg.at[0], sq_send.at[step])


def reduce_grads(count, dp_count, attn, done, feed_low, feed_high, dout, pieces):
    rows = D // count
    planes = count // 2
    stages = 2 + planes.bit_length() + max(0, dp_count.bit_length() - 3)
    dma = pltpu.SemaphoreType.DMA
    vmem = pl.BlockSpec(memory_space=pltpu.VMEM)
    return pl.pallas_call(
        functools.partial(reduce_kernel, count),
        out_shape=[
            jax.ShapeDtypeStruct((count, 4, rows, D), bf16),
            jax.ShapeDtypeStruct((UNITS, rows, D), bf16),
            jax.ShapeDtypeStruct((SMALL, D), f32),
            jax.ShapeDtypeStruct((8, 128), f32),
        ],
        in_specs=[pl.BlockSpec(memory_space=pl.ANY)] + [vmem] * 10,
        out_specs=[vmem] * 4,
        scratch_shapes=[
            pltpu.VMEM((SMALL, D), f32),
            pltpu.VMEM((SMALL, D), f32),
            pltpu.VMEM((SMALL, D), f32),
            pltpu.VMEM((stages, SMALL // 2, D), f32),
            pltpu.VMEM((count, 8, 128), f32),
            pltpu.VMEM((GROUPS, 8, 128), f32),
            pltpu.VMEM((2, rows, D), bf16),
            pltpu.VMEM((2, rows, D), bf16),
            dma((2,)),
            dma((2,)),
            dma((stages + 2,)),
            dma((stages + 2,)),
            dma((4,)),
            dma((count,)),
            dma((2,)),
            dma((count,)),
            dma((count,)),
            dma((3,)),
            dma((3,)),
        ]
        + carry_scratch("attn", rows, count, dp_count),
        compiler_params=pltpu.CompilerParams(
            collective_id=1, has_side_effects=True, vmem_limit_bytes=VMEM_LIMIT
        ),
        cost_estimate=pl.CostEstimate(flops=10**8, bytes_accessed=10**8, transcendentals=0),
        name="reduce_grads",
    )(attn.reshape(2, 2, count, rows, D), done, feed_low, feed_high, dout, *pieces)


def halves(value):
    high = value.astype(bf16)
    return high, (value - high.astype(f32)).astype(bf16)


def times(left, right):
    (left_high, left_low), (right_high, right_low) = left, right
    return dot_nn(
        jnp.concatenate([left_high, left_high, left_low], 1),
        jnp.concatenate([right_high, right_low, right_high], 0),
    )


def mirrored(first, second, third):
    return jnp.concatenate(
        [
            jnp.concatenate([first, second], 1),
            jnp.concatenate([jnp.transpose(second), third], 1),
        ],
        0,
    )


def times_even(left, right):
    (left_high, left_low), (right_high, right_low) = left, right
    wide = jnp.concatenate([left_high, left_high, left_low], 1)
    tall = jnp.concatenate([right_high, right_low, right_high], 0)
    return mirrored(
        dot_nn(wide[:HALF], tall[:, :HALF]),
        dot_nn(wide[:HALF], tall[:, HALF:]),
        dot_nn(wide[HALF:], tall[:, HALF:]),
    )


def gram_of(both):
    high, low = both
    wide = jnp.concatenate([high, high, low], 1)
    tall = jnp.concatenate([high, low, high], 1)
    return mirrored(
        dot_nt(wide[:HALF], tall[:HALF]),
        dot_nt(wide[:HALF], tall[HALF:]),
        dot_nt(wide[HALF:], tall[HALF:]),
    )


def clip_of(norm):
    return jnp.minimum(1.0, 0.25 / (norm + 1e-06))


def muon_kernel(
    count,
    square_ref,
    whole_ref,
    mom_ref,
    own_ref,
    update_ref,
    every_ref,
    norm_ref,
    made_ref,
    x_s,
    q_s,
    gram_s,
    high_s,
    low_s,
    send,
    recv,
    on_send,
    on_recv,
    own_send,
    own_recv,
):
    seg, dp, core, x, y, across_core, near, far = peers()
    group = 2 * y + x
    plane = seg // 2
    targets = [{"seg": other} for other in others(seg, count)] + list(near)
    hail(targets)
    is_down = group >= 2
    norm = jnp.sqrt(square_ref[0:1, 0:1])
    norm_ref[...] = jnp.broadcast_to(norm, norm_ref.shape)
    clip = clip_of(norm)
    eye = (
        lax.broadcasted_iota(jnp.int32, (D, D), 0) == lax.broadcasted_iota(jnp.int32, (D, D), 1)
    ).astype(f32)
    rows = whole_ref.shape[2]
    makers = [attn for _, _, attn, _ in owners(count)]
    units = [makers[0], makers[1], makers[2], makers[2], makers[3], makers[3]]

    def own_rows(side):
        return remote(own_ref, every_ref.at[group], own_send.at[side], own_recv.at[side], near[side])

    def gift(unit, slot, other):
        return remote(
            made_ref.at[other, slot],
            update_ref.at[group, unit],
            send.at[slot, other],
            recv.at[unit],
            {"seg": other},
        )

    def give(unit, slot):
        for other in others(seg, count):
            gift(unit, slot, other).start()
        update_ref[group, unit] = made_ref[seg, slot]

    def onward(unit, side):
        block = update_ref.at[group, unit]
        return remote(block, block, on_send.at[side, unit], on_recv.at[side, unit], near[side])

    meet(targets)
    for side in range(3):
        own_rows(side).start()
    every_ref[group] = own_ref[...]

    @pl.when(plane == count // 4 - 1)
    def _():
        start = (0.5 * mom_ref[:, core].astype(f32)).reshape(D, D)
        start = start + clip * whole_ref[:, 0].astype(f32).reshape(D, D)
        size = jnp.sum(jnp.sum(start * start, 0, keepdims=True), 1, keepdims=True)
        x_s[...] = start / (jnp.sqrt(size) + 1e-07)

        def sweep(_, carry):
            value = x_s[...]
            both = halves(value)
            gram = gram_of(both)
            gram_both = halves(gram)
            poly = -4.775 * gram + 2.0315 * times_even(gram_both, gram_both)
            x_s[...] = 3.4445 * value + times(halves(poly), both)
            return carry

        lax.fori_loop(0, 5, sweep, 0)
        made_ref[:, 0] = x_s[...].astype(bf16).reshape(count, rows, D)
        for unit in range(2):

            @pl.when(core == unit)
            def _():
                give(unit, 0)

    @pl.when(plane == count // 4)
    def _():
        gram_s[...] = jnp.zeros_like(gram_s)

        def gather(tile, size):
            value = (0.5 * mom_ref[:, 2 + tile].astype(f32)).reshape(D, D)
            value = value + clip * whole_ref[:, tile].astype(f32).reshape(D, D)
            high, low = halves(value)
            high_s[tile] = high
            low_s[tile] = low

            @pl.when(is_down)
            def _():
                high_s[tile] = jnp.transpose(high_s[tile])
                low_s[tile] = jnp.transpose(low_s[tile])

            both = high_s[tile], low_s[tile]
            gram_s[...] += gram_of(both)
            return size + jnp.sum(jnp.sum(value * value, 0, keepdims=True), 1, keepdims=True)

        size = lax.fori_loop(0, 4, gather, jnp.zeros((1, 1), f32))
        scale = 1.0 / (jnp.sqrt(size) + 1e-07)
        gram_s[...] = gram_s[...] * (scale * scale)

        def poly_of(gram, gram_both):
            return 3.4445 * eye - 4.775 * gram + 2.0315 * times_even(gram_both, gram_both)

        def advance(gram_both, poly_both):
            gram_s[...] = times_even(halves(times_even(gram_both, poly_both)), poly_both)

        gram = gram_s[...]
        gram_both = halves(gram)
        poly = poly_of(gram, gram_both)
        q_s[...] = poly
        advance(gram_both, halves(poly))

        def sweep(_, carry):
            gram = gram_s[...]
            gram_both = halves(gram)
            poly_both = halves(poly_of(gram, gram_both))
            q_s[...] = times_even(halves(q_s[...]), poly_both)
            advance(gram_both, poly_both)
            return carry

        lax.fori_loop(0, 3, sweep, 0)
        gram = gram_s[...]
        last = times_even(halves(q_s[...]), halves(poly_of(gram, halves(gram)))) * scale
        last_both = halves(last)
        for slot in range(2):
            tile = 2 * core + slot
            x_s[...] = times(last_both, (high_s[tile], low_s[tile]))

            @pl.when(is_down)
            def _():
                x_s[...] = jnp.transpose(x_s[...])

            made_ref[:, slot] = x_s[...].astype(bf16).reshape(count, rows, D)
            for half in range(2):

                @pl.when(core == half)
                def _():
                    give(2 + 2 * half + slot, slot)

    for unit in (0, 1, 2, 4, 3, 5):

        @pl.when(seg != units[unit])
        def _():
            wait_bytes(update_ref.at[group, unit], recv.at[unit])

        for side in range(3):
            onward(unit, side).start()
    for side in range(3):
        own_rows(side).wait()
    for unit in range(UNITS):
        for side in range(3):
            onward(unit, side).wait()

        @pl.when(seg == units[unit])
        def _():
            slot = 0 if unit < 2 else unit % 2
            for other in others(seg, count):
                gift(unit, slot, other).wait_send()


def muon(count, squares, whole, momenta, own):
    rows = whole.shape[2]
    dma = pltpu.SemaphoreType.DMA
    vmem = pl.BlockSpec(memory_space=pltpu.VMEM)
    blocks = jax.ShapeDtypeStruct((GROUPS, UNITS, rows, D), bf16)
    return pl.pallas_call(
        functools.partial(muon_kernel, count),
        out_shape=[blocks, blocks, jax.ShapeDtypeStruct((8, 128), f32)],
        in_specs=[vmem] * 4,
        out_specs=[vmem] * 3,
        scratch_shapes=[
            pltpu.VMEM((count, 2, rows, D), bf16),
            pltpu.VMEM((D, D), f32),
            pltpu.VMEM((D, D), f32),
            pltpu.VMEM((D, D), f32),
            pltpu.VMEM((4, D, D), bf16),
            pltpu.VMEM((4, D, D), bf16),
            dma((2, count)),
            dma((UNITS,)),
            dma((3, UNITS)),
            dma((3, UNITS)),
            dma((3,)),
            dma((3,)),
        ],
        compiler_params=pltpu.CompilerParams(
            collective_id=2, has_side_effects=True, vmem_limit_bytes=VMEM_LIMIT
        ),
        cost_estimate=pl.CostEstimate(flops=2 * 10**10, bytes_accessed=4 * 10**7, transcendentals=0),
        name="muon",
    )(squares, whole, momenta, own)


def embed_kernel(
    count,
    frames_ref,
    mask_ref,
    in_ref,
    outer_ref,
    attn_mom_ref,
    up_mom_ref,
    down_mom_ref,
    x_ref,
    mem_ref,
    total_ref,
    owned_ref,
    got_s,
    count_s,
    mom_s,
    mom_sem,
    frame_send,
    frame_recv,
    count_send,
    count_recv,
):
    seg = lax.axis_index("seg")
    after, before = lax.rem(seg + 1, count), lax.rem(seg + count - 1, count)
    streams = frames_ref.shape[0]
    group = lax.rem(lax.axis_index("dp"), GROUPS)
    for depth in range(LAYERS):
        pltpu.make_async_copy(attn_mom_ref.at[depth, group], mom_s.at[depth], mom_sem.at[0]).start()

        @pl.when(group == FEED_UP[depth])
        def _():
            for tile in range(4):
                source = up_mom_ref.at[depth, :, pl.ds(tile * TILE, TILE)]
                pltpu.make_async_copy(source, mom_s.at[2 + tile], mom_sem.at[0]).start()

        @pl.when(group == FEED_DOWN[depth])
        def _():
            pltpu.make_async_copy(down_mom_ref.at[depth], mom_s.at[2:6], mom_sem.at[0]).start()

    tally = jnp.sum(mask_ref[...].astype(f32), 1, keepdims=True)
    count_s[seg] = jnp.broadcast_to(
        jnp.concatenate([tally, jnp.zeros((8 - streams, 1), f32)], 0), (8, 128)
    )
    greet(seg, count, (), ())
    frame_copy = remote(frames_ref, got_s, frame_send.at[0], frame_recv.at[0], {"seg": after})
    frame_copy.start()
    for step, other in enumerate(others(seg, count)):
        remote(count_s.at[seg], count_s.at[seg], count_send.at[step], count_recv.at[seg], {"seg": other}).start()
    weight, shift = in_ref[...], outer_ref[0:1, :]
    for stream in range(streams):
        x_ref[stream] = dot_nn(jnp.transpose(frames_ref[stream]), weight) + shift
    wait_bytes(mom_s, mom_sem.at[0])
    owned_ref[...] = mom_s[...].astype(bf16)
    frame_copy.wait()
    for stream in range(streams):
        mem_ref[stream] = (dot_nn(jnp.transpose(got_s[stream]), weight) + shift).astype(bf16)
    for other in others(seg, count):
        wait_bytes(count_s.at[other], count_recv.at[other])
    total_ref[...] = jnp.sum(count_s[...], 0)
    for step in range(count - 1):
        wait_bytes(count_s.at[0], count_send.at[step])


def embed(count, frames, mask, in_weight, outer_vectors, attn_mom, up_mom, down_mom):
    streams = frames.shape[0]
    rows = D // count
    dma = pltpu.SemaphoreType.DMA
    return pl.pallas_call(
        functools.partial(embed_kernel, count),
        out_shape=[
            jax.ShapeDtypeStruct((streams, SEG, D), f32),
            jax.ShapeDtypeStruct((streams, SEG, D), bf16),
            jax.ShapeDtypeStruct((8, 128), f32),
            jax.ShapeDtypeStruct((UNITS, rows, D), bf16),
        ],
        in_specs=[pl.BlockSpec(memory_space=pltpu.VMEM)] * 4 + [pl.BlockSpec(memory_space=pl.ANY)] * 3,
        out_specs=[pl.BlockSpec(memory_space=pltpu.VMEM)] * 4,
        scratch_shapes=[
            pltpu.VMEM(frames.shape, bf16),
            pltpu.VMEM((count, 8, 128), f32),
            pltpu.VMEM((UNITS, rows, D), f32),
            dma((1,)),
            dma((1,)),
            dma((1,)),
            dma((count,)),
            dma((count,)),
        ],
        compiler_params=pltpu.CompilerParams(
            collective_id=3, has_side_effects=True, vmem_limit_bytes=VMEM_LIMIT
        ),
        cost_estimate=pl.CostEstimate(flops=2 * 10**8, bytes_accessed=4 * 10**6, transcendentals=0),
        name="embed",
    )(frames, mask, in_weight, outer_vectors, attn_mom, up_mom, down_mom.reshape(LAYERS, 4, rows, D))


FEED_UP = (1, 0)
FEED_DOWN = (2, 3)
KEEP = 1.0 - 0.3 * 0.01


def finish_kernel(norm_ref, every_ref, update_ref, dout_ref, small_ref, *refs):
    (
        attn_ref,
        attn_mom_ref,
        up_ref,
        up_mom_ref,
        down_ref,
        down_mom_ref,
        out_ref,
        out_mom_ref,
        out_sec_ref,
        in_ref,
        in_mom_ref,
        in_sec_ref,
        vec_ref,
        vec_mom_ref,
        vec_sec_ref,
        outer_ref,
        outer_mom_ref,
        outer_sec_ref,
        attn_new,
        attn_mom_new,
        attn_copy_new,
        up_new,
        up_mom_new,
        up_copy_new,
        down_new,
        down_mom_new,
        down_copy_new,
        out_new,
        out_mom_new,
        out_sec_new,
        out_copy_new,
        in_new,
        in_mom_new,
        in_sec_new,
        in_copy_new,
        vec_new,
        vec_mom_new,
        vec_sec_new,
        outer_new,
        outer_mom_new,
        outer_sec_new,
        loss_new,
        norm_new,
    ) = refs
    clip = clip_of(norm_ref[0:1, 0:1])

    def muon_step(weight, momentum, grad, update, scale):
        weight = weight * KEEP - (0.3 * scale) * update.astype(f32)
        return weight, 0.5 * momentum + clip * grad.astype(f32)

    up_scale, down_scale = max(1.0, FF / D) ** 0.5, max(1.0, D / FF) ** 0.5
    for depth in range(LAYERS):
        for kind in range(4):
            weight, momentum = muon_step(
                attn_ref[depth, kind],
                attn_mom_ref[depth, kind],
                every_ref[kind, depth],
                update_ref[kind, depth],
                1.0,
            )
            attn_new[depth, kind] = weight
            attn_mom_new[depth, kind] = momentum
            attn_copy_new[depth, kind] = weight.astype(bf16)
            columns = slice(kind * TILE, (kind + 1) * TILE)
            weight, momentum = muon_step(
                up_ref[depth, :, columns],
                up_mom_ref[depth, :, columns],
                every_ref[FEED_UP[depth], 2 + kind],
                update_ref[FEED_UP[depth], 2 + kind],
                up_scale,
            )
            up_new[depth, :, columns] = weight
            up_mom_new[depth, :, columns] = momentum
            up_copy_new[depth, :, columns] = weight.astype(bf16)
            weight, momentum = muon_step(
                down_ref[depth, kind],
                down_mom_ref[depth, kind],
                every_ref[FEED_DOWN[depth], 2 + kind],
                update_ref[FEED_DOWN[depth], 2 + kind],
                down_scale,
            )
            down_new[depth, kind] = weight
            down_mom_new[depth, kind] = momentum
            down_copy_new[depth, kind] = weight.astype(bf16)
    for low in range(2):
        for right in range(2):
            columns = slice(right * D, (right + 1) * D)
            weight, moment, second = adamw(
                out_ref[low, :, columns],
                out_mom_ref[low, :, columns],
                out_sec_ref[low, :, columns],
                dout_ref[2 * right + low].astype(f32) * clip,
                0.05,
                0.01,
            )
            out_new[low, :, columns] = weight
            out_mom_new[low, :, columns] = moment
            out_sec_new[low, :, columns] = second
            out_copy_new[low, :, columns] = weight.astype(bf16)

    @pl.when(pl.program_id(0) == 0)
    def _():
        inputs = in_ref.shape[0]
        weight, moment, second = adamw(
            in_ref[...], in_mom_ref[...], in_sec_ref[...], small_ref[0:inputs, :] * clip, 0.05, 0.01
        )
        in_new[...] = weight
        in_mom_new[...] = moment
        in_sec_new[...] = second
        in_copy_new[...] = weight.astype(bf16)

        norm_new[...] = norm_ref[0:1, 0:1]
        loss_new[...] = small_ref[inputs + 37 : inputs + 38, 0:1]

        def rows_of(first, last, base):
            return small_ref[inputs + base + first : inputs + base + last, :]

        for depth in range(LAYERS):
            base = 16 * depth
            for low, high, grad in (
                (0, 2, rows_of(0, 2, base)),
                (2, 4, rows_of(0, 2, base + 8)),
                (4, 7, rows_of(2, 5, base)),
                (7, 8, rows_of(2, 3, base + 8)),
                (8, 12, rows_of(4, 8, base + 8)),
            ):
                weight, moment, second = adamw(
                    vec_ref[low:high, depth],
                    vec_mom_ref[low:high, depth],
                    vec_sec_ref[low:high, depth],
                    grad * clip,
                    0.25,
                    0.0,
                )
                vec_new[low:high, depth] = weight
                vec_mom_new[low:high, depth] = moment
                vec_sec_new[low:high, depth] = second
        for low, high, grad in ((0, 1, rows_of(5, 6, 0)), (1, 5, rows_of(1, 5, 32))):
            weight, moment, second = adamw(
                outer_ref[low:high, :], outer_mom_ref[low:high, :], outer_sec_ref[low:high, :], grad * clip, 0.25, 0.0
            )
            outer_new[low:high, :] = weight
            outer_mom_new[low:high, :] = moment
            outer_sec_new[low:high, :] = second


def finish(rows, norm, every, updates, dout, small, arrays):
    steps = rows // 16
    attn, _, up, _, down, _, out, _, _, inp, _, _, vec, _, _, outer, _, _ = arrays
    codes = out.shape[2]
    part = out.shape[1] // steps
    blocks = pl.BlockSpec((GROUPS, UNITS, 16, D), lambda i: (0, 0, i, 0))
    attn_spec = pl.BlockSpec((LAYERS, 4, 16, D), lambda i: (0, 0, i, 0))
    up_spec = pl.BlockSpec((LAYERS, 16, FF), lambda i: (0, i, 0))
    out_spec = pl.BlockSpec((2, part, codes), lambda i: (0, i, 0))
    dout_spec = pl.BlockSpec((GROUPS, part, D), lambda i: (0, i, 0))
    in_spec, vec_spec, outer_spec = whole_spec(inp.shape), whole_spec(vec.shape), whole_spec(outer.shape)

    def like(array, dtype=f32):
        return jax.ShapeDtypeStruct(array.shape, dtype)

    return pl.pallas_call(
        finish_kernel,
        grid=(steps,),
        out_shape=[like(attn), like(attn), like(attn, bf16)]
        + [like(up), like(up), like(up, bf16)]
        + [like(down), like(down), like(down, bf16)]
        + [like(out)] * 3
        + [like(out, bf16)]
        + [like(inp)] * 3
        + [like(inp, bf16)]
        + [like(vec)] * 3
        + [like(outer)] * 3
        + [jax.ShapeDtypeStruct((1, 1), f32)] * 2,
        in_specs=[whole_spec((8, 128)), blocks, blocks, dout_spec, whole_spec(small.shape)]
        + [attn_spec] * 2
        + [up_spec] * 2
        + [attn_spec] * 2
        + [out_spec] * 3
        + [in_spec] * 3
        + [vec_spec] * 3
        + [outer_spec] * 3,
        out_specs=[attn_spec] * 3
        + [up_spec] * 3
        + [attn_spec] * 3
        + [out_spec] * 4
        + [in_spec] * 4
        + [vec_spec] * 3
        + [outer_spec] * 3
        + [whole_spec((1, 1))] * 2,
        compiler_params=pltpu.CompilerParams(vmem_limit_bytes=VMEM_LIMIT),
        cost_estimate=pl.CostEstimate(flops=10**8, bytes_accessed=4 * 10**7, transcendentals=0),
        name="finish",
    )(norm, every, updates, dout, small, *arrays)


def local(
    frames,
    speech_mask,
    targets,
    in_proj,
    in_moment,
    in_second,
    out_proj,
    out_moment,
    out_second,
    layer_vectors,
    vectors_moment,
    vectors_second,
    outer_vectors,
    outer_moment,
    outer_second,
    attn_proj,
    attn_momentum,
    ff_up,
    up_momentum,
    ff_down,
    down_momentum,
    in_copy,
    out_copy,
    attn_copy,
    up_copy,
    down_copy,
):
    segment = lax.axis_index("seg")
    count, dp_count = lax.axis_size("seg"), lax.axis_size("dp")
    rows = D // count
    streams = frames.shape[0]
    stream_total = streams * dp_count
    frames_t = jnp.swapaxes(frames, 1, 2)
    bias = jnp.where(segment > 0, 0.0, -1e30).astype(f32)[None]
    hidden, memory, totals, owned = embed(
        count, frames_t, speech_mask, in_copy, outer_vectors, attn_momentum, up_momentum, down_momentum
    )
    momenta = lax.all_gather(owned, "seg", axis=0, tiled=False)
    memory = [memory] * streams
    kept = []
    for depth in range(LAYERS):
        saved, passed = None, []
        for stream in range(streams):
            saved, short = forward_layer(
                depth,
                stream,
                streams,
                bias,
                hidden,
                memory[stream],
                attn_copy,
                up_copy,
                down_copy,
                layer_vectors,
                saved,
            )
            if depth + 1 < LAYERS:
                passed.append(from_behind(short, "seg", 1))
        kept.append((hidden, saved[8], saved))
        hidden = saved[0]
        memory = passed
    grad_hidden, grad_out, head_outer = head(
        hidden, targets, speech_mask, totals, out_copy, outer_vectors, 1.0 / stream_total, momenta
    )
    vector_grads, feed_done = [], [None, None]
    carried = grad_out.reshape(GROUPS * D // 2, D)
    carried_done = []
    for depth in reversed(range(LAYERS)):
        entering, held, saved = kept[depth]
        dafter, grad_up, grad_down, feed_vec, sums = feed_back(
            depth, grad_hidden, saved[7], up_copy, down_copy, layer_vectors, count, dp_count, carried
        )
        grad_hidden, grad_attn, attn_vec, grad_in, feed_done[depth], done = attend_back(
            depth,
            bias,
            dafter,
            entering,
            held,
            saved[1:7],
            attn_copy,
            layer_vectors,
            frames_t,
            grad_up,
            grad_down,
            sums,
            count,
            dp_count,
        )
        carried_done.append(done)
        carried = grad_attn.reshape(4 * D, D)
        vector_grads = [attn_vec, feed_vec] + vector_grads
    out_done, attn_done = carried_done
    every_out = lax.all_gather(out_done, ("dp", "seg"), axis=0, tiled=True)[: GROUPS * D // 2]
    every_out = every_out.reshape(GROUPS, D // 2, D)
    whole, own, small, squares = reduce_grads(
        count,
        dp_count,
        grad_attn,
        attn_done,
        feed_done[0],
        feed_done[1],
        out_done,
        [grad_in] + vector_grads + [head_outer],
    )
    updates, every, norm = muon(count, squares, whole, momenta, own)
    split = (LAYERS, 4, rows, D)
    halved = (2, D // 2, out_proj.shape[1])
    (
        attn_new,
        attn_mom,
        attn_copy_new,
        up_new,
        up_mom,
        up_copy_new,
        down_new,
        down_mom,
        down_copy_new,
        out_new,
        out_moment_new,
        out_second_new,
        out_copy_new,
        in_new,
        in_moment_new,
        in_second_new,
        in_copy_new,
        vectors_new,
        vectors_moment_new,
        vectors_second_new,
        outer_new,
        outer_moment_new,
        outer_second_new,
        loss_sum,
        norm,
    ) = finish(
        rows,
        norm,
        every,
        updates,
        every_out,
        small,
        [
            attn_proj,
            attn_momentum,
            ff_up,
            up_momentum,
            ff_down.reshape(split),
            down_momentum.reshape(split),
            out_proj.reshape(halved),
            out_moment.reshape(halved),
            out_second.reshape(halved),
            in_proj,
            in_moment,
            in_second,
            jnp.swapaxes(layer_vectors, 0, 1),
            jnp.swapaxes(vectors_moment, 0, 1),
            jnp.swapaxes(vectors_second, 0, 1),
            outer_vectors,
            outer_moment,
            outer_second,
        ],
    )
    return (
        loss_sum.reshape(()),
        norm.reshape(()),
        in_new,
        in_moment_new,
        in_second_new,
        out_new.reshape(out_proj.shape),
        out_moment_new.reshape(out_proj.shape),
        out_second_new.reshape(out_proj.shape),
        jnp.swapaxes(vectors_new, 0, 1),
        jnp.swapaxes(vectors_moment_new, 0, 1),
        jnp.swapaxes(vectors_second_new, 0, 1),
        outer_new,
        outer_moment_new,
        outer_second_new,
        attn_new,
        attn_mom,
        up_new,
        up_mom,
        down_new.reshape(ff_down.shape),
        down_mom.reshape(ff_down.shape),
        in_copy_new,
        out_copy_new.reshape(out_proj.shape),
        attn_copy_new,
        up_copy_new,
        down_copy_new.reshape(ff_down.shape),
    )


def solution(mesh):
    return jax.shard_map(
        local,
        mesh=mesh,
        in_specs=(
            P("dp", "seg", None),
            P("dp", "seg"),
            P("dp", "seg"),
            P(),
            P(),
            P(),
            P(),
            P(),
            P(),
            P(),
            P(),
            P(),
            P(),
            P(),
            P(),
            P(None, None, "seg", None),
            P(None, None, "seg", None),
            P(None, "seg", None),
            P(None, "seg", None),
            P(None, "seg", None),
            P(None, "seg", None),
            P(),
            P(),
            P(),
            P(),
            P(),
        ),
        out_specs=(
            P(),
            P(),
            P(),
            P(),
            P(),
            P(),
            P(),
            P(),
            P(),
            P(),
            P(),
            P(),
            P(),
            P(),
            P(None, None, "seg", None),
            P(None, None, "seg", None),
            P(None, "seg", None),
            P(None, "seg", None),
            P(None, "seg", None),
            P(None, "seg", None),
            P(),
            P(),
            P(None, None, "seg", None),
            P(None, "seg", None),
            P(None, "seg", None),
        ),
        check_vma=False,
    )
```

```python
import functools
import math

import jax
import jax.numpy as jnp
from jax import lax
from jax.experimental import pallas as pl
from jax.experimental.pallas import tpu as pltpu
from jax.sharding import PartitionSpec as P

D = 512
HEAD_DIM = 64
HEADS = D // HEAD_DIM
FF = 2048
LAYERS = 2
STEP = 10
SEG = 512
HALF = 256
PAIR = 2 * HEAD_DIM
TILE = 512
VMEM_LIMIT = 56 * 1024 * 1024
GELU_SCALE = math.sqrt(2.0 / math.pi)

f32 = jnp.float32
bf16 = jnp.bfloat16


def dot_nn(left, right):
    return lax.dot_general(left, right, (((1,), (0,)), ((), ())), preferred_element_type=f32)


def dot_nt(left, right):
    return lax.dot_general(left, right, (((1,), (1,)), ((), ())), preferred_element_type=f32)


def dot_tn(left, right):
    return lax.dot_general(left, right, (((0,), (0,)), ((), ())), preferred_element_type=f32)


def normalised(values):
    centred = values - jnp.mean(values, -1, keepdims=True)
    scale = lax.rsqrt(jnp.mean(centred * centred, -1, keepdims=True) + 1e-05)
    return centred * scale, scale


def norm_back(grad, gain, unit, scale):
    part = grad * gain
    mean_part = jnp.mean(part, -1, keepdims=True)
    mean_unit = jnp.mean(part * unit, -1, keepdims=True)
    return scale * (part - mean_part - unit * mean_unit)


def column_sum(values):
    return jnp.sum(values, 0, keepdims=True)


def head_masks():
    lane = lax.broadcasted_iota(jnp.int32, (1, PAIR), 1)
    return (lane < HEAD_DIM).astype(bf16), (lane >= HEAD_DIM).astype(bf16)


def pair_lanes(pair):
    return pl.ds(pl.multiple_of(pair * PAIR, PAIR), PAIR)


def forward_kernel(
    depth,
    stream,
    bias_ref,
    x_ref,
    mem_ref,
    attn_ref,
    up_ref,
    down_ref,
    vec_ref,
    *refs,
):
    (
        hid_ref,
        hid16_ref,
        keyin_out,
        q_out,
        k_out,
        v_out,
        lse_ref,
        mixed_ref,
        after_ref,
        kept_out,
        act_s,
        lse_s,
        up_s,
        down_s,
        keyin_ref,
        q_ref,
        k_ref,
        v_ref,
        in_sem,
        out_sem,
    ) = refs[-20:]
    weights_in = (
        pltpu.make_async_copy(up_ref.at[depth], up_s, in_sem.at[0]),
        pltpu.make_async_copy(down_ref.at[depth], down_s, in_sem.at[1]),
    )
    for copy in weights_in:
        copy.start()
    saved_out = [
        pltpu.make_async_copy(source, target.at[stream], out_sem.at[place])
        for place, (source, target) in enumerate(
            ((keyin_ref, keyin_out), (q_ref, q_out), (k_ref, k_out), (v_ref, v_out))
        )
    ]
    kept_out[...] = mem_ref[...]
    x = x_ref[...]
    own_unit, _ = normalised(x)
    gain, shift = vec_ref[0:1, :], vec_ref[1:2, :]
    normed = (own_unit * gain + shift).astype(bf16)
    mem_unit, _ = normalised(mem_ref[...].astype(f32))
    mem_normed = (mem_unit * gain + shift).astype(bf16)
    keyin_ref[0:SEG, :] = mem_normed
    keyin_ref[SEG:, :] = normed
    q_ref[...] = (dot_nn(normed, attn_ref[0]) + vec_ref[4:5, :]).astype(bf16) * jnp.asarray(HEAD_DIM**-0.5, bf16)
    k_ref[0:SEG, :] = dot_nn(mem_normed, attn_ref[1]).astype(bf16)
    k_ref[SEG:, :] = dot_nn(normed, attn_ref[1]).astype(bf16)
    v_ref[0:SEG, :] = (dot_nn(mem_normed, attn_ref[2]) + vec_ref[5:6, :]).astype(bf16)
    v_ref[SEG:, :] = (dot_nn(normed, attn_ref[2]) + vec_ref[5:6, :]).astype(bf16)
    for copy in saved_out:
        copy.start()
    first, second = head_masks()
    memory_bias = bias_ref[0]
    lane = lax.broadcasted_iota(jnp.int32, (HALF, PAIR), 1)
    query_pos = lax.broadcasted_iota(jnp.int32, (2 * HALF, HALF), 0) % HALF
    key_pos = lax.broadcasted_iota(jnp.int32, (2 * HALF, HALF), 1)
    diagonal = key_pos <= query_pos
    lse_s[...] = jnp.zeros_like(lse_s)

    def pair_body(pair, carry):
        lanes = pair_lanes(pair)
        for block in range(2):
            rows = slice(block * HALF, (block + 1) * HALF)
            q_pair = q_ref[rows, lanes]
            q_both = jnp.concatenate([q_pair * first, q_pair * second], 0)
            spans = [(0, SEG, 0)]
            if block:
                spans.append((SEG, SEG + HALF, 1))
            spans.append((SEG + block * HALF, SEG + (block + 1) * HALF, 2))
            scores = []
            for low, high, kind in spans:
                part = dot_nt(q_both, k_ref[low:high, lanes])
                if kind == 2:
                    part = jnp.where(diagonal, part, -1e30)
                scores.append(part)
            peaks = [jnp.max(part, -1, keepdims=True) for part in scores]
            peaks[0] = peaks[0] + memory_bias
            most = functools.reduce(jnp.maximum, peaks)
            weights = [
                jnp.exp(part - (most if place else most - memory_bias)) for place, part in enumerate(scores)
            ]
            total = functools.reduce(jnp.add, [jnp.sum(part, -1, keepdims=True) for part in weights])
            mixed = functools.reduce(
                jnp.add,
                [
                    dot_nn(part.astype(bf16), v_ref[low:high, lanes])
                    for part, (low, high, kind) in zip(weights, spans)
                ],
            )
            mixed = mixed / total
            mixed_ref[rows, lanes] = jnp.where(lane < HEAD_DIM, mixed[:HALF], mixed[HALF:]).astype(bf16)
            lse = most + jnp.log(total)
            kept = jnp.where(lane == 2 * pair, lse[:HALF], lse_s[rows, :])
            lse_s[rows, :] = jnp.where(lane == 2 * pair + 1, lse[HALF:], kept)
        return carry

    lax.fori_loop(0, HEADS // 2, pair_body, 0)
    lse_ref[...] = jnp.transpose(lse_s[...])[0:HEADS, :]
    after = x + (dot_nn(mixed_ref[...], attn_ref[3]) + vec_ref[6:7, :])
    after_ref[...] = after
    unit, _ = normalised(after)
    normed_two = (unit * vec_ref[2:3, :] + vec_ref[3:4, :]).astype(bf16)
    for copy in weights_in:
        copy.wait()
    for tile in range(FF // TILE):
        columns = slice(tile * TILE, (tile + 1) * TILE)
        inner = dot_nn(normed_two, up_s[:, columns]) + vec_ref[8 + tile : 9 + tile, :]
        act_s[:, columns] = (
            0.5 * inner * (1.0 + jnp.tanh(GELU_SCALE * (inner + 0.044715 * inner * inner * inner)))
        ).astype(bf16)
    hidden = after + (dot_nn(act_s[...], down_s[...]) + vec_ref[7:8, :])
    hid_ref[...] = hidden
    hid16_ref[...] = hidden.astype(bf16)
    for copy in saved_out:
        copy.wait()


SAVED = (
    ((SEG, D), f32),
    ((2 * SEG, D), bf16),
    ((SEG, D), bf16),
    ((2 * SEG, D), bf16),
    ((2 * SEG, D), bf16),
    ((HEADS, SEG), f32),
    ((SEG, D), bf16),
    ((SEG, D), f32),
    ((SEG, D), bf16),
)


def whole_spec(shape):
    return pl.BlockSpec(shape, lambda *_: (0,) * len(shape))


def stream_spec(shape, stream=None):
    zeros = (0,) * len(shape)
    if stream is None:
        return pl.BlockSpec((None,) + shape, lambda i: (i,) + zeros)
    return pl.BlockSpec((None,) + shape, lambda i: (stream,) + zeros)


def layer_spec(shape, depth):
    zeros = (0,) * len(shape)
    return pl.BlockSpec((None,) + shape, lambda *_: (depth,) + zeros)


def forward_layer(depth, stream, streams, bias, hidden, memory, attn, upper, lower, vectors, earlier):
    saved_shapes = [jax.ShapeDtypeStruct((streams,) + shape, dtype) for shape, dtype in SAVED]
    saved_specs = [stream_spec(shape, stream) for shape, dtype in SAVED]
    out_shape = [saved_shapes[0], jax.ShapeDtypeStruct((SEG, D), bf16)] + saved_shapes[1:]
    out_specs = [saved_specs[0], whole_spec((SEG, D))] + saved_specs[1:]
    for place in (2, 3, 4, 5):
        out_specs[place] = pl.BlockSpec(memory_space=pl.ANY)
    operands = [bias, hidden, memory, attn, upper, lower, vectors]
    in_specs = [
        pl.BlockSpec(memory_space=pltpu.SMEM),
        stream_spec((SEG, D), stream),
        stream_spec((SEG, D), stream) if memory.ndim == 3 else whole_spec((SEG, D)),
        layer_spec(attn.shape[1:], depth),
        pl.BlockSpec(memory_space=pl.ANY),
        pl.BlockSpec(memory_space=pl.ANY),
        layer_spec(vectors.shape[1:], depth),
    ]
    aliases = {}
    if earlier is not None:
        for place, array in enumerate(earlier):
            aliases[len(operands)] = place if place == 0 else place + 1
            operands.append(array)
            in_specs.append(pl.BlockSpec(memory_space=pl.ANY))
    out = pl.pallas_call(
        functools.partial(forward_kernel, depth, stream),
        grid=(1,),
        out_shape=out_shape,
        in_specs=in_specs,
        out_specs=out_specs,
        scratch_shapes=[
            pltpu.VMEM((SEG, FF), bf16),
            pltpu.VMEM((SEG, PAIR), f32),
            pltpu.VMEM((D, FF), bf16),
            pltpu.VMEM((FF, D), bf16),
            pltpu.VMEM((2 * SEG, D), bf16),
            pltpu.VMEM((SEG, D), bf16),
            pltpu.VMEM((2 * SEG, D), bf16),
            pltpu.VMEM((2 * SEG, D), bf16),
            pltpu.SemaphoreType.DMA((2,)),
            pltpu.SemaphoreType.DMA((4,)),
        ],
        input_output_aliases=aliases,
        compiler_params=pltpu.CompilerParams(vmem_limit_bytes=VMEM_LIMIT),
        cost_estimate=pl.CostEstimate(flops=10**10, bytes_accessed=2 * 10**7, transcendentals=10**7),
        name="layer_forward",
    )(*operands)
    return [out[0]] + list(out[2:]), out[1]


def head_kernel(scale, x_ref, target_ref, mask_ref, total_ref, out_ref, outer_ref, mom_ref, g_ref, dout_ref, douter_ref, acc_s):
    step = pl.program_id(0)

    @pl.when(step == 0)
    def _():
        acc_s[...] = jnp.zeros_like(acc_s)
        douter_ref[...] = jnp.zeros_like(douter_ref)

    unit, rscale = normalised(x_ref[...])
    gain = outer_ref[1:2, :]
    normed = (unit * gain + outer_ref[2:3, :]).astype(bf16)
    shift = jnp.concatenate([outer_ref[3:4, :], outer_ref[4:5, :]], 1)
    logits = dot_nn(normed, out_ref[...]) + shift
    most = jnp.max(logits, -1, keepdims=True)
    powers = jnp.exp(logits - most)
    total = jnp.sum(powers, -1, keepdims=True)
    target_row = target_ref[pl.ds(step, 1), :].astype(f32)
    weight_row = mask_ref[pl.ds(step, 1), :].astype(f32) * (1.0 / total_ref[pl.ds(step, 1), 0:1])
    columns = jnp.transpose(jnp.concatenate([target_row, weight_row, jnp.zeros((6, SEG), f32)], 0))
    target, weight = columns[:, 0:1].astype(jnp.int32), columns[:, 1:2]
    chosen = lax.broadcasted_iota(jnp.int32, logits.shape, 1) == target
    picked = jnp.sum(jnp.where(chosen, logits, 0.0), -1, keepdims=True)
    loss = jnp.sum(weight * (most + jnp.log(total) - picked), 0, keepdims=True)
    spread = weight * scale
    dlogits = (powers * (spread / total) - jnp.where(chosen, spread, 0.0)).astype(bf16)
    acc_s[...] += dot_nn(jnp.transpose(normed), dlogits)
    bias_grad = column_sum(dlogits.astype(f32))
    dnormed = dot_nt(dlogits, out_ref[...])
    g_ref[...] = norm_back(dnormed, gain, unit, rscale)
    douter_ref[1:2, :] += column_sum(dnormed * unit)
    douter_ref[2:3, :] += column_sum(dnormed)
    douter_ref[3:4, :] += bias_grad[:, :D]
    douter_ref[4:5, :] += bias_grad[:, D:]
    douter_ref[5:6, :] += jnp.broadcast_to(loss, (1, D))

    @pl.when(step == pl.num_programs(0) - 1)
    def _():
        half = D // 2
        for right in range(2):
            for low in range(2):
                dout_ref[right, low] = acc_s[
                    low * half : (low + 1) * half, right * D : (right + 1) * D
                ]


def head(hidden, targets, mask, totals, out_weight, outer_vectors, scale, momenta):
    streams = hidden.shape[0]
    codes = out_weight.shape[1]
    return pl.pallas_call(
        functools.partial(head_kernel, scale),
        grid=(streams,),
        out_shape=[
            jax.ShapeDtypeStruct((streams, SEG, D), f32),
            jax.ShapeDtypeStruct((2, 2, D // 2, D), f32),
            jax.ShapeDtypeStruct((8, D), f32),
        ],
        in_specs=[
            stream_spec((SEG, D)),
            whole_spec((streams, SEG)),
            whole_spec((streams, SEG)),
            whole_spec((8, 128)),
            whole_spec((D, codes)),
            whole_spec(outer_vectors.shape),
            pl.BlockSpec(memory_space=pl.ANY),
        ],
        out_specs=[stream_spec((SEG, D)), whole_spec((2, 2, D // 2, D)), whole_spec((8, D))],
        scratch_shapes=[pltpu.VMEM((D, codes), f32)],
        compiler_params=pltpu.CompilerParams(vmem_limit_bytes=VMEM_LIMIT),
        cost_estimate=pl.CostEstimate(flops=33 * 10**8, bytes_accessed=10**7, transcendentals=10**6),
        name="head",
    )(hidden, targets, mask, totals, out_weight, outer_vectors, momenta)


def feed_back_kernel(streams, g_ref, after_ref, up_ref, down_ref, vec_ref, *refs):
    step = pl.program_id(0)
    grad_ref, dafter_ref, dup_ref, ddown_ref, dvec_ref, done_ref, normed_s, branch_s, act_s, inner_s = refs[:10]
    carry = AttnCarry(grad_ref, refs[10 : 10 + CARRY_REFS], refs[10 + CARRY_REFS :], done_ref)
    planes = carry.planes
    early, late = range(planes // 2), range(planes // 2, planes)
    beats = [
        [("b", place) for place in range(planes)],
        [("m", place) for place in early],
        [("m", place) for place in late],
        [("e", place) for place in early],
        [("e", place) for place in late],
    ]

    @pl.when(step == 0)
    def _():
        hail(carry.targets)
        carry.load_all()
        dvec_ref[...] = jnp.zeros_like(dvec_ref)

    rows = pl.ds(pl.multiple_of(step * SEG, SEG), SEG)
    grad = g_ref[...]
    branch = grad.astype(bf16)
    dvec_ref[2:3, :] += column_sum(branch.astype(f32))
    unit, scale = normalised(after_ref[...])
    gain = vec_ref[2:3, :]
    normed = (unit * gain + vec_ref[3:4, :]).astype(bf16)
    normed_s[:, rows] = jnp.transpose(normed)
    branch_s[:, rows] = jnp.transpose(branch)

    @pl.when(step == 0)
    def _():
        meet(carry.targets)
        carry.send_all()

    for tile in range(FF // TILE):
        columns = slice(tile * TILE, (tile + 1) * TILE)
        inner = dot_nn(normed, up_ref[:, columns]) + vec_ref[8 + tile : 9 + tile, :]
        dact = dot_nt(branch, down_ref[columns, :])
        square = inner * inner
        bent = jnp.tanh(inner * (GELU_SCALE + (GELU_SCALE * 0.044715) * square))
        half = 0.5 * (1.0 + bent)
        act_s[rows, columns] = (inner * half).astype(bf16)
        slope = half + inner * (half * (1.0 - bent)) * (GELU_SCALE + (GELU_SCALE * 0.134145) * square)
        dinner = (dact * slope).astype(bf16)
        inner_s[rows, columns] = dinner
        dvec_ref[4 + tile : 5 + tile, :] += column_sum(dinner.astype(f32))

    @pl.when(step == 0)
    def _():
        carry.run(beats[0])

    @pl.when(step == streams - 1)
    def _():
        carry.run(beats[1])

    dnormed = dot_nt(inner_s[rows, :], up_ref[...])
    dvec_ref[0:1, :] += column_sum(dnormed * unit)
    dvec_ref[1:2, :] += column_sum(dnormed)
    dafter_ref[...] = grad + norm_back(dnormed, gain, unit, scale)

    @pl.when(step == streams - 1)
    def _():
        carry.run(beats[2])
        for tile in range(FF // TILE):
            columns = slice(tile * TILE, (tile + 1) * TILE)
            dup_ref[tile] = dot_nn(normed_s[...], inner_s[:, columns]).astype(bf16)
        carry.run(beats[3])
        for tile in range(FF // TILE):
            columns = slice(tile * TILE, (tile + 1) * TILE)
            ddown_ref[columns, :] = jnp.transpose(dot_nn(branch_s[...], act_s[:, columns]).astype(bf16))
        carry.run(beats[4])
        carry.drain()


def feed_back(depth, grad, after, upper, lower, vectors, count, dp_count, attn_grad):
    streams = grad.shape[0]
    rows = attn_grad.shape[0] // (GROUPS * count)
    in_specs = [
        stream_spec((SEG, D)),
        stream_spec((SEG, D)),
        layer_spec(upper.shape[1:], depth),
        layer_spec(lower.shape[1:], depth),
        layer_spec(vectors.shape[1:], depth),
    ]
    out_shape = [
        jax.ShapeDtypeStruct((streams, SEG, D), f32),
        jax.ShapeDtypeStruct((FF // TILE, D, TILE), bf16),
        jax.ShapeDtypeStruct((FF, D), bf16),
        jax.ShapeDtypeStruct((8, D), f32),
    ]
    out_specs = [
        stream_spec((SEG, D)),
        whole_spec((FF // TILE, D, TILE)),
        whole_spec((FF, D)),
        whole_spec((8, D)),
    ]
    scratch = [
        pltpu.VMEM((D, streams * SEG), bf16),
        pltpu.VMEM((D, streams * SEG), bf16),
        pltpu.VMEM((streams * SEG, FF), bf16),
        pltpu.VMEM((streams * SEG, FF), bf16),
    ]
    operands = [grad, after, upper, lower, vectors]
    in_specs.append(pl.BlockSpec(memory_space=pl.ANY))
    operands.append(attn_grad.reshape(2, 2, count, rows, D))
    out_shape.append(jax.ShapeDtypeStruct((count // 2, rows, D), attn_grad.dtype))
    out_specs.append(whole_spec((count // 2, rows, D)))
    scratch = scratch + carry_scratch("attn", rows, count, dp_count, attn_grad.dtype)
    params = {"collective_id": 6 + depth, "has_side_effects": True}
    return pl.pallas_call(
        functools.partial(feed_back_kernel, streams),
        grid=(streams,),
        out_shape=out_shape,
        in_specs=in_specs,
        out_specs=out_specs,
        scratch_shapes=scratch,
        compiler_params=pltpu.CompilerParams(vmem_limit_bytes=VMEM_LIMIT, **params),
        cost_estimate=pl.CostEstimate(flops=11 * 10**9, bytes_accessed=2 * 10**7, transcendentals=2 * 10**6),
        name="feed_back",
    )(*operands)


def attend_back_kernel(
    streams,
    depth,
    bias_ref,
    dafter_ref,
    x_ref,
    mem_ref,
    keyin_ref,
    q_ref,
    k_ref,
    v_ref,
    lse_ref,
    mixed_ref,
    attn_ref,
    vec_ref,
    frames_ref,
    dup_ref,
    ddown_ref,
    sums_ref,
    dx_ref,
    dattn_ref,
    dvec_ref,
    din_ref,
    done_ref,
    along_ref,
    attn_s,
    dmixed_s,
    dq_s,
    dk_s,
    dv_s,
    ds_s,
    delta_s,
    *refs,
):
    step = pl.program_id(0)
    pairs = HEADS // 2
    split = CARRY_REFS + 1 + CARRY_SEMS
    carry = FeedCarry(depth, dup_ref, ddown_ref, refs[: CARRY_REFS + 1], refs[CARRY_REFS + 1 : split])
    along = ZCarry(refs[split : split + Z_REFS], refs[split + Z_REFS :])
    plans, (free, bound) = carry.plans(), along.plans()

    @pl.when(step == 0)
    def _():
        hail(carry.targets)
        carry.load_all()
        along.sums[...] = sums_ref[...]
        attn_s[...] = jnp.zeros_like(attn_s)
        dvec_ref[...] = jnp.zeros_like(dvec_ref)
        din_ref[...] = jnp.zeros_like(din_ref)

    dafter = dafter_ref[...]
    branch = dafter.astype(bf16)
    dvec_ref[4:5, :] += column_sum(branch.astype(f32))
    dmixed = dot_nt(branch, attn_ref[3]).astype(bf16)
    dmixed_s[...] = dmixed
    attn_s[3] += dot_nn(jnp.transpose(mixed_ref[...]), branch)
    product = dmixed.astype(f32) * mixed_ref[...].astype(f32)
    high = product.astype(bf16)
    rest = (product - high.astype(f32)).astype(bf16)
    owner = lax.broadcasted_iota(jnp.int32, (HEADS, D), 1) // HEAD_DIM
    pick = (owner == lax.broadcasted_iota(jnp.int32, (HEADS, D), 0)).astype(bf16)
    delta_s[...] = dot_nt(pick, high) + dot_nt(pick, rest)
    first, second = head_masks()
    memory_bias = bias_ref[0]
    key_pos = lax.broadcasted_iota(jnp.int32, (HALF, 2 * HALF), 0)
    query_pos = lax.broadcasted_iota(jnp.int32, (HALF, 2 * HALF), 1) % HALF
    diagonal = key_pos <= query_pos
    head_row = lax.broadcasted_iota(jnp.int32, (PAIR, HALF), 0)

    @pl.when(step == 0)
    def _():
        meet(carry.targets)
        carry.send_all()
        along.run(free)

    @pl.when(step == 1)
    def _():
        carry.run(plans[-1])

    def pair_body(pair, state):
        lanes = pair_lanes(pair)
        q_pair, do_pair = q_ref[:, lanes], dmixed_s[:, lanes]

        def spread(value):
            return jnp.concatenate(
                [value[:HALF] * first, value[:HALF] * second, value[HALF:] * first, value[HALF:] * second], 0
            )

        q_all, do_all = spread(q_pair), spread(do_pair)

        def rows_of(ref):
            one, two = ref[pl.ds(2 * pair, 1), :], ref[pl.ds(2 * pair + 1, 1), :]
            return jnp.concatenate([one[:, :HALF], two[:, :HALF], one[:, HALF:], two[:, HALF:]], 1)

        lse_all, delta_all = rows_of(lse_ref), rows_of(delta_s)
        for block in range(4):
            keys = slice(block * HALF, (block + 1) * HALF)
            start = 2 * HALF if block == 3 else 0
            scores = dot_nt(k_ref[keys, lanes], q_all[start:])
            shift = lse_all - memory_bias if block < 2 else lse_all[:, start:]
            weights = jnp.exp(scores - shift)
            if block == 2:
                weights = jnp.concatenate(
                    [jnp.where(diagonal, weights[:, : 2 * HALF], 0.0), weights[:, 2 * HALF :]], 1
                )
            if block == 3:
                weights = jnp.where(diagonal, weights, 0.0)
            dweights = dot_nt(v_ref[keys, lanes], do_all[start:])
            dscores = (weights * (dweights - delta_all[:, start:])).astype(bf16)
            dv_s[keys, lanes] = dot_nn(weights.astype(bf16), do_all[start:]).astype(bf16)
            dk_s[keys, lanes] = dot_nn(dscores, q_all[start:]).astype(bf16)
            ds_s[keys, start:] = dscores
        k_t = jnp.transpose(k_ref[:, lanes])
        for block in range(2):
            seen = SEG + (block + 1) * HALF
            grads = dot_nn(k_t[:, :seen], ds_s[:seen, block * 2 * HALF : (block + 1) * 2 * HALF])
            grads = jnp.where(head_row < HEAD_DIM, grads[:, :HALF], grads[:, HALF:])
            dq_s[block * HALF : (block + 1) * HALF, lanes] = (
                jnp.transpose(grads) * (HEAD_DIM**-0.5)
            ).astype(bf16)
        for time, acts in enumerate(plans[:-1]):
            if acts:

                @pl.when(pairs * step + pair == time)
                def _():
                    carry.run(acts)
                    if time == 3:
                        along.run(bound)

        return state

    lax.fori_loop(0, pairs, pair_body, 0)
    dq, dk, dv = dq_s[...], dk_s[...], dv_s[...]
    keyin_t = jnp.transpose(keyin_ref[...])
    attn_s[0] += dot_nn(keyin_t[:, SEG:], dq)
    attn_s[1] += dot_nn(keyin_t, dk)
    attn_s[2] += dot_nn(keyin_t, dv)
    dvec_ref[2:3, :] += column_sum(dq.astype(f32))
    dvec_ref[3:4, :] += column_sum(dv.astype(f32))
    dkeyin = dot_nt(dk, attn_ref[1]) + dot_nt(dv, attn_ref[2])
    dmem = dkeyin[:SEG]
    down = dkeyin[SEG:] + dot_nt(dq, attn_ref[0])
    gain = vec_ref[0:1, :]
    unit, scale = normalised(x_ref[...])
    mem_unit, _ = normalised(mem_ref[...].astype(f32))
    dvec_ref[0:1, :] += column_sum(down * unit + dmem * mem_unit)
    dvec_ref[1:2, :] += column_sum(down + dmem)
    dx = dafter + norm_back(down, gain, unit, scale)
    dx_ref[...] = dx
    if depth == 0:
        dx_high = dx.astype(bf16)
        dx_rest = (dx - dx_high.astype(f32)).astype(bf16)
        din_ref[...] += dot_nn(frames_ref[...], dx_high) + dot_nn(frames_ref[...], dx_rest)
        dvec_ref[5:6, :] += column_sum(dx)

    @pl.when(step == pl.num_programs(0) - 1)
    def _():
        dattn_ref[...] = attn_s[...].astype(bf16)
        carry.finish(done_ref)
        along.finish(along_ref)


def attend_back(depth, bias, dafter, x, memory, saved, attn, vectors, frames, up_grad, down_grad, sums, count, dp_count):
    streams = dafter.shape[0]
    keyin, q, k, v, lse, mixed = saved
    inputs = frames.shape[1]
    rows = D // count
    up_grad, down_grad = up_grad.reshape(4, count, rows, D), down_grad.reshape(count, 4, rows, D)
    return pl.pallas_call(
        functools.partial(attend_back_kernel, streams, depth),
        grid=(streams,),
        out_shape=[
            jax.ShapeDtypeStruct((streams, SEG, D), f32),
            jax.ShapeDtypeStruct((4, D, D), bf16),
            jax.ShapeDtypeStruct((8, D), f32),
            jax.ShapeDtypeStruct((inputs, D), f32),
            jax.ShapeDtypeStruct((2, rows, D), bf16),
            jax.ShapeDtypeStruct(sums.shape[1:], bf16),
        ],
        in_specs=[
            pl.BlockSpec(memory_space=pltpu.SMEM),
            stream_spec((SEG, D)),
            stream_spec((SEG, D)),
            stream_spec((SEG, D)),
            stream_spec((2 * SEG, D)),
            stream_spec((SEG, D)),
            stream_spec((2 * SEG, D)),
            stream_spec((2 * SEG, D)),
            stream_spec((HEADS, SEG)),
            stream_spec((SEG, D)),
            layer_spec(attn.shape[1:], depth),
            layer_spec(vectors.shape[1:], depth),
            stream_spec((inputs, SEG)),
            pl.BlockSpec(memory_space=pl.ANY),
            pl.BlockSpec(memory_space=pl.ANY),
            whole_spec(sums.shape),
        ],
        out_specs=[
            stream_spec((SEG, D)),
            whole_spec((4, D, D)),
            whole_spec((8, D)),
            whole_spec((inputs, D)),
            whole_spec((2, rows, D)),
            whole_spec(sums.shape[1:]),
        ],
        scratch_shapes=[
            pltpu.VMEM((4, D, D), f32),
            pltpu.VMEM((SEG, D), bf16),
            pltpu.VMEM((SEG, D), bf16),
            pltpu.VMEM((2 * SEG, D), bf16),
            pltpu.VMEM((2 * SEG, D), bf16),
            pltpu.VMEM((2 * SEG, 2 * SEG), bf16),
            pltpu.VMEM((HEADS, SEG), f32),
        ]
        + carry_scratch("feed", rows, count, dp_count)
        + z_scratch(sums.shape[1], count, dp_count, sums.dtype),
        compiler_params=pltpu.CompilerParams(
            collective_id=4 + depth, has_side_effects=True, vmem_limit_bytes=VMEM_LIMIT
        ),
        cost_estimate=pl.CostEstimate(flops=3 * 10**10, bytes_accessed=2 * 10**7, transcendentals=10**7),
        name="attend_back",
    )(bias, dafter, x, memory, keyin, q, k, v, lse, mixed, attn, vectors, frames, up_grad, down_grad, sums)


def from_behind(value, axis, steps):
    count = lax.axis_size(axis)
    leading, last = (max(0, -steps), min(count, count - steps))
    return lax.ppermute(value, axis, [(source, source + steps) for source in range(leading, last)])


def adamw(weight, moment, second, grad, rate, decay):
    moment = 0.5 * moment + 0.5 * grad
    second = 0.99 * second + 0.01 * grad * grad
    fixed_moment = moment / (1.0 - 0.5**STEP)
    fixed_second = second / (1.0 - 0.99**STEP)
    weight = weight * (1.0 - rate * decay) - rate * fixed_moment / (jnp.sqrt(fixed_second) + 1e-08)
    return (weight, moment, second)


GROUPS = 4
UNITS = 6
SMALL = 128


def peers():
    count = {"seg": lax.axis_size("seg"), "dp": lax.axis_size("dp")}
    seg, dp = lax.axis_index("seg"), lax.axis_index("dp")
    core, x, y = seg % 2, dp % 2, (dp // 2) % 2
    across_core = {"seg": seg + 1 - 2 * core}
    across_x = {"dp": dp + 1 - 2 * x}
    across_y = {"dp": dp + 2 - 4 * y}
    across_both = {"dp": dp + 3 - 2 * x - 4 * y}
    far = []
    step = GROUPS
    while step < count["dp"]:
        far.append({"dp": dp + step - 2 * step * ((dp // step) % 2)})
        step *= 2
    return seg, dp, core, x, y, across_core, (across_x, across_y, across_both), far


def others(seg, count):
    return [lax.rem(seg + step, count) for step in range(1, count)]


def hail(targets):
    barrier = pltpu.get_barrier_semaphore()
    for target in targets:
        pl.semaphore_signal(barrier, inc=1, device_id=target, device_id_type=pl.DeviceIdType.MESH)


def meet(targets):
    pl.semaphore_wait(pltpu.get_barrier_semaphore(), len(targets))


def greet(seg, count, near, far):
    targets = [{"seg": other} for other in others(seg, count)] + list(near) + list(far)
    hail(targets)
    meet(targets)


def remote(source, target, send, recv, device):
    return pltpu.make_async_remote_copy(
        src_ref=source,
        dst_ref=target,
        send_sem=send,
        recv_sem=recv,
        device_id=device,
        device_id_type=pl.DeviceIdType.MESH,
    )


def wait_bytes(ref, sem):
    pltpu.make_async_copy(ref, ref, sem).wait()


def plus(left, right):
    return (left.astype(f32) + right.astype(f32)).astype(left.dtype)


def owners(count):
    low, high = count // 4 - 1, count // 4
    return (
        (0, 1, 0, 0),
        (1, 1, count - 2, 0),
        (2, 2, 2 * low, 0),
        (4, 2, 2 * low + 1, 2),
        (2, 2, 2 * high, 0),
        (4, 2, 2 * high + 1, 2),
    )


def lowest_bit(mask, planes):
    bit = 1
    while bit < planes and not mask & bit:
        bit *= 2
    return bit


class Carry:
    def __init__(self, refs, sems):
        self.mine, self.got0, self.got1, self.got2, self.got3, self.goth = refs
        (
            self.load,
            self.send0,
            self.recv0,
            self.send1,
            self.recv1,
            self.send2,
            self.recv2,
            self.send3,
            self.recv3,
            self.sendh,
            self.recvh,
        ) = sems
        self.settle(self.mine.shape[0])

    def settle(self, planes):
        self.seg, self.dp, self.core, self.x, self.y, self.across_core, near, self.far = peers()
        self.across_x, self.across_y, _ = near
        self.planes = planes
        self.plane = self.seg // 2
        self.targets = [self.across_core, self.across_x, self.across_y] + self.far
        bit = 1
        while bit < planes:
            self.targets.append({"seg": 2 * self.toggled(bit) + self.core})
            bit *= 2
        self.order = list(reversed(range(planes)))

    def toggled(self, mask):
        place, bit = self.plane, 1
        while bit <= mask:
            if mask & bit:
                place = place + bit - 2 * bit * ((self.plane // bit) % 2)
            bit *= 2
        return place

    def load_all(self):
        for step in range(self.planes):
            for source, place in self.pieces(2 * self.toggled(self.order[step]) + self.core):
                pltpu.make_async_copy(source, self.mine.at[(step,) + place], self.load.at[step]).start()

    def send_all(self):
        for step in range(self.planes):
            for source, place in self.pieces(2 * self.toggled(self.order[step]) + 1 - self.core):
                remote(
                    source, self.got0.at[(step,) + place], self.send0.at[step], self.recv0.at[step], self.across_core
                ).start()

    def begin(self, step):
        wait_bytes(self.mine.at[step], self.load.at[step])
        wait_bytes(self.got0.at[step], self.recv0.at[step])
        for place in range(2):
            self.mine[step, place] = plus(self.mine[step, place], self.got0[step, place])
        for copy in self.first(step):
            copy.start()

    def across(self, place, step):
        return remote(
            self.held(step),
            self.goth.at[place, step],
            self.sendh.at[place, step],
            self.recvh.at[place, step],
            self.far[place],
        )

    def third(self, step):
        mask = self.order[step]
        return remote(
            self.held(step),
            self.got3.at[mask],
            self.send3.at[step],
            self.recv3.at[mask],
            {"seg": 2 * self.toggled(lowest_bit(mask, self.planes)) + self.core},
        )

    def onward(self, step):
        held = self.held(step)
        for place in range(len(self.far)):
            copy = self.across(place, step)
            copy.start()
            copy.wait()
            held[...] = plus(held[...], self.goth[place, step])
        mask = self.order[step]
        if mask:
            self.gathered(mask, held)
            self.third(step).start()

    def gathered(self, mask, held):
        value, bit = held[...].astype(f32), 1
        while bit < lowest_bit(mask, self.planes):
            wait_bytes(self.got3.at[mask + bit], self.recv3.at[mask + bit])
            value = value + self.got3[mask + bit].astype(f32)
            bit *= 2
        held[...] = value.astype(held.dtype)

    def total(self):
        held = self.held(self.planes - 1)
        self.gathered(0, held)
        return held[...]

    def run(self, acts):
        for kind, step in acts:
            getattr(self, {"b": "begin", "m": "middle", "e": "end", "z": "onward"}[kind])(step)


class ZCarry(Carry):
    def __init__(self, refs, sems):
        self.sums, self.got3, self.goth = refs
        self.send3, self.recv3, self.sendh, self.recvh = sems
        self.settle(self.sums.shape[0])

    def held(self, step):
        return self.sums.at[step]

    def plans(self):
        free = [("z", step) for step in range(self.planes) if self.order[step] % 2]
        bound = [("z", step) for step in range(self.planes) if self.order[step] and not self.order[step] % 2]
        return free, bound

    def finish(self, out_ref):
        out_ref[...] = self.total().astype(out_ref.dtype)
        for step in range(self.planes - 1):
            self.third(step).wait_send()


class AttnCarry(Carry):
    def __init__(self, source, refs, sems, sums=None):
        super().__init__(refs, sems)
        self.source, self.sums = source, sums

    def pieces(self, row):
        return ((self.source.at[:, :, row], ()),)

    def held(self, step):
        return self.mine.at[step, self.y, self.x]

    def first(self, step):
        half = self.mine.shape[3] // 2
        return (
            remote(
                self.mine.at[step, :, 1 - self.x, 0:half],
                self.got1.at[step, 0],
                self.send1.at[step, 0],
                self.recv1.at[step, 0],
                self.across_x,
            ),
            remote(
                self.mine.at[step, 1 - self.y, :, half:],
                self.got1.at[step, 1],
                self.send1.at[step, 1],
                self.recv1.at[step, 1],
                self.across_y,
            ),
        )

    def second(self, step):
        half = self.mine.shape[3] // 2
        return (
            remote(
                self.mine.at[step, 1 - self.y, self.x, 0:half],
                self.got2.at[step, 0],
                self.send2.at[step, 0],
                self.recv2.at[step, 0],
                self.across_y,
            ),
            remote(
                self.mine.at[step, self.y, 1 - self.x, half:],
                self.got2.at[step, 1],
                self.send2.at[step, 1],
                self.recv2.at[step, 1],
                self.across_x,
            ),
        )

    def middle(self, step):
        mine, half = self.mine, self.mine.shape[3] // 2
        for copy in self.first(step):
            copy.wait_recv()
        for place in range(2):
            mine[step, place, self.x, 0:half] = plus(mine[step, place, self.x, 0:half], self.got1[step, 0, place])
            mine[step, self.y, place, half:] = plus(mine[step, self.y, place, half:], self.got1[step, 1, place])
        for copy in self.second(step):
            copy.start()

    def end(self, step):
        mine, half = self.mine, self.mine.shape[3] // 2
        for copy in self.second(step):
            copy.wait_recv()
        upper = plus(mine[step, self.y, self.x, 0:half], self.got2[step, 0])
        lower = plus(mine[step, self.y, self.x, half:], self.got2[step, 1])
        if self.sums is not None:
            self.sums[step, 0:half] = upper
            self.sums[step, half:] = lower
            return
        mine[step, self.y, self.x, 0:half] = upper
        mine[step, self.y, self.x, half:] = lower
        self.onward(step)

    def drain(self):
        for step in range(self.planes):
            wait_bytes(self.mine.at[step], self.send0.at[step])
            for copy in self.first(step) + self.second(step):
                copy.wait_send()
            if self.sums is None and step < self.planes - 1:
                self.third(step).wait_send()


class FeedCarry(Carry):
    def __init__(self, depth, up, down, refs, sems):
        super().__init__(refs[:CARRY_REFS], sems)
        (self.sums,) = refs[CARRY_REFS:]
        self.up, self.down = up, down
        self.keep = self.x if depth == 1 else 1 - self.x

    def pieces(self, row):
        return ((self.up.at[:, row], (0,)), (self.down.at[row], (1,)))

    def held(self, step):
        return self.sums.at[step]

    def first(self, step):
        return (
            remote(
                self.mine.at[step, 1 - self.keep, 0:2],
                self.got1.at[step, 0],
                self.send1.at[step, 0],
                self.recv1.at[step, 0],
                self.across_x,
            ),
            remote(
                self.mine.at[step, 1 - self.y, 2:4],
                self.got1.at[step, 1],
                self.send1.at[step, 1],
                self.recv1.at[step, 1],
                self.across_y,
            ),
        )

    def second(self, step):
        return (
            remote(
                self.mine.at[step, self.keep, 1 - self.y],
                self.got2.at[step, 0],
                self.send2.at[step, 0],
                self.recv2.at[step, 0],
                self.across_y,
            ),
            remote(
                self.mine.at[step, self.y, 3 - self.x],
                self.got2.at[step, 1],
                self.send2.at[step, 1],
                self.recv2.at[step, 1],
                self.across_x,
            ),
        )

    def middle(self, step):
        for copy in self.first(step):
            copy.wait_recv()
        self.mine[step, self.keep, 0:2] = plus(self.mine[step, self.keep, 0:2], self.got1[step, 0])
        self.mine[step, self.y, 2:4] = plus(self.mine[step, self.y, 2:4], self.got1[step, 1])
        for copy in self.second(step):
            copy.start()

    def end(self, step):
        for copy in self.second(step):
            copy.wait_recv()
        self.sums[step, 0] = plus(self.mine[step, self.keep, self.y], self.got2[step, 0])
        self.sums[step, 1] = plus(self.mine[step, self.y, 2 + self.x], self.got2[step, 1])
        self.onward(step)

    def plans(self):
        planes = self.planes
        return (
            [("b", step) for step in range(planes - 1)],
            [],
            [("m", 0), ("b", planes - 1)],
            [("m", 1)],
            [("m", step) for step in range(3, planes)],
            [("e", 1)],
            [("e", 2)],
            [("e", step) for step in range(3, planes)],
            [("m", 2), ("e", 0)],
        )

    def finish(self, out_ref):
        out_ref[...] = self.total()
        for step in range(self.planes):
            wait_bytes(self.mine.at[step], self.send0.at[step])
            for copy in self.first(step) + self.second(step):
                copy.wait_send()
            if step < self.planes - 1:
                self.third(step).wait_send()


CARRY_REFS = 6
CARRY_SEMS = 11


def carry_scratch(kind, rows, count, dp_count, dtype=bf16):
    planes = count // 2
    far = max(1, dp_count.bit_length() - 3)
    dma = pltpu.SemaphoreType.DMA
    half = rows // 2
    if kind == "attn":
        shapes = (
            (planes, 2, 2, rows),
            (planes, 2, 2, rows),
            (planes, 2, 2, half),
            (planes, 2, half),
            (planes, rows),
            (far, planes, rows),
        )
    else:
        shapes = (
            (planes, 2, 4, rows),
            (planes, 2, 4, rows),
            (planes, 2, 2, rows),
            (planes, 2, rows),
            (planes, 2, rows),
            (far, planes, 2, rows),
            (planes, 2, rows),
        )
    pair = (planes, 2)
    one = (planes,)
    sems = (one, one, one, pair, pair, pair, pair, one, one, (far, planes), (far, planes))
    return [pltpu.VMEM(shape + (D,), dtype) for shape in shapes] + [dma(shape) for shape in sems]


def z_scratch(rows, count, dp_count, dtype):
    planes = count // 2
    far = max(1, dp_count.bit_length() - 3)
    dma = pltpu.SemaphoreType.DMA
    shapes = ((planes, rows), (planes, rows), (far, planes, rows))
    sems = ((planes,), (planes,), (far, planes), (far, planes))
    return [pltpu.VMEM(shape + (D,), dtype) for shape in shapes] + [dma(shape) for shape in sems]


Z_REFS = 3
Z_SEMS = 4


def halves(value):
    high = value.astype(bf16)
    return high, (value - high.astype(f32)).astype(bf16)


def times(left, right):
    (left_high, left_low), (right_high, right_low) = left, right
    return dot_nn(
        jnp.concatenate([left_high, left_high, left_low], 1),
        jnp.concatenate([right_high, right_low, right_high], 0),
    )


def mirrored(first, second, third):
    return jnp.concatenate(
        [
            jnp.concatenate([first, second], 1),
            jnp.concatenate([jnp.transpose(second), third], 1),
        ],
        0,
    )


def times_even(left, right):
    (left_high, left_low), (right_high, right_low) = left, right
    wide = jnp.concatenate([left_high, left_high, left_low], 1)
    tall = jnp.concatenate([right_high, right_low, right_high], 0)
    return mirrored(
        dot_nn(wide[:HALF], tall[:, :HALF]),
        dot_nn(wide[:HALF], tall[:, HALF:]),
        dot_nn(wide[HALF:], tall[:, HALF:]),
    )


def gram_of(both):
    high, low = both
    wide = jnp.concatenate([high, high, low], 1)
    tall = jnp.concatenate([high, low, high], 1)
    return mirrored(
        dot_nt(wide[:HALF], tall[:HALF]),
        dot_nt(wide[:HALF], tall[HALF:]),
        dot_nt(wide[HALF:], tall[HALF:]),
    )


def clip_of(norm):
    return jnp.minimum(1.0, 0.25 / (norm + 1e-06))


def tail_kernel(
    count,
    attn_grad_ref,
    attn_done_ref,
    feed_low_ref,
    feed_high_ref,
    dout_ref,
    din_ref,
    vec0_ref,
    vec1_ref,
    vec2_ref,
    vec3_ref,
    outer_ref,
    mom_ref,
    update_ref,
    every_ref,
    small_out,
    norm_ref,
    whole_ref,
    own_ref,
    mom_s,
    small_ref,
    small_s,
    got_core,
    got_x,
    got_y,
    got_z,
    sq_seg,
    sq_dp,
    keep_s,
    give_s,
    made_ref,
    x_s,
    q_s,
    gram_s,
    high_s,
    low_s,
    mom_sem,
    last_send,
    last_recv,
    small_send,
    small_recv,
    join_send,
    join_recv,
    whole_send,
    whole_recv,
    half_sem,
    sq_send,
    sq_recv,
    sqd_send,
    sqd_recv,
    send,
    recv,
    on_send,
    on_recv,
    own_send,
    own_recv,
    *refs,
):
    carry = AttnCarry(attn_grad_ref, refs[:CARRY_REFS], refs[CARRY_REFS:])
    seg, dp, core, x, y, across_core, near, far = peers()
    across_x, across_y, across_both = near
    planes = count // 2
    plane = seg // 2
    group = 2 * y + x
    rows = own_ref.shape[1]
    targets = [{"seg": other} for other in others(seg, count)] + list(near) + list(far)
    hail(targets)
    carry.load_all()
    mom_copy = pltpu.make_async_copy(mom_ref, mom_s, mom_sem.at[0])
    mom_copy.start()
    own_ref[1] = attn_done_ref[...]

    @pl.when(x == y)
    def _():
        keep_s[...] = feed_high_ref[...]
        give_s[...] = feed_low_ref[...]

    @pl.when(x != y)
    def _():
        keep_s[...] = feed_low_ref[...]
        give_s[...] = feed_high_ref[...]

    own_ref[2 + y] = keep_s[0]
    own_ref[4 + x] = keep_s[1]
    last = (
        remote(give_s.at[0], own_ref.at[2 + y], last_send.at[0], last_recv.at[0], across_y),
        remote(give_s.at[1], own_ref.at[4 + x], last_send.at[1], last_recv.at[1], across_x),
    )
    inputs = din_ref.shape[0]
    small_ref[0:inputs, :] = din_ref[...]
    for place, ref in enumerate((vec0_ref, vec1_ref, vec2_ref, vec3_ref, outer_ref)):
        small_ref[inputs + 8 * place : inputs + 8 * place + 8, :] = ref[...]
    small_ref[inputs + 40 :, :] = jnp.zeros((SMALL - inputs - 40, D), f32)
    meet(targets)

    def span(first, size):
        return pl.ds(pl.multiple_of(first, 8), size)

    by_core, by_x, by_y = SMALL // 2, SMALL // 4, SMALL // 8
    core_at = core * by_core
    x_at = core_at + x * by_x
    y_at = x_at + y * by_y

    def small_steps():
        kept = span(core_at, by_core)
        copy = remote(
            small_ref.at[span(by_core - core_at, by_core)], got_core, small_send.at[0], small_recv.at[0], across_core
        )
        copy.start()
        yield
        copy.wait()
        small_s[kept, :] = small_ref[kept, :] + got_core[...]
        sent = span(core_at + by_x - x * by_x, by_x)
        copy = remote(small_s.at[sent], got_x, small_send.at[1], small_recv.at[1], across_x)
        copy.start()
        yield
        copy.wait()
        small_s[span(x_at, by_x), :] += got_x[...]
        sent = span(x_at + by_y - y * by_y, by_y)
        copy = remote(small_s.at[sent], got_y, small_send.at[2], small_recv.at[2], across_y)
        copy.start()
        yield
        copy.wait()
        kept = span(y_at, by_y)
        small_s[kept, :] += got_y[...]
        partners, step = list(far), 1
        while step < planes:
            partners.append({"seg": 2 * carry.toggled(step) + core})
            step *= 2
        for place, partner in enumerate(partners):
            copy = remote(
                small_s.at[kept], got_z.at[place], small_send.at[3 + place], small_recv.at[3 + place], partner
            )
            copy.start()
            yield
            copy.wait()
            small_s[kept, :] += got_z[place]

    small_run = small_steps()
    next(small_run)
    carry.send_all()
    for copy in last:
        copy.start()
    roles = owners(count)

    def gift(place):
        first, width, owner, spot = roles[place]
        return remote(
            own_ref.at[first : first + width],
            whole_ref.at[seg, spot : spot + width],
            whole_send.at[place],
            whole_recv.at[seg],
            {"seg": owner},
        )

    def give(place):
        first, width, owner, spot = roles[place]

        @pl.when(seg != owner)
        def _():
            gift(place).start()

        @pl.when(seg == owner)
        def _():
            whole_ref[seg, spot : spot + width] = own_ref[first : first + width]

    acts = [
        [("b", step) for step in range(planes - 1)],
        [("m", 0), ("b", planes - 1)],
        [("m", 1)],
        [("m", 2), ("e", 0)],
        [("m", step) for step in range(3, planes)],
    ] + [[("e", step)] for step in range(1, planes)]
    give(1)
    next(small_run)
    for turn, part in enumerate(acts):
        carry.run(part)
        if turn == 0:
            for copy in last:
                copy.wait()
            for place in range(2, 6):
                give(place)
        next(small_run, None)
    own_ref[0] = carry.total()
    give(0)
    for _ in small_run:
        pass

    mine = span(y_at, by_y)
    small_out[mine, :] = small_s[mine, :]

    def join(place):
        first, size, partner = ((y_at, by_y, across_y), (x_at, by_x, across_x), (core_at, by_core, across_core))[place]
        block = small_out.at[span(first, size)]
        return remote(block, block, join_send.at[place], join_recv.at[place], partner)

    join(0).start()
    shard = dout_ref[...].astype(f32)
    square = jnp.sum(jnp.sum(shard * shard, 0, keepdims=True), 1, keepdims=True)
    for unit in range(UNITS):
        value = own_ref[unit].astype(f32)
        square = square + jnp.sum(jnp.sum(value * value, 0, keepdims=True), 1, keepdims=True)
    sums = small_s[mine, :]
    is_loss = lax.broadcasted_iota(jnp.int32, (by_y, D), 0) + y_at == inputs + 37
    sums = jnp.where(is_loss, 0.0, sums)
    square = square + jnp.sum(jnp.sum(sums * sums, 0, keepdims=True), 1, keepdims=True) * (1.0 / planes)
    sq_seg[seg] = jnp.broadcast_to(square, (8, 128))
    for step, other in enumerate(others(seg, count)):
        remote(sq_seg.at[seg], sq_seg.at[seg], sq_send.at[step], sq_recv.at[seg], {"seg": other}).start()

    def halves_copy(spot):
        part = slice(spot, spot + 2)
        return remote(whole_ref.at[:, part], whole_ref.at[:, part], half_sem.at[0], half_sem.at[1], across_core)

    for place, (first, width, owner, spot) in enumerate(roles):
        if width == 2:

            @pl.when(seg == owner)
            def _():
                for other in others(seg, count):
                    wait_bytes(whole_ref.at[other, spot : spot + width], whole_recv.at[other])
                halves_copy(spot).start()

    for other in others(seg, count):
        wait_bytes(sq_seg.at[other], sq_recv.at[other])
    sq_dp[group] = jnp.sum(sq_seg[...], 0)
    for place, target in enumerate(near):
        remote(sq_dp.at[group], sq_dp.at[group], sqd_send.at[place], sqd_recv.at[place], target).start()
    join(0).wait()
    join(1).start()
    for place, target in enumerate(near):
        remote(sq_dp.at[group], sq_dp.at[group], sqd_send.at[place], sqd_recv.at[place], target).wait()
    norm = jnp.sqrt(jnp.sum(sq_dp[...], 0)[0:1, 0:1])
    norm_ref[...] = jnp.broadcast_to(norm, norm_ref.shape)
    clip = clip_of(norm)

    def own_rows(side):
        return remote(own_ref, every_ref.at[group], own_send.at[side], own_recv.at[side], near[side])

    for side in range(3):
        own_rows(side).start()
    every_ref[group] = own_ref[...]
    mom_copy.wait()

    for place, (first, width, owner, spot) in enumerate(roles):

        @pl.when(seg == owner)
        def _():
            if width == 2:
                halves_copy(spot).wait()
            else:
                for other in others(seg, count):
                    wait_bytes(whole_ref.at[other, spot : spot + width], whole_recv.at[other])

    is_down = group >= 2
    eye = (
        lax.broadcasted_iota(jnp.int32, (D, D), 0) == lax.broadcasted_iota(jnp.int32, (D, D), 1)
    ).astype(f32)
    low = count // 4 - 1
    half = plane // (planes // 2)
    base = half * planes
    neighbours = [base + lax.rem(seg - base + step, planes) for step in range(1, planes)]
    feed_maker = 2 * (low + half)
    makers = [0, count - 2, feed_maker, feed_maker, feed_maker + 1, feed_maker + 1]

    def receivers(unit):
        return others(seg, count) if unit < 2 else neighbours

    def present(unit, slot, other):
        return remote(
            made_ref.at[other, slot],
            update_ref.at[group, unit],
            send.at[slot, other],
            recv.at[unit],
            {"seg": other},
        )

    def hand_out(unit, slot):
        for other in receivers(unit):
            present(unit, slot, other).start()
        update_ref[group, unit] = made_ref[seg, slot]

    def onward(unit, side):
        block = update_ref.at[group, unit]
        return remote(block, block, on_send.at[side, unit], on_recv.at[side, unit], near[side])

    @pl.when((seg == 0) | (seg == count - 2))
    def _():
        start = (0.5 * mom_s[:, plane // (planes - 1)].astype(f32)).reshape(D, D)
        start = start + clip * whole_ref[:, 0].astype(f32).reshape(D, D)
        size = jnp.sum(jnp.sum(start * start, 0, keepdims=True), 1, keepdims=True)
        x_s[...] = start / (jnp.sqrt(size) + 1e-07)

        def sweep(_, state):
            value = x_s[...]
            both = halves(value)
            gram = gram_of(both)
            gram_both = halves(gram)
            poly = -4.775 * gram + 2.0315 * times_even(gram_both, gram_both)
            x_s[...] = 3.4445 * value + times(halves(poly), both)
            return state

        lax.fori_loop(0, 5, sweep, 0)
        made_ref[:, 0] = x_s[...].astype(bf16).reshape(count, rows, D)
        for unit in range(2):

            @pl.when(seg == makers[unit])
            def _():
                hand_out(unit, 0)

    @pl.when((plane == low) | (plane == low + 1))
    def _():
        gram_s[...] = jnp.zeros_like(gram_s)

        def gather(tile, size):
            value = (0.5 * mom_s[:, 2 + tile].astype(f32)).reshape(D, D)
            value = value + clip * whole_ref[:, tile].astype(f32).reshape(D, D)
            high, rest = halves(value)
            high_s[tile] = high
            low_s[tile] = rest

            @pl.when(is_down)
            def _():
                high_s[tile] = jnp.transpose(high_s[tile])
                low_s[tile] = jnp.transpose(low_s[tile])

            gram_s[...] += gram_of((high_s[tile], low_s[tile]))
            return size + jnp.sum(jnp.sum(value * value, 0, keepdims=True), 1, keepdims=True)

        size = lax.fori_loop(0, 4, gather, jnp.zeros((1, 1), f32))
        scale = 1.0 / (jnp.sqrt(size) + 1e-07)
        gram_s[...] = gram_s[...] * (scale * scale)

        def poly_of(gram, gram_both):
            return 3.4445 * eye - 4.775 * gram + 2.0315 * times_even(gram_both, gram_both)

        def advance(gram_both, poly_both):
            gram_s[...] = times_even(halves(times_even(gram_both, poly_both)), poly_both)

        gram = gram_s[...]
        gram_both = halves(gram)
        poly = poly_of(gram, gram_both)
        q_s[...] = poly
        advance(gram_both, halves(poly))

        def sweep(_, state):
            gram = gram_s[...]
            gram_both = halves(gram)
            poly_both = halves(poly_of(gram, gram_both))
            q_s[...] = times_even(halves(q_s[...]), poly_both)
            advance(gram_both, poly_both)
            return state

        lax.fori_loop(0, 3, sweep, 0)
        gram = gram_s[...]
        last_both = halves(times_even(halves(q_s[...]), halves(poly_of(gram, halves(gram)))) * scale)
        for slot in range(2):
            tile = 2 * core + slot
            x_s[...] = times(last_both, (high_s[tile], low_s[tile]))

            @pl.when(is_down)
            def _():
                x_s[...] = jnp.transpose(x_s[...])

            made_ref[:, slot] = x_s[...].astype(bf16).reshape(count, rows, D)
            for side in range(2):

                @pl.when(core == side)
                def _():
                    hand_out(2 + 2 * side + slot, slot)

    join(1).wait()
    join(2).start()
    for unit in (0, 1, 2, 4, 3, 5):

        @pl.when(seg != makers[unit])
        def _():
            wait_bytes(update_ref.at[group, unit], recv.at[unit])

        for side in range(3):
            onward(unit, side).start()
    join(2).wait()
    for side in range(3):
        own_rows(side).wait()
    carry.drain()
    for place, (first, width, owner, spot) in enumerate(roles):

        @pl.when(seg != owner)
        def _():
            gift(place).wait_send()

    for step in range(count - 1):
        wait_bytes(sq_seg.at[0], sq_send.at[step])
    for unit in range(UNITS):
        for side in range(3):
            onward(unit, side).wait()

        @pl.when(seg == makers[unit])
        def _():
            slot = 0 if unit < 2 else unit % 2
            for other in receivers(unit):
                present(unit, slot, other).wait_send()


def tail(count, dp_count, attn, done, feed_low, feed_high, dout, pieces, momenta):
    rows = D // count
    planes = count // 2
    stages = planes.bit_length() + max(0, dp_count.bit_length() - 3)
    dma = pltpu.SemaphoreType.DMA
    vmem, anywhere = pl.BlockSpec(memory_space=pltpu.VMEM), pl.BlockSpec(memory_space=pl.ANY)
    blocks = jax.ShapeDtypeStruct((GROUPS, UNITS, rows, D), bf16)
    return pl.pallas_call(
        functools.partial(tail_kernel, count),
        out_shape=[
            blocks,
            blocks,
            jax.ShapeDtypeStruct((SMALL, D), f32),
            jax.ShapeDtypeStruct((8, 128), f32),
        ],
        in_specs=[anywhere] + [vmem] * 10 + [anywhere],
        out_specs=[vmem] * 4,
        scratch_shapes=[
            pltpu.VMEM((count, 4, rows, D), bf16),
            pltpu.VMEM((UNITS, rows, D), bf16),
            pltpu.VMEM(momenta.shape, bf16),
            pltpu.VMEM((SMALL, D), f32),
            pltpu.VMEM((SMALL, D), f32),
            pltpu.VMEM((SMALL // 2, D), f32),
            pltpu.VMEM((SMALL // 4, D), f32),
            pltpu.VMEM((SMALL // 8, D), f32),
            pltpu.VMEM((stages, SMALL // 8, D), f32),
            pltpu.VMEM((count, 8, 128), f32),
            pltpu.VMEM((GROUPS, 8, 128), f32),
            pltpu.VMEM((2, rows, D), bf16),
            pltpu.VMEM((2, rows, D), bf16),
            pltpu.VMEM((count, 2, rows, D), bf16),
            pltpu.VMEM((D, D), f32),
            pltpu.VMEM((D, D), f32),
            pltpu.VMEM((D, D), f32),
            pltpu.VMEM((4, D, D), bf16),
            pltpu.VMEM((4, D, D), bf16),
            dma((1,)),
            dma((2,)),
            dma((2,)),
            dma((stages + 3,)),
            dma((stages + 3,)),
            dma((3,)),
            dma((3,)),
            dma((6,)),
            dma((count,)),
            dma((2,)),
            dma((count,)),
            dma((count,)),
            dma((3,)),
            dma((3,)),
            dma((2, count)),
            dma((UNITS,)),
            dma((3, UNITS)),
            dma((3, UNITS)),
            dma((3,)),
            dma((3,)),
        ]
        + carry_scratch("attn", rows, count, dp_count),
        compiler_params=pltpu.CompilerParams(
            collective_id=1, has_side_effects=True, vmem_limit_bytes=VMEM_LIMIT
        ),
        cost_estimate=pl.CostEstimate(flops=2 * 10**10, bytes_accessed=10**8, transcendentals=0),
        name="tail",
    )(attn.reshape(2, 2, count, rows, D), done, feed_low, feed_high, dout, *pieces, momenta)


def embed_kernel(
    count,
    frames_ref,
    mask_ref,
    in_ref,
    outer_ref,
    attn_mom_ref,
    up_mom_ref,
    down_mom_ref,
    x_ref,
    mem_ref,
    total_ref,
    owned_ref,
    got_s,
    count_s,
    mom_s,
    mom_sem,
    frame_send,
    frame_recv,
    count_send,
    count_recv,
):
    seg = lax.axis_index("seg")
    after, before = lax.rem(seg + 1, count), lax.rem(seg + count - 1, count)
    streams = frames_ref.shape[0]
    group = lax.rem(lax.axis_index("dp"), GROUPS)
    for depth in range(LAYERS):
        pltpu.make_async_copy(attn_mom_ref.at[depth, group], mom_s.at[depth], mom_sem.at[0]).start()

        @pl.when(group == FEED_UP[depth])
        def _():
            for tile in range(4):
                source = up_mom_ref.at[depth, :, pl.ds(tile * TILE, TILE)]
                pltpu.make_async_copy(source, mom_s.at[2 + tile], mom_sem.at[0]).start()

        @pl.when(group == FEED_DOWN[depth])
        def _():
            pltpu.make_async_copy(down_mom_ref.at[depth], mom_s.at[2:6], mom_sem.at[0]).start()

    tally = jnp.sum(mask_ref[...].astype(f32), 1, keepdims=True)
    count_s[seg] = jnp.broadcast_to(
        jnp.concatenate([tally, jnp.zeros((8 - streams, 1), f32)], 0), (8, 128)
    )
    greet(seg, count, (), ())
    frame_copy = remote(frames_ref, got_s, frame_send.at[0], frame_recv.at[0], {"seg": after})
    frame_copy.start()
    for step, other in enumerate(others(seg, count)):
        remote(count_s.at[seg], count_s.at[seg], count_send.at[step], count_recv.at[seg], {"seg": other}).start()
    weight, shift = in_ref[...], outer_ref[0:1, :]
    for stream in range(streams):
        x_ref[stream] = dot_nn(jnp.transpose(frames_ref[stream]), weight) + shift
    wait_bytes(mom_s, mom_sem.at[0])
    owned_ref[...] = mom_s[...].astype(bf16)
    frame_copy.wait()
    for stream in range(streams):
        mem_ref[stream] = (dot_nn(jnp.transpose(got_s[stream]), weight) + shift).astype(bf16)
    for other in others(seg, count):
        wait_bytes(count_s.at[other], count_recv.at[other])
    total_ref[...] = jnp.sum(count_s[...], 0)
    for step in range(count - 1):
        wait_bytes(count_s.at[0], count_send.at[step])


def embed(count, frames, mask, in_weight, outer_vectors, attn_mom, up_mom, down_mom):
    streams = frames.shape[0]
    rows = D // count
    dma = pltpu.SemaphoreType.DMA
    return pl.pallas_call(
        functools.partial(embed_kernel, count),
        out_shape=[
            jax.ShapeDtypeStruct((streams, SEG, D), f32),
            jax.ShapeDtypeStruct((streams, SEG, D), bf16),
            jax.ShapeDtypeStruct((8, 128), f32),
            jax.ShapeDtypeStruct((UNITS, rows, D), bf16),
        ],
        in_specs=[pl.BlockSpec(memory_space=pltpu.VMEM)] * 4 + [pl.BlockSpec(memory_space=pl.ANY)] * 3,
        out_specs=[pl.BlockSpec(memory_space=pltpu.VMEM)] * 4,
        scratch_shapes=[
            pltpu.VMEM(frames.shape, bf16),
            pltpu.VMEM((count, 8, 128), f32),
            pltpu.VMEM((UNITS, rows, D), f32),
            dma((1,)),
            dma((1,)),
            dma((1,)),
            dma((count,)),
            dma((count,)),
        ],
        compiler_params=pltpu.CompilerParams(
            collective_id=3, has_side_effects=True, vmem_limit_bytes=VMEM_LIMIT
        ),
        cost_estimate=pl.CostEstimate(flops=2 * 10**8, bytes_accessed=4 * 10**6, transcendentals=0),
        name="embed",
    )(frames, mask, in_weight, outer_vectors, attn_mom, up_mom, down_mom.reshape(LAYERS, 4, rows, D))


FEED_UP = (1, 0)
FEED_DOWN = (2, 3)
KEEP = 1.0 - 0.3 * 0.01


def finish_kernel(norm_ref, every_ref, update_ref, dout_ref, small_ref, *refs):
    (
        attn_ref,
        attn_mom_ref,
        up_ref,
        up_mom_ref,
        down_ref,
        down_mom_ref,
        out_ref,
        out_mom_ref,
        out_sec_ref,
        in_ref,
        in_mom_ref,
        in_sec_ref,
        vec_ref,
        vec_mom_ref,
        vec_sec_ref,
        outer_ref,
        outer_mom_ref,
        outer_sec_ref,
        attn_new,
        attn_mom_new,
        attn_copy_new,
        up_new,
        up_mom_new,
        up_copy_new,
        down_new,
        down_mom_new,
        down_copy_new,
        out_new,
        out_mom_new,
        out_sec_new,
        out_copy_new,
        in_new,
        in_mom_new,
        in_sec_new,
        in_copy_new,
        vec_new,
        vec_mom_new,
        vec_sec_new,
        outer_new,
        outer_mom_new,
        outer_sec_new,
        loss_new,
        norm_new,
    ) = refs
    clip = clip_of(norm_ref[0:1, 0:1])

    def muon_step(weight, momentum, grad, update, scale):
        weight = weight * KEEP - (0.3 * scale) * update.astype(f32)
        return weight, 0.5 * momentum + clip * grad.astype(f32)

    up_scale, down_scale = max(1.0, FF / D) ** 0.5, max(1.0, D / FF) ** 0.5
    for depth in range(LAYERS):
        for kind in range(4):
            weight, momentum = muon_step(
                attn_ref[depth, kind],
                attn_mom_ref[depth, kind],
                every_ref[kind, depth],
                update_ref[kind, depth],
                1.0,
            )
            attn_new[depth, kind] = weight
            attn_mom_new[depth, kind] = momentum
            attn_copy_new[depth, kind] = weight.astype(bf16)
            columns = slice(kind * TILE, (kind + 1) * TILE)
            weight, momentum = muon_step(
                up_ref[depth, :, columns],
                up_mom_ref[depth, :, columns],
                every_ref[FEED_UP[depth], 2 + kind],
                update_ref[FEED_UP[depth], 2 + kind],
                up_scale,
            )
            up_new[depth, :, columns] = weight
            up_mom_new[depth, :, columns] = momentum
            up_copy_new[depth, :, columns] = weight.astype(bf16)
            weight, momentum = muon_step(
                down_ref[depth, kind],
                down_mom_ref[depth, kind],
                every_ref[FEED_DOWN[depth], 2 + kind],
                update_ref[FEED_DOWN[depth], 2 + kind],
                down_scale,
            )
            down_new[depth, kind] = weight
            down_mom_new[depth, kind] = momentum
            down_copy_new[depth, kind] = weight.astype(bf16)
    for low in range(2):
        for right in range(2):
            columns = slice(right * D, (right + 1) * D)
            weight, moment, second = adamw(
                out_ref[low, :, columns],
                out_mom_ref[low, :, columns],
                out_sec_ref[low, :, columns],
                dout_ref[2 * right + low].astype(f32) * clip,
                0.05,
                0.01,
            )
            out_new[low, :, columns] = weight
            out_mom_new[low, :, columns] = moment
            out_sec_new[low, :, columns] = second
            out_copy_new[low, :, columns] = weight.astype(bf16)

    @pl.when(pl.program_id(0) == 0)
    def _():
        inputs = in_ref.shape[0]
        weight, moment, second = adamw(
            in_ref[...], in_mom_ref[...], in_sec_ref[...], small_ref[0:inputs, :] * clip, 0.05, 0.01
        )
        in_new[...] = weight
        in_mom_new[...] = moment
        in_sec_new[...] = second
        in_copy_new[...] = weight.astype(bf16)

        norm_new[...] = norm_ref[0:1, 0:1]
        loss_new[...] = small_ref[inputs + 37 : inputs + 38, 0:1]

        def rows_of(first, last, base):
            return small_ref[inputs + base + first : inputs + base + last, :]

        for depth in range(LAYERS):
            base = 16 * depth
            for low, high, grad in (
                (0, 2, rows_of(0, 2, base)),
                (2, 4, rows_of(0, 2, base + 8)),
                (4, 7, rows_of(2, 5, base)),
                (7, 8, rows_of(2, 3, base + 8)),
                (8, 12, rows_of(4, 8, base + 8)),
            ):
                weight, moment, second = adamw(
                    vec_ref[low:high, depth],
                    vec_mom_ref[low:high, depth],
                    vec_sec_ref[low:high, depth],
                    grad * clip,
                    0.25,
                    0.0,
                )
                vec_new[low:high, depth] = weight
                vec_mom_new[low:high, depth] = moment
                vec_sec_new[low:high, depth] = second
        for low, high, grad in ((0, 1, rows_of(5, 6, 0)), (1, 5, rows_of(1, 5, 32))):
            weight, moment, second = adamw(
                outer_ref[low:high, :], outer_mom_ref[low:high, :], outer_sec_ref[low:high, :], grad * clip, 0.25, 0.0
            )
            outer_new[low:high, :] = weight
            outer_mom_new[low:high, :] = moment
            outer_sec_new[low:high, :] = second


def finish(rows, norm, every, updates, dout, small, arrays):
    steps = rows // 16
    attn, _, up, _, down, _, out, _, _, inp, _, _, vec, _, _, outer, _, _ = arrays
    codes = out.shape[2]
    part = out.shape[1] // steps
    blocks = pl.BlockSpec((GROUPS, UNITS, 16, D), lambda i: (0, 0, i, 0))
    attn_spec = pl.BlockSpec((LAYERS, 4, 16, D), lambda i: (0, 0, i, 0))
    up_spec = pl.BlockSpec((LAYERS, 16, FF), lambda i: (0, i, 0))
    out_spec = pl.BlockSpec((2, part, codes), lambda i: (0, i, 0))
    dout_spec = pl.BlockSpec((GROUPS, part, D), lambda i: (0, i, 0))
    in_spec, vec_spec, outer_spec = whole_spec(inp.shape), whole_spec(vec.shape), whole_spec(outer.shape)

    def like(array, dtype=f32):
        return jax.ShapeDtypeStruct(array.shape, dtype)

    return pl.pallas_call(
        finish_kernel,
        grid=(steps,),
        out_shape=[like(attn), like(attn), like(attn, bf16)]
        + [like(up), like(up), like(up, bf16)]
        + [like(down), like(down), like(down, bf16)]
        + [like(out)] * 3
        + [like(out, bf16)]
        + [like(inp)] * 3
        + [like(inp, bf16)]
        + [like(vec)] * 3
        + [like(outer)] * 3
        + [jax.ShapeDtypeStruct((1, 1), f32)] * 2,
        in_specs=[whole_spec((8, 128)), blocks, blocks, dout_spec, whole_spec(small.shape)]
        + [attn_spec] * 2
        + [up_spec] * 2
        + [attn_spec] * 2
        + [out_spec] * 3
        + [in_spec] * 3
        + [vec_spec] * 3
        + [outer_spec] * 3,
        out_specs=[attn_spec] * 3
        + [up_spec] * 3
        + [attn_spec] * 3
        + [out_spec] * 4
        + [in_spec] * 4
        + [vec_spec] * 3
        + [outer_spec] * 3
        + [whole_spec((1, 1))] * 2,
        compiler_params=pltpu.CompilerParams(vmem_limit_bytes=VMEM_LIMIT),
        cost_estimate=pl.CostEstimate(flops=10**8, bytes_accessed=4 * 10**7, transcendentals=0),
        name="finish",
    )(norm, every, updates, dout, small, *arrays)


def local(
    frames,
    speech_mask,
    targets,
    in_proj,
    in_moment,
    in_second,
    out_proj,
    out_moment,
    out_second,
    layer_vectors,
    vectors_moment,
    vectors_second,
    outer_vectors,
    outer_moment,
    outer_second,
    attn_proj,
    attn_momentum,
    ff_up,
    up_momentum,
    ff_down,
    down_momentum,
    in_copy,
    out_copy,
    attn_copy,
    up_copy,
    down_copy,
):
    segment = lax.axis_index("seg")
    count, dp_count = lax.axis_size("seg"), lax.axis_size("dp")
    rows = D // count
    streams = frames.shape[0]
    stream_total = streams * dp_count
    frames_t = jnp.swapaxes(frames, 1, 2)
    bias = jnp.where(segment > 0, 0.0, -1e30).astype(f32)[None]
    hidden, memory, totals, owned = embed(
        count, frames_t, speech_mask, in_copy, outer_vectors, attn_momentum, up_momentum, down_momentum
    )
    momenta = lax.all_gather(owned, "seg", axis=0, tiled=False)
    memory = [memory] * streams
    kept = []
    for depth in range(LAYERS):
        saved, passed = None, []
        for stream in range(streams):
            saved, short = forward_layer(
                depth,
                stream,
                streams,
                bias,
                hidden,
                memory[stream],
                attn_copy,
                up_copy,
                down_copy,
                layer_vectors,
                saved,
            )
            if depth + 1 < LAYERS:
                passed.append(from_behind(short, "seg", 1))
        kept.append((hidden, saved[8], saved))
        hidden = saved[0]
        memory = passed
    grad_hidden, grad_out, head_outer = head(
        hidden, targets, speech_mask, totals, out_copy, outer_vectors, 1.0 / stream_total, momenta
    )
    vector_grads, feed_done = [], [None, None]
    carried = grad_out.reshape(GROUPS * D // 2, D)
    carried_done = []
    for depth in reversed(range(LAYERS)):
        entering, held, saved = kept[depth]
        dafter, grad_up, grad_down, feed_vec, sums = feed_back(
            depth, grad_hidden, saved[7], up_copy, down_copy, layer_vectors, count, dp_count, carried
        )
        grad_hidden, grad_attn, attn_vec, grad_in, feed_done[depth], done = attend_back(
            depth,
            bias,
            dafter,
            entering,
            held,
            saved[1:7],
            attn_copy,
            layer_vectors,
            frames_t,
            grad_up,
            grad_down,
            sums,
            count,
            dp_count,
        )
        carried_done.append(done)
        carried = grad_attn.reshape(4 * D, D)
        vector_grads = [attn_vec, feed_vec] + vector_grads
    out_done, attn_done = carried_done
    every_out = lax.all_gather(out_done, ("dp", "seg"), axis=0, tiled=True)[: GROUPS * D // 2]
    every_out = every_out.reshape(GROUPS, D // 2, D)
    updates, every, small, norm = tail(
        count,
        dp_count,
        grad_attn,
        attn_done,
        feed_done[0],
        feed_done[1],
        out_done,
        [grad_in] + vector_grads + [head_outer],
        momenta,
    )
    split = (LAYERS, 4, rows, D)
    halved = (2, D // 2, out_proj.shape[1])
    (
        attn_new,
        attn_mom,
        attn_copy_new,
        up_new,
        up_mom,
        up_copy_new,
        down_new,
        down_mom,
        down_copy_new,
        out_new,
        out_moment_new,
        out_second_new,
        out_copy_new,
        in_new,
        in_moment_new,
        in_second_new,
        in_copy_new,
        vectors_new,
        vectors_moment_new,
        vectors_second_new,
        outer_new,
        outer_moment_new,
        outer_second_new,
        loss_sum,
        norm,
    ) = finish(
        rows,
        norm,
        every,
        updates,
        every_out,
        small,
        [
            attn_proj,
            attn_momentum,
            ff_up,
            up_momentum,
            ff_down.reshape(split),
            down_momentum.reshape(split),
            out_proj.reshape(halved),
            out_moment.reshape(halved),
            out_second.reshape(halved),
            in_proj,
            in_moment,
            in_second,
            jnp.swapaxes(layer_vectors, 0, 1),
            jnp.swapaxes(vectors_moment, 0, 1),
            jnp.swapaxes(vectors_second, 0, 1),
            outer_vectors,
            outer_moment,
            outer_second,
        ],
    )
    return (
        loss_sum.reshape(()),
        norm.reshape(()),
        in_new,
        in_moment_new,
        in_second_new,
        out_new.reshape(out_proj.shape),
        out_moment_new.reshape(out_proj.shape),
        out_second_new.reshape(out_proj.shape),
        jnp.swapaxes(vectors_new, 0, 1),
        jnp.swapaxes(vectors_moment_new, 0, 1),
        jnp.swapaxes(vectors_second_new, 0, 1),
        outer_new,
        outer_moment_new,
        outer_second_new,
        attn_new,
        attn_mom,
        up_new,
        up_mom,
        down_new.reshape(ff_down.shape),
        down_mom.reshape(ff_down.shape),
        in_copy_new,
        out_copy_new.reshape(out_proj.shape),
        attn_copy_new,
        up_copy_new,
        down_copy_new.reshape(ff_down.shape),
    )


def solution(mesh):
    return jax.shard_map(
        local,
        mesh=mesh,
        in_specs=(
            P("dp", "seg", None),
            P("dp", "seg"),
            P("dp", "seg"),
            P(),
            P(),
            P(),
            P(),
            P(),
            P(),
            P(),
            P(),
            P(),
            P(),
            P(),
            P(),
            P(None, None, "seg", None),
            P(None, None, "seg", None),
            P(None, "seg", None),
            P(None, "seg", None),
            P(None, "seg", None),
            P(None, "seg", None),
            P(),
            P(),
            P(),
            P(),
            P(),
        ),
        out_specs=(
            P(),
            P(),
            P(),
            P(),
            P(),
            P(),
            P(),
            P(),
            P(),
            P(),
            P(),
            P(),
            P(),
            P(),
            P(None, None, "seg", None),
            P(None, None, "seg", None),
            P(None, "seg", None),
            P(None, "seg", None),
            P(None, "seg", None),
            P(None, "seg", None),
            P(),
            P(),
            P(None, None, "seg", None),
            P(None, "seg", None),
            P(None, "seg", None),
        ),
        check_vma=False,
    )
```

```python
import functools
import math

import jax
import jax.numpy as jnp
from jax import lax
from jax.experimental import pallas as pl
from jax.experimental.pallas import tpu as pltpu
from jax.sharding import PartitionSpec as P

D = 512
HEAD_DIM = 64
HEADS = D // HEAD_DIM
FF = 2048
LAYERS = 2
STEP = 10
SEG = 512
HALF = 256
PAIR = 2 * HEAD_DIM
TILE = 512
VMEM_LIMIT = 56 * 1024 * 1024
TAIL_LIMIT = 32 * 1024 * 1024
GELU_SCALE = math.sqrt(2.0 / math.pi)

f32 = jnp.float32
bf16 = jnp.bfloat16


def dot_nn(left, right):
    return lax.dot_general(left, right, (((1,), (0,)), ((), ())), preferred_element_type=f32)


def dot_nt(left, right):
    return lax.dot_general(left, right, (((1,), (1,)), ((), ())), preferred_element_type=f32)


def dot_tn(left, right):
    return lax.dot_general(left, right, (((0,), (0,)), ((), ())), preferred_element_type=f32)


def normalised(values):
    centred = values - jnp.mean(values, -1, keepdims=True)
    scale = lax.rsqrt(jnp.mean(centred * centred, -1, keepdims=True) + 1e-05)
    return centred * scale, scale


def norm_back(grad, gain, unit, scale):
    part = grad * gain
    mean_part = jnp.mean(part, -1, keepdims=True)
    mean_unit = jnp.mean(part * unit, -1, keepdims=True)
    return scale * (part - mean_part - unit * mean_unit)


def column_sum(values):
    return jnp.sum(values, 0, keepdims=True)


def head_masks():
    lane = lax.broadcasted_iota(jnp.int32, (1, PAIR), 1)
    return (lane < HEAD_DIM).astype(bf16), (lane >= HEAD_DIM).astype(bf16)


def pair_lanes(pair):
    return pl.ds(pl.multiple_of(pair * PAIR, PAIR), PAIR)


def forward_kernel(
    depth,
    stream,
    bias_ref,
    x_ref,
    mem_ref,
    attn_ref,
    up_ref,
    down_ref,
    vec_ref,
    *refs,
):
    (
        hid_ref,
        hid16_ref,
        keyin_out,
        q_out,
        k_out,
        v_out,
        lse_ref,
        mixed_ref,
        after_ref,
        kept_out,
        act_s,
        lse_s,
        up_s,
        down_s,
        keyin_ref,
        q_ref,
        k_ref,
        v_ref,
        in_sem,
        out_sem,
    ) = refs[-20:]
    weights_in = (
        pltpu.make_async_copy(up_ref.at[depth], up_s, in_sem.at[0]),
        pltpu.make_async_copy(down_ref.at[depth], down_s, in_sem.at[1]),
    )
    for copy in weights_in:
        copy.start()
    saved_out = [
        pltpu.make_async_copy(source, target.at[stream], out_sem.at[place])
        for place, (source, target) in enumerate(
            ((keyin_ref, keyin_out), (q_ref, q_out), (k_ref, k_out), (v_ref, v_out))
        )
    ]
    kept_out[...] = mem_ref[...]
    x = x_ref[...]
    own_unit, _ = normalised(x)
    gain, shift = vec_ref[0:1, :], vec_ref[1:2, :]
    normed = (own_unit * gain + shift).astype(bf16)
    mem_unit, _ = normalised(mem_ref[...].astype(f32))
    mem_normed = (mem_unit * gain + shift).astype(bf16)
    keyin_ref[0:SEG, :] = mem_normed
    keyin_ref[SEG:, :] = normed
    q_ref[...] = (dot_nn(normed, attn_ref[0]) + vec_ref[4:5, :]).astype(bf16) * jnp.asarray(HEAD_DIM**-0.5, bf16)
    k_ref[0:SEG, :] = dot_nn(mem_normed, attn_ref[1]).astype(bf16)
    k_ref[SEG:, :] = dot_nn(normed, attn_ref[1]).astype(bf16)
    v_ref[0:SEG, :] = (dot_nn(mem_normed, attn_ref[2]) + vec_ref[5:6, :]).astype(bf16)
    v_ref[SEG:, :] = (dot_nn(normed, attn_ref[2]) + vec_ref[5:6, :]).astype(bf16)
    for copy in saved_out:
        copy.start()
    first, second = head_masks()
    memory_bias = bias_ref[0]
    lane = lax.broadcasted_iota(jnp.int32, (HALF, PAIR), 1)
    query_pos = lax.broadcasted_iota(jnp.int32, (2 * HALF, HALF), 0) % HALF
    key_pos = lax.broadcasted_iota(jnp.int32, (2 * HALF, HALF), 1)
    diagonal = key_pos <= query_pos
    lse_s[...] = jnp.zeros_like(lse_s)

    def pair_body(pair, carry):
        lanes = pair_lanes(pair)
        blocks = []
        for block in range(2):
            rows = slice(block * HALF, (block + 1) * HALF)
            q_pair = q_ref[rows, lanes]
            q_both = jnp.concatenate([q_pair * first, q_pair * second], 0)
            spans = [(0, SEG)]
            if block:
                spans.append((SEG, SEG + HALF))
            spans.append((SEG + block * HALF, SEG + (block + 1) * HALF))
            scores = [dot_nt(q_both, k_ref[low:high, lanes]) for low, high in spans]
            scores[-1] = jnp.where(diagonal, scores[-1], -1e30)
            blocks.append((rows, spans, scores))
        results = []
        for rows, spans, scores in blocks:
            peaks = [jnp.max(part, -1, keepdims=True) for part in scores]
            peaks[0] = peaks[0] + memory_bias
            most = functools.reduce(jnp.maximum, peaks)
            weights = [
                jnp.exp(part - (most if place else most - memory_bias)) for place, part in enumerate(scores)
            ]
            total = functools.reduce(jnp.add, [jnp.sum(part, -1, keepdims=True) for part in weights])
            mixed = functools.reduce(
                jnp.add,
                [
                    dot_nn(part.astype(bf16), v_ref[low:high, lanes])
                    for part, (low, high) in zip(weights, spans)
                ],
            )
            results.append((rows, mixed / total, most + jnp.log(total)))
        for rows, mixed, lse in results:
            mixed_ref[rows, lanes] = jnp.where(lane < HEAD_DIM, mixed[:HALF], mixed[HALF:]).astype(bf16)
            kept = jnp.where(lane == 2 * pair, lse[:HALF], lse_s[rows, :])
            lse_s[rows, :] = jnp.where(lane == 2 * pair + 1, lse[HALF:], kept)
        return carry

    lax.fori_loop(0, HEADS // 2, pair_body, 0)
    lse_ref[...] = jnp.transpose(lse_s[...])[0:HEADS, :]
    after = x + (dot_nn(mixed_ref[...], attn_ref[3]) + vec_ref[6:7, :])
    after_ref[...] = after
    unit, _ = normalised(after)
    normed_two = (unit * vec_ref[2:3, :] + vec_ref[3:4, :]).astype(bf16)
    for copy in weights_in:
        copy.wait()
    for tile in range(FF // TILE):
        columns = slice(tile * TILE, (tile + 1) * TILE)
        inner = dot_nn(normed_two, up_s[:, columns]) + vec_ref[8 + tile : 9 + tile, :]
        act_s[:, columns] = (
            0.5 * inner * (1.0 + jnp.tanh(GELU_SCALE * (inner + 0.044715 * inner * inner * inner)))
        ).astype(bf16)
    hidden = after + (dot_nn(act_s[...], down_s[...]) + vec_ref[7:8, :])
    hid_ref[...] = hidden
    hid16_ref[...] = hidden.astype(bf16)
    for copy in saved_out:
        copy.wait()


SAVED = (
    ((SEG, D), f32),
    ((2 * SEG, D), bf16),
    ((SEG, D), bf16),
    ((2 * SEG, D), bf16),
    ((2 * SEG, D), bf16),
    ((HEADS, SEG), f32),
    ((SEG, D), bf16),
    ((SEG, D), f32),
    ((SEG, D), bf16),
)


def whole_spec(shape):
    return pl.BlockSpec(shape, lambda *_: (0,) * len(shape))


def stream_spec(shape, stream=None):
    zeros = (0,) * len(shape)
    if stream is None:
        return pl.BlockSpec((None,) + shape, lambda i: (i,) + zeros)
    return pl.BlockSpec((None,) + shape, lambda i: (stream,) + zeros)


def layer_spec(shape, depth):
    zeros = (0,) * len(shape)
    return pl.BlockSpec((None,) + shape, lambda *_: (depth,) + zeros)


def forward_layer(depth, stream, streams, bias, hidden, memory, attn, upper, lower, vectors, earlier):
    saved_shapes = [jax.ShapeDtypeStruct((streams,) + shape, dtype) for shape, dtype in SAVED]
    saved_specs = [stream_spec(shape, stream) for shape, dtype in SAVED]
    out_shape = [saved_shapes[0], jax.ShapeDtypeStruct((SEG, D), bf16)] + saved_shapes[1:]
    out_specs = [saved_specs[0], whole_spec((SEG, D))] + saved_specs[1:]
    for place in (2, 3, 4, 5):
        out_specs[place] = pl.BlockSpec(memory_space=pl.ANY)
    operands = [bias, hidden, memory, attn, upper, lower, vectors]
    in_specs = [
        pl.BlockSpec(memory_space=pltpu.SMEM),
        stream_spec((SEG, D), stream),
        stream_spec((SEG, D), stream) if memory.ndim == 3 else whole_spec((SEG, D)),
        layer_spec(attn.shape[1:], depth),
        pl.BlockSpec(memory_space=pl.ANY),
        pl.BlockSpec(memory_space=pl.ANY),
        layer_spec(vectors.shape[1:], depth),
    ]
    aliases = {}
    if earlier is not None:
        for place, array in enumerate(earlier):
            aliases[len(operands)] = place if place == 0 else place + 1
            operands.append(array)
            in_specs.append(pl.BlockSpec(memory_space=pl.ANY))
    out = pl.pallas_call(
        functools.partial(forward_kernel, depth, stream),
        grid=(1,),
        out_shape=out_shape,
        in_specs=in_specs,
        out_specs=out_specs,
        scratch_shapes=[
            pltpu.VMEM((SEG, FF), bf16),
            pltpu.VMEM((SEG, PAIR), f32),
            pltpu.VMEM((D, FF), bf16),
            pltpu.VMEM((FF, D), bf16),
            pltpu.VMEM((2 * SEG, D), bf16),
            pltpu.VMEM((SEG, D), bf16),
            pltpu.VMEM((2 * SEG, D), bf16),
            pltpu.VMEM((2 * SEG, D), bf16),
            pltpu.SemaphoreType.DMA((2,)),
            pltpu.SemaphoreType.DMA((4,)),
        ],
        input_output_aliases=aliases,
        compiler_params=pltpu.CompilerParams(vmem_limit_bytes=VMEM_LIMIT),
        cost_estimate=pl.CostEstimate(flops=10**10, bytes_accessed=2 * 10**7, transcendentals=10**7),
        name="layer_forward",
    )(*operands)
    return [out[0]] + list(out[2:]), out[1]


def head_kernel(scale, x_ref, target_ref, mask_ref, total_ref, out_ref, outer_ref, mom_ref, g_ref, dout_ref, douter_ref, acc_s):
    step = pl.program_id(0)

    @pl.when(step == 0)
    def _():
        acc_s[...] = jnp.zeros_like(acc_s)
        douter_ref[...] = jnp.zeros_like(douter_ref)

    unit, rscale = normalised(x_ref[...])
    gain = outer_ref[1:2, :]
    normed = (unit * gain + outer_ref[2:3, :]).astype(bf16)
    shift = jnp.concatenate([outer_ref[3:4, :], outer_ref[4:5, :]], 1)
    logits = dot_nn(normed, out_ref[...]) + shift
    most = jnp.max(logits, -1, keepdims=True)
    powers = jnp.exp(logits - most)
    total = jnp.sum(powers, -1, keepdims=True)
    target_row = target_ref[pl.ds(step, 1), :].astype(f32)
    weight_row = mask_ref[pl.ds(step, 1), :].astype(f32) * (1.0 / total_ref[pl.ds(step, 1), 0:1])
    columns = jnp.transpose(jnp.concatenate([target_row, weight_row, jnp.zeros((6, SEG), f32)], 0))
    target, weight = columns[:, 0:1].astype(jnp.int32), columns[:, 1:2]
    chosen = lax.broadcasted_iota(jnp.int32, logits.shape, 1) == target
    picked = jnp.sum(jnp.where(chosen, logits, 0.0), -1, keepdims=True)
    loss = jnp.sum(weight * (most + jnp.log(total) - picked), 0, keepdims=True)
    spread = weight * scale
    dlogits = (powers * (spread / total) - jnp.where(chosen, spread, 0.0)).astype(bf16)
    acc_s[...] += dot_nn(jnp.transpose(normed), dlogits)
    bias_grad = column_sum(dlogits.astype(f32))
    dnormed = dot_nt(dlogits, out_ref[...])
    g_ref[...] = norm_back(dnormed, gain, unit, rscale)
    douter_ref[1:2, :] += column_sum(dnormed * unit)
    douter_ref[2:3, :] += column_sum(dnormed)
    douter_ref[3:4, :] += bias_grad[:, :D]
    douter_ref[4:5, :] += bias_grad[:, D:]
    douter_ref[5:6, :] += jnp.broadcast_to(loss, (1, D))

    @pl.when(step == pl.num_programs(0) - 1)
    def _():
        half = D // 2
        for right in range(2):
            for low in range(2):
                dout_ref[right, low] = acc_s[
                    low * half : (low + 1) * half, right * D : (right + 1) * D
                ]


def head(hidden, targets, mask, totals, out_weight, outer_vectors, scale, momenta):
    streams = hidden.shape[0]
    codes = out_weight.shape[1]
    return pl.pallas_call(
        functools.partial(head_kernel, scale),
        grid=(streams,),
        out_shape=[
            jax.ShapeDtypeStruct((streams, SEG, D), f32),
            jax.ShapeDtypeStruct((2, 2, D // 2, D), f32),
            jax.ShapeDtypeStruct((8, D), f32),
        ],
        in_specs=[
            stream_spec((SEG, D)),
            whole_spec((streams, SEG)),
            whole_spec((streams, SEG)),
            whole_spec((8, 128)),
            whole_spec((D, codes)),
            whole_spec(outer_vectors.shape),
            pl.BlockSpec(memory_space=pl.ANY),
        ],
        out_specs=[stream_spec((SEG, D)), whole_spec((2, 2, D // 2, D)), whole_spec((8, D))],
        scratch_shapes=[pltpu.VMEM((D, codes), f32)],
        compiler_params=pltpu.CompilerParams(vmem_limit_bytes=VMEM_LIMIT),
        cost_estimate=pl.CostEstimate(flops=33 * 10**8, bytes_accessed=10**7, transcendentals=10**6),
        name="head",
    )(hidden, targets, mask, totals, out_weight, outer_vectors, momenta)


def feed_back_kernel(streams, g_ref, after_ref, up_ref, down_ref, vec_ref, *refs):
    step = pl.program_id(0)
    grad_ref, dafter_ref, dup_ref, ddown_ref, dvec_ref, done_ref, normed_s, branch_s, act_s, inner_s = refs[:10]
    carry = AttnCarry(grad_ref, refs[10 : 10 + CARRY_REFS], refs[10 + CARRY_REFS :], done_ref)
    planes = carry.planes
    early, late = range(planes // 2), range(planes // 2, planes)
    beats = [
        [("b", place) for place in range(planes)],
        [("m", place) for place in early],
        [("m", place) for place in late],
        [("e", place) for place in early],
        [("e", place) for place in late],
    ]

    @pl.when(step == 0)
    def _():
        hail(carry.targets)
        carry.load_all()
        dvec_ref[...] = jnp.zeros_like(dvec_ref)

    rows = pl.ds(pl.multiple_of(step * SEG, SEG), SEG)
    grad = g_ref[...]
    branch = grad.astype(bf16)
    dvec_ref[2:3, :] += column_sum(branch.astype(f32))
    unit, scale = normalised(after_ref[...])
    gain = vec_ref[2:3, :]
    normed = (unit * gain + vec_ref[3:4, :]).astype(bf16)
    normed_s[:, rows] = jnp.transpose(normed)
    branch_s[:, rows] = jnp.transpose(branch)

    @pl.when(step == 0)
    def _():
        meet(carry.targets)
        carry.send_all()

    for tile in range(FF // TILE):
        columns = slice(tile * TILE, (tile + 1) * TILE)
        inner = dot_nn(normed, up_ref[:, columns]) + vec_ref[8 + tile : 9 + tile, :]
        dact = dot_nt(branch, down_ref[columns, :])
        square = inner * inner
        bent = jnp.tanh(inner * (GELU_SCALE + (GELU_SCALE * 0.044715) * square))
        half = 0.5 * (1.0 + bent)
        act_s[rows, columns] = (inner * half).astype(bf16)
        slope = half + inner * (half * (1.0 - bent)) * (GELU_SCALE + (GELU_SCALE * 0.134145) * square)
        dinner = (dact * slope).astype(bf16)
        inner_s[rows, columns] = dinner
        dvec_ref[4 + tile : 5 + tile, :] += column_sum(dinner.astype(f32))

    @pl.when(step == 0)
    def _():
        carry.run(beats[0])

    @pl.when(step == streams - 1)
    def _():
        carry.run(beats[1])

    dnormed = dot_nt(inner_s[rows, :], up_ref[...])
    dvec_ref[0:1, :] += column_sum(dnormed * unit)
    dvec_ref[1:2, :] += column_sum(dnormed)
    dafter_ref[...] = grad + norm_back(dnormed, gain, unit, scale)

    @pl.when(step == streams - 1)
    def _():
        carry.run(beats[2])
        for tile in range(FF // TILE):
            columns = slice(tile * TILE, (tile + 1) * TILE)
            dup_ref[tile] = dot_nn(normed_s[...], inner_s[:, columns]).astype(bf16)
        carry.run(beats[3])
        for tile in range(FF // TILE):
            columns = slice(tile * TILE, (tile + 1) * TILE)
            ddown_ref[columns, :] = jnp.transpose(dot_nn(branch_s[...], act_s[:, columns]).astype(bf16))
        carry.run(beats[4])
        carry.drain()


def feed_back(depth, grad, after, upper, lower, vectors, count, dp_count, attn_grad):
    streams = grad.shape[0]
    rows = attn_grad.shape[0] // (GROUPS * count)
    in_specs = [
        stream_spec((SEG, D)),
        stream_spec((SEG, D)),
        layer_spec(upper.shape[1:], depth),
        layer_spec(lower.shape[1:], depth),
        layer_spec(vectors.shape[1:], depth),
    ]
    out_shape = [
        jax.ShapeDtypeStruct((streams, SEG, D), f32),
        jax.ShapeDtypeStruct((FF // TILE, D, TILE), bf16),
        jax.ShapeDtypeStruct((FF, D), bf16),
        jax.ShapeDtypeStruct((8, D), f32),
    ]
    out_specs = [
        stream_spec((SEG, D)),
        whole_spec((FF // TILE, D, TILE)),
        whole_spec((FF, D)),
        whole_spec((8, D)),
    ]
    scratch = [
        pltpu.VMEM((D, streams * SEG), bf16),
        pltpu.VMEM((D, streams * SEG), bf16),
        pltpu.VMEM((streams * SEG, FF), bf16),
        pltpu.VMEM((streams * SEG, FF), bf16),
    ]
    operands = [grad, after, upper, lower, vectors]
    in_specs.append(pl.BlockSpec(memory_space=pl.ANY))
    operands.append(attn_grad.reshape(2, 2, count, rows, D))
    out_shape.append(jax.ShapeDtypeStruct((count // 2, rows, D), attn_grad.dtype))
    out_specs.append(whole_spec((count // 2, rows, D)))
    scratch = scratch + carry_scratch("attn", rows, count, dp_count, attn_grad.dtype)
    params = {"collective_id": 6 + depth, "has_side_effects": True}
    return pl.pallas_call(
        functools.partial(feed_back_kernel, streams),
        grid=(streams,),
        out_shape=out_shape,
        in_specs=in_specs,
        out_specs=out_specs,
        scratch_shapes=scratch,
        compiler_params=pltpu.CompilerParams(vmem_limit_bytes=VMEM_LIMIT, **params),
        cost_estimate=pl.CostEstimate(flops=11 * 10**9, bytes_accessed=2 * 10**7, transcendentals=2 * 10**6),
        name="feed_back",
    )(*operands)


def attend_back_kernel(
    streams,
    depth,
    bias_ref,
    dafter_ref,
    x_ref,
    mem_ref,
    keyin_ref,
    q_ref,
    k_ref,
    v_ref,
    lse_ref,
    mixed_ref,
    attn_ref,
    vec_ref,
    frames_ref,
    dup_ref,
    ddown_ref,
    sums_ref,
    dx_ref,
    dattn_ref,
    dvec_ref,
    din_ref,
    done_ref,
    along_ref,
    attn_s,
    dmixed_s,
    dq_s,
    dk_s,
    dv_s,
    ds_s,
    delta_s,
    *refs,
):
    step = pl.program_id(0)
    pairs = HEADS // 2
    split = CARRY_REFS + 1 + CARRY_SEMS
    carry = FeedCarry(depth, dup_ref, ddown_ref, refs[: CARRY_REFS + 1], refs[CARRY_REFS + 1 : split])
    along = ZCarry(refs[split : split + Z_REFS], refs[split + Z_REFS :])
    plans, (free, bound) = carry.plans(), along.plans()

    @pl.when(step == 0)
    def _():
        hail(carry.targets)
        carry.load_all()
        along.sums[...] = sums_ref[...]
        attn_s[...] = jnp.zeros_like(attn_s)
        dvec_ref[...] = jnp.zeros_like(dvec_ref)
        din_ref[...] = jnp.zeros_like(din_ref)

    dafter = dafter_ref[...]
    branch = dafter.astype(bf16)
    dvec_ref[4:5, :] += column_sum(branch.astype(f32))
    dmixed = dot_nt(branch, attn_ref[3]).astype(bf16)
    dmixed_s[...] = dmixed
    attn_s[3] += dot_nn(jnp.transpose(mixed_ref[...]), branch)
    product = dmixed.astype(f32) * mixed_ref[...].astype(f32)
    high = product.astype(bf16)
    rest = (product - high.astype(f32)).astype(bf16)
    owner = lax.broadcasted_iota(jnp.int32, (HEADS, D), 1) // HEAD_DIM
    pick = (owner == lax.broadcasted_iota(jnp.int32, (HEADS, D), 0)).astype(bf16)
    delta_s[...] = dot_nt(pick, high) + dot_nt(pick, rest)
    first, second = head_masks()
    memory_bias = bias_ref[0]
    key_pos = lax.broadcasted_iota(jnp.int32, (HALF, 2 * HALF), 0)
    query_pos = lax.broadcasted_iota(jnp.int32, (HALF, 2 * HALF), 1) % HALF
    diagonal = key_pos <= query_pos
    head_row = lax.broadcasted_iota(jnp.int32, (PAIR, HALF), 0)

    @pl.when(step == 0)
    def _():
        meet(carry.targets)
        carry.send_all()
        along.run(free)

    @pl.when(step == 1)
    def _():
        carry.run(plans[-1])

    def pair_body(pair, state):
        lanes = pair_lanes(pair)
        q_pair, do_pair = q_ref[:, lanes], dmixed_s[:, lanes]

        def spread(value):
            return jnp.concatenate(
                [value[:HALF] * first, value[:HALF] * second, value[HALF:] * first, value[HALF:] * second], 0
            )

        q_all, do_all = spread(q_pair), spread(do_pair)

        def rows_of(ref):
            one, two = ref[pl.ds(2 * pair, 1), :], ref[pl.ds(2 * pair + 1, 1), :]
            return jnp.concatenate([one[:, :HALF], two[:, :HALF], one[:, HALF:], two[:, HALF:]], 1)

        lse_all, delta_all = rows_of(lse_ref), rows_of(delta_s)
        starts = (0, 0, 0, 2 * HALF)

        def products(block):
            keys = slice(block * HALF, (block + 1) * HALF)
            scores = dot_nt(k_ref[keys, lanes], q_all[starts[block] :])
            return scores, dot_nt(v_ref[keys, lanes], do_all[starts[block] :])

        ahead = products(0)
        for block in range(4):
            scores, dweights = ahead
            if block < 3:
                ahead = products(block + 1)
            keys = slice(block * HALF, (block + 1) * HALF)
            start = starts[block]
            shift = lse_all - memory_bias if block < 2 else lse_all[:, start:]
            weights = jnp.exp(scores - shift)
            if block == 2:
                weights = jnp.concatenate(
                    [jnp.where(diagonal, weights[:, : 2 * HALF], 0.0), weights[:, 2 * HALF :]], 1
                )
            if block == 3:
                weights = jnp.where(diagonal, weights, 0.0)
            dscores = (weights * (dweights - delta_all[:, start:])).astype(bf16)
            dv_s[keys, lanes] = dot_nn(weights.astype(bf16), do_all[start:]).astype(bf16)
            dk_s[keys, lanes] = dot_nn(dscores, q_all[start:]).astype(bf16)
            ds_s[keys, start:] = dscores
        k_t = jnp.transpose(k_ref[:, lanes])
        for block in range(2):
            seen = SEG + (block + 1) * HALF
            grads = dot_nn(k_t[:, :seen], ds_s[:seen, block * 2 * HALF : (block + 1) * 2 * HALF])
            grads = jnp.where(head_row < HEAD_DIM, grads[:, :HALF], grads[:, HALF:])
            dq_s[block * HALF : (block + 1) * HALF, lanes] = (
                jnp.transpose(grads) * (HEAD_DIM**-0.5)
            ).astype(bf16)
        for time, acts in enumerate(plans[:-1]):
            if acts:

                @pl.when(pairs * step + pair == time)
                def _():
                    carry.run(acts)
                    if time == 3:
                        along.run(bound)

        return state

    lax.fori_loop(0, pairs, pair_body, 0)
    dq, dk, dv = dq_s[...], dk_s[...], dv_s[...]
    keyin_t = jnp.transpose(keyin_ref[...])
    attn_s[0] += dot_nn(keyin_t[:, SEG:], dq)
    attn_s[1] += dot_nn(keyin_t, dk)
    attn_s[2] += dot_nn(keyin_t, dv)
    dvec_ref[2:3, :] += column_sum(dq.astype(f32))
    dvec_ref[3:4, :] += column_sum(dv.astype(f32))
    dkeyin = dot_nt(dk, attn_ref[1]) + dot_nt(dv, attn_ref[2])
    dmem = dkeyin[:SEG]
    down = dkeyin[SEG:] + dot_nt(dq, attn_ref[0])
    gain = vec_ref[0:1, :]
    unit, scale = normalised(x_ref[...])
    mem_unit, _ = normalised(mem_ref[...].astype(f32))
    dvec_ref[0:1, :] += column_sum(down * unit + dmem * mem_unit)
    dvec_ref[1:2, :] += column_sum(down + dmem)
    dx = dafter + norm_back(down, gain, unit, scale)
    dx_ref[...] = dx
    if depth == 0:
        dx_high = dx.astype(bf16)
        dx_rest = (dx - dx_high.astype(f32)).astype(bf16)
        din_ref[...] += dot_nn(frames_ref[...], dx_high) + dot_nn(frames_ref[...], dx_rest)
        dvec_ref[5:6, :] += column_sum(dx)

    @pl.when(step == pl.num_programs(0) - 1)
    def _():
        dattn_ref[...] = attn_s[...].astype(bf16)
        carry.finish(done_ref)
        along.finish(along_ref)


def attend_back(depth, bias, dafter, x, memory, saved, attn, vectors, frames, up_grad, down_grad, sums, count, dp_count):
    streams = dafter.shape[0]
    keyin, q, k, v, lse, mixed = saved
    inputs = frames.shape[1]
    rows = D // count
    up_grad, down_grad = up_grad.reshape(4, count, rows, D), down_grad.reshape(count, 4, rows, D)
    return pl.pallas_call(
        functools.partial(attend_back_kernel, streams, depth),
        grid=(streams,),
        out_shape=[
            jax.ShapeDtypeStruct((streams, SEG, D), f32),
            jax.ShapeDtypeStruct((4, D, D), bf16),
            jax.ShapeDtypeStruct((8, D), f32),
            jax.ShapeDtypeStruct((inputs, D), f32),
            jax.ShapeDtypeStruct((2, rows, D), bf16),
            jax.ShapeDtypeStruct(sums.shape[1:], bf16),
        ],
        in_specs=[
            pl.BlockSpec(memory_space=pltpu.SMEM),
            stream_spec((SEG, D)),
            stream_spec((SEG, D)),
            stream_spec((SEG, D)),
            stream_spec((2 * SEG, D)),
            stream_spec((SEG, D)),
            stream_spec((2 * SEG, D)),
            stream_spec((2 * SEG, D)),
            stream_spec((HEADS, SEG)),
            stream_spec((SEG, D)),
            layer_spec(attn.shape[1:], depth),
            layer_spec(vectors.shape[1:], depth),
            stream_spec((inputs, SEG)),
            pl.BlockSpec(memory_space=pl.ANY),
            pl.BlockSpec(memory_space=pl.ANY),
            whole_spec(sums.shape),
        ],
        out_specs=[
            stream_spec((SEG, D)),
            whole_spec((4, D, D)),
            whole_spec((8, D)),
            whole_spec((inputs, D)),
            whole_spec((2, rows, D)),
            whole_spec(sums.shape[1:]),
        ],
        scratch_shapes=[
            pltpu.VMEM((4, D, D), f32),
            pltpu.VMEM((SEG, D), bf16),
            pltpu.VMEM((SEG, D), bf16),
            pltpu.VMEM((2 * SEG, D), bf16),
            pltpu.VMEM((2 * SEG, D), bf16),
            pltpu.VMEM((2 * SEG, 2 * SEG), bf16),
            pltpu.VMEM((HEADS, SEG), f32),
        ]
        + carry_scratch("feed", rows, count, dp_count)
        + z_scratch(sums.shape[1], count, dp_count, sums.dtype),
        compiler_params=pltpu.CompilerParams(
            collective_id=4 + depth, has_side_effects=True, vmem_limit_bytes=VMEM_LIMIT
        ),
        cost_estimate=pl.CostEstimate(flops=3 * 10**10, bytes_accessed=2 * 10**7, transcendentals=10**7),
        name="attend_back",
    )(bias, dafter, x, memory, keyin, q, k, v, lse, mixed, attn, vectors, frames, up_grad, down_grad, sums)


def from_behind(value, axis, steps):
    count = lax.axis_size(axis)
    leading, last = (max(0, -steps), min(count, count - steps))
    return lax.ppermute(value, axis, [(source, source + steps) for source in range(leading, last)])


def adamw(weight, moment, second, grad, rate, decay):
    moment = 0.5 * moment + 0.5 * grad
    second = 0.99 * second + 0.01 * grad * grad
    fixed_moment = moment / (1.0 - 0.5**STEP)
    fixed_second = second / (1.0 - 0.99**STEP)
    weight = weight * (1.0 - rate * decay) - rate * fixed_moment / (jnp.sqrt(fixed_second) + 1e-08)
    return (weight, moment, second)


GROUPS = 4
UNITS = 6
SMALL = 128


def peers():
    count = {"seg": lax.axis_size("seg"), "dp": lax.axis_size("dp")}
    seg, dp = lax.axis_index("seg"), lax.axis_index("dp")
    core, x, y = seg % 2, dp % 2, (dp // 2) % 2
    across_core = {"seg": seg + 1 - 2 * core}
    across_x = {"dp": dp + 1 - 2 * x}
    across_y = {"dp": dp + 2 - 4 * y}
    across_both = {"dp": dp + 3 - 2 * x - 4 * y}
    far = []
    step = GROUPS
    while step < count["dp"]:
        far.append({"dp": dp + step - 2 * step * ((dp // step) % 2)})
        step *= 2
    return seg, dp, core, x, y, across_core, (across_x, across_y, across_both), far


def others(seg, count):
    return [lax.rem(seg + step, count) for step in range(1, count)]


def hail(targets):
    barrier = pltpu.get_barrier_semaphore()
    for target in targets:
        pl.semaphore_signal(barrier, inc=1, device_id=target, device_id_type=pl.DeviceIdType.MESH)


def meet(targets):
    pl.semaphore_wait(pltpu.get_barrier_semaphore(), len(targets))


def greet(seg, count, near, far):
    targets = [{"seg": other} for other in others(seg, count)] + list(near) + list(far)
    hail(targets)
    meet(targets)


def remote(source, target, send, recv, device):
    return pltpu.make_async_remote_copy(
        src_ref=source,
        dst_ref=target,
        send_sem=send,
        recv_sem=recv,
        device_id=device,
        device_id_type=pl.DeviceIdType.MESH,
    )


def wait_bytes(ref, sem):
    pltpu.make_async_copy(ref, ref, sem).wait()


def plus(left, right):
    return (left.astype(f32) + right.astype(f32)).astype(left.dtype)


def owners(count):
    low, high = count // 4 - 1, count // 4
    return (
        (0, 1, 0, 0),
        (1, 1, count - 2, 0),
        (2, 2, 2 * low, 0),
        (4, 2, 2 * low + 1, 2),
        (2, 2, 2 * high, 0),
        (4, 2, 2 * high + 1, 2),
    )


def lowest_bit(mask, planes):
    bit = 1
    while bit < planes and not mask & bit:
        bit *= 2
    return bit


class Carry:
    def __init__(self, refs, sems):
        self.mine, self.got0, self.got1, self.got2, self.got3, self.goth = refs
        (
            self.load,
            self.send0,
            self.recv0,
            self.send1,
            self.recv1,
            self.send2,
            self.recv2,
            self.send3,
            self.recv3,
            self.sendh,
            self.recvh,
        ) = sems
        self.settle(self.mine.shape[0])

    def settle(self, planes):
        self.seg, self.dp, self.core, self.x, self.y, self.across_core, near, self.far = peers()
        self.across_x, self.across_y, _ = near
        self.planes = planes
        self.plane = self.seg // 2
        self.targets = [self.across_core, self.across_x, self.across_y] + self.far
        bit = 1
        while bit < planes:
            self.targets.append({"seg": 2 * self.toggled(bit) + self.core})
            bit *= 2
        self.order = list(reversed(range(planes)))

    def toggled(self, mask):
        place, bit = self.plane, 1
        while bit <= mask:
            if mask & bit:
                place = place + bit - 2 * bit * ((self.plane // bit) % 2)
            bit *= 2
        return place

    def load_all(self):
        for step in range(self.planes):
            for source, place in self.pieces(2 * self.toggled(self.order[step]) + self.core):
                pltpu.make_async_copy(source, self.mine.at[(step,) + place], self.load.at[step]).start()

    def send_all(self):
        for step in range(self.planes):
            for source, place in self.pieces(2 * self.toggled(self.order[step]) + 1 - self.core):
                remote(
                    source, self.got0.at[(step,) + place], self.send0.at[step], self.recv0.at[step], self.across_core
                ).start()

    def begin(self, step):
        wait_bytes(self.mine.at[step], self.load.at[step])
        wait_bytes(self.got0.at[step], self.recv0.at[step])
        for place in range(2):
            self.mine[step, place] = plus(self.mine[step, place], self.got0[step, place])
        for copy in self.first(step):
            copy.start()

    def across(self, place, step):
        return remote(
            self.held(step),
            self.goth.at[place, step],
            self.sendh.at[place, step],
            self.recvh.at[place, step],
            self.far[place],
        )

    def third(self, step):
        mask = self.order[step]
        return remote(
            self.held(step),
            self.got3.at[mask],
            self.send3.at[step],
            self.recv3.at[mask],
            {"seg": 2 * self.toggled(lowest_bit(mask, self.planes)) + self.core},
        )

    def onward(self, step):
        held = self.held(step)
        for place in range(len(self.far)):
            copy = self.across(place, step)
            copy.start()
            copy.wait()
            held[...] = plus(held[...], self.goth[place, step])
        mask = self.order[step]
        if mask:
            self.gathered(mask, held)
            self.third(step).start()

    def gathered(self, mask, held):
        value, bit = held[...].astype(f32), 1
        while bit < lowest_bit(mask, self.planes):
            wait_bytes(self.got3.at[mask + bit], self.recv3.at[mask + bit])
            value = value + self.got3[mask + bit].astype(f32)
            bit *= 2
        held[...] = value.astype(held.dtype)

    def total(self):
        held = self.held(self.planes - 1)
        self.gathered(0, held)
        return held[...]

    def run(self, acts):
        for kind, step in acts:
            getattr(self, {"b": "begin", "m": "middle", "e": "end", "z": "onward"}[kind])(step)


class ZCarry(Carry):
    def __init__(self, refs, sems):
        self.sums, self.got3, self.goth = refs
        self.send3, self.recv3, self.sendh, self.recvh = sems
        self.settle(self.sums.shape[0])

    def held(self, step):
        return self.sums.at[step]

    def plans(self):
        free = [("z", step) for step in range(self.planes) if self.order[step] % 2]
        bound = [("z", step) for step in range(self.planes) if self.order[step] and not self.order[step] % 2]
        return free, bound

    def finish(self, out_ref):
        out_ref[...] = self.total().astype(out_ref.dtype)
        for step in range(self.planes - 1):
            self.third(step).wait_send()


class AttnCarry(Carry):
    def __init__(self, source, refs, sems, sums=None):
        super().__init__(refs, sems)
        self.source, self.sums = source, sums

    def pieces(self, row):
        return ((self.source.at[:, :, row], ()),)

    def held(self, step):
        return self.mine.at[step, self.y, self.x]

    def first(self, step):
        half = self.mine.shape[3] // 2
        return (
            remote(
                self.mine.at[step, :, 1 - self.x, 0:half],
                self.got1.at[step, 0],
                self.send1.at[step, 0],
                self.recv1.at[step, 0],
                self.across_x,
            ),
            remote(
                self.mine.at[step, 1 - self.y, :, half:],
                self.got1.at[step, 1],
                self.send1.at[step, 1],
                self.recv1.at[step, 1],
                self.across_y,
            ),
        )

    def second(self, step):
        half = self.mine.shape[3] // 2
        return (
            remote(
                self.mine.at[step, 1 - self.y, self.x, 0:half],
                self.got2.at[step, 0],
                self.send2.at[step, 0],
                self.recv2.at[step, 0],
                self.across_y,
            ),
            remote(
                self.mine.at[step, self.y, 1 - self.x, half:],
                self.got2.at[step, 1],
                self.send2.at[step, 1],
                self.recv2.at[step, 1],
                self.across_x,
            ),
        )

    def middle(self, step):
        mine, half = self.mine, self.mine.shape[3] // 2
        for copy in self.first(step):
            copy.wait_recv()
        for place in range(2):
            mine[step, place, self.x, 0:half] = plus(mine[step, place, self.x, 0:half], self.got1[step, 0, place])
            mine[step, self.y, place, half:] = plus(mine[step, self.y, place, half:], self.got1[step, 1, place])
        for copy in self.second(step):
            copy.start()

    def end(self, step):
        mine, half = self.mine, self.mine.shape[3] // 2
        for copy in self.second(step):
            copy.wait_recv()
        upper = plus(mine[step, self.y, self.x, 0:half], self.got2[step, 0])
        lower = plus(mine[step, self.y, self.x, half:], self.got2[step, 1])
        if self.sums is not None:
            self.sums[step, 0:half] = upper
            self.sums[step, half:] = lower
            return
        mine[step, self.y, self.x, 0:half] = upper
        mine[step, self.y, self.x, half:] = lower
        self.onward(step)

    def drain(self):
        for step in range(self.planes):
            wait_bytes(self.mine.at[step], self.send0.at[step])
            for copy in self.first(step) + self.second(step):
                copy.wait_send()
            if self.sums is None and step < self.planes - 1:
                self.third(step).wait_send()


class FeedCarry(Carry):
    def __init__(self, depth, up, down, refs, sems):
        super().__init__(refs[:CARRY_REFS], sems)
        (self.sums,) = refs[CARRY_REFS:]
        self.up, self.down = up, down
        self.keep = self.x if depth == 1 else 1 - self.x

    def pieces(self, row):
        return ((self.up.at[:, row], (0,)), (self.down.at[row], (1,)))

    def held(self, step):
        return self.sums.at[step]

    def first(self, step):
        return (
            remote(
                self.mine.at[step, 1 - self.keep, 0:2],
                self.got1.at[step, 0],
                self.send1.at[step, 0],
                self.recv1.at[step, 0],
                self.across_x,
            ),
            remote(
                self.mine.at[step, 1 - self.y, 2:4],
                self.got1.at[step, 1],
                self.send1.at[step, 1],
                self.recv1.at[step, 1],
                self.across_y,
            ),
        )

    def second(self, step):
        return (
            remote(
                self.mine.at[step, self.keep, 1 - self.y],
                self.got2.at[step, 0],
                self.send2.at[step, 0],
                self.recv2.at[step, 0],
                self.across_y,
            ),
            remote(
                self.mine.at[step, self.y, 3 - self.x],
                self.got2.at[step, 1],
                self.send2.at[step, 1],
                self.recv2.at[step, 1],
                self.across_x,
            ),
        )

    def middle(self, step):
        for copy in self.first(step):
            copy.wait_recv()
        self.mine[step, self.keep, 0:2] = plus(self.mine[step, self.keep, 0:2], self.got1[step, 0])
        self.mine[step, self.y, 2:4] = plus(self.mine[step, self.y, 2:4], self.got1[step, 1])
        for copy in self.second(step):
            copy.start()

    def end(self, step):
        for copy in self.second(step):
            copy.wait_recv()
        self.sums[step, 0] = plus(self.mine[step, self.keep, self.y], self.got2[step, 0])
        self.sums[step, 1] = plus(self.mine[step, self.y, 2 + self.x], self.got2[step, 1])
        self.onward(step)

    def plans(self):
        planes = self.planes
        return (
            [("b", step) for step in range(planes - 1)],
            [],
            [("m", 0), ("b", planes - 1)],
            [("m", 1)],
            [("m", step) for step in range(3, planes)],
            [("e", 1)],
            [("e", 2)],
            [("e", step) for step in range(3, planes)],
            [("m", 2), ("e", 0)],
        )

    def finish(self, out_ref):
        out_ref[...] = self.total()
        for step in range(self.planes):
            wait_bytes(self.mine.at[step], self.send0.at[step])
            for copy in self.first(step) + self.second(step):
                copy.wait_send()
            if step < self.planes - 1:
                self.third(step).wait_send()


CARRY_REFS = 6
CARRY_SEMS = 11


def carry_scratch(kind, rows, count, dp_count, dtype=bf16):
    planes = count // 2
    far = max(1, dp_count.bit_length() - 3)
    dma = pltpu.SemaphoreType.DMA
    half = rows // 2
    if kind == "attn":
        shapes = (
            (planes, 2, 2, rows),
            (planes, 2, 2, rows),
            (planes, 2, 2, half),
            (planes, 2, half),
            (planes, rows),
            (far, planes, rows),
        )
    else:
        shapes = (
            (planes, 2, 4, rows),
            (planes, 2, 4, rows),
            (planes, 2, 2, rows),
            (planes, 2, rows),
            (planes, 2, rows),
            (far, planes, 2, rows),
            (planes, 2, rows),
        )
    pair = (planes, 2)
    one = (planes,)
    sems = (one, one, one, pair, pair, pair, pair, one, one, (far, planes), (far, planes))
    return [pltpu.VMEM(shape + (D,), dtype) for shape in shapes] + [dma(shape) for shape in sems]


def z_scratch(rows, count, dp_count, dtype):
    planes = count // 2
    far = max(1, dp_count.bit_length() - 3)
    dma = pltpu.SemaphoreType.DMA
    shapes = ((planes, rows), (planes, rows), (far, planes, rows))
    sems = ((planes,), (planes,), (far, planes), (far, planes))
    return [pltpu.VMEM(shape + (D,), dtype) for shape in shapes] + [dma(shape) for shape in sems]


Z_REFS = 3
Z_SEMS = 4


def halves(value):
    high = value.astype(bf16)
    return high, (value - high.astype(f32)).astype(bf16)


def times(left, right):
    (left_high, left_low), (right_high, right_low) = left, right
    return dot_nn(
        jnp.concatenate([left_high, left_high, left_low], 1),
        jnp.concatenate([right_high, right_low, right_high], 0),
    )


def mirrored(first, second, third):
    return jnp.concatenate(
        [
            jnp.concatenate([first, second], 1),
            jnp.concatenate([jnp.transpose(second), third], 1),
        ],
        0,
    )


def times_even(left, right):
    (left_high, left_low), (right_high, right_low) = left, right
    wide = jnp.concatenate([left_high, left_high, left_low], 1)
    tall = jnp.concatenate([right_high, right_low, right_high], 0)
    return mirrored(
        dot_nn(wide[:HALF], tall[:, :HALF]),
        dot_nn(wide[:HALF], tall[:, HALF:]),
        dot_nn(wide[HALF:], tall[:, HALF:]),
    )


def gram_of(both):
    high, low = both
    wide = jnp.concatenate([high, high, low], 1)
    tall = jnp.concatenate([high, low, high], 1)
    return mirrored(
        dot_nt(wide[:HALF], tall[:HALF]),
        dot_nt(wide[:HALF], tall[HALF:]),
        dot_nt(wide[HALF:], tall[HALF:]),
    )


def clip_of(norm):
    return jnp.minimum(1.0, 0.25 / (norm + 1e-06))


def tail_kernel(
    count,
    attn_grad_ref,
    attn_done_ref,
    feed_low_ref,
    feed_high_ref,
    dout_ref,
    din_ref,
    vec0_ref,
    vec1_ref,
    vec2_ref,
    vec3_ref,
    outer_ref,
    mom_ref,
    update_ref,
    every_ref,
    small_out,
    norm_ref,
    whole_ref,
    own_ref,
    mom_s,
    small_ref,
    small_s,
    got_core,
    got_x,
    got_y,
    got_z,
    sq_seg,
    sq_dp,
    keep_s,
    give_s,
    made_ref,
    x_s,
    q_s,
    gram_s,
    high_s,
    low_s,
    mom_sem,
    last_send,
    last_recv,
    small_send,
    small_recv,
    join_send,
    join_recv,
    whole_send,
    whole_recv,
    half_sem,
    sq_send,
    sq_recv,
    sqd_send,
    sqd_recv,
    send,
    recv,
    on_send,
    on_recv,
    own_send,
    own_recv,
    *refs,
):
    carry = AttnCarry(attn_grad_ref, refs[:CARRY_REFS], refs[CARRY_REFS:])
    seg, dp, core, x, y, across_core, near, far = peers()
    across_x, across_y, across_both = near
    planes = count // 2
    plane = seg // 2
    group = 2 * y + x
    rows = own_ref.shape[1]
    targets = [{"seg": other} for other in others(seg, count)] + list(near) + list(far)
    hail(targets)
    carry.load_all()
    mom_copy = pltpu.make_async_copy(mom_ref, mom_s, mom_sem.at[0])
    mom_copy.start()
    own_ref[1] = attn_done_ref[...]

    @pl.when(x == y)
    def _():
        keep_s[...] = feed_high_ref[...]
        give_s[...] = feed_low_ref[...]

    @pl.when(x != y)
    def _():
        keep_s[...] = feed_low_ref[...]
        give_s[...] = feed_high_ref[...]

    own_ref[2 + y] = keep_s[0]
    own_ref[4 + x] = keep_s[1]
    last = (
        remote(give_s.at[0], own_ref.at[2 + y], last_send.at[0], last_recv.at[0], across_y),
        remote(give_s.at[1], own_ref.at[4 + x], last_send.at[1], last_recv.at[1], across_x),
    )
    inputs = din_ref.shape[0]
    small_ref[0:inputs, :] = din_ref[...]
    for place, ref in enumerate((vec0_ref, vec1_ref, vec2_ref, vec3_ref, outer_ref)):
        small_ref[inputs + 8 * place : inputs + 8 * place + 8, :] = ref[...]
    small_ref[inputs + 40 :, :] = jnp.zeros((SMALL - inputs - 40, D), f32)
    meet(targets)

    def span(first, size):
        return pl.ds(pl.multiple_of(first, 8), size)

    by_core, by_x, by_y = SMALL // 2, SMALL // 4, SMALL // 8
    core_at = core * by_core
    x_at = core_at + x * by_x
    y_at = x_at + y * by_y

    def small_steps():
        kept = span(core_at, by_core)
        copy = remote(
            small_ref.at[span(by_core - core_at, by_core)], got_core, small_send.at[0], small_recv.at[0], across_core
        )
        copy.start()
        yield
        copy.wait()
        small_s[kept, :] = small_ref[kept, :] + got_core[...]
        sent = span(core_at + by_x - x * by_x, by_x)
        copy = remote(small_s.at[sent], got_x, small_send.at[1], small_recv.at[1], across_x)
        copy.start()
        yield
        copy.wait()
        small_s[span(x_at, by_x), :] += got_x[...]
        sent = span(x_at + by_y - y * by_y, by_y)
        copy = remote(small_s.at[sent], got_y, small_send.at[2], small_recv.at[2], across_y)
        copy.start()
        yield
        copy.wait()
        kept = span(y_at, by_y)
        small_s[kept, :] += got_y[...]
        partners, step = list(far), 1
        while step < planes:
            partners.append({"seg": 2 * carry.toggled(step) + core})
            step *= 2
        for place, partner in enumerate(partners):
            copy = remote(
                small_s.at[kept], got_z.at[place], small_send.at[3 + place], small_recv.at[3 + place], partner
            )
            copy.start()
            yield
            copy.wait()
            small_s[kept, :] += got_z[place]

    small_run = small_steps()
    next(small_run)
    carry.send_all()
    for copy in last:
        copy.start()
    roles = owners(count)

    def gift(place):
        first, width, owner, spot = roles[place]
        return remote(
            own_ref.at[first : first + width],
            whole_ref.at[seg, spot : spot + width],
            whole_send.at[place],
            whole_recv.at[seg],
            {"seg": owner},
        )

    def give(place):
        first, width, owner, spot = roles[place]

        @pl.when(seg != owner)
        def _():
            gift(place).start()

        @pl.when(seg == owner)
        def _():
            whole_ref[seg, spot : spot + width] = own_ref[first : first + width]

    acts = [
        [("b", step) for step in range(planes - 1)],
        [("m", 0), ("b", planes - 1)],
        [("m", 1)],
        [("m", 2), ("e", 0)],
        [("m", step) for step in range(3, planes)],
    ] + [[("e", step)] for step in range(1, planes)]
    give(1)
    next(small_run)
    for turn, part in enumerate(acts):
        carry.run(part)
        if turn == 0:
            for copy in last:
                copy.wait()
            for place in range(2, 6):
                give(place)
        next(small_run, None)
    own_ref[0] = carry.total()
    give(0)
    for _ in small_run:
        pass

    mine = span(y_at, by_y)
    small_out[mine, :] = small_s[mine, :]

    def join(place):
        first, size, partner = ((y_at, by_y, across_y), (x_at, by_x, across_x), (core_at, by_core, across_core))[place]
        block = small_out.at[span(first, size)]
        return remote(block, block, join_send.at[place], join_recv.at[place], partner)

    join(0).start()
    shard = dout_ref[...].astype(f32)
    square = jnp.sum(jnp.sum(shard * shard, 0, keepdims=True), 1, keepdims=True)
    for unit in range(UNITS):
        value = own_ref[unit].astype(f32)
        square = square + jnp.sum(jnp.sum(value * value, 0, keepdims=True), 1, keepdims=True)
    sums = small_s[mine, :]
    is_loss = lax.broadcasted_iota(jnp.int32, (by_y, D), 0) + y_at == inputs + 37
    sums = jnp.where(is_loss, 0.0, sums)
    square = square + jnp.sum(jnp.sum(sums * sums, 0, keepdims=True), 1, keepdims=True) * (1.0 / planes)
    sq_seg[seg] = jnp.broadcast_to(square, (8, 128))
    for step, other in enumerate(others(seg, count)):
        remote(sq_seg.at[seg], sq_seg.at[seg], sq_send.at[step], sq_recv.at[seg], {"seg": other}).start()

    def halves_copy(spot):
        part = slice(spot, spot + 2)
        return remote(whole_ref.at[:, part], whole_ref.at[:, part], half_sem.at[0], half_sem.at[1], across_core)

    for place, (first, width, owner, spot) in enumerate(roles):
        if width == 2:

            @pl.when(seg == owner)
            def _():
                for other in others(seg, count):
                    wait_bytes(whole_ref.at[other, spot : spot + width], whole_recv.at[other])
                halves_copy(spot).start()

    for other in others(seg, count):
        wait_bytes(sq_seg.at[other], sq_recv.at[other])
    sq_dp[group] = jnp.sum(sq_seg[...], 0)
    for place, target in enumerate(near):
        remote(sq_dp.at[group], sq_dp.at[group], sqd_send.at[place], sqd_recv.at[place], target).start()
    join(0).wait()
    join(1).start()
    for place, target in enumerate(near):
        remote(sq_dp.at[group], sq_dp.at[group], sqd_send.at[place], sqd_recv.at[place], target).wait()
    norm = jnp.sqrt(jnp.sum(sq_dp[...], 0)[0:1, 0:1])
    norm_ref[...] = jnp.broadcast_to(norm, norm_ref.shape)
    clip = clip_of(norm)

    def own_rows(side):
        return remote(own_ref, every_ref.at[group], own_send.at[side], own_recv.at[side], near[side])

    for side in range(3):
        own_rows(side).start()
    every_ref[group] = own_ref[...]
    mom_copy.wait()

    for place, (first, width, owner, spot) in enumerate(roles):

        @pl.when(seg == owner)
        def _():
            if width == 2:
                halves_copy(spot).wait()
            else:
                for other in others(seg, count):
                    wait_bytes(whole_ref.at[other, spot : spot + width], whole_recv.at[other])

    is_down = group >= 2
    eye = (
        lax.broadcasted_iota(jnp.int32, (D, D), 0) == lax.broadcasted_iota(jnp.int32, (D, D), 1)
    ).astype(f32)
    low = count // 4 - 1
    half = plane // (planes // 2)
    base = half * planes
    neighbours = [base + lax.rem(seg - base + step, planes) for step in range(1, planes)]
    feed_maker = 2 * (low + half)
    makers = [0, count - 2, feed_maker, feed_maker, feed_maker + 1, feed_maker + 1]

    def receivers(unit):
        return others(seg, count) if unit < 2 else neighbours

    def present(unit, slot, other):
        return remote(
            made_ref.at[other, slot],
            update_ref.at[group, unit],
            send.at[slot, other],
            recv.at[unit],
            {"seg": other},
        )

    def hand_out(unit, slot):
        for other in receivers(unit):
            present(unit, slot, other).start()
        update_ref[group, unit] = made_ref[seg, slot]

    def onward(unit, side):
        block = update_ref.at[group, unit]
        return remote(block, block, on_send.at[side, unit], on_recv.at[side, unit], near[side])

    @pl.when((seg == 0) | (seg == count - 2))
    def _():
        start = (0.5 * mom_s[:, plane // (planes - 1)].astype(f32)).reshape(D, D)
        start = start + clip * whole_ref[:, 0].astype(f32).reshape(D, D)
        size = jnp.sum(jnp.sum(start * start, 0, keepdims=True), 1, keepdims=True)
        x_s[...] = start / (jnp.sqrt(size) + 1e-07)

        def sweep(_, state):
            value = x_s[...]
            both = halves(value)
            gram = gram_of(both)
            gram_both = halves(gram)
            poly = -4.775 * gram + 2.0315 * times_even(gram_both, gram_both)
            x_s[...] = 3.4445 * value + times(halves(poly), both)
            return state

        lax.fori_loop(0, 5, sweep, 0)
        made_ref[:, 0] = x_s[...].astype(bf16).reshape(count, rows, D)
        for unit in range(2):

            @pl.when(seg == makers[unit])
            def _():
                hand_out(unit, 0)

    @pl.when((plane == low) | (plane == low + 1))
    def _():
        gram_s[...] = jnp.zeros_like(gram_s)

        def gather(tile, size):
            value = (0.5 * mom_s[:, 2 + tile].astype(f32)).reshape(D, D)
            value = value + clip * whole_ref[:, tile].astype(f32).reshape(D, D)
            high, rest = halves(value)
            high_s[tile] = high
            low_s[tile] = rest

            @pl.when(is_down)
            def _():
                high_s[tile] = jnp.transpose(high_s[tile])
                low_s[tile] = jnp.transpose(low_s[tile])

            gram_s[...] += gram_of((high_s[tile], low_s[tile]))
            return size + jnp.sum(jnp.sum(value * value, 0, keepdims=True), 1, keepdims=True)

        size = lax.fori_loop(0, 4, gather, jnp.zeros((1, 1), f32))
        scale = 1.0 / (jnp.sqrt(size) + 1e-07)
        gram_s[...] = gram_s[...] * (scale * scale)

        def poly_of(gram, gram_both):
            return 3.4445 * eye - 4.775 * gram + 2.0315 * times_even(gram_both, gram_both)

        def advance(gram_both, poly_both):
            gram_s[...] = times_even(halves(times_even(gram_both, poly_both)), poly_both)

        gram = gram_s[...]
        gram_both = halves(gram)
        poly = poly_of(gram, gram_both)
        q_s[...] = poly
        advance(gram_both, halves(poly))

        def sweep(_, state):
            gram = gram_s[...]
            gram_both = halves(gram)
            poly_both = halves(poly_of(gram, gram_both))
            q_s[...] = times_even(halves(q_s[...]), poly_both)
            advance(gram_both, poly_both)
            return state

        lax.fori_loop(0, 3, sweep, 0)
        gram = gram_s[...]
        last_both = halves(times_even(halves(q_s[...]), halves(poly_of(gram, halves(gram)))) * scale)
        for slot in range(2):
            tile = 2 * core + slot
            x_s[...] = times(last_both, (high_s[tile], low_s[tile]))

            @pl.when(is_down)
            def _():
                x_s[...] = jnp.transpose(x_s[...])

            made_ref[:, slot] = x_s[...].astype(bf16).reshape(count, rows, D)
            for side in range(2):

                @pl.when(core == side)
                def _():
                    hand_out(2 + 2 * side + slot, slot)

    join(1).wait()
    join(2).start()
    for unit in (0, 1, 2, 4, 3, 5):

        @pl.when(seg != makers[unit])
        def _():
            wait_bytes(update_ref.at[group, unit], recv.at[unit])

        for side in range(3):
            onward(unit, side).start()
    join(2).wait()
    for side in range(3):
        own_rows(side).wait()
    carry.drain()
    for place, (first, width, owner, spot) in enumerate(roles):

        @pl.when(seg != owner)
        def _():
            gift(place).wait_send()

    for step in range(count - 1):
        wait_bytes(sq_seg.at[0], sq_send.at[step])
    for unit in range(UNITS):
        for side in range(3):
            onward(unit, side).wait()

        @pl.when(seg == makers[unit])
        def _():
            slot = 0 if unit < 2 else unit % 2
            for other in receivers(unit):
                present(unit, slot, other).wait_send()


def tail(count, dp_count, attn, done, feed_low, feed_high, dout, pieces, momenta):
    rows = D // count
    planes = count // 2
    stages = planes.bit_length() + max(0, dp_count.bit_length() - 3)
    dma = pltpu.SemaphoreType.DMA
    vmem, anywhere = pl.BlockSpec(memory_space=pltpu.VMEM), pl.BlockSpec(memory_space=pl.ANY)
    blocks = jax.ShapeDtypeStruct((GROUPS, UNITS, rows, D), bf16)
    return pl.pallas_call(
        functools.partial(tail_kernel, count),
        out_shape=[
            blocks,
            blocks,
            jax.ShapeDtypeStruct((SMALL, D), f32),
            jax.ShapeDtypeStruct((8, 128), f32),
        ],
        in_specs=[anywhere] + [vmem] * 10 + [anywhere],
        out_specs=[vmem] * 4,
        scratch_shapes=[
            pltpu.VMEM((count, 4, rows, D), bf16),
            pltpu.VMEM((UNITS, rows, D), bf16),
            pltpu.VMEM(momenta.shape, bf16),
            pltpu.VMEM((SMALL, D), f32),
            pltpu.VMEM((SMALL, D), f32),
            pltpu.VMEM((SMALL // 2, D), f32),
            pltpu.VMEM((SMALL // 4, D), f32),
            pltpu.VMEM((SMALL // 8, D), f32),
            pltpu.VMEM((stages, SMALL // 8, D), f32),
            pltpu.VMEM((count, 8, 128), f32),
            pltpu.VMEM((GROUPS, 8, 128), f32),
            pltpu.VMEM((2, rows, D), bf16),
            pltpu.VMEM((2, rows, D), bf16),
            pltpu.VMEM((count, 2, rows, D), bf16),
            pltpu.VMEM((D, D), f32),
            pltpu.VMEM((D, D), f32),
            pltpu.VMEM((D, D), f32),
            pltpu.VMEM((4, D, D), bf16),
            pltpu.VMEM((4, D, D), bf16),
            dma((1,)),
            dma((2,)),
            dma((2,)),
            dma((stages + 3,)),
            dma((stages + 3,)),
            dma((3,)),
            dma((3,)),
            dma((6,)),
            dma((count,)),
            dma((2,)),
            dma((count,)),
            dma((count,)),
            dma((3,)),
            dma((3,)),
            dma((2, count)),
            dma((UNITS,)),
            dma((3, UNITS)),
            dma((3, UNITS)),
            dma((3,)),
            dma((3,)),
        ]
        + carry_scratch("attn", rows, count, dp_count),
        compiler_params=pltpu.CompilerParams(
            collective_id=1, has_side_effects=True, vmem_limit_bytes=TAIL_LIMIT
        ),
        cost_estimate=pl.CostEstimate(flops=2 * 10**10, bytes_accessed=10**8, transcendentals=0),
        name="tail",
    )(attn.reshape(2, 2, count, rows, D), done, feed_low, feed_high, dout, *pieces, momenta)


def embed_kernel(
    count,
    frames_ref,
    mask_ref,
    in_ref,
    outer_ref,
    attn_mom_ref,
    up_mom_ref,
    down_mom_ref,
    x_ref,
    mem_ref,
    total_ref,
    owned_ref,
    got_s,
    count_s,
    mom_s,
    mom_sem,
    frame_send,
    frame_recv,
    count_send,
    count_recv,
):
    seg = lax.axis_index("seg")
    after, before = lax.rem(seg + 1, count), lax.rem(seg + count - 1, count)
    streams = frames_ref.shape[0]
    group = lax.rem(lax.axis_index("dp"), GROUPS)
    for depth in range(LAYERS):
        pltpu.make_async_copy(attn_mom_ref.at[depth, group], mom_s.at[depth], mom_sem.at[0]).start()

        @pl.when(group == FEED_UP[depth])
        def _():
            for tile in range(4):
                source = up_mom_ref.at[depth, :, pl.ds(tile * TILE, TILE)]
                pltpu.make_async_copy(source, mom_s.at[2 + tile], mom_sem.at[0]).start()

        @pl.when(group == FEED_DOWN[depth])
        def _():
            pltpu.make_async_copy(down_mom_ref.at[depth], mom_s.at[2:6], mom_sem.at[0]).start()

    tally = jnp.sum(mask_ref[...].astype(f32), 1, keepdims=True)
    count_s[seg] = jnp.broadcast_to(
        jnp.concatenate([tally, jnp.zeros((8 - streams, 1), f32)], 0), (8, 128)
    )
    greet(seg, count, (), ())
    frame_copy = remote(frames_ref, got_s, frame_send.at[0], frame_recv.at[0], {"seg": after})
    frame_copy.start()
    for step, other in enumerate(others(seg, count)):
        remote(count_s.at[seg], count_s.at[seg], count_send.at[step], count_recv.at[seg], {"seg": other}).start()
    weight, shift = in_ref[...], outer_ref[0:1, :]
    for stream in range(streams):
        x_ref[stream] = dot_nn(jnp.transpose(frames_ref[stream]), weight) + shift
    wait_bytes(mom_s, mom_sem.at[0])
    owned_ref[...] = mom_s[...].astype(bf16)
    frame_copy.wait()
    for stream in range(streams):
        mem_ref[stream] = (dot_nn(jnp.transpose(got_s[stream]), weight) + shift).astype(bf16)
    for other in others(seg, count):
        wait_bytes(count_s.at[other], count_recv.at[other])
    total_ref[...] = jnp.sum(count_s[...], 0)
    for step in range(count - 1):
        wait_bytes(count_s.at[0], count_send.at[step])


def embed(count, frames, mask, in_weight, outer_vectors, attn_mom, up_mom, down_mom):
    streams = frames.shape[0]
    rows = D // count
    dma = pltpu.SemaphoreType.DMA
    return pl.pallas_call(
        functools.partial(embed_kernel, count),
        out_shape=[
            jax.ShapeDtypeStruct((streams, SEG, D), f32),
            jax.ShapeDtypeStruct((streams, SEG, D), bf16),
            jax.ShapeDtypeStruct((8, 128), f32),
            jax.ShapeDtypeStruct((UNITS, rows, D), bf16),
        ],
        in_specs=[pl.BlockSpec(memory_space=pltpu.VMEM)] * 4 + [pl.BlockSpec(memory_space=pl.ANY)] * 3,
        out_specs=[pl.BlockSpec(memory_space=pltpu.VMEM)] * 4,
        scratch_shapes=[
            pltpu.VMEM(frames.shape, bf16),
            pltpu.VMEM((count, 8, 128), f32),
            pltpu.VMEM((UNITS, rows, D), f32),
            dma((1,)),
            dma((1,)),
            dma((1,)),
            dma((count,)),
            dma((count,)),
        ],
        compiler_params=pltpu.CompilerParams(
            collective_id=3, has_side_effects=True, vmem_limit_bytes=VMEM_LIMIT
        ),
        cost_estimate=pl.CostEstimate(flops=2 * 10**8, bytes_accessed=4 * 10**6, transcendentals=0),
        name="embed",
    )(frames, mask, in_weight, outer_vectors, attn_mom, up_mom, down_mom.reshape(LAYERS, 4, rows, D))


FEED_UP = (1, 0)
FEED_DOWN = (2, 3)
KEEP = 1.0 - 0.3 * 0.01


def finish_kernel(norm_ref, every_ref, update_ref, dout_ref, small_ref, *refs):
    (
        attn_ref,
        attn_mom_ref,
        up_ref,
        up_mom_ref,
        down_ref,
        down_mom_ref,
        out_ref,
        out_mom_ref,
        out_sec_ref,
        in_ref,
        in_mom_ref,
        in_sec_ref,
        vec_ref,
        vec_mom_ref,
        vec_sec_ref,
        outer_ref,
        outer_mom_ref,
        outer_sec_ref,
        attn_new,
        attn_mom_new,
        attn_copy_new,
        up_new,
        up_mom_new,
        up_copy_new,
        down_new,
        down_mom_new,
        down_copy_new,
        out_new,
        out_mom_new,
        out_sec_new,
        out_copy_new,
        in_new,
        in_mom_new,
        in_sec_new,
        in_copy_new,
        vec_new,
        vec_mom_new,
        vec_sec_new,
        outer_new,
        outer_mom_new,
        outer_sec_new,
        loss_new,
        norm_new,
    ) = refs
    clip = clip_of(norm_ref[0:1, 0:1])

    def muon_step(weight, momentum, grad, update, scale):
        weight = weight * KEEP - (0.3 * scale) * update.astype(f32)
        return weight, 0.5 * momentum + clip * grad.astype(f32)

    up_scale, down_scale = max(1.0, FF / D) ** 0.5, max(1.0, D / FF) ** 0.5
    for depth in range(LAYERS):
        for kind in range(4):
            weight, momentum = muon_step(
                attn_ref[depth, kind],
                attn_mom_ref[depth, kind],
                every_ref[kind, depth],
                update_ref[kind, depth],
                1.0,
            )
            attn_new[depth, kind] = weight
            attn_mom_new[depth, kind] = momentum
            attn_copy_new[depth, kind] = weight.astype(bf16)
            columns = slice(kind * TILE, (kind + 1) * TILE)
            weight, momentum = muon_step(
                up_ref[depth, :, columns],
                up_mom_ref[depth, :, columns],
                every_ref[FEED_UP[depth], 2 + kind],
                update_ref[FEED_UP[depth], 2 + kind],
                up_scale,
            )
            up_new[depth, :, columns] = weight
            up_mom_new[depth, :, columns] = momentum
            up_copy_new[depth, :, columns] = weight.astype(bf16)
            weight, momentum = muon_step(
                down_ref[depth, kind],
                down_mom_ref[depth, kind],
                every_ref[FEED_DOWN[depth], 2 + kind],
                update_ref[FEED_DOWN[depth], 2 + kind],
                down_scale,
            )
            down_new[depth, kind] = weight
            down_mom_new[depth, kind] = momentum
            down_copy_new[depth, kind] = weight.astype(bf16)
    for low in range(2):
        for right in range(2):
            columns = slice(right * D, (right + 1) * D)
            weight, moment, second = adamw(
                out_ref[low, :, columns],
                out_mom_ref[low, :, columns],
                out_sec_ref[low, :, columns],
                dout_ref[2 * right + low].astype(f32) * clip,
                0.05,
                0.01,
            )
            out_new[low, :, columns] = weight
            out_mom_new[low, :, columns] = moment
            out_sec_new[low, :, columns] = second
            out_copy_new[low, :, columns] = weight.astype(bf16)

    @pl.when(pl.program_id(0) == 0)
    def _():
        inputs = in_ref.shape[0]
        weight, moment, second = adamw(
            in_ref[...], in_mom_ref[...], in_sec_ref[...], small_ref[0:inputs, :] * clip, 0.05, 0.01
        )
        in_new[...] = weight
        in_mom_new[...] = moment
        in_sec_new[...] = second
        in_copy_new[...] = weight.astype(bf16)

        norm_new[...] = norm_ref[0:1, 0:1]
        loss_new[...] = small_ref[inputs + 37 : inputs + 38, 0:1]

        def rows_of(first, last, base):
            return small_ref[inputs + base + first : inputs + base + last, :]

        for depth in range(LAYERS):
            base = 16 * depth
            for low, high, grad in (
                (0, 2, rows_of(0, 2, base)),
                (2, 4, rows_of(0, 2, base + 8)),
                (4, 7, rows_of(2, 5, base)),
                (7, 8, rows_of(2, 3, base + 8)),
                (8, 12, rows_of(4, 8, base + 8)),
            ):
                weight, moment, second = adamw(
                    vec_ref[low:high, depth],
                    vec_mom_ref[low:high, depth],
                    vec_sec_ref[low:high, depth],
                    grad * clip,
                    0.25,
                    0.0,
                )
                vec_new[low:high, depth] = weight
                vec_mom_new[low:high, depth] = moment
                vec_sec_new[low:high, depth] = second
        for low, high, grad in ((0, 1, rows_of(5, 6, 0)), (1, 5, rows_of(1, 5, 32))):
            weight, moment, second = adamw(
                outer_ref[low:high, :], outer_mom_ref[low:high, :], outer_sec_ref[low:high, :], grad * clip, 0.25, 0.0
            )
            outer_new[low:high, :] = weight
            outer_mom_new[low:high, :] = moment
            outer_sec_new[low:high, :] = second


def finish(rows, norm, every, updates, dout, small, arrays):
    steps = rows // 16
    attn, _, up, _, down, _, out, _, _, inp, _, _, vec, _, _, outer, _, _ = arrays
    codes = out.shape[2]
    part = out.shape[1] // steps
    blocks = pl.BlockSpec((GROUPS, UNITS, 16, D), lambda i: (0, 0, i, 0))
    attn_spec = pl.BlockSpec((LAYERS, 4, 16, D), lambda i: (0, 0, i, 0))
    up_spec = pl.BlockSpec((LAYERS, 16, FF), lambda i: (0, i, 0))
    out_spec = pl.BlockSpec((2, part, codes), lambda i: (0, i, 0))
    dout_spec = pl.BlockSpec((GROUPS, part, D), lambda i: (0, i, 0))
    in_spec, vec_spec, outer_spec = whole_spec(inp.shape), whole_spec(vec.shape), whole_spec(outer.shape)

    def like(array, dtype=f32):
        return jax.ShapeDtypeStruct(array.shape, dtype)

    return pl.pallas_call(
        finish_kernel,
        grid=(steps,),
        out_shape=[like(attn), like(attn), like(attn, bf16)]
        + [like(up), like(up), like(up, bf16)]
        + [like(down), like(down), like(down, bf16)]
        + [like(out)] * 3
        + [like(out, bf16)]
        + [like(inp)] * 3
        + [like(inp, bf16)]
        + [like(vec)] * 3
        + [like(outer)] * 3
        + [jax.ShapeDtypeStruct((1, 1), f32)] * 2,
        in_specs=[whole_spec((8, 128)), blocks, blocks, dout_spec, whole_spec(small.shape)]
        + [attn_spec] * 2
        + [up_spec] * 2
        + [attn_spec] * 2
        + [out_spec] * 3
        + [in_spec] * 3
        + [vec_spec] * 3
        + [outer_spec] * 3,
        out_specs=[attn_spec] * 3
        + [up_spec] * 3
        + [attn_spec] * 3
        + [out_spec] * 4
        + [in_spec] * 4
        + [vec_spec] * 3
        + [outer_spec] * 3
        + [whole_spec((1, 1))] * 2,
        compiler_params=pltpu.CompilerParams(vmem_limit_bytes=(8 + 48 // steps) * 1024 * 1024),
        cost_estimate=pl.CostEstimate(flops=10**8, bytes_accessed=4 * 10**7, transcendentals=0),
        name="finish",
    )(norm, every, updates, dout, small, *arrays)


def local(
    frames,
    speech_mask,
    targets,
    in_proj,
    in_moment,
    in_second,
    out_proj,
    out_moment,
    out_second,
    layer_vectors,
    vectors_moment,
    vectors_second,
    outer_vectors,
    outer_moment,
    outer_second,
    attn_proj,
    attn_momentum,
    ff_up,
    up_momentum,
    ff_down,
    down_momentum,
    in_copy,
    out_copy,
    attn_copy,
    up_copy,
    down_copy,
):
    segment = lax.axis_index("seg")
    count, dp_count = lax.axis_size("seg"), lax.axis_size("dp")
    rows = D // count
    streams = frames.shape[0]
    stream_total = streams * dp_count
    frames_t = jnp.swapaxes(frames, 1, 2)
    bias = jnp.where(segment > 0, 0.0, -1e30).astype(f32)[None]
    hidden, memory, totals, owned = embed(
        count, frames_t, speech_mask, in_copy, outer_vectors, attn_momentum, up_momentum, down_momentum
    )
    momenta = lax.all_gather(owned, "seg", axis=0, tiled=False)
    memory = [memory] * streams
    kept = []
    for depth in range(LAYERS):
        saved, passed = None, []
        for stream in range(streams):
            saved, short = forward_layer(
                depth,
                stream,
                streams,
                bias,
                hidden,
                memory[stream],
                attn_copy,
                up_copy,
                down_copy,
                layer_vectors,
                saved,
            )
            if depth + 1 < LAYERS:
                passed.append(from_behind(short, "seg", 1))
        kept.append((hidden, saved[8], saved))
        hidden = saved[0]
        memory = passed
    grad_hidden, grad_out, head_outer = head(
        hidden, targets, speech_mask, totals, out_copy, outer_vectors, 1.0 / stream_total, momenta
    )
    vector_grads, feed_done = [], [None, None]
    carried = grad_out.reshape(GROUPS * D // 2, D)
    carried_done = []
    for depth in reversed(range(LAYERS)):
        entering, held, saved = kept[depth]
        dafter, grad_up, grad_down, feed_vec, sums = feed_back(
            depth, grad_hidden, saved[7], up_copy, down_copy, layer_vectors, count, dp_count, carried
        )
        grad_hidden, grad_attn, attn_vec, grad_in, feed_done[depth], done = attend_back(
            depth,
            bias,
            dafter,
            entering,
            held,
            saved[1:7],
            attn_copy,
            layer_vectors,
            frames_t,
            grad_up,
            grad_down,
            sums,
            count,
            dp_count,
        )
        carried_done.append(done)
        carried = grad_attn.reshape(4 * D, D)
        vector_grads = [attn_vec, feed_vec] + vector_grads
    out_done, attn_done = carried_done
    every_out = lax.all_gather(out_done, ("dp", "seg"), axis=0, tiled=True)[: GROUPS * D // 2]
    every_out = every_out.reshape(GROUPS, D // 2, D)
    updates, every, small, norm = tail(
        count,
        dp_count,
        grad_attn,
        attn_done,
        feed_done[0],
        feed_done[1],
        out_done,
        [grad_in] + vector_grads + [head_outer],
        momenta,
    )
    split = (LAYERS, 4, rows, D)
    halved = (2, D // 2, out_proj.shape[1])
    (
        attn_new,
        attn_mom,
        attn_copy_new,
        up_new,
        up_mom,
        up_copy_new,
        down_new,
        down_mom,
        down_copy_new,
        out_new,
        out_moment_new,
        out_second_new,
        out_copy_new,
        in_new,
        in_moment_new,
        in_second_new,
        in_copy_new,
        vectors_new,
        vectors_moment_new,
        vectors_second_new,
        outer_new,
        outer_moment_new,
        outer_second_new,
        loss_sum,
        norm,
    ) = finish(
        rows,
        norm,
        every,
        updates,
        every_out,
        small,
        [
            attn_proj,
            attn_momentum,
            ff_up,
            up_momentum,
            ff_down.reshape(split),
            down_momentum.reshape(split),
            out_proj.reshape(halved),
            out_moment.reshape(halved),
            out_second.reshape(halved),
            in_proj,
            in_moment,
            in_second,
            jnp.swapaxes(layer_vectors, 0, 1),
            jnp.swapaxes(vectors_moment, 0, 1),
            jnp.swapaxes(vectors_second, 0, 1),
            outer_vectors,
            outer_moment,
            outer_second,
        ],
    )
    return (
        loss_sum.reshape(()),
        norm.reshape(()),
        in_new,
        in_moment_new,
        in_second_new,
        out_new.reshape(out_proj.shape),
        out_moment_new.reshape(out_proj.shape),
        out_second_new.reshape(out_proj.shape),
        jnp.swapaxes(vectors_new, 0, 1),
        jnp.swapaxes(vectors_moment_new, 0, 1),
        jnp.swapaxes(vectors_second_new, 0, 1),
        outer_new,
        outer_moment_new,
        outer_second_new,
        attn_new,
        attn_mom,
        up_new,
        up_mom,
        down_new.reshape(ff_down.shape),
        down_mom.reshape(ff_down.shape),
        in_copy_new,
        out_copy_new.reshape(out_proj.shape),
        attn_copy_new,
        up_copy_new,
        down_copy_new.reshape(ff_down.shape),
    )


def solution(mesh):
    return jax.shard_map(
        local,
        mesh=mesh,
        in_specs=(
            P("dp", "seg", None),
            P("dp", "seg"),
            P("dp", "seg"),
            P(),
            P(),
            P(),
            P(),
            P(),
            P(),
            P(),
            P(),
            P(),
            P(),
            P(),
            P(),
            P(None, None, "seg", None),
            P(None, None, "seg", None),
            P(None, "seg", None),
            P(None, "seg", None),
            P(None, "seg", None),
            P(None, "seg", None),
            P(),
            P(),
            P(),
            P(),
            P(),
        ),
        out_specs=(
            P(),
            P(),
            P(),
            P(),
            P(),
            P(),
            P(),
            P(),
            P(),
            P(),
            P(),
            P(),
            P(),
            P(),
            P(None, None, "seg", None),
            P(None, None, "seg", None),
            P(None, "seg", None),
            P(None, "seg", None),
            P(None, "seg", None),
            P(None, "seg", None),
            P(),
            P(),
            P(None, None, "seg", None),
            P(None, "seg", None),
            P(None, "seg", None),
        ),
        check_vma=False,
    )
```

```python
import functools
import math

import jax
import jax.numpy as jnp
from jax import lax
from jax.experimental import pallas as pl
from jax.experimental.pallas import tpu as pltpu
from jax.sharding import PartitionSpec as P

D = 512
HEAD_DIM = 64
HEADS = D // HEAD_DIM
FF = 2048
LAYERS = 2
STEP = 10
SEG = 512
HALF = 256
PAIR = 2 * HEAD_DIM
TILE = 512
VMEM_LIMIT = 56 * 1024 * 1024
GELU_SCALE = math.sqrt(2.0 / math.pi)

f32 = jnp.float32
bf16 = jnp.bfloat16


def dot_nn(left, right):
    return lax.dot_general(left, right, (((1,), (0,)), ((), ())), preferred_element_type=f32)


def dot_nt(left, right):
    return lax.dot_general(left, right, (((1,), (1,)), ((), ())), preferred_element_type=f32)


def dot_tn(left, right):
    return lax.dot_general(left, right, (((0,), (0,)), ((), ())), preferred_element_type=f32)


def normalised(values):
    centred = values - jnp.mean(values, -1, keepdims=True)
    scale = lax.rsqrt(jnp.mean(centred * centred, -1, keepdims=True) + 1e-05)
    return centred * scale, scale


def norm_back(grad, gain, unit, scale):
    part = grad * gain
    mean_part = jnp.mean(part, -1, keepdims=True)
    mean_unit = jnp.mean(part * unit, -1, keepdims=True)
    return scale * (part - mean_part - unit * mean_unit)


def column_sum(values):
    return jnp.sum(values, 0, keepdims=True)


def head_masks():
    lane = lax.broadcasted_iota(jnp.int32, (1, PAIR), 1)
    return (lane < HEAD_DIM).astype(bf16), (lane >= HEAD_DIM).astype(bf16)


def pair_lanes(pair):
    return pl.ds(pl.multiple_of(pair * PAIR, PAIR), PAIR)


def forward_kernel(
    depth,
    stream,
    bias_ref,
    x_ref,
    mem_ref,
    attn_ref,
    up_ref,
    down_ref,
    vec_ref,
    *refs,
):
    (
        hid_ref,
        hid16_ref,
        keyin_out,
        q_out,
        k_out,
        v_out,
        lse_ref,
        mixed_ref,
        after_ref,
        kept_out,
        act_s,
        lse_s,
        up_s,
        down_s,
        keyin_ref,
        q_ref,
        k_ref,
        v_ref,
        in_sem,
        out_sem,
    ) = refs[-20:]
    weights_in = (
        pltpu.make_async_copy(up_ref.at[depth], up_s, in_sem.at[0]),
        pltpu.make_async_copy(down_ref.at[depth], down_s, in_sem.at[1]),
    )
    for copy in weights_in:
        copy.start()
    saved_out = [
        pltpu.make_async_copy(source, target.at[stream], out_sem.at[place])
        for place, (source, target) in enumerate(
            ((keyin_ref, keyin_out), (q_ref, q_out), (k_ref, k_out), (v_ref, v_out))
        )
    ]
    kept_out[...] = mem_ref[...]
    x = x_ref[...]
    own_unit, _ = normalised(x)
    gain, shift = vec_ref[0:1, :], vec_ref[1:2, :]
    normed = (own_unit * gain + shift).astype(bf16)
    mem_unit, _ = normalised(mem_ref[...].astype(f32))
    mem_normed = (mem_unit * gain + shift).astype(bf16)
    keyin_ref[0:SEG, :] = mem_normed
    keyin_ref[SEG:, :] = normed
    q_ref[...] = (dot_nn(normed, attn_ref[0]) + vec_ref[4:5, :]).astype(bf16) * jnp.asarray(HEAD_DIM**-0.5, bf16)
    k_ref[0:SEG, :] = dot_nn(mem_normed, attn_ref[1]).astype(bf16)
    k_ref[SEG:, :] = dot_nn(normed, attn_ref[1]).astype(bf16)
    v_ref[0:SEG, :] = (dot_nn(mem_normed, attn_ref[2]) + vec_ref[5:6, :]).astype(bf16)
    v_ref[SEG:, :] = (dot_nn(normed, attn_ref[2]) + vec_ref[5:6, :]).astype(bf16)
    for copy in saved_out:
        copy.start()
    first, second = head_masks()
    memory_bias = bias_ref[0]
    lane = lax.broadcasted_iota(jnp.int32, (HALF, PAIR), 1)
    query_pos = lax.broadcasted_iota(jnp.int32, (2 * HALF, HALF), 0) % HALF
    key_pos = lax.broadcasted_iota(jnp.int32, (2 * HALF, HALF), 1)
    diagonal = key_pos <= query_pos
    lse_s[...] = jnp.zeros_like(lse_s)

    def pair_body(pair, carry):
        lanes = pair_lanes(pair)
        blocks = []
        for block in range(2):
            rows = slice(block * HALF, (block + 1) * HALF)
            q_pair = q_ref[rows, lanes]
            q_both = jnp.concatenate([q_pair * first, q_pair * second], 0)
            spans = [(0, SEG)]
            if block:
                spans.append((SEG, SEG + HALF))
            spans.append((SEG + block * HALF, SEG + (block + 1) * HALF))
            scores = [dot_nt(q_both, k_ref[low:high, lanes]) for low, high in spans]
            scores[-1] = jnp.where(diagonal, scores[-1], -1e30)
            blocks.append((rows, spans, scores))
        results = []
        for rows, spans, scores in blocks:
            peaks = [jnp.max(part, -1, keepdims=True) for part in scores]
            peaks[0] = peaks[0] + memory_bias
            most = functools.reduce(jnp.maximum, peaks)
            weights = [
                jnp.exp(part - (most if place else most - memory_bias)) for place, part in enumerate(scores)
            ]
            total = functools.reduce(jnp.add, [jnp.sum(part, -1, keepdims=True) for part in weights])
            mixed = functools.reduce(
                jnp.add,
                [
                    dot_nn(part.astype(bf16), v_ref[low:high, lanes])
                    for part, (low, high) in zip(weights, spans)
                ],
            )
            results.append((rows, mixed / total, most + jnp.log(total)))
        for rows, mixed, lse in results:
            mixed_ref[rows, lanes] = jnp.where(lane < HEAD_DIM, mixed[:HALF], mixed[HALF:]).astype(bf16)
            kept = jnp.where(lane == 2 * pair, lse[:HALF], lse_s[rows, :])
            lse_s[rows, :] = jnp.where(lane == 2 * pair + 1, lse[HALF:], kept)
        return carry

    lax.fori_loop(0, HEADS // 2, pair_body, 0)
    lse_ref[...] = jnp.transpose(lse_s[...])[0:HEADS, :]
    after = x + (dot_nn(mixed_ref[...], attn_ref[3]) + vec_ref[6:7, :])
    after_ref[...] = after
    unit, _ = normalised(after)
    normed_two = (unit * vec_ref[2:3, :] + vec_ref[3:4, :]).astype(bf16)
    for copy in weights_in:
        copy.wait()

    def inner_of(tile):
        columns = slice(tile * TILE, (tile + 1) * TILE)
        return dot_nn(normed_two, up_s[:, columns]) + vec_ref[8 + tile : 9 + tile, :]

    ahead = inner_of(0)
    for tile in range(FF // TILE):
        columns = slice(tile * TILE, (tile + 1) * TILE)
        inner = ahead
        if tile + 1 < FF // TILE:
            ahead = inner_of(tile + 1)
        act_s[:, columns] = (
            0.5 * inner * (1.0 + jnp.tanh(GELU_SCALE * (inner + 0.044715 * inner * inner * inner)))
        ).astype(bf16)
    hidden = after + (dot_nn(act_s[...], down_s[...]) + vec_ref[7:8, :])
    hid_ref[...] = hidden
    hid16_ref[...] = hidden.astype(bf16)
    for copy in saved_out:
        copy.wait()


SAVED = (
    ((SEG, D), f32),
    ((2 * SEG, D), bf16),
    ((SEG, D), bf16),
    ((2 * SEG, D), bf16),
    ((2 * SEG, D), bf16),
    ((HEADS, SEG), f32),
    ((SEG, D), bf16),
    ((SEG, D), f32),
    ((SEG, D), bf16),
)


def whole_spec(shape):
    return pl.BlockSpec(shape, lambda *_: (0,) * len(shape))


def stream_spec(shape, stream=None):
    zeros = (0,) * len(shape)
    if stream is None:
        return pl.BlockSpec((None,) + shape, lambda i: (i,) + zeros)
    return pl.BlockSpec((None,) + shape, lambda i: (stream,) + zeros)


def layer_spec(shape, depth):
    zeros = (0,) * len(shape)
    return pl.BlockSpec((None,) + shape, lambda *_: (depth,) + zeros)


def forward_layer(depth, stream, streams, bias, hidden, memory, attn, upper, lower, vectors, earlier):
    saved_shapes = [jax.ShapeDtypeStruct((streams,) + shape, dtype) for shape, dtype in SAVED]
    saved_specs = [stream_spec(shape, stream) for shape, dtype in SAVED]
    out_shape = [saved_shapes[0], jax.ShapeDtypeStruct((SEG, D), bf16)] + saved_shapes[1:]
    out_specs = [saved_specs[0], whole_spec((SEG, D))] + saved_specs[1:]
    for place in (2, 3, 4, 5):
        out_specs[place] = pl.BlockSpec(memory_space=pl.ANY)
    operands = [bias, hidden, memory, attn, upper, lower, vectors]
    in_specs = [
        pl.BlockSpec(memory_space=pltpu.SMEM),
        stream_spec((SEG, D), stream),
        stream_spec((SEG, D), stream) if memory.ndim == 3 else whole_spec((SEG, D)),
        layer_spec(attn.shape[1:], depth),
        pl.BlockSpec(memory_space=pl.ANY),
        pl.BlockSpec(memory_space=pl.ANY),
        layer_spec(vectors.shape[1:], depth),
    ]
    aliases = {}
    if earlier is not None:
        for place, array in enumerate(earlier):
            aliases[len(operands)] = place if place == 0 else place + 1
            operands.append(array)
            in_specs.append(pl.BlockSpec(memory_space=pl.ANY))
    out = pl.pallas_call(
        functools.partial(forward_kernel, depth, stream),
        grid=(1,),
        out_shape=out_shape,
        in_specs=in_specs,
        out_specs=out_specs,
        scratch_shapes=[
            pltpu.VMEM((SEG, FF), bf16),
            pltpu.VMEM((SEG, PAIR), f32),
            pltpu.VMEM((D, FF), bf16),
            pltpu.VMEM((FF, D), bf16),
            pltpu.VMEM((2 * SEG, D), bf16),
            pltpu.VMEM((SEG, D), bf16),
            pltpu.VMEM((2 * SEG, D), bf16),
            pltpu.VMEM((2 * SEG, D), bf16),
            pltpu.SemaphoreType.DMA((2,)),
            pltpu.SemaphoreType.DMA((4,)),
        ],
        input_output_aliases=aliases,
        compiler_params=pltpu.CompilerParams(vmem_limit_bytes=VMEM_LIMIT),
        cost_estimate=pl.CostEstimate(flops=10**10, bytes_accessed=2 * 10**7, transcendentals=10**7),
        name="layer_forward",
    )(*operands)
    return [out[0]] + list(out[2:]), out[1]


def head_kernel(scale, x_ref, target_ref, mask_ref, total_ref, out_ref, outer_ref, mom_ref, g_ref, dout_ref, douter_ref, acc_s):
    step = pl.program_id(0)

    @pl.when(step == 0)
    def _():
        acc_s[...] = jnp.zeros_like(acc_s)
        douter_ref[...] = jnp.zeros_like(douter_ref)

    unit, rscale = normalised(x_ref[...])
    gain = outer_ref[1:2, :]
    normed = (unit * gain + outer_ref[2:3, :]).astype(bf16)
    shift = jnp.concatenate([outer_ref[3:4, :], outer_ref[4:5, :]], 1)
    logits = dot_nn(normed, out_ref[...]) + shift
    most = jnp.max(logits, -1, keepdims=True)
    powers = jnp.exp(logits - most)
    total = jnp.sum(powers, -1, keepdims=True)
    target_row = target_ref[pl.ds(step, 1), :].astype(f32)
    weight_row = mask_ref[pl.ds(step, 1), :].astype(f32) * (1.0 / total_ref[pl.ds(step, 1), 0:1])
    columns = jnp.transpose(jnp.concatenate([target_row, weight_row, jnp.zeros((6, SEG), f32)], 0))
    target, weight = columns[:, 0:1].astype(jnp.int32), columns[:, 1:2]
    chosen = lax.broadcasted_iota(jnp.int32, logits.shape, 1) == target
    picked = jnp.sum(jnp.where(chosen, logits, 0.0), -1, keepdims=True)
    loss = jnp.sum(weight * (most + jnp.log(total) - picked), 0, keepdims=True)
    spread = weight * scale
    dlogits = (powers * (spread / total) - jnp.where(chosen, spread, 0.0)).astype(bf16)
    acc_s[...] += dot_nn(jnp.transpose(normed), dlogits)
    bias_grad = column_sum(dlogits.astype(f32))
    dnormed = dot_nt(dlogits, out_ref[...])
    g_ref[...] = norm_back(dnormed, gain, unit, rscale)
    douter_ref[1:2, :] += column_sum(dnormed * unit)
    douter_ref[2:3, :] += column_sum(dnormed)
    douter_ref[3:4, :] += bias_grad[:, :D]
    douter_ref[4:5, :] += bias_grad[:, D:]
    douter_ref[5:6, :] += jnp.broadcast_to(loss, (1, D))

    @pl.when(step == pl.num_programs(0) - 1)
    def _():
        half = D // 2
        for right in range(2):
            for low in range(2):
                dout_ref[right, low] = acc_s[
                    low * half : (low + 1) * half, right * D : (right + 1) * D
                ]


def head(hidden, targets, mask, totals, out_weight, outer_vectors, scale, momenta):
    streams = hidden.shape[0]
    codes = out_weight.shape[1]
    return pl.pallas_call(
        functools.partial(head_kernel, scale),
        grid=(streams,),
        out_shape=[
            jax.ShapeDtypeStruct((streams, SEG, D), f32),
            jax.ShapeDtypeStruct((2, 2, D // 2, D), f32),
            jax.ShapeDtypeStruct((8, D), f32),
        ],
        in_specs=[
            stream_spec((SEG, D)),
            whole_spec((streams, SEG)),
            whole_spec((streams, SEG)),
            whole_spec((8, 128)),
            whole_spec((D, codes)),
            whole_spec(outer_vectors.shape),
            pl.BlockSpec(memory_space=pl.ANY),
        ],
        out_specs=[stream_spec((SEG, D)), whole_spec((2, 2, D // 2, D)), whole_spec((8, D))],
        scratch_shapes=[pltpu.VMEM((D, codes), f32)],
        compiler_params=pltpu.CompilerParams(vmem_limit_bytes=VMEM_LIMIT),
        cost_estimate=pl.CostEstimate(flops=33 * 10**8, bytes_accessed=10**7, transcendentals=10**6),
        name="head",
    )(hidden, targets, mask, totals, out_weight, outer_vectors, momenta)


def feed_back_kernel(streams, g_ref, after_ref, up_ref, down_ref, vec_ref, *refs):
    step = pl.program_id(0)
    grad_ref, dafter_ref, dup_ref, ddown_ref, dvec_ref, done_ref, normed_s, branch_s, act_s, inner_s = refs[:10]
    carry = AttnCarry(grad_ref, refs[10 : 10 + CARRY_REFS], refs[10 + CARRY_REFS :], done_ref)
    planes = carry.planes
    early, late = range(planes // 2), range(planes // 2, planes)
    beats = [
        [("b", place) for place in range(planes)],
        [("m", place) for place in early],
        [("m", place) for place in late],
        [("e", place) for place in early],
        [("e", place) for place in late],
    ]

    @pl.when(step == 0)
    def _():
        hail(carry.targets)
        carry.load_all()
        dvec_ref[...] = jnp.zeros_like(dvec_ref)

    rows = pl.ds(pl.multiple_of(step * SEG, SEG), SEG)
    grad = g_ref[...]
    branch = grad.astype(bf16)
    dvec_ref[2:3, :] += column_sum(branch.astype(f32))
    unit, scale = normalised(after_ref[...])
    gain = vec_ref[2:3, :]
    normed = (unit * gain + vec_ref[3:4, :]).astype(bf16)
    normed_s[:, rows] = jnp.transpose(normed)
    branch_s[:, rows] = jnp.transpose(branch)

    @pl.when(step == 0)
    def _():
        meet(carry.targets)
        carry.send_all()

    def products(tile):
        columns = slice(tile * TILE, (tile + 1) * TILE)
        inner = dot_nn(normed, up_ref[:, columns]) + vec_ref[8 + tile : 9 + tile, :]
        return inner, dot_nt(branch, down_ref[columns, :])

    ahead = products(0)
    for tile in range(FF // TILE):
        columns = slice(tile * TILE, (tile + 1) * TILE)
        inner, dact = ahead
        if tile + 1 < FF // TILE:
            ahead = products(tile + 1)
        square = inner * inner
        bent = jnp.tanh(inner * (GELU_SCALE + (GELU_SCALE * 0.044715) * square))
        half = 0.5 * (1.0 + bent)
        act_s[rows, columns] = (inner * half).astype(bf16)
        slope = half + inner * (half * (1.0 - bent)) * (GELU_SCALE + (GELU_SCALE * 0.134145) * square)
        dinner = (dact * slope).astype(bf16)
        inner_s[rows, columns] = dinner
        dvec_ref[4 + tile : 5 + tile, :] += column_sum(dinner.astype(f32))

    @pl.when(step == 0)
    def _():
        carry.run(beats[0])

    @pl.when(step == streams - 1)
    def _():
        carry.run(beats[1])

    dnormed = dot_nt(inner_s[rows, :], up_ref[...])
    dvec_ref[0:1, :] += column_sum(dnormed * unit)
    dvec_ref[1:2, :] += column_sum(dnormed)
    dafter_ref[...] = grad + norm_back(dnormed, gain, unit, scale)

    @pl.when(step == streams - 1)
    def _():
        carry.run(beats[2])
        for tile in range(FF // TILE):
            columns = slice(tile * TILE, (tile + 1) * TILE)
            dup_ref[tile] = dot_nn(normed_s[...], inner_s[:, columns]).astype(bf16)
        carry.run(beats[3])
        for tile in range(FF // TILE):
            columns = slice(tile * TILE, (tile + 1) * TILE)
            ddown_ref[columns, :] = jnp.transpose(dot_nn(branch_s[...], act_s[:, columns]).astype(bf16))
        carry.run(beats[4])
        carry.drain()


def feed_back(depth, grad, after, upper, lower, vectors, count, dp_count, attn_grad):
    streams = grad.shape[0]
    rows = attn_grad.shape[0] // (GROUPS * count)
    in_specs = [
        stream_spec((SEG, D)),
        stream_spec((SEG, D)),
        layer_spec(upper.shape[1:], depth),
        layer_spec(lower.shape[1:], depth),
        layer_spec(vectors.shape[1:], depth),
    ]
    out_shape = [
        jax.ShapeDtypeStruct((streams, SEG, D), f32),
        jax.ShapeDtypeStruct((FF // TILE, D, TILE), bf16),
        jax.ShapeDtypeStruct((FF, D), bf16),
        jax.ShapeDtypeStruct((8, D), f32),
    ]
    out_specs = [
        stream_spec((SEG, D)),
        whole_spec((FF // TILE, D, TILE)),
        whole_spec((FF, D)),
        whole_spec((8, D)),
    ]
    scratch = [
        pltpu.VMEM((D, streams * SEG), bf16),
        pltpu.VMEM((D, streams * SEG), bf16),
        pltpu.VMEM((streams * SEG, FF), bf16),
        pltpu.VMEM((streams * SEG, FF), bf16),
    ]
    operands = [grad, after, upper, lower, vectors]
    in_specs.append(pl.BlockSpec(memory_space=pl.ANY))
    operands.append(attn_grad.reshape(2, 2, count, rows, D))
    out_shape.append(jax.ShapeDtypeStruct((count // 2, rows, D), attn_grad.dtype))
    out_specs.append(whole_spec((count // 2, rows, D)))
    scratch = scratch + carry_scratch("attn", rows, count, dp_count, attn_grad.dtype)
    params = {"collective_id": 6 + depth, "has_side_effects": True}
    return pl.pallas_call(
        functools.partial(feed_back_kernel, streams),
        grid=(streams,),
        out_shape=out_shape,
        in_specs=in_specs,
        out_specs=out_specs,
        scratch_shapes=scratch,
        compiler_params=pltpu.CompilerParams(vmem_limit_bytes=VMEM_LIMIT, **params),
        cost_estimate=pl.CostEstimate(flops=11 * 10**9, bytes_accessed=2 * 10**7, transcendentals=2 * 10**6),
        name="feed_back",
    )(*operands)


def attend_back_kernel(
    streams,
    depth,
    bias_ref,
    dafter_ref,
    x_ref,
    mem_ref,
    keyin_ref,
    q_ref,
    k_ref,
    v_ref,
    lse_ref,
    mixed_ref,
    attn_ref,
    vec_ref,
    frames_ref,
    dup_ref,
    ddown_ref,
    sums_ref,
    dx_ref,
    dattn_ref,
    dvec_ref,
    din_ref,
    done_ref,
    along_ref,
    attn_s,
    dmixed_s,
    dq_s,
    dk_s,
    dv_s,
    ds_s,
    delta_s,
    *refs,
):
    step = pl.program_id(0)
    pairs = HEADS // 2
    split = CARRY_REFS + 1 + CARRY_SEMS
    carry = FeedCarry(depth, dup_ref, ddown_ref, refs[: CARRY_REFS + 1], refs[CARRY_REFS + 1 : split])
    along = ZCarry(refs[split : split + Z_REFS], refs[split + Z_REFS :])
    plans, (free, bound) = carry.plans(), along.plans()

    @pl.when(step == 0)
    def _():
        hail(carry.targets)
        carry.load_all()
        along.sums[...] = sums_ref[...]
        attn_s[...] = jnp.zeros_like(attn_s)
        dvec_ref[...] = jnp.zeros_like(dvec_ref)
        din_ref[...] = jnp.zeros_like(din_ref)

    dafter = dafter_ref[...]
    branch = dafter.astype(bf16)
    dvec_ref[4:5, :] += column_sum(branch.astype(f32))
    dmixed = dot_nt(branch, attn_ref[3]).astype(bf16)
    dmixed_s[...] = dmixed
    attn_s[3] += dot_nn(jnp.transpose(mixed_ref[...]), branch)
    product = dmixed.astype(f32) * mixed_ref[...].astype(f32)
    high = product.astype(bf16)
    rest = (product - high.astype(f32)).astype(bf16)
    owner = lax.broadcasted_iota(jnp.int32, (HEADS, D), 1) // HEAD_DIM
    pick = (owner == lax.broadcasted_iota(jnp.int32, (HEADS, D), 0)).astype(bf16)
    delta_s[...] = dot_nt(pick, high) + dot_nt(pick, rest)
    first, second = head_masks()
    memory_bias = bias_ref[0]
    key_pos = lax.broadcasted_iota(jnp.int32, (HALF, 2 * HALF), 0)
    query_pos = lax.broadcasted_iota(jnp.int32, (HALF, 2 * HALF), 1) % HALF
    diagonal = key_pos <= query_pos
    head_row = lax.broadcasted_iota(jnp.int32, (PAIR, HALF), 0)

    @pl.when(step == 0)
    def _():
        meet(carry.targets)
        carry.send_all()
        along.run(free)

    @pl.when(step == 1)
    def _():
        carry.run(plans[-1])

    def pair_body(pair, state):
        lanes = pair_lanes(pair)
        q_pair, do_pair = q_ref[:, lanes], dmixed_s[:, lanes]

        def spread(value):
            return jnp.concatenate(
                [value[:HALF] * first, value[:HALF] * second, value[HALF:] * first, value[HALF:] * second], 0
            )

        q_all, do_all = spread(q_pair), spread(do_pair)

        def rows_of(ref):
            one, two = ref[pl.ds(2 * pair, 1), :], ref[pl.ds(2 * pair + 1, 1), :]
            return jnp.concatenate([one[:, :HALF], two[:, :HALF], one[:, HALF:], two[:, HALF:]], 1)

        lse_all, delta_all = rows_of(lse_ref), rows_of(delta_s)
        starts = (0, 0, 0, 2 * HALF)

        def products(block):
            keys = slice(block * HALF, (block + 1) * HALF)
            scores = dot_nt(k_ref[keys, lanes], q_all[starts[block] :])
            return scores, dot_nt(v_ref[keys, lanes], do_all[starts[block] :])

        ahead = products(0)
        for block in range(4):
            scores, dweights = ahead
            if block < 3:
                ahead = products(block + 1)
            keys = slice(block * HALF, (block + 1) * HALF)
            start = starts[block]
            shift = lse_all - memory_bias if block < 2 else lse_all[:, start:]
            weights = jnp.exp(scores - shift)
            if block == 2:
                weights = jnp.concatenate(
                    [jnp.where(diagonal, weights[:, : 2 * HALF], 0.0), weights[:, 2 * HALF :]], 1
                )
            if block == 3:
                weights = jnp.where(diagonal, weights, 0.0)
            dscores = (weights * (dweights - delta_all[:, start:])).astype(bf16)
            dv_s[keys, lanes] = dot_nn(weights.astype(bf16), do_all[start:]).astype(bf16)
            dk_s[keys, lanes] = dot_nn(dscores, q_all[start:]).astype(bf16)
            ds_s[keys, start:] = dscores
        k_t = jnp.transpose(k_ref[:, lanes])
        for block in range(2):
            seen = SEG + (block + 1) * HALF
            grads = dot_nn(k_t[:, :seen], ds_s[:seen, block * 2 * HALF : (block + 1) * 2 * HALF])
            grads = jnp.where(head_row < HEAD_DIM, grads[:, :HALF], grads[:, HALF:])
            dq_s[block * HALF : (block + 1) * HALF, lanes] = (
                jnp.transpose(grads) * (HEAD_DIM**-0.5)
            ).astype(bf16)
        for time, acts in enumerate(plans[:-1]):
            if acts:

                @pl.when(pairs * step + pair == time)
                def _():
                    carry.run(acts)
                    if time == 3:
                        along.run(bound)

        return state

    lax.fori_loop(0, pairs, pair_body, 0)
    dq, dk, dv = dq_s[...], dk_s[...], dv_s[...]
    keyin_t = jnp.transpose(keyin_ref[...])
    attn_s[0] += dot_nn(keyin_t[:, SEG:], dq)
    attn_s[1] += dot_nn(keyin_t, dk)
    attn_s[2] += dot_nn(keyin_t, dv)
    dvec_ref[2:3, :] += column_sum(dq.astype(f32))
    dvec_ref[3:4, :] += column_sum(dv.astype(f32))
    dkeyin = dot_nt(dk, attn_ref[1]) + dot_nt(dv, attn_ref[2])
    dmem = dkeyin[:SEG]
    down = dkeyin[SEG:] + dot_nt(dq, attn_ref[0])
    gain = vec_ref[0:1, :]
    unit, scale = normalised(x_ref[...])
    mem_unit, _ = normalised(mem_ref[...].astype(f32))
    dvec_ref[0:1, :] += column_sum(down * unit + dmem * mem_unit)
    dvec_ref[1:2, :] += column_sum(down + dmem)
    dx = dafter + norm_back(down, gain, unit, scale)
    dx_ref[...] = dx
    if depth == 0:
        dx_high = dx.astype(bf16)
        dx_rest = (dx - dx_high.astype(f32)).astype(bf16)
        din_ref[...] += dot_nn(frames_ref[...], dx_high) + dot_nn(frames_ref[...], dx_rest)
        dvec_ref[5:6, :] += column_sum(dx)

    @pl.when(step == pl.num_programs(0) - 1)
    def _():
        dattn_ref[...] = attn_s[...].astype(bf16)
        carry.finish(done_ref)
        along.finish(along_ref)


def attend_back(depth, bias, dafter, x, memory, saved, attn, vectors, frames, up_grad, down_grad, sums, count, dp_count):
    streams = dafter.shape[0]
    keyin, q, k, v, lse, mixed = saved
    inputs = frames.shape[1]
    rows = D // count
    up_grad, down_grad = up_grad.reshape(4, count, rows, D), down_grad.reshape(count, 4, rows, D)
    return pl.pallas_call(
        functools.partial(attend_back_kernel, streams, depth),
        grid=(streams,),
        out_shape=[
            jax.ShapeDtypeStruct((streams, SEG, D), f32),
            jax.ShapeDtypeStruct((4, D, D), bf16),
            jax.ShapeDtypeStruct((8, D), f32),
            jax.ShapeDtypeStruct((inputs, D), f32),
            jax.ShapeDtypeStruct((2, rows, D), bf16),
            jax.ShapeDtypeStruct(sums.shape[1:], bf16),
        ],
        in_specs=[
            pl.BlockSpec(memory_space=pltpu.SMEM),
            stream_spec((SEG, D)),
            stream_spec((SEG, D)),
            stream_spec((SEG, D)),
            stream_spec((2 * SEG, D)),
            stream_spec((SEG, D)),
            stream_spec((2 * SEG, D)),
            stream_spec((2 * SEG, D)),
            stream_spec((HEADS, SEG)),
            stream_spec((SEG, D)),
            layer_spec(attn.shape[1:], depth),
            layer_spec(vectors.shape[1:], depth),
            stream_spec((inputs, SEG)),
            pl.BlockSpec(memory_space=pl.ANY),
            pl.BlockSpec(memory_space=pl.ANY),
            whole_spec(sums.shape),
        ],
        out_specs=[
            stream_spec((SEG, D)),
            whole_spec((4, D, D)),
            whole_spec((8, D)),
            whole_spec((inputs, D)),
            whole_spec((2, rows, D)),
            whole_spec(sums.shape[1:]),
        ],
        scratch_shapes=[
            pltpu.VMEM((4, D, D), f32),
            pltpu.VMEM((SEG, D), bf16),
            pltpu.VMEM((SEG, D), bf16),
            pltpu.VMEM((2 * SEG, D), bf16),
            pltpu.VMEM((2 * SEG, D), bf16),
            pltpu.VMEM((2 * SEG, 2 * SEG), bf16),
            pltpu.VMEM((HEADS, SEG), f32),
        ]
        + carry_scratch("feed", rows, count, dp_count)
        + z_scratch(sums.shape[1], count, dp_count, sums.dtype),
        compiler_params=pltpu.CompilerParams(
            collective_id=4 + depth, has_side_effects=True, vmem_limit_bytes=VMEM_LIMIT
        ),
        cost_estimate=pl.CostEstimate(flops=3 * 10**10, bytes_accessed=2 * 10**7, transcendentals=10**7),
        name="attend_back",
    )(bias, dafter, x, memory, keyin, q, k, v, lse, mixed, attn, vectors, frames, up_grad, down_grad, sums)


def from_behind(value, axis, steps):
    count = lax.axis_size(axis)
    leading, last = (max(0, -steps), min(count, count - steps))
    return lax.ppermute(value, axis, [(source, source + steps) for source in range(leading, last)])


def adamw(weight, moment, second, grad, rate, decay):
    moment = 0.5 * moment + 0.5 * grad
    second = 0.99 * second + 0.01 * grad * grad
    fixed_moment = moment / (1.0 - 0.5**STEP)
    fixed_second = second / (1.0 - 0.99**STEP)
    weight = weight * (1.0 - rate * decay) - rate * fixed_moment / (jnp.sqrt(fixed_second) + 1e-08)
    return (weight, moment, second)


GROUPS = 4
UNITS = 6
SMALL = 128


def peers():
    count = {"seg": lax.axis_size("seg"), "dp": lax.axis_size("dp")}
    seg, dp = lax.axis_index("seg"), lax.axis_index("dp")
    core, x, y = seg % 2, dp % 2, (dp // 2) % 2
    across_core = {"seg": seg + 1 - 2 * core}
    across_x = {"dp": dp + 1 - 2 * x}
    across_y = {"dp": dp + 2 - 4 * y}
    across_both = {"dp": dp + 3 - 2 * x - 4 * y}
    far = []
    step = GROUPS
    while step < count["dp"]:
        far.append({"dp": dp + step - 2 * step * ((dp // step) % 2)})
        step *= 2
    return seg, dp, core, x, y, across_core, (across_x, across_y, across_both), far


def others(seg, count):
    return [lax.rem(seg + step, count) for step in range(1, count)]


def hail(targets):
    barrier = pltpu.get_barrier_semaphore()
    for target in targets:
        pl.semaphore_signal(barrier, inc=1, device_id=target, device_id_type=pl.DeviceIdType.MESH)


def meet(targets):
    pl.semaphore_wait(pltpu.get_barrier_semaphore(), len(targets))


def greet(seg, count, near, far):
    targets = [{"seg": other} for other in others(seg, count)] + list(near) + list(far)
    hail(targets)
    meet(targets)


def remote(source, target, send, recv, device):
    return pltpu.make_async_remote_copy(
        src_ref=source,
        dst_ref=target,
        send_sem=send,
        recv_sem=recv,
        device_id=device,
        device_id_type=pl.DeviceIdType.MESH,
    )


def wait_bytes(ref, sem):
    pltpu.make_async_copy(ref, ref, sem).wait()


def plus(left, right):
    return (left.astype(f32) + right.astype(f32)).astype(left.dtype)


def owners(count):
    low, high = count // 4 - 1, count // 4
    return (
        (0, 1, 0, 0),
        (1, 1, count - 2, 0),
        (2, 2, 2 * low, 0),
        (4, 2, 2 * low + 1, 2),
        (2, 2, 2 * high, 0),
        (4, 2, 2 * high + 1, 2),
    )


def lowest_bit(mask, planes):
    bit = 1
    while bit < planes and not mask & bit:
        bit *= 2
    return bit


class Carry:
    def __init__(self, refs, sems):
        self.mine, self.got0, self.got1, self.got2, self.got3, self.goth = refs
        (
            self.load,
            self.send0,
            self.recv0,
            self.send1,
            self.recv1,
            self.send2,
            self.recv2,
            self.send3,
            self.recv3,
            self.sendh,
            self.recvh,
        ) = sems
        self.settle(self.mine.shape[0])

    def settle(self, planes):
        self.seg, self.dp, self.core, self.x, self.y, self.across_core, near, self.far = peers()
        self.across_x, self.across_y, _ = near
        self.planes = planes
        self.plane = self.seg // 2
        self.targets = [self.across_core, self.across_x, self.across_y] + self.far
        bit = 1
        while bit < planes:
            self.targets.append({"seg": 2 * self.toggled(bit) + self.core})
            bit *= 2
        self.order = list(reversed(range(planes)))

    def toggled(self, mask):
        place, bit = self.plane, 1
        while bit <= mask:
            if mask & bit:
                place = place + bit - 2 * bit * ((self.plane // bit) % 2)
            bit *= 2
        return place

    def load_all(self):
        for step in range(self.planes):
            for source, place in self.pieces(2 * self.toggled(self.order[step]) + self.core):
                pltpu.make_async_copy(source, self.mine.at[(step,) + place], self.load.at[step]).start()

    def send_all(self):
        for step in range(self.planes):
            for source, place in self.pieces(2 * self.toggled(self.order[step]) + 1 - self.core):
                remote(
                    source, self.got0.at[(step,) + place], self.send0.at[step], self.recv0.at[step], self.across_core
                ).start()

    def begin(self, step):
        wait_bytes(self.mine.at[step], self.load.at[step])
        wait_bytes(self.got0.at[step], self.recv0.at[step])
        for place in range(2):
            self.mine[step, place] = plus(self.mine[step, place], self.got0[step, place])
        for copy in self.first(step):
            copy.start()

    def across(self, place, step):
        return remote(
            self.held(step),
            self.goth.at[place, step],
            self.sendh.at[place, step],
            self.recvh.at[place, step],
            self.far[place],
        )

    def third(self, step):
        mask = self.order[step]
        return remote(
            self.held(step),
            self.got3.at[mask],
            self.send3.at[step],
            self.recv3.at[mask],
            {"seg": 2 * self.toggled(lowest_bit(mask, self.planes)) + self.core},
        )

    def onward(self, step):
        held = self.held(step)
        for place in range(len(self.far)):
            copy = self.across(place, step)
            copy.start()
            copy.wait()
            held[...] = plus(held[...], self.goth[place, step])
        mask = self.order[step]
        if mask:
            self.gathered(mask, held)
            self.third(step).start()

    def gathered(self, mask, held):
        value, bit = held[...].astype(f32), 1
        while bit < lowest_bit(mask, self.planes):
            wait_bytes(self.got3.at[mask + bit], self.recv3.at[mask + bit])
            value = value + self.got3[mask + bit].astype(f32)
            bit *= 2
        held[...] = value.astype(held.dtype)

    def total(self):
        held = self.held(self.planes - 1)
        self.gathered(0, held)
        return held[...]

    def run(self, acts):
        for kind, step in acts:
            getattr(self, {"b": "begin", "m": "middle", "e": "end", "z": "onward"}[kind])(step)


class ZCarry(Carry):
    def __init__(self, refs, sems):
        self.sums, self.got3, self.goth = refs
        self.send3, self.recv3, self.sendh, self.recvh = sems
        self.settle(self.sums.shape[0])

    def held(self, step):
        return self.sums.at[step]

    def plans(self):
        free = [("z", step) for step in range(self.planes) if self.order[step] % 2]
        bound = [("z", step) for step in range(self.planes) if self.order[step] and not self.order[step] % 2]
        return free, bound

    def finish(self, out_ref):
        out_ref[...] = self.total().astype(out_ref.dtype)
        for step in range(self.planes - 1):
            self.third(step).wait_send()


class AttnCarry(Carry):
    def __init__(self, source, refs, sems, sums=None):
        super().__init__(refs, sems)
        self.source, self.sums = source, sums

    def pieces(self, row):
        return ((self.source.at[:, :, row], ()),)

    def held(self, step):
        return self.mine.at[step, self.y, self.x]

    def first(self, step):
        half = self.mine.shape[3] // 2
        return (
            remote(
                self.mine.at[step, :, 1 - self.x, 0:half],
                self.got1.at[step, 0],
                self.send1.at[step, 0],
                self.recv1.at[step, 0],
                self.across_x,
            ),
            remote(
                self.mine.at[step, 1 - self.y, :, half:],
                self.got1.at[step, 1],
                self.send1.at[step, 1],
                self.recv1.at[step, 1],
                self.across_y,
            ),
        )

    def second(self, step):
        half = self.mine.shape[3] // 2
        return (
            remote(
                self.mine.at[step, 1 - self.y, self.x, 0:half],
                self.got2.at[step, 0],
                self.send2.at[step, 0],
                self.recv2.at[step, 0],
                self.across_y,
            ),
            remote(
                self.mine.at[step, self.y, 1 - self.x, half:],
                self.got2.at[step, 1],
                self.send2.at[step, 1],
                self.recv2.at[step, 1],
                self.across_x,
            ),
        )

    def middle(self, step):
        mine, half = self.mine, self.mine.shape[3] // 2
        for copy in self.first(step):
            copy.wait_recv()
        for place in range(2):
            mine[step, place, self.x, 0:half] = plus(mine[step, place, self.x, 0:half], self.got1[step, 0, place])
            mine[step, self.y, place, half:] = plus(mine[step, self.y, place, half:], self.got1[step, 1, place])
        for copy in self.second(step):
            copy.start()

    def end(self, step):
        mine, half = self.mine, self.mine.shape[3] // 2
        for copy in self.second(step):
            copy.wait_recv()
        upper = plus(mine[step, self.y, self.x, 0:half], self.got2[step, 0])
        lower = plus(mine[step, self.y, self.x, half:], self.got2[step, 1])
        if self.sums is not None:
            self.sums[step, 0:half] = upper
            self.sums[step, half:] = lower
            return
        mine[step, self.y, self.x, 0:half] = upper
        mine[step, self.y, self.x, half:] = lower
        self.onward(step)

    def drain(self):
        for step in range(self.planes):
            wait_bytes(self.mine.at[step], self.send0.at[step])
            for copy in self.first(step) + self.second(step):
                copy.wait_send()
            if self.sums is None and step < self.planes - 1:
                self.third(step).wait_send()


class FeedCarry(Carry):
    def __init__(self, depth, up, down, refs, sems):
        super().__init__(refs[:CARRY_REFS], sems)
        (self.sums,) = refs[CARRY_REFS:]
        self.up, self.down = up, down
        self.keep = self.x if depth == 1 else 1 - self.x

    def pieces(self, row):
        return ((self.up.at[:, row], (0,)), (self.down.at[row], (1,)))

    def held(self, step):
        return self.sums.at[step]

    def first(self, step):
        return (
            remote(
                self.mine.at[step, 1 - self.keep, 0:2],
                self.got1.at[step, 0],
                self.send1.at[step, 0],
                self.recv1.at[step, 0],
                self.across_x,
            ),
            remote(
                self.mine.at[step, 1 - self.y, 2:4],
                self.got1.at[step, 1],
                self.send1.at[step, 1],
                self.recv1.at[step, 1],
                self.across_y,
            ),
        )

    def second(self, step):
        return (
            remote(
                self.mine.at[step, self.keep, 1 - self.y],
                self.got2.at[step, 0],
                self.send2.at[step, 0],
                self.recv2.at[step, 0],
                self.across_y,
            ),
            remote(
                self.mine.at[step, self.y, 3 - self.x],
                self.got2.at[step, 1],
                self.send2.at[step, 1],
                self.recv2.at[step, 1],
                self.across_x,
            ),
        )

    def middle(self, step):
        for copy in self.first(step):
            copy.wait_recv()
        self.mine[step, self.keep, 0:2] = plus(self.mine[step, self.keep, 0:2], self.got1[step, 0])
        self.mine[step, self.y, 2:4] = plus(self.mine[step, self.y, 2:4], self.got1[step, 1])
        for copy in self.second(step):
            copy.start()

    def end(self, step):
        for copy in self.second(step):
            copy.wait_recv()
        self.sums[step, 0] = plus(self.mine[step, self.keep, self.y], self.got2[step, 0])
        self.sums[step, 1] = plus(self.mine[step, self.y, 2 + self.x], self.got2[step, 1])
        self.onward(step)

    def plans(self):
        planes = self.planes
        return (
            [("b", step) for step in range(planes - 1)],
            [],
            [("m", 0), ("b", planes - 1)],
            [("m", 1)],
            [("m", step) for step in range(3, planes)],
            [("e", 1)],
            [("e", 2)],
            [("e", step) for step in range(3, planes)],
            [("m", 2), ("e", 0)],
        )

    def finish(self, out_ref):
        out_ref[...] = self.total()
        for step in range(self.planes):
            wait_bytes(self.mine.at[step], self.send0.at[step])
            for copy in self.first(step) + self.second(step):
                copy.wait_send()
            if step < self.planes - 1:
                self.third(step).wait_send()


CARRY_REFS = 6
CARRY_SEMS = 11


def carry_scratch(kind, rows, count, dp_count, dtype=bf16):
    planes = count // 2
    far = max(1, dp_count.bit_length() - 3)
    dma = pltpu.SemaphoreType.DMA
    half = rows // 2
    if kind == "attn":
        shapes = (
            (planes, 2, 2, rows),
            (planes, 2, 2, rows),
            (planes, 2, 2, half),
            (planes, 2, half),
            (planes, rows),
            (far, planes, rows),
        )
    else:
        shapes = (
            (planes, 2, 4, rows),
            (planes, 2, 4, rows),
            (planes, 2, 2, rows),
            (planes, 2, rows),
            (planes, 2, rows),
            (far, planes, 2, rows),
            (planes, 2, rows),
        )
    pair = (planes, 2)
    one = (planes,)
    sems = (one, one, one, pair, pair, pair, pair, one, one, (far, planes), (far, planes))
    return [pltpu.VMEM(shape + (D,), dtype) for shape in shapes] + [dma(shape) for shape in sems]


def z_scratch(rows, count, dp_count, dtype):
    planes = count // 2
    far = max(1, dp_count.bit_length() - 3)
    dma = pltpu.SemaphoreType.DMA
    shapes = ((planes, rows), (planes, rows), (far, planes, rows))
    sems = ((planes,), (planes,), (far, planes), (far, planes))
    return [pltpu.VMEM(shape + (D,), dtype) for shape in shapes] + [dma(shape) for shape in sems]


Z_REFS = 3
Z_SEMS = 4


def halves(value):
    high = value.astype(bf16)
    return high, (value - high.astype(f32)).astype(bf16)


def times(left, right):
    (left_high, left_low), (right_high, right_low) = left, right
    return dot_nn(
        jnp.concatenate([left_high, left_high, left_low], 1),
        jnp.concatenate([right_high, right_low, right_high], 0),
    )


def mirrored(first, second, third):
    return jnp.concatenate(
        [
            jnp.concatenate([first, second], 1),
            jnp.concatenate([jnp.transpose(second), third], 1),
        ],
        0,
    )


def times_even(left, right):
    (left_high, left_low), (right_high, right_low) = left, right
    wide = jnp.concatenate([left_high, left_high, left_low], 1)
    tall = jnp.concatenate([right_high, right_low, right_high], 0)
    return mirrored(
        dot_nn(wide[:HALF], tall[:, :HALF]),
        dot_nn(wide[:HALF], tall[:, HALF:]),
        dot_nn(wide[HALF:], tall[:, HALF:]),
    )


def gram_of(both):
    high, low = both
    wide = jnp.concatenate([high, high, low], 1)
    tall = jnp.concatenate([high, low, high], 1)
    return mirrored(
        dot_nt(wide[:HALF], tall[:HALF]),
        dot_nt(wide[:HALF], tall[HALF:]),
        dot_nt(wide[HALF:], tall[HALF:]),
    )


def clip_of(norm):
    return jnp.minimum(1.0, 0.25 / (norm + 1e-06))


def tail_kernel(
    count,
    attn_grad_ref,
    attn_done_ref,
    feed_low_ref,
    feed_high_ref,
    dout_ref,
    din_ref,
    vec0_ref,
    vec1_ref,
    vec2_ref,
    vec3_ref,
    outer_ref,
    mom_ref,
    update_ref,
    every_ref,
    small_out,
    norm_ref,
    whole_ref,
    own_ref,
    mom_s,
    small_ref,
    small_s,
    got_core,
    got_x,
    got_y,
    got_z,
    sq_seg,
    sq_dp,
    keep_s,
    give_s,
    made_ref,
    x_s,
    q_s,
    gram_s,
    high_s,
    low_s,
    mom_sem,
    last_send,
    last_recv,
    small_send,
    small_recv,
    join_send,
    join_recv,
    whole_send,
    whole_recv,
    half_sem,
    sq_send,
    sq_recv,
    sqd_send,
    sqd_recv,
    send,
    recv,
    on_send,
    on_recv,
    own_send,
    own_recv,
    *refs,
):
    carry = AttnCarry(attn_grad_ref, refs[:CARRY_REFS], refs[CARRY_REFS:])
    seg, dp, core, x, y, across_core, near, far = peers()
    across_x, across_y, across_both = near
    planes = count // 2
    plane = seg // 2
    group = 2 * y + x
    rows = own_ref.shape[1]
    targets = [{"seg": other} for other in others(seg, count)] + list(near) + list(far)
    hail(targets)
    carry.load_all()
    mom_copy = pltpu.make_async_copy(mom_ref, mom_s, mom_sem.at[0])
    mom_copy.start()
    own_ref[1] = attn_done_ref[...]

    @pl.when(x == y)
    def _():
        keep_s[...] = feed_high_ref[...]
        give_s[...] = feed_low_ref[...]

    @pl.when(x != y)
    def _():
        keep_s[...] = feed_low_ref[...]
        give_s[...] = feed_high_ref[...]

    own_ref[2 + y] = keep_s[0]
    own_ref[4 + x] = keep_s[1]
    last = (
        remote(give_s.at[0], own_ref.at[2 + y], last_send.at[0], last_recv.at[0], across_y),
        remote(give_s.at[1], own_ref.at[4 + x], last_send.at[1], last_recv.at[1], across_x),
    )
    inputs = din_ref.shape[0]
    small_ref[0:inputs, :] = din_ref[...]
    for place, ref in enumerate((vec0_ref, vec1_ref, vec2_ref, vec3_ref, outer_ref)):
        small_ref[inputs + 8 * place : inputs + 8 * place + 8, :] = ref[...]
    small_ref[inputs + 40 :, :] = jnp.zeros((SMALL - inputs - 40, D), f32)
    meet(targets)

    def span(first, size):
        return pl.ds(pl.multiple_of(first, 8), size)

    by_core, by_x, by_y = SMALL // 2, SMALL // 4, SMALL // 8
    core_at = core * by_core
    x_at = core_at + x * by_x
    y_at = x_at + y * by_y

    def small_steps():
        kept = span(core_at, by_core)
        copy = remote(
            small_ref.at[span(by_core - core_at, by_core)], got_core, small_send.at[0], small_recv.at[0], across_core
        )
        copy.start()
        yield
        copy.wait()
        small_s[kept, :] = small_ref[kept, :] + got_core[...]
        sent = span(core_at + by_x - x * by_x, by_x)
        copy = remote(small_s.at[sent], got_x, small_send.at[1], small_recv.at[1], across_x)
        copy.start()
        yield
        copy.wait()
        small_s[span(x_at, by_x), :] += got_x[...]
        sent = span(x_at + by_y - y * by_y, by_y)
        copy = remote(small_s.at[sent], got_y, small_send.at[2], small_recv.at[2], across_y)
        copy.start()
        yield
        copy.wait()
        kept = span(y_at, by_y)
        small_s[kept, :] += got_y[...]
        partners, step = list(far), 1
        while step < planes:
            partners.append({"seg": 2 * carry.toggled(step) + core})
            step *= 2
        for place, partner in enumerate(partners):
            copy = remote(
                small_s.at[kept], got_z.at[place], small_send.at[3 + place], small_recv.at[3 + place], partner
            )
            copy.start()
            yield
            copy.wait()
            small_s[kept, :] += got_z[place]

    small_run = small_steps()
    next(small_run)
    carry.send_all()
    for copy in last:
        copy.start()
    roles = owners(count)
    parts = []
    for place, (first, width, owner, spot) in enumerate(roles):
        if width == 1:
            parts.append((place, first, spot))
        elif spot == 0:
            parts += [(place, 2 + y, y), (place, 3 - y, 1 - y)]
        else:
            parts += [(place, 4 + x, 2 + x), (place, 5 - x, 3 - x)]

    def gift(part):
        place, unit, spot = parts[part]
        return remote(
            own_ref.at[unit],
            whole_ref.at[seg, spot],
            whole_send.at[part],
            whole_recv.at[seg],
            {"seg": roles[place][2]},
        )

    def give(part):
        place, unit, spot = parts[part]

        @pl.when(seg != roles[place][2])
        def _():
            gift(part).start()

        @pl.when(seg == roles[place][2])
        def _():
            whole_ref[seg, spot] = own_ref[unit]

    acts = [
        [("b", step) for step in range(planes - 1)],
        [("m", 0), ("b", planes - 1)],
        [("m", 1)],
        [("m", 2), ("e", 0)],
        [("m", step) for step in range(3, planes)],
    ] + [[("e", step)] for step in range(1, planes)]
    for part in (2, 4, 6, 8, 1):
        give(part)
    next(small_run)
    for turn, part in enumerate(acts):
        carry.run(part)
        if turn == 0:
            for copy in last:
                copy.wait()
            for later in (3, 5, 7, 9):
                give(later)
        next(small_run, None)
    own_ref[0] = carry.total()
    give(0)
    for _ in small_run:
        pass

    mine = span(y_at, by_y)
    small_out[mine, :] = small_s[mine, :]

    def join(place):
        first, size, partner = ((y_at, by_y, across_y), (x_at, by_x, across_x), (core_at, by_core, across_core))[place]
        block = small_out.at[span(first, size)]
        return remote(block, block, join_send.at[place], join_recv.at[place], partner)

    join(0).start()
    shard = dout_ref[...].astype(f32)
    square = jnp.sum(jnp.sum(shard * shard, 0, keepdims=True), 1, keepdims=True)
    for unit in range(UNITS):
        value = own_ref[unit].astype(f32)
        square = square + jnp.sum(jnp.sum(value * value, 0, keepdims=True), 1, keepdims=True)
    sums = small_s[mine, :]
    is_loss = lax.broadcasted_iota(jnp.int32, (by_y, D), 0) + y_at == inputs + 37
    sums = jnp.where(is_loss, 0.0, sums)
    square = square + jnp.sum(jnp.sum(sums * sums, 0, keepdims=True), 1, keepdims=True) * (1.0 / planes)
    sq_seg[seg] = jnp.broadcast_to(square, (8, 128))
    for step, other in enumerate(others(seg, count)):
        remote(sq_seg.at[seg], sq_seg.at[seg], sq_send.at[step], sq_recv.at[seg], {"seg": other}).start()

    def halves_copy(spot):
        part = slice(spot, spot + 2)
        return remote(whole_ref.at[:, part], whole_ref.at[:, part], half_sem.at[0], half_sem.at[1], across_core)

    for place, (first, width, owner, spot) in enumerate(roles):
        if width == 2:

            @pl.when(seg == owner)
            def _():
                for other in others(seg, count):
                    wait_bytes(whole_ref.at[other, spot : spot + width], whole_recv.at[other])
                halves_copy(spot).start()

    for other in others(seg, count):
        wait_bytes(sq_seg.at[other], sq_recv.at[other])
    sq_dp[group] = jnp.sum(sq_seg[...], 0)
    for place, target in enumerate(near):
        remote(sq_dp.at[group], sq_dp.at[group], sqd_send.at[place], sqd_recv.at[place], target).start()
    join(0).wait()
    join(1).start()
    for place, target in enumerate(near):
        remote(sq_dp.at[group], sq_dp.at[group], sqd_send.at[place], sqd_recv.at[place], target).wait()
    norm = jnp.sqrt(jnp.sum(sq_dp[...], 0)[0:1, 0:1])
    norm_ref[...] = jnp.broadcast_to(norm, norm_ref.shape)
    clip = clip_of(norm)

    def own_rows(side):
        return remote(own_ref, every_ref.at[group], own_send.at[side], own_recv.at[side], near[side])

    for side in range(3):
        own_rows(side).start()
    every_ref[group] = own_ref[...]
    mom_copy.wait()

    for place, (first, width, owner, spot) in enumerate(roles):

        @pl.when(seg == owner)
        def _():
            if width == 2:
                halves_copy(spot).wait()
            else:
                for other in others(seg, count):
                    wait_bytes(whole_ref.at[other, spot : spot + width], whole_recv.at[other])

    is_down = group >= 2
    eye = (
        lax.broadcasted_iota(jnp.int32, (D, D), 0) == lax.broadcasted_iota(jnp.int32, (D, D), 1)
    ).astype(f32)
    low = count // 4 - 1
    half = plane // (planes // 2)
    base = half * planes
    neighbours = [base + lax.rem(seg - base + step, planes) for step in range(1, planes)]
    feed_maker = 2 * (low + half)
    makers = [0, count - 2, feed_maker, feed_maker, feed_maker + 1, feed_maker + 1]

    def receivers(unit):
        return others(seg, count) if unit < 2 else neighbours

    def present(unit, slot, other):
        return remote(
            made_ref.at[other, slot],
            update_ref.at[group, unit],
            send.at[slot, other],
            recv.at[unit],
            {"seg": other},
        )

    def hand_out(unit, slot):
        for other in receivers(unit):
            present(unit, slot, other).start()
        update_ref[group, unit] = made_ref[seg, slot]

    def onward(unit, side):
        block = update_ref.at[group, unit]
        return remote(block, block, on_send.at[side, unit], on_recv.at[side, unit], near[side])

    @pl.when((seg == 0) | (seg == count - 2))
    def _():
        start = (0.5 * mom_s[:, plane // (planes - 1)].astype(f32)).reshape(D, D)
        start = start + clip * whole_ref[:, 0].astype(f32).reshape(D, D)
        size = jnp.sum(jnp.sum(start * start, 0, keepdims=True), 1, keepdims=True)
        x_s[...] = start / (jnp.sqrt(size) + 1e-07)

        def sweep(_, state):
            value = x_s[...]
            both = halves(value)
            gram = gram_of(both)
            gram_both = halves(gram)
            poly = -4.775 * gram + 2.0315 * times_even(gram_both, gram_both)
            x_s[...] = 3.4445 * value + times(halves(poly), both)
            return state

        lax.fori_loop(0, 5, sweep, 0)
        made_ref[:, 0] = x_s[...].astype(bf16).reshape(count, rows, D)
        for unit in range(2):

            @pl.when(seg == makers[unit])
            def _():
                hand_out(unit, 0)

    @pl.when((plane == low) | (plane == low + 1))
    def _():
        gram_s[...] = jnp.zeros_like(gram_s)

        def gather(tile, size):
            value = (0.5 * mom_s[:, 2 + tile].astype(f32)).reshape(D, D)
            value = value + clip * whole_ref[:, tile].astype(f32).reshape(D, D)
            high, rest = halves(value)
            high_s[tile] = high
            low_s[tile] = rest

            @pl.when(is_down)
            def _():
                high_s[tile] = jnp.transpose(high_s[tile])
                low_s[tile] = jnp.transpose(low_s[tile])

            gram_s[...] += gram_of((high_s[tile], low_s[tile]))
            return size + jnp.sum(jnp.sum(value * value, 0, keepdims=True), 1, keepdims=True)

        size = lax.fori_loop(0, 4, gather, jnp.zeros((1, 1), f32))
        scale = 1.0 / (jnp.sqrt(size) + 1e-07)
        gram_s[...] = gram_s[...] * (scale * scale)

        def poly_of(gram, gram_both):
            return 3.4445 * eye - 4.775 * gram + 2.0315 * times_even(gram_both, gram_both)

        def advance(gram_both, poly_both):
            gram_s[...] = times_even(halves(times_even(gram_both, poly_both)), poly_both)

        gram = gram_s[...]
        gram_both = halves(gram)
        poly = poly_of(gram, gram_both)
        q_s[...] = poly
        advance(gram_both, halves(poly))

        def sweep(_, state):
            gram = gram_s[...]
            gram_both = halves(gram)
            poly_both = halves(poly_of(gram, gram_both))
            q_s[...] = times_even(halves(q_s[...]), poly_both)
            advance(gram_both, poly_both)
            return state

        lax.fori_loop(0, 3, sweep, 0)
        gram = gram_s[...]
        last_both = halves(times_even(halves(q_s[...]), halves(poly_of(gram, halves(gram)))) * scale)
        for slot in range(2):
            tile = 2 * core + slot
            x_s[...] = times(last_both, (high_s[tile], low_s[tile]))

            @pl.when(is_down)
            def _():
                x_s[...] = jnp.transpose(x_s[...])

            made_ref[:, slot] = x_s[...].astype(bf16).reshape(count, rows, D)
            for side in range(2):

                @pl.when(core == side)
                def _():
                    hand_out(2 + 2 * side + slot, slot)

    join(1).wait()
    join(2).start()
    for unit in (0, 1, 2, 4, 3, 5):

        @pl.when(seg != makers[unit])
        def _():
            wait_bytes(update_ref.at[group, unit], recv.at[unit])

        for side in range(3):
            onward(unit, side).start()
    join(2).wait()
    for side in range(3):
        own_rows(side).wait()
    carry.drain()
    for part, (place, unit, spot) in enumerate(parts):

        @pl.when(seg != roles[place][2])
        def _():
            gift(part).wait_send()

    for step in range(count - 1):
        wait_bytes(sq_seg.at[0], sq_send.at[step])
    for unit in range(UNITS):
        for side in range(3):
            onward(unit, side).wait()

        @pl.when(seg == makers[unit])
        def _():
            slot = 0 if unit < 2 else unit % 2
            for other in receivers(unit):
                present(unit, slot, other).wait_send()


def tail(count, dp_count, attn, done, feed_low, feed_high, dout, pieces, momenta):
    rows = D // count
    planes = count // 2
    stages = planes.bit_length() + max(0, dp_count.bit_length() - 3)
    dma = pltpu.SemaphoreType.DMA
    vmem, anywhere = pl.BlockSpec(memory_space=pltpu.VMEM), pl.BlockSpec(memory_space=pl.ANY)
    blocks = jax.ShapeDtypeStruct((GROUPS, UNITS, rows, D), bf16)
    return pl.pallas_call(
        functools.partial(tail_kernel, count),
        out_shape=[
            blocks,
            blocks,
            jax.ShapeDtypeStruct((SMALL, D), f32),
            jax.ShapeDtypeStruct((8, 128), f32),
        ],
        in_specs=[anywhere] + [vmem] * 10 + [anywhere],
        out_specs=[vmem] * 4,
        scratch_shapes=[
            pltpu.VMEM((count, 4, rows, D), bf16),
            pltpu.VMEM((UNITS, rows, D), bf16),
            pltpu.VMEM(momenta.shape, bf16),
            pltpu.VMEM((SMALL, D), f32),
            pltpu.VMEM((SMALL, D), f32),
            pltpu.VMEM((SMALL // 2, D), f32),
            pltpu.VMEM((SMALL // 4, D), f32),
            pltpu.VMEM((SMALL // 8, D), f32),
            pltpu.VMEM((stages, SMALL // 8, D), f32),
            pltpu.VMEM((count, 8, 128), f32),
            pltpu.VMEM((GROUPS, 8, 128), f32),
            pltpu.VMEM((2, rows, D), bf16),
            pltpu.VMEM((2, rows, D), bf16),
            pltpu.VMEM((count, 2, rows, D), bf16),
            pltpu.VMEM((D, D), f32),
            pltpu.VMEM((D, D), f32),
            pltpu.VMEM((D, D), f32),
            pltpu.VMEM((4, D, D), bf16),
            pltpu.VMEM((4, D, D), bf16),
            dma((1,)),
            dma((2,)),
            dma((2,)),
            dma((stages + 3,)),
            dma((stages + 3,)),
            dma((3,)),
            dma((3,)),
            dma((10,)),
            dma((count,)),
            dma((2,)),
            dma((count,)),
            dma((count,)),
            dma((3,)),
            dma((3,)),
            dma((2, count)),
            dma((UNITS,)),
            dma((3, UNITS)),
            dma((3, UNITS)),
            dma((3,)),
            dma((3,)),
        ]
        + carry_scratch("attn", rows, count, dp_count),
        compiler_params=pltpu.CompilerParams(
            collective_id=1, has_side_effects=True, vmem_limit_bytes=VMEM_LIMIT
        ),
        cost_estimate=pl.CostEstimate(flops=2 * 10**10, bytes_accessed=10**8, transcendentals=0),
        name="tail",
    )(attn.reshape(2, 2, count, rows, D), done, feed_low, feed_high, dout, *pieces, momenta)


def embed_kernel(
    count,
    frames_ref,
    mask_ref,
    in_ref,
    outer_ref,
    attn_mom_ref,
    up_mom_ref,
    down_mom_ref,
    x_ref,
    mem_ref,
    total_ref,
    owned_ref,
    got_s,
    count_s,
    mom_s,
    mom_sem,
    frame_send,
    frame_recv,
    count_send,
    count_recv,
):
    seg = lax.axis_index("seg")
    after, before = lax.rem(seg + 1, count), lax.rem(seg + count - 1, count)
    streams = frames_ref.shape[0]
    group = lax.rem(lax.axis_index("dp"), GROUPS)
    for depth in range(LAYERS):
        pltpu.make_async_copy(attn_mom_ref.at[depth, group], mom_s.at[depth], mom_sem.at[0]).start()

        @pl.when(group == FEED_UP[depth])
        def _():
            for tile in range(4):
                source = up_mom_ref.at[depth, :, pl.ds(tile * TILE, TILE)]
                pltpu.make_async_copy(source, mom_s.at[2 + tile], mom_sem.at[0]).start()

        @pl.when(group == FEED_DOWN[depth])
        def _():
            pltpu.make_async_copy(down_mom_ref.at[depth], mom_s.at[2:6], mom_sem.at[0]).start()

    tally = jnp.sum(mask_ref[...].astype(f32), 1, keepdims=True)
    count_s[seg] = jnp.broadcast_to(
        jnp.concatenate([tally, jnp.zeros((8 - streams, 1), f32)], 0), (8, 128)
    )
    greet(seg, count, (), ())
    frame_copy = remote(frames_ref, got_s, frame_send.at[0], frame_recv.at[0], {"seg": after})
    frame_copy.start()
    for step, other in enumerate(others(seg, count)):
        remote(count_s.at[seg], count_s.at[seg], count_send.at[step], count_recv.at[seg], {"seg": other}).start()
    weight, shift = in_ref[...], outer_ref[0:1, :]
    for stream in range(streams):
        x_ref[stream] = dot_nn(jnp.transpose(frames_ref[stream]), weight) + shift
    wait_bytes(mom_s, mom_sem.at[0])
    owned_ref[...] = mom_s[...].astype(bf16)
    frame_copy.wait()
    for stream in range(streams):
        mem_ref[stream] = (dot_nn(jnp.transpose(got_s[stream]), weight) + shift).astype(bf16)
    for other in others(seg, count):
        wait_bytes(count_s.at[other], count_recv.at[other])
    total_ref[...] = jnp.sum(count_s[...], 0)
    for step in range(count - 1):
        wait_bytes(count_s.at[0], count_send.at[step])


def embed(count, frames, mask, in_weight, outer_vectors, attn_mom, up_mom, down_mom):
    streams = frames.shape[0]
    rows = D // count
    dma = pltpu.SemaphoreType.DMA
    return pl.pallas_call(
        functools.partial(embed_kernel, count),
        out_shape=[
            jax.ShapeDtypeStruct((streams, SEG, D), f32),
            jax.ShapeDtypeStruct((streams, SEG, D), bf16),
            jax.ShapeDtypeStruct((8, 128), f32),
            jax.ShapeDtypeStruct((UNITS, rows, D), bf16),
        ],
        in_specs=[pl.BlockSpec(memory_space=pltpu.VMEM)] * 4 + [pl.BlockSpec(memory_space=pl.ANY)] * 3,
        out_specs=[pl.BlockSpec(memory_space=pltpu.VMEM)] * 4,
        scratch_shapes=[
            pltpu.VMEM(frames.shape, bf16),
            pltpu.VMEM((count, 8, 128), f32),
            pltpu.VMEM((UNITS, rows, D), f32),
            dma((1,)),
            dma((1,)),
            dma((1,)),
            dma((count,)),
            dma((count,)),
        ],
        compiler_params=pltpu.CompilerParams(
            collective_id=3, has_side_effects=True, vmem_limit_bytes=VMEM_LIMIT
        ),
        cost_estimate=pl.CostEstimate(flops=2 * 10**8, bytes_accessed=4 * 10**6, transcendentals=0),
        name="embed",
    )(frames, mask, in_weight, outer_vectors, attn_mom, up_mom, down_mom.reshape(LAYERS, 4, rows, D))


FEED_UP = (1, 0)
FEED_DOWN = (2, 3)
KEEP = 1.0 - 0.3 * 0.01


def finish_kernel(norm_ref, every_ref, update_ref, dout_ref, small_ref, *refs):
    (
        attn_ref,
        attn_mom_ref,
        up_ref,
        up_mom_ref,
        down_ref,
        down_mom_ref,
        out_ref,
        out_mom_ref,
        out_sec_ref,
        in_ref,
        in_mom_ref,
        in_sec_ref,
        vec_ref,
        vec_mom_ref,
        vec_sec_ref,
        outer_ref,
        outer_mom_ref,
        outer_sec_ref,
        attn_new,
        attn_mom_new,
        attn_copy_new,
        up_new,
        up_mom_new,
        up_copy_new,
        down_new,
        down_mom_new,
        down_copy_new,
        out_new,
        out_mom_new,
        out_sec_new,
        out_copy_new,
        in_new,
        in_mom_new,
        in_sec_new,
        in_copy_new,
        vec_new,
        vec_mom_new,
        vec_sec_new,
        outer_new,
        outer_mom_new,
        outer_sec_new,
        loss_new,
        norm_new,
    ) = refs
    clip = clip_of(norm_ref[0:1, 0:1])

    def muon_step(weight, momentum, grad, update, scale):
        weight = weight * KEEP - (0.3 * scale) * update.astype(f32)
        return weight, 0.5 * momentum + clip * grad.astype(f32)

    up_scale, down_scale = max(1.0, FF / D) ** 0.5, max(1.0, D / FF) ** 0.5
    for depth in range(LAYERS):
        for kind in range(4):
            weight, momentum = muon_step(
                attn_ref[depth, kind],
                attn_mom_ref[depth, kind],
                every_ref[kind, depth],
                update_ref[kind, depth],
                1.0,
            )
            attn_new[depth, kind] = weight
            attn_mom_new[depth, kind] = momentum
            attn_copy_new[depth, kind] = weight.astype(bf16)
            columns = slice(kind * TILE, (kind + 1) * TILE)
            weight, momentum = muon_step(
                up_ref[depth, :, columns],
                up_mom_ref[depth, :, columns],
                every_ref[FEED_UP[depth], 2 + kind],
                update_ref[FEED_UP[depth], 2 + kind],
                up_scale,
            )
            up_new[depth, :, columns] = weight
            up_mom_new[depth, :, columns] = momentum
            up_copy_new[depth, :, columns] = weight.astype(bf16)
            weight, momentum = muon_step(
                down_ref[depth, kind],
                down_mom_ref[depth, kind],
                every_ref[FEED_DOWN[depth], 2 + kind],
                update_ref[FEED_DOWN[depth], 2 + kind],
                down_scale,
            )
            down_new[depth, kind] = weight
            down_mom_new[depth, kind] = momentum
            down_copy_new[depth, kind] = weight.astype(bf16)
    for low in range(2):
        for right in range(2):
            columns = slice(right * D, (right + 1) * D)
            weight, moment, second = adamw(
                out_ref[low, :, columns],
                out_mom_ref[low, :, columns],
                out_sec_ref[low, :, columns],
                dout_ref[2 * right + low].astype(f32) * clip,
                0.05,
                0.01,
            )
            out_new[low, :, columns] = weight
            out_mom_new[low, :, columns] = moment
            out_sec_new[low, :, columns] = second
            out_copy_new[low, :, columns] = weight.astype(bf16)

    @pl.when(pl.program_id(0) == 0)
    def _():
        inputs = in_ref.shape[0]
        weight, moment, second = adamw(
            in_ref[...], in_mom_ref[...], in_sec_ref[...], small_ref[0:inputs, :] * clip, 0.05, 0.01
        )
        in_new[...] = weight
        in_mom_new[...] = moment
        in_sec_new[...] = second
        in_copy_new[...] = weight.astype(bf16)

        norm_new[...] = norm_ref[0:1, 0:1]
        loss_new[...] = small_ref[inputs + 37 : inputs + 38, 0:1]

        def rows_of(first, last, base):
            return small_ref[inputs + base + first : inputs + base + last, :]

        for depth in range(LAYERS):
            base = 16 * depth
            for low, high, grad in (
                (0, 2, rows_of(0, 2, base)),
                (2, 4, rows_of(0, 2, base + 8)),
                (4, 7, rows_of(2, 5, base)),
                (7, 8, rows_of(2, 3, base + 8)),
                (8, 12, rows_of(4, 8, base + 8)),
            ):
                weight, moment, second = adamw(
                    vec_ref[low:high, depth],
                    vec_mom_ref[low:high, depth],
                    vec_sec_ref[low:high, depth],
                    grad * clip,
                    0.25,
                    0.0,
                )
                vec_new[low:high, depth] = weight
                vec_mom_new[low:high, depth] = moment
                vec_sec_new[low:high, depth] = second
        for low, high, grad in ((0, 1, rows_of(5, 6, 0)), (1, 5, rows_of(1, 5, 32))):
            weight, moment, second = adamw(
                outer_ref[low:high, :], outer_mom_ref[low:high, :], outer_sec_ref[low:high, :], grad * clip, 0.25, 0.0
            )
            outer_new[low:high, :] = weight
            outer_mom_new[low:high, :] = moment
            outer_sec_new[low:high, :] = second


def finish(rows, norm, every, updates, dout, small, arrays):
    steps = rows // 16
    attn, _, up, _, down, _, out, _, _, inp, _, _, vec, _, _, outer, _, _ = arrays
    codes = out.shape[2]
    part = out.shape[1] // steps
    blocks = pl.BlockSpec((GROUPS, UNITS, 16, D), lambda i: (0, 0, i, 0))
    attn_spec = pl.BlockSpec((LAYERS, 4, 16, D), lambda i: (0, 0, i, 0))
    up_spec = pl.BlockSpec((LAYERS, 16, FF), lambda i: (0, i, 0))
    out_spec = pl.BlockSpec((2, part, codes), lambda i: (0, i, 0))
    dout_spec = pl.BlockSpec((GROUPS, part, D), lambda i: (0, i, 0))
    in_spec, vec_spec, outer_spec = whole_spec(inp.shape), whole_spec(vec.shape), whole_spec(outer.shape)

    def like(array, dtype=f32):
        return jax.ShapeDtypeStruct(array.shape, dtype)

    return pl.pallas_call(
        finish_kernel,
        grid=(steps,),
        out_shape=[like(attn), like(attn), like(attn, bf16)]
        + [like(up), like(up), like(up, bf16)]
        + [like(down), like(down), like(down, bf16)]
        + [like(out)] * 3
        + [like(out, bf16)]
        + [like(inp)] * 3
        + [like(inp, bf16)]
        + [like(vec)] * 3
        + [like(outer)] * 3
        + [jax.ShapeDtypeStruct((1, 1), f32)] * 2,
        in_specs=[whole_spec((8, 128)), blocks, blocks, dout_spec, whole_spec(small.shape)]
        + [attn_spec] * 2
        + [up_spec] * 2
        + [attn_spec] * 2
        + [out_spec] * 3
        + [in_spec] * 3
        + [vec_spec] * 3
        + [outer_spec] * 3,
        out_specs=[attn_spec] * 3
        + [up_spec] * 3
        + [attn_spec] * 3
        + [out_spec] * 4
        + [in_spec] * 4
        + [vec_spec] * 3
        + [outer_spec] * 3
        + [whole_spec((1, 1))] * 2,
        compiler_params=pltpu.CompilerParams(vmem_limit_bytes=VMEM_LIMIT),
        cost_estimate=pl.CostEstimate(flops=10**8, bytes_accessed=4 * 10**7, transcendentals=0),
        name="finish",
    )(norm, every, updates, dout, small, *arrays)


def local(
    frames,
    speech_mask,
    targets,
    in_proj,
    in_moment,
    in_second,
    out_proj,
    out_moment,
    out_second,
    layer_vectors,
    vectors_moment,
    vectors_second,
    outer_vectors,
    outer_moment,
    outer_second,
    attn_proj,
    attn_momentum,
    ff_up,
    up_momentum,
    ff_down,
    down_momentum,
    in_copy,
    out_copy,
    attn_copy,
    up_copy,
    down_copy,
):
    segment = lax.axis_index("seg")
    count, dp_count = lax.axis_size("seg"), lax.axis_size("dp")
    rows = D // count
    streams = frames.shape[0]
    stream_total = streams * dp_count
    frames_t = jnp.swapaxes(frames, 1, 2)
    bias = jnp.where(segment > 0, 0.0, -1e30).astype(f32)[None]
    hidden, memory, totals, owned = embed(
        count, frames_t, speech_mask, in_copy, outer_vectors, attn_momentum, up_momentum, down_momentum
    )
    momenta = lax.all_gather(owned, "seg", axis=0, tiled=False)
    memory = [memory] * streams
    kept = []
    for depth in range(LAYERS):
        saved, passed = None, []
        for stream in range(streams):
            saved, short = forward_layer(
                depth,
                stream,
                streams,
                bias,
                hidden,
                memory[stream],
                attn_copy,
                up_copy,
                down_copy,
                layer_vectors,
                saved,
            )
            if depth + 1 < LAYERS:
                passed.append(from_behind(short, "seg", 1))
        kept.append((hidden, saved[8], saved))
        hidden = saved[0]
        memory = passed
    grad_hidden, grad_out, head_outer = head(
        hidden, targets, speech_mask, totals, out_copy, outer_vectors, 1.0 / stream_total, momenta
    )
    vector_grads, feed_done = [], [None, None]
    carried = grad_out.reshape(GROUPS * D // 2, D)
    carried_done = []
    for depth in reversed(range(LAYERS)):
        entering, held, saved = kept[depth]
        dafter, grad_up, grad_down, feed_vec, sums = feed_back(
            depth, grad_hidden, saved[7], up_copy, down_copy, layer_vectors, count, dp_count, carried
        )
        grad_hidden, grad_attn, attn_vec, grad_in, feed_done[depth], done = attend_back(
            depth,
            bias,
            dafter,
            entering,
            held,
            saved[1:7],
            attn_copy,
            layer_vectors,
            frames_t,
            grad_up,
            grad_down,
            sums,
            count,
            dp_count,
        )
        carried_done.append(done)
        carried = grad_attn.reshape(4 * D, D)
        vector_grads = [attn_vec, feed_vec] + vector_grads
    out_done, attn_done = carried_done
    every_out = lax.all_gather(out_done, ("dp", "seg"), axis=0, tiled=True)[: GROUPS * D // 2]
    every_out = every_out.reshape(GROUPS, D // 2, D)
    updates, every, small, norm = tail(
        count,
        dp_count,
        grad_attn,
        attn_done,
        feed_done[0],
        feed_done[1],
        out_done,
        [grad_in] + vector_grads + [head_outer],
        momenta,
    )
    split = (LAYERS, 4, rows, D)
    halved = (2, D // 2, out_proj.shape[1])
    (
        attn_new,
        attn_mom,
        attn_copy_new,
        up_new,
        up_mom,
        up_copy_new,
        down_new,
        down_mom,
        down_copy_new,
        out_new,
        out_moment_new,
        out_second_new,
        out_copy_new,
        in_new,
        in_moment_new,
        in_second_new,
        in_copy_new,
        vectors_new,
        vectors_moment_new,
        vectors_second_new,
        outer_new,
        outer_moment_new,
        outer_second_new,
        loss_sum,
        norm,
    ) = finish(
        rows,
        norm,
        every,
        updates,
        every_out,
        small,
        [
            attn_proj,
            attn_momentum,
            ff_up,
            up_momentum,
            ff_down.reshape(split),
            down_momentum.reshape(split),
            out_proj.reshape(halved),
            out_moment.reshape(halved),
            out_second.reshape(halved),
            in_proj,
            in_moment,
            in_second,
            jnp.swapaxes(layer_vectors, 0, 1),
            jnp.swapaxes(vectors_moment, 0, 1),
            jnp.swapaxes(vectors_second, 0, 1),
            outer_vectors,
            outer_moment,
            outer_second,
        ],
    )
    return (
        loss_sum.reshape(()),
        norm.reshape(()),
        in_new,
        in_moment_new,
        in_second_new,
        out_new.reshape(out_proj.shape),
        out_moment_new.reshape(out_proj.shape),
        out_second_new.reshape(out_proj.shape),
        jnp.swapaxes(vectors_new, 0, 1),
        jnp.swapaxes(vectors_moment_new, 0, 1),
        jnp.swapaxes(vectors_second_new, 0, 1),
        outer_new,
        outer_moment_new,
        outer_second_new,
        attn_new,
        attn_mom,
        up_new,
        up_mom,
        down_new.reshape(ff_down.shape),
        down_mom.reshape(ff_down.shape),
        in_copy_new,
        out_copy_new.reshape(out_proj.shape),
        attn_copy_new,
        up_copy_new,
        down_copy_new.reshape(ff_down.shape),
    )


def solution(mesh):
    return jax.shard_map(
        local,
        mesh=mesh,
        in_specs=(
            P("dp", "seg", None),
            P("dp", "seg"),
            P("dp", "seg"),
            P(),
            P(),
            P(),
            P(),
            P(),
            P(),
            P(),
            P(),
            P(),
            P(),
            P(),
            P(),
            P(None, None, "seg", None),
            P(None, None, "seg", None),
            P(None, "seg", None),
            P(None, "seg", None),
            P(None, "seg", None),
            P(None, "seg", None),
            P(),
            P(),
            P(),
            P(),
            P(),
        ),
        out_specs=(
            P(),
            P(),
            P(),
            P(),
            P(),
            P(),
            P(),
            P(),
            P(),
            P(),
            P(),
            P(),
            P(),
            P(),
            P(None, None, "seg", None),
            P(None, None, "seg", None),
            P(None, "seg", None),
            P(None, "seg", None),
            P(None, "seg", None),
            P(None, "seg", None),
            P(),
            P(),
            P(None, None, "seg", None),
            P(None, "seg", None),
            P(None, "seg", None),
        ),
        check_vma=False,
    )
```

```python
import functools
import math

import jax
import jax.numpy as jnp
from jax import lax
from jax.experimental import pallas as pl
from jax.experimental.pallas import tpu as pltpu
from jax.sharding import PartitionSpec as P

D = 512
HEAD_DIM = 64
HEADS = D // HEAD_DIM
FF = 2048
LAYERS = 2
STEP = 10
SEG = 512
HALF = 256
PAIR = 2 * HEAD_DIM
TILE = 512
VMEM_LIMIT = 56 * 1024 * 1024
GELU_SCALE = math.sqrt(2.0 / math.pi)

f32 = jnp.float32
bf16 = jnp.bfloat16


def dot_nn(left, right):
    return lax.dot_general(left, right, (((1,), (0,)), ((), ())), preferred_element_type=f32)


def dot_nt(left, right):
    return lax.dot_general(left, right, (((1,), (1,)), ((), ())), preferred_element_type=f32)


def dot_tn(left, right):
    return lax.dot_general(left, right, (((0,), (0,)), ((), ())), preferred_element_type=f32)


def normalised(values):
    centred = values - jnp.mean(values, -1, keepdims=True)
    scale = lax.rsqrt(jnp.mean(centred * centred, -1, keepdims=True) + 1e-05)
    return centred * scale, scale


def norm_back(grad, gain, unit, scale):
    part = grad * gain
    mean_part = jnp.mean(part, -1, keepdims=True)
    mean_unit = jnp.mean(part * unit, -1, keepdims=True)
    return scale * (part - mean_part - unit * mean_unit)


def column_sum(values):
    return jnp.sum(values, 0, keepdims=True)


def head_masks():
    lane = lax.broadcasted_iota(jnp.int32, (1, PAIR), 1)
    return (lane < HEAD_DIM).astype(bf16), (lane >= HEAD_DIM).astype(bf16)


def pair_lanes(pair):
    return pl.ds(pl.multiple_of(pair * PAIR, PAIR), PAIR)


def forward_kernel(
    depth,
    stream,
    bias_ref,
    x_ref,
    mem_ref,
    attn_ref,
    up_ref,
    down_ref,
    vec_ref,
    *refs,
):
    (
        hid_ref,
        hid16_ref,
        keyin_out,
        q_out,
        k_out,
        v_out,
        lse_ref,
        mixed_ref,
        after_ref,
        kept_out,
        act_s,
        lse_s,
        up_s,
        down_s,
        keyin_ref,
        q_ref,
        k_ref,
        v_ref,
        in_sem,
        out_sem,
    ) = refs[-20:]
    weights_in = (
        pltpu.make_async_copy(up_ref.at[depth], up_s, in_sem.at[0]),
        pltpu.make_async_copy(down_ref.at[depth], down_s, in_sem.at[1]),
    )
    for copy in weights_in:
        copy.start()
    saved_out = [
        pltpu.make_async_copy(source, target.at[stream], out_sem.at[place])
        for place, (source, target) in enumerate(
            ((keyin_ref, keyin_out), (q_ref, q_out), (k_ref, k_out), (v_ref, v_out))
        )
    ]
    kept_out[...] = mem_ref[...]
    x = x_ref[...]
    own_unit, _ = normalised(x)
    gain, shift = vec_ref[0:1, :], vec_ref[1:2, :]
    normed = (own_unit * gain + shift).astype(bf16)
    mem_unit, _ = normalised(mem_ref[...].astype(f32))
    mem_normed = (mem_unit * gain + shift).astype(bf16)
    keyin_ref[0:SEG, :] = mem_normed
    keyin_ref[SEG:, :] = normed
    q_ref[...] = (dot_nn(normed, attn_ref[0]) + vec_ref[4:5, :]).astype(bf16) * jnp.asarray(HEAD_DIM**-0.5, bf16)
    k_ref[0:SEG, :] = dot_nn(mem_normed, attn_ref[1]).astype(bf16)
    k_ref[SEG:, :] = dot_nn(normed, attn_ref[1]).astype(bf16)
    v_ref[0:SEG, :] = (dot_nn(mem_normed, attn_ref[2]) + vec_ref[5:6, :]).astype(bf16)
    v_ref[SEG:, :] = (dot_nn(normed, attn_ref[2]) + vec_ref[5:6, :]).astype(bf16)
    for copy in saved_out:
        copy.start()
    first, second = head_masks()
    memory_bias = bias_ref[0]
    lane = lax.broadcasted_iota(jnp.int32, (HALF, PAIR), 1)
    query_pos = lax.broadcasted_iota(jnp.int32, (2 * HALF, HALF), 0) % HALF
    key_pos = lax.broadcasted_iota(jnp.int32, (2 * HALF, HALF), 1)
    diagonal = key_pos <= query_pos
    lse_s[...] = jnp.zeros_like(lse_s)

    def pair_body(pair, carry):
        lanes = pair_lanes(pair)
        blocks = []
        for block in range(2):
            rows = slice(block * HALF, (block + 1) * HALF)
            q_pair = q_ref[rows, lanes]
            q_both = jnp.concatenate([q_pair * first, q_pair * second], 0)
            spans = [(0, SEG)]
            if block:
                spans.append((SEG, SEG + HALF))
            spans.append((SEG + block * HALF, SEG + (block + 1) * HALF))
            scores = [dot_nt(q_both, k_ref[low:high, lanes]) for low, high in spans]
            scores[-1] = jnp.where(diagonal, scores[-1], -1e30)
            blocks.append((rows, spans, scores))
        results = []
        for rows, spans, scores in blocks:
            peaks = [jnp.max(part, -1, keepdims=True) for part in scores]
            peaks[0] = peaks[0] + memory_bias
            most = functools.reduce(jnp.maximum, peaks)
            weights = [
                jnp.exp(part - (most if place else most - memory_bias)) for place, part in enumerate(scores)
            ]
            total = functools.reduce(jnp.add, [jnp.sum(part, -1, keepdims=True) for part in weights])
            mixed = functools.reduce(
                jnp.add,
                [
                    dot_nn(part.astype(bf16), v_ref[low:high, lanes])
                    for part, (low, high) in zip(weights, spans)
                ],
            )
            results.append((rows, mixed / total, most + jnp.log(total)))
        for rows, mixed, lse in results:
            mixed_ref[rows, lanes] = jnp.where(lane < HEAD_DIM, mixed[:HALF], mixed[HALF:]).astype(bf16)
            kept = jnp.where(lane == 2 * pair, lse[:HALF], lse_s[rows, :])
            lse_s[rows, :] = jnp.where(lane == 2 * pair + 1, lse[HALF:], kept)
        return carry

    lax.fori_loop(0, HEADS // 2, pair_body, 0)
    lse_ref[...] = jnp.transpose(lse_s[...])[0:HEADS, :]
    after = x + (dot_nn(mixed_ref[...], attn_ref[3]) + vec_ref[6:7, :])
    after_ref[...] = after
    unit, _ = normalised(after)
    normed_two = (unit * vec_ref[2:3, :] + vec_ref[3:4, :]).astype(bf16)
    for copy in weights_in:
        copy.wait()

    def inner_of(tile):
        columns = slice(tile * TILE, (tile + 1) * TILE)
        return dot_nn(normed_two, up_s[:, columns]) + vec_ref[8 + tile : 9 + tile, :]

    ahead = inner_of(0)
    for tile in range(FF // TILE):
        columns = slice(tile * TILE, (tile + 1) * TILE)
        inner = ahead
        if tile + 1 < FF // TILE:
            ahead = inner_of(tile + 1)
        act_s[:, columns] = (
            0.5 * inner * (1.0 + jnp.tanh(GELU_SCALE * (inner + 0.044715 * inner * inner * inner)))
        ).astype(bf16)
    hidden = after + (dot_nn(act_s[...], down_s[...]) + vec_ref[7:8, :])
    hid_ref[...] = hidden
    hid16_ref[...] = hidden.astype(bf16)
    for copy in saved_out:
        copy.wait()


SAVED = (
    ((SEG, D), f32),
    ((2 * SEG, D), bf16),
    ((SEG, D), bf16),
    ((2 * SEG, D), bf16),
    ((2 * SEG, D), bf16),
    ((HEADS, SEG), f32),
    ((SEG, D), bf16),
    ((SEG, D), f32),
    ((SEG, D), bf16),
)


def whole_spec(shape):
    return pl.BlockSpec(shape, lambda *_: (0,) * len(shape))


def stream_spec(shape, stream=None):
    zeros = (0,) * len(shape)
    if stream is None:
        return pl.BlockSpec((None,) + shape, lambda i: (i,) + zeros)
    return pl.BlockSpec((None,) + shape, lambda i: (stream,) + zeros)


def layer_spec(shape, depth):
    zeros = (0,) * len(shape)
    return pl.BlockSpec((None,) + shape, lambda *_: (depth,) + zeros)


def forward_layer(depth, stream, streams, bias, hidden, memory, attn, upper, lower, vectors, earlier):
    saved_shapes = [jax.ShapeDtypeStruct((streams,) + shape, dtype) for shape, dtype in SAVED]
    saved_specs = [stream_spec(shape, stream) for shape, dtype in SAVED]
    out_shape = [saved_shapes[0], jax.ShapeDtypeStruct((SEG, D), bf16)] + saved_shapes[1:]
    out_specs = [saved_specs[0], whole_spec((SEG, D))] + saved_specs[1:]
    for place in (2, 3, 4, 5):
        out_specs[place] = pl.BlockSpec(memory_space=pl.ANY)
    operands = [bias, hidden, memory, attn, upper, lower, vectors]
    in_specs = [
        pl.BlockSpec(memory_space=pltpu.SMEM),
        stream_spec((SEG, D), stream),
        stream_spec((SEG, D), stream) if memory.ndim == 3 else whole_spec((SEG, D)),
        layer_spec(attn.shape[1:], depth),
        pl.BlockSpec(memory_space=pl.ANY),
        pl.BlockSpec(memory_space=pl.ANY),
        layer_spec(vectors.shape[1:], depth),
    ]
    aliases = {}
    if earlier is not None:
        for place, array in enumerate(earlier):
            aliases[len(operands)] = place if place == 0 else place + 1
            operands.append(array)
            in_specs.append(pl.BlockSpec(memory_space=pl.ANY))
    out = pl.pallas_call(
        functools.partial(forward_kernel, depth, stream),
        grid=(1,),
        out_shape=out_shape,
        in_specs=in_specs,
        out_specs=out_specs,
        scratch_shapes=[
            pltpu.VMEM((SEG, FF), bf16),
            pltpu.VMEM((SEG, PAIR), f32),
            pltpu.VMEM((D, FF), bf16),
            pltpu.VMEM((FF, D), bf16),
            pltpu.VMEM((2 * SEG, D), bf16),
            pltpu.VMEM((SEG, D), bf16),
            pltpu.VMEM((2 * SEG, D), bf16),
            pltpu.VMEM((2 * SEG, D), bf16),
            pltpu.SemaphoreType.DMA((2,)),
            pltpu.SemaphoreType.DMA((4,)),
        ],
        input_output_aliases=aliases,
        compiler_params=pltpu.CompilerParams(vmem_limit_bytes=VMEM_LIMIT),
        cost_estimate=pl.CostEstimate(flops=10**10, bytes_accessed=2 * 10**7, transcendentals=10**7),
        name="layer_forward",
    )(*operands)
    return [out[0]] + list(out[2:]), out[1]


def head_kernel(scale, x_ref, target_ref, mask_ref, total_ref, out_ref, outer_ref, mom_ref, g_ref, dout_ref, douter_ref, acc_s):
    step = pl.program_id(0)

    @pl.when(step == 0)
    def _():
        acc_s[...] = jnp.zeros_like(acc_s)
        douter_ref[...] = jnp.zeros_like(douter_ref)

    unit, rscale = normalised(x_ref[...])
    gain = outer_ref[1:2, :]
    normed = (unit * gain + outer_ref[2:3, :]).astype(bf16)
    shift = jnp.concatenate([outer_ref[3:4, :], outer_ref[4:5, :]], 1)
    logits = dot_nn(normed, out_ref[...]) + shift
    most = jnp.max(logits, -1, keepdims=True)
    powers = jnp.exp(logits - most)
    total = jnp.sum(powers, -1, keepdims=True)
    target_row = target_ref[pl.ds(step, 1), :].astype(f32)
    weight_row = mask_ref[pl.ds(step, 1), :].astype(f32) * (1.0 / total_ref[pl.ds(step, 1), 0:1])
    columns = jnp.transpose(jnp.concatenate([target_row, weight_row, jnp.zeros((6, SEG), f32)], 0))
    target, weight = columns[:, 0:1].astype(jnp.int32), columns[:, 1:2]
    chosen = lax.broadcasted_iota(jnp.int32, logits.shape, 1) == target
    picked = jnp.sum(jnp.where(chosen, logits, 0.0), -1, keepdims=True)
    loss = jnp.sum(weight * (most + jnp.log(total) - picked), 0, keepdims=True)
    spread = weight * scale
    dlogits = (powers * (spread / total) - jnp.where(chosen, spread, 0.0)).astype(bf16)
    acc_s[...] += dot_nn(jnp.transpose(normed), dlogits)
    bias_grad = column_sum(dlogits.astype(f32))
    dnormed = dot_nt(dlogits, out_ref[...])
    g_ref[...] = norm_back(dnormed, gain, unit, rscale)
    douter_ref[1:2, :] += column_sum(dnormed * unit)
    douter_ref[2:3, :] += column_sum(dnormed)
    douter_ref[3:4, :] += bias_grad[:, :D]
    douter_ref[4:5, :] += bias_grad[:, D:]
    douter_ref[5:6, :] += jnp.broadcast_to(loss, (1, D))

    @pl.when(step == pl.num_programs(0) - 1)
    def _():
        half = D // 2
        for right in range(2):
            for low in range(2):
                dout_ref[right, low] = acc_s[
                    low * half : (low + 1) * half, right * D : (right + 1) * D
                ]


def head(hidden, targets, mask, totals, out_weight, outer_vectors, scale, momenta):
    streams = hidden.shape[0]
    codes = out_weight.shape[1]
    return pl.pallas_call(
        functools.partial(head_kernel, scale),
        grid=(streams,),
        out_shape=[
            jax.ShapeDtypeStruct((streams, SEG, D), f32),
            jax.ShapeDtypeStruct((2, 2, D // 2, D), f32),
            jax.ShapeDtypeStruct((8, D), f32),
        ],
        in_specs=[
            stream_spec((SEG, D)),
            whole_spec((streams, SEG)),
            whole_spec((streams, SEG)),
            whole_spec((8, 128)),
            whole_spec((D, codes)),
            whole_spec(outer_vectors.shape),
            pl.BlockSpec(memory_space=pl.ANY),
        ],
        out_specs=[stream_spec((SEG, D)), whole_spec((2, 2, D // 2, D)), whole_spec((8, D))],
        scratch_shapes=[pltpu.VMEM((D, codes), f32)],
        compiler_params=pltpu.CompilerParams(vmem_limit_bytes=VMEM_LIMIT),
        cost_estimate=pl.CostEstimate(flops=33 * 10**8, bytes_accessed=10**7, transcendentals=10**6),
        name="head",
    )(hidden, targets, mask, totals, out_weight, outer_vectors, momenta)


def feed_back_kernel(streams, g_ref, after_ref, up_ref, down_ref, vec_ref, *refs):
    step = pl.program_id(0)
    grad_ref, dafter_ref, dup_ref, ddown_ref, dvec_ref, done_ref, normed_s, branch_s, act_s, inner_s = refs[:10]
    carry = AttnCarry(grad_ref, refs[10 : 10 + CARRY_REFS], refs[10 + CARRY_REFS :], done_ref)
    planes = carry.planes
    early, late = range(planes // 2), range(planes // 2, planes)
    beats = [
        [("b", place) for place in range(planes)],
        [("m", place) for place in early],
        [("m", place) for place in late],
        [("e", place) for place in early],
        [("e", place) for place in late],
    ]

    @pl.when(step == 0)
    def _():
        hail(carry.targets[:3])
        carry.load_all()
        dvec_ref[...] = jnp.zeros_like(dvec_ref)

    rows = pl.ds(pl.multiple_of(step * SEG, SEG), SEG)
    grad = g_ref[...]
    branch = grad.astype(bf16)
    dvec_ref[2:3, :] += column_sum(branch.astype(f32))
    unit, scale = normalised(after_ref[...])
    gain = vec_ref[2:3, :]
    normed = (unit * gain + vec_ref[3:4, :]).astype(bf16)
    normed_s[:, rows] = jnp.transpose(normed)
    branch_s[:, rows] = jnp.transpose(branch)

    @pl.when(step == 0)
    def _():
        meet(carry.targets[:3])
        carry.send_all()

    def products(tile):
        columns = slice(tile * TILE, (tile + 1) * TILE)
        inner = dot_nn(normed, up_ref[:, columns]) + vec_ref[8 + tile : 9 + tile, :]
        return inner, dot_nt(branch, down_ref[columns, :])

    ahead = products(0)
    for tile in range(FF // TILE):
        columns = slice(tile * TILE, (tile + 1) * TILE)
        inner, dact = ahead
        if tile + 1 < FF // TILE:
            ahead = products(tile + 1)
        square = inner * inner
        bent = jnp.tanh(inner * (GELU_SCALE + (GELU_SCALE * 0.044715) * square))
        half = 0.5 * (1.0 + bent)
        act_s[rows, columns] = (inner * half).astype(bf16)
        slope = half + inner * (half * (1.0 - bent)) * (GELU_SCALE + (GELU_SCALE * 0.134145) * square)
        dinner = (dact * slope).astype(bf16)
        inner_s[rows, columns] = dinner
        dvec_ref[4 + tile : 5 + tile, :] += column_sum(dinner.astype(f32))

    @pl.when(step == 0)
    def _():
        carry.run(beats[0])

    @pl.when(step == streams - 1)
    def _():
        carry.run(beats[1])

    dnormed = dot_nt(inner_s[rows, :], up_ref[...])
    dvec_ref[0:1, :] += column_sum(dnormed * unit)
    dvec_ref[1:2, :] += column_sum(dnormed)
    dafter_ref[...] = grad + norm_back(dnormed, gain, unit, scale)

    @pl.when(step == streams - 1)
    def _():
        carry.run(beats[2])
        for tile in range(FF // TILE):
            columns = slice(tile * TILE, (tile + 1) * TILE)
            dup_ref[tile] = dot_nn(normed_s[...], inner_s[:, columns]).astype(bf16)
        carry.run(beats[3])
        for tile in range(FF // TILE):
            columns = slice(tile * TILE, (tile + 1) * TILE)
            ddown_ref[columns, :] = jnp.transpose(dot_nn(branch_s[...], act_s[:, columns]).astype(bf16))
        carry.run(beats[4])
        carry.drain()


def feed_back(depth, grad, after, upper, lower, vectors, count, dp_count, attn_grad):
    streams = grad.shape[0]
    rows = attn_grad.shape[0] // (GROUPS * count)
    in_specs = [
        stream_spec((SEG, D)),
        stream_spec((SEG, D)),
        layer_spec(upper.shape[1:], depth),
        layer_spec(lower.shape[1:], depth),
        layer_spec(vectors.shape[1:], depth),
    ]
    out_shape = [
        jax.ShapeDtypeStruct((streams, SEG, D), f32),
        jax.ShapeDtypeStruct((FF // TILE, D, TILE), bf16),
        jax.ShapeDtypeStruct((FF, D), bf16),
        jax.ShapeDtypeStruct((8, D), f32),
    ]
    out_specs = [
        stream_spec((SEG, D)),
        whole_spec((FF // TILE, D, TILE)),
        whole_spec((FF, D)),
        whole_spec((8, D)),
    ]
    scratch = [
        pltpu.VMEM((D, streams * SEG), bf16),
        pltpu.VMEM((D, streams * SEG), bf16),
        pltpu.VMEM((streams * SEG, FF), bf16),
        pltpu.VMEM((streams * SEG, FF), bf16),
    ]
    operands = [grad, after, upper, lower, vectors]
    in_specs.append(pl.BlockSpec(memory_space=pl.ANY))
    operands.append(attn_grad.reshape(2, 2, count, rows, D))
    out_shape.append(jax.ShapeDtypeStruct((count // 2, rows, D), attn_grad.dtype))
    out_specs.append(whole_spec((count // 2, rows, D)))
    scratch = scratch + carry_scratch("attn", rows, count, dp_count, attn_grad.dtype)
    params = {"collective_id": 6 + depth, "has_side_effects": True}
    return pl.pallas_call(
        functools.partial(feed_back_kernel, streams),
        grid=(streams,),
        out_shape=out_shape,
        in_specs=in_specs,
        out_specs=out_specs,
        scratch_shapes=scratch,
        compiler_params=pltpu.CompilerParams(vmem_limit_bytes=VMEM_LIMIT, **params),
        cost_estimate=pl.CostEstimate(flops=11 * 10**9, bytes_accessed=2 * 10**7, transcendentals=2 * 10**6),
        name="feed_back",
    )(*operands)


def attend_back_kernel(
    streams,
    depth,
    bias_ref,
    dafter_ref,
    x_ref,
    mem_ref,
    keyin_ref,
    q_ref,
    k_ref,
    v_ref,
    lse_ref,
    mixed_ref,
    attn_ref,
    vec_ref,
    frames_ref,
    dup_ref,
    ddown_ref,
    sums_ref,
    dx_ref,
    dattn_ref,
    dvec_ref,
    din_ref,
    done_ref,
    along_ref,
    attn_s,
    dmixed_s,
    dq_s,
    dk_s,
    dv_s,
    ds_s,
    delta_s,
    *refs,
):
    step = pl.program_id(0)
    pairs = HEADS // 2
    split = CARRY_REFS + 1 + CARRY_SEMS
    carry = FeedCarry(depth, dup_ref, ddown_ref, refs[: CARRY_REFS + 1], refs[CARRY_REFS + 1 : split])
    along = ZCarry(refs[split : split + Z_REFS], refs[split + Z_REFS :])
    plans, (free, bound) = carry.plans(), along.plans()

    @pl.when(step == 0)
    def _():
        hail(carry.targets)
        carry.load_all()
        along.sums[...] = sums_ref[...]
        attn_s[...] = jnp.zeros_like(attn_s)
        dvec_ref[...] = jnp.zeros_like(dvec_ref)
        din_ref[...] = jnp.zeros_like(din_ref)

    dafter = dafter_ref[...]
    branch = dafter.astype(bf16)
    dvec_ref[4:5, :] += column_sum(branch.astype(f32))
    dmixed = dot_nt(branch, attn_ref[3]).astype(bf16)
    dmixed_s[...] = dmixed
    attn_s[3] += dot_nn(jnp.transpose(mixed_ref[...]), branch)
    product = dmixed.astype(f32) * mixed_ref[...].astype(f32)
    high = product.astype(bf16)
    rest = (product - high.astype(f32)).astype(bf16)
    owner = lax.broadcasted_iota(jnp.int32, (HEADS, D), 1) // HEAD_DIM
    pick = (owner == lax.broadcasted_iota(jnp.int32, (HEADS, D), 0)).astype(bf16)
    delta_s[...] = dot_nt(pick, high) + dot_nt(pick, rest)
    first, second = head_masks()
    memory_bias = bias_ref[0]
    key_pos = lax.broadcasted_iota(jnp.int32, (HALF, 2 * HALF), 0)
    query_pos = lax.broadcasted_iota(jnp.int32, (HALF, 2 * HALF), 1) % HALF
    diagonal = key_pos <= query_pos
    head_row = lax.broadcasted_iota(jnp.int32, (PAIR, HALF), 0)

    @pl.when(step == 0)
    def _():
        meet(carry.targets)
        carry.send_all()
        along.run(free)

    @pl.when(step == 1)
    def _():
        carry.run(plans[-1])

    def pair_body(pair, state):
        lanes = pair_lanes(pair)
        q_pair, do_pair = q_ref[:, lanes], dmixed_s[:, lanes]

        def spread(value):
            return jnp.concatenate(
                [value[:HALF] * first, value[:HALF] * second, value[HALF:] * first, value[HALF:] * second], 0
            )

        q_all, do_all = spread(q_pair), spread(do_pair)

        def rows_of(ref):
            one, two = ref[pl.ds(2 * pair, 1), :], ref[pl.ds(2 * pair + 1, 1), :]
            return jnp.concatenate([one[:, :HALF], two[:, :HALF], one[:, HALF:], two[:, HALF:]], 1)

        lse_all, delta_all = rows_of(lse_ref), rows_of(delta_s)
        starts = (0, 0, 0, 2 * HALF)

        def products(block):
            keys = slice(block * HALF, (block + 1) * HALF)
            scores = dot_nt(k_ref[keys, lanes], q_all[starts[block] :])
            return scores, dot_nt(v_ref[keys, lanes], do_all[starts[block] :])

        ahead = products(0)
        for block in range(4):
            scores, dweights = ahead
            if block < 3:
                ahead = products(block + 1)
            keys = slice(block * HALF, (block + 1) * HALF)
            start = starts[block]
            shift = lse_all - memory_bias if block < 2 else lse_all[:, start:]
            weights = jnp.exp(scores - shift)
            if block == 2:
                weights = jnp.concatenate(
                    [jnp.where(diagonal, weights[:, : 2 * HALF], 0.0), weights[:, 2 * HALF :]], 1
                )
            if block == 3:
                weights = jnp.where(diagonal, weights, 0.0)
            dscores = (weights * (dweights - delta_all[:, start:])).astype(bf16)
            dv_s[keys, lanes] = dot_nn(weights.astype(bf16), do_all[start:]).astype(bf16)
            dk_s[keys, lanes] = dot_nn(dscores, q_all[start:]).astype(bf16)
            ds_s[keys, start:] = dscores
        k_t = jnp.transpose(k_ref[:, lanes])
        for block in range(2):
            seen = SEG + (block + 1) * HALF
            grads = dot_nn(k_t[:, :seen], ds_s[:seen, block * 2 * HALF : (block + 1) * 2 * HALF])
            grads = jnp.where(head_row < HEAD_DIM, grads[:, :HALF], grads[:, HALF:])
            dq_s[block * HALF : (block + 1) * HALF, lanes] = (
                jnp.transpose(grads) * (HEAD_DIM**-0.5)
            ).astype(bf16)
        for time, acts in enumerate(plans[:-1]):
            if acts:

                @pl.when(pairs * step + pair == time)
                def _():
                    carry.run(acts)
                    if time == 3:
                        along.run(bound)

        return state

    lax.fori_loop(0, pairs, pair_body, 0)
    dq, dk, dv = dq_s[...], dk_s[...], dv_s[...]
    keyin_t = jnp.transpose(keyin_ref[...])
    attn_s[0] += dot_nn(keyin_t[:, SEG:], dq)
    attn_s[1] += dot_nn(keyin_t, dk)
    attn_s[2] += dot_nn(keyin_t, dv)
    dvec_ref[2:3, :] += column_sum(dq.astype(f32))
    dvec_ref[3:4, :] += column_sum(dv.astype(f32))
    dkeyin = dot_nt(dk, attn_ref[1]) + dot_nt(dv, attn_ref[2])
    dmem = dkeyin[:SEG]
    down = dkeyin[SEG:] + dot_nt(dq, attn_ref[0])
    gain = vec_ref[0:1, :]
    unit, scale = normalised(x_ref[...])
    mem_unit, _ = normalised(mem_ref[...].astype(f32))
    dvec_ref[0:1, :] += column_sum(down * unit + dmem * mem_unit)
    dvec_ref[1:2, :] += column_sum(down + dmem)
    dx = dafter + norm_back(down, gain, unit, scale)
    dx_ref[...] = dx
    if depth == 0:
        dx_high = dx.astype(bf16)
        dx_rest = (dx - dx_high.astype(f32)).astype(bf16)
        din_ref[...] += dot_nn(frames_ref[...], dx_high) + dot_nn(frames_ref[...], dx_rest)
        dvec_ref[5:6, :] += column_sum(dx)

    @pl.when(step == pl.num_programs(0) - 1)
    def _():
        dattn_ref[...] = attn_s[...].astype(bf16)
        carry.finish(done_ref)
        along.finish(along_ref)


def attend_back(depth, bias, dafter, x, memory, saved, attn, vectors, frames, up_grad, down_grad, sums, count, dp_count):
    streams = dafter.shape[0]
    keyin, q, k, v, lse, mixed = saved
    inputs = frames.shape[1]
    rows = D // count
    up_grad, down_grad = up_grad.reshape(4, count, rows, D), down_grad.reshape(count, 4, rows, D)
    return pl.pallas_call(
        functools.partial(attend_back_kernel, streams, depth),
        grid=(streams,),
        out_shape=[
            jax.ShapeDtypeStruct((streams, SEG, D), f32),
            jax.ShapeDtypeStruct((4, D, D), bf16),
            jax.ShapeDtypeStruct((8, D), f32),
            jax.ShapeDtypeStruct((inputs, D), f32),
            jax.ShapeDtypeStruct((2, rows, D), bf16),
            jax.ShapeDtypeStruct(sums.shape[1:], bf16),
        ],
        in_specs=[
            pl.BlockSpec(memory_space=pltpu.SMEM),
            stream_spec((SEG, D)),
            stream_spec((SEG, D)),
            stream_spec((SEG, D)),
            stream_spec((2 * SEG, D)),
            stream_spec((SEG, D)),
            stream_spec((2 * SEG, D)),
            stream_spec((2 * SEG, D)),
            stream_spec((HEADS, SEG)),
            stream_spec((SEG, D)),
            layer_spec(attn.shape[1:], depth),
            layer_spec(vectors.shape[1:], depth),
            stream_spec((inputs, SEG)),
            pl.BlockSpec(memory_space=pl.ANY),
            pl.BlockSpec(memory_space=pl.ANY),
            whole_spec(sums.shape),
        ],
        out_specs=[
            stream_spec((SEG, D)),
            whole_spec((4, D, D)),
            whole_spec((8, D)),
            whole_spec((inputs, D)),
            whole_spec((2, rows, D)),
            whole_spec(sums.shape[1:]),
        ],
        scratch_shapes=[
            pltpu.VMEM((4, D, D), f32),
            pltpu.VMEM((SEG, D), bf16),
            pltpu.VMEM((SEG, D), bf16),
            pltpu.VMEM((2 * SEG, D), bf16),
            pltpu.VMEM((2 * SEG, D), bf16),
            pltpu.VMEM((2 * SEG, 2 * SEG), bf16),
            pltpu.VMEM((HEADS, SEG), f32),
        ]
        + carry_scratch("feed", rows, count, dp_count)
        + z_scratch(sums.shape[1], count, dp_count, sums.dtype),
        compiler_params=pltpu.CompilerParams(
            collective_id=4 + depth, has_side_effects=True, vmem_limit_bytes=VMEM_LIMIT
        ),
        cost_estimate=pl.CostEstimate(flops=3 * 10**10, bytes_accessed=2 * 10**7, transcendentals=10**7),
        name="attend_back",
    )(bias, dafter, x, memory, keyin, q, k, v, lse, mixed, attn, vectors, frames, up_grad, down_grad, sums)


def from_behind(value, axis, steps):
    count = lax.axis_size(axis)
    leading, last = (max(0, -steps), min(count, count - steps))
    return lax.ppermute(value, axis, [(source, source + steps) for source in range(leading, last)])


def adamw(weight, moment, second, grad, rate, decay):
    moment = 0.5 * moment + 0.5 * grad
    second = 0.99 * second + 0.01 * grad * grad
    fixed_moment = moment / (1.0 - 0.5**STEP)
    fixed_second = second / (1.0 - 0.99**STEP)
    weight = weight * (1.0 - rate * decay) - rate * fixed_moment / (jnp.sqrt(fixed_second) + 1e-08)
    return (weight, moment, second)


GROUPS = 4
UNITS = 6
SMALL = 128


def peers():
    count = {"seg": lax.axis_size("seg"), "dp": lax.axis_size("dp")}
    seg, dp = lax.axis_index("seg"), lax.axis_index("dp")
    core, x, y = seg % 2, dp % 2, (dp // 2) % 2
    across_core = {"seg": seg + 1 - 2 * core}
    across_x = {"dp": dp + 1 - 2 * x}
    across_y = {"dp": dp + 2 - 4 * y}
    across_both = {"dp": dp + 3 - 2 * x - 4 * y}
    far = []
    step = GROUPS
    while step < count["dp"]:
        far.append({"dp": dp + step - 2 * step * ((dp // step) % 2)})
        step *= 2
    return seg, dp, core, x, y, across_core, (across_x, across_y, across_both), far


def others(seg, count):
    return [lax.rem(seg + step, count) for step in range(1, count)]


def hail(targets):
    barrier = pltpu.get_barrier_semaphore()
    for target in targets:
        pl.semaphore_signal(barrier, inc=1, device_id=target, device_id_type=pl.DeviceIdType.MESH)


def meet(targets):
    pl.semaphore_wait(pltpu.get_barrier_semaphore(), len(targets))


def greet(seg, count, near, far):
    targets = [{"seg": other} for other in others(seg, count)] + list(near) + list(far)
    hail(targets)
    meet(targets)


def remote(source, target, send, recv, device):
    return pltpu.make_async_remote_copy(
        src_ref=source,
        dst_ref=target,
        send_sem=send,
        recv_sem=recv,
        device_id=device,
        device_id_type=pl.DeviceIdType.MESH,
    )


def wait_bytes(ref, sem):
    pltpu.make_async_copy(ref, ref, sem).wait()


def plus(left, right):
    return (left.astype(f32) + right.astype(f32)).astype(left.dtype)


def owners(count):
    low, high = count // 4 - 1, count // 4
    return (
        (0, 1, 0, 0),
        (1, 1, count - 2, 0),
        (2, 2, 2 * low, 0),
        (4, 2, 2 * low + 1, 2),
        (2, 2, 2 * high, 0),
        (4, 2, 2 * high + 1, 2),
    )


def lowest_bit(mask, planes):
    bit = 1
    while bit < planes and not mask & bit:
        bit *= 2
    return bit


class Carry:
    def __init__(self, refs, sems):
        self.mine, self.got0, self.got1, self.got2, self.got3, self.goth = refs
        (
            self.load,
            self.send0,
            self.recv0,
            self.send1,
            self.recv1,
            self.send2,
            self.recv2,
            self.send3,
            self.recv3,
            self.sendh,
            self.recvh,
        ) = sems
        self.settle(self.mine.shape[0])

    def settle(self, planes):
        self.seg, self.dp, self.core, self.x, self.y, self.across_core, near, self.far = peers()
        self.across_x, self.across_y, _ = near
        self.planes = planes
        self.plane = self.seg // 2
        self.targets = [self.across_core, self.across_x, self.across_y] + self.far
        bit = 1
        while bit < planes:
            self.targets.append({"seg": 2 * self.toggled(bit) + self.core})
            bit *= 2
        self.order = list(reversed(range(planes)))

    def toggled(self, mask):
        place, bit = self.plane, 1
        while bit <= mask:
            if mask & bit:
                place = place + bit - 2 * bit * ((self.plane // bit) % 2)
            bit *= 2
        return place

    def load_all(self):
        for step in range(self.planes):
            for source, place in self.pieces(2 * self.toggled(self.order[step]) + self.core):
                pltpu.make_async_copy(source, self.mine.at[(step,) + place], self.load.at[step]).start()

    def send_all(self):
        for step in range(self.planes):
            for source, place in self.pieces(2 * self.toggled(self.order[step]) + 1 - self.core):
                remote(
                    source, self.got0.at[(step,) + place], self.send0.at[step], self.recv0.at[step], self.across_core
                ).start()

    def begin(self, step):
        wait_bytes(self.mine.at[step], self.load.at[step])
        wait_bytes(self.got0.at[step], self.recv0.at[step])
        for place in range(2):
            self.mine[step, place] = plus(self.mine[step, place], self.got0[step, place])
        for copy in self.first(step):
            copy.start()

    def across(self, place, step):
        return remote(
            self.held(step),
            self.goth.at[place, step],
            self.sendh.at[place, step],
            self.recvh.at[place, step],
            self.far[place],
        )

    def third(self, step):
        mask = self.order[step]
        return remote(
            self.held(step),
            self.got3.at[mask],
            self.send3.at[step],
            self.recv3.at[mask],
            {"seg": 2 * self.toggled(lowest_bit(mask, self.planes)) + self.core},
        )

    def onward(self, step):
        held = self.held(step)
        for place in range(len(self.far)):
            copy = self.across(place, step)
            copy.start()
            copy.wait()
            held[...] = plus(held[...], self.goth[place, step])
        mask = self.order[step]
        if mask:
            self.gathered(mask, held)
            self.third(step).start()

    def gathered(self, mask, held):
        value, bit = held[...].astype(f32), 1
        while bit < lowest_bit(mask, self.planes):
            wait_bytes(self.got3.at[mask + bit], self.recv3.at[mask + bit])
            value = value + self.got3[mask + bit].astype(f32)
            bit *= 2
        held[...] = value.astype(held.dtype)

    def total(self):
        held = self.held(self.planes - 1)
        self.gathered(0, held)
        return held[...]

    def run(self, acts):
        for kind, step in acts:
            getattr(self, {"b": "begin", "m": "middle", "e": "end", "z": "onward"}[kind])(step)


class ZCarry(Carry):
    def __init__(self, refs, sems):
        self.sums, self.got3, self.goth = refs
        self.send3, self.recv3, self.sendh, self.recvh = sems
        self.settle(self.sums.shape[0])

    def held(self, step):
        return self.sums.at[step]

    def plans(self):
        free = [("z", step) for step in range(self.planes) if self.order[step] % 2]
        bound = [("z", step) for step in range(self.planes) if self.order[step] and not self.order[step] % 2]
        return free, bound

    def finish(self, out_ref):
        out_ref[...] = self.total().astype(out_ref.dtype)
        for step in range(self.planes - 1):
            self.third(step).wait_send()


class AttnCarry(Carry):
    def __init__(self, source, refs, sems, sums=None):
        super().__init__(refs, sems)
        self.source, self.sums = source, sums

    def pieces(self, row):
        return ((self.source.at[:, :, row], ()),)

    def held(self, step):
        return self.mine.at[step, self.y, self.x]

    def first(self, step):
        half = self.mine.shape[3] // 2
        return (
            remote(
                self.mine.at[step, :, 1 - self.x, 0:half],
                self.got1.at[step, 0],
                self.send1.at[step, 0],
                self.recv1.at[step, 0],
                self.across_x,
            ),
            remote(
                self.mine.at[step, 1 - self.y, :, half:],
                self.got1.at[step, 1],
                self.send1.at[step, 1],
                self.recv1.at[step, 1],
                self.across_y,
            ),
        )

    def second(self, step):
        half = self.mine.shape[3] // 2
        return (
            remote(
                self.mine.at[step, 1 - self.y, self.x, 0:half],
                self.got2.at[step, 0],
                self.send2.at[step, 0],
                self.recv2.at[step, 0],
                self.across_y,
            ),
            remote(
                self.mine.at[step, self.y, 1 - self.x, half:],
                self.got2.at[step, 1],
                self.send2.at[step, 1],
                self.recv2.at[step, 1],
                self.across_x,
            ),
        )

    def middle(self, step):
        mine, half = self.mine, self.mine.shape[3] // 2
        for copy in self.first(step):
            copy.wait_recv()
        for place in range(2):
            mine[step, place, self.x, 0:half] = plus(mine[step, place, self.x, 0:half], self.got1[step, 0, place])
            mine[step, self.y, place, half:] = plus(mine[step, self.y, place, half:], self.got1[step, 1, place])
        for copy in self.second(step):
            copy.start()

    def end(self, step):
        mine, half = self.mine, self.mine.shape[3] // 2
        for copy in self.second(step):
            copy.wait_recv()
        upper = plus(mine[step, self.y, self.x, 0:half], self.got2[step, 0])
        lower = plus(mine[step, self.y, self.x, half:], self.got2[step, 1])
        if self.sums is not None:
            self.sums[step, 0:half] = upper
            self.sums[step, half:] = lower
            return
        mine[step, self.y, self.x, 0:half] = upper
        mine[step, self.y, self.x, half:] = lower
        self.onward(step)

    def drain(self):
        for step in range(self.planes):
            wait_bytes(self.mine.at[step], self.send0.at[step])
            for copy in self.first(step) + self.second(step):
                copy.wait_send()
            if self.sums is None and step < self.planes - 1:
                self.third(step).wait_send()


class FeedCarry(Carry):
    def __init__(self, depth, up, down, refs, sems):
        super().__init__(refs[:CARRY_REFS], sems)
        (self.sums,) = refs[CARRY_REFS:]
        self.up, self.down = up, down
        self.keep = self.x if depth == 1 else 1 - self.x

    def pieces(self, row):
        return ((self.up.at[:, row], (0,)), (self.down.at[row], (1,)))

    def held(self, step):
        return self.sums.at[step]

    def first(self, step):
        return (
            remote(
                self.mine.at[step, 1 - self.keep, 0:2],
                self.got1.at[step, 0],
                self.send1.at[step, 0],
                self.recv1.at[step, 0],
                self.across_x,
            ),
            remote(
                self.mine.at[step, 1 - self.y, 2:4],
                self.got1.at[step, 1],
                self.send1.at[step, 1],
                self.recv1.at[step, 1],
                self.across_y,
            ),
        )

    def second(self, step):
        return (
            remote(
                self.mine.at[step, self.keep, 1 - self.y],
                self.got2.at[step, 0],
                self.send2.at[step, 0],
                self.recv2.at[step, 0],
                self.across_y,
            ),
            remote(
                self.mine.at[step, self.y, 3 - self.x],
                self.got2.at[step, 1],
                self.send2.at[step, 1],
                self.recv2.at[step, 1],
                self.across_x,
            ),
        )

    def middle(self, step):
        for copy in self.first(step):
            copy.wait_recv()
        self.mine[step, self.keep, 0:2] = plus(self.mine[step, self.keep, 0:2], self.got1[step, 0])
        self.mine[step, self.y, 2:4] = plus(self.mine[step, self.y, 2:4], self.got1[step, 1])
        for copy in self.second(step):
            copy.start()

    def end(self, step):
        for copy in self.second(step):
            copy.wait_recv()
        self.sums[step, 0] = plus(self.mine[step, self.keep, self.y], self.got2[step, 0])
        self.sums[step, 1] = plus(self.mine[step, self.y, 2 + self.x], self.got2[step, 1])
        self.onward(step)

    def plans(self):
        planes = self.planes
        return (
            [("b", step) for step in range(planes - 1)],
            [],
            [("m", 0), ("b", planes - 1)],
            [("m", 1)],
            [("m", step) for step in range(3, planes)],
            [("e", 1)],
            [("e", 2)],
            [("e", step) for step in range(3, planes)],
            [("m", 2), ("e", 0)],
        )

    def finish(self, out_ref):
        out_ref[...] = self.total()
        for step in range(self.planes):
            wait_bytes(self.mine.at[step], self.send0.at[step])
            for copy in self.first(step) + self.second(step):
                copy.wait_send()
            if step < self.planes - 1:
                self.third(step).wait_send()


CARRY_REFS = 6
CARRY_SEMS = 11


def carry_scratch(kind, rows, count, dp_count, dtype=bf16):
    planes = count // 2
    far = max(1, dp_count.bit_length() - 3)
    dma = pltpu.SemaphoreType.DMA
    half = rows // 2
    if kind == "attn":
        shapes = (
            (planes, 2, 2, rows),
            (planes, 2, 2, rows),
            (planes, 2, 2, half),
            (planes, 2, half),
            (planes, rows),
            (far, planes, rows),
        )
    else:
        shapes = (
            (planes, 2, 4, rows),
            (planes, 2, 4, rows),
            (planes, 2, 2, rows),
            (planes, 2, rows),
            (planes, 2, rows),
            (far, planes, 2, rows),
            (planes, 2, rows),
        )
    pair = (planes, 2)
    one = (planes,)
    sems = (one, one, one, pair, pair, pair, pair, one, one, (far, planes), (far, planes))
    return [pltpu.VMEM(shape + (D,), dtype) for shape in shapes] + [dma(shape) for shape in sems]


def z_scratch(rows, count, dp_count, dtype):
    planes = count // 2
    far = max(1, dp_count.bit_length() - 3)
    dma = pltpu.SemaphoreType.DMA
    shapes = ((planes, rows), (planes, rows), (far, planes, rows))
    sems = ((planes,), (planes,), (far, planes), (far, planes))
    return [pltpu.VMEM(shape + (D,), dtype) for shape in shapes] + [dma(shape) for shape in sems]


Z_REFS = 3
Z_SEMS = 4


def halves(value):
    high = value.astype(bf16)
    return high, (value - high.astype(f32)).astype(bf16)


def times(left, right):
    (left_high, left_low), (right_high, right_low) = left, right
    return dot_nn(
        jnp.concatenate([left_high, left_high, left_low], 1),
        jnp.concatenate([right_high, right_low, right_high], 0),
    )


def mirrored(first, second, third):
    return jnp.concatenate(
        [
            jnp.concatenate([first, second], 1),
            jnp.concatenate([jnp.transpose(second), third], 1),
        ],
        0,
    )


def times_even(left, right):
    (left_high, left_low), (right_high, right_low) = left, right
    wide = jnp.concatenate([left_high, left_high, left_low], 1)
    tall = jnp.concatenate([right_high, right_low, right_high], 0)
    return mirrored(
        dot_nn(wide[:HALF], tall[:, :HALF]),
        dot_nn(wide[:HALF], tall[:, HALF:]),
        dot_nn(wide[HALF:], tall[:, HALF:]),
    )


def gram_of(both):
    high, low = both
    wide = jnp.concatenate([high, high, low], 1)
    tall = jnp.concatenate([high, low, high], 1)
    return mirrored(
        dot_nt(wide[:HALF], tall[:HALF]),
        dot_nt(wide[:HALF], tall[HALF:]),
        dot_nt(wide[HALF:], tall[HALF:]),
    )


def clip_of(norm):
    return jnp.minimum(1.0, 0.25 / (norm + 1e-06))


def tail_kernel(
    count,
    attn_grad_ref,
    attn_done_ref,
    feed_low_ref,
    feed_high_ref,
    dout_ref,
    din_ref,
    vec0_ref,
    vec1_ref,
    vec2_ref,
    vec3_ref,
    outer_ref,
    mom_ref,
    update_ref,
    every_ref,
    small_out,
    norm_ref,
    whole_ref,
    own_ref,
    mom_s,
    small_ref,
    small_s,
    got_core,
    got_x,
    got_y,
    got_z,
    sq_seg,
    sq_dp,
    keep_s,
    give_s,
    made_ref,
    x_s,
    q_s,
    gram_s,
    high_s,
    low_s,
    mom_sem,
    last_send,
    last_recv,
    small_send,
    small_recv,
    join_send,
    join_recv,
    whole_send,
    whole_recv,
    half_sem,
    sq_send,
    sq_recv,
    sqd_send,
    sqd_recv,
    send,
    recv,
    on_send,
    on_recv,
    own_send,
    own_recv,
    *refs,
):
    carry = AttnCarry(attn_grad_ref, refs[:CARRY_REFS], refs[CARRY_REFS:])
    seg, dp, core, x, y, across_core, near, far = peers()
    across_x, across_y, across_both = near
    planes = count // 2
    plane = seg // 2
    group = 2 * y + x
    rows = own_ref.shape[1]
    targets = [{"seg": other} for other in others(seg, count)] + list(near) + list(far)
    hail(targets)
    carry.load_all()
    mom_copy = pltpu.make_async_copy(mom_ref, mom_s, mom_sem.at[0])
    mom_copy.start()
    own_ref[1] = attn_done_ref[...]

    @pl.when(x == y)
    def _():
        keep_s[...] = feed_high_ref[...]
        give_s[...] = feed_low_ref[...]

    @pl.when(x != y)
    def _():
        keep_s[...] = feed_low_ref[...]
        give_s[...] = feed_high_ref[...]

    own_ref[2 + y] = keep_s[0]
    own_ref[4 + x] = keep_s[1]
    last = (
        remote(give_s.at[0], own_ref.at[2 + y], last_send.at[0], last_recv.at[0], across_y),
        remote(give_s.at[1], own_ref.at[4 + x], last_send.at[1], last_recv.at[1], across_x),
    )
    inputs = din_ref.shape[0]
    small_ref[0:inputs, :] = din_ref[...]
    for place, ref in enumerate((vec0_ref, vec1_ref, vec2_ref, vec3_ref, outer_ref)):
        small_ref[inputs + 8 * place : inputs + 8 * place + 8, :] = ref[...]
    small_ref[inputs + 40 :, :] = jnp.zeros((SMALL - inputs - 40, D), f32)
    meet(targets)

    def span(first, size):
        return pl.ds(pl.multiple_of(first, 8), size)

    by_core, by_x, by_y = SMALL // 2, SMALL // 4, SMALL // 8
    core_at = core * by_core
    x_at = core_at + x * by_x
    y_at = x_at + y * by_y

    def small_steps():
        kept = span(core_at, by_core)
        copy = remote(
            small_ref.at[span(by_core - core_at, by_core)], got_core, small_send.at[0], small_recv.at[0], across_core
        )
        copy.start()
        yield
        copy.wait()
        small_s[kept, :] = small_ref[kept, :] + got_core[...]
        sent = span(core_at + by_x - x * by_x, by_x)
        copy = remote(small_s.at[sent], got_x, small_send.at[1], small_recv.at[1], across_x)
        copy.start()
        yield
        copy.wait()
        small_s[span(x_at, by_x), :] += got_x[...]
        sent = span(x_at + by_y - y * by_y, by_y)
        copy = remote(small_s.at[sent], got_y, small_send.at[2], small_recv.at[2], across_y)
        copy.start()
        yield
        copy.wait()
        kept = span(y_at, by_y)
        small_s[kept, :] += got_y[...]
        partners, step = list(far), 1
        while step < planes:
            partners.append({"seg": 2 * carry.toggled(step) + core})
            step *= 2
        for place, partner in enumerate(partners):
            copy = remote(
                small_s.at[kept], got_z.at[place], small_send.at[3 + place], small_recv.at[3 + place], partner
            )
            copy.start()
            yield
            copy.wait()
            small_s[kept, :] += got_z[place]

    small_run = small_steps()
    next(small_run)
    carry.send_all()
    for copy in last:
        copy.start()
    roles = owners(count)
    parts = []
    for place, (first, width, owner, spot) in enumerate(roles):
        if width == 1:
            parts.append((place, first, spot))
        elif spot == 0:
            parts += [(place, 2 + y, y), (place, 3 - y, 1 - y)]
        else:
            parts += [(place, 4 + x, 2 + x), (place, 5 - x, 3 - x)]

    def gift(part):
        place, unit, spot = parts[part]
        return remote(
            own_ref.at[unit],
            whole_ref.at[seg, spot],
            whole_send.at[part],
            whole_recv.at[seg],
            {"seg": roles[place][2]},
        )

    def give(part):
        place, unit, spot = parts[part]

        @pl.when(seg != roles[place][2])
        def _():
            gift(part).start()

        @pl.when(seg == roles[place][2])
        def _():
            whole_ref[seg, spot] = own_ref[unit]

    acts = [
        [("b", step) for step in range(planes - 1)],
        [("m", 0), ("b", planes - 1)],
        [("m", 1)],
        [("m", 2), ("e", 0)],
        [("m", step) for step in range(3, planes)],
    ] + [[("e", step)] for step in range(1, planes)]
    for part in (2, 4, 6, 8, 1):
        give(part)
    next(small_run)
    for turn, part in enumerate(acts):
        carry.run(part)
        if turn == 0:
            for copy in last:
                copy.wait()
            for later in (3, 5, 7, 9):
                give(later)
        next(small_run, None)
    own_ref[0] = carry.total()
    give(0)
    for _ in small_run:
        pass

    mine = span(y_at, by_y)
    small_out[mine, :] = small_s[mine, :]

    def join(place):
        first, size, partner = ((y_at, by_y, across_y), (x_at, by_x, across_x), (core_at, by_core, across_core))[place]
        block = small_out.at[span(first, size)]
        return remote(block, block, join_send.at[place], join_recv.at[place], partner)

    join(0).start()
    shard = dout_ref[...].astype(f32)
    square = jnp.sum(jnp.sum(shard * shard, 0, keepdims=True), 1, keepdims=True)
    for unit in range(UNITS):
        value = own_ref[unit].astype(f32)
        square = square + jnp.sum(jnp.sum(value * value, 0, keepdims=True), 1, keepdims=True)
    sums = small_s[mine, :]
    is_loss = lax.broadcasted_iota(jnp.int32, (by_y, D), 0) + y_at == inputs + 37
    sums = jnp.where(is_loss, 0.0, sums)
    square = square + jnp.sum(jnp.sum(sums * sums, 0, keepdims=True), 1, keepdims=True) * (1.0 / planes)
    sq_seg[seg] = jnp.broadcast_to(square, (8, 128))
    for step, other in enumerate(others(seg, count)):
        remote(sq_seg.at[seg], sq_seg.at[seg], sq_send.at[step], sq_recv.at[seg], {"seg": other}).start()

    def halves_copy(spot):
        part = slice(spot, spot + 2)
        return remote(whole_ref.at[:, part], whole_ref.at[:, part], half_sem.at[0], half_sem.at[1], across_core)

    for place, (first, width, owner, spot) in enumerate(roles):
        if width == 2:

            @pl.when(seg == owner)
            def _():
                for other in others(seg, count):
                    wait_bytes(whole_ref.at[other, spot : spot + width], whole_recv.at[other])
                halves_copy(spot).start()

    for other in others(seg, count):
        wait_bytes(sq_seg.at[other], sq_recv.at[other])
    sq_dp[group] = jnp.sum(sq_seg[...], 0)
    for place, target in enumerate(near):
        remote(sq_dp.at[group], sq_dp.at[group], sqd_send.at[place], sqd_recv.at[place], target).start()
    join(0).wait()
    join(1).start()
    for place, target in enumerate(near):
        remote(sq_dp.at[group], sq_dp.at[group], sqd_send.at[place], sqd_recv.at[place], target).wait()
    norm = jnp.sqrt(jnp.sum(sq_dp[...], 0)[0:1, 0:1])
    norm_ref[...] = jnp.broadcast_to(norm, norm_ref.shape)
    clip = clip_of(norm)

    def own_rows(side):
        return remote(own_ref, every_ref.at[group], own_send.at[side], own_recv.at[side], near[side])

    for side in range(3):
        own_rows(side).start()
    every_ref[group] = own_ref[...]
    mom_copy.wait()

    for place, (first, width, owner, spot) in enumerate(roles):

        @pl.when(seg == owner)
        def _():
            if width == 2:
                halves_copy(spot).wait()
            else:
                for other in others(seg, count):
                    wait_bytes(whole_ref.at[other, spot : spot + width], whole_recv.at[other])

    is_down = group >= 2
    eye = (
        lax.broadcasted_iota(jnp.int32, (D, D), 0) == lax.broadcasted_iota(jnp.int32, (D, D), 1)
    ).astype(f32)
    low = count // 4 - 1
    half = plane // (planes // 2)
    base = half * planes
    neighbours = [base + lax.rem(seg - base + step, planes) for step in range(1, planes)]
    feed_maker = 2 * (low + half)
    makers = [0, count - 2, feed_maker, feed_maker, feed_maker + 1, feed_maker + 1]

    def receivers(unit):
        return others(seg, count) if unit < 2 else neighbours

    def present(unit, slot, other):
        return remote(
            made_ref.at[other, slot],
            update_ref.at[group, unit],
            send.at[slot, other],
            recv.at[unit],
            {"seg": other},
        )

    def hand_out(unit, slot):
        for other in receivers(unit):
            present(unit, slot, other).start()
        update_ref[group, unit] = made_ref[seg, slot]

    def onward(unit, side):
        block = update_ref.at[group, unit]
        return remote(block, block, on_send.at[side, unit], on_recv.at[side, unit], near[side])

    @pl.when((seg == 0) | (seg == count - 2))
    def _():
        start = (0.5 * mom_s[:, plane // (planes - 1)].astype(f32)).reshape(D, D)
        start = start + clip * whole_ref[:, 0].astype(f32).reshape(D, D)
        size = jnp.sum(jnp.sum(start * start, 0, keepdims=True), 1, keepdims=True)
        x_s[...] = start / (jnp.sqrt(size) + 1e-07)

        def sweep(_, state):
            value = x_s[...]
            both = halves(value)
            gram = gram_of(both)
            gram_both = halves(gram)
            poly = -4.775 * gram + 2.0315 * times_even(gram_both, gram_both)
            x_s[...] = 3.4445 * value + times(halves(poly), both)
            return state

        lax.fori_loop(0, 5, sweep, 0)
        made_ref[:, 0] = x_s[...].astype(bf16).reshape(count, rows, D)
        for unit in range(2):

            @pl.when(seg == makers[unit])
            def _():
                hand_out(unit, 0)

    @pl.when((plane == low) | (plane == low + 1))
    def _():
        gram_s[...] = jnp.zeros_like(gram_s)

        def gather(tile, size):
            value = (0.5 * mom_s[:, 2 + tile].astype(f32)).reshape(D, D)
            value = value + clip * whole_ref[:, tile].astype(f32).reshape(D, D)
            high, rest = halves(value)
            high_s[tile] = high
            low_s[tile] = rest

            @pl.when(is_down)
            def _():
                high_s[tile] = jnp.transpose(high_s[tile])
                low_s[tile] = jnp.transpose(low_s[tile])

            gram_s[...] += gram_of((high_s[tile], low_s[tile]))
            return size + jnp.sum(jnp.sum(value * value, 0, keepdims=True), 1, keepdims=True)

        size = lax.fori_loop(0, 4, gather, jnp.zeros((1, 1), f32))
        scale = 1.0 / (jnp.sqrt(size) + 1e-07)
        gram_s[...] = gram_s[...] * (scale * scale)

        def poly_of(gram, gram_both):
            return 3.4445 * eye - 4.775 * gram + 2.0315 * times_even(gram_both, gram_both)

        def advance(gram_both, poly_both):
            gram_s[...] = times_even(halves(times_even(gram_both, poly_both)), poly_both)

        gram = gram_s[...]
        gram_both = halves(gram)
        poly = poly_of(gram, gram_both)
        q_s[...] = poly
        advance(gram_both, halves(poly))

        def sweep(_, state):
            gram = gram_s[...]
            gram_both = halves(gram)
            poly_both = halves(poly_of(gram, gram_both))
            q_s[...] = times_even(halves(q_s[...]), poly_both)
            advance(gram_both, poly_both)
            return state

        lax.fori_loop(0, 3, sweep, 0)
        gram = gram_s[...]
        last_both = halves(times_even(halves(q_s[...]), halves(poly_of(gram, halves(gram)))) * scale)
        for slot in range(2):
            tile = 2 * core + slot
            x_s[...] = times(last_both, (high_s[tile], low_s[tile]))

            @pl.when(is_down)
            def _():
                x_s[...] = jnp.transpose(x_s[...])

            made_ref[:, slot] = x_s[...].astype(bf16).reshape(count, rows, D)
            for side in range(2):

                @pl.when(core == side)
                def _():
                    hand_out(2 + 2 * side + slot, slot)

    join(1).wait()
    join(2).start()
    for unit in (0, 1, 2, 4, 3, 5):

        @pl.when(seg != makers[unit])
        def _():
            wait_bytes(update_ref.at[group, unit], recv.at[unit])

        for side in range(3):
            onward(unit, side).start()
    join(2).wait()
    for side in range(3):
        own_rows(side).wait()
    carry.drain()
    for part, (place, unit, spot) in enumerate(parts):

        @pl.when(seg != roles[place][2])
        def _():
            gift(part).wait_send()

    for step in range(count - 1):
        wait_bytes(sq_seg.at[0], sq_send.at[step])
    for unit in range(UNITS):
        for side in range(3):
            onward(unit, side).wait()

        @pl.when(seg == makers[unit])
        def _():
            slot = 0 if unit < 2 else unit % 2
            for other in receivers(unit):
                present(unit, slot, other).wait_send()


def tail(count, dp_count, attn, done, feed_low, feed_high, dout, pieces, momenta):
    rows = D // count
    planes = count // 2
    stages = planes.bit_length() + max(0, dp_count.bit_length() - 3)
    dma = pltpu.SemaphoreType.DMA
    vmem, anywhere = pl.BlockSpec(memory_space=pltpu.VMEM), pl.BlockSpec(memory_space=pl.ANY)
    blocks = jax.ShapeDtypeStruct((GROUPS, UNITS, rows, D), bf16)
    return pl.pallas_call(
        functools.partial(tail_kernel, count),
        out_shape=[
            blocks,
            blocks,
            jax.ShapeDtypeStruct((SMALL, D), f32),
            jax.ShapeDtypeStruct((8, 128), f32),
        ],
        in_specs=[anywhere] + [vmem] * 10 + [anywhere],
        out_specs=[vmem] * 4,
        scratch_shapes=[
            pltpu.VMEM((count, 4, rows, D), bf16),
            pltpu.VMEM((UNITS, rows, D), bf16),
            pltpu.VMEM(momenta.shape, bf16),
            pltpu.VMEM((SMALL, D), f32),
            pltpu.VMEM((SMALL, D), f32),
            pltpu.VMEM((SMALL // 2, D), f32),
            pltpu.VMEM((SMALL // 4, D), f32),
            pltpu.VMEM((SMALL // 8, D), f32),
            pltpu.VMEM((stages, SMALL // 8, D), f32),
            pltpu.VMEM((count, 8, 128), f32),
            pltpu.VMEM((GROUPS, 8, 128), f32),
            pltpu.VMEM((2, rows, D), bf16),
            pltpu.VMEM((2, rows, D), bf16),
            pltpu.VMEM((count, 2, rows, D), bf16),
            pltpu.VMEM((D, D), f32),
            pltpu.VMEM((D, D), f32),
            pltpu.VMEM((D, D), f32),
            pltpu.VMEM((4, D, D), bf16),
            pltpu.VMEM((4, D, D), bf16),
            dma((1,)),
            dma((2,)),
            dma((2,)),
            dma((stages + 3,)),
            dma((stages + 3,)),
            dma((3,)),
            dma((3,)),
            dma((10,)),
            dma((count,)),
            dma((2,)),
            dma((count,)),
            dma((count,)),
            dma((3,)),
            dma((3,)),
            dma((2, count)),
            dma((UNITS,)),
            dma((3, UNITS)),
            dma((3, UNITS)),
            dma((3,)),
            dma((3,)),
        ]
        + carry_scratch("attn", rows, count, dp_count),
        compiler_params=pltpu.CompilerParams(
            collective_id=1, has_side_effects=True, vmem_limit_bytes=VMEM_LIMIT
        ),
        cost_estimate=pl.CostEstimate(flops=2 * 10**10, bytes_accessed=10**8, transcendentals=0),
        name="tail",
    )(attn.reshape(2, 2, count, rows, D), done, feed_low, feed_high, dout, *pieces, momenta)


def embed_kernel(
    count,
    frames_ref,
    mask_ref,
    in_ref,
    outer_ref,
    attn_mom_ref,
    up_mom_ref,
    down_mom_ref,
    x_ref,
    mem_ref,
    total_ref,
    owned_ref,
    got_s,
    count_s,
    mom_s,
    mom_sem,
    frame_send,
    frame_recv,
    count_send,
    count_recv,
):
    seg = lax.axis_index("seg")
    after, before = lax.rem(seg + 1, count), lax.rem(seg + count - 1, count)
    streams = frames_ref.shape[0]
    group = lax.rem(lax.axis_index("dp"), GROUPS)
    for depth in range(LAYERS):
        pltpu.make_async_copy(attn_mom_ref.at[depth, group], mom_s.at[depth], mom_sem.at[0]).start()

        @pl.when(group == FEED_UP[depth])
        def _():
            for tile in range(4):
                source = up_mom_ref.at[depth, :, pl.ds(tile * TILE, TILE)]
                pltpu.make_async_copy(source, mom_s.at[2 + tile], mom_sem.at[0]).start()

        @pl.when(group == FEED_DOWN[depth])
        def _():
            pltpu.make_async_copy(down_mom_ref.at[depth], mom_s.at[2:6], mom_sem.at[0]).start()

    tally = jnp.sum(mask_ref[...].astype(f32), 1, keepdims=True)
    count_s[seg] = jnp.broadcast_to(
        jnp.concatenate([tally, jnp.zeros((8 - streams, 1), f32)], 0), (8, 128)
    )
    greet(seg, count, (), ())
    frame_copy = remote(frames_ref, got_s, frame_send.at[0], frame_recv.at[0], {"seg": after})
    frame_copy.start()
    for step, other in enumerate(others(seg, count)):
        remote(count_s.at[seg], count_s.at[seg], count_send.at[step], count_recv.at[seg], {"seg": other}).start()
    weight, shift = in_ref[...], outer_ref[0:1, :]
    for stream in range(streams):
        x_ref[stream] = dot_nn(jnp.transpose(frames_ref[stream]), weight) + shift
    wait_bytes(mom_s, mom_sem.at[0])
    owned_ref[...] = mom_s[...].astype(bf16)
    frame_copy.wait()
    for stream in range(streams):
        mem_ref[stream] = (dot_nn(jnp.transpose(got_s[stream]), weight) + shift).astype(bf16)
    for other in others(seg, count):
        wait_bytes(count_s.at[other], count_recv.at[other])
    total_ref[...] = jnp.sum(count_s[...], 0)
    for step in range(count - 1):
        wait_bytes(count_s.at[0], count_send.at[step])


def embed(count, frames, mask, in_weight, outer_vectors, attn_mom, up_mom, down_mom):
    streams = frames.shape[0]
    rows = D // count
    dma = pltpu.SemaphoreType.DMA
    return pl.pallas_call(
        functools.partial(embed_kernel, count),
        out_shape=[
            jax.ShapeDtypeStruct((streams, SEG, D), f32),
            jax.ShapeDtypeStruct((streams, SEG, D), bf16),
            jax.ShapeDtypeStruct((8, 128), f32),
            jax.ShapeDtypeStruct((UNITS, rows, D), bf16),
        ],
        in_specs=[pl.BlockSpec(memory_space=pltpu.VMEM)] * 4 + [pl.BlockSpec(memory_space=pl.ANY)] * 3,
        out_specs=[pl.BlockSpec(memory_space=pltpu.VMEM)] * 4,
        scratch_shapes=[
            pltpu.VMEM(frames.shape, bf16),
            pltpu.VMEM((count, 8, 128), f32),
            pltpu.VMEM((UNITS, rows, D), f32),
            dma((1,)),
            dma((1,)),
            dma((1,)),
            dma((count,)),
            dma((count,)),
        ],
        compiler_params=pltpu.CompilerParams(
            collective_id=3, has_side_effects=True, vmem_limit_bytes=VMEM_LIMIT
        ),
        cost_estimate=pl.CostEstimate(flops=2 * 10**8, bytes_accessed=4 * 10**6, transcendentals=0),
        name="embed",
    )(frames, mask, in_weight, outer_vectors, attn_mom, up_mom, down_mom.reshape(LAYERS, 4, rows, D))


FEED_UP = (1, 0)
FEED_DOWN = (2, 3)
KEEP = 1.0 - 0.3 * 0.01


def finish_kernel(norm_ref, every_ref, update_ref, dout_ref, small_ref, *refs):
    (
        attn_ref,
        attn_mom_ref,
        up_ref,
        up_mom_ref,
        down_ref,
        down_mom_ref,
        out_ref,
        out_mom_ref,
        out_sec_ref,
        in_ref,
        in_mom_ref,
        in_sec_ref,
        vec_ref,
        vec_mom_ref,
        vec_sec_ref,
        outer_ref,
        outer_mom_ref,
        outer_sec_ref,
        attn_new,
        attn_mom_new,
        attn_copy_new,
        up_new,
        up_mom_new,
        up_copy_new,
        down_new,
        down_mom_new,
        down_copy_new,
        out_new,
        out_mom_new,
        out_sec_new,
        out_copy_new,
        in_new,
        in_mom_new,
        in_sec_new,
        in_copy_new,
        vec_new,
        vec_mom_new,
        vec_sec_new,
        outer_new,
        outer_mom_new,
        outer_sec_new,
        loss_new,
        norm_new,
    ) = refs
    clip = clip_of(norm_ref[0:1, 0:1])

    def muon_step(weight, momentum, grad, update, scale):
        weight = weight * KEEP - (0.3 * scale) * update.astype(f32)
        return weight, 0.5 * momentum + clip * grad.astype(f32)

    up_scale, down_scale = max(1.0, FF / D) ** 0.5, max(1.0, D / FF) ** 0.5
    for depth in range(LAYERS):
        for kind in range(4):
            weight, momentum = muon_step(
                attn_ref[depth, kind],
                attn_mom_ref[depth, kind],
                every_ref[kind, depth],
                update_ref[kind, depth],
                1.0,
            )
            attn_new[depth, kind] = weight
            attn_mom_new[depth, kind] = momentum
            attn_copy_new[depth, kind] = weight.astype(bf16)
            columns = slice(kind * TILE, (kind + 1) * TILE)
            weight, momentum = muon_step(
                up_ref[depth, :, columns],
                up_mom_ref[depth, :, columns],
                every_ref[FEED_UP[depth], 2 + kind],
                update_ref[FEED_UP[depth], 2 + kind],
                up_scale,
            )
            up_new[depth, :, columns] = weight
            up_mom_new[depth, :, columns] = momentum
            up_copy_new[depth, :, columns] = weight.astype(bf16)
            weight, momentum = muon_step(
                down_ref[depth, kind],
                down_mom_ref[depth, kind],
                every_ref[FEED_DOWN[depth], 2 + kind],
                update_ref[FEED_DOWN[depth], 2 + kind],
                down_scale,
            )
            down_new[depth, kind] = weight
            down_mom_new[depth, kind] = momentum
            down_copy_new[depth, kind] = weight.astype(bf16)
    for low in range(2):
        for right in range(2):
            columns = slice(right * D, (right + 1) * D)
            weight, moment, second = adamw(
                out_ref[low, :, columns],
                out_mom_ref[low, :, columns],
                out_sec_ref[low, :, columns],
                dout_ref[2 * right + low].astype(f32) * clip,
                0.05,
                0.01,
            )
            out_new[low, :, columns] = weight
            out_mom_new[low, :, columns] = moment
            out_sec_new[low, :, columns] = second
            out_copy_new[low, :, columns] = weight.astype(bf16)

    @pl.when(pl.program_id(0) == 0)
    def _():
        inputs = in_ref.shape[0]
        weight, moment, second = adamw(
            in_ref[...], in_mom_ref[...], in_sec_ref[...], small_ref[0:inputs, :] * clip, 0.05, 0.01
        )
        in_new[...] = weight
        in_mom_new[...] = moment
        in_sec_new[...] = second
        in_copy_new[...] = weight.astype(bf16)

        norm_new[...] = norm_ref[0:1, 0:1]
        loss_new[...] = small_ref[inputs + 37 : inputs + 38, 0:1]

        def rows_of(first, last, base):
            return small_ref[inputs + base + first : inputs + base + last, :]

        for depth in range(LAYERS):
            base = 16 * depth
            for low, high, grad in (
                (0, 2, rows_of(0, 2, base)),
                (2, 4, rows_of(0, 2, base + 8)),
                (4, 7, rows_of(2, 5, base)),
                (7, 8, rows_of(2, 3, base + 8)),
                (8, 12, rows_of(4, 8, base + 8)),
            ):
                weight, moment, second = adamw(
                    vec_ref[low:high, depth],
                    vec_mom_ref[low:high, depth],
                    vec_sec_ref[low:high, depth],
                    grad * clip,
                    0.25,
                    0.0,
                )
                vec_new[low:high, depth] = weight
                vec_mom_new[low:high, depth] = moment
                vec_sec_new[low:high, depth] = second
        for low, high, grad in ((0, 1, rows_of(5, 6, 0)), (1, 5, rows_of(1, 5, 32))):
            weight, moment, second = adamw(
                outer_ref[low:high, :], outer_mom_ref[low:high, :], outer_sec_ref[low:high, :], grad * clip, 0.25, 0.0
            )
            outer_new[low:high, :] = weight
            outer_mom_new[low:high, :] = moment
            outer_sec_new[low:high, :] = second


def finish(rows, norm, every, updates, dout, small, arrays):
    steps = rows // 16
    attn, _, up, _, down, _, out, _, _, inp, _, _, vec, _, _, outer, _, _ = arrays
    codes = out.shape[2]
    part = out.shape[1] // steps
    blocks = pl.BlockSpec((GROUPS, UNITS, 16, D), lambda i: (0, 0, i, 0))
    attn_spec = pl.BlockSpec((LAYERS, 4, 16, D), lambda i: (0, 0, i, 0))
    up_spec = pl.BlockSpec((LAYERS, 16, FF), lambda i: (0, i, 0))
    out_spec = pl.BlockSpec((2, part, codes), lambda i: (0, i, 0))
    dout_spec = pl.BlockSpec((GROUPS, part, D), lambda i: (0, i, 0))
    in_spec, vec_spec, outer_spec = whole_spec(inp.shape), whole_spec(vec.shape), whole_spec(outer.shape)

    def like(array, dtype=f32):
        return jax.ShapeDtypeStruct(array.shape, dtype)

    return pl.pallas_call(
        finish_kernel,
        grid=(steps,),
        out_shape=[like(attn), like(attn), like(attn, bf16)]
        + [like(up), like(up), like(up, bf16)]
        + [like(down), like(down), like(down, bf16)]
        + [like(out)] * 3
        + [like(out, bf16)]
        + [like(inp)] * 3
        + [like(inp, bf16)]
        + [like(vec)] * 3
        + [like(outer)] * 3
        + [jax.ShapeDtypeStruct((1, 1), f32)] * 2,
        in_specs=[whole_spec((8, 128)), blocks, blocks, dout_spec, whole_spec(small.shape)]
        + [attn_spec] * 2
        + [up_spec] * 2
        + [attn_spec] * 2
        + [out_spec] * 3
        + [in_spec] * 3
        + [vec_spec] * 3
        + [outer_spec] * 3,
        out_specs=[attn_spec] * 3
        + [up_spec] * 3
        + [attn_spec] * 3
        + [out_spec] * 4
        + [in_spec] * 4
        + [vec_spec] * 3
        + [outer_spec] * 3
        + [whole_spec((1, 1))] * 2,
        compiler_params=pltpu.CompilerParams(vmem_limit_bytes=VMEM_LIMIT),
        cost_estimate=pl.CostEstimate(flops=10**8, bytes_accessed=4 * 10**7, transcendentals=0),
        name="finish",
    )(norm, every, updates, dout, small, *arrays)


def local(
    frames,
    speech_mask,
    targets,
    in_proj,
    in_moment,
    in_second,
    out_proj,
    out_moment,
    out_second,
    layer_vectors,
    vectors_moment,
    vectors_second,
    outer_vectors,
    outer_moment,
    outer_second,
    attn_proj,
    attn_momentum,
    ff_up,
    up_momentum,
    ff_down,
    down_momentum,
    in_copy,
    out_copy,
    attn_copy,
    up_copy,
    down_copy,
):
    segment = lax.axis_index("seg")
    count, dp_count = lax.axis_size("seg"), lax.axis_size("dp")
    rows = D // count
    streams = frames.shape[0]
    stream_total = streams * dp_count
    frames_t = jnp.swapaxes(frames, 1, 2)
    bias = jnp.where(segment > 0, 0.0, -1e30).astype(f32)[None]
    hidden, memory, totals, owned = embed(
        count, frames_t, speech_mask, in_copy, outer_vectors, attn_momentum, up_momentum, down_momentum
    )
    momenta = lax.all_gather(owned, "seg", axis=0, tiled=False)
    memory = [memory] * streams
    kept = []
    for depth in range(LAYERS):
        saved, passed = None, []
        for stream in range(streams):
            saved, short = forward_layer(
                depth,
                stream,
                streams,
                bias,
                hidden,
                memory[stream],
                attn_copy,
                up_copy,
                down_copy,
                layer_vectors,
                saved,
            )
            if depth + 1 < LAYERS:
                passed.append(from_behind(short, "seg", 1))
        kept.append((hidden, saved[8], saved))
        hidden = saved[0]
        memory = passed
    grad_hidden, grad_out, head_outer = head(
        hidden, targets, speech_mask, totals, out_copy, outer_vectors, 1.0 / stream_total, momenta
    )
    vector_grads, feed_done = [], [None, None]
    carried = grad_out.reshape(GROUPS * D // 2, D)
    carried_done = []
    for depth in reversed(range(LAYERS)):
        entering, held, saved = kept[depth]
        dafter, grad_up, grad_down, feed_vec, sums = feed_back(
            depth, grad_hidden, saved[7], up_copy, down_copy, layer_vectors, count, dp_count, carried
        )
        grad_hidden, grad_attn, attn_vec, grad_in, feed_done[depth], done = attend_back(
            depth,
            bias,
            dafter,
            entering,
            held,
            saved[1:7],
            attn_copy,
            layer_vectors,
            frames_t,
            grad_up,
            grad_down,
            sums,
            count,
            dp_count,
        )
        carried_done.append(done)
        carried = grad_attn.reshape(4 * D, D)
        vector_grads = [attn_vec, feed_vec] + vector_grads
    out_done, attn_done = carried_done
    every_out = lax.all_gather(out_done, ("dp", "seg"), axis=0, tiled=True)[: GROUPS * D // 2]
    every_out = every_out.reshape(GROUPS, D // 2, D)
    updates, every, small, norm = tail(
        count,
        dp_count,
        grad_attn,
        attn_done,
        feed_done[0],
        feed_done[1],
        out_done,
        [grad_in] + vector_grads + [head_outer],
        momenta,
    )
    split = (LAYERS, 4, rows, D)
    halved = (2, D // 2, out_proj.shape[1])
    (
        attn_new,
        attn_mom,
        attn_copy_new,
        up_new,
        up_mom,
        up_copy_new,
        down_new,
        down_mom,
        down_copy_new,
        out_new,
        out_moment_new,
        out_second_new,
        out_copy_new,
        in_new,
        in_moment_new,
        in_second_new,
        in_copy_new,
        vectors_new,
        vectors_moment_new,
        vectors_second_new,
        outer_new,
        outer_moment_new,
        outer_second_new,
        loss_sum,
        norm,
    ) = finish(
        rows,
        norm,
        every,
        updates,
        every_out,
        small,
        [
            attn_proj,
            attn_momentum,
            ff_up,
            up_momentum,
            ff_down.reshape(split),
            down_momentum.reshape(split),
            out_proj.reshape(halved),
            out_moment.reshape(halved),
            out_second.reshape(halved),
            in_proj,
            in_moment,
            in_second,
            jnp.swapaxes(layer_vectors, 0, 1),
            jnp.swapaxes(vectors_moment, 0, 1),
            jnp.swapaxes(vectors_second, 0, 1),
            outer_vectors,
            outer_moment,
            outer_second,
        ],
    )
    return (
        loss_sum.reshape(()),
        norm.reshape(()),
        in_new,
        in_moment_new,
        in_second_new,
        out_new.reshape(out_proj.shape),
        out_moment_new.reshape(out_proj.shape),
        out_second_new.reshape(out_proj.shape),
        jnp.swapaxes(vectors_new, 0, 1),
        jnp.swapaxes(vectors_moment_new, 0, 1),
        jnp.swapaxes(vectors_second_new, 0, 1),
        outer_new,
        outer_moment_new,
        outer_second_new,
        attn_new,
        attn_mom,
        up_new,
        up_mom,
        down_new.reshape(ff_down.shape),
        down_mom.reshape(ff_down.shape),
        in_copy_new,
        out_copy_new.reshape(out_proj.shape),
        attn_copy_new,
        up_copy_new,
        down_copy_new.reshape(ff_down.shape),
    )


def solution(mesh):
    return jax.shard_map(
        local,
        mesh=mesh,
        in_specs=(
            P("dp", "seg", None),
            P("dp", "seg"),
            P("dp", "seg"),
            P(),
            P(),
            P(),
            P(),
            P(),
            P(),
            P(),
            P(),
            P(),
            P(),
            P(),
            P(),
            P(None, None, "seg", None),
            P(None, None, "seg", None),
            P(None, "seg", None),
            P(None, "seg", None),
            P(None, "seg", None),
            P(None, "seg", None),
            P(),
            P(),
            P(),
            P(),
            P(),
        ),
        out_specs=(
            P(),
            P(),
            P(),
            P(),
            P(),
            P(),
            P(),
            P(),
            P(),
            P(),
            P(),
            P(),
            P(),
            P(),
            P(None, None, "seg", None),
            P(None, None, "seg", None),
            P(None, "seg", None),
            P(None, "seg", None),
            P(None, "seg", None),
            P(None, "seg", None),
            P(),
            P(),
            P(None, None, "seg", None),
            P(None, "seg", None),
            P(None, "seg", None),
        ),
        check_vma=False,
    )
```
